32 devices in a mesh: section: 2 (over core), batch: 4 (over y, x), rows: 4 (over z).
Axes of the slice: x: 2, y: 2, z: 4, core: 2. Of those that a mesh axis runs over, the one named last changes fastest.
Arguments:
- frames: float32 [32, 12, 16, 64], P(('section', 'batch'), None, 'rows'), may hold values from -32 to 32
- counts: int32 [32], P(('section', 'batch')), may hold values from 1 to 4
- cell_mask: int32 [32, 16, 64], P(('section', 'batch'), 'rows'), may hold values 0 or 1
- step_index: int32 [32], P(('section', 'batch')), may hold values from 0 to 3
- lift_weight: float32 [12, 128], replicated, may hold values from -1.75 to 1.75
- lift_bias: float32 [128], replicated, may hold values from -3 to 3
- enc_norm1_gain: float32 [128], replicated, may hold values from 0.25 to 1.75
- enc_norm1_bias: float32 [128], replicated, may hold values from -3 to 3
- enc_conv1: float32 [3, 3, 128, 128], replicated, may hold values from -0.1875 to 0.1875
- enc_step_table: float32 [4, 256], replicated, may hold values from -2 to 2
- enc_norm2_gain: float32 [128], replicated, may hold values from 0.25 to 1.75
- enc_norm2_bias: float32 [128], replicated, may hold values from -3 to 3
- enc_conv2: float32 [3, 3, 128, 128], replicated, may hold values from -0.1875 to 0.1875
- enc_conv2_bias: float32 [128], replicated, may hold values from -3 to 3
- reducer_weight: float32 [2, 2, 128, 128], replicated, may hold values from -0.25 to 0.25
- reducer_bias: float32 [128], replicated, may hold values from -3 to 3
- up_weight: float32 [2, 2, 128, 128], replicated, may hold values from -0.5 to 0.5
- up_bias: float32 [128], replicated, may hold values from -3 to 3
- dec_norm1_gain: float32 [256], replicated, may hold values from 0.25 to 1.75
- dec_norm1_bias: float32 [256], replicated, may hold values from -3 to 3
- dec_conv1: float32 [3, 3, 256, 128], replicated, may hold values from -0.125 to 0.125
- dec_step_table: float32 [4, 256], replicated, may hold values from -2 to 2
- dec_norm2_gain: float32 [128], replicated, may hold values from 0.25 to 1.75
- dec_norm2_bias: float32 [128], replicated, may hold values from -3 to 3
- dec_conv2: float32 [3, 3, 128, 128], replicated, may hold values from -0.1875 to 0.1875
- dec_conv2_bias: float32 [128], replicated, may hold values from -3 to 3
- skip_weight: float32 [256, 128], replicated, may hold values from -0.375 to 0.375
- skip_bias: float32 [128], replicated, may hold values from -3 to 3
- cotangent: float32 [32, 16, 64, 128], P(('section', 'batch'), 'rows'), may hold values from -6 to 6
Outputs:
- output: float32 [32, 16, 64, 128], P(('section', 'batch'), 'rows')
- frames_grad: float32 [32, 12, 16, 64], P(('section', 'batch'), None, 'rows')
- grad_lift_weight: float32 [12, 128], replicated
- grad_lift_bias: float32 [128], replicated
- grad_enc_norm1_gain: float32 [128], replicated
- grad_enc_norm1_bias: float32 [128], replicated
- grad_enc_conv1: float32 [3, 3, 128, 128], replicated
- grad_enc_step_table: float32 [4, 256], replicated
- grad_enc_norm2_gain: float32 [128], replicated
- grad_enc_norm2_bias: float32 [128], replicated
- grad_enc_conv2: float32 [3, 3, 128, 128], replicated
- grad_enc_conv2_bias: float32 [128], replicated
- grad_down_weight: float32 [2, 2, 128, 128], replicated
- grad_down_bias: float32 [128], replicated
- grad_up_weight: float32 [2, 2, 128, 128], replicated
- grad_up_bias: float32 [128], replicated
- grad_dec_norm1_gain: float32 [256], replicated
- grad_dec_norm1_bias: float32 [256], replicated
- grad_dec_conv1: float32 [3, 3, 256, 128], replicated
- grad_dec_step_table: float32 [4, 256], replicated
- grad_dec_norm2_gain: float32 [128], replicated
- grad_dec_norm2_bias: float32 [128], replicated
- grad_dec_conv2: float32 [3, 3, 128, 128], replicated
- grad_dec_conv2_bias: float32 [128], replicated
- grad_skip_weight: float32 [256, 128], replicated
- grad_skip_bias: float32 [128], replicated
The draws below stay inside these ranges and needn't reach their ends.
All inputs are finite; a program needn't handle non-finite values. No bound on the sum of `cell_mask` on one device may be relied on, other than what follows from the above.
Results may differ from the reference program's by a relative error of at most 0.0003.
Values sent between devices are 32-bit elements; how exact they have to be, the bound alone decides.
A program may use at most 128 MiB of HBM per device.

```python
import jax
import jax.numpy as jnp
from jax import lax

C = 128
GROUPS = 8
FIELDS = 3
HIST = 4
STEPS = 4
FR = 12
W = 64
H = 16
ITEMS = 32


def draw_frames(key, part):
    key = jax.random.fold_in(key, 17)
    base_key, rough_key = jax.random.split(key)
    extent = (ITEMS, FR, H, W)
    position = jnp.arange(H, dtype=jnp.float32) / max(H - 1, 1)
    base_values = jax.random.truncated_normal(base_key, -4.0, 4.0, extent, jnp.float32)
    rising = jnp.exp(jnp.log(3.0) * position)
    roughness = jnp.exp(jax.random.uniform(rough_key, extent, jnp.float32, jnp.log(0.6), jnp.log(1.6)))
    return base_values * roughness * rising[None, None, :, None]


def with_ends(entries, key, least, top_value):
    longest = entries.shape.index(max(entries.shape))
    spots = []
    for shift in (0, 1):
        where = [jax.random.randint(jax.random.fold_in(key, axis), (), 0, length) for axis, length in enumerate(entries.shape)]
        where[longest] = (where[longest] + shift) % entries.shape[longest]
        spots.append(tuple(where))
    return entries.at[spots[0]].set(least).at[spots[1]].set(top_value)


def levels(stream_key, shape, cuts, least, top_value):
    def one(dim, parts):
        steps = jax.random.uniform(jax.random.fold_in(jax.random.fold_in(stream_key, 6), dim), (parts,), jnp.float32, least / len(cuts), top_value / len(cuts))
        return jnp.repeat(jnp.exp(steps), shape[dim] // parts).reshape((-1,) + (1,) * (len(shape) - dim - 1))

    loudness = one(*cuts[0])
    for cut in cuts[1:]:
        loudness = loudness * one(*cut)
    return loudness


def bell_draw(stream_key, shape, scale, most, cuts=(), kind=jnp.bfloat16):
    loudness = levels(stream_key, shape, cuts, -0.22, 0.18) if cuts else 1.0
    array = jax.random.normal(stream_key, shape, jnp.float32) * scale * loudness
    return jnp.minimum(jnp.maximum(array, -most), most).astype(kind)


def setup_inputs(seed: int = 0) -> dict:
    splits = jax.random.split(jax.random.key(seed), 30)
    return {
        "frames": draw_frames(jax.random.fold_in(splits[29], 71), 0),
        "counts": with_ends(jax.random.randint(splits[1], (ITEMS,), 1, HIST + 1), jax.random.fold_in(splits[1], 1), 1, HIST).astype(jnp.int32),
        "cell_mask": with_ends((jax.random.randint(splits[2], (ITEMS, H, W), 0, 8) < 7).astype(jnp.int32), jax.random.fold_in(splits[2], 1), 0, 1),
        "step_index": with_ends(jax.random.randint(splits[3], (ITEMS,), 0, STEPS), jax.random.fold_in(splits[3], 1), 0, STEPS - 1).astype(jnp.int32),
        "lift_weight": bell_draw(splits[4], (FR, C), FR ** -0.5, 1.75, (), jnp.float32),
        "lift_bias": bell_draw(splits[5], (C,), 0.5, 3.0, (), jnp.float32),
        "enc_norm1_gain": jnp.clip(1.0 + 0.15 * jax.random.normal(splits[6], (C,), jnp.float32), 0.25, 1.75),
        "enc_norm1_bias": bell_draw(splits[7], (C,), 0.4, 3.0, (), jnp.float32),
        "enc_conv1": bell_draw(splits[8], (3, 3, C, C), (9 * C) ** -0.5, 0.1875, (), jnp.float32),
        "enc_step_table": bell_draw(splits[9], (STEPS, 2 * C), 0.3, 2.0, (), jnp.float32),
        "enc_norm2_gain": jnp.clip(1.0 + 0.15 * jax.random.normal(splits[10], (C,), jnp.float32), 0.25, 1.75),
        "enc_norm2_bias": bell_draw(splits[11], (C,), 0.4, 3.0, (), jnp.float32),
        "enc_conv2": bell_draw(splits[12], (3, 3, C, C), (9 * C) ** -0.5, 0.1875, (), jnp.float32),
        "enc_conv2_bias": bell_draw(splits[13], (C,), 0.4, 3.0, (), jnp.float32),
        "reducer_weight": bell_draw(splits[14], (2, 2, C, C), (4 * C) ** -0.5, 0.25, (), jnp.float32),
        "reducer_bias": bell_draw(splits[15], (C,), 0.4, 3.0, (), jnp.float32),
        "up_weight": bell_draw(splits[16], (2, 2, C, C), C ** -0.5, 0.5, (), jnp.float32),
        "up_bias": bell_draw(splits[17], (C,), 0.4, 3.0, (), jnp.float32),
        "dec_norm1_gain": jnp.clip(1.0 + 0.15 * jax.random.normal(splits[18], (2 * C,), jnp.float32), 0.25, 1.75),
        "dec_norm1_bias": bell_draw(splits[19], (2 * C,), 0.4, 3.0, (), jnp.float32),
        "dec_conv1": bell_draw(splits[20], (3, 3, 2 * C, C), (18 * C) ** -0.5, 0.125, (), jnp.float32),
        "dec_step_table": bell_draw(splits[21], (STEPS, 2 * C), 0.3, 2.0, (), jnp.float32),
        "dec_norm2_gain": jnp.clip(1.0 + 0.15 * jax.random.normal(splits[22], (C,), jnp.float32), 0.25, 1.75),
        "dec_norm2_bias": bell_draw(splits[23], (C,), 0.4, 3.0, (), jnp.float32),
        "dec_conv2": bell_draw(splits[24], (3, 3, C, C), (9 * C) ** -0.5, 0.1875, (), jnp.float32),
        "dec_conv2_bias": bell_draw(splits[25], (C,), 0.4, 3.0, (), jnp.float32),
        "skip_weight": bell_draw(splits[26], (2 * C, C), (2 * C) ** -0.5, 0.375, (), jnp.float32),
        "skip_bias": bell_draw(splits[27], (C,), 0.4, 3.0, (), jnp.float32),
        "cotangent": bell_draw(splits[28], (ITEMS, H, W, C), 1.0, 6.0, ((0, 8), (1, 4)), jnp.float32),
    }


@jax.custom_vjp
def low(v):
    return lax.optimization_barrier(v.astype(jnp.bfloat16)).astype(jnp.float32)

@jax.custom_vjp
def low_back(v):
    return v

def low_keep(v):
    return (low(v), None)

def low_pass(kept, grad):
    return (grad,)

def back_keep(v):
    return (v, None)

def back_low(kept, grad):
    return (low(grad),)
low.defvjp(low_keep, low_pass)
low_back.defvjp(back_keep, back_low)
EPS = 1e-05
HIGH = lax.Precision.HIGHEST

def group_norm(value_arrays, norm_gain, norm_bias):
    extent = value_arrays.shape
    grouped = value_arrays.reshape(extent[:-1] + (GROUPS, extent[-1] // GROUPS))
    group_mean = lax.optimization_barrier(jnp.mean(grouped, axis=(0, 1, 3)))
    group_square = lax.optimization_barrier(jnp.mean(grouped * grouped, axis=(0, 1, 3)))
    inverse = lax.rsqrt(group_square - group_mean * group_mean + EPS)
    normed = (grouped - group_mean[:, None]) * inverse[:, None]
    return normed.reshape(extent) * norm_gain + norm_bias

def conv_three(value_arrays, kernel):
    return lax.conv_general_dilated(value_arrays[None], kernel, (1, 1), ((1, 1), (1, 1)), dimension_numbers=('NHWC', 'HWIO', 'NHWC'), precision=HIGH)[0]

def res_block(inputs, step_item, norm1_gain, norm1_bias, conv1, table, norm2_gain, norm2_bias, conv2, conv2_bias):
    one_hot = (jnp.arange(STEPS, dtype=jnp.int32) == step_item).astype(jnp.float32)
    condition = jnp.dot(one_hot, table, precision=HIGH)
    half_width = table.shape[1] // 2
    scale_part = condition[:half_width]
    shift_part = condition[half_width:]
    first_act = jax.nn.gelu(group_norm(inputs, norm1_gain, norm1_bias), approximate=False)
    middle = conv_three(first_act, conv1)
    shaped = group_norm(middle, norm2_gain, norm2_bias) * (1.0 + scale_part) + shift_part
    return conv_three(jax.nn.gelu(shaped, approximate=False), conv2) + conv2_bias

def item_forward(frames_item, mask_item, count_item, step_item, weights):
    lift_weight, lift_bias, enc_norm1_gain, enc_norm1_bias, enc_conv1, enc_step_table, enc_norm2_gain, enc_norm2_bias, enc_conv2, enc_conv2_bias, reducer_weight, reducer_bias, up_weight, up_bias, dec_norm1_gain, dec_norm1_bias, dec_conv1, dec_step_table, dec_norm2_gain, dec_norm2_bias, dec_conv2, dec_conv2_bias, skip_weight, skip_bias = weights
    history = jnp.arange(HIST, dtype=jnp.int32) >= HIST - count_item
    keep = jnp.repeat(history, FIELDS).astype(jnp.float32)
    lifted = jnp.einsum('fhw,fc->hwc', frames_item * keep[:, None, None], lift_weight, precision=HIGH) + lift_bias
    lifted = lifted * mask_item[:, :, None].astype(jnp.float32)
    encoder_result = lifted + res_block(lifted, step_item, enc_norm1_gain, enc_norm1_bias, enc_conv1, enc_step_table, enc_norm2_gain, enc_norm2_bias, enc_conv2, enc_conv2_bias)
    extent = encoder_result.shape
    blocks = encoder_result.reshape(extent[0] // 2, 2, extent[1] // 2, 2, extent[2])
    coarse_field = jnp.einsum('iajbk,abkc->ijc', blocks, reducer_weight, precision=HIGH) + reducer_bias
    raised = jnp.einsum('ijk,abkc->iajbc', coarse_field, up_weight, precision=HIGH).reshape(extent) + up_bias
    joined = jnp.concatenate([raised, encoder_result], axis=-1)
    branch = res_block(joined, step_item, dec_norm1_gain, dec_norm1_bias, dec_conv1, dec_step_table, dec_norm2_gain, dec_norm2_bias, dec_conv2, dec_conv2_bias)
    return jnp.dot(joined, skip_weight, precision=HIGH) + skip_bias + branch

def reference(frames, counts, cell_mask, step_index, lift_weight, lift_bias, enc_norm1_gain, enc_norm1_bias, enc_conv1, enc_step_table, enc_norm2_gain, enc_norm2_bias, enc_conv2, enc_conv2_bias, reducer_weight, reducer_bias, up_weight, up_bias, dec_norm1_gain, dec_norm1_bias, dec_conv1, dec_step_table, dec_norm2_gain, dec_norm2_bias, dec_conv2, dec_conv2_bias, skip_weight, skip_bias, cotangent):
    params = (lift_weight, lift_bias, enc_norm1_gain, enc_norm1_bias, enc_conv1, enc_step_table, enc_norm2_gain, enc_norm2_bias, enc_conv2, enc_conv2_bias, reducer_weight, reducer_bias, up_weight, up_bias, dec_norm1_gain, dec_norm1_bias, dec_conv1, dec_step_table, dec_norm2_gain, dec_norm2_bias, dec_conv2, dec_conv2_bias, skip_weight, skip_bias)

    def forward(frames_in, weights):
        return jax.vmap(item_forward, in_axes=(0, 0, 0, 0, None))(frames_in, cell_mask, counts, step_index, weights)
    output, pull = jax.vjp(forward, frames, params)
    frames_grad, grads = pull(cotangent)
    return (output, frames_grad, grads[0], grads[1], grads[2], grads[3], grads[4], grads[5], grads[6], grads[7], grads[8], grads[9], grads[10], grads[11], grads[12], grads[13], grads[14], grads[15], grads[16], grads[17], grads[18], grads[19], grads[20], grads[21], grads[22], grads[23])
```

```python
import functools
from types import SimpleNamespace
from typing import Any, NamedTuple

import jax
import jax.numpy as jnp
from jax import lax
from jax.experimental import pallas as pl
from jax.experimental.pallas import tpu as pltpu
from jax.sharding import PartitionSpec as P

GROUPS = 8
FIELDS = 3
HIST = 4


EPS = 1e-05
HIGH = lax.Precision.HIGHEST


def extended(cells, sides, width):
    for axis, dim in sides:
        count = lax.axis_size(axis)
        ends = count - 1
        head = lax.slice_in_dim(cells, 0, width, axis=dim)
        tail = lax.slice_in_dim(cells, cells.shape[dim] - width, cells.shape[dim], axis=dim)
        cells = jnp.concatenate(
            [
                lax.ppermute(tail, axis, [(i, (i + 1) % count) for i in range(ends)]),
                cells,
                lax.ppermute(head, axis, [((i + 1) % count, i) for i in range(ends)]),
            ],
            axis=dim,
        )
    return cells


def from_behind(value, axis, steps):
    count = lax.axis_size(axis)
    pairs = [(source, (source + steps) % count) for source in range(count)]
    return lax.ppermute(value, axis, pairs)


def group_view(value_arrays):
    extent = value_arrays.shape
    return value_arrays.reshape(extent[:-1] + (GROUPS, extent[-1] // GROUPS))


def global_sums(value_arrays):
    grouped = group_view(value_arrays)
    flat = grouped.reshape(-1, GROUPS, grouped.shape[-1])
    first_sum = jnp.sum(flat, axis=(0, 2))
    second_sum = jnp.sum(flat * flat, axis=(0, 2))
    return lax.psum((first_sum, second_sum), "rows")


def apply_norm(value_arrays, sum_one, sum_two, norm_gain, norm_bias, total):
    grouped = group_view(value_arrays)
    group_mean = sum_one / total
    variance = sum_two / total - group_mean * group_mean
    inverse = lax.rsqrt(variance + EPS)
    normed = (grouped - group_mean[:, None]) * inverse[:, None]
    return normed.reshape(value_arrays.shape) * norm_gain + norm_bias


def norm_back(value_arrays, grad_one, grad_two):
    grouped = group_view(value_arrays)
    extra = grad_one[:, None] + 2.0 * grouped * grad_two[:, None]
    return extra.reshape(value_arrays.shape)


def reduce_grads(grad_one, grad_two):
    return lax.psum((grad_one, grad_two), "rows")


def conv_rows(padded, kernel):
    widened = jnp.pad(padded, ((0, 0), (1, 1), (0, 0)))
    return lax.conv_general_dilated(
        widened[None],
        kernel,
        (1, 1),
        "VALID",
        dimension_numbers=("NHWC", "HWIO", "NHWC"),
        precision=HIGH,
    )[0]


def flipped(kernel):
    return jnp.transpose(kernel[::-1, ::-1], (0, 1, 3, 2))


def pad_grads(value_arrays):
    return extended(value_arrays, (("rows", 0),), 1)


def totals_of(inputs, conv1):
    strip = inputs.shape[0]
    cells = strip * lax.axis_size("rows") * inputs.shape[1]
    return (cells * (inputs.shape[2] // GROUPS), cells * (conv1.shape[3] // GROUPS))


def block_forward(inputs, weights, scale_part, shift_part):
    norm1_gain, norm1_bias, conv1, norm2_gain, norm2_bias, conv2, conv2_bias = weights
    total_in, total_mid = totals_of(inputs, conv1)
    sums_in = global_sums(inputs)

    def pad_rows(value_arrays):
        return extended(value_arrays, (("rows", 0),), 1)

    act_one = pad_rows(
        jax.nn.gelu(
            apply_norm(inputs, sums_in[0], sums_in[1], norm1_gain, norm1_bias, total_in),
            approximate=False,
        )
    )
    middle = conv_rows(act_one, conv1)
    sums_mid = global_sums(middle)
    shaped = (
        apply_norm(middle, sums_mid[0], sums_mid[1], norm2_gain, norm2_bias, total_mid)
        * (1.0 + scale_part)
        + shift_part
    )
    act_two = pad_rows(jax.nn.gelu(shaped, approximate=False))
    branch = conv_rows(act_two, conv2) + conv2_bias
    return (branch, (sums_in[0], sums_in[1], act_one, middle, sums_mid[0], sums_mid[1], act_two))


def block_backward(inputs, weights, scale_part, shift_part, kept, grad_out):
    norm1_gain, norm1_bias, conv1, norm2_gain, norm2_bias, conv2, conv2_bias = weights
    in_one, in_two, act_one, middle, mid_one, mid_two, act_two = kept
    total_in, total_mid = totals_of(inputs, conv1)
    grad_conv2 = jax.vjp(lambda kernel: conv_rows(act_two, kernel), conv2)[1](grad_out)[0]
    grad_bias2 = jnp.sum(grad_out, axis=(0, 1))
    grad_act_two = conv_rows(pad_grads(grad_out), flipped(conv2))

    def second_piece(middle_in, sum_one, sum_two, gain_in, incoming_bias, scale_in, shift_in):
        shaped = (
            apply_norm(middle_in, sum_one, sum_two, gain_in, incoming_bias, total_mid)
            * (1.0 + scale_in)
            + shift_in
        )
        return jax.nn.gelu(shaped, approximate=False)

    second_pull = jax.vjp(
        second_piece, middle, mid_one, mid_two, norm2_gain, norm2_bias, scale_part, shift_part
    )[1](grad_act_two)
    summed_one, summed_two = reduce_grads(second_pull[1], second_pull[2])
    grad_middle = second_pull[0] + norm_back(middle, summed_one, summed_two)
    grad_conv1 = jax.vjp(lambda kernel: conv_rows(act_one, kernel), conv1)[1](grad_middle)[0]
    grad_act_one = conv_rows(pad_grads(grad_middle), flipped(conv1))

    def first_piece(inputs_in, sum_one, sum_two, gain_in, incoming_bias):
        return jax.nn.gelu(
            apply_norm(inputs_in, sum_one, sum_two, gain_in, incoming_bias, total_in),
            approximate=False,
        )

    first_pull = jax.vjp(first_piece, inputs, in_one, in_two, norm1_gain, norm1_bias)[1](
        grad_act_one
    )
    first_one, first_two = reduce_grads(first_pull[1], first_pull[2])
    grad_inputs = first_pull[0] + norm_back(inputs, first_one, first_two)
    grads = (
        first_pull[3],
        first_pull[4],
        grad_conv1,
        second_pull[3],
        second_pull[4],
        grad_conv2,
        grad_bias2,
    )
    return (grad_inputs, grads, second_pull[5], second_pull[6])


def conditioning(step_item, table):
    one_hot = (jnp.arange(table.shape[0], dtype=jnp.int32) == step_item).astype(jnp.float32)
    condition = jnp.dot(one_hot, table, precision=HIGH)
    half_width = table.shape[1] // 2
    return (condition[:half_width], condition[half_width:], one_hot)


def project_in(frames_item, mask_item, count_item, incoming_weight, incoming_bias):
    history = jnp.arange(HIST, dtype=jnp.int32) >= HIST - count_item
    keep = jnp.repeat(history, FIELDS).astype(jnp.float32)
    lifted = (
        jnp.einsum(
            "fhw,fc->hwc", frames_item * keep[:, None, None], incoming_weight, precision=HIGH
        )
        + incoming_bias
    )
    return lifted * mask_item[:, :, None].astype(jnp.float32)


def coarsen_field(value_arrays, incoming_weight, incoming_bias):
    rows_here, width_here, depth_here = value_arrays.shape
    blocks = value_arrays.reshape(rows_here // 2, 2, width_here // 2, 2, depth_here)
    return jnp.einsum("iajbk,abkc->ijc", blocks, incoming_weight, precision=HIGH) + incoming_bias


def upsample(value_arrays, incoming_weight, incoming_bias):
    result = jnp.einsum("ijk,abkc->iajbc", value_arrays, incoming_weight, precision=HIGH)
    extent = result.shape
    return result.reshape(extent[0] * 2, extent[2] * 2, extent[4]) + incoming_bias


def flatten_all(pieces):
    return jnp.concatenate([piece.reshape(-1) for piece in pieces])


def unflatten_all(flat, templates):
    pieces = []
    offset_at = 0
    for template in templates:
        count_here = template.size
        pieces.append(flat[offset_at : offset_at + count_here].reshape(template.shape))
        offset_at += count_here
    return tuple(pieces)


def strips_body(
    frames,
    counts,
    cell_mask,
    step_index,
    lift_weight,
    lift_bias,
    enc_norm1_gain,
    enc_norm1_bias,
    enc_conv1,
    enc_step_table,
    enc_norm2_gain,
    enc_norm2_bias,
    enc_conv2,
    enc_conv2_bias,
    reducer_weight,
    reducer_bias,
    up_weight,
    up_bias,
    dec_norm1_gain,
    dec_norm1_bias,
    dec_conv1,
    dec_step_table,
    dec_norm2_gain,
    dec_norm2_bias,
    dec_conv2,
    dec_conv2_bias,
    skip_weight,
    skip_bias,
    cotangent,
):
    enc_weights = (
        enc_norm1_gain,
        enc_norm1_bias,
        enc_conv1,
        enc_norm2_gain,
        enc_norm2_bias,
        enc_conv2,
        enc_conv2_bias,
    )
    dec_weights = (
        dec_norm1_gain,
        dec_norm1_bias,
        dec_conv1,
        dec_norm2_gain,
        dec_norm2_bias,
        dec_conv2,
        dec_conv2_bias,
    )
    params = (
        lift_weight,
        lift_bias,
        enc_norm1_gain,
        enc_norm1_bias,
        enc_conv1,
        enc_step_table,
        enc_norm2_gain,
        enc_norm2_bias,
        enc_conv2,
        enc_conv2_bias,
        reducer_weight,
        reducer_bias,
        up_weight,
        up_bias,
        dec_norm1_gain,
        dec_norm1_bias,
        dec_conv1,
        dec_step_table,
        dec_norm2_gain,
        dec_norm2_bias,
        dec_conv2,
        dec_conv2_bias,
        skip_weight,
        skip_bias,
    )

    def forward_micro(carry, sliced):
        frames_item, mask_item, count_item, step_item = sliced
        lifted = project_in(frames_item, mask_item, count_item, lift_weight, lift_bias)
        enc_scale, enc_shift, unused_hot = conditioning(step_item, enc_step_table)
        enc_branch, enc_kept = block_forward(lifted, enc_weights, enc_scale, enc_shift)
        encoder_result = lifted + enc_branch
        coarse_field = coarsen_field(encoder_result, reducer_weight, reducer_bias)
        foreign = from_behind(coarse_field, "section", 1)
        raised_foreign = upsample(foreign, up_weight, up_bias)
        raised = from_behind(raised_foreign, "section", 1)
        joined = jnp.concatenate([raised, encoder_result], axis=-1)
        dec_scale, dec_shift, unused_again = conditioning(step_item, dec_step_table)
        dec_branch, dec_kept = block_forward(joined, dec_weights, dec_scale, dec_shift)
        output_item = jnp.dot(joined, skip_weight, precision=HIGH) + skip_bias + dec_branch
        return (carry, (output_item, (lifted, enc_kept, encoder_result, foreign, joined, dec_kept)))

    unused, (output, kept_all) = lax.scan(
        forward_micro, jnp.zeros((), jnp.float32), (frames, cell_mask, counts, step_index)
    )

    def backward_micro(totals, sliced):
        frames_item, mask_item, count_item, step_item, grad_out, kept = sliced
        lifted, enc_kept, encoder_result, foreign, joined, dec_kept = kept
        dec_scale, dec_shift, one_hot = conditioning(step_item, dec_step_table)
        grad_joined, dec_grads, dec_gscale, dec_gshift = block_backward(
            joined, dec_weights, dec_scale, dec_shift, dec_kept, grad_out
        )
        grad_skip_weight = jnp.einsum("hwk,hwc->kc", joined, grad_out, precision=HIGH)
        grad_skip_bias = jnp.sum(grad_out, axis=(0, 1))
        grad_joined = grad_joined + jnp.dot(grad_out, skip_weight.T, precision=HIGH)
        half_width = joined.shape[-1] // 2
        grad_raised = grad_joined[..., :half_width]
        grad_encoded = grad_joined[..., half_width:]
        grad_foreign_up = from_behind(grad_raised, "section", 1)
        up_pull = jax.vjp(upsample, foreign, up_weight, up_bias)[1](grad_foreign_up)
        coarse_gradient = from_behind(up_pull[0], "section", 1)
        reducer_pullback = jax.vjp(coarsen_field, encoder_result, reducer_weight, reducer_bias)[1](
            coarse_gradient
        )
        grad_encoded = grad_encoded + reducer_pullback[0]
        enc_scale, enc_shift, enc_hot = conditioning(step_item, enc_step_table)
        grad_lifted, enc_grads, enc_gscale, enc_gshift = block_backward(
            lifted, enc_weights, enc_scale, enc_shift, enc_kept, grad_encoded
        )
        grad_lifted = grad_lifted + grad_encoded
        proj_pull = jax.vjp(
            lambda frames_in, incoming_weight, incoming_bias: project_in(
                frames_in, mask_item, count_item, incoming_weight, incoming_bias
            ),
            frames_item,
            lift_weight,
            lift_bias,
        )[1](grad_lifted)
        enc_table_grad = enc_hot[:, None] * jnp.concatenate([enc_gscale, enc_gshift])[None, :]
        dec_table_grad = one_hot[:, None] * jnp.concatenate([dec_gscale, dec_gshift])[None, :]
        micro_list = (
            proj_pull[1],
            proj_pull[2],
            enc_grads[0],
            enc_grads[1],
            enc_grads[2],
            enc_table_grad,
            enc_grads[3],
            enc_grads[4],
            enc_grads[5],
            enc_grads[6],
            reducer_pullback[1],
            reducer_pullback[2],
            up_pull[1],
            up_pull[2],
            dec_grads[0],
            dec_grads[1],
            dec_grads[2],
            dec_table_grad,
            dec_grads[3],
            dec_grads[4],
            dec_grads[5],
            dec_grads[6],
            grad_skip_weight,
            grad_skip_bias,
        )
        micro_flat = flatten_all(micro_list)
        return (totals + micro_flat, proj_pull[0])

    total_size = sum((piece.size for piece in params))
    start_totals = jnp.zeros((total_size,), jnp.float32)
    flat_totals, frames_grad = lax.scan(
        backward_micro,
        start_totals,
        (frames, cell_mask, counts, step_index, cotangent, kept_all),
        reverse=True,
    )
    flat_totals = lax.psum(flat_totals, ("section", "batch", "rows"))
    grads = unflatten_all(flat_totals, params)
    return (output, frames_grad) + grads


F32 = jnp.float32
BF16 = jnp.bfloat16
MESH = pl.DeviceIdType.MESH
NN = ((1,), (0,))
NT = ((1,), (1,))
TN = ((0,), (0,))
HIGH_AT = (0, 2, 1)
LOW_AT = (4, 3, 5)
CHUNK = 256
class Given(NamedTuple):
    frames: Any
    counts: Any
    cell_mask: Any
    step_index: Any
    lift_weight: Any
    lift_bias: Any
    enc_norm1_gain: Any
    enc_norm1_bias: Any
    enc_conv1: Any
    enc_step_table: Any
    enc_norm2_gain: Any
    enc_norm2_bias: Any
    enc_conv2: Any
    enc_conv2_bias: Any
    reducer_weight: Any
    reducer_bias: Any
    up_weight: Any
    up_bias: Any
    dec_norm1_gain: Any
    dec_norm1_bias: Any
    dec_conv1: Any
    dec_step_table: Any
    dec_norm2_gain: Any
    dec_norm2_bias: Any
    dec_conv2: Any
    dec_conv2_bias: Any
    skip_weight: Any
    skip_bias: Any
    cotangent: Any


ARGUMENTS = Given._fields
LARGE = tuple(dict(
    dec_conv2=0,
    skip_weight=0,
    dec_conv1=0,
    up_weight=0,
    reducer_weight=0,
    enc_conv2=0,
    enc_conv1=0,
))
IN_HBM = tuple(dict(frames=0, cell_mask=0, cotangent=0)) + LARGE
IN_SMEM = tuple(dict(counts=0, step_index=0))
SMALL_ROWS = dict(
    lift_weight=(0, 12),
    lift_bias=(12, 1),
    enc_norm1_gain=(16, 1),
    enc_norm1_bias=(17, 1),
    enc_norm2_gain=(18, 1),
    enc_norm2_bias=(19, 1),
    enc_conv2_bias=(20, 1),
    reducer_bias=(21, 1),
    up_bias=(22, 1),
    dec_conv2_bias=(23, 1),
    skip_bias=(23, 1),
    dec_norm1_gain=(24, 2),
    dec_norm1_bias=(26, 2),
    dec_norm2_gain=(28, 1),
    dec_norm2_bias=(29, 1),
    enc_step_table=(32, 8),
    dec_step_table=(40, 8),
)
SMALL_COUNT = 64
OUTPUTS = tuple(dict(output=0, frames_grad=0)) + LARGE + tuple(SMALL_ROWS)


def split(value):
    high = value.astype(BF16)
    return high, (value - high.astype(F32)).astype(BF16)


def dot(left, right, dims=NN, precision=None):
    return lax.dot_general(
        left, right, (dims, ((), ())), precision=precision, preferred_element_type=F32
    )


def fold(value):
    half = value.shape[1] // 2
    return value[:, :half] + value[:, half:]


def fold_rows(value):
    half = value.shape[0] // 2
    return value[:half] + value[half:]


def tile_sums(value):
    return jnp.sum(value.reshape(-1, 8, value.shape[-1]), axis=0)


def column_sum(tiles):
    return jnp.sum(tiles, axis=0, keepdims=True)


def group_ones(channels, size):
    rows = lax.broadcasted_iota(jnp.int32, (channels, channels), 0) // size
    columns = lax.broadcasted_iota(jnp.int32, (channels, channels), 1) // size
    return (rows == columns).astype(F32)


def group_sums(first, second, ones):
    both = dot(jnp.concatenate([first, second], axis=0), ones, precision=HIGH)
    return column_sum(both[:8]), column_sum(both[8:])


class Exchange:

    def __init__(self, place, start, rows, landing, first_sem):
        self.place, self.start, self.rows, self.landing = place, start, rows, landing
        self.sem = first_sem
        self.stage = 0
        self.copies = []
        line = place.line
        self.at = [start]
        size = rows
        for bit in (place.core, place.first, place.second):
            size //= 2
            self.at.append(self.at[-1] + bit * size)
        self.shard = size // line
        self.at.append(self.at[-1] + place.row * self.shard)

    def count(self):
        return 6 + 2 * (self.place.line - 1)

    def _copy(self, source, target, device):
        place = self.place
        copy = pltpu.make_async_remote_copy(
            src_ref=source,
            dst_ref=target,
            send_sem=place.send.at[self.sem],
            recv_sem=place.recv.at[self.sem],
            device_id=device,
            device_id_type=MESH,
        )
        self.sem += 1
        copy.start()
        self.copies.append(copy)
        return copy

    def _halve(self, level):
        place = self.place
        size = self.rows >> (level + 1)
        bit = (place.core, place.first, place.second)[level]
        other = pl.multiple_of(self.at[level] + (1 - bit) * size, 8)
        self.land = self.landing
        self.landing += size
        self.waiting = [
            self._copy(
                place.sums.at[pl.ds(other, size)],
                place.landing.at[pl.ds(self.land, size)],
                place.partners[level],
            )
        ]

    def _add(self, level):
        place = self.place
        size = self.rows >> (level + 1)
        block = 128 >> level
        sums, landing = place.sums, place.landing
        base = self.at[level + 1]
        land = self.land

        def step(i, carry):
            here = pl.ds(pl.multiple_of(base + i * block, 8), block)
            there = pl.ds(pl.multiple_of(land + i * block, 8), block)
            sums[here] = sums[here] + landing[there]
            return carry

        lax.fori_loop(0, size // block, step, 0)

    def _wait(self):
        for copy in self.waiting:
            copy.wait_recv()

    def _spread(self, level):
        place = self.place
        size = self.rows >> (level + 1)
        here = pl.ds(pl.multiple_of(self.at[level + 1], 8), size)
        self.waiting = [
            self._copy(
                place.final.at[here], place.final.at[here], place.partners[level]
            )
        ]

    def advance(self):
        place = self.place
        line, row = place.line, place.row
        shard = self.shard
        stage = self.stage
        self.stage += 1
        if stage == 0:
            self._halve(0)
        elif stage in (1, 2):
            self._wait()
            self._add(stage - 1)
            self._halve(stage)
        elif stage == 3:
            self._wait()
            self._add(2)
            self.waiting = []
            self.land = self.landing
            for k in range(1, line):
                to = lax.rem(row + k, line)
                source = pl.ds(pl.multiple_of(self.at[3] + to * shard, 8), shard)
                target = pl.ds(self.landing, shard)
                self.landing += shard
                self.waiting.append(
                    self._copy(
                        place.sums.at[source],
                        place.landing.at[target],
                        place.device_at(to),
                    )
                )
        elif stage == 4:
            self._wait()
            here = pl.ds(pl.multiple_of(self.at[4], 8), shard)
            total = place.sums[here]
            for k in range(line - 1):
                total = total + place.landing[pl.ds(self.land + k * shard, shard)]
            place.final[here] = total
            self.waiting = []
            for k in range(1, line):
                self.waiting.append(
                    self._copy(
                        place.final.at[here],
                        place.final.at[here],
                        place.device_at(lax.rem(row + k, line)),
                    )
                )
        elif stage in (5, 6, 7):
            self._wait()
            self._spread(7 - stage)
        else:
            self._wait()

    def done(self):
        return self.stage > 8


def layout_of(shapes):
    starts = {}
    at = 0
    for name in LARGE:
        starts[name] = at
        at += shapes[name][0]
    small = at
    unit = 256
    total = -(-(at + SMALL_COUNT) // unit) * unit
    begins = SimpleNamespace(**starts)
    ready = (
        begins.dec_conv1,
        begins.up_weight,
        begins.enc_conv2,
        begins.enc_conv1,
    )
    edges = [0] + [edge // unit * unit for edge in ready] + [total]
    runs = [(a, b - a) for a, b in zip(edges[:-1], edges[1:])]
    return starts, small, total, runs


def item_kernel(sizes, scratch_names, *refs):
    line, strip, width, shapes, big_layout = sizes
    begins, small_at, total_rows, runs = big_layout
    starts = SimpleNamespace(**begins)
    inputs = Given(*refs[: len(ARGUMENTS)])
    refs = refs[len(ARGUMENTS) :]
    output_names = OUTPUTS
    outputs = SimpleNamespace(**dict(zip(output_names, refs)))
    scratch = SimpleNamespace(**dict(zip(scratch_names, refs[len(output_names) :])))

    def w_of(name):
        return getattr(scratch, name)

    height = strip * line
    cells = height * width
    c = inputs.lift_weight.shape[1]
    strip_cells = strip * width
    history = inputs.frames.shape[1]

    core = lax.axis_index("section")
    plane = lax.axis_index("batch")
    row = lax.axis_index("rows")
    y, x = plane // 2, lax.rem(plane, 2)
    along_x = plane + 1 - 2 * x
    along_y = plane + 2 - 4 * y
    place = SimpleNamespace(
        line=line,
        row=row,
        core=core,
        first=x * (1 - core) + y * core,
        second=y * (1 - core) + x * core,
        partners=(
            (1 - core, plane, row),
            (core, along_x * (1 - core) + along_y * core, row),
            (core, along_y * (1 - core) + along_x * core, row),
        ),
        device_at=lambda to: (core, plane, to),
        sums=scratch.sums,
        final=scratch.final,
        landing=scratch.landing,
        send=scratch.send,
        recv=scratch.recv,
    )
    local_sem = scratch.local

    weight_copies = {}
    for k, name in enumerate(LARGE):
        copy = pltpu.make_async_copy(getattr(inputs, name), w_of(name), local_sem.at[k])
        weight_copies[name] = copy
        copy.start()
    frames_in, mask_in, cot = scratch.frames_in, scratch.mask_in, scratch.cot
    here_rows = pl.ds(pl.multiple_of(row * strip_cells, strip_cells), strip_cells)
    own = (
        pltpu.make_async_copy(inputs.frames.at[row], frames_in.at[row], local_sem.at[7]),
        pltpu.make_async_copy(inputs.cell_mask.at[row], mask_in.at[row], local_sem.at[8]),
        pltpu.make_async_copy(
            inputs.cotangent.at[row], cot.at[here_rows], local_sem.at[9]
        ),
    )
    for copy in own:
        copy.start()

    barrier = pltpu.get_barrier_semaphore()
    peers = [place.device_at(lax.rem(row + k, line)) for k in range(1, line)]
    for device in tuple(peers) + place.partners:
        pl.semaphore_signal(barrier, inc=1, device_id=device, device_id_type=MESH)
    pl.semaphore_wait(barrier, len(peers) + 3)

    next_sem = 0

    def send(source, target, device):
        nonlocal next_sem
        copy = pltpu.make_async_remote_copy(
            src_ref=source,
            dst_ref=target,
            send_sem=scratch.send.at[next_sem],
            recv_sem=scratch.recv.at[next_sem],
            device_id=device,
            device_id_type=MESH,
        )
        next_sem += 1
        copy.start()
        return copy

    frame_copies, cot_copies, output_copies = [], [], []
    for k in range(1, line):
        to = lax.rem(row + k, line)
        device = place.device_at(to)
        frame_copies.append(send(inputs.frames.at[to], frames_in.at[row], device))
        frame_copies.append(send(inputs.cell_mask.at[to], mask_in.at[row], device))
    for k in range(1, line):
        to = lax.rem(row + k, line)
        cot_copies.append(
            send(inputs.cotangent.at[to], cot.at[here_rows], place.device_at(to))
        )

    copied = SimpleNamespace(**weight_copies)
    def stack_conv(source, half, depth, forward, backward):
        for a in range(3):
            for b in range(3):
                at = (3 * a + b) * depth + half * c
                high, low = split(source[at : at + c, :])
                for block in (HIGH_AT[b], LOW_AT[b]):
                    rows = slice(block * c, (block + 1) * c)
                    forward[a, rows, 0:c] = high
                    forward[a, rows, c : 2 * c] = low
                for block in (HIGH_AT[2 - b], LOW_AT[2 - b]):
                    columns = slice(block * c, (block + 1) * c)
                    backward[2 - a, 0:c, columns] = high
                    backward[2 - a, c : 2 * c, columns] = low

    copied.enc_conv1.wait()
    stack_conv(scratch.enc_conv1, 0, c, scratch.fe1, scratch.be1)
    copied.enc_conv2.wait()
    stack_conv(scratch.enc_conv2, 0, c, scratch.fe2, scratch.be2)
    copied.reducer_weight.wait()
    for k in range(4):
        high, low = split(scratch.reducer_weight[k * c : (k + 1) * c, :])
        for block in (k, k + 4):
            scratch.f_down[block * c : (block + 1) * c, 0:c] = high
            scratch.f_down[block * c : (block + 1) * c, c : 2 * c] = low
        for block in (0, 1):
            columns = slice(block * c, (block + 1) * c)
            scratch.b_down[k, 0:c, columns] = high
            scratch.b_down[k, c : 2 * c, columns] = low
    copied.up_weight.wait()
    for k in range(4):
        high, low = split(scratch.up_weight[k * c : (k + 1) * c, :])
        for block in (0, 1):
            rows = slice(block * c, (block + 1) * c)
            scratch.f_up[k, rows, 0:c] = high
            scratch.f_up[k, rows, c : 2 * c] = low
        for block in (k, k + 4):
            columns = slice(block * c, (block + 1) * c)
            scratch.b_up[0:c, columns] = high
            scratch.b_up[c : 2 * c, columns] = low
    copied.dec_conv1.wait()
    stack_conv(scratch.dec_conv1, 0, 2 * c, scratch.fd1a, scratch.bd1a)
    stack_conv(scratch.dec_conv1, 1, 2 * c, scratch.fd1b, scratch.bd1b)
    copied.dec_conv2.wait()
    stack_conv(scratch.dec_conv2, 0, c, scratch.fd2, scratch.bd2)
    copied.skip_weight.wait()
    for half in range(2):
        high, low = split(scratch.skip_weight[half * c : (half + 1) * c, :])
        for block in (half, half + 2):
            scratch.f_skip[block * c : (block + 1) * c, 0:c] = high
            scratch.f_skip[block * c : (block + 1) * c, c : 2 * c] = low
        for block in (0, 1):
            columns = slice(block * c, (block + 1) * c)
            scratch.b_skip[half, 0:c, columns] = high
            scratch.b_skip[half, c : 2 * c, columns] = low

    for buffer in (scratch.xe1, scratch.xe2, scratch.xd1a, scratch.xd1b, scratch.xd2, scratch.xg):
        edge = jnp.zeros((width, 6 * c), BF16)
        buffer[0:width, :] = edge
        buffer[cells + width : cells + 2 * width, :] = edge

    lift = scratch.lift
    lift[...] = jnp.zeros(lift.shape, F32)
    lift[0:history, :] = inputs.lift_weight[...]
    lift[history : history + 1, :] = inputs.lift_bias[...]

    column = lax.broadcasted_iota(jnp.int32, (width, c), 0)
    at_first, at_last = column == 0, column == width - 1
    zeros8 = jnp.zeros((8, c), F32)
    ones16 = group_ones(c, c // GROUPS)
    ones32 = group_ones(c, 2 * c // GROUPS)
    count16 = float(cells * (c // GROUPS))
    count32 = float(cells * (2 * c // GROUPS))

    def grid_rows(step, carry=0):
        return lax.fori_loop(0, height, step, carry)

    def row_at(h):
        return pl.ds(pl.multiple_of(h * width, width), width)

    def chunk_at(i):
        return pl.ds(pl.multiple_of(i * CHUNK, CHUNK), CHUNK)

    def put_row(target, h, value):
        rows = pl.ds(pl.multiple_of((h + 1) * width, width), width)
        left = jnp.where(at_first, 0.0, pltpu.roll(value, 1, 0))
        right = jnp.where(at_last, 0.0, pltpu.roll(value, width - 1, 0))
        for b, piece in enumerate((left, value, right)):
            high, low = split(piece)
            target[rows, HIGH_AT[b] * c : (HIGH_AT[b] + 1) * c] = high
            target[rows, LOW_AT[b] * c : (LOW_AT[b] + 1) * c] = low

    def conv_chunk(pairs, i, dims=NN):
        total = None
        for data, weight in pairs:
            for a in range(3):
                rows = pl.ds(pl.multiple_of(i * CHUNK + a * width, width), CHUNK)
                part = dot(data[rows, :], weight[a], dims)
                total = part if total is None else total + part
        return total

    def norm_of(first, second, ones, count):
        one, two = group_sums(first, second, ones)
        mean = one / count
        return mean, lax.rsqrt(two / count - mean * mean + EPS)

    def activate(source, target, slope, scale, shift):
        def step(h, carry):
            value = source[row_at(h), :] * scale + shift
            below = 0.5 + 0.5 * lax.erf(value * 0.7071067811865476)
            slope[row_at(h), :] = below + value * (
                0.3989422804014327 * jnp.exp(-0.5 * value * value)
            )
            put_row(target, h, value * below)
            return carry

        grid_rows(step)

    def conv_norm(pairs, target):
        def step(i, carry):
            value = fold(conv_chunk(pairs, i))
            target[chunk_at(i), :] = value
            return carry[0] + tile_sums(value), carry[1] + tile_sums(value * value)

        return lax.fori_loop(0, cells // CHUNK, step, (zeros8, zeros8))

    def sums_of(source):
        def step(h, carry):
            value = source[row_at(h), :]
            return carry[0] + tile_sums(value), carry[1] + tile_sums(value * value)

        return grid_rows(step, (zeros8, zeros8))

    step_here = jnp.full((1, c), inputs.step_index[row], jnp.int32)

    def condition(table):
        total = jnp.zeros((1, 2 * c), F32)
        chosen = jnp.concatenate([step_here, step_here], axis=1)
        for s in range(table.shape[0]):
            total = total + jnp.where(chosen == s, table[s : s + 1, :], 0.0)
        return total[:, :c], total[:, c:]

    for copy in own[:2]:
        copy.wait()
    for copy in frame_copies:
        copy.wait_recv()
    fields = scratch.fields
    fields[...] = jnp.zeros(fields.shape, F32)
    frame_of = lax.broadcasted_iota(jnp.int32, (history, width), 0) // FIELDS
    keep = (frame_of >= HIST - inputs.counts[row]).astype(F32)
    masks = []
    for source in range(line):
        for k in range(strip):
            columns = slice((source * strip + k) * width, (source * strip + k + 1) * width)
            mask = mask_in[source, k : k + 1, :].astype(F32)
            masks.append(mask)
            fields[0:history, columns] = frames_in[source, :, k, :] * keep * mask
            fields[history : history + 1, columns] = mask
    lifted = scratch.lifted
    lifted[...] = dot(fields[...], lift[...], TN, HIGH)

    enc_scale, enc_shift = condition(inputs.enc_step_table)
    dec_scale, dec_shift = condition(inputs.dec_step_table)

    mean_e1, inv_e1 = norm_of(*sums_of(lifted), ones16, count16)
    gain_e1, bias_e1 = inputs.enc_norm1_gain[...], inputs.enc_norm1_bias[...]
    a_e1 = inv_e1 * gain_e1
    activate(lifted, scratch.xe1, scratch.slope_e1, a_e1, bias_e1 - mean_e1 * a_e1)
    middle_e = scratch.middle_e
    mean_e2, inv_e2 = norm_of(
        *conv_norm([(scratch.xe1, scratch.fe1)], middle_e), ones16, count16
    )
    gain_e2, bias_e2 = inputs.enc_norm2_gain[...], inputs.enc_norm2_bias[...]
    a_e2 = inv_e2 * gain_e2
    activate(
        middle_e,
        scratch.xe2,
        scratch.slope_e2,
        a_e2 * (1.0 + enc_scale),
        (bias_e2 - mean_e2 * a_e2) * (1.0 + enc_scale) + enc_shift,
    )
    encoded = scratch.encoded
    conv2_bias = inputs.enc_conv2_bias[...]
    joined = scratch.joined

    def encode(i, carry):
        value = fold(conv_chunk([(scratch.xe2, scratch.fe2)], i))
        value = value + conv2_bias + lifted[chunk_at(i), :]
        encoded[chunk_at(i), :] = value
        high, low = split(value)
        joined[chunk_at(i), c : 2 * c] = high
        joined[chunk_at(i), 3 * c : 4 * c] = low
        return carry[0] + tile_sums(value), carry[1] + tile_sums(value * value)

    sums_enc = lax.fori_loop(0, cells // CHUNK, encode, (zeros8, zeros8))

    half_cells, quarter = cells // 2, cells // 4

    def pick(source):
        pieces = []
        for b in range(2):
            value = source[pl.ds(b, half_cells, stride=2), :]
            value = value.reshape(height // 2, 2, width // 2, c)
            pieces.append([value[:, a].reshape(quarter, c) for a in range(2)])
        return [pieces[b][a] for a in range(2) for b in range(2)]

    def place_cells(target, pieces):
        for b in range(2):
            both = [pieces[2 * a + b].reshape(height // 2, 1, width // 2, c) for a in range(2)]
            value = jnp.concatenate(both, axis=1).reshape(half_cells, c)
            target[pl.ds(b, half_cells, stride=2), :] = value

    x_down = scratch.x_down
    for k, piece in enumerate(pick(encoded)):
        high, low = split(piece)
        x_down[:, k * c : (k + 1) * c] = high
        x_down[:, (k + 4) * c : (k + 5) * c] = low
    lowered = fold(dot(x_down[...], scratch.f_down[...])) + inputs.reducer_bias[...]
    x_up = scratch.x_up
    high, low = split(lowered)
    x_up[:, 0:c] = high
    x_up[:, c : 2 * c] = low
    raised = scratch.raised
    up_bias = inputs.up_bias[...]
    place_cells(
        raised, [fold(dot(x_up[...], scratch.f_up[k])) + up_bias for k in range(4)]
    )

    def raise_row(h, carry):
        value = raised[row_at(h), :]
        high, low = split(value)
        joined[row_at(h), 0:c] = high
        joined[row_at(h), 2 * c : 3 * c] = low
        return carry[0] + tile_sums(value), carry[1] + tile_sums(value * value)

    sums_raised = grid_rows(raise_row, (zeros8, zeros8))

    halves = []
    for half, (source, sums) in enumerate(((raised, sums_raised), (encoded, sums_enc))):
        mean, inv = norm_of(*sums, ones32, count32)
        gain = inputs.dec_norm1_gain[half : half + 1, :]
        bias = inputs.dec_norm1_bias[half : half + 1, :]
        scale = inv * gain
        activate(
            source,
            (scratch.xd1a, scratch.xd1b)[half],
            (scratch.slope_d1a, scratch.slope_d1b)[half],
            scale,
            bias - mean * scale,
        )
        halves.append((source, mean, inv, gain))
    middle_d = scratch.middle_d
    pairs = [(scratch.xd1a, scratch.fd1a), (scratch.xd1b, scratch.fd1b)]
    mean_d2, inv_d2 = norm_of(*conv_norm(pairs, middle_d), ones16, count16)
    gain_d2, bias_d2 = inputs.dec_norm2_gain[...], inputs.dec_norm2_bias[...]
    a_d2 = inv_d2 * gain_d2
    activate(
        middle_d,
        scratch.xd2,
        scratch.slope_d2,
        a_d2 * (1.0 + dec_scale),
        (bias_d2 - mean_d2 * a_d2) * (1.0 + dec_scale) + dec_shift,
    )
    result = scratch.result
    last_bias = inputs.dec_conv2_bias[...] + inputs.skip_bias[...]

    def decode(i, carry):
        value = conv_chunk([(scratch.xd2, scratch.fd2)], i)
        value = value + dot(joined[chunk_at(i), :], scratch.f_skip[...])
        result[chunk_at(i), :] = fold(value) + last_bias
        return carry

    lax.fori_loop(0, cells // CHUNK, decode, 0)
    own_output = pltpu.make_async_copy(
        result.at[here_rows], outputs.output.at[row], local_sem.at[10]
    )
    own_output.start()
    for k in range(1, line):
        to = lax.rem(row + k, line)
        there = pl.ds(pl.multiple_of(to * strip_cells, strip_cells), strip_cells)
        output_copies.append(
            send(result.at[there], outputs.output.at[row], place.device_at(to))
        )

    exchanges = []
    waiting_runs = list(runs)
    landing_at = 0
    sem_at = 4 * (line - 1) + 2 * (line - 1)
    sums, final = scratch.sums, scratch.final

    def begin():
        nonlocal landing_at, sem_at
        start, rows = waiting_runs.pop(0)
        exchange = Exchange(place, start, rows, landing_at, sem_at)
        landing_at += rows - rows // (8 * line)
        sem_at += exchange.count()
        exchanges.append(exchange)
        exchange.advance()

    written = []
    final_copies = []

    def publish():
        ready = 0
        for exchange in exchanges:
            if not exchange.done():
                break
            ready = exchange.start + exchange.rows
        for k, name in enumerate(LARGE):
            rows = shapes[name][0]
            if name not in written and begins[name] + rows <= ready:
                written.append(name)
                copy = pltpu.make_async_copy(
                    final.at[pl.ds(begins[name], rows)], getattr(outputs, name), local_sem.at[11 + k]
                )
                copy.start()
                final_copies.append(copy)

    def tick():
        for exchange in exchanges:
            if not exchange.done():
                exchange.advance()
        publish()

    def small_row(k, value):
        sums[small_at + k : small_at + k + 1, :] = value

    def spread_grad(source):
        def step(h, carry):
            value = source[row_at(h), :]
            put_row(scratch.xg, h, value)
            return carry + tile_sums(value)

        return grid_rows(step, zeros8)

    def weight_grad(data, at, depth):
        lhs = data[width : cells + width, :]
        for a in range(3):
            rows = pl.ds((2 - a) * width, cells)
            part = fold(dot(lhs, scratch.xg[rows, 2 * c : 4 * c], TN))
            for b in range(3):
                high, low = HIGH_AT[b] * c, LOW_AT[b] * c
                to = at + (3 * a + b) * depth
                sums[to : to + c, :] = part[high : high + c] + part[low : low + c]

    def back_conv(weight, slope, target, source, mean, inv):
        def step(i, carry):
            value = fold(conv_chunk([(scratch.xg, weight)], i, NT)) * slope[chunk_at(i), :]
            target[chunk_at(i), :] = value
            normed = (source[chunk_at(i), :] - mean) * inv
            return carry[0] + tile_sums(value), carry[1] + tile_sums(value * normed)

        return lax.fori_loop(0, cells // CHUNK, step, (zeros8, zeros8))

    def norm_grad(sums_in, scale, ones, count):
        one, two = group_sums(sums_in[0] * scale, sums_in[1] * scale, ones)
        return one / count, two / count

    own[2].wait()
    for copy in cot_copies:
        copy.wait_recv()
    total_cot = column_sum(spread_grad(cot))
    weight_grad(scratch.xd2, starts.dec_conv2, c)
    part = fold(dot(joined[...], scratch.xg[width : cells + width, 2 * c : 4 * c], TN))
    sums[starts.skip_weight : starts.skip_weight + 2 * c, :] = fold_rows(part)
    small_row(23, total_cot)
    begin()

    grad = scratch.grad
    sums_d2 = back_conv(scratch.bd2, scratch.slope_d2, grad, middle_d, mean_d2, inv_d2)
    side_grads = (scratch.grad_a, scratch.grad_b)
    for half in range(2):

        def skip_back(i, carry, half=half):
            rows = pl.ds(pl.multiple_of(i * CHUNK + width, width), CHUNK)
            value = dot(scratch.xg[rows, 2 * c : 4 * c], scratch.b_skip[half], NT)
            side_grads[half][chunk_at(i), :] = fold(value)
            return carry

        lax.fori_loop(0, cells // CHUNK, skip_back, 0)
    tick()

    def table_rows(k, sums_in, gain, bias, one_plus):
        plain, times = column_sum(sums_in[0]), column_sum(sums_in[1])
        for s in range(inputs.enc_step_table.shape[0]):
            small_row(k + 2 * s, jnp.where(step_here == s, gain * times + bias * plain, 0.0))
            small_row(k + 2 * s + 1, jnp.where(step_here == s, plain, 0.0))
        return one_plus * times, one_plus * plain

    def middle_grad(source, mean, inv, scale, sums_in):
        zero, slope = norm_grad(sums_in, scale, ones16, count16)

        def step(h, carry):
            normed = (source[row_at(h), :] - mean) * inv
            value = inv * (grad[row_at(h), :] * scale - zero - normed * slope)
            put_row(scratch.xg, h, value)
            return carry

        grid_rows(step)

    gain_row, bias_row = table_rows(40, sums_d2, gain_d2, bias_d2, 1.0 + dec_scale)
    small_row(28, gain_row)
    small_row(29, bias_row)
    middle_grad(middle_d, mean_d2, inv_d2, gain_d2 * (1.0 + dec_scale), sums_d2)
    weight_grad(scratch.xd1a, starts.dec_conv1, 2 * c)
    tick()
    weight_grad(scratch.xd1b, starts.dec_conv1 + c, 2 * c)
    begin()

    for half, (source, mean, inv, gain) in enumerate(halves):
        sums_in = back_conv(
            (scratch.bd1a, scratch.bd1b)[half],
            (scratch.slope_d1a, scratch.slope_d1b)[half],
            grad,
            source,
            mean,
            inv,
        )
        small_row(24 + half, column_sum(sums_in[1]))
        small_row(26 + half, column_sum(sums_in[0]))
        zero, slope = norm_grad(sums_in, gain, ones32, count32)
        target = side_grads[half]

        def input_grad(h, carry):
            normed = (source[row_at(h), :] - mean) * inv
            value = inv * (grad[row_at(h), :] * gain - zero - normed * slope)
            value = target[row_at(h), :] + value
            target[row_at(h), :] = value
            return carry + tile_sums(value)

        total = grid_rows(input_grad, zeros8)
        if half == 0:
            small_row(22, column_sum(total))
        tick()

    grad_raised, grad_encoded = side_grads
    x_grad_up = scratch.x_grad_up
    for k, piece in enumerate(pick(grad_raised)):
        high, low = split(piece)
        x_grad_up[:, k * c : (k + 1) * c] = high
        x_grad_up[:, (k + 4) * c : (k + 5) * c] = low
    grad_lowered = fold(dot(x_grad_up[...], scratch.b_up[...], NT))
    small_row(21, jnp.sum(grad_lowered, axis=0, keepdims=True))
    x_grad_low = scratch.x_grad_low
    high, low = split(grad_lowered)
    x_grad_low[:, 0:c] = high
    x_grad_low[:, c : 2 * c] = low
    part = fold(fold_rows(dot(x_up[...], x_grad_up[...], TN)))
    for k in range(4):
        at = starts.up_weight + k * c
        sums[at : at + c, :] = part[:, k * c : (k + 1) * c]
    part = fold_rows(fold(dot(x_down[...], x_grad_low[...], TN)))
    sums[starts.reducer_weight : starts.reducer_weight + 4 * c, :] = part
    begin()
    place_cells(
        grad, [fold(dot(x_grad_low[...], scratch.b_down[k], NT)) for k in range(4)]
    )

    def join_row(h, carry):
        value = grad_encoded[row_at(h), :] + grad[row_at(h), :]
        grad_encoded[row_at(h), :] = value
        put_row(scratch.xg, h, value)
        return carry + tile_sums(value)

    small_row(20, column_sum(grid_rows(join_row, zeros8)))
    tick()
    weight_grad(scratch.xe2, starts.enc_conv2, c)
    begin()
    sums_e2 = back_conv(scratch.be2, scratch.slope_e2, grad, middle_e, mean_e2, inv_e2)
    gain_row, bias_row = table_rows(32, sums_e2, gain_e2, bias_e2, 1.0 + enc_scale)
    small_row(18, gain_row)
    small_row(19, bias_row)
    middle_grad(middle_e, mean_e2, inv_e2, gain_e2 * (1.0 + enc_scale), sums_e2)
    tick()
    weight_grad(scratch.xe1, starts.enc_conv1, c)
    tick()
    sums_e1 = back_conv(scratch.be1, scratch.slope_e1, grad, lifted, mean_e1, inv_e1)
    small_row(16, column_sum(sums_e1[1]))
    small_row(17, column_sum(sums_e1[0]))
    zero, slope = norm_grad(sums_e1, gain_e1, ones16, count16)

    def lifted_grad(h, carry):
        normed = (lifted[row_at(h), :] - mean_e1) * inv_e1
        value = inv_e1 * (grad[row_at(h), :] * gain_e1 - zero - normed * slope)
        grad[row_at(h), :] = grad_encoded[row_at(h), :] + value
        return carry

    grid_rows(lifted_grad)
    tick()

    sums[small_at : small_at + 16, :] = dot(fields[...], grad[...], NN, HIGH)
    for k in (30, 31):
        small_row(k, jnp.zeros((1, c), F32))
    rest = small_at + 48
    sums[rest:total_rows, :] = jnp.zeros((total_rows - rest, c), F32)
    begin()
    back = dot(lift[...], grad[...], NT, HIGH)
    frames_out = scratch.frames_out
    for source in range(line):
        for k in range(strip):
            h = source * strip + k
            value = back[0:history, h * width : (h + 1) * width]
            frames_out[source, :, k, :] = value * keep * masks[h]
    own_frames = pltpu.make_async_copy(
        frames_out.at[row], outputs.frames_grad.at[row], local_sem.at[18]
    )
    own_frames.start()
    for k in range(1, line):
        to = lax.rem(row + k, line)
        output_copies.append(
            send(frames_out.at[to], outputs.frames_grad.at[row], place.device_at(to))
        )

    while not all(exchange.done() for exchange in exchanges):
        tick()

    for name, (k, rows) in SMALL_ROWS.items():
        at = small_at + k
        target = getattr(outputs, name)
        if rows == 8:
            for s in range(target.shape[0]):
                target[s : s + 1, 0:c] = final[at + 2 * s : at + 2 * s + 1, :]
                target[s : s + 1, c : 2 * c] = final[at + 2 * s + 1 : at + 2 * s + 2, :]
        else:
            target[...] = final[at : at + rows, :]

    for copy in output_copies:
        copy.wait_recv()
    own_output.wait()
    own_frames.wait()
    for copy in final_copies:
        copy.wait()
    for copy in frame_copies + cot_copies + output_copies:
        copy.wait_send()
    for exchange in exchanges:
        for copy in exchange.copies:
            copy.wait_send()


def whole_items(shape, *arguments):
    line = shape["rows"]
    whole = Given(*arguments)
    given = whole._asdict()
    frames, cotangent = whole.frames, whole.cotangent
    items, history, strip, width = frames.shape
    c = cotangent.shape[-1]
    cells = strip * line * width
    flat = {}
    for name, value in given.items():
        if value is cotangent:
            value = value.reshape(items, strip * width, c)
        elif name in LARGE:
            value = value.reshape(-1, c)
        elif value.ndim == 1 and name not in IN_SMEM:
            value = value.reshape(-1, c)
        flat[name] = value
    shapes = {name: flat[name].shape for name in LARGE}
    big_layout = layout_of(shapes)
    starts, small_at, total_rows, runs = big_layout
    copies = 6 * (line - 1) + len(runs) * (6 + 2 * (line - 1)) + line - 1
    landing = sum(rows - rows // (8 * line) for _, rows in runs)
    shifted = pltpu.VMEM((cells + 2 * width, 6 * c), BF16)
    forward = pltpu.VMEM((3, 6 * c, 2 * c), BF16)
    backward = pltpu.VMEM((3, 2 * c, 6 * c), BF16)
    field = pltpu.VMEM((cells, c), F32)
    quarter = cells // 4
    scratch = dict(
        send=pltpu.SemaphoreType.DMA((copies,)),
        recv=pltpu.SemaphoreType.DMA((copies,)),
        local=pltpu.SemaphoreType.DMA((19,)),
        sums=pltpu.VMEM((total_rows, c), F32),
        final=pltpu.VMEM((total_rows, c), F32),
        landing=pltpu.VMEM((landing, c), F32),
        frames_in=pltpu.VMEM((line, history, strip, width), F32),
        mask_in=pltpu.VMEM((line, strip, width), jnp.int32),
        frames_out=pltpu.VMEM((line, history, strip, width), F32),
        fields=pltpu.VMEM((16, cells), F32),
        lift=pltpu.VMEM((16, c), F32),
        joined=pltpu.VMEM((cells, 4 * c), BF16),
        x_down=pltpu.VMEM((quarter, 8 * c), BF16),
        x_grad_up=pltpu.VMEM((quarter, 8 * c), BF16),
        x_up=pltpu.VMEM((quarter, 2 * c), BF16),
        x_grad_low=pltpu.VMEM((quarter, 2 * c), BF16),
        f_down=pltpu.VMEM((8 * c, 2 * c), BF16),
        b_down=pltpu.VMEM((4, 2 * c, 2 * c), BF16),
        f_up=pltpu.VMEM((4, 2 * c, 2 * c), BF16),
        b_up=pltpu.VMEM((2 * c, 8 * c), BF16),
        f_skip=pltpu.VMEM((4 * c, 2 * c), BF16),
        b_skip=pltpu.VMEM((2, 2 * c, 2 * c), BF16),
        xe1=shifted,
        xe2=shifted,
        xd1a=shifted,
        xd1b=shifted,
        xd2=shifted,
        xg=shifted,
        fe1=forward,
        fe2=forward,
        fd1a=forward,
        fd1b=forward,
        fd2=forward,
        be1=backward,
        be2=backward,
        bd1a=backward,
        bd1b=backward,
        bd2=backward,
        slope_e1=field,
        slope_e2=field,
        slope_d1a=field,
        slope_d1b=field,
        slope_d2=field,
        lifted=field,
        middle_e=field,
        encoded=field,
        raised=field,
        middle_d=field,
        result=field,
        cot=field,
        grad=field,
        grad_a=field,
        grad_b=field,
    )
    scratch.update({name: pltpu.VMEM(shapes[name], F32) for name in LARGE})

    in_hbm = pl.BlockSpec(memory_space=pl.ANY)
    in_vmem = pl.BlockSpec(memory_space=pltpu.VMEM)
    in_smem = pl.BlockSpec(memory_space=pltpu.SMEM)
    in_specs = [
        in_hbm if name in IN_HBM else in_smem if name in IN_SMEM else in_vmem
        for name in ARGUMENTS
    ]
    out_shape = [
        jax.ShapeDtypeStruct((items, strip * width, c), F32),
        jax.ShapeDtypeStruct(frames.shape, F32),
    ]
    out_shape += [jax.ShapeDtypeStruct(shapes[name], F32) for name in LARGE]
    out_shape += [jax.ShapeDtypeStruct(flat[name].shape, F32) for name in SMALL_ROWS]
    out_specs = [in_hbm] * (2 + len(LARGE)) + [in_vmem] * len(SMALL_ROWS)
    results = pl.pallas_call(
        functools.partial(
            item_kernel,
            (line, strip, width, shapes, big_layout),
            tuple(scratch),
        ),
        out_shape=out_shape,
        in_specs=in_specs,
        out_specs=out_specs,
        scratch_shapes=list(scratch.values()),
        compiler_params=pltpu.CompilerParams(
            collective_id=0, has_side_effects=True, vmem_limit_bytes=62 * 1024 * 1024
        ),
    )(*[flat[name] for name in ARGUMENTS])
    output, frames_grad = results[:2]
    grads = dict(zip(OUTPUTS[2:], results[2:]))
    ordered = [name for name in ARGUMENTS if name in grads]
    return (output.reshape(cotangent.shape), frames_grad) + tuple(
        grads[name].reshape(given[name].shape) for name in ordered
    )


def body(shape, *arguments):
    items, _, strip, width = arguments[0].shape
    line = shape["rows"]
    whole = (
        shape["section"] == 2
        and shape["batch"] == 4
        and items == line
        and arguments[-1].shape[-1] == 128
        and (strip * line * width) % CHUNK == 0
    )
    return whole_items(shape, *arguments) if whole else strips_body(*arguments)


def solution(mesh):
    in_specs = (
        P(("section", "batch"), None, "rows", None),
        P(("section", "batch")),
        P(("section", "batch"), "rows", None),
        P(("section", "batch")),
        P(),
        P(),
        P(),
        P(),
        P(),
        P(),
        P(),
        P(),
        P(),
        P(),
        P(),
        P(),
        P(),
        P(),
        P(),
        P(),
        P(),
        P(),
        P(),
        P(),
        P(),
        P(),
        P(),
        P(),
        P(("section", "batch"), "rows", None, None),
    )
    out_specs = (
        P(("section", "batch"), "rows", None, None),
        P(("section", "batch"), None, "rows", None),
        P(),
        P(),
        P(),
        P(),
        P(),
        P(),
        P(),
        P(),
        P(),
        P(),
        P(),
        P(),
        P(),
        P(),
        P(),
        P(),
        P(),
        P(),
        P(),
        P(),
        P(),
        P(),
        P(),
        P(),
    )
    return jax.shard_map(functools.partial(body, mesh.shape), mesh=mesh, in_specs=in_specs, out_specs=out_specs, check_vma=False)
```

```python
import functools
from types import SimpleNamespace
from typing import Any, NamedTuple

import jax
import jax.numpy as jnp
from jax import lax
from jax.experimental import pallas as pl
from jax.experimental.pallas import tpu as pltpu
from jax.sharding import PartitionSpec as P

GROUPS = 8
FIELDS = 3
HIST = 4


EPS = 1e-05
HIGH = lax.Precision.HIGHEST


def extended(cells, sides, width):
    for axis, dim in sides:
        count = lax.axis_size(axis)
        ends = count - 1
        head = lax.slice_in_dim(cells, 0, width, axis=dim)
        tail = lax.slice_in_dim(cells, cells.shape[dim] - width, cells.shape[dim], axis=dim)
        cells = jnp.concatenate(
            [
                lax.ppermute(tail, axis, [(i, (i + 1) % count) for i in range(ends)]),
                cells,
                lax.ppermute(head, axis, [((i + 1) % count, i) for i in range(ends)]),
            ],
            axis=dim,
        )
    return cells


def from_behind(value, axis, steps):
    count = lax.axis_size(axis)
    pairs = [(source, (source + steps) % count) for source in range(count)]
    return lax.ppermute(value, axis, pairs)


def group_view(value_arrays):
    extent = value_arrays.shape
    return value_arrays.reshape(extent[:-1] + (GROUPS, extent[-1] // GROUPS))


def global_sums(value_arrays):
    grouped = group_view(value_arrays)
    flat = grouped.reshape(-1, GROUPS, grouped.shape[-1])
    first_sum = jnp.sum(flat, axis=(0, 2))
    second_sum = jnp.sum(flat * flat, axis=(0, 2))
    return lax.psum((first_sum, second_sum), "rows")


def apply_norm(value_arrays, sum_one, sum_two, norm_gain, norm_bias, total):
    grouped = group_view(value_arrays)
    group_mean = sum_one / total
    variance = sum_two / total - group_mean * group_mean
    inverse = lax.rsqrt(variance + EPS)
    normed = (grouped - group_mean[:, None]) * inverse[:, None]
    return normed.reshape(value_arrays.shape) * norm_gain + norm_bias


def norm_back(value_arrays, grad_one, grad_two):
    grouped = group_view(value_arrays)
    extra = grad_one[:, None] + 2.0 * grouped * grad_two[:, None]
    return extra.reshape(value_arrays.shape)


def reduce_grads(grad_one, grad_two):
    return lax.psum((grad_one, grad_two), "rows")


def conv_rows(padded, kernel):
    widened = jnp.pad(padded, ((0, 0), (1, 1), (0, 0)))
    return lax.conv_general_dilated(
        widened[None],
        kernel,
        (1, 1),
        "VALID",
        dimension_numbers=("NHWC", "HWIO", "NHWC"),
        precision=HIGH,
    )[0]


def flipped(kernel):
    return jnp.transpose(kernel[::-1, ::-1], (0, 1, 3, 2))


def pad_grads(value_arrays):
    return extended(value_arrays, (("rows", 0),), 1)


def totals_of(inputs, conv1):
    strip = inputs.shape[0]
    cells = strip * lax.axis_size("rows") * inputs.shape[1]
    return (cells * (inputs.shape[2] // GROUPS), cells * (conv1.shape[3] // GROUPS))


def block_forward(inputs, weights, scale_part, shift_part):
    norm1_gain, norm1_bias, conv1, norm2_gain, norm2_bias, conv2, conv2_bias = weights
    total_in, total_mid = totals_of(inputs, conv1)
    sums_in = global_sums(inputs)

    def pad_rows(value_arrays):
        return extended(value_arrays, (("rows", 0),), 1)

    act_one = pad_rows(
        jax.nn.gelu(
            apply_norm(inputs, sums_in[0], sums_in[1], norm1_gain, norm1_bias, total_in),
            approximate=False,
        )
    )
    middle = conv_rows(act_one, conv1)
    sums_mid = global_sums(middle)
    shaped = (
        apply_norm(middle, sums_mid[0], sums_mid[1], norm2_gain, norm2_bias, total_mid)
        * (1.0 + scale_part)
        + shift_part
    )
    act_two = pad_rows(jax.nn.gelu(shaped, approximate=False))
    branch = conv_rows(act_two, conv2) + conv2_bias
    return (branch, (sums_in[0], sums_in[1], act_one, middle, sums_mid[0], sums_mid[1], act_two))


def block_backward(inputs, weights, scale_part, shift_part, kept, grad_out):
    norm1_gain, norm1_bias, conv1, norm2_gain, norm2_bias, conv2, conv2_bias = weights
    in_one, in_two, act_one, middle, mid_one, mid_two, act_two = kept
    total_in, total_mid = totals_of(inputs, conv1)
    grad_conv2 = jax.vjp(lambda kernel: conv_rows(act_two, kernel), conv2)[1](grad_out)[0]
    grad_bias2 = jnp.sum(grad_out, axis=(0, 1))
    grad_act_two = conv_rows(pad_grads(grad_out), flipped(conv2))

    def second_piece(middle_in, sum_one, sum_two, gain_in, incoming_bias, scale_in, shift_in):
        shaped = (
            apply_norm(middle_in, sum_one, sum_two, gain_in, incoming_bias, total_mid)
            * (1.0 + scale_in)
            + shift_in
        )
        return jax.nn.gelu(shaped, approximate=False)

    second_pull = jax.vjp(
        second_piece, middle, mid_one, mid_two, norm2_gain, norm2_bias, scale_part, shift_part
    )[1](grad_act_two)
    summed_one, summed_two = reduce_grads(second_pull[1], second_pull[2])
    grad_middle = second_pull[0] + norm_back(middle, summed_one, summed_two)
    grad_conv1 = jax.vjp(lambda kernel: conv_rows(act_one, kernel), conv1)[1](grad_middle)[0]
    grad_act_one = conv_rows(pad_grads(grad_middle), flipped(conv1))

    def first_piece(inputs_in, sum_one, sum_two, gain_in, incoming_bias):
        return jax.nn.gelu(
            apply_norm(inputs_in, sum_one, sum_two, gain_in, incoming_bias, total_in),
            approximate=False,
        )

    first_pull = jax.vjp(first_piece, inputs, in_one, in_two, norm1_gain, norm1_bias)[1](
        grad_act_one
    )
    first_one, first_two = reduce_grads(first_pull[1], first_pull[2])
    grad_inputs = first_pull[0] + norm_back(inputs, first_one, first_two)
    grads = (
        first_pull[3],
        first_pull[4],
        grad_conv1,
        second_pull[3],
        second_pull[4],
        grad_conv2,
        grad_bias2,
    )
    return (grad_inputs, grads, second_pull[5], second_pull[6])


def conditioning(step_item, table):
    one_hot = (jnp.arange(table.shape[0], dtype=jnp.int32) == step_item).astype(jnp.float32)
    condition = jnp.dot(one_hot, table, precision=HIGH)
    half_width = table.shape[1] // 2
    return (condition[:half_width], condition[half_width:], one_hot)


def project_in(frames_item, mask_item, count_item, incoming_weight, incoming_bias):
    history = jnp.arange(HIST, dtype=jnp.int32) >= HIST - count_item
    keep = jnp.repeat(history, FIELDS).astype(jnp.float32)
    lifted = (
        jnp.einsum(
            "fhw,fc->hwc", frames_item * keep[:, None, None], incoming_weight, precision=HIGH
        )
        + incoming_bias
    )
    return lifted * mask_item[:, :, None].astype(jnp.float32)


def coarsen_field(value_arrays, incoming_weight, incoming_bias):
    rows_here, width_here, depth_here = value_arrays.shape
    blocks = value_arrays.reshape(rows_here // 2, 2, width_here // 2, 2, depth_here)
    return jnp.einsum("iajbk,abkc->ijc", blocks, incoming_weight, precision=HIGH) + incoming_bias


def upsample(value_arrays, incoming_weight, incoming_bias):
    result = jnp.einsum("ijk,abkc->iajbc", value_arrays, incoming_weight, precision=HIGH)
    extent = result.shape
    return result.reshape(extent[0] * 2, extent[2] * 2, extent[4]) + incoming_bias


def flatten_all(pieces):
    return jnp.concatenate([piece.reshape(-1) for piece in pieces])


def unflatten_all(flat, templates):
    pieces = []
    offset_at = 0
    for template in templates:
        count_here = template.size
        pieces.append(flat[offset_at : offset_at + count_here].reshape(template.shape))
        offset_at += count_here
    return tuple(pieces)


def strips_body(
    frames,
    counts,
    cell_mask,
    step_index,
    lift_weight,
    lift_bias,
    enc_norm1_gain,
    enc_norm1_bias,
    enc_conv1,
    enc_step_table,
    enc_norm2_gain,
    enc_norm2_bias,
    enc_conv2,
    enc_conv2_bias,
    reducer_weight,
    reducer_bias,
    up_weight,
    up_bias,
    dec_norm1_gain,
    dec_norm1_bias,
    dec_conv1,
    dec_step_table,
    dec_norm2_gain,
    dec_norm2_bias,
    dec_conv2,
    dec_conv2_bias,
    skip_weight,
    skip_bias,
    cotangent,
):
    enc_weights = (
        enc_norm1_gain,
        enc_norm1_bias,
        enc_conv1,
        enc_norm2_gain,
        enc_norm2_bias,
        enc_conv2,
        enc_conv2_bias,
    )
    dec_weights = (
        dec_norm1_gain,
        dec_norm1_bias,
        dec_conv1,
        dec_norm2_gain,
        dec_norm2_bias,
        dec_conv2,
        dec_conv2_bias,
    )
    params = (
        lift_weight,
        lift_bias,
        enc_norm1_gain,
        enc_norm1_bias,
        enc_conv1,
        enc_step_table,
        enc_norm2_gain,
        enc_norm2_bias,
        enc_conv2,
        enc_conv2_bias,
        reducer_weight,
        reducer_bias,
        up_weight,
        up_bias,
        dec_norm1_gain,
        dec_norm1_bias,
        dec_conv1,
        dec_step_table,
        dec_norm2_gain,
        dec_norm2_bias,
        dec_conv2,
        dec_conv2_bias,
        skip_weight,
        skip_bias,
    )

    def forward_micro(carry, sliced):
        frames_item, mask_item, count_item, step_item = sliced
        lifted = project_in(frames_item, mask_item, count_item, lift_weight, lift_bias)
        enc_scale, enc_shift, unused_hot = conditioning(step_item, enc_step_table)
        enc_branch, enc_kept = block_forward(lifted, enc_weights, enc_scale, enc_shift)
        encoder_result = lifted + enc_branch
        coarse_field = coarsen_field(encoder_result, reducer_weight, reducer_bias)
        foreign = from_behind(coarse_field, "section", 1)
        raised_foreign = upsample(foreign, up_weight, up_bias)
        raised = from_behind(raised_foreign, "section", 1)
        joined = jnp.concatenate([raised, encoder_result], axis=-1)
        dec_scale, dec_shift, unused_again = conditioning(step_item, dec_step_table)
        dec_branch, dec_kept = block_forward(joined, dec_weights, dec_scale, dec_shift)
        output_item = jnp.dot(joined, skip_weight, precision=HIGH) + skip_bias + dec_branch
        return (carry, (output_item, (lifted, enc_kept, encoder_result, foreign, joined, dec_kept)))

    unused, (output, kept_all) = lax.scan(
        forward_micro, jnp.zeros((), jnp.float32), (frames, cell_mask, counts, step_index)
    )

    def backward_micro(totals, sliced):
        frames_item, mask_item, count_item, step_item, grad_out, kept = sliced
        lifted, enc_kept, encoder_result, foreign, joined, dec_kept = kept
        dec_scale, dec_shift, one_hot = conditioning(step_item, dec_step_table)
        grad_joined, dec_grads, dec_gscale, dec_gshift = block_backward(
            joined, dec_weights, dec_scale, dec_shift, dec_kept, grad_out
        )
        grad_skip_weight = jnp.einsum("hwk,hwc->kc", joined, grad_out, precision=HIGH)
        grad_skip_bias = jnp.sum(grad_out, axis=(0, 1))
        grad_joined = grad_joined + jnp.dot(grad_out, skip_weight.T, precision=HIGH)
        half_width = joined.shape[-1] // 2
        grad_raised = grad_joined[..., :half_width]
        grad_encoded = grad_joined[..., half_width:]
        grad_foreign_up = from_behind(grad_raised, "section", 1)
        up_pull = jax.vjp(upsample, foreign, up_weight, up_bias)[1](grad_foreign_up)
        coarse_gradient = from_behind(up_pull[0], "section", 1)
        reducer_pullback = jax.vjp(coarsen_field, encoder_result, reducer_weight, reducer_bias)[1](
            coarse_gradient
        )
        grad_encoded = grad_encoded + reducer_pullback[0]
        enc_scale, enc_shift, enc_hot = conditioning(step_item, enc_step_table)
        grad_lifted, enc_grads, enc_gscale, enc_gshift = block_backward(
            lifted, enc_weights, enc_scale, enc_shift, enc_kept, grad_encoded
        )
        grad_lifted = grad_lifted + grad_encoded
        proj_pull = jax.vjp(
            lambda frames_in, incoming_weight, incoming_bias: project_in(
                frames_in, mask_item, count_item, incoming_weight, incoming_bias
            ),
            frames_item,
            lift_weight,
            lift_bias,
        )[1](grad_lifted)
        enc_table_grad = enc_hot[:, None] * jnp.concatenate([enc_gscale, enc_gshift])[None, :]
        dec_table_grad = one_hot[:, None] * jnp.concatenate([dec_gscale, dec_gshift])[None, :]
        micro_list = (
            proj_pull[1],
            proj_pull[2],
            enc_grads[0],
            enc_grads[1],
            enc_grads[2],
            enc_table_grad,
            enc_grads[3],
            enc_grads[4],
            enc_grads[5],
            enc_grads[6],
            reducer_pullback[1],
            reducer_pullback[2],
            up_pull[1],
            up_pull[2],
            dec_grads[0],
            dec_grads[1],
            dec_grads[2],
            dec_table_grad,
            dec_grads[3],
            dec_grads[4],
            dec_grads[5],
            dec_grads[6],
            grad_skip_weight,
            grad_skip_bias,
        )
        micro_flat = flatten_all(micro_list)
        return (totals + micro_flat, proj_pull[0])

    total_size = sum((piece.size for piece in params))
    start_totals = jnp.zeros((total_size,), jnp.float32)
    flat_totals, frames_grad = lax.scan(
        backward_micro,
        start_totals,
        (frames, cell_mask, counts, step_index, cotangent, kept_all),
        reverse=True,
    )
    flat_totals = lax.psum(flat_totals, ("section", "batch", "rows"))
    grads = unflatten_all(flat_totals, params)
    return (output, frames_grad) + grads


F32 = jnp.float32
BF16 = jnp.bfloat16
MESH = pl.DeviceIdType.MESH
NN = ((1,), (0,))
NT = ((1,), (1,))
TN = ((0,), (0,))
HIGH_AT = (0, 2, 1)
LOW_AT = (4, 3, 5)
CHUNK = 512
class Given(NamedTuple):
    frames: Any
    counts: Any
    cell_mask: Any
    step_index: Any
    lift_weight: Any
    lift_bias: Any
    enc_norm1_gain: Any
    enc_norm1_bias: Any
    enc_conv1: Any
    enc_step_table: Any
    enc_norm2_gain: Any
    enc_norm2_bias: Any
    enc_conv2: Any
    enc_conv2_bias: Any
    reducer_weight: Any
    reducer_bias: Any
    up_weight: Any
    up_bias: Any
    dec_norm1_gain: Any
    dec_norm1_bias: Any
    dec_conv1: Any
    dec_step_table: Any
    dec_norm2_gain: Any
    dec_norm2_bias: Any
    dec_conv2: Any
    dec_conv2_bias: Any
    skip_weight: Any
    skip_bias: Any
    cotangent: Any


ARGUMENTS = Given._fields
LARGE = tuple(dict(
    dec_conv2=0,
    skip_weight=0,
    dec_conv1=0,
    up_weight=0,
    reducer_weight=0,
    enc_conv2=0,
    enc_conv1=0,
))
IN_HBM = tuple(dict(frames=0, cell_mask=0, cotangent=0)) + LARGE
IN_SMEM = tuple(dict(counts=0, step_index=0))
SMALL_ROWS = dict(
    lift_weight=(0, 12),
    lift_bias=(12, 1),
    enc_norm1_gain=(16, 1),
    enc_norm1_bias=(17, 1),
    enc_norm2_gain=(18, 1),
    enc_norm2_bias=(19, 1),
    enc_conv2_bias=(20, 1),
    reducer_bias=(21, 1),
    up_bias=(22, 1),
    dec_conv2_bias=(23, 1),
    skip_bias=(23, 1),
    dec_norm1_gain=(24, 2),
    dec_norm1_bias=(26, 2),
    dec_norm2_gain=(28, 1),
    dec_norm2_bias=(29, 1),
    enc_step_table=(32, 8),
    dec_step_table=(40, 8),
)
SMALL_COUNT = 64
OUTPUTS = tuple(dict(output=0, frames_grad=0, gradients=0))


def split(value):
    high = value.astype(BF16)
    return high, (value - high.astype(F32)).astype(BF16)


def dot(left, right, dims=NN, precision=None):
    return lax.dot_general(
        left, right, (dims, ((), ())), precision=precision, preferred_element_type=F32
    )


def fold(value):
    half = value.shape[1] // 2
    return value[:, :half] + value[:, half:]


def fold_rows(value):
    half = value.shape[0] // 2
    return value[:half] + value[half:]


def tile_sums(value):
    return jnp.sum(value.reshape(-1, 8, value.shape[-1]), axis=0)


def column_sum(tiles):
    return jnp.sum(tiles, axis=0, keepdims=True)


def group_ones(channels, size):
    rows = lax.broadcasted_iota(jnp.int32, (channels, channels), 0) // size
    columns = lax.broadcasted_iota(jnp.int32, (channels, channels), 1) // size
    return (rows == columns).astype(F32)


def group_sums(first, second, ones):
    both = dot(jnp.concatenate([first, second], axis=0), ones, precision=HIGH)
    return column_sum(both[:8]), column_sum(both[8:])


class Exchange:

    def __init__(self, place, start, rows, landing, first_sem):
        self.place, self.start, self.rows, self.landing = place, start, rows, landing
        self.sem = first_sem
        self.stage = 0
        self.copies = []
        line = place.line
        self.at = [start]
        size = rows
        for bit in (place.core, place.first, place.second):
            size //= 2
            self.at.append(self.at[-1] + bit * size)
        self.shard = size // line
        self.at.append(self.at[-1] + place.row * self.shard)

    def count(self):
        return 6 + 2 * (self.place.line - 1)

    def _copy(self, source, target, device):
        place = self.place
        copy = pltpu.make_async_remote_copy(
            src_ref=source,
            dst_ref=target,
            send_sem=place.send.at[self.sem],
            recv_sem=place.recv.at[self.sem],
            device_id=device,
            device_id_type=MESH,
        )
        self.sem += 1
        copy.start()
        self.copies.append(copy)
        return copy

    def _halve(self, level):
        place = self.place
        size = self.rows >> (level + 1)
        bit = (place.core, place.first, place.second)[level]
        other = pl.multiple_of(self.at[level] + (1 - bit) * size, 8)
        self.land = self.landing
        self.landing += size
        self.waiting = [
            self._copy(
                place.sums.at[pl.ds(other, size)],
                place.landing.at[pl.ds(self.land, size)],
                place.partners[level],
            )
        ]

    def _add(self, level):
        place = self.place
        size = self.rows >> (level + 1)
        block = 128 >> level
        sums, landing = place.sums, place.landing
        base = self.at[level + 1]
        land = self.land

        def step(i, carry):
            here = pl.ds(pl.multiple_of(base + i * block, 8), block)
            there = pl.ds(pl.multiple_of(land + i * block, 8), block)
            sums[here] = sums[here] + landing[there]
            return carry

        lax.fori_loop(0, size // block, step, 0)

    def _wait(self):
        for copy in self.waiting:
            copy.wait_recv()

    def _spread(self, level):
        place = self.place
        size = self.rows >> (level + 1)
        here = pl.ds(pl.multiple_of(self.at[level + 1], 8), size)
        self.waiting = [
            self._copy(
                place.final.at[here], place.final.at[here], place.partners[level]
            )
        ]

    def advance(self):
        place = self.place
        line, row = place.line, place.row
        shard = self.shard
        stage = self.stage
        self.stage += 1
        if stage == 0:
            self._halve(0)
        elif stage in (1, 2):
            self._wait()
            self._add(stage - 1)
            self._halve(stage)
        elif stage == 3:
            self._wait()
            self._add(2)
            self.waiting = []
            self.land = self.landing
            for k in range(1, line):
                to = lax.rem(row + k, line)
                source = pl.ds(pl.multiple_of(self.at[3] + to * shard, 8), shard)
                target = pl.ds(self.landing, shard)
                self.landing += shard
                self.waiting.append(
                    self._copy(
                        place.sums.at[source],
                        place.landing.at[target],
                        place.device_at(to),
                    )
                )
        elif stage == 4:
            self._wait()
            here = pl.ds(pl.multiple_of(self.at[4], 8), shard)
            total = place.sums[here]
            for k in range(line - 1):
                total = total + place.landing[pl.ds(self.land + k * shard, shard)]
            place.final[here] = total
            self.waiting = []
            for k in range(1, line):
                self.waiting.append(
                    self._copy(
                        place.final.at[here],
                        place.final.at[here],
                        place.device_at(lax.rem(row + k, line)),
                    )
                )
        elif stage in (5, 6, 7):
            self._wait()
            self._spread(7 - stage)
        else:
            self._wait()

    def done(self):
        return self.stage > 8


def layout_of(shapes):
    starts = {}
    at = 0
    for name in LARGE:
        starts[name] = at
        at += shapes[name][0]
    small = at
    unit = 256
    total = -(-(at + SMALL_COUNT) // unit) * unit
    begins = SimpleNamespace(**starts)
    ready = (
        begins.dec_conv1,
        begins.up_weight,
        begins.enc_conv2,
        begins.enc_conv1,
        small,
    )
    edges = [0] + [edge // unit * unit for edge in ready] + [total]
    runs = [(a, b - a) for a, b in zip(edges[:-1], edges[1:])]
    return starts, small, total, runs


def item_kernel(sizes, scratch_names, *refs):
    line, strip, width, shapes, big_layout = sizes
    begins, small_at, total_rows, runs = big_layout
    starts = SimpleNamespace(**begins)
    inputs = Given(*refs[: len(ARGUMENTS)])
    refs = refs[len(ARGUMENTS) :]
    output_names = OUTPUTS
    outputs = SimpleNamespace(**dict(zip(output_names, refs)))
    scratch = SimpleNamespace(**dict(zip(scratch_names, refs[len(output_names) :])))

    def w_of(name):
        return getattr(scratch, name)

    height = strip * line
    cells = height * width
    c = inputs.lift_weight.shape[1]
    strip_cells = strip * width
    history = inputs.frames.shape[1]

    core = lax.axis_index("section")
    plane = lax.axis_index("batch")
    row = lax.axis_index("rows")
    y, x = plane // 2, lax.rem(plane, 2)
    along_x = plane + 1 - 2 * x
    along_y = plane + 2 - 4 * y
    place = SimpleNamespace(
        line=line,
        row=row,
        core=core,
        first=x * (1 - core) + y * core,
        second=y * (1 - core) + x * core,
        partners=(
            (1 - core, plane, row),
            (core, along_x * (1 - core) + along_y * core, row),
            (core, along_y * (1 - core) + along_x * core, row),
        ),
        device_at=lambda to: (core, plane, to),
        sums=scratch.sums,
        final=scratch.final,
        landing=scratch.landing,
        send=scratch.send,
        recv=scratch.recv,
    )
    local_sem = scratch.local

    weight_copies = {}
    for k, name in enumerate(LARGE):
        copy = pltpu.make_async_copy(getattr(inputs, name), w_of(name), local_sem.at[k])
        weight_copies[name] = copy
        copy.start()
    frames_in, mask_in, cot = scratch.frames_in, scratch.mask_in, scratch.cot
    here_rows = pl.ds(pl.multiple_of(row * strip_cells, strip_cells), strip_cells)
    own = (
        pltpu.make_async_copy(inputs.frames.at[row], frames_in.at[row], local_sem.at[7]),
        pltpu.make_async_copy(inputs.cell_mask.at[row], mask_in.at[row], local_sem.at[8]),
        pltpu.make_async_copy(
            inputs.cotangent.at[row], cot.at[here_rows], local_sem.at[9]
        ),
    )
    for copy in own:
        copy.start()

    barrier = pltpu.get_barrier_semaphore()
    peers = [place.device_at(lax.rem(row + k, line)) for k in range(1, line)]
    for device in tuple(peers) + place.partners:
        pl.semaphore_signal(barrier, inc=1, device_id=device, device_id_type=MESH)
    pl.semaphore_wait(barrier, len(peers) + 3)

    next_sem = 0

    def send(source, target, device):
        nonlocal next_sem
        copy = pltpu.make_async_remote_copy(
            src_ref=source,
            dst_ref=target,
            send_sem=scratch.send.at[next_sem],
            recv_sem=scratch.recv.at[next_sem],
            device_id=device,
            device_id_type=MESH,
        )
        next_sem += 1
        copy.start()
        return copy

    frame_copies, cot_copies, output_copies = [], [], []
    for k in range(1, line):
        to = lax.rem(row + k, line)
        device = place.device_at(to)
        frame_copies.append(send(inputs.frames.at[to], frames_in.at[row], device))
        frame_copies.append(send(inputs.cell_mask.at[to], mask_in.at[row], device))
    for k in range(1, line):
        to = lax.rem(row + k, line)
        cot_copies.append(
            send(inputs.cotangent.at[to], cot.at[here_rows], place.device_at(to))
        )

    copied = SimpleNamespace(**weight_copies)
    def stack_conv(source, half, depth, forward, backward):
        for a in range(3):
            for b in range(3):
                at = (3 * a + b) * depth + half * c
                high, low = split(source[at : at + c, :])
                for block in (HIGH_AT[b], LOW_AT[b]):
                    rows = slice(block * c, (block + 1) * c)
                    forward[a, rows, 0:c] = high
                    forward[a, rows, c : 2 * c] = low
                for block in (HIGH_AT[2 - b], LOW_AT[2 - b]):
                    columns = slice(block * c, (block + 1) * c)
                    backward[2 - a, 0:c, columns] = high
                    backward[2 - a, c : 2 * c, columns] = low

    copied.enc_conv1.wait()
    stack_conv(scratch.enc_conv1, 0, c, scratch.fe1, scratch.be1)
    copied.enc_conv2.wait()
    stack_conv(scratch.enc_conv2, 0, c, scratch.fe2, scratch.be2)
    copied.reducer_weight.wait()
    for k in range(4):
        high, low = split(scratch.reducer_weight[k * c : (k + 1) * c, :])
        for block in (k, k + 4):
            scratch.f_down[block * c : (block + 1) * c, 0:c] = high
            scratch.f_down[block * c : (block + 1) * c, c : 2 * c] = low
        for block in (0, 1):
            columns = slice(block * c, (block + 1) * c)
            scratch.b_down[k, 0:c, columns] = high
            scratch.b_down[k, c : 2 * c, columns] = low
    copied.up_weight.wait()
    for k in range(4):
        high, low = split(scratch.up_weight[k * c : (k + 1) * c, :])
        for block in (0, 1):
            rows = slice(block * c, (block + 1) * c)
            scratch.f_up[k, rows, 0:c] = high
            scratch.f_up[k, rows, c : 2 * c] = low
        for block in (k, k + 4):
            columns = slice(block * c, (block + 1) * c)
            scratch.b_up[0:c, columns] = high
            scratch.b_up[c : 2 * c, columns] = low
    copied.dec_conv1.wait()
    stack_conv(scratch.dec_conv1, 0, 2 * c, scratch.fd1a, scratch.bd1a)
    stack_conv(scratch.dec_conv1, 1, 2 * c, scratch.fd1b, scratch.bd1b)
    copied.dec_conv2.wait()
    stack_conv(scratch.dec_conv2, 0, c, scratch.fd2, scratch.bd2)
    copied.skip_weight.wait()
    for half in range(2):
        high, low = split(scratch.skip_weight[half * c : (half + 1) * c, :])
        for block in (half, half + 2):
            scratch.f_skip[block * c : (block + 1) * c, 0:c] = high
            scratch.f_skip[block * c : (block + 1) * c, c : 2 * c] = low
        for block in (0, 1):
            columns = slice(block * c, (block + 1) * c)
            scratch.b_skip[half, 0:c, columns] = high
            scratch.b_skip[half, c : 2 * c, columns] = low

    for buffer in (scratch.xe1, scratch.xe2, scratch.xd1a, scratch.xd1b, scratch.xd2, scratch.xg):
        edge = jnp.zeros((width, 6 * c), BF16)
        buffer[0:width, :] = edge
        buffer[cells + width : cells + 2 * width, :] = edge

    lift = scratch.lift
    lift[...] = jnp.zeros(lift.shape, F32)
    lift[0:history, :] = inputs.lift_weight[...]
    lift[history : history + 1, :] = inputs.lift_bias[...]

    block = 2 * width
    column = lax.rem(lax.broadcasted_iota(jnp.int32, (block, c), 0), width)
    at_first, at_last = column == 0, column == width - 1
    zeros8 = jnp.zeros((8, c), F32)
    ones16 = group_ones(c, c // GROUPS)
    ones32 = group_ones(c, 2 * c // GROUPS)
    count16 = float(cells * (c // GROUPS))
    count32 = float(cells * (2 * c // GROUPS))

    def grid_rows(step, carry=0):
        return lax.fori_loop(0, cells // block, step, carry, unroll=2)

    def row_at(h):
        return pl.ds(pl.multiple_of(h * block, block), block)

    def chunk_at(i):
        return pl.ds(pl.multiple_of(i * CHUNK, CHUNK), CHUNK)

    def put_row(target, h, value):
        rows = pl.ds(pl.multiple_of(h * block + width, width), block)
        left = jnp.where(at_first, 0.0, pltpu.roll(value, 1, 0))
        right = jnp.where(at_last, 0.0, pltpu.roll(value, block - 1, 0))
        for b, piece in enumerate((left, value, right)):
            high, low = split(piece)
            target[rows, HIGH_AT[b] * c : (HIGH_AT[b] + 1) * c] = high
            target[rows, LOW_AT[b] * c : (LOW_AT[b] + 1) * c] = low

    def put_turned(target, columns, value, first=0, second=1):
        high, low = split(value.T)
        target[first * c : (first + 1) * c, columns] = high
        target[second * c : (second + 1) * c, columns] = low

    def conv_chunk(pairs, i, dims=NN):
        total = None
        for data, weight in pairs:
            for a in range(3):
                rows = pl.ds(pl.multiple_of(i * CHUNK + a * width, width), CHUNK)
                part = dot(data[rows, :], weight[a], dims)
                total = part if total is None else total + part
        return total

    def norm_of(first, second, ones, count):
        one, two = group_sums(first, second, ones)
        mean = one / count
        return mean, lax.rsqrt(two / count - mean * mean + EPS)

    def activate(source, target, turned, slope, scale, shift):
        def step(h, carry):
            value = source[row_at(h), :] * scale + shift
            below = 0.5 + 0.5 * lax.erf(value * 0.7071067811865476)
            slope[row_at(h), :] = below + value * (
                0.3989422804014327 * jnp.exp(-0.5 * value * value)
            )
            value = value * below
            put_row(target, h, value)
            put_turned(turned, row_at(h), value)
            return carry

        grid_rows(step)

    def conv_norm(pairs, target):
        def step(i, carry):
            value = fold(conv_chunk(pairs, i))
            target[chunk_at(i), :] = value
            return carry[0] + tile_sums(value), carry[1] + tile_sums(value * value)

        return lax.fori_loop(0, cells // CHUNK, step, (zeros8, zeros8))

    def sums_of(source):
        def step(h, carry):
            value = source[row_at(h), :]
            return carry[0] + tile_sums(value), carry[1] + tile_sums(value * value)

        return grid_rows(step, (zeros8, zeros8))

    step_here = jnp.full((1, c), inputs.step_index[row], jnp.int32)

    def condition(table):
        total = jnp.zeros((1, 2 * c), F32)
        chosen = jnp.concatenate([step_here, step_here], axis=1)
        for s in range(table.shape[0]):
            total = total + jnp.where(chosen == s, table[s : s + 1, :], 0.0)
        return total[:, :c], total[:, c:]

    for copy in own[:2]:
        copy.wait()
    for copy in frame_copies:
        copy.wait_recv()
    fields = scratch.fields
    fields[...] = jnp.zeros(fields.shape, F32)
    frame_of = lax.broadcasted_iota(jnp.int32, (history, width), 0) // FIELDS
    keep = (frame_of >= HIST - inputs.counts[row]).astype(F32)
    masks = []
    for source in range(line):
        for k in range(strip):
            columns = slice((source * strip + k) * width, (source * strip + k + 1) * width)
            mask = mask_in[source, k : k + 1, :].astype(F32)
            masks.append(mask)
            fields[0:history, columns] = frames_in[source, :, k, :] * keep * mask
            fields[history : history + 1, columns] = mask
    lifted = scratch.lifted
    lifted[...] = dot(fields[...], lift[...], TN, HIGH)

    enc_scale, enc_shift = condition(inputs.enc_step_table)
    dec_scale, dec_shift = condition(inputs.dec_step_table)

    mean_e1, inv_e1 = norm_of(*sums_of(lifted), ones16, count16)
    gain_e1, bias_e1 = inputs.enc_norm1_gain[...], inputs.enc_norm1_bias[...]
    a_e1 = inv_e1 * gain_e1
    activate(lifted, scratch.xe1, scratch.te1, scratch.slope_e1, a_e1, bias_e1 - mean_e1 * a_e1)
    middle_e = scratch.middle_e
    mean_e2, inv_e2 = norm_of(
        *conv_norm([(scratch.xe1, scratch.fe1)], middle_e), ones16, count16
    )
    gain_e2, bias_e2 = inputs.enc_norm2_gain[...], inputs.enc_norm2_bias[...]
    a_e2 = inv_e2 * gain_e2
    activate(
        middle_e,
        scratch.xe2,
        scratch.te2,
        scratch.slope_e2,
        a_e2 * (1.0 + enc_scale),
        (bias_e2 - mean_e2 * a_e2) * (1.0 + enc_scale) + enc_shift,
    )
    encoded = scratch.encoded
    conv2_bias = inputs.enc_conv2_bias[...]
    joined = scratch.joined

    def encode(i, carry):
        value = fold(conv_chunk([(scratch.xe2, scratch.fe2)], i))
        value = value + conv2_bias + lifted[chunk_at(i), :]
        encoded[chunk_at(i), :] = value
        high, low = split(value)
        joined[chunk_at(i), c : 2 * c] = high
        joined[chunk_at(i), 3 * c : 4 * c] = low
        put_turned(scratch.turned, chunk_at(i), value, 1, 3)
        return carry[0] + tile_sums(value), carry[1] + tile_sums(value * value)

    sums_enc = lax.fori_loop(0, cells // CHUNK, encode, (zeros8, zeros8))

    half_cells, quarter = cells // 2, cells // 4

    def pick(source):
        pieces = []
        for b in range(2):
            value = source[pl.ds(b, half_cells, stride=2), :]
            value = value.reshape(height // 2, 2, width // 2, c)
            pieces.append([value[:, a].reshape(quarter, c) for a in range(2)])
        return [pieces[b][a] for a in range(2) for b in range(2)]

    def place_cells(target, pieces):
        for b in range(2):
            both = [pieces[2 * a + b].reshape(height // 2, 1, width // 2, c) for a in range(2)]
            value = jnp.concatenate(both, axis=1).reshape(half_cells, c)
            target[pl.ds(b, half_cells, stride=2), :] = value

    x_down = scratch.x_down
    for k, piece in enumerate(pick(encoded)):
        high, low = split(piece)
        x_down[:, k * c : (k + 1) * c] = high
        x_down[:, (k + 4) * c : (k + 5) * c] = low
    lowered = fold(dot(x_down[...], scratch.f_down[...])) + inputs.reducer_bias[...]
    x_up = scratch.x_up
    high, low = split(lowered)
    x_up[:, 0:c] = high
    x_up[:, c : 2 * c] = low
    raised = scratch.raised
    up_bias = inputs.up_bias[...]
    place_cells(
        raised, [fold(dot(x_up[...], scratch.f_up[k])) + up_bias for k in range(4)]
    )

    def raise_row(h, carry):
        value = raised[row_at(h), :]
        high, low = split(value)
        joined[row_at(h), 0:c] = high
        joined[row_at(h), 2 * c : 3 * c] = low
        put_turned(scratch.turned, row_at(h), value, 0, 2)
        return carry[0] + tile_sums(value), carry[1] + tile_sums(value * value)

    sums_raised = grid_rows(raise_row, (zeros8, zeros8))

    halves = []
    for half, (source, sums) in enumerate(((raised, sums_raised), (encoded, sums_enc))):
        mean, inv = norm_of(*sums, ones32, count32)
        gain = inputs.dec_norm1_gain[half : half + 1, :]
        bias = inputs.dec_norm1_bias[half : half + 1, :]
        scale = inv * gain
        activate(
            source,
            (scratch.xd1a, scratch.xd1b)[half],
            (scratch.td1a, scratch.td1b)[half],
            (scratch.slope_d1a, scratch.slope_d1b)[half],
            scale,
            bias - mean * scale,
        )
        halves.append((source, mean, inv, gain))
    middle_d = scratch.middle_d
    pairs = [(scratch.xd1a, scratch.fd1a), (scratch.xd1b, scratch.fd1b)]
    mean_d2, inv_d2 = norm_of(*conv_norm(pairs, middle_d), ones16, count16)
    gain_d2, bias_d2 = inputs.dec_norm2_gain[...], inputs.dec_norm2_bias[...]
    a_d2 = inv_d2 * gain_d2
    activate(
        middle_d,
        scratch.xd2,
        scratch.td2,
        scratch.slope_d2,
        a_d2 * (1.0 + dec_scale),
        (bias_d2 - mean_d2 * a_d2) * (1.0 + dec_scale) + dec_shift,
    )
    result = scratch.result
    last_bias = inputs.dec_conv2_bias[...] + inputs.skip_bias[...]

    def decode(i, carry):
        value = conv_chunk([(scratch.xd2, scratch.fd2)], i)
        value = value + dot(joined[chunk_at(i), :], scratch.f_skip[...])
        result[chunk_at(i), :] = fold(value) + last_bias
        return carry

    lax.fori_loop(0, cells // CHUNK, decode, 0)
    own_output = pltpu.make_async_copy(
        result.at[here_rows], outputs.output.at[row], local_sem.at[10]
    )
    own_output.start()
    for k in range(1, line):
        to = lax.rem(row + k, line)
        there = pl.ds(pl.multiple_of(to * strip_cells, strip_cells), strip_cells)
        output_copies.append(
            send(result.at[there], outputs.output.at[row], place.device_at(to))
        )

    exchanges = []
    waiting_runs = list(runs)
    landing_at = 0
    sem_at = 4 * (line - 1) + 2 * (line - 1)
    sums, final = scratch.sums, scratch.final

    def begin():
        nonlocal landing_at, sem_at
        start, rows = waiting_runs.pop(0)
        exchange = Exchange(place, start, rows, landing_at, sem_at)
        landing_at += rows - rows // (8 * line)
        sem_at += exchange.count()
        exchanges.append(exchange)
        exchange.advance()

    final_copies = []

    def publish():
        for k, exchange in enumerate(exchanges):
            if k == len(final_copies) and exchange.done():
                rows = pl.ds(exchange.start, exchange.rows)
                copy = pltpu.make_async_copy(
                    final.at[rows], outputs.gradients.at[rows], local_sem.at[11 + k]
                )
                copy.start()
                final_copies.append(copy)

    def tick():
        for exchange in exchanges:
            if not exchange.done():
                exchange.advance()
        publish()

    def small_row(k, value):
        sums[small_at + k : small_at + k + 1, :] = value

    def spread_grad(source):
        def step(h, carry):
            value = source[row_at(h), :]
            put_row(scratch.xg, h, value)
            return carry + tile_sums(value)

        return grid_rows(step, zeros8)

    def weight_grad(turned, at, depth):
        lhs = turned[...]
        for a in range(3):
            rows = pl.ds((2 - a) * width, cells)
            part = fold_rows(dot(lhs, scratch.xg[rows, :]))
            for b in range(3):
                high, low = HIGH_AT[2 - b] * c, LOW_AT[2 - b] * c
                to = at + (3 * a + b) * depth
                sums[to : to + c, :] = part[:, high : high + c] + part[:, low : low + c]

    def back_conv(weight, slope, target, source, mean, inv):
        def step(i, carry):
            value = fold(conv_chunk([(scratch.xg, weight)], i, NT)) * slope[chunk_at(i), :]
            target[chunk_at(i), :] = value
            normed = (source[chunk_at(i), :] - mean) * inv
            return carry[0] + tile_sums(value), carry[1] + tile_sums(value * normed)

        return lax.fori_loop(0, cells // CHUNK, step, (zeros8, zeros8))

    def norm_grad(sums_in, scale, ones, count):
        one, two = group_sums(sums_in[0] * scale, sums_in[1] * scale, ones)
        return one / count, two / count

    own[2].wait()
    for copy in cot_copies:
        copy.wait_recv()
    total_cot = column_sum(spread_grad(cot))
    weight_grad(scratch.td2, starts.dec_conv2, c)
    part = fold(dot(scratch.turned[...], scratch.xg[width : cells + width, 2 * c : 4 * c]))
    sums[starts.skip_weight : starts.skip_weight + 2 * c, :] = fold_rows(part)
    small_row(23, total_cot)
    begin()

    grad = scratch.grad
    sums_d2 = back_conv(scratch.bd2, scratch.slope_d2, grad, middle_d, mean_d2, inv_d2)
    side_grads = (scratch.grad_a, scratch.grad_b)
    for half in range(2):

        def skip_back(i, carry, half=half):
            rows = pl.ds(pl.multiple_of(i * CHUNK + width, width), CHUNK)
            value = dot(scratch.xg[rows, 2 * c : 4 * c], scratch.b_skip[half], NT)
            side_grads[half][chunk_at(i), :] = fold(value)
            return carry

        lax.fori_loop(0, cells // CHUNK, skip_back, 0)
    tick()

    def table_rows(k, sums_in, gain, bias, one_plus):
        plain, times = column_sum(sums_in[0]), column_sum(sums_in[1])
        for s in range(inputs.enc_step_table.shape[0]):
            small_row(k + 2 * s, jnp.where(step_here == s, gain * times + bias * plain, 0.0))
            small_row(k + 2 * s + 1, jnp.where(step_here == s, plain, 0.0))
        return one_plus * times, one_plus * plain

    def middle_grad(source, mean, inv, scale, sums_in):
        zero, slope = norm_grad(sums_in, scale, ones16, count16)

        def step(h, carry):
            normed = (source[row_at(h), :] - mean) * inv
            value = inv * (grad[row_at(h), :] * scale - zero - normed * slope)
            put_row(scratch.xg, h, value)
            return carry

        grid_rows(step)

    gain_row, bias_row = table_rows(40, sums_d2, gain_d2, bias_d2, 1.0 + dec_scale)
    small_row(28, gain_row)
    small_row(29, bias_row)
    middle_grad(middle_d, mean_d2, inv_d2, gain_d2 * (1.0 + dec_scale), sums_d2)
    weight_grad(scratch.td1a, starts.dec_conv1, 2 * c)
    tick()
    weight_grad(scratch.td1b, starts.dec_conv1 + c, 2 * c)
    begin()

    for half, (source, mean, inv, gain) in enumerate(halves):
        sums_in = back_conv(
            (scratch.bd1a, scratch.bd1b)[half],
            (scratch.slope_d1a, scratch.slope_d1b)[half],
            grad,
            source,
            mean,
            inv,
        )
        small_row(24 + half, column_sum(sums_in[1]))
        small_row(26 + half, column_sum(sums_in[0]))
        zero, slope = norm_grad(sums_in, gain, ones32, count32)
        target = side_grads[half]

        def input_grad(h, carry):
            normed = (source[row_at(h), :] - mean) * inv
            value = inv * (grad[row_at(h), :] * gain - zero - normed * slope)
            value = target[row_at(h), :] + value
            target[row_at(h), :] = value
            return carry + tile_sums(value)

        total = grid_rows(input_grad, zeros8)
        if half == 0:
            small_row(22, column_sum(total))
        tick()

    grad_raised, grad_encoded = side_grads
    x_grad_up = scratch.x_grad_up
    for k, piece in enumerate(pick(grad_raised)):
        high, low = split(piece)
        x_grad_up[:, k * c : (k + 1) * c] = high
        x_grad_up[:, (k + 4) * c : (k + 5) * c] = low
    grad_lowered = fold(dot(x_grad_up[...], scratch.b_up[...], NT))
    small_row(21, jnp.sum(grad_lowered, axis=0, keepdims=True))
    x_grad_low = scratch.x_grad_low
    high, low = split(grad_lowered)
    x_grad_low[:, 0:c] = high
    x_grad_low[:, c : 2 * c] = low
    part = fold(fold_rows(dot(x_up[...], x_grad_up[...], TN)))
    for k in range(4):
        at = starts.up_weight + k * c
        sums[at : at + c, :] = part[:, k * c : (k + 1) * c]
    part = fold_rows(fold(dot(x_down[...], x_grad_low[...], TN)))
    sums[starts.reducer_weight : starts.reducer_weight + 4 * c, :] = part
    begin()
    place_cells(
        grad, [fold(dot(x_grad_low[...], scratch.b_down[k], NT)) for k in range(4)]
    )

    def join_row(h, carry):
        value = grad_encoded[row_at(h), :] + grad[row_at(h), :]
        grad_encoded[row_at(h), :] = value
        put_row(scratch.xg, h, value)
        return carry + tile_sums(value)

    small_row(20, column_sum(grid_rows(join_row, zeros8)))
    tick()
    weight_grad(scratch.te2, starts.enc_conv2, c)
    begin()
    sums_e2 = back_conv(scratch.be2, scratch.slope_e2, grad, middle_e, mean_e2, inv_e2)
    gain_row, bias_row = table_rows(32, sums_e2, gain_e2, bias_e2, 1.0 + enc_scale)
    small_row(18, gain_row)
    small_row(19, bias_row)
    middle_grad(middle_e, mean_e2, inv_e2, gain_e2 * (1.0 + enc_scale), sums_e2)
    tick()
    weight_grad(scratch.te1, starts.enc_conv1, c)
    begin()
    tick()
    sums_e1 = back_conv(scratch.be1, scratch.slope_e1, grad, lifted, mean_e1, inv_e1)
    small_row(16, column_sum(sums_e1[1]))
    small_row(17, column_sum(sums_e1[0]))
    zero, slope = norm_grad(sums_e1, gain_e1, ones16, count16)

    def lifted_grad(h, carry):
        normed = (lifted[row_at(h), :] - mean_e1) * inv_e1
        value = inv_e1 * (grad[row_at(h), :] * gain_e1 - zero - normed * slope)
        grad[row_at(h), :] = grad_encoded[row_at(h), :] + value
        return carry

    grid_rows(lifted_grad)
    tick()

    sums[small_at : small_at + 16, :] = dot(fields[...], grad[...], NN, HIGH)
    for k in (30, 31):
        small_row(k, jnp.zeros((1, c), F32))
    rest = small_at + 48
    sums[rest:total_rows, :] = jnp.zeros((total_rows - rest, c), F32)
    begin()
    back = dot(lift[...], grad[...], NT, HIGH)
    frames_out = scratch.frames_out
    for source in range(line):
        for k in range(strip):
            h = source * strip + k
            value = back[0:history, h * width : (h + 1) * width]
            frames_out[source, :, k, :] = value * keep * masks[h]
    own_frames = pltpu.make_async_copy(
        frames_out.at[row], outputs.frames_grad.at[row], local_sem.at[18]
    )
    own_frames.start()
    for k in range(1, line):
        to = lax.rem(row + k, line)
        output_copies.append(
            send(frames_out.at[to], outputs.frames_grad.at[row], place.device_at(to))
        )

    while not all(exchange.done() for exchange in exchanges):
        tick()

    for copy in output_copies:
        copy.wait_recv()
    own_output.wait()
    own_frames.wait()
    for copy in final_copies:
        copy.wait()
    for copy in frame_copies + cot_copies + output_copies:
        copy.wait_send()
    for exchange in exchanges:
        for copy in exchange.copies:
            copy.wait_send()


def write_kernel(layout, *refs):
    shapes, starts, small_at = layout
    output, frames_grad, gradients = refs[:3]
    outputs = refs[3:-2]
    rows_here, sem = refs[-2:]
    c = gradients.shape[1]
    copies = [
        pltpu.make_async_copy(
            gradients.at[pl.ds(small_at, SMALL_COUNT)], rows_here, sem.at[0]
        ),
        pltpu.make_async_copy(output, outputs[0], sem.at[1]),
        pltpu.make_async_copy(frames_grad, outputs[1], sem.at[2]),
    ]
    for k, name in enumerate(LARGE):
        rows = pl.ds(starts[name], shapes[name][0])
        copies.append(pltpu.make_async_copy(gradients.at[rows], outputs[2 + k], sem.at[3 + k]))
    for copy in copies:
        copy.start()
    copies[0].wait()
    for target, (k, rows) in zip(outputs[2 + len(LARGE) :], SMALL_ROWS.values()):
        if rows == 8:
            for s in range(target.shape[0]):
                target[s : s + 1, 0:c] = rows_here[k + 2 * s : k + 2 * s + 1, :]
                target[s : s + 1, c : 2 * c] = rows_here[k + 2 * s + 1 : k + 2 * s + 2, :]
        else:
            target[...] = rows_here[k : k + rows, :]
    for copy in copies[1:]:
        copy.wait()


def whole_items(shape, *arguments):
    line = shape["rows"]
    whole = Given(*arguments)
    given = whole._asdict()
    frames, cotangent = whole.frames, whole.cotangent
    items, history, strip, width = frames.shape
    c = cotangent.shape[-1]
    cells = strip * line * width
    flat = {}
    for name, value in given.items():
        if value is cotangent:
            value = value.reshape(items, strip * width, c)
        elif name in LARGE:
            value = value.reshape(-1, c)
        elif value.ndim == 1 and name not in IN_SMEM:
            value = value.reshape(-1, c)
        flat[name] = value
    shapes = {name: flat[name].shape for name in LARGE}
    big_layout = layout_of(shapes)
    starts, small_at, total_rows, runs = big_layout
    copies = 6 * (line - 1) + len(runs) * (6 + 2 * (line - 1)) + line - 1
    landing = sum(rows - rows // (8 * line) for _, rows in runs)
    shifted = pltpu.VMEM((cells + 2 * width, 6 * c), BF16)
    forward = pltpu.VMEM((3, 6 * c, 2 * c), BF16)
    backward = pltpu.VMEM((3, 2 * c, 6 * c), BF16)
    field = pltpu.VMEM((cells, c), F32)
    flipped_field = pltpu.VMEM((2 * c, cells), BF16)
    quarter = cells // 4
    scratch = dict(
        send=pltpu.SemaphoreType.DMA((copies,)),
        recv=pltpu.SemaphoreType.DMA((copies,)),
        local=pltpu.SemaphoreType.DMA((19,)),
        sums=pltpu.VMEM((total_rows, c), F32),
        final=pltpu.VMEM((total_rows, c), F32),
        landing=pltpu.VMEM((landing, c), F32),
        frames_in=pltpu.VMEM((line, history, strip, width), F32),
        mask_in=pltpu.VMEM((line, strip, width), jnp.int32),
        frames_out=pltpu.VMEM((line, history, strip, width), F32),
        fields=pltpu.VMEM((16, cells), F32),
        lift=pltpu.VMEM((16, c), F32),
        joined=pltpu.VMEM((cells, 4 * c), BF16),
        x_down=pltpu.VMEM((quarter, 8 * c), BF16),
        x_grad_up=pltpu.VMEM((quarter, 8 * c), BF16),
        x_up=pltpu.VMEM((quarter, 2 * c), BF16),
        x_grad_low=pltpu.VMEM((quarter, 2 * c), BF16),
        f_down=pltpu.VMEM((8 * c, 2 * c), BF16),
        b_down=pltpu.VMEM((4, 2 * c, 2 * c), BF16),
        f_up=pltpu.VMEM((4, 2 * c, 2 * c), BF16),
        b_up=pltpu.VMEM((2 * c, 8 * c), BF16),
        f_skip=pltpu.VMEM((4 * c, 2 * c), BF16),
        b_skip=pltpu.VMEM((2, 2 * c, 2 * c), BF16),
        xe1=shifted,
        xe2=shifted,
        xd1a=shifted,
        xd1b=shifted,
        xd2=shifted,
        xg=shifted,
        te1=flipped_field,
        te2=flipped_field,
        td1a=flipped_field,
        td1b=flipped_field,
        td2=flipped_field,
        turned=pltpu.VMEM((4 * c, cells), BF16),
        fe1=forward,
        fe2=forward,
        fd1a=forward,
        fd1b=forward,
        fd2=forward,
        be1=backward,
        be2=backward,
        bd1a=backward,
        bd1b=backward,
        bd2=backward,
        slope_e1=field,
        slope_e2=field,
        slope_d1a=field,
        slope_d1b=field,
        slope_d2=field,
        lifted=field,
        middle_e=field,
        encoded=field,
        raised=field,
        middle_d=field,
        result=field,
        cot=field,
        grad=field,
        grad_a=field,
        grad_b=field,
    )
    scratch.update({name: pltpu.VMEM(shapes[name], F32) for name in LARGE})

    in_hbm = pl.BlockSpec(memory_space=pl.ANY)
    in_vmem = pl.BlockSpec(memory_space=pltpu.VMEM)
    in_smem = pl.BlockSpec(memory_space=pltpu.SMEM)
    in_specs = [
        in_hbm if name in IN_HBM else in_smem if name in IN_SMEM else in_vmem
        for name in ARGUMENTS
    ]
    out_shape = [
        jax.ShapeDtypeStruct((items, strip * width, c), F32),
        jax.ShapeDtypeStruct(frames.shape, F32),
        jax.ShapeDtypeStruct((total_rows, c), F32),
    ]
    out_specs = [in_hbm] * 3
    results = pl.pallas_call(
        functools.partial(
            item_kernel,
            (line, strip, width, shapes, big_layout),
            tuple(scratch),
        ),
        out_shape=out_shape,
        in_specs=in_specs,
        out_specs=out_specs,
        scratch_shapes=list(scratch.values()),
        compiler_params=pltpu.CompilerParams(
            collective_id=0, has_side_effects=True, vmem_limit_bytes=62 * 1024 * 1024
        ),
    )(*[flat[name] for name in ARGUMENTS])
    names = LARGE + tuple(SMALL_ROWS)
    written = pl.pallas_call(
        functools.partial(write_kernel, (shapes, starts, small_at)),
        out_shape=out_shape[:2] + [jax.ShapeDtypeStruct(flat[name].shape, F32) for name in names],
        in_specs=[pl.BlockSpec(memory_space=pltpu.HBM)] * 3,
        out_specs=[in_hbm] * (2 + len(LARGE)) + [in_vmem] * len(SMALL_ROWS),
        scratch_shapes=[
            pltpu.VMEM((SMALL_COUNT, c), F32),
            pltpu.SemaphoreType.DMA((3 + len(LARGE),)),
        ],
    )(*results)
    grads = dict(zip(names, written[2:]))
    ordered = [name for name in ARGUMENTS if name in grads]
    return (written[0].reshape(cotangent.shape), written[1]) + tuple(
        grads[name].reshape(given[name].shape) for name in ordered
    )


def body(shape, *arguments):
    items, _, strip, width = arguments[0].shape
    line = shape["rows"]
    whole = (
        shape["section"] == 2
        and shape["batch"] == 4
        and items == line
        and arguments[-1].shape[-1] == 128
        and (strip * line * width) % CHUNK == 0
    )
    return whole_items(shape, *arguments) if whole else strips_body(*arguments)


def solution(mesh):
    in_specs = (
        P(("section", "batch"), None, "rows", None),
        P(("section", "batch")),
        P(("section", "batch"), "rows", None),
        P(("section", "batch")),
        P(),
        P(),
        P(),
        P(),
        P(),
        P(),
        P(),
        P(),
        P(),
        P(),
        P(),
        P(),
        P(),
        P(),
        P(),
        P(),
        P(),
        P(),
        P(),
        P(),
        P(),
        P(),
        P(),
        P(),
        P(("section", "batch"), "rows", None, None),
    )
    out_specs = (
        P(("section", "batch"), "rows", None, None),
        P(("section", "batch"), None, "rows", None),
        P(),
        P(),
        P(),
        P(),
        P(),
        P(),
        P(),
        P(),
        P(),
        P(),
        P(),
        P(),
        P(),
        P(),
        P(),
        P(),
        P(),
        P(),
        P(),
        P(),
        P(),
        P(),
        P(),
        P(),
    )
    return jax.shard_map(functools.partial(body, mesh.shape), mesh=mesh, in_specs=in_specs, out_specs=out_specs, check_vma=False)
```

```python
import functools
from types import SimpleNamespace
from typing import Any, NamedTuple

import jax
import jax.numpy as jnp
from jax import lax
from jax.experimental import pallas as pl
from jax.experimental.pallas import tpu as pltpu
from jax.sharding import PartitionSpec as P

GROUPS = 8
FIELDS = 3
HIST = 4


EPS = 1e-05
HIGH = lax.Precision.HIGHEST


def extended(cells, sides, width):
    for axis, dim in sides:
        count = lax.axis_size(axis)
        ends = count - 1
        head = lax.slice_in_dim(cells, 0, width, axis=dim)
        tail = lax.slice_in_dim(cells, cells.shape[dim] - width, cells.shape[dim], axis=dim)
        cells = jnp.concatenate(
            [
                lax.ppermute(tail, axis, [(i, (i + 1) % count) for i in range(ends)]),
                cells,
                lax.ppermute(head, axis, [((i + 1) % count, i) for i in range(ends)]),
            ],
            axis=dim,
        )
    return cells


def from_behind(value, axis, steps):
    count = lax.axis_size(axis)
    pairs = [(source, (source + steps) % count) for source in range(count)]
    return lax.ppermute(value, axis, pairs)


def group_view(value_arrays):
    extent = value_arrays.shape
    return value_arrays.reshape(extent[:-1] + (GROUPS, extent[-1] // GROUPS))


def global_sums(value_arrays):
    grouped = group_view(value_arrays)
    flat = grouped.reshape(-1, GROUPS, grouped.shape[-1])
    first_sum = jnp.sum(flat, axis=(0, 2))
    second_sum = jnp.sum(flat * flat, axis=(0, 2))
    return lax.psum((first_sum, second_sum), "rows")


def apply_norm(value_arrays, sum_one, sum_two, norm_gain, norm_bias, total):
    grouped = group_view(value_arrays)
    group_mean = sum_one / total
    variance = sum_two / total - group_mean * group_mean
    inverse = lax.rsqrt(variance + EPS)
    normed = (grouped - group_mean[:, None]) * inverse[:, None]
    return normed.reshape(value_arrays.shape) * norm_gain + norm_bias


def norm_back(value_arrays, grad_one, grad_two):
    grouped = group_view(value_arrays)
    extra = grad_one[:, None] + 2.0 * grouped * grad_two[:, None]
    return extra.reshape(value_arrays.shape)


def reduce_grads(grad_one, grad_two):
    return lax.psum((grad_one, grad_two), "rows")


def conv_rows(padded, kernel):
    widened = jnp.pad(padded, ((0, 0), (1, 1), (0, 0)))
    return lax.conv_general_dilated(
        widened[None],
        kernel,
        (1, 1),
        "VALID",
        dimension_numbers=("NHWC", "HWIO", "NHWC"),
        precision=HIGH,
    )[0]


def flipped(kernel):
    return jnp.transpose(kernel[::-1, ::-1], (0, 1, 3, 2))


def pad_grads(value_arrays):
    return extended(value_arrays, (("rows", 0),), 1)


def totals_of(inputs, conv1):
    strip = inputs.shape[0]
    cells = strip * lax.axis_size("rows") * inputs.shape[1]
    return (cells * (inputs.shape[2] // GROUPS), cells * (conv1.shape[3] // GROUPS))


def block_forward(inputs, weights, scale_part, shift_part):
    norm1_gain, norm1_bias, conv1, norm2_gain, norm2_bias, conv2, conv2_bias = weights
    total_in, total_mid = totals_of(inputs, conv1)
    sums_in = global_sums(inputs)

    def pad_rows(value_arrays):
        return extended(value_arrays, (("rows", 0),), 1)

    act_one = pad_rows(
        jax.nn.gelu(
            apply_norm(inputs, sums_in[0], sums_in[1], norm1_gain, norm1_bias, total_in),
            approximate=False,
        )
    )
    middle = conv_rows(act_one, conv1)
    sums_mid = global_sums(middle)
    shaped = (
        apply_norm(middle, sums_mid[0], sums_mid[1], norm2_gain, norm2_bias, total_mid)
        * (1.0 + scale_part)
        + shift_part
    )
    act_two = pad_rows(jax.nn.gelu(shaped, approximate=False))
    branch = conv_rows(act_two, conv2) + conv2_bias
    return (branch, (sums_in[0], sums_in[1], act_one, middle, sums_mid[0], sums_mid[1], act_two))


def block_backward(inputs, weights, scale_part, shift_part, kept, grad_out):
    norm1_gain, norm1_bias, conv1, norm2_gain, norm2_bias, conv2, conv2_bias = weights
    in_one, in_two, act_one, middle, mid_one, mid_two, act_two = kept
    total_in, total_mid = totals_of(inputs, conv1)
    grad_conv2 = jax.vjp(lambda kernel: conv_rows(act_two, kernel), conv2)[1](grad_out)[0]
    grad_bias2 = jnp.sum(grad_out, axis=(0, 1))
    grad_act_two = conv_rows(pad_grads(grad_out), flipped(conv2))

    def second_piece(middle_in, sum_one, sum_two, gain_in, incoming_bias, scale_in, shift_in):
        shaped = (
            apply_norm(middle_in, sum_one, sum_two, gain_in, incoming_bias, total_mid)
            * (1.0 + scale_in)
            + shift_in
        )
        return jax.nn.gelu(shaped, approximate=False)

    second_pull = jax.vjp(
        second_piece, middle, mid_one, mid_two, norm2_gain, norm2_bias, scale_part, shift_part
    )[1](grad_act_two)
    summed_one, summed_two = reduce_grads(second_pull[1], second_pull[2])
    grad_middle = second_pull[0] + norm_back(middle, summed_one, summed_two)
    grad_conv1 = jax.vjp(lambda kernel: conv_rows(act_one, kernel), conv1)[1](grad_middle)[0]
    grad_act_one = conv_rows(pad_grads(grad_middle), flipped(conv1))

    def first_piece(inputs_in, sum_one, sum_two, gain_in, incoming_bias):
        return jax.nn.gelu(
            apply_norm(inputs_in, sum_one, sum_two, gain_in, incoming_bias, total_in),
            approximate=False,
        )

    first_pull = jax.vjp(first_piece, inputs, in_one, in_two, norm1_gain, norm1_bias)[1](
        grad_act_one
    )
    first_one, first_two = reduce_grads(first_pull[1], first_pull[2])
    grad_inputs = first_pull[0] + norm_back(inputs, first_one, first_two)
    grads = (
        first_pull[3],
        first_pull[4],
        grad_conv1,
        second_pull[3],
        second_pull[4],
        grad_conv2,
        grad_bias2,
    )
    return (grad_inputs, grads, second_pull[5], second_pull[6])


def conditioning(step_item, table):
    one_hot = (jnp.arange(table.shape[0], dtype=jnp.int32) == step_item).astype(jnp.float32)
    condition = jnp.dot(one_hot, table, precision=HIGH)
    half_width = table.shape[1] // 2
    return (condition[:half_width], condition[half_width:], one_hot)


def project_in(frames_item, mask_item, count_item, incoming_weight, incoming_bias):
    history = jnp.arange(HIST, dtype=jnp.int32) >= HIST - count_item
    keep = jnp.repeat(history, FIELDS).astype(jnp.float32)
    lifted = (
        jnp.einsum(
            "fhw,fc->hwc", frames_item * keep[:, None, None], incoming_weight, precision=HIGH
        )
        + incoming_bias
    )
    return lifted * mask_item[:, :, None].astype(jnp.float32)


def coarsen_field(value_arrays, incoming_weight, incoming_bias):
    rows_here, width_here, depth_here = value_arrays.shape
    blocks = value_arrays.reshape(rows_here // 2, 2, width_here // 2, 2, depth_here)
    return jnp.einsum("iajbk,abkc->ijc", blocks, incoming_weight, precision=HIGH) + incoming_bias


def upsample(value_arrays, incoming_weight, incoming_bias):
    result = jnp.einsum("ijk,abkc->iajbc", value_arrays, incoming_weight, precision=HIGH)
    extent = result.shape
    return result.reshape(extent[0] * 2, extent[2] * 2, extent[4]) + incoming_bias


def flatten_all(pieces):
    return jnp.concatenate([piece.reshape(-1) for piece in pieces])


def unflatten_all(flat, templates):
    pieces = []
    offset_at = 0
    for template in templates:
        count_here = template.size
        pieces.append(flat[offset_at : offset_at + count_here].reshape(template.shape))
        offset_at += count_here
    return tuple(pieces)


def strips_body(
    frames,
    counts,
    cell_mask,
    step_index,
    lift_weight,
    lift_bias,
    enc_norm1_gain,
    enc_norm1_bias,
    enc_conv1,
    enc_step_table,
    enc_norm2_gain,
    enc_norm2_bias,
    enc_conv2,
    enc_conv2_bias,
    reducer_weight,
    reducer_bias,
    up_weight,
    up_bias,
    dec_norm1_gain,
    dec_norm1_bias,
    dec_conv1,
    dec_step_table,
    dec_norm2_gain,
    dec_norm2_bias,
    dec_conv2,
    dec_conv2_bias,
    skip_weight,
    skip_bias,
    cotangent,
):
    enc_weights = (
        enc_norm1_gain,
        enc_norm1_bias,
        enc_conv1,
        enc_norm2_gain,
        enc_norm2_bias,
        enc_conv2,
        enc_conv2_bias,
    )
    dec_weights = (
        dec_norm1_gain,
        dec_norm1_bias,
        dec_conv1,
        dec_norm2_gain,
        dec_norm2_bias,
        dec_conv2,
        dec_conv2_bias,
    )
    params = (
        lift_weight,
        lift_bias,
        enc_norm1_gain,
        enc_norm1_bias,
        enc_conv1,
        enc_step_table,
        enc_norm2_gain,
        enc_norm2_bias,
        enc_conv2,
        enc_conv2_bias,
        reducer_weight,
        reducer_bias,
        up_weight,
        up_bias,
        dec_norm1_gain,
        dec_norm1_bias,
        dec_conv1,
        dec_step_table,
        dec_norm2_gain,
        dec_norm2_bias,
        dec_conv2,
        dec_conv2_bias,
        skip_weight,
        skip_bias,
    )

    def forward_micro(carry, sliced):
        frames_item, mask_item, count_item, step_item = sliced
        lifted = project_in(frames_item, mask_item, count_item, lift_weight, lift_bias)
        enc_scale, enc_shift, unused_hot = conditioning(step_item, enc_step_table)
        enc_branch, enc_kept = block_forward(lifted, enc_weights, enc_scale, enc_shift)
        encoder_result = lifted + enc_branch
        coarse_field = coarsen_field(encoder_result, reducer_weight, reducer_bias)
        foreign = from_behind(coarse_field, "section", 1)
        raised_foreign = upsample(foreign, up_weight, up_bias)
        raised = from_behind(raised_foreign, "section", 1)
        joined = jnp.concatenate([raised, encoder_result], axis=-1)
        dec_scale, dec_shift, unused_again = conditioning(step_item, dec_step_table)
        dec_branch, dec_kept = block_forward(joined, dec_weights, dec_scale, dec_shift)
        output_item = jnp.dot(joined, skip_weight, precision=HIGH) + skip_bias + dec_branch
        return (carry, (output_item, (lifted, enc_kept, encoder_result, foreign, joined, dec_kept)))

    unused, (output, kept_all) = lax.scan(
        forward_micro, jnp.zeros((), jnp.float32), (frames, cell_mask, counts, step_index)
    )

    def backward_micro(totals, sliced):
        frames_item, mask_item, count_item, step_item, grad_out, kept = sliced
        lifted, enc_kept, encoder_result, foreign, joined, dec_kept = kept
        dec_scale, dec_shift, one_hot = conditioning(step_item, dec_step_table)
        grad_joined, dec_grads, dec_gscale, dec_gshift = block_backward(
            joined, dec_weights, dec_scale, dec_shift, dec_kept, grad_out
        )
        grad_skip_weight = jnp.einsum("hwk,hwc->kc", joined, grad_out, precision=HIGH)
        grad_skip_bias = jnp.sum(grad_out, axis=(0, 1))
        grad_joined = grad_joined + jnp.dot(grad_out, skip_weight.T, precision=HIGH)
        half_width = joined.shape[-1] // 2
        grad_raised = grad_joined[..., :half_width]
        grad_encoded = grad_joined[..., half_width:]
        grad_foreign_up = from_behind(grad_raised, "section", 1)
        up_pull = jax.vjp(upsample, foreign, up_weight, up_bias)[1](grad_foreign_up)
        coarse_gradient = from_behind(up_pull[0], "section", 1)
        reducer_pullback = jax.vjp(coarsen_field, encoder_result, reducer_weight, reducer_bias)[1](
            coarse_gradient
        )
        grad_encoded = grad_encoded + reducer_pullback[0]
        enc_scale, enc_shift, enc_hot = conditioning(step_item, enc_step_table)
        grad_lifted, enc_grads, enc_gscale, enc_gshift = block_backward(
            lifted, enc_weights, enc_scale, enc_shift, enc_kept, grad_encoded
        )
        grad_lifted = grad_lifted + grad_encoded
        proj_pull = jax.vjp(
            lambda frames_in, incoming_weight, incoming_bias: project_in(
                frames_in, mask_item, count_item, incoming_weight, incoming_bias
            ),
            frames_item,
            lift_weight,
            lift_bias,
        )[1](grad_lifted)
        enc_table_grad = enc_hot[:, None] * jnp.concatenate([enc_gscale, enc_gshift])[None, :]
        dec_table_grad = one_hot[:, None] * jnp.concatenate([dec_gscale, dec_gshift])[None, :]
        micro_list = (
            proj_pull[1],
            proj_pull[2],
            enc_grads[0],
            enc_grads[1],
            enc_grads[2],
            enc_table_grad,
            enc_grads[3],
            enc_grads[4],
            enc_grads[5],
            enc_grads[6],
            reducer_pullback[1],
            reducer_pullback[2],
            up_pull[1],
            up_pull[2],
            dec_grads[0],
            dec_grads[1],
            dec_grads[2],
            dec_table_grad,
            dec_grads[3],
            dec_grads[4],
            dec_grads[5],
            dec_grads[6],
            grad_skip_weight,
            grad_skip_bias,
        )
        micro_flat = flatten_all(micro_list)
        return (totals + micro_flat, proj_pull[0])

    total_size = sum((piece.size for piece in params))
    start_totals = jnp.zeros((total_size,), jnp.float32)
    flat_totals, frames_grad = lax.scan(
        backward_micro,
        start_totals,
        (frames, cell_mask, counts, step_index, cotangent, kept_all),
        reverse=True,
    )
    flat_totals = lax.psum(flat_totals, ("section", "batch", "rows"))
    grads = unflatten_all(flat_totals, params)
    return (output, frames_grad) + grads


F32 = jnp.float32
BF16 = jnp.bfloat16
MESH = pl.DeviceIdType.MESH
NN = ((1,), (0,))
NT = ((1,), (1,))
TN = ((0,), (0,))
HIGH_AT = (0, 2, 1)
LOW_AT = (4, 3, 5)
CHUNK = 512
class Given(NamedTuple):
    frames: Any
    counts: Any
    cell_mask: Any
    step_index: Any
    lift_weight: Any
    lift_bias: Any
    enc_norm1_gain: Any
    enc_norm1_bias: Any
    enc_conv1: Any
    enc_step_table: Any
    enc_norm2_gain: Any
    enc_norm2_bias: Any
    enc_conv2: Any
    enc_conv2_bias: Any
    reducer_weight: Any
    reducer_bias: Any
    up_weight: Any
    up_bias: Any
    dec_norm1_gain: Any
    dec_norm1_bias: Any
    dec_conv1: Any
    dec_step_table: Any
    dec_norm2_gain: Any
    dec_norm2_bias: Any
    dec_conv2: Any
    dec_conv2_bias: Any
    skip_weight: Any
    skip_bias: Any
    cotangent: Any


ARGUMENTS = Given._fields
LARGE = tuple(dict(
    dec_conv2=0,
    skip_weight=0,
    dec_conv1=0,
    up_weight=0,
    reducer_weight=0,
    enc_conv2=0,
    enc_conv1=0,
))
IN_HBM = tuple(dict(frames=0, cell_mask=0, cotangent=0)) + LARGE
IN_SMEM = tuple(dict(counts=0, step_index=0))
SMALL_ROWS = dict(
    lift_weight=(0, 12),
    lift_bias=(12, 1),
    enc_norm1_gain=(16, 1),
    enc_norm1_bias=(17, 1),
    enc_norm2_gain=(18, 1),
    enc_norm2_bias=(19, 1),
    enc_conv2_bias=(20, 1),
    reducer_bias=(21, 1),
    up_bias=(22, 1),
    dec_conv2_bias=(23, 1),
    skip_bias=(23, 1),
    dec_norm1_gain=(24, 2),
    dec_norm1_bias=(26, 2),
    dec_norm2_gain=(28, 1),
    dec_norm2_bias=(29, 1),
    enc_step_table=(32, 8),
    dec_step_table=(40, 8),
)
SMALL_COUNT = 64
OUTPUTS = tuple(dict(output=0, frames_grad=0, gradients=0))


def split(value):
    high = value.astype(BF16)
    return high, (value - high.astype(F32)).astype(BF16)


def dot(left, right, dims=NN, precision=None):
    return lax.dot_general(
        left, right, (dims, ((), ())), precision=precision, preferred_element_type=F32
    )


def fold(value):
    half = value.shape[1] // 2
    return value[:, :half] + value[:, half:]


def fold_rows(value):
    half = value.shape[0] // 2
    return value[:half] + value[half:]


def tile_sums(value):
    return jnp.sum(value.reshape(-1, 8, value.shape[-1]), axis=0)


def column_sum(tiles):
    return jnp.sum(tiles, axis=0, keepdims=True)


def group_ones(channels, size):
    rows = lax.broadcasted_iota(jnp.int32, (channels, channels), 0) // size
    columns = lax.broadcasted_iota(jnp.int32, (channels, channels), 1) // size
    return (rows == columns).astype(F32)


def group_sums(first, second, ones):
    both = dot(jnp.concatenate([first, second], axis=0), ones, precision=HIGH)
    return column_sum(both[:8]), column_sum(both[8:])


class Exchange:

    def __init__(self, place, start, rows, landing, first_sem):
        self.place, self.start, self.rows, self.landing = place, start, rows, landing
        self.sem = first_sem
        self.stage = 0
        self.copies = []
        line = place.line
        self.at = [start]
        size = rows
        for bit in (place.core, place.first, place.second):
            size //= 2
            self.at.append(self.at[-1] + bit * size)
        self.shard = size // line
        self.at.append(self.at[-1] + place.row * self.shard)

    def count(self):
        return 6 + 2 * (self.place.line - 1)

    def _copy(self, source, target, device):
        place = self.place
        copy = pltpu.make_async_remote_copy(
            src_ref=source,
            dst_ref=target,
            send_sem=place.send.at[self.sem],
            recv_sem=place.recv.at[self.sem],
            device_id=device,
            device_id_type=MESH,
        )
        self.sem += 1
        copy.start()
        self.copies.append(copy)
        return copy

    def _halve(self, level):
        place = self.place
        size = self.rows >> (level + 1)
        bit = (place.core, place.first, place.second)[level]
        other = pl.multiple_of(self.at[level] + (1 - bit) * size, 8)
        self.land = self.landing
        self.landing += size
        self.waiting = [
            self._copy(
                place.sums.at[pl.ds(other, size)],
                place.landing.at[pl.ds(self.land, size)],
                place.partners[level],
            )
        ]

    def _add(self, level):
        place = self.place
        size = self.rows >> (level + 1)
        block = 128 >> level
        sums, landing = place.sums, place.landing
        base = self.at[level + 1]
        land = self.land

        def step(i, carry):
            here = pl.ds(pl.multiple_of(base + i * block, 8), block)
            there = pl.ds(pl.multiple_of(land + i * block, 8), block)
            sums[here] = sums[here] + landing[there]
            return carry

        lax.fori_loop(0, size // block, step, 0)

    def _wait(self):
        for copy in self.waiting:
            copy.wait_recv()

    def _spread(self, level):
        place = self.place
        size = self.rows >> (level + 1)
        here = pl.ds(pl.multiple_of(self.at[level + 1], 8), size)
        self.waiting = [
            self._copy(
                place.final.at[here], place.final.at[here], place.partners[level]
            )
        ]

    def advance(self):
        place = self.place
        line, row = place.line, place.row
        shard = self.shard
        stage = self.stage
        self.stage += 1
        if stage == 0:
            self._halve(0)
        elif stage in (1, 2):
            self._wait()
            self._add(stage - 1)
            self._halve(stage)
        elif stage == 3:
            self._wait()
            self._add(2)
            self.waiting = []
            self.land = self.landing
            for k in range(1, line):
                to = lax.rem(row + k, line)
                source = pl.ds(pl.multiple_of(self.at[3] + to * shard, 8), shard)
                target = pl.ds(self.landing, shard)
                self.landing += shard
                self.waiting.append(
                    self._copy(
                        place.sums.at[source],
                        place.landing.at[target],
                        place.device_at(to),
                    )
                )
        elif stage == 4:
            self._wait()
            here = pl.ds(pl.multiple_of(self.at[4], 8), shard)
            total = place.sums[here]
            for k in range(line - 1):
                total = total + place.landing[pl.ds(self.land + k * shard, shard)]
            place.final[here] = total
            self.waiting = []
            for k in range(1, line):
                self.waiting.append(
                    self._copy(
                        place.final.at[here],
                        place.final.at[here],
                        place.device_at(lax.rem(row + k, line)),
                    )
                )
        elif stage in (5, 6, 7):
            self._wait()
            self._spread(7 - stage)
        else:
            self._wait()

    def done(self):
        return self.stage > 8


def layout_of(shapes):
    starts = {}
    at = 0
    for name in LARGE:
        starts[name] = at
        at += shapes[name][0]
    small = at
    unit = 256
    total = -(-(at + SMALL_COUNT) // unit) * unit
    begins = SimpleNamespace(**starts)
    ready = (
        begins.dec_conv1,
        begins.up_weight,
        begins.enc_conv2,
        begins.enc_conv1,
        small,
    )
    edges = [0] + [edge // unit * unit for edge in ready] + [total]
    runs = [(a, b - a) for a, b in zip(edges[:-1], edges[1:])]
    return starts, small, total, runs


def item_kernel(sizes, scratch_names, *refs):
    line, strip, width, shapes, big_layout = sizes
    begins, small_at, total_rows, runs = big_layout
    starts = SimpleNamespace(**begins)
    inputs = Given(*refs[: len(ARGUMENTS)])
    refs = refs[len(ARGUMENTS) :]
    output_names = OUTPUTS
    outputs = SimpleNamespace(**dict(zip(output_names, refs)))
    scratch = SimpleNamespace(**dict(zip(scratch_names, refs[len(output_names) :])))

    def w_of(name):
        return getattr(scratch, name)

    height = strip * line
    cells = height * width
    c = inputs.lift_weight.shape[1]
    strip_cells = strip * width
    history = inputs.frames.shape[1]

    core = lax.axis_index("section")
    plane = lax.axis_index("batch")
    row = lax.axis_index("rows")
    y, x = plane // 2, lax.rem(plane, 2)
    along_x = plane + 1 - 2 * x
    along_y = plane + 2 - 4 * y
    place = SimpleNamespace(
        line=line,
        row=row,
        core=core,
        first=x * (1 - core) + y * core,
        second=y * (1 - core) + x * core,
        partners=(
            (1 - core, plane, row),
            (core, along_x * (1 - core) + along_y * core, row),
            (core, along_y * (1 - core) + along_x * core, row),
        ),
        device_at=lambda to: (core, plane, to),
        sums=scratch.sums,
        final=scratch.final,
        landing=scratch.landing,
        send=scratch.send,
        recv=scratch.recv,
    )
    local_sem = scratch.local

    weight_copies = {}
    for k, name in enumerate(LARGE):
        copy = pltpu.make_async_copy(getattr(inputs, name), w_of(name), local_sem.at[k])
        weight_copies[name] = copy
        copy.start()
    frames_in, mask_in, cot = scratch.frames_in, scratch.mask_in, scratch.cot
    here_rows = pl.ds(pl.multiple_of(row * strip_cells, strip_cells), strip_cells)
    own = (
        pltpu.make_async_copy(inputs.frames.at[row], frames_in.at[row], local_sem.at[7]),
        pltpu.make_async_copy(inputs.cell_mask.at[row], mask_in.at[row], local_sem.at[8]),
        pltpu.make_async_copy(
            inputs.cotangent.at[row], cot.at[here_rows], local_sem.at[9]
        ),
    )
    for copy in own:
        copy.start()

    barrier = pltpu.get_barrier_semaphore()
    peers = [place.device_at(lax.rem(row + k, line)) for k in range(1, line)]
    for device in tuple(peers) + place.partners:
        pl.semaphore_signal(barrier, inc=1, device_id=device, device_id_type=MESH)
    pl.semaphore_wait(barrier, len(peers) + 3)

    next_sem = 0

    def send(source, target, device):
        nonlocal next_sem
        copy = pltpu.make_async_remote_copy(
            src_ref=source,
            dst_ref=target,
            send_sem=scratch.send.at[next_sem],
            recv_sem=scratch.recv.at[next_sem],
            device_id=device,
            device_id_type=MESH,
        )
        next_sem += 1
        copy.start()
        return copy

    frame_copies, cot_copies, output_copies = [], [], []
    for k in range(1, line):
        to = lax.rem(row + k, line)
        device = place.device_at(to)
        frame_copies.append(send(inputs.frames.at[to], frames_in.at[row], device))
        frame_copies.append(send(inputs.cell_mask.at[to], mask_in.at[row], device))
    for k in range(1, line):
        to = lax.rem(row + k, line)
        cot_copies.append(
            send(inputs.cotangent.at[to], cot.at[here_rows], place.device_at(to))
        )

    copied = SimpleNamespace(**weight_copies)
    def stack_conv(source, half, depth, forward, backward):
        for a in range(3):
            for b in range(3):
                at = (3 * a + b) * depth + half * c
                high, low = split(source[at : at + c, :])
                for block in (HIGH_AT[b], LOW_AT[b]):
                    rows = slice((6 * a + block) * c, (6 * a + block + 1) * c)
                    forward[rows, 0:c] = high
                    forward[rows, c : 2 * c] = low
                for block in (HIGH_AT[2 - b], LOW_AT[2 - b]):
                    tap = 6 * (2 - a) + block
                    columns = slice(tap * c, (tap + 1) * c)
                    backward[0:c, columns] = high
                    backward[c : 2 * c, columns] = low

    copied.enc_conv1.wait()
    stack_conv(scratch.enc_conv1, 0, c, scratch.fe1, scratch.be1)
    copied.enc_conv2.wait()
    stack_conv(scratch.enc_conv2, 0, c, scratch.fe2, scratch.be2)
    copied.reducer_weight.wait()
    for k in range(4):
        high, low = split(scratch.reducer_weight[k * c : (k + 1) * c, :])
        for block in (k, k + 4):
            scratch.f_down[block * c : (block + 1) * c, 0:c] = high
            scratch.f_down[block * c : (block + 1) * c, c : 2 * c] = low
        for block in (0, 1):
            columns = slice(block * c, (block + 1) * c)
            scratch.b_down[k, 0:c, columns] = high
            scratch.b_down[k, c : 2 * c, columns] = low
    copied.up_weight.wait()
    for k in range(4):
        high, low = split(scratch.up_weight[k * c : (k + 1) * c, :])
        for block in (0, 1):
            rows = slice(block * c, (block + 1) * c)
            scratch.f_up[k, rows, 0:c] = high
            scratch.f_up[k, rows, c : 2 * c] = low
        for block in (k, k + 4):
            columns = slice(block * c, (block + 1) * c)
            scratch.b_up[0:c, columns] = high
            scratch.b_up[c : 2 * c, columns] = low
    copied.dec_conv1.wait()
    stack_conv(scratch.dec_conv1, 0, 2 * c, scratch.fd1a, scratch.bd1a)
    stack_conv(scratch.dec_conv1, 1, 2 * c, scratch.fd1b, scratch.bd1b)
    copied.dec_conv2.wait()
    stack_conv(scratch.dec_conv2, 0, c, scratch.fd2, scratch.bd2)
    copied.skip_weight.wait()
    for half in range(2):
        high, low = split(scratch.skip_weight[half * c : (half + 1) * c, :])
        for block in (half, half + 2):
            scratch.f_skip[block * c : (block + 1) * c, 0:c] = high
            scratch.f_skip[block * c : (block + 1) * c, c : 2 * c] = low
        for block in (0, 1):
            columns = slice(block * c, (block + 1) * c)
            scratch.b_skip[half, 0:c, columns] = high
            scratch.b_skip[half, c : 2 * c, columns] = low

    for buffer in (scratch.xe1, scratch.xe2, scratch.xd1a, scratch.xd1b, scratch.xd2, scratch.xg):
        edge = jnp.zeros((width, 6 * c), BF16)
        buffer[0:width, :] = edge
        buffer[cells + width : cells + 2 * width, :] = edge

    lift = scratch.lift
    lift[...] = jnp.zeros(lift.shape, F32)
    lift[0:history, :] = inputs.lift_weight[...]
    lift[history : history + 1, :] = inputs.lift_bias[...]

    block = 2 * width
    column = lax.rem(lax.broadcasted_iota(jnp.int32, (block, c), 0), width)
    at_first, at_last = column == 0, column == width - 1
    zeros8 = jnp.zeros((8, c), F32)
    ones16 = group_ones(c, c // GROUPS)
    ones32 = group_ones(c, 2 * c // GROUPS)
    count16 = float(cells * (c // GROUPS))
    count32 = float(cells * (2 * c // GROUPS))

    def grid_rows(step, carry=0):
        return lax.fori_loop(0, cells // block, step, carry, unroll=2)

    def row_at(h):
        return pl.ds(pl.multiple_of(h * block, block), block)

    def chunk_at(i):
        return pl.ds(pl.multiple_of(i * CHUNK, CHUNK), CHUNK)

    def put_row(target, h, value):
        rows = pl.ds(pl.multiple_of(h * block + width, width), block)
        left = jnp.where(at_first, 0.0, pltpu.roll(value, 1, 0))
        right = jnp.where(at_last, 0.0, pltpu.roll(value, block - 1, 0))
        for b, piece in enumerate((left, value, right)):
            high, low = split(piece)
            target[rows, HIGH_AT[b] * c : (HIGH_AT[b] + 1) * c] = high
            target[rows, LOW_AT[b] * c : (LOW_AT[b] + 1) * c] = low

    def put_turned(target, columns, value, first=0, second=1):
        high, low = split(value.T)
        target[first * c : (first + 1) * c, columns] = high
        target[second * c : (second + 1) * c, columns] = low

    def conv_chunk(pairs, i, dims=NN):
        total = None
        for data, weight in pairs:
            taps = []
            for a in range(3):
                rows = pl.ds(pl.multiple_of(i * CHUNK + a * width, width), CHUNK)
                taps.append(data[rows, :])
            part = dot(jnp.concatenate(taps, axis=1), weight[...], dims)
            total = part if total is None else total + part
        return total

    def norm_of(first, second, ones, count):
        one, two = group_sums(first, second, ones)
        mean = one / count
        return mean, lax.rsqrt(two / count - mean * mean + EPS)

    def activate(source, target, turned, slope, scale, shift):
        def step(h, carry):
            value = source[row_at(h), :] * scale + shift
            below = 0.5 + 0.5 * lax.erf(value * 0.7071067811865476)
            slope[row_at(h), :] = below + value * (
                0.3989422804014327 * jnp.exp(-0.5 * value * value)
            )
            value = value * below
            put_row(target, h, value)
            put_turned(turned, row_at(h), value)
            return carry

        grid_rows(step)

    def conv_norm(pairs, target):
        def step(i, carry):
            value = fold(conv_chunk(pairs, i))
            target[chunk_at(i), :] = value
            return carry[0] + tile_sums(value), carry[1] + tile_sums(value * value)

        return lax.fori_loop(0, cells // CHUNK, step, (zeros8, zeros8))

    def sums_of(source):
        def step(h, carry):
            value = source[row_at(h), :]
            return carry[0] + tile_sums(value), carry[1] + tile_sums(value * value)

        return grid_rows(step, (zeros8, zeros8))

    step_here = jnp.full((1, c), inputs.step_index[row], jnp.int32)

    def condition(table):
        total = jnp.zeros((1, 2 * c), F32)
        chosen = jnp.concatenate([step_here, step_here], axis=1)
        for s in range(table.shape[0]):
            total = total + jnp.where(chosen == s, table[s : s + 1, :], 0.0)
        return total[:, :c], total[:, c:]

    for copy in own[:2]:
        copy.wait()
    for copy in frame_copies:
        copy.wait_recv()
    fields = scratch.fields
    fields[...] = jnp.zeros(fields.shape, F32)
    frame_of = lax.broadcasted_iota(jnp.int32, (history, width), 0) // FIELDS
    keep = (frame_of >= HIST - inputs.counts[row]).astype(F32)
    masks = []
    for source in range(line):
        for k in range(strip):
            columns = slice((source * strip + k) * width, (source * strip + k + 1) * width)
            mask = mask_in[source, k : k + 1, :].astype(F32)
            masks.append(mask)
            fields[0:history, columns] = frames_in[source, :, k, :] * keep * mask
            fields[history : history + 1, columns] = mask
    lifted = scratch.lifted
    lifted[...] = dot(fields[...], lift[...], TN, HIGH)

    enc_scale, enc_shift = condition(inputs.enc_step_table)
    dec_scale, dec_shift = condition(inputs.dec_step_table)

    mean_e1, inv_e1 = norm_of(*sums_of(lifted), ones16, count16)
    gain_e1, bias_e1 = inputs.enc_norm1_gain[...], inputs.enc_norm1_bias[...]
    a_e1 = inv_e1 * gain_e1
    activate(lifted, scratch.xe1, scratch.te1, scratch.slope_e1, a_e1, bias_e1 - mean_e1 * a_e1)
    middle_e = scratch.middle_e
    mean_e2, inv_e2 = norm_of(
        *conv_norm([(scratch.xe1, scratch.fe1)], middle_e), ones16, count16
    )
    gain_e2, bias_e2 = inputs.enc_norm2_gain[...], inputs.enc_norm2_bias[...]
    a_e2 = inv_e2 * gain_e2
    activate(
        middle_e,
        scratch.xe2,
        scratch.te2,
        scratch.slope_e2,
        a_e2 * (1.0 + enc_scale),
        (bias_e2 - mean_e2 * a_e2) * (1.0 + enc_scale) + enc_shift,
    )
    encoded = scratch.encoded
    conv2_bias = inputs.enc_conv2_bias[...]
    joined = scratch.joined

    def encode(i, carry):
        value = fold(conv_chunk([(scratch.xe2, scratch.fe2)], i))
        value = value + conv2_bias + lifted[chunk_at(i), :]
        encoded[chunk_at(i), :] = value
        high, low = split(value)
        joined[chunk_at(i), c : 2 * c] = high
        joined[chunk_at(i), 3 * c : 4 * c] = low
        put_turned(scratch.turned, chunk_at(i), value, 1, 3)
        return carry[0] + tile_sums(value), carry[1] + tile_sums(value * value)

    sums_enc = lax.fori_loop(0, cells // CHUNK, encode, (zeros8, zeros8))

    half_cells, quarter = cells // 2, cells // 4

    def pick(source):
        pieces = []
        for b in range(2):
            value = source[pl.ds(b, half_cells, stride=2), :]
            value = value.reshape(height // 2, 2, width // 2, c)
            pieces.append([value[:, a].reshape(quarter, c) for a in range(2)])
        return [pieces[b][a] for a in range(2) for b in range(2)]

    def place_cells(target, pieces):
        for b in range(2):
            both = [pieces[2 * a + b].reshape(height // 2, 1, width // 2, c) for a in range(2)]
            value = jnp.concatenate(both, axis=1).reshape(half_cells, c)
            target[pl.ds(b, half_cells, stride=2), :] = value

    x_down = scratch.x_down
    for k, piece in enumerate(pick(encoded)):
        high, low = split(piece)
        x_down[:, k * c : (k + 1) * c] = high
        x_down[:, (k + 4) * c : (k + 5) * c] = low
    lowered = fold(dot(x_down[...], scratch.f_down[...])) + inputs.reducer_bias[...]
    x_up = scratch.x_up
    high, low = split(lowered)
    x_up[:, 0:c] = high
    x_up[:, c : 2 * c] = low
    raised = scratch.raised
    up_bias = inputs.up_bias[...]
    place_cells(
        raised, [fold(dot(x_up[...], scratch.f_up[k])) + up_bias for k in range(4)]
    )

    def raise_row(h, carry):
        value = raised[row_at(h), :]
        high, low = split(value)
        joined[row_at(h), 0:c] = high
        joined[row_at(h), 2 * c : 3 * c] = low
        put_turned(scratch.turned, row_at(h), value, 0, 2)
        return carry[0] + tile_sums(value), carry[1] + tile_sums(value * value)

    sums_raised = grid_rows(raise_row, (zeros8, zeros8))

    halves = []
    for half, (source, sums) in enumerate(((raised, sums_raised), (encoded, sums_enc))):
        mean, inv = norm_of(*sums, ones32, count32)
        gain = inputs.dec_norm1_gain[half : half + 1, :]
        bias = inputs.dec_norm1_bias[half : half + 1, :]
        scale = inv * gain
        activate(
            source,
            (scratch.xd1a, scratch.xd1b)[half],
            (scratch.td1a, scratch.td1b)[half],
            (scratch.slope_d1a, scratch.slope_d1b)[half],
            scale,
            bias - mean * scale,
        )
        halves.append((source, mean, inv, gain))
    middle_d = scratch.middle_d
    pairs = [(scratch.xd1a, scratch.fd1a), (scratch.xd1b, scratch.fd1b)]
    mean_d2, inv_d2 = norm_of(*conv_norm(pairs, middle_d), ones16, count16)
    gain_d2, bias_d2 = inputs.dec_norm2_gain[...], inputs.dec_norm2_bias[...]
    a_d2 = inv_d2 * gain_d2
    activate(
        middle_d,
        scratch.xd2,
        scratch.td2,
        scratch.slope_d2,
        a_d2 * (1.0 + dec_scale),
        (bias_d2 - mean_d2 * a_d2) * (1.0 + dec_scale) + dec_shift,
    )
    result = scratch.result
    last_bias = inputs.dec_conv2_bias[...] + inputs.skip_bias[...]

    def decode(i, carry):
        value = conv_chunk([(scratch.xd2, scratch.fd2)], i)
        value = value + dot(joined[chunk_at(i), :], scratch.f_skip[...])
        result[chunk_at(i), :] = fold(value) + last_bias
        return carry

    lax.fori_loop(0, cells // CHUNK, decode, 0)
    own_output = pltpu.make_async_copy(
        result.at[here_rows], outputs.output.at[row], local_sem.at[10]
    )
    own_output.start()
    for k in range(1, line):
        to = lax.rem(row + k, line)
        there = pl.ds(pl.multiple_of(to * strip_cells, strip_cells), strip_cells)
        output_copies.append(
            send(result.at[there], outputs.output.at[row], place.device_at(to))
        )

    exchanges = []
    waiting_runs = list(runs)
    landing_at = 0
    sem_at = 4 * (line - 1) + 2 * (line - 1)
    sums, final = scratch.sums, scratch.final

    def begin():
        nonlocal landing_at, sem_at
        start, rows = waiting_runs.pop(0)
        exchange = Exchange(place, start, rows, landing_at, sem_at)
        landing_at += rows - rows // (8 * line)
        sem_at += exchange.count()
        exchanges.append(exchange)
        exchange.advance()

    final_copies = []

    def publish():
        for k, exchange in enumerate(exchanges):
            if k == len(final_copies) and exchange.done():
                rows = pl.ds(exchange.start, exchange.rows)
                copy = pltpu.make_async_copy(
                    final.at[rows], outputs.gradients.at[rows], local_sem.at[11 + k]
                )
                copy.start()
                final_copies.append(copy)

    def tick():
        for exchange in exchanges:
            if not exchange.done():
                exchange.advance()
        publish()

    def small_row(k, value):
        sums[small_at + k : small_at + k + 1, :] = value

    def spread_grad(source):
        def step(h, carry):
            value = source[row_at(h), :]
            put_row(scratch.xg, h, value)
            return carry + tile_sums(value)

        return grid_rows(step, zeros8)

    def weight_grad(turned, at, depth):
        lhs = turned[...]
        for a in range(3):
            rows = pl.ds((2 - a) * width, cells)
            part = fold_rows(dot(lhs, scratch.xg[rows, :]))
            for b in range(3):
                high, low = HIGH_AT[2 - b] * c, LOW_AT[2 - b] * c
                to = at + (3 * a + b) * depth
                sums[to : to + c, :] = part[:, high : high + c] + part[:, low : low + c]

    def back_conv(weight, slope, target, source, mean, inv):
        def step(i, carry):
            value = fold(conv_chunk([(scratch.xg, weight)], i, NT)) * slope[chunk_at(i), :]
            target[chunk_at(i), :] = value
            normed = (source[chunk_at(i), :] - mean) * inv
            return carry[0] + tile_sums(value), carry[1] + tile_sums(value * normed)

        return lax.fori_loop(0, cells // CHUNK, step, (zeros8, zeros8))

    def norm_grad(sums_in, scale, ones, count):
        one, two = group_sums(sums_in[0] * scale, sums_in[1] * scale, ones)
        return one / count, two / count

    own[2].wait()
    for copy in cot_copies:
        copy.wait_recv()
    total_cot = column_sum(spread_grad(cot))
    weight_grad(scratch.td2, starts.dec_conv2, c)
    part = fold(dot(scratch.turned[...], scratch.xg[width : cells + width, 2 * c : 4 * c]))
    sums[starts.skip_weight : starts.skip_weight + 2 * c, :] = fold_rows(part)
    small_row(23, total_cot)
    begin()

    grad = scratch.grad
    sums_d2 = back_conv(scratch.bd2, scratch.slope_d2, grad, middle_d, mean_d2, inv_d2)
    side_grads = (scratch.grad_a, scratch.grad_b)
    for half in range(2):

        def skip_back(i, carry, half=half):
            rows = pl.ds(pl.multiple_of(i * CHUNK + width, width), CHUNK)
            value = dot(scratch.xg[rows, 2 * c : 4 * c], scratch.b_skip[half], NT)
            side_grads[half][chunk_at(i), :] = fold(value)
            return carry

        lax.fori_loop(0, cells // CHUNK, skip_back, 0)
    tick()

    def table_rows(k, sums_in, gain, bias, one_plus):
        plain, times = column_sum(sums_in[0]), column_sum(sums_in[1])
        for s in range(inputs.enc_step_table.shape[0]):
            small_row(k + 2 * s, jnp.where(step_here == s, gain * times + bias * plain, 0.0))
            small_row(k + 2 * s + 1, jnp.where(step_here == s, plain, 0.0))
        return one_plus * times, one_plus * plain

    def middle_grad(source, mean, inv, scale, sums_in):
        zero, slope = norm_grad(sums_in, scale, ones16, count16)

        def step(h, carry):
            normed = (source[row_at(h), :] - mean) * inv
            value = inv * (grad[row_at(h), :] * scale - zero - normed * slope)
            put_row(scratch.xg, h, value)
            return carry

        grid_rows(step)

    gain_row, bias_row = table_rows(40, sums_d2, gain_d2, bias_d2, 1.0 + dec_scale)
    small_row(28, gain_row)
    small_row(29, bias_row)
    middle_grad(middle_d, mean_d2, inv_d2, gain_d2 * (1.0 + dec_scale), sums_d2)
    weight_grad(scratch.td1a, starts.dec_conv1, 2 * c)
    tick()
    weight_grad(scratch.td1b, starts.dec_conv1 + c, 2 * c)
    begin()

    for half, (source, mean, inv, gain) in enumerate(halves):
        sums_in = back_conv(
            (scratch.bd1a, scratch.bd1b)[half],
            (scratch.slope_d1a, scratch.slope_d1b)[half],
            grad,
            source,
            mean,
            inv,
        )
        small_row(24 + half, column_sum(sums_in[1]))
        small_row(26 + half, column_sum(sums_in[0]))
        zero, slope = norm_grad(sums_in, gain, ones32, count32)
        target = side_grads[half]

        def input_grad(h, carry):
            normed = (source[row_at(h), :] - mean) * inv
            value = inv * (grad[row_at(h), :] * gain - zero - normed * slope)
            value = target[row_at(h), :] + value
            target[row_at(h), :] = value
            return carry + tile_sums(value)

        total = grid_rows(input_grad, zeros8)
        if half == 0:
            small_row(22, column_sum(total))
        tick()

    grad_raised, grad_encoded = side_grads
    x_grad_up = scratch.x_grad_up
    for k, piece in enumerate(pick(grad_raised)):
        high, low = split(piece)
        x_grad_up[:, k * c : (k + 1) * c] = high
        x_grad_up[:, (k + 4) * c : (k + 5) * c] = low
    grad_lowered = fold(dot(x_grad_up[...], scratch.b_up[...], NT))
    small_row(21, jnp.sum(grad_lowered, axis=0, keepdims=True))
    x_grad_low = scratch.x_grad_low
    high, low = split(grad_lowered)
    x_grad_low[:, 0:c] = high
    x_grad_low[:, c : 2 * c] = low
    part = fold(fold_rows(dot(x_up[...], x_grad_up[...], TN)))
    for k in range(4):
        at = starts.up_weight + k * c
        sums[at : at + c, :] = part[:, k * c : (k + 1) * c]
    part = fold_rows(fold(dot(x_down[...], x_grad_low[...], TN)))
    sums[starts.reducer_weight : starts.reducer_weight + 4 * c, :] = part
    begin()
    place_cells(
        grad, [fold(dot(x_grad_low[...], scratch.b_down[k], NT)) for k in range(4)]
    )

    def join_row(h, carry):
        value = grad_encoded[row_at(h), :] + grad[row_at(h), :]
        grad_encoded[row_at(h), :] = value
        put_row(scratch.xg, h, value)
        return carry + tile_sums(value)

    small_row(20, column_sum(grid_rows(join_row, zeros8)))
    tick()
    weight_grad(scratch.te2, starts.enc_conv2, c)
    begin()
    sums_e2 = back_conv(scratch.be2, scratch.slope_e2, grad, middle_e, mean_e2, inv_e2)
    gain_row, bias_row = table_rows(32, sums_e2, gain_e2, bias_e2, 1.0 + enc_scale)
    small_row(18, gain_row)
    small_row(19, bias_row)
    middle_grad(middle_e, mean_e2, inv_e2, gain_e2 * (1.0 + enc_scale), sums_e2)
    tick()
    weight_grad(scratch.te1, starts.enc_conv1, c)
    begin()
    tick()
    sums_e1 = back_conv(scratch.be1, scratch.slope_e1, grad, lifted, mean_e1, inv_e1)
    small_row(16, column_sum(sums_e1[1]))
    small_row(17, column_sum(sums_e1[0]))
    zero, slope = norm_grad(sums_e1, gain_e1, ones16, count16)

    def lifted_grad(h, carry):
        normed = (lifted[row_at(h), :] - mean_e1) * inv_e1
        value = inv_e1 * (grad[row_at(h), :] * gain_e1 - zero - normed * slope)
        grad[row_at(h), :] = grad_encoded[row_at(h), :] + value
        return carry

    grid_rows(lifted_grad)
    tick()

    sums[small_at : small_at + 16, :] = dot(fields[...], grad[...], NN, HIGH)
    for k in (30, 31):
        small_row(k, jnp.zeros((1, c), F32))
    rest = small_at + 48
    sums[rest:total_rows, :] = jnp.zeros((total_rows - rest, c), F32)
    begin()
    back = dot(lift[...], grad[...], NT, HIGH)
    frames_out = scratch.frames_out
    for source in range(line):
        for k in range(strip):
            h = source * strip + k
            value = back[0:history, h * width : (h + 1) * width]
            frames_out[source, :, k, :] = value * keep * masks[h]
    own_frames = pltpu.make_async_copy(
        frames_out.at[row], outputs.frames_grad.at[row], local_sem.at[18]
    )
    own_frames.start()
    for k in range(1, line):
        to = lax.rem(row + k, line)
        output_copies.append(
            send(frames_out.at[to], outputs.frames_grad.at[row], place.device_at(to))
        )

    while not all(exchange.done() for exchange in exchanges):
        tick()

    for copy in output_copies:
        copy.wait_recv()
    own_output.wait()
    own_frames.wait()
    for copy in final_copies:
        copy.wait()
    for copy in frame_copies + cot_copies + output_copies:
        copy.wait_send()
    for exchange in exchanges:
        for copy in exchange.copies:
            copy.wait_send()


def write_kernel(layout, *refs):
    shapes, starts, small_at = layout
    output, frames_grad, gradients = refs[:3]
    outputs = refs[3:-4]
    output_here, frames_here, gradients_here, sem = refs[-4:]
    c = gradients.shape[1]
    moves = [(frames_grad, frames_here, outputs[1])]
    for k, name in enumerate(LARGE):
        rows = pl.ds(starts[name], shapes[name][0])
        moves.append((gradients.at[rows], gradients_here.at[rows], outputs[2 + k]))
    moves.append((output, output_here, outputs[0]))
    small = pl.ds(small_at, SMALL_COUNT)
    first = pltpu.make_async_copy(gradients.at[small], gradients_here.at[small], sem.at[0])
    first.start()
    arriving, leaving = [], []
    for k, (source, here, _) in enumerate(moves):
        arriving.append(pltpu.make_async_copy(source, here, sem.at[1 + 2 * k]))
        arriving[-1].start()
    first.wait()
    for target, (k, rows) in zip(outputs[2 + len(LARGE) :], SMALL_ROWS.values()):
        at = small_at + k
        if rows == 8:
            for s in range(target.shape[0]):
                target[s : s + 1, 0:c] = gradients_here[at + 2 * s : at + 2 * s + 1, :]
                target[s : s + 1, c : 2 * c] = gradients_here[at + 2 * s + 1 : at + 2 * s + 2, :]
        else:
            target[...] = gradients_here[at : at + rows, :]
    for k, (_, here, target) in enumerate(moves):
        arriving[k].wait()
        leaving.append(pltpu.make_async_copy(here, target, sem.at[2 + 2 * k]))
        leaving[-1].start()
    for copy in leaving:
        copy.wait()


def whole_items(shape, *arguments):
    line = shape["rows"]
    whole = Given(*arguments)
    given = whole._asdict()
    frames, cotangent = whole.frames, whole.cotangent
    items, history, strip, width = frames.shape
    c = cotangent.shape[-1]
    cells = strip * line * width
    flat = {}
    for name, value in given.items():
        if value is cotangent:
            value = value.reshape(items, strip * width, c)
        elif name in LARGE:
            value = value.reshape(-1, c)
        elif value.ndim == 1 and name not in IN_SMEM:
            value = value.reshape(-1, c)
        flat[name] = value
    shapes = {name: flat[name].shape for name in LARGE}
    big_layout = layout_of(shapes)
    starts, small_at, total_rows, runs = big_layout
    copies = 6 * (line - 1) + len(runs) * (6 + 2 * (line - 1)) + line - 1
    landing = sum(rows - rows // (8 * line) for _, rows in runs)
    shifted = pltpu.VMEM((cells + 2 * width, 6 * c), BF16)
    forward = pltpu.VMEM((18 * c, 2 * c), BF16)
    backward = pltpu.VMEM((2 * c, 18 * c), BF16)
    field = pltpu.VMEM((cells, c), F32)
    flipped_field = pltpu.VMEM((2 * c, cells), BF16)
    quarter = cells // 4
    scratch = dict(
        send=pltpu.SemaphoreType.DMA((copies,)),
        recv=pltpu.SemaphoreType.DMA((copies,)),
        local=pltpu.SemaphoreType.DMA((19,)),
        sums=pltpu.VMEM((total_rows, c), F32),
        final=pltpu.VMEM((total_rows, c), F32),
        landing=pltpu.VMEM((landing, c), F32),
        frames_in=pltpu.VMEM((line, history, strip, width), F32),
        mask_in=pltpu.VMEM((line, strip, width), jnp.int32),
        frames_out=pltpu.VMEM((line, history, strip, width), F32),
        fields=pltpu.VMEM((16, cells), F32),
        lift=pltpu.VMEM((16, c), F32),
        joined=pltpu.VMEM((cells, 4 * c), BF16),
        x_down=pltpu.VMEM((quarter, 8 * c), BF16),
        x_grad_up=pltpu.VMEM((quarter, 8 * c), BF16),
        x_up=pltpu.VMEM((quarter, 2 * c), BF16),
        x_grad_low=pltpu.VMEM((quarter, 2 * c), BF16),
        f_down=pltpu.VMEM((8 * c, 2 * c), BF16),
        b_down=pltpu.VMEM((4, 2 * c, 2 * c), BF16),
        f_up=pltpu.VMEM((4, 2 * c, 2 * c), BF16),
        b_up=pltpu.VMEM((2 * c, 8 * c), BF16),
        f_skip=pltpu.VMEM((4 * c, 2 * c), BF16),
        b_skip=pltpu.VMEM((2, 2 * c, 2 * c), BF16),
        xe1=shifted,
        xe2=shifted,
        xd1a=shifted,
        xd1b=shifted,
        xd2=shifted,
        xg=shifted,
        te1=flipped_field,
        te2=flipped_field,
        td1a=flipped_field,
        td1b=flipped_field,
        td2=flipped_field,
        turned=pltpu.VMEM((4 * c, cells), BF16),
        fe1=forward,
        fe2=forward,
        fd1a=forward,
        fd1b=forward,
        fd2=forward,
        be1=backward,
        be2=backward,
        bd1a=backward,
        bd1b=backward,
        bd2=backward,
        slope_e1=field,
        slope_e2=field,
        slope_d1a=field,
        slope_d1b=field,
        slope_d2=field,
        lifted=field,
        middle_e=field,
        encoded=field,
        raised=field,
        middle_d=field,
        result=field,
        cot=field,
        grad=field,
        grad_a=field,
        grad_b=field,
    )
    scratch.update({name: pltpu.VMEM(shapes[name], F32) for name in LARGE})

    in_hbm = pl.BlockSpec(memory_space=pl.ANY)
    in_vmem = pl.BlockSpec(memory_space=pltpu.VMEM)
    in_smem = pl.BlockSpec(memory_space=pltpu.SMEM)
    in_specs = [
        in_hbm if name in IN_HBM else in_smem if name in IN_SMEM else in_vmem
        for name in ARGUMENTS
    ]
    out_shape = [
        jax.ShapeDtypeStruct((items, strip * width, c), F32),
        jax.ShapeDtypeStruct(frames.shape, F32),
        jax.ShapeDtypeStruct((total_rows, c), F32),
    ]
    out_specs = [in_hbm] * 3
    results = pl.pallas_call(
        functools.partial(
            item_kernel,
            (line, strip, width, shapes, big_layout),
            tuple(scratch),
        ),
        out_shape=out_shape,
        in_specs=in_specs,
        out_specs=out_specs,
        scratch_shapes=list(scratch.values()),
        compiler_params=pltpu.CompilerParams(
            collective_id=0, has_side_effects=True, vmem_limit_bytes=62 * 1024 * 1024
        ),
    )(*[flat[name] for name in ARGUMENTS])
    names = LARGE + tuple(SMALL_ROWS)
    written = pl.pallas_call(
        functools.partial(write_kernel, (shapes, starts, small_at)),
        out_shape=out_shape[:2] + [jax.ShapeDtypeStruct(flat[name].shape, F32) for name in names],
        in_specs=[pl.BlockSpec(memory_space=pltpu.HBM)] * 3,
        out_specs=[in_hbm] * (2 + len(LARGE)) + [in_vmem] * len(SMALL_ROWS),
        scratch_shapes=[
            pltpu.VMEM((items, strip * width, c), F32),
            pltpu.VMEM(frames.shape, F32),
            pltpu.VMEM((total_rows, c), F32),
            pltpu.SemaphoreType.DMA((1 + 2 * (2 + len(LARGE)),)),
        ],
        compiler_params=pltpu.CompilerParams(vmem_limit_bytes=60 * 1024 * 1024),
    )(*results)
    grads = dict(zip(names, written[2:]))
    ordered = [name for name in ARGUMENTS if name in grads]
    return (written[0].reshape(cotangent.shape), written[1]) + tuple(
        grads[name].reshape(given[name].shape) for name in ordered
    )


def body(shape, *arguments):
    items, _, strip, width = arguments[0].shape
    line = shape["rows"]
    whole = (
        shape["section"] == 2
        and shape["batch"] == 4
        and items == line
        and arguments[-1].shape[-1] == 128
        and (strip * line * width) % CHUNK == 0
    )
    return whole_items(shape, *arguments) if whole else strips_body(*arguments)


def solution(mesh):
    in_specs = (
        P(("section", "batch"), None, "rows", None),
        P(("section", "batch")),
        P(("section", "batch"), "rows", None),
        P(("section", "batch")),
        P(),
        P(),
        P(),
        P(),
        P(),
        P(),
        P(),
        P(),
        P(),
        P(),
        P(),
        P(),
        P(),
        P(),
        P(),
        P(),
        P(),
        P(),
        P(),
        P(),
        P(),
        P(),
        P(),
        P(),
        P(("section", "batch"), "rows", None, None),
    )
    out_specs = (
        P(("section", "batch"), "rows", None, None),
        P(("section", "batch"), None, "rows", None),
        P(),
        P(),
        P(),
        P(),
        P(),
        P(),
        P(),
        P(),
        P(),
        P(),
        P(),
        P(),
        P(),
        P(),
        P(),
        P(),
        P(),
        P(),
        P(),
        P(),
        P(),
        P(),
        P(),
        P(),
    )
    return jax.shard_map(functools.partial(body, mesh.shape), mesh=mesh, in_specs=in_specs, out_specs=out_specs, check_vma=False)
```

```python
import functools
from types import SimpleNamespace
from typing import Any, NamedTuple

import jax
import jax.numpy as jnp
from jax import lax
from jax.experimental import pallas as pl
from jax.experimental.pallas import tpu as pltpu
from jax.sharding import PartitionSpec as P

GROUPS = 8
FIELDS = 3
HIST = 4


EPS = 1e-05
HIGH = lax.Precision.HIGHEST


def extended(cells, sides, width):
    for axis, dim in sides:
        count = lax.axis_size(axis)
        ends = count - 1
        head = lax.slice_in_dim(cells, 0, width, axis=dim)
        tail = lax.slice_in_dim(cells, cells.shape[dim] - width, cells.shape[dim], axis=dim)
        cells = jnp.concatenate(
            [
                lax.ppermute(tail, axis, [(i, (i + 1) % count) for i in range(ends)]),
                cells,
                lax.ppermute(head, axis, [((i + 1) % count, i) for i in range(ends)]),
            ],
            axis=dim,
        )
    return cells


def from_behind(value, axis, steps):
    count = lax.axis_size(axis)
    pairs = [(source, (source + steps) % count) for source in range(count)]
    return lax.ppermute(value, axis, pairs)


def group_view(value_arrays):
    extent = value_arrays.shape
    return value_arrays.reshape(extent[:-1] + (GROUPS, extent[-1] // GROUPS))


def global_sums(value_arrays):
    grouped = group_view(value_arrays)
    flat = grouped.reshape(-1, GROUPS, grouped.shape[-1])
    first_sum = jnp.sum(flat, axis=(0, 2))
    second_sum = jnp.sum(flat * flat, axis=(0, 2))
    return lax.psum((first_sum, second_sum), "rows")


def apply_norm(value_arrays, sum_one, sum_two, norm_gain, norm_bias, total):
    grouped = group_view(value_arrays)
    group_mean = sum_one / total
    variance = sum_two / total - group_mean * group_mean
    inverse = lax.rsqrt(variance + EPS)
    normed = (grouped - group_mean[:, None]) * inverse[:, None]
    return normed.reshape(value_arrays.shape) * norm_gain + norm_bias


def norm_back(value_arrays, grad_one, grad_two):
    grouped = group_view(value_arrays)
    extra = grad_one[:, None] + 2.0 * grouped * grad_two[:, None]
    return extra.reshape(value_arrays.shape)


def reduce_grads(grad_one, grad_two):
    return lax.psum((grad_one, grad_two), "rows")


def conv_rows(padded, kernel):
    widened = jnp.pad(padded, ((0, 0), (1, 1), (0, 0)))
    return lax.conv_general_dilated(
        widened[None],
        kernel,
        (1, 1),
        "VALID",
        dimension_numbers=("NHWC", "HWIO", "NHWC"),
        precision=HIGH,
    )[0]


def flipped(kernel):
    return jnp.transpose(kernel[::-1, ::-1], (0, 1, 3, 2))


def pad_grads(value_arrays):
    return extended(value_arrays, (("rows", 0),), 1)


def totals_of(inputs, conv1):
    strip = inputs.shape[0]
    cells = strip * lax.axis_size("rows") * inputs.shape[1]
    return (cells * (inputs.shape[2] // GROUPS), cells * (conv1.shape[3] // GROUPS))


def block_forward(inputs, weights, scale_part, shift_part):
    norm1_gain, norm1_bias, conv1, norm2_gain, norm2_bias, conv2, conv2_bias = weights
    total_in, total_mid = totals_of(inputs, conv1)
    sums_in = global_sums(inputs)

    def pad_rows(value_arrays):
        return extended(value_arrays, (("rows", 0),), 1)

    act_one = pad_rows(
        jax.nn.gelu(
            apply_norm(inputs, sums_in[0], sums_in[1], norm1_gain, norm1_bias, total_in),
            approximate=False,
        )
    )
    middle = conv_rows(act_one, conv1)
    sums_mid = global_sums(middle)
    shaped = (
        apply_norm(middle, sums_mid[0], sums_mid[1], norm2_gain, norm2_bias, total_mid)
        * (1.0 + scale_part)
        + shift_part
    )
    act_two = pad_rows(jax.nn.gelu(shaped, approximate=False))
    branch = conv_rows(act_two, conv2) + conv2_bias
    return (branch, (sums_in[0], sums_in[1], act_one, middle, sums_mid[0], sums_mid[1], act_two))


def block_backward(inputs, weights, scale_part, shift_part, kept, grad_out):
    norm1_gain, norm1_bias, conv1, norm2_gain, norm2_bias, conv2, conv2_bias = weights
    in_one, in_two, act_one, middle, mid_one, mid_two, act_two = kept
    total_in, total_mid = totals_of(inputs, conv1)
    grad_conv2 = jax.vjp(lambda kernel: conv_rows(act_two, kernel), conv2)[1](grad_out)[0]
    grad_bias2 = jnp.sum(grad_out, axis=(0, 1))
    grad_act_two = conv_rows(pad_grads(grad_out), flipped(conv2))

    def second_piece(middle_in, sum_one, sum_two, gain_in, incoming_bias, scale_in, shift_in):
        shaped = (
            apply_norm(middle_in, sum_one, sum_two, gain_in, incoming_bias, total_mid)
            * (1.0 + scale_in)
            + shift_in
        )
        return jax.nn.gelu(shaped, approximate=False)

    second_pull = jax.vjp(
        second_piece, middle, mid_one, mid_two, norm2_gain, norm2_bias, scale_part, shift_part
    )[1](grad_act_two)
    summed_one, summed_two = reduce_grads(second_pull[1], second_pull[2])
    grad_middle = second_pull[0] + norm_back(middle, summed_one, summed_two)
    grad_conv1 = jax.vjp(lambda kernel: conv_rows(act_one, kernel), conv1)[1](grad_middle)[0]
    grad_act_one = conv_rows(pad_grads(grad_middle), flipped(conv1))

    def first_piece(inputs_in, sum_one, sum_two, gain_in, incoming_bias):
        return jax.nn.gelu(
            apply_norm(inputs_in, sum_one, sum_two, gain_in, incoming_bias, total_in),
            approximate=False,
        )

    first_pull = jax.vjp(first_piece, inputs, in_one, in_two, norm1_gain, norm1_bias)[1](
        grad_act_one
    )
    first_one, first_two = reduce_grads(first_pull[1], first_pull[2])
    grad_inputs = first_pull[0] + norm_back(inputs, first_one, first_two)
    grads = (
        first_pull[3],
        first_pull[4],
        grad_conv1,
        second_pull[3],
        second_pull[4],
        grad_conv2,
        grad_bias2,
    )
    return (grad_inputs, grads, second_pull[5], second_pull[6])


def conditioning(step_item, table):
    one_hot = (jnp.arange(table.shape[0], dtype=jnp.int32) == step_item).astype(jnp.float32)
    condition = jnp.dot(one_hot, table, precision=HIGH)
    half_width = table.shape[1] // 2
    return (condition[:half_width], condition[half_width:], one_hot)


def project_in(frames_item, mask_item, count_item, incoming_weight, incoming_bias):
    history = jnp.arange(HIST, dtype=jnp.int32) >= HIST - count_item
    keep = jnp.repeat(history, FIELDS).astype(jnp.float32)
    lifted = (
        jnp.einsum(
            "fhw,fc->hwc", frames_item * keep[:, None, None], incoming_weight, precision=HIGH
        )
        + incoming_bias
    )
    return lifted * mask_item[:, :, None].astype(jnp.float32)


def coarsen_field(value_arrays, incoming_weight, incoming_bias):
    rows_here, width_here, depth_here = value_arrays.shape
    blocks = value_arrays.reshape(rows_here // 2, 2, width_here // 2, 2, depth_here)
    return jnp.einsum("iajbk,abkc->ijc", blocks, incoming_weight, precision=HIGH) + incoming_bias


def upsample(value_arrays, incoming_weight, incoming_bias):
    result = jnp.einsum("ijk,abkc->iajbc", value_arrays, incoming_weight, precision=HIGH)
    extent = result.shape
    return result.reshape(extent[0] * 2, extent[2] * 2, extent[4]) + incoming_bias


def flatten_all(pieces):
    return jnp.concatenate([piece.reshape(-1) for piece in pieces])


def unflatten_all(flat, templates):
    pieces = []
    offset_at = 0
    for template in templates:
        count_here = template.size
        pieces.append(flat[offset_at : offset_at + count_here].reshape(template.shape))
        offset_at += count_here
    return tuple(pieces)


def strips_body(
    frames,
    counts,
    cell_mask,
    step_index,
    lift_weight,
    lift_bias,
    enc_norm1_gain,
    enc_norm1_bias,
    enc_conv1,
    enc_step_table,
    enc_norm2_gain,
    enc_norm2_bias,
    enc_conv2,
    enc_conv2_bias,
    reducer_weight,
    reducer_bias,
    up_weight,
    up_bias,
    dec_norm1_gain,
    dec_norm1_bias,
    dec_conv1,
    dec_step_table,
    dec_norm2_gain,
    dec_norm2_bias,
    dec_conv2,
    dec_conv2_bias,
    skip_weight,
    skip_bias,
    cotangent,
):
    enc_weights = (
        enc_norm1_gain,
        enc_norm1_bias,
        enc_conv1,
        enc_norm2_gain,
        enc_norm2_bias,
        enc_conv2,
        enc_conv2_bias,
    )
    dec_weights = (
        dec_norm1_gain,
        dec_norm1_bias,
        dec_conv1,
        dec_norm2_gain,
        dec_norm2_bias,
        dec_conv2,
        dec_conv2_bias,
    )
    params = (
        lift_weight,
        lift_bias,
        enc_norm1_gain,
        enc_norm1_bias,
        enc_conv1,
        enc_step_table,
        enc_norm2_gain,
        enc_norm2_bias,
        enc_conv2,
        enc_conv2_bias,
        reducer_weight,
        reducer_bias,
        up_weight,
        up_bias,
        dec_norm1_gain,
        dec_norm1_bias,
        dec_conv1,
        dec_step_table,
        dec_norm2_gain,
        dec_norm2_bias,
        dec_conv2,
        dec_conv2_bias,
        skip_weight,
        skip_bias,
    )

    def forward_micro(carry, sliced):
        frames_item, mask_item, count_item, step_item = sliced
        lifted = project_in(frames_item, mask_item, count_item, lift_weight, lift_bias)
        enc_scale, enc_shift, unused_hot = conditioning(step_item, enc_step_table)
        enc_branch, enc_kept = block_forward(lifted, enc_weights, enc_scale, enc_shift)
        encoder_result = lifted + enc_branch
        coarse_field = coarsen_field(encoder_result, reducer_weight, reducer_bias)
        foreign = from_behind(coarse_field, "section", 1)
        raised_foreign = upsample(foreign, up_weight, up_bias)
        raised = from_behind(raised_foreign, "section", 1)
        joined = jnp.concatenate([raised, encoder_result], axis=-1)
        dec_scale, dec_shift, unused_again = conditioning(step_item, dec_step_table)
        dec_branch, dec_kept = block_forward(joined, dec_weights, dec_scale, dec_shift)
        output_item = jnp.dot(joined, skip_weight, precision=HIGH) + skip_bias + dec_branch
        return (carry, (output_item, (lifted, enc_kept, encoder_result, foreign, joined, dec_kept)))

    unused, (output, kept_all) = lax.scan(
        forward_micro, jnp.zeros((), jnp.float32), (frames, cell_mask, counts, step_index)
    )

    def backward_micro(totals, sliced):
        frames_item, mask_item, count_item, step_item, grad_out, kept = sliced
        lifted, enc_kept, encoder_result, foreign, joined, dec_kept = kept
        dec_scale, dec_shift, one_hot = conditioning(step_item, dec_step_table)
        grad_joined, dec_grads, dec_gscale, dec_gshift = block_backward(
            joined, dec_weights, dec_scale, dec_shift, dec_kept, grad_out
        )
        grad_skip_weight = jnp.einsum("hwk,hwc->kc", joined, grad_out, precision=HIGH)
        grad_skip_bias = jnp.sum(grad_out, axis=(0, 1))
        grad_joined = grad_joined + jnp.dot(grad_out, skip_weight.T, precision=HIGH)
        half_width = joined.shape[-1] // 2
        grad_raised = grad_joined[..., :half_width]
        grad_encoded = grad_joined[..., half_width:]
        grad_foreign_up = from_behind(grad_raised, "section", 1)
        up_pull = jax.vjp(upsample, foreign, up_weight, up_bias)[1](grad_foreign_up)
        coarse_gradient = from_behind(up_pull[0], "section", 1)
        reducer_pullback = jax.vjp(coarsen_field, encoder_result, reducer_weight, reducer_bias)[1](
            coarse_gradient
        )
        grad_encoded = grad_encoded + reducer_pullback[0]
        enc_scale, enc_shift, enc_hot = conditioning(step_item, enc_step_table)
        grad_lifted, enc_grads, enc_gscale, enc_gshift = block_backward(
            lifted, enc_weights, enc_scale, enc_shift, enc_kept, grad_encoded
        )
        grad_lifted = grad_lifted + grad_encoded
        proj_pull = jax.vjp(
            lambda frames_in, incoming_weight, incoming_bias: project_in(
                frames_in, mask_item, count_item, incoming_weight, incoming_bias
            ),
            frames_item,
            lift_weight,
            lift_bias,
        )[1](grad_lifted)
        enc_table_grad = enc_hot[:, None] * jnp.concatenate([enc_gscale, enc_gshift])[None, :]
        dec_table_grad = one_hot[:, None] * jnp.concatenate([dec_gscale, dec_gshift])[None, :]
        micro_list = (
            proj_pull[1],
            proj_pull[2],
            enc_grads[0],
            enc_grads[1],
            enc_grads[2],
            enc_table_grad,
            enc_grads[3],
            enc_grads[4],
            enc_grads[5],
            enc_grads[6],
            reducer_pullback[1],
            reducer_pullback[2],
            up_pull[1],
            up_pull[2],
            dec_grads[0],
            dec_grads[1],
            dec_grads[2],
            dec_table_grad,
            dec_grads[3],
            dec_grads[4],
            dec_grads[5],
            dec_grads[6],
            grad_skip_weight,
            grad_skip_bias,
        )
        micro_flat = flatten_all(micro_list)
        return (totals + micro_flat, proj_pull[0])

    total_size = sum((piece.size for piece in params))
    start_totals = jnp.zeros((total_size,), jnp.float32)
    flat_totals, frames_grad = lax.scan(
        backward_micro,
        start_totals,
        (frames, cell_mask, counts, step_index, cotangent, kept_all),
        reverse=True,
    )
    flat_totals = lax.psum(flat_totals, ("section", "batch", "rows"))
    grads = unflatten_all(flat_totals, params)
    return (output, frames_grad) + grads


F32 = jnp.float32
BF16 = jnp.bfloat16
MESH = pl.DeviceIdType.MESH
NN = ((1,), (0,))
NT = ((1,), (1,))
TN = ((0,), (0,))
HIGH_AT = (0, 2, 1)
LOW_AT = (4, 3, 5)
CHUNK = 512
class Given(NamedTuple):
    frames: Any
    counts: Any
    cell_mask: Any
    step_index: Any
    lift_weight: Any
    lift_bias: Any
    enc_norm1_gain: Any
    enc_norm1_bias: Any
    enc_conv1: Any
    enc_step_table: Any
    enc_norm2_gain: Any
    enc_norm2_bias: Any
    enc_conv2: Any
    enc_conv2_bias: Any
    reducer_weight: Any
    reducer_bias: Any
    up_weight: Any
    up_bias: Any
    dec_norm1_gain: Any
    dec_norm1_bias: Any
    dec_conv1: Any
    dec_step_table: Any
    dec_norm2_gain: Any
    dec_norm2_bias: Any
    dec_conv2: Any
    dec_conv2_bias: Any
    skip_weight: Any
    skip_bias: Any
    cotangent: Any


ARGUMENTS = Given._fields
LARGE = tuple(dict(
    dec_conv2=0,
    skip_weight=0,
    dec_conv1=0,
    up_weight=0,
    reducer_weight=0,
    enc_conv2=0,
    enc_conv1=0,
))
IN_HBM = tuple(dict(frames=0, cell_mask=0, cotangent=0)) + LARGE
IN_SMEM = tuple(dict(counts=0, step_index=0))
SMALL_ROWS = dict(
    lift_weight=(0, 12),
    lift_bias=(12, 1),
    enc_norm1_gain=(16, 1),
    enc_norm1_bias=(17, 1),
    enc_norm2_gain=(18, 1),
    enc_norm2_bias=(19, 1),
    enc_conv2_bias=(20, 1),
    reducer_bias=(21, 1),
    up_bias=(22, 1),
    dec_conv2_bias=(23, 1),
    skip_bias=(23, 1),
    dec_norm1_gain=(24, 2),
    dec_norm1_bias=(26, 2),
    dec_norm2_gain=(28, 1),
    dec_norm2_bias=(29, 1),
    enc_step_table=(32, 8),
    dec_step_table=(40, 8),
)
SMALL_COUNT = 64
OUTPUTS = tuple(dict(output=0, frames_grad=0, gradients=0))


def split(value):
    high = value.astype(BF16)
    return high, (value - high.astype(F32)).astype(BF16)


def dot(left, right, dims=NN, precision=None):
    return lax.dot_general(
        left, right, (dims, ((), ())), precision=precision, preferred_element_type=F32
    )


def fold(value):
    half = value.shape[1] // 2
    return value[:, :half] + value[:, half:]


def fold_rows(value):
    half = value.shape[0] // 2
    return value[:half] + value[half:]


def tile_sums(value):
    return jnp.sum(value.reshape(-1, 8, value.shape[-1]), axis=0)


def column_sum(tiles):
    return jnp.sum(tiles, axis=0, keepdims=True)


def group_ones(channels, size):
    rows = lax.broadcasted_iota(jnp.int32, (channels, channels), 0) // size
    columns = lax.broadcasted_iota(jnp.int32, (channels, channels), 1) // size
    return (rows == columns).astype(F32)


def group_sums(first, second, ones):
    both = dot(jnp.concatenate([first, second], axis=0), ones, precision=HIGH)
    return column_sum(both[:8]), column_sum(both[8:])


class Exchange:

    def __init__(self, place, start, rows, landing, first_sem):
        self.place, self.start, self.rows, self.landing = place, start, rows, landing
        self.sem = first_sem
        self.stage = 0
        self.copies = []
        line = place.line
        self.at = [start]
        size = rows
        for bit in (place.core, place.first, place.second):
            size //= 2
            self.at.append(self.at[-1] + bit * size)
        self.shard = size // line
        self.at.append(self.at[-1] + place.row * self.shard)

    def count(self):
        return 6 + 2 * (self.place.line - 1)

    def _copy(self, source, target, device):
        place = self.place
        copy = pltpu.make_async_remote_copy(
            src_ref=source,
            dst_ref=target,
            send_sem=place.send.at[self.sem],
            recv_sem=place.recv.at[self.sem],
            device_id=device,
            device_id_type=MESH,
        )
        self.sem += 1
        copy.start()
        self.copies.append(copy)
        return copy

    def _halve(self, level):
        place = self.place
        size = self.rows >> (level + 1)
        bit = (place.core, place.first, place.second)[level]
        other = pl.multiple_of(self.at[level] + (1 - bit) * size, 8)
        self.land = self.landing
        self.landing += size
        self.waiting = [
            self._copy(
                place.sums.at[pl.ds(other, size)],
                place.landing.at[pl.ds(self.land, size)],
                place.partners[level],
            )
        ]

    def _add(self, level):
        place = self.place
        size = self.rows >> (level + 1)
        block = 128 >> level
        sums, landing = place.sums, place.landing
        base = self.at[level + 1]
        land = self.land

        def step(i, carry):
            here = pl.ds(pl.multiple_of(base + i * block, 8), block)
            there = pl.ds(pl.multiple_of(land + i * block, 8), block)
            sums[here] = sums[here] + landing[there]
            return carry

        lax.fori_loop(0, size // block, step, 0)

    def _wait(self):
        for copy in self.waiting:
            copy.wait_recv()

    def _spread(self, level):
        place = self.place
        size = self.rows >> (level + 1)
        here = pl.ds(pl.multiple_of(self.at[level + 1], 8), size)
        self.waiting = [
            self._copy(
                place.final.at[here], place.final.at[here], place.partners[level]
            )
        ]

    def advance(self):
        place = self.place
        line, row = place.line, place.row
        shard = self.shard
        stage = self.stage
        self.stage += 1
        if stage == 0:
            self._halve(0)
        elif stage in (1, 2):
            self._wait()
            self._add(stage - 1)
            self._halve(stage)
        elif stage == 3:
            self._wait()
            self._add(2)
            self.waiting = []
            self.land = self.landing
            for k in range(1, line):
                to = lax.rem(row + k, line)
                source = pl.ds(pl.multiple_of(self.at[3] + to * shard, 8), shard)
                target = pl.ds(self.landing, shard)
                self.landing += shard
                self.waiting.append(
                    self._copy(
                        place.sums.at[source],
                        place.landing.at[target],
                        place.device_at(to),
                    )
                )
        elif stage == 4:
            self._wait()
            here = pl.ds(pl.multiple_of(self.at[4], 8), shard)
            total = place.sums[here]
            for k in range(line - 1):
                total = total + place.landing[pl.ds(self.land + k * shard, shard)]
            place.final[here] = total
            self.waiting = []
            for k in range(1, line):
                self.waiting.append(
                    self._copy(
                        place.final.at[here],
                        place.final.at[here],
                        place.device_at(lax.rem(row + k, line)),
                    )
                )
        elif stage in (5, 6, 7):
            self._wait()
            self._spread(7 - stage)
        else:
            self._wait()

    def done(self):
        return self.stage > 8


class SmallExchange(Exchange):
    def __init__(self, place, start, rows, landing, first_sem):
        super().__init__(place, start, rows, landing, first_sem)
        self.part = rows // 8
        self.own = start + place.number * self.part
        self.shard = self.part // place.line
        self.last = self.own + place.row * self.shard

    def count(self):
        return 2 * 7 + 2 * (self.place.line - 1)

    def _plane(self, source_of, target_of):
        place = self.place
        self.waiting = []
        for k in range(1, 8):
            to = lax.rem(place.number + k, 8)
            device = (to // 4, lax.rem(to, 4), place.row)
            self.waiting.append(self._copy(source_of(to), target_of(k), device))

    def _line(self, source_of, target_of):
        place = self.place
        self.waiting = []
        for k in range(1, place.line):
            to = lax.rem(place.row + k, place.line)
            self.waiting.append(self._copy(source_of(to), target_of(k), place.device_at(to)))

    def advance(self):
        place = self.place
        part, shard = self.part, self.shard
        sums, final, landing = place.sums, place.final, place.landing
        stage = self.stage
        self.stage += 1

        def rows(at, size):
            return pl.ds(pl.multiple_of(at, 8), size)

        if stage > 0:
            self._wait()
        if stage == 0:
            first = self.landing
            self._plane(
                lambda to: sums.at[rows(self.start + to * part, part)],
                lambda k: landing.at[pl.ds(first + (k - 1) * part, part)],
            )
        elif stage == 1:
            total = sums[rows(self.own, part)]
            for k in range(7):
                total = total + landing[pl.ds(self.landing + k * part, part)]
            sums[rows(self.own, part)] = total
            self.landing += 7 * part
            first = self.landing
            self._line(
                lambda to: sums.at[rows(self.own + to * shard, shard)],
                lambda k: landing.at[pl.ds(first + (k - 1) * shard, shard)],
            )
        elif stage == 2:
            here = rows(self.last, shard)
            total = sums[here]
            for k in range(place.line - 1):
                total = total + landing[pl.ds(self.landing + k * shard, shard)]
            final[here] = total
            self._line(lambda to: final.at[here], lambda k: final.at[here])
        elif stage == 3:
            here = rows(self.own, part)
            self._plane(lambda to: final.at[here], lambda k: final.at[here])

    def done(self):
        return self.stage > 4


def layout_of(shapes):
    starts = {}
    at = 0
    for name in LARGE:
        starts[name] = at
        at += shapes[name][0]
    small = at
    unit = 256
    total = -(-(at + SMALL_COUNT) // unit) * unit
    begins = SimpleNamespace(**starts)
    ready = (
        begins.dec_conv1,
        begins.up_weight,
        begins.enc_conv2,
        begins.enc_conv1,
        small,
    )
    edges = [0] + [edge // unit * unit for edge in ready] + [total]
    runs = [(a, b - a) for a, b in zip(edges[:-1], edges[1:])]
    return starts, small, total, runs


def item_kernel(sizes, scratch_names, *refs):
    line, strip, width, shapes, big_layout = sizes
    begins, small_at, total_rows, runs = big_layout
    starts = SimpleNamespace(**begins)
    inputs = Given(*refs[: len(ARGUMENTS)])
    refs = refs[len(ARGUMENTS) :]
    output_names = OUTPUTS
    outputs = SimpleNamespace(**dict(zip(output_names, refs)))
    scratch = SimpleNamespace(**dict(zip(scratch_names, refs[len(output_names) :])))

    def w_of(name):
        return getattr(scratch, name)

    height = strip * line
    cells = height * width
    c = inputs.lift_weight.shape[1]
    strip_cells = strip * width
    history = inputs.frames.shape[1]

    core = lax.axis_index("section")
    plane = lax.axis_index("batch")
    row = lax.axis_index("rows")
    y, x = plane // 2, lax.rem(plane, 2)
    along_x = plane + 1 - 2 * x
    along_y = plane + 2 - 4 * y
    place = SimpleNamespace(
        line=line,
        row=row,
        number=core * 4 + plane,
        core=core,
        first=x * (1 - core) + y * core,
        second=y * (1 - core) + x * core,
        partners=(
            (1 - core, plane, row),
            (core, along_x * (1 - core) + along_y * core, row),
            (core, along_y * (1 - core) + along_x * core, row),
        ),
        device_at=lambda to: (core, plane, to),
        sums=scratch.sums,
        final=scratch.final,
        landing=scratch.landing,
        send=scratch.send,
        recv=scratch.recv,
    )
    local_sem = scratch.local

    weight_copies = {}
    for k, name in enumerate(LARGE):
        copy = pltpu.make_async_copy(getattr(inputs, name), w_of(name), local_sem.at[k])
        weight_copies[name] = copy
        copy.start()
    frames_in, mask_in, cot = scratch.frames_in, scratch.mask_in, scratch.cot
    here_rows = pl.ds(pl.multiple_of(row * strip_cells, strip_cells), strip_cells)
    own = (
        pltpu.make_async_copy(inputs.frames.at[row], frames_in.at[row], local_sem.at[7]),
        pltpu.make_async_copy(inputs.cell_mask.at[row], mask_in.at[row], local_sem.at[8]),
        pltpu.make_async_copy(
            inputs.cotangent.at[row], cot.at[here_rows], local_sem.at[9]
        ),
    )
    for copy in own:
        copy.start()

    barrier = pltpu.get_barrier_semaphore()
    peers = [place.device_at(lax.rem(row + k, line)) for k in range(1, line)]
    for k in range(1, 8):
        to = lax.rem(place.number + k, 8)
        peers.append((to // 4, lax.rem(to, 4), row))
    for device in peers:
        pl.semaphore_signal(barrier, inc=1, device_id=device, device_id_type=MESH)
    pl.semaphore_wait(barrier, len(peers))

    next_sem = 0

    def send(source, target, device):
        nonlocal next_sem
        copy = pltpu.make_async_remote_copy(
            src_ref=source,
            dst_ref=target,
            send_sem=scratch.send.at[next_sem],
            recv_sem=scratch.recv.at[next_sem],
            device_id=device,
            device_id_type=MESH,
        )
        next_sem += 1
        copy.start()
        return copy

    frame_copies, cot_copies, output_copies = [], [], []
    for k in range(1, line):
        to = lax.rem(row + k, line)
        device = place.device_at(to)
        frame_copies.append(send(inputs.frames.at[to], frames_in.at[row], device))
        frame_copies.append(send(inputs.cell_mask.at[to], mask_in.at[row], device))
    for k in range(1, line):
        to = lax.rem(row + k, line)
        cot_copies.append(
            send(inputs.cotangent.at[to], cot.at[here_rows], place.device_at(to))
        )

    copied = SimpleNamespace(**weight_copies)
    def stack_conv(source, half, depth, forward, backward):
        for a in range(3):
            for b in range(3):
                at = (3 * a + b) * depth + half * c
                high, low = split(source[at : at + c, :])
                for block in (HIGH_AT[b], LOW_AT[b]):
                    rows = slice((6 * a + block) * c, (6 * a + block + 1) * c)
                    forward[rows, 0:c] = high
                    forward[rows, c : 2 * c] = low
                for block in (HIGH_AT[2 - b], LOW_AT[2 - b]):
                    tap = 6 * (2 - a) + block
                    columns = slice(tap * c, (tap + 1) * c)
                    backward[0:c, columns] = high
                    backward[c : 2 * c, columns] = low

    copied.enc_conv1.wait()
    stack_conv(scratch.enc_conv1, 0, c, scratch.fe1, scratch.be1)
    copied.enc_conv2.wait()
    stack_conv(scratch.enc_conv2, 0, c, scratch.fe2, scratch.be2)
    copied.reducer_weight.wait()
    for k in range(4):
        high, low = split(scratch.reducer_weight[k * c : (k + 1) * c, :])
        for block in (k, k + 4):
            scratch.f_down[block * c : (block + 1) * c, 0:c] = high
            scratch.f_down[block * c : (block + 1) * c, c : 2 * c] = low
        for block in (0, 1):
            columns = slice(block * c, (block + 1) * c)
            scratch.b_down[k, 0:c, columns] = high
            scratch.b_down[k, c : 2 * c, columns] = low
    copied.up_weight.wait()
    for k in range(4):
        high, low = split(scratch.up_weight[k * c : (k + 1) * c, :])
        for block in (0, 1):
            rows = slice(block * c, (block + 1) * c)
            scratch.f_up[k, rows, 0:c] = high
            scratch.f_up[k, rows, c : 2 * c] = low
        for block in (k, k + 4):
            columns = slice(block * c, (block + 1) * c)
            scratch.b_up[0:c, columns] = high
            scratch.b_up[c : 2 * c, columns] = low
    copied.dec_conv1.wait()
    stack_conv(scratch.dec_conv1, 0, 2 * c, scratch.fd1a, scratch.bd1a)
    stack_conv(scratch.dec_conv1, 1, 2 * c, scratch.fd1b, scratch.bd1b)
    copied.dec_conv2.wait()
    stack_conv(scratch.dec_conv2, 0, c, scratch.fd2, scratch.bd2)
    copied.skip_weight.wait()
    for half in range(2):
        high, low = split(scratch.skip_weight[half * c : (half + 1) * c, :])
        for block in (half, half + 2):
            scratch.f_skip[block * c : (block + 1) * c, 0:c] = high
            scratch.f_skip[block * c : (block + 1) * c, c : 2 * c] = low
        for block in (0, 1):
            columns = slice(block * c, (block + 1) * c)
            scratch.b_skip[half, 0:c, columns] = high
            scratch.b_skip[half, c : 2 * c, columns] = low

    for buffer in (scratch.xe1, scratch.xe2, scratch.xd1a, scratch.xd1b, scratch.xd2, scratch.xg):
        edge = jnp.zeros((width, 6 * c), BF16)
        buffer[0:width, :] = edge
        buffer[cells + width : cells + 2 * width, :] = edge

    lift = scratch.lift
    lift[...] = jnp.zeros(lift.shape, F32)
    lift[0:history, :] = inputs.lift_weight[...]
    lift[history : history + 1, :] = inputs.lift_bias[...]

    block = 2 * width
    column = lax.rem(lax.broadcasted_iota(jnp.int32, (block, c), 0), width)
    at_first, at_last = column == 0, column == width - 1
    zeros8 = jnp.zeros((8, c), F32)
    ones16 = group_ones(c, c // GROUPS)
    ones32 = group_ones(c, 2 * c // GROUPS)
    count16 = float(cells * (c // GROUPS))
    count32 = float(cells * (2 * c // GROUPS))

    def grid_rows(step, carry=0):
        return lax.fori_loop(0, cells // block, step, carry, unroll=2)

    def row_at(h):
        return pl.ds(pl.multiple_of(h * block, block), block)

    def chunk_at(i):
        return pl.ds(pl.multiple_of(i * CHUNK, CHUNK), CHUNK)

    def put_row(target, h, value):
        rows = pl.ds(pl.multiple_of(h * block + width, width), block)
        left = jnp.where(at_first, 0.0, pltpu.roll(value, 1, 0))
        right = jnp.where(at_last, 0.0, pltpu.roll(value, block - 1, 0))
        for b, piece in enumerate((left, value, right)):
            high, low = split(piece)
            target[rows, HIGH_AT[b] * c : (HIGH_AT[b] + 1) * c] = high
            target[rows, LOW_AT[b] * c : (LOW_AT[b] + 1) * c] = low

    def put_turned(target, columns, value, first=0, second=1):
        high, low = split(value.T)
        target[first * c : (first + 1) * c, columns] = high
        target[second * c : (second + 1) * c, columns] = low

    def conv_chunk(pairs, i, dims=NN):
        total = None
        for data, weight in pairs:
            taps = []
            for a in range(3):
                rows = pl.ds(pl.multiple_of(i * CHUNK + a * width, width), CHUNK)
                taps.append(data[rows, :])
            part = dot(jnp.concatenate(taps, axis=1), weight[...], dims)
            total = part if total is None else total + part
        return total

    def norm_of(first, second, ones, count):
        one, two = group_sums(first, second, ones)
        mean = one / count
        return mean, lax.rsqrt(two / count - mean * mean + EPS)

    def activate(source, target, turned, slope, scale, shift):
        def step(h, carry):
            value = source[row_at(h), :] * scale + shift
            below = 0.5 + 0.5 * lax.erf(value * 0.7071067811865476)
            slope[row_at(h), :] = below + value * (
                0.3989422804014327 * jnp.exp(-0.5 * value * value)
            )
            value = value * below
            put_row(target, h, value)
            put_turned(turned, row_at(h), value)
            return carry

        grid_rows(step)

    def conv_norm(pairs, target):
        def step(i, carry):
            value = fold(conv_chunk(pairs, i))
            target[chunk_at(i), :] = value
            return carry[0] + tile_sums(value), carry[1] + tile_sums(value * value)

        return lax.fori_loop(0, cells // CHUNK, step, (zeros8, zeros8))

    def sums_of(source):
        def step(h, carry):
            value = source[row_at(h), :]
            return carry[0] + tile_sums(value), carry[1] + tile_sums(value * value)

        return grid_rows(step, (zeros8, zeros8))

    step_here = jnp.full((1, c), inputs.step_index[row], jnp.int32)

    def condition(table):
        total = jnp.zeros((1, 2 * c), F32)
        chosen = jnp.concatenate([step_here, step_here], axis=1)
        for s in range(table.shape[0]):
            total = total + jnp.where(chosen == s, table[s : s + 1, :], 0.0)
        return total[:, :c], total[:, c:]

    for copy in own[:2]:
        copy.wait()
    for copy in frame_copies:
        copy.wait_recv()
    fields = scratch.fields
    fields[...] = jnp.zeros(fields.shape, F32)
    frame_of = lax.broadcasted_iota(jnp.int32, (history, width), 0) // FIELDS
    keep = (frame_of >= HIST - inputs.counts[row]).astype(F32)
    masks = []
    for source in range(line):
        for k in range(strip):
            columns = slice((source * strip + k) * width, (source * strip + k + 1) * width)
            mask = mask_in[source, k : k + 1, :].astype(F32)
            masks.append(mask)
            fields[0:history, columns] = frames_in[source, :, k, :] * keep * mask
            fields[history : history + 1, columns] = mask
    lifted = scratch.lifted
    lifted[...] = dot(fields[...], lift[...], TN, HIGH)

    enc_scale, enc_shift = condition(inputs.enc_step_table)
    dec_scale, dec_shift = condition(inputs.dec_step_table)

    mean_e1, inv_e1 = norm_of(*sums_of(lifted), ones16, count16)
    gain_e1, bias_e1 = inputs.enc_norm1_gain[...], inputs.enc_norm1_bias[...]
    a_e1 = inv_e1 * gain_e1
    activate(lifted, scratch.xe1, scratch.te1, scratch.slope_e1, a_e1, bias_e1 - mean_e1 * a_e1)
    middle_e = scratch.middle_e
    mean_e2, inv_e2 = norm_of(
        *conv_norm([(scratch.xe1, scratch.fe1)], middle_e), ones16, count16
    )
    gain_e2, bias_e2 = inputs.enc_norm2_gain[...], inputs.enc_norm2_bias[...]
    a_e2 = inv_e2 * gain_e2
    activate(
        middle_e,
        scratch.xe2,
        scratch.te2,
        scratch.slope_e2,
        a_e2 * (1.0 + enc_scale),
        (bias_e2 - mean_e2 * a_e2) * (1.0 + enc_scale) + enc_shift,
    )
    encoded = scratch.encoded
    conv2_bias = inputs.enc_conv2_bias[...]
    joined = scratch.joined

    def encode(i, carry):
        value = fold(conv_chunk([(scratch.xe2, scratch.fe2)], i))
        value = value + conv2_bias + lifted[chunk_at(i), :]
        encoded[chunk_at(i), :] = value
        high, low = split(value)
        joined[chunk_at(i), c : 2 * c] = high
        joined[chunk_at(i), 3 * c : 4 * c] = low
        put_turned(scratch.turned, chunk_at(i), value, 1, 3)
        return carry[0] + tile_sums(value), carry[1] + tile_sums(value * value)

    sums_enc = lax.fori_loop(0, cells // CHUNK, encode, (zeros8, zeros8))

    half_cells, quarter = cells // 2, cells // 4

    def pick(source):
        pieces = []
        for b in range(2):
            value = source[pl.ds(b, half_cells, stride=2), :]
            value = value.reshape(height // 2, 2, width // 2, c)
            pieces.append([value[:, a].reshape(quarter, c) for a in range(2)])
        return [pieces[b][a] for a in range(2) for b in range(2)]

    def place_cells(target, pieces):
        for b in range(2):
            both = [pieces[2 * a + b].reshape(height // 2, 1, width // 2, c) for a in range(2)]
            value = jnp.concatenate(both, axis=1).reshape(half_cells, c)
            target[pl.ds(b, half_cells, stride=2), :] = value

    x_down = scratch.x_down
    for k, piece in enumerate(pick(encoded)):
        high, low = split(piece)
        x_down[:, k * c : (k + 1) * c] = high
        x_down[:, (k + 4) * c : (k + 5) * c] = low
    lowered = fold(dot(x_down[...], scratch.f_down[...])) + inputs.reducer_bias[...]
    x_up = scratch.x_up
    high, low = split(lowered)
    x_up[:, 0:c] = high
    x_up[:, c : 2 * c] = low
    raised = scratch.raised
    up_bias = inputs.up_bias[...]
    place_cells(
        raised, [fold(dot(x_up[...], scratch.f_up[k])) + up_bias for k in range(4)]
    )

    def raise_row(h, carry):
        value = raised[row_at(h), :]
        high, low = split(value)
        joined[row_at(h), 0:c] = high
        joined[row_at(h), 2 * c : 3 * c] = low
        put_turned(scratch.turned, row_at(h), value, 0, 2)
        return carry[0] + tile_sums(value), carry[1] + tile_sums(value * value)

    sums_raised = grid_rows(raise_row, (zeros8, zeros8))

    halves = []
    for half, (source, sums) in enumerate(((raised, sums_raised), (encoded, sums_enc))):
        mean, inv = norm_of(*sums, ones32, count32)
        gain = inputs.dec_norm1_gain[half : half + 1, :]
        bias = inputs.dec_norm1_bias[half : half + 1, :]
        scale = inv * gain
        activate(
            source,
            (scratch.xd1a, scratch.xd1b)[half],
            (scratch.td1a, scratch.td1b)[half],
            (scratch.slope_d1a, scratch.slope_d1b)[half],
            scale,
            bias - mean * scale,
        )
        halves.append((source, mean, inv, gain))
    middle_d = scratch.middle_d
    pairs = [(scratch.xd1a, scratch.fd1a), (scratch.xd1b, scratch.fd1b)]
    mean_d2, inv_d2 = norm_of(*conv_norm(pairs, middle_d), ones16, count16)
    gain_d2, bias_d2 = inputs.dec_norm2_gain[...], inputs.dec_norm2_bias[...]
    a_d2 = inv_d2 * gain_d2
    activate(
        middle_d,
        scratch.xd2,
        scratch.td2,
        scratch.slope_d2,
        a_d2 * (1.0 + dec_scale),
        (bias_d2 - mean_d2 * a_d2) * (1.0 + dec_scale) + dec_shift,
    )
    result = scratch.result
    last_bias = inputs.dec_conv2_bias[...] + inputs.skip_bias[...]

    def decode(i, carry):
        value = conv_chunk([(scratch.xd2, scratch.fd2)], i)
        value = value + dot(joined[chunk_at(i), :], scratch.f_skip[...])
        result[chunk_at(i), :] = fold(value) + last_bias
        return carry

    lax.fori_loop(0, cells // CHUNK, decode, 0)
    own_output = pltpu.make_async_copy(
        result.at[here_rows], outputs.output.at[row], local_sem.at[10]
    )
    own_output.start()
    for k in range(1, line):
        to = lax.rem(row + k, line)
        there = pl.ds(pl.multiple_of(to * strip_cells, strip_cells), strip_cells)
        output_copies.append(
            send(result.at[there], outputs.output.at[row], place.device_at(to))
        )

    exchanges = []
    waiting_runs = list(runs)
    landing_at = 0
    sem_at = 4 * (line - 1) + 2 * (line - 1)
    sums, final = scratch.sums, scratch.final

    def begin():
        nonlocal landing_at, sem_at
        start, rows = waiting_runs.pop(0)
        kind = Exchange if waiting_runs else SmallExchange
        exchange = kind(place, start, rows, landing_at, sem_at)
        landing_at += rows - rows // (8 * line)
        sem_at += exchange.count()
        exchanges.append(exchange)
        exchange.advance()

    final_copies = []

    def publish():
        for k, exchange in enumerate(exchanges):
            if k == len(final_copies) and exchange.done():
                rows = pl.ds(exchange.start, exchange.rows)
                copy = pltpu.make_async_copy(
                    final.at[rows], outputs.gradients.at[rows], local_sem.at[11 + k]
                )
                copy.start()
                final_copies.append(copy)

    def tick():
        for exchange in exchanges:
            if not exchange.done():
                exchange.advance()
        publish()

    def small_row(k, value):
        sums[small_at + k : small_at + k + 1, :] = value

    def spread_grad(source):
        def step(h, carry):
            value = source[row_at(h), :]
            put_row(scratch.xg, h, value)
            return carry + tile_sums(value)

        return grid_rows(step, zeros8)

    def weight_grad(turned, at, depth):
        lhs = turned[...]
        for a in range(3):
            rows = pl.ds((2 - a) * width, cells)
            part = fold_rows(dot(lhs, scratch.xg[rows, :]))
            for b in range(3):
                high, low = HIGH_AT[2 - b] * c, LOW_AT[2 - b] * c
                to = at + (3 * a + b) * depth
                sums[to : to + c, :] = part[:, high : high + c] + part[:, low : low + c]
            if a == 1:
                tick()

    def back_conv(weight, slope, target, source, mean, inv):
        def step(i, carry):
            value = fold(conv_chunk([(scratch.xg, weight)], i, NT)) * slope[chunk_at(i), :]
            target[chunk_at(i), :] = value
            normed = (source[chunk_at(i), :] - mean) * inv
            return carry[0] + tile_sums(value), carry[1] + tile_sums(value * normed)

        return lax.fori_loop(0, cells // CHUNK, step, (zeros8, zeros8))

    def norm_grad(sums_in, scale, ones, count):
        one, two = group_sums(sums_in[0] * scale, sums_in[1] * scale, ones)
        return one / count, two / count

    own[2].wait()
    for copy in cot_copies:
        copy.wait_recv()
    total_cot = column_sum(spread_grad(cot))
    weight_grad(scratch.td2, starts.dec_conv2, c)
    part = fold(dot(scratch.turned[...], scratch.xg[width : cells + width, 2 * c : 4 * c]))
    sums[starts.skip_weight : starts.skip_weight + 2 * c, :] = fold_rows(part)
    small_row(23, total_cot)
    begin()

    grad = scratch.grad
    sums_d2 = back_conv(scratch.bd2, scratch.slope_d2, grad, middle_d, mean_d2, inv_d2)
    tick()
    side_grads = (scratch.grad_a, scratch.grad_b)
    for half in range(2):

        def skip_back(i, carry, half=half):
            rows = pl.ds(pl.multiple_of(i * CHUNK + width, width), CHUNK)
            value = dot(scratch.xg[rows, 2 * c : 4 * c], scratch.b_skip[half], NT)
            side_grads[half][chunk_at(i), :] = fold(value)
            return carry

        lax.fori_loop(0, cells // CHUNK, skip_back, 0)
    tick()

    def table_rows(k, sums_in, gain, bias, one_plus):
        plain, times = column_sum(sums_in[0]), column_sum(sums_in[1])
        for s in range(inputs.enc_step_table.shape[0]):
            small_row(k + 2 * s, jnp.where(step_here == s, gain * times + bias * plain, 0.0))
            small_row(k + 2 * s + 1, jnp.where(step_here == s, plain, 0.0))
        return one_plus * times, one_plus * plain

    def middle_grad(source, mean, inv, scale, sums_in):
        zero, slope = norm_grad(sums_in, scale, ones16, count16)

        def step(h, carry):
            normed = (source[row_at(h), :] - mean) * inv
            value = inv * (grad[row_at(h), :] * scale - zero - normed * slope)
            put_row(scratch.xg, h, value)
            return carry

        grid_rows(step)

    gain_row, bias_row = table_rows(40, sums_d2, gain_d2, bias_d2, 1.0 + dec_scale)
    small_row(28, gain_row)
    small_row(29, bias_row)
    middle_grad(middle_d, mean_d2, inv_d2, gain_d2 * (1.0 + dec_scale), sums_d2)
    weight_grad(scratch.td1a, starts.dec_conv1, 2 * c)
    tick()
    weight_grad(scratch.td1b, starts.dec_conv1 + c, 2 * c)
    tick()
    begin()

    for half, (source, mean, inv, gain) in enumerate(halves):
        sums_in = back_conv(
            (scratch.bd1a, scratch.bd1b)[half],
            (scratch.slope_d1a, scratch.slope_d1b)[half],
            grad,
            source,
            mean,
            inv,
        )
        tick()
        small_row(24 + half, column_sum(sums_in[1]))
        small_row(26 + half, column_sum(sums_in[0]))
        zero, slope = norm_grad(sums_in, gain, ones32, count32)
        target = side_grads[half]

        def input_grad(h, carry):
            normed = (source[row_at(h), :] - mean) * inv
            value = inv * (grad[row_at(h), :] * gain - zero - normed * slope)
            value = target[row_at(h), :] + value
            target[row_at(h), :] = value
            return carry + tile_sums(value)

        total = grid_rows(input_grad, zeros8)
        if half == 0:
            small_row(22, column_sum(total))

    grad_raised, grad_encoded = side_grads
    x_grad_up = scratch.x_grad_up
    for k, piece in enumerate(pick(grad_raised)):
        high, low = split(piece)
        x_grad_up[:, k * c : (k + 1) * c] = high
        x_grad_up[:, (k + 4) * c : (k + 5) * c] = low
    grad_lowered = fold(dot(x_grad_up[...], scratch.b_up[...], NT))
    small_row(21, jnp.sum(grad_lowered, axis=0, keepdims=True))
    x_grad_low = scratch.x_grad_low
    high, low = split(grad_lowered)
    x_grad_low[:, 0:c] = high
    x_grad_low[:, c : 2 * c] = low
    part = fold(fold_rows(dot(x_up[...], x_grad_up[...], TN)))
    for k in range(4):
        at = starts.up_weight + k * c
        sums[at : at + c, :] = part[:, k * c : (k + 1) * c]
    part = fold_rows(fold(dot(x_down[...], x_grad_low[...], TN)))
    sums[starts.reducer_weight : starts.reducer_weight + 4 * c, :] = part
    begin()
    place_cells(
        grad, [fold(dot(x_grad_low[...], scratch.b_down[k], NT)) for k in range(4)]
    )

    def join_row(h, carry):
        value = grad_encoded[row_at(h), :] + grad[row_at(h), :]
        grad_encoded[row_at(h), :] = value
        put_row(scratch.xg, h, value)
        return carry + tile_sums(value)

    small_row(20, column_sum(grid_rows(join_row, zeros8)))
    tick()
    weight_grad(scratch.te2, starts.enc_conv2, c)
    tick()
    begin()
    sums_e2 = back_conv(scratch.be2, scratch.slope_e2, grad, middle_e, mean_e2, inv_e2)
    tick()
    gain_row, bias_row = table_rows(32, sums_e2, gain_e2, bias_e2, 1.0 + enc_scale)
    small_row(18, gain_row)
    small_row(19, bias_row)
    middle_grad(middle_e, mean_e2, inv_e2, gain_e2 * (1.0 + enc_scale), sums_e2)
    weight_grad(scratch.te1, starts.enc_conv1, c)
    tick()
    begin()
    sums_e1 = back_conv(scratch.be1, scratch.slope_e1, grad, lifted, mean_e1, inv_e1)
    tick()
    small_row(16, column_sum(sums_e1[1]))
    small_row(17, column_sum(sums_e1[0]))
    zero, slope = norm_grad(sums_e1, gain_e1, ones16, count16)

    def lifted_grad(h, carry):
        normed = (lifted[row_at(h), :] - mean_e1) * inv_e1
        value = inv_e1 * (grad[row_at(h), :] * gain_e1 - zero - normed * slope)
        grad[row_at(h), :] = grad_encoded[row_at(h), :] + value
        return carry

    grid_rows(lifted_grad)
    tick()

    sums[small_at : small_at + 16, :] = dot(fields[...], grad[...], NN, HIGH)
    for k in (30, 31):
        small_row(k, jnp.zeros((1, c), F32))
    rest = small_at + 48
    sums[rest:total_rows, :] = jnp.zeros((total_rows - rest, c), F32)
    begin()
    back = dot(lift[...], grad[...], NT, HIGH)
    frames_out = scratch.frames_out
    for source in range(line):
        for k in range(strip):
            h = source * strip + k
            value = back[0:history, h * width : (h + 1) * width]
            frames_out[source, :, k, :] = value * keep * masks[h]
    own_frames = pltpu.make_async_copy(
        frames_out.at[row], outputs.frames_grad.at[row], local_sem.at[18]
    )
    own_frames.start()
    for k in range(1, line):
        to = lax.rem(row + k, line)
        output_copies.append(
            send(frames_out.at[to], outputs.frames_grad.at[row], place.device_at(to))
        )

    while not all(exchange.done() for exchange in exchanges):
        tick()

    for copy in output_copies:
        copy.wait_recv()
    own_output.wait()
    own_frames.wait()
    for copy in final_copies:
        copy.wait()
    for copy in frame_copies + cot_copies + output_copies:
        copy.wait_send()
    for exchange in exchanges:
        for copy in exchange.copies:
            copy.wait_send()


def write_kernel(layout, *refs):
    shapes, starts, small_at = layout
    output, frames_grad, gradients = refs[:3]
    outputs = refs[3:-4]
    output_here, frames_here, gradients_here, sem = refs[-4:]
    c = gradients.shape[1]
    moves = [(frames_grad, frames_here, outputs[1])]
    for k, name in enumerate(LARGE):
        rows = pl.ds(starts[name], shapes[name][0])
        moves.append((gradients.at[rows], gradients_here.at[rows], outputs[2 + k]))
    moves.append((output, output_here, outputs[0]))
    small = pl.ds(small_at, SMALL_COUNT)
    first = pltpu.make_async_copy(gradients.at[small], gradients_here.at[small], sem.at[0])
    first.start()
    arriving, leaving = [], []
    for k, (source, here, _) in enumerate(moves):
        arriving.append(pltpu.make_async_copy(source, here, sem.at[1 + 2 * k]))
        arriving[-1].start()
    first.wait()
    for target, (k, rows) in zip(outputs[2 + len(LARGE) :], SMALL_ROWS.values()):
        at = small_at + k
        if rows == 8:
            for s in range(target.shape[0]):
                target[s : s + 1, 0:c] = gradients_here[at + 2 * s : at + 2 * s + 1, :]
                target[s : s + 1, c : 2 * c] = gradients_here[at + 2 * s + 1 : at + 2 * s + 2, :]
        else:
            target[...] = gradients_here[at : at + rows, :]
    for k, (_, here, target) in enumerate(moves):
        arriving[k].wait()
        leaving.append(pltpu.make_async_copy(here, target, sem.at[2 + 2 * k]))
        leaving[-1].start()
    for copy in leaving:
        copy.wait()


def whole_items(shape, *arguments):
    line = shape["rows"]
    whole = Given(*arguments)
    given = whole._asdict()
    frames, cotangent = whole.frames, whole.cotangent
    items, history, strip, width = frames.shape
    c = cotangent.shape[-1]
    cells = strip * line * width
    flat = {}
    for name, value in given.items():
        if value is cotangent:
            value = value.reshape(items, strip * width, c)
        elif name in LARGE:
            value = value.reshape(-1, c)
        elif value.ndim == 1 and name not in IN_SMEM:
            value = value.reshape(-1, c)
        flat[name] = value
    shapes = {name: flat[name].shape for name in LARGE}
    big_layout = layout_of(shapes)
    starts, small_at, total_rows, runs = big_layout
    copies = 7 * (line - 1) + len(runs) * (6 + 2 * (line - 1)) + 8
    landing = sum(rows - rows // (8 * line) for _, rows in runs)
    shifted = pltpu.VMEM((cells + 2 * width, 6 * c), BF16)
    forward = pltpu.VMEM((18 * c, 2 * c), BF16)
    backward = pltpu.VMEM((2 * c, 18 * c), BF16)
    field = pltpu.VMEM((cells, c), F32)
    flipped_field = pltpu.VMEM((2 * c, cells), BF16)
    quarter = cells // 4
    scratch = dict(
        send=pltpu.SemaphoreType.DMA((copies,)),
        recv=pltpu.SemaphoreType.DMA((copies,)),
        local=pltpu.SemaphoreType.DMA((19,)),
        sums=pltpu.VMEM((total_rows, c), F32),
        final=pltpu.VMEM((total_rows, c), F32),
        landing=pltpu.VMEM((landing, c), F32),
        frames_in=pltpu.VMEM((line, history, strip, width), F32),
        mask_in=pltpu.VMEM((line, strip, width), jnp.int32),
        frames_out=pltpu.VMEM((line, history, strip, width), F32),
        fields=pltpu.VMEM((16, cells), F32),
        lift=pltpu.VMEM((16, c), F32),
        joined=pltpu.VMEM((cells, 4 * c), BF16),
        x_down=pltpu.VMEM((quarter, 8 * c), BF16),
        x_grad_up=pltpu.VMEM((quarter, 8 * c), BF16),
        x_up=pltpu.VMEM((quarter, 2 * c), BF16),
        x_grad_low=pltpu.VMEM((quarter, 2 * c), BF16),
        f_down=pltpu.VMEM((8 * c, 2 * c), BF16),
        b_down=pltpu.VMEM((4, 2 * c, 2 * c), BF16),
        f_up=pltpu.VMEM((4, 2 * c, 2 * c), BF16),
        b_up=pltpu.VMEM((2 * c, 8 * c), BF16),
        f_skip=pltpu.VMEM((4 * c, 2 * c), BF16),
        b_skip=pltpu.VMEM((2, 2 * c, 2 * c), BF16),
        xe1=shifted,
        xe2=shifted,
        xd1a=shifted,
        xd1b=shifted,
        xd2=shifted,
        xg=shifted,
        te1=flipped_field,
        te2=flipped_field,
        td1a=flipped_field,
        td1b=flipped_field,
        td2=flipped_field,
        turned=pltpu.VMEM((4 * c, cells), BF16),
        fe1=forward,
        fe2=forward,
        fd1a=forward,
        fd1b=forward,
        fd2=forward,
        be1=backward,
        be2=backward,
        bd1a=backward,
        bd1b=backward,
        bd2=backward,
        slope_e1=field,
        slope_e2=field,
        slope_d1a=field,
        slope_d1b=field,
        slope_d2=field,
        lifted=field,
        middle_e=field,
        encoded=field,
        raised=field,
        middle_d=field,
        result=field,
        cot=field,
        grad=field,
        grad_a=field,
        grad_b=field,
    )
    scratch.update({name: pltpu.VMEM(shapes[name], F32) for name in LARGE})

    in_hbm = pl.BlockSpec(memory_space=pl.ANY)
    in_vmem = pl.BlockSpec(memory_space=pltpu.VMEM)
    in_smem = pl.BlockSpec(memory_space=pltpu.SMEM)
    in_specs = [
        in_hbm if name in IN_HBM else in_smem if name in IN_SMEM else in_vmem
        for name in ARGUMENTS
    ]
    out_shape = [
        jax.ShapeDtypeStruct((items, strip * width, c), F32),
        jax.ShapeDtypeStruct(frames.shape, F32),
        jax.ShapeDtypeStruct((total_rows, c), F32),
    ]
    out_specs = [in_hbm] * 3
    results = pl.pallas_call(
        functools.partial(
            item_kernel,
            (line, strip, width, shapes, big_layout),
            tuple(scratch),
        ),
        out_shape=out_shape,
        in_specs=in_specs,
        out_specs=out_specs,
        scratch_shapes=list(scratch.values()),
        compiler_params=pltpu.CompilerParams(
            collective_id=0, has_side_effects=True, vmem_limit_bytes=62 * 1024 * 1024
        ),
    )(*[flat[name] for name in ARGUMENTS])
    names = LARGE + tuple(SMALL_ROWS)
    written = pl.pallas_call(
        functools.partial(write_kernel, (shapes, starts, small_at)),
        out_shape=out_shape[:2] + [jax.ShapeDtypeStruct(flat[name].shape, F32) for name in names],
        in_specs=[pl.BlockSpec(memory_space=pltpu.HBM)] * 3,
        out_specs=[in_hbm] * (2 + len(LARGE)) + [in_vmem] * len(SMALL_ROWS),
        scratch_shapes=[
            pltpu.VMEM((items, strip * width, c), F32),
            pltpu.VMEM(frames.shape, F32),
            pltpu.VMEM((total_rows, c), F32),
            pltpu.SemaphoreType.DMA((1 + 2 * (2 + len(LARGE)),)),
        ],
        compiler_params=pltpu.CompilerParams(vmem_limit_bytes=60 * 1024 * 1024),
    )(*results)
    grads = dict(zip(names, written[2:]))
    ordered = [name for name in ARGUMENTS if name in grads]
    return (written[0].reshape(cotangent.shape), written[1]) + tuple(
        grads[name].reshape(given[name].shape) for name in ordered
    )


def body(shape, *arguments):
    items, _, strip, width = arguments[0].shape
    line = shape["rows"]
    whole = (
        shape["section"] == 2
        and shape["batch"] == 4
        and items == line
        and arguments[-1].shape[-1] == 128
        and (strip * line * width) % CHUNK == 0
    )
    return whole_items(shape, *arguments) if whole else strips_body(*arguments)


def solution(mesh):
    in_specs = (
        P(("section", "batch"), None, "rows", None),
        P(("section", "batch")),
        P(("section", "batch"), "rows", None),
        P(("section", "batch")),
        P(),
        P(),
        P(),
        P(),
        P(),
        P(),
        P(),
        P(),
        P(),
        P(),
        P(),
        P(),
        P(),
        P(),
        P(),
        P(),
        P(),
        P(),
        P(),
        P(),
        P(),
        P(),
        P(),
        P(),
        P(("section", "batch"), "rows", None, None),
    )
    out_specs = (
        P(("section", "batch"), "rows", None, None),
        P(("section", "batch"), None, "rows", None),
        P(),
        P(),
        P(),
        P(),
        P(),
        P(),
        P(),
        P(),
        P(),
        P(),
        P(),
        P(),
        P(),
        P(),
        P(),
        P(),
        P(),
        P(),
        P(),
        P(),
        P(),
        P(),
        P(),
        P(),
    )
    return jax.shard_map(functools.partial(body, mesh.shape), mesh=mesh, in_specs=in_specs, out_specs=out_specs, check_vma=False)
```

```python
import functools
from types import SimpleNamespace
from typing import Any, NamedTuple

import jax
import jax.numpy as jnp
from jax import lax
from jax.experimental import pallas as pl
from jax.experimental.pallas import tpu as pltpu
from jax.sharding import PartitionSpec as P

GROUPS = 8
FIELDS = 3
HIST = 4


EPS = 1e-05
HIGH = lax.Precision.HIGHEST


def extended(cells, sides, width):
    for axis, dim in sides:
        count = lax.axis_size(axis)
        ends = count - 1
        head = lax.slice_in_dim(cells, 0, width, axis=dim)
        tail = lax.slice_in_dim(cells, cells.shape[dim] - width, cells.shape[dim], axis=dim)
        cells = jnp.concatenate(
            [
                lax.ppermute(tail, axis, [(i, (i + 1) % count) for i in range(ends)]),
                cells,
                lax.ppermute(head, axis, [((i + 1) % count, i) for i in range(ends)]),
            ],
            axis=dim,
        )
    return cells


def from_behind(value, axis, steps):
    count = lax.axis_size(axis)
    pairs = [(source, (source + steps) % count) for source in range(count)]
    return lax.ppermute(value, axis, pairs)


def group_view(value_arrays):
    extent = value_arrays.shape
    return value_arrays.reshape(extent[:-1] + (GROUPS, extent[-1] // GROUPS))


def global_sums(value_arrays):
    grouped = group_view(value_arrays)
    flat = grouped.reshape(-1, GROUPS, grouped.shape[-1])
    first_sum = jnp.sum(flat, axis=(0, 2))
    second_sum = jnp.sum(flat * flat, axis=(0, 2))
    return lax.psum((first_sum, second_sum), "rows")


def apply_norm(value_arrays, sum_one, sum_two, norm_gain, norm_bias, total):
    grouped = group_view(value_arrays)
    group_mean = sum_one / total
    variance = sum_two / total - group_mean * group_mean
    inverse = lax.rsqrt(variance + EPS)
    normed = (grouped - group_mean[:, None]) * inverse[:, None]
    return normed.reshape(value_arrays.shape) * norm_gain + norm_bias


def norm_back(value_arrays, grad_one, grad_two):
    grouped = group_view(value_arrays)
    extra = grad_one[:, None] + 2.0 * grouped * grad_two[:, None]
    return extra.reshape(value_arrays.shape)


def reduce_grads(grad_one, grad_two):
    return lax.psum((grad_one, grad_two), "rows")


def conv_rows(padded, kernel):
    widened = jnp.pad(padded, ((0, 0), (1, 1), (0, 0)))
    return lax.conv_general_dilated(
        widened[None],
        kernel,
        (1, 1),
        "VALID",
        dimension_numbers=("NHWC", "HWIO", "NHWC"),
        precision=HIGH,
    )[0]


def flipped(kernel):
    return jnp.transpose(kernel[::-1, ::-1], (0, 1, 3, 2))


def pad_grads(value_arrays):
    return extended(value_arrays, (("rows", 0),), 1)


def totals_of(inputs, conv1):
    strip = inputs.shape[0]
    cells = strip * lax.axis_size("rows") * inputs.shape[1]
    return (cells * (inputs.shape[2] // GROUPS), cells * (conv1.shape[3] // GROUPS))


def block_forward(inputs, weights, scale_part, shift_part):
    norm1_gain, norm1_bias, conv1, norm2_gain, norm2_bias, conv2, conv2_bias = weights
    total_in, total_mid = totals_of(inputs, conv1)
    sums_in = global_sums(inputs)

    def pad_rows(value_arrays):
        return extended(value_arrays, (("rows", 0),), 1)

    act_one = pad_rows(
        jax.nn.gelu(
            apply_norm(inputs, sums_in[0], sums_in[1], norm1_gain, norm1_bias, total_in),
            approximate=False,
        )
    )
    middle = conv_rows(act_one, conv1)
    sums_mid = global_sums(middle)
    shaped = (
        apply_norm(middle, sums_mid[0], sums_mid[1], norm2_gain, norm2_bias, total_mid)
        * (1.0 + scale_part)
        + shift_part
    )
    act_two = pad_rows(jax.nn.gelu(shaped, approximate=False))
    branch = conv_rows(act_two, conv2) + conv2_bias
    return (branch, (sums_in[0], sums_in[1], act_one, middle, sums_mid[0], sums_mid[1], act_two))


def block_backward(inputs, weights, scale_part, shift_part, kept, grad_out):
    norm1_gain, norm1_bias, conv1, norm2_gain, norm2_bias, conv2, conv2_bias = weights
    in_one, in_two, act_one, middle, mid_one, mid_two, act_two = kept
    total_in, total_mid = totals_of(inputs, conv1)
    grad_conv2 = jax.vjp(lambda kernel: conv_rows(act_two, kernel), conv2)[1](grad_out)[0]
    grad_bias2 = jnp.sum(grad_out, axis=(0, 1))
    grad_act_two = conv_rows(pad_grads(grad_out), flipped(conv2))

    def second_piece(middle_in, sum_one, sum_two, gain_in, incoming_bias, scale_in, shift_in):
        shaped = (
            apply_norm(middle_in, sum_one, sum_two, gain_in, incoming_bias, total_mid)
            * (1.0 + scale_in)
            + shift_in
        )
        return jax.nn.gelu(shaped, approximate=False)

    second_pull = jax.vjp(
        second_piece, middle, mid_one, mid_two, norm2_gain, norm2_bias, scale_part, shift_part
    )[1](grad_act_two)
    summed_one, summed_two = reduce_grads(second_pull[1], second_pull[2])
    grad_middle = second_pull[0] + norm_back(middle, summed_one, summed_two)
    grad_conv1 = jax.vjp(lambda kernel: conv_rows(act_one, kernel), conv1)[1](grad_middle)[0]
    grad_act_one = conv_rows(pad_grads(grad_middle), flipped(conv1))

    def first_piece(inputs_in, sum_one, sum_two, gain_in, incoming_bias):
        return jax.nn.gelu(
            apply_norm(inputs_in, sum_one, sum_two, gain_in, incoming_bias, total_in),
            approximate=False,
        )

    first_pull = jax.vjp(first_piece, inputs, in_one, in_two, norm1_gain, norm1_bias)[1](
        grad_act_one
    )
    first_one, first_two = reduce_grads(first_pull[1], first_pull[2])
    grad_inputs = first_pull[0] + norm_back(inputs, first_one, first_two)
    grads = (
        first_pull[3],
        first_pull[4],
        grad_conv1,
        second_pull[3],
        second_pull[4],
        grad_conv2,
        grad_bias2,
    )
    return (grad_inputs, grads, second_pull[5], second_pull[6])


def conditioning(step_item, table):
    one_hot = (jnp.arange(table.shape[0], dtype=jnp.int32) == step_item).astype(jnp.float32)
    condition = jnp.dot(one_hot, table, precision=HIGH)
    half_width = table.shape[1] // 2
    return (condition[:half_width], condition[half_width:], one_hot)


def project_in(frames_item, mask_item, count_item, incoming_weight, incoming_bias):
    history = jnp.arange(HIST, dtype=jnp.int32) >= HIST - count_item
    keep = jnp.repeat(history, FIELDS).astype(jnp.float32)
    lifted = (
        jnp.einsum(
            "fhw,fc->hwc", frames_item * keep[:, None, None], incoming_weight, precision=HIGH
        )
        + incoming_bias
    )
    return lifted * mask_item[:, :, None].astype(jnp.float32)


def coarsen_field(value_arrays, incoming_weight, incoming_bias):
    rows_here, width_here, depth_here = value_arrays.shape
    blocks = value_arrays.reshape(rows_here // 2, 2, width_here // 2, 2, depth_here)
    return jnp.einsum("iajbk,abkc->ijc", blocks, incoming_weight, precision=HIGH) + incoming_bias


def upsample(value_arrays, incoming_weight, incoming_bias):
    result = jnp.einsum("ijk,abkc->iajbc", value_arrays, incoming_weight, precision=HIGH)
    extent = result.shape
    return result.reshape(extent[0] * 2, extent[2] * 2, extent[4]) + incoming_bias


def flatten_all(pieces):
    return jnp.concatenate([piece.reshape(-1) for piece in pieces])


def unflatten_all(flat, templates):
    pieces = []
    offset_at = 0
    for template in templates:
        count_here = template.size
        pieces.append(flat[offset_at : offset_at + count_here].reshape(template.shape))
        offset_at += count_here
    return tuple(pieces)


def strips_body(
    frames,
    counts,
    cell_mask,
    step_index,
    lift_weight,
    lift_bias,
    enc_norm1_gain,
    enc_norm1_bias,
    enc_conv1,
    enc_step_table,
    enc_norm2_gain,
    enc_norm2_bias,
    enc_conv2,
    enc_conv2_bias,
    reducer_weight,
    reducer_bias,
    up_weight,
    up_bias,
    dec_norm1_gain,
    dec_norm1_bias,
    dec_conv1,
    dec_step_table,
    dec_norm2_gain,
    dec_norm2_bias,
    dec_conv2,
    dec_conv2_bias,
    skip_weight,
    skip_bias,
    cotangent,
):
    enc_weights = (
        enc_norm1_gain,
        enc_norm1_bias,
        enc_conv1,
        enc_norm2_gain,
        enc_norm2_bias,
        enc_conv2,
        enc_conv2_bias,
    )
    dec_weights = (
        dec_norm1_gain,
        dec_norm1_bias,
        dec_conv1,
        dec_norm2_gain,
        dec_norm2_bias,
        dec_conv2,
        dec_conv2_bias,
    )
    params = (
        lift_weight,
        lift_bias,
        enc_norm1_gain,
        enc_norm1_bias,
        enc_conv1,
        enc_step_table,
        enc_norm2_gain,
        enc_norm2_bias,
        enc_conv2,
        enc_conv2_bias,
        reducer_weight,
        reducer_bias,
        up_weight,
        up_bias,
        dec_norm1_gain,
        dec_norm1_bias,
        dec_conv1,
        dec_step_table,
        dec_norm2_gain,
        dec_norm2_bias,
        dec_conv2,
        dec_conv2_bias,
        skip_weight,
        skip_bias,
    )

    def forward_micro(carry, sliced):
        frames_item, mask_item, count_item, step_item = sliced
        lifted = project_in(frames_item, mask_item, count_item, lift_weight, lift_bias)
        enc_scale, enc_shift, unused_hot = conditioning(step_item, enc_step_table)
        enc_branch, enc_kept = block_forward(lifted, enc_weights, enc_scale, enc_shift)
        encoder_result = lifted + enc_branch
        coarse_field = coarsen_field(encoder_result, reducer_weight, reducer_bias)
        foreign = from_behind(coarse_field, "section", 1)
        raised_foreign = upsample(foreign, up_weight, up_bias)
        raised = from_behind(raised_foreign, "section", 1)
        joined = jnp.concatenate([raised, encoder_result], axis=-1)
        dec_scale, dec_shift, unused_again = conditioning(step_item, dec_step_table)
        dec_branch, dec_kept = block_forward(joined, dec_weights, dec_scale, dec_shift)
        output_item = jnp.dot(joined, skip_weight, precision=HIGH) + skip_bias + dec_branch
        return (carry, (output_item, (lifted, enc_kept, encoder_result, foreign, joined, dec_kept)))

    unused, (output, kept_all) = lax.scan(
        forward_micro, jnp.zeros((), jnp.float32), (frames, cell_mask, counts, step_index)
    )

    def backward_micro(totals, sliced):
        frames_item, mask_item, count_item, step_item, grad_out, kept = sliced
        lifted, enc_kept, encoder_result, foreign, joined, dec_kept = kept
        dec_scale, dec_shift, one_hot = conditioning(step_item, dec_step_table)
        grad_joined, dec_grads, dec_gscale, dec_gshift = block_backward(
            joined, dec_weights, dec_scale, dec_shift, dec_kept, grad_out
        )
        grad_skip_weight = jnp.einsum("hwk,hwc->kc", joined, grad_out, precision=HIGH)
        grad_skip_bias = jnp.sum(grad_out, axis=(0, 1))
        grad_joined = grad_joined + jnp.dot(grad_out, skip_weight.T, precision=HIGH)
        half_width = joined.shape[-1] // 2
        grad_raised = grad_joined[..., :half_width]
        grad_encoded = grad_joined[..., half_width:]
        grad_foreign_up = from_behind(grad_raised, "section", 1)
        up_pull = jax.vjp(upsample, foreign, up_weight, up_bias)[1](grad_foreign_up)
        coarse_gradient = from_behind(up_pull[0], "section", 1)
        reducer_pullback = jax.vjp(coarsen_field, encoder_result, reducer_weight, reducer_bias)[1](
            coarse_gradient
        )
        grad_encoded = grad_encoded + reducer_pullback[0]
        enc_scale, enc_shift, enc_hot = conditioning(step_item, enc_step_table)
        grad_lifted, enc_grads, enc_gscale, enc_gshift = block_backward(
            lifted, enc_weights, enc_scale, enc_shift, enc_kept, grad_encoded
        )
        grad_lifted = grad_lifted + grad_encoded
        proj_pull = jax.vjp(
            lambda frames_in, incoming_weight, incoming_bias: project_in(
                frames_in, mask_item, count_item, incoming_weight, incoming_bias
            ),
            frames_item,
            lift_weight,
            lift_bias,
        )[1](grad_lifted)
        enc_table_grad = enc_hot[:, None] * jnp.concatenate([enc_gscale, enc_gshift])[None, :]
        dec_table_grad = one_hot[:, None] * jnp.concatenate([dec_gscale, dec_gshift])[None, :]
        micro_list = (
            proj_pull[1],
            proj_pull[2],
            enc_grads[0],
            enc_grads[1],
            enc_grads[2],
            enc_table_grad,
            enc_grads[3],
            enc_grads[4],
            enc_grads[5],
            enc_grads[6],
            reducer_pullback[1],
            reducer_pullback[2],
            up_pull[1],
            up_pull[2],
            dec_grads[0],
            dec_grads[1],
            dec_grads[2],
            dec_table_grad,
            dec_grads[3],
            dec_grads[4],
            dec_grads[5],
            dec_grads[6],
            grad_skip_weight,
            grad_skip_bias,
        )
        micro_flat = flatten_all(micro_list)
        return (totals + micro_flat, proj_pull[0])

    total_size = sum((piece.size for piece in params))
    start_totals = jnp.zeros((total_size,), jnp.float32)
    flat_totals, frames_grad = lax.scan(
        backward_micro,
        start_totals,
        (frames, cell_mask, counts, step_index, cotangent, kept_all),
        reverse=True,
    )
    flat_totals = lax.psum(flat_totals, ("section", "batch", "rows"))
    grads = unflatten_all(flat_totals, params)
    return (output, frames_grad) + grads


F32 = jnp.float32
BF16 = jnp.bfloat16
MESH = pl.DeviceIdType.MESH
NN = ((1,), (0,))
NT = ((1,), (1,))
TN = ((0,), (0,))
HIGH_AT = (0, 2, 1)
LOW_AT = (4, 3, 5)
CHUNK = 512
class Given(NamedTuple):
    frames: Any
    counts: Any
    cell_mask: Any
    step_index: Any
    lift_weight: Any
    lift_bias: Any
    enc_norm1_gain: Any
    enc_norm1_bias: Any
    enc_conv1: Any
    enc_step_table: Any
    enc_norm2_gain: Any
    enc_norm2_bias: Any
    enc_conv2: Any
    enc_conv2_bias: Any
    reducer_weight: Any
    reducer_bias: Any
    up_weight: Any
    up_bias: Any
    dec_norm1_gain: Any
    dec_norm1_bias: Any
    dec_conv1: Any
    dec_step_table: Any
    dec_norm2_gain: Any
    dec_norm2_bias: Any
    dec_conv2: Any
    dec_conv2_bias: Any
    skip_weight: Any
    skip_bias: Any
    cotangent: Any


ARGUMENTS = Given._fields
LARGE = tuple(dict(
    dec_conv2=0,
    skip_weight=0,
    dec_conv1=0,
    up_weight=0,
    reducer_weight=0,
    enc_conv2=0,
    enc_conv1=0,
))
IN_HBM = tuple(dict(frames=0, cell_mask=0, cotangent=0)) + LARGE
IN_SMEM = tuple(dict(counts=0, step_index=0))
SMALL_ROWS = dict(
    lift_weight=(0, 12),
    lift_bias=(12, 1),
    enc_norm1_gain=(16, 1),
    enc_norm1_bias=(17, 1),
    enc_norm2_gain=(18, 1),
    enc_norm2_bias=(19, 1),
    enc_conv2_bias=(20, 1),
    reducer_bias=(21, 1),
    up_bias=(22, 1),
    dec_conv2_bias=(23, 1),
    skip_bias=(23, 1),
    dec_norm1_gain=(24, 2),
    dec_norm1_bias=(26, 2),
    dec_norm2_gain=(28, 1),
    dec_norm2_bias=(29, 1),
    enc_step_table=(32, 8),
    dec_step_table=(40, 8),
)
SMALL_COUNT = 64
OUTPUTS = tuple(dict(output=0, frames_grad=0, gradients=0))


def split(value):
    high = value.astype(BF16)
    return high, (value - high.astype(F32)).astype(BF16)


def dot(left, right, dims=NN, precision=None):
    return lax.dot_general(
        left, right, (dims, ((), ())), precision=precision, preferred_element_type=F32
    )


def fold(value):
    half = value.shape[1] // 2
    return value[:, :half] + value[:, half:]


def fold_rows(value):
    half = value.shape[0] // 2
    return value[:half] + value[half:]


def tile_sums(value):
    return jnp.sum(value.reshape(-1, 8, value.shape[-1]), axis=0)


def column_sum(tiles):
    return jnp.sum(tiles, axis=0, keepdims=True)


def group_ones(channels, size):
    rows = lax.broadcasted_iota(jnp.int32, (channels, channels), 0) // size
    columns = lax.broadcasted_iota(jnp.int32, (channels, channels), 1) // size
    return (rows == columns).astype(F32)


def group_sums(first, second, ones):
    both = dot(jnp.concatenate([first, second], axis=0), ones, precision=HIGH)
    return column_sum(both[:8]), column_sum(both[8:])


class Exchange:

    def __init__(self, place, start, rows, landing, first_sem):
        self.place, self.start, self.rows, self.landing = place, start, rows, landing
        self.sem = first_sem
        self.stage = 0
        self.copies = []
        self.waiting = []
        self.group = place.plane_group
        self.half = rows // 2
        self.base = start + place.core * self.half
        self._finish(self.half)

    def _finish(self, size):
        self.part = size // self.group.count
        self.own = self.base + self.group.here * self.part
        self.shard = self.part // self.place.line.count
        self.last = self.own + self.place.line.here * self.shard

    def count(self):
        return 2 + 2 * (self.group.count - 1) + 2 * (self.place.line.count - 1)

    def _copy(self, source, target, device):
        place = self.place
        copy = pltpu.make_async_remote_copy(
            src_ref=source,
            dst_ref=target,
            send_sem=place.send.at[self.sem],
            recv_sem=place.recv.at[self.sem],
            device_id=device,
            device_id_type=MESH,
        )
        self.sem += 1
        copy.start()
        self.copies.append(copy)
        self.waiting.append(copy)

    def _wait(self):
        for copy in self.waiting:
            copy.wait_recv()
        self.waiting = []

    def _rows(self, at, size):
        return pl.ds(pl.multiple_of(at, 8), size)

    def _swap(self):
        place = self.place
        other = self._rows(self.start + (1 - place.core) * self.half, self.half)
        self.land = self.landing
        self.landing += self.half
        self._copy(
            place.sums.at[other], place.landing.at[pl.ds(self.land, self.half)], place.partner
        )

    def _add_swap(self):
        place = self.place
        block = 128

        def step(i, carry):
            here = self._rows(self.base + i * block, block)
            there = self._rows(self.land + i * block, block)
            place.sums[here] = place.sums[here] + place.landing[there]
            return carry

        lax.fori_loop(0, self.half // block, step, 0)

    def _scatter(self, group, base, size):
        place = self.place
        self.land = self.landing
        for k in range(1, group.count):
            to = lax.rem(group.here + k, group.count)
            self._copy(
                place.sums.at[self._rows(base + to * size, size)],
                place.landing.at[pl.ds(self.landing, size)],
                group.device(to),
            )
            self.landing += size

    def _total(self, group, own, size, target):
        place = self.place
        block = 8 if size % 32 else 32

        def step(i, carry):
            here = self._rows(own + i * block, block)
            total = place.sums[here]
            for k in range(group.count - 1):
                there = self._rows(self.land + k * size + i * block, block)
                total = total + place.landing[there]
            target[here] = total
            return carry

        lax.fori_loop(0, size // block, step, 0)

    def _gather(self, group, own, size):
        final = self.place.final
        here = self._rows(own, size)
        for k in range(1, group.count):
            to = lax.rem(group.here + k, group.count)
            self._copy(final.at[here], final.at[here], group.device(to))

    def _steps(self):
        place, group = self.place, self.group
        yield self._swap()
        self._wait()
        self._add_swap()
        yield from self._both()
        final = place.final
        here = self._rows(self.base, self.half)
        self._copy(final.at[here], final.at[here], place.partner)
        yield
        self._wait()
        yield

    def _both(self):
        place, group = self.place, self.group
        line = place.line
        self._scatter(group, self.base, self.part)
        yield
        self._wait()
        self._total(group, self.own, self.part, place.sums)
        self._scatter(line, self.own, self.shard)
        yield
        self._wait()
        self._total(line, self.last, self.shard, place.final)
        self._gather(line, self.last, self.shard)
        yield
        self._wait()
        self._gather(group, self.own, self.part)
        yield
        self._wait()

    def advance(self):
        if self.stage == 0:
            self.steps = self._steps()
        self.stage += 1
        next(self.steps)

    def done(self):
        return self.stage == 7


class SmallExchange(Exchange):

    def __init__(self, place, start, rows, landing, first_sem):
        super().__init__(place, start, rows, landing, first_sem)
        self.group = place.cores_group
        self.base = start
        self._finish(rows)

    def _steps(self):
        yield from self._both()
        yield

    def done(self):
        return self.stage == 5


def layout_of(shapes):
    starts = {}
    at = 0
    for name in LARGE:
        starts[name] = at
        at += shapes[name][0]
    small = at
    unit = 256
    total = -(-(at + SMALL_COUNT) // unit) * unit
    begins = SimpleNamespace(**starts)
    ready = (
        begins.dec_conv1,
        begins.up_weight,
        begins.enc_conv2,
        begins.enc_conv1,
        small,
    )
    edges = [0] + [edge // unit * unit for edge in ready] + [total]
    runs = [(a, b - a) for a, b in zip(edges[:-1], edges[1:])]
    return starts, small, total, runs


def item_kernel(sizes, scratch_names, *refs):
    line, strip, width, shapes, big_layout = sizes
    begins, small_at, total_rows, runs = big_layout
    starts = SimpleNamespace(**begins)
    inputs = Given(*refs[: len(ARGUMENTS)])
    refs = refs[len(ARGUMENTS) :]
    output_names = OUTPUTS
    outputs = SimpleNamespace(**dict(zip(output_names, refs)))
    scratch = SimpleNamespace(**dict(zip(scratch_names, refs[len(output_names) :])))

    def w_of(name):
        return getattr(scratch, name)

    height = strip * line
    cells = height * width
    c = inputs.lift_weight.shape[1]
    strip_cells = strip * width
    history = inputs.frames.shape[1]

    core = lax.axis_index("section")
    plane = lax.axis_index("batch")
    row = lax.axis_index("rows")
    def device_at(to):
        return (core, plane, to)

    place = SimpleNamespace(
        core=core,
        partner=(1 - core, plane, row),
        line=SimpleNamespace(count=line, here=row, device=device_at),
        plane_group=SimpleNamespace(
            count=4, here=plane, device=lambda to: (core, to, row)
        ),
        cores_group=SimpleNamespace(
            count=8,
            here=core * 4 + plane,
            device=lambda to: (to // 4, lax.rem(to, 4), row),
        ),
        sums=scratch.sums,
        final=scratch.final,
        landing=scratch.landing,
        send=scratch.send,
        recv=scratch.recv,
    )
    local_sem = scratch.local

    weight_copies = {}
    for k, name in enumerate(LARGE):
        copy = pltpu.make_async_copy(getattr(inputs, name), w_of(name), local_sem.at[k])
        weight_copies[name] = copy
        copy.start()
    frames_in, mask_in, cot = scratch.frames_in, scratch.mask_in, scratch.cot
    here_rows = pl.ds(pl.multiple_of(row * strip_cells, strip_cells), strip_cells)
    own = (
        pltpu.make_async_copy(inputs.frames.at[row], frames_in.at[row], local_sem.at[7]),
        pltpu.make_async_copy(inputs.cell_mask.at[row], mask_in.at[row], local_sem.at[8]),
        pltpu.make_async_copy(
            inputs.cotangent.at[row], cot.at[here_rows], local_sem.at[9]
        ),
    )
    for copy in own:
        copy.start()

    barrier = pltpu.get_barrier_semaphore()
    peers = [device_at(lax.rem(row + k, line)) for k in range(1, line)]
    cores_group = place.cores_group
    for k in range(1, 8):
        peers.append(cores_group.device(lax.rem(cores_group.here + k, 8)))
    for device in peers:
        pl.semaphore_signal(barrier, inc=1, device_id=device, device_id_type=MESH)
    pl.semaphore_wait(barrier, len(peers))

    next_sem = 0

    def send(source, target, device):
        nonlocal next_sem
        copy = pltpu.make_async_remote_copy(
            src_ref=source,
            dst_ref=target,
            send_sem=scratch.send.at[next_sem],
            recv_sem=scratch.recv.at[next_sem],
            device_id=device,
            device_id_type=MESH,
        )
        next_sem += 1
        copy.start()
        return copy

    frame_copies, cot_copies, output_copies = [], [], []
    for k in range(1, line):
        to = lax.rem(row + k, line)
        device = device_at(to)
        frame_copies.append(send(inputs.frames.at[to], frames_in.at[row], device))
        frame_copies.append(send(inputs.cell_mask.at[to], mask_in.at[row], device))
    for k in range(1, line):
        to = lax.rem(row + k, line)
        cot_copies.append(
            send(inputs.cotangent.at[to], cot.at[here_rows], device_at(to))
        )

    copied = SimpleNamespace(**weight_copies)
    def stack_conv(source, half, depth, forward, backward):
        for a in range(3):
            for b in range(3):
                at = (3 * a + b) * depth + half * c
                high, low = split(source[at : at + c, :])
                for block in (HIGH_AT[b], LOW_AT[b]):
                    rows = slice((6 * a + block) * c, (6 * a + block + 1) * c)
                    forward[rows, 0:c] = high
                    forward[rows, c : 2 * c] = low
                for block in (HIGH_AT[2 - b], LOW_AT[2 - b]):
                    tap = 6 * (2 - a) + block
                    columns = slice(tap * c, (tap + 1) * c)
                    backward[0:c, columns] = high
                    backward[c : 2 * c, columns] = low

    copied.enc_conv1.wait()
    stack_conv(scratch.enc_conv1, 0, c, scratch.fe1, scratch.be1)
    copied.enc_conv2.wait()
    stack_conv(scratch.enc_conv2, 0, c, scratch.fe2, scratch.be2)
    copied.reducer_weight.wait()
    for k in range(4):
        high, low = split(scratch.reducer_weight[k * c : (k + 1) * c, :])
        for block in (k, k + 4):
            scratch.f_down[block * c : (block + 1) * c, 0:c] = high
            scratch.f_down[block * c : (block + 1) * c, c : 2 * c] = low
        for block in (0, 1):
            columns = slice(block * c, (block + 1) * c)
            scratch.b_down[k, 0:c, columns] = high
            scratch.b_down[k, c : 2 * c, columns] = low
    copied.up_weight.wait()
    for k in range(4):
        high, low = split(scratch.up_weight[k * c : (k + 1) * c, :])
        for block in (0, 1):
            rows = slice(block * c, (block + 1) * c)
            scratch.f_up[k, rows, 0:c] = high
            scratch.f_up[k, rows, c : 2 * c] = low
        for block in (k, k + 4):
            columns = slice(block * c, (block + 1) * c)
            scratch.b_up[0:c, columns] = high
            scratch.b_up[c : 2 * c, columns] = low
    copied.dec_conv1.wait()
    stack_conv(scratch.dec_conv1, 0, 2 * c, scratch.fd1a, scratch.bd1a)
    stack_conv(scratch.dec_conv1, 1, 2 * c, scratch.fd1b, scratch.bd1b)
    copied.dec_conv2.wait()
    stack_conv(scratch.dec_conv2, 0, c, scratch.fd2, scratch.bd2)
    copied.skip_weight.wait()
    for half in range(2):
        high, low = split(scratch.skip_weight[half * c : (half + 1) * c, :])
        for block in (half, half + 2):
            scratch.f_skip[block * c : (block + 1) * c, 0:c] = high
            scratch.f_skip[block * c : (block + 1) * c, c : 2 * c] = low
        for block in (0, 1):
            columns = slice(block * c, (block + 1) * c)
            scratch.b_skip[half, 0:c, columns] = high
            scratch.b_skip[half, c : 2 * c, columns] = low

    for buffer in (scratch.xe1, scratch.xe2, scratch.xd1a, scratch.xd1b, scratch.xd2, scratch.xg):
        edge = jnp.zeros((width, 6 * c), BF16)
        buffer[0:width, :] = edge
        buffer[cells + width : cells + 2 * width, :] = edge

    lift = scratch.lift
    lift[...] = jnp.zeros(lift.shape, F32)
    lift[0:history, :] = inputs.lift_weight[...]
    lift[history : history + 1, :] = inputs.lift_bias[...]

    block = 2 * width
    column = lax.rem(lax.broadcasted_iota(jnp.int32, (block, c), 0), width)
    at_first, at_last = column == 0, column == width - 1
    zeros8 = jnp.zeros((8, c), F32)
    ones16 = group_ones(c, c // GROUPS)
    ones32 = group_ones(c, 2 * c // GROUPS)
    count16 = float(cells * (c // GROUPS))
    count32 = float(cells * (2 * c // GROUPS))

    def grid_rows(step, carry=0):
        return lax.fori_loop(0, cells // block, step, carry, unroll=2)

    def row_at(h):
        return pl.ds(pl.multiple_of(h * block, block), block)

    def chunk_at(i):
        return pl.ds(pl.multiple_of(i * CHUNK, CHUNK), CHUNK)

    def put_row(target, h, value):
        rows = pl.ds(pl.multiple_of(h * block + width, width), block)
        left = jnp.where(at_first, 0.0, pltpu.roll(value, 1, 0))
        right = jnp.where(at_last, 0.0, pltpu.roll(value, block - 1, 0))
        for b, piece in enumerate((left, value, right)):
            high, low = split(piece)
            target[rows, HIGH_AT[b] * c : (HIGH_AT[b] + 1) * c] = high
            target[rows, LOW_AT[b] * c : (LOW_AT[b] + 1) * c] = low

    def put_turned(target, columns, value, first=0, second=1):
        high, low = split(value.T)
        target[first * c : (first + 1) * c, columns] = high
        target[second * c : (second + 1) * c, columns] = low

    def conv_chunk(pairs, i, dims=NN):
        total = None
        for data, weight in pairs:
            taps = []
            for a in range(3):
                rows = pl.ds(pl.multiple_of(i * CHUNK + a * width, width), CHUNK)
                taps.append(data[rows, :])
            part = dot(jnp.concatenate(taps, axis=1), weight[...], dims)
            total = part if total is None else total + part
        return total

    def norm_of(first, second, ones, count):
        one, two = group_sums(first, second, ones)
        mean = one / count
        return mean, lax.rsqrt(two / count - mean * mean + EPS)

    def activate(source, target, turned, slope, scale, shift):
        def step(h, carry):
            value = source[row_at(h), :] * scale + shift
            below = 0.5 + 0.5 * lax.erf(value * 0.7071067811865476)
            slope[row_at(h), :] = below + value * (
                0.3989422804014327 * jnp.exp(-0.5 * value * value)
            )
            value = value * below
            put_row(target, h, value)
            put_turned(turned, row_at(h), value)
            return carry

        grid_rows(step)

    def conv_norm(pairs, target):
        def step(i, carry):
            value = fold(conv_chunk(pairs, i))
            target[chunk_at(i), :] = value
            return carry[0] + tile_sums(value), carry[1] + tile_sums(value * value)

        return lax.fori_loop(0, cells // CHUNK, step, (zeros8, zeros8))

    def sums_of(source):
        def step(h, carry):
            value = source[row_at(h), :]
            return carry[0] + tile_sums(value), carry[1] + tile_sums(value * value)

        return grid_rows(step, (zeros8, zeros8))

    step_here = jnp.full((1, c), inputs.step_index[row], jnp.int32)

    def condition(table):
        total = jnp.zeros((1, 2 * c), F32)
        chosen = jnp.concatenate([step_here, step_here], axis=1)
        for s in range(table.shape[0]):
            total = total + jnp.where(chosen == s, table[s : s + 1, :], 0.0)
        return total[:, :c], total[:, c:]

    for copy in own[:2]:
        copy.wait()
    for copy in frame_copies:
        copy.wait_recv()
    fields = scratch.fields
    fields[...] = jnp.zeros(fields.shape, F32)
    frame_of = lax.broadcasted_iota(jnp.int32, (history, width), 0) // FIELDS
    keep = (frame_of >= HIST - inputs.counts[row]).astype(F32)
    masks = []
    for source in range(line):
        for k in range(strip):
            columns = slice((source * strip + k) * width, (source * strip + k + 1) * width)
            mask = mask_in[source, k : k + 1, :].astype(F32)
            masks.append(mask)
            fields[0:history, columns] = frames_in[source, :, k, :] * keep * mask
            fields[history : history + 1, columns] = mask
    lifted = scratch.lifted
    lifted[...] = dot(fields[...], lift[...], TN, HIGH)

    enc_scale, enc_shift = condition(inputs.enc_step_table)
    dec_scale, dec_shift = condition(inputs.dec_step_table)

    mean_e1, inv_e1 = norm_of(*sums_of(lifted), ones16, count16)
    gain_e1, bias_e1 = inputs.enc_norm1_gain[...], inputs.enc_norm1_bias[...]
    a_e1 = inv_e1 * gain_e1
    activate(lifted, scratch.xe1, scratch.te1, scratch.slope_e1, a_e1, bias_e1 - mean_e1 * a_e1)
    middle_e = scratch.middle_e
    mean_e2, inv_e2 = norm_of(
        *conv_norm([(scratch.xe1, scratch.fe1)], middle_e), ones16, count16
    )
    gain_e2, bias_e2 = inputs.enc_norm2_gain[...], inputs.enc_norm2_bias[...]
    a_e2 = inv_e2 * gain_e2
    activate(
        middle_e,
        scratch.xe2,
        scratch.te2,
        scratch.slope_e2,
        a_e2 * (1.0 + enc_scale),
        (bias_e2 - mean_e2 * a_e2) * (1.0 + enc_scale) + enc_shift,
    )
    encoded = scratch.encoded
    conv2_bias = inputs.enc_conv2_bias[...]
    joined = scratch.joined

    def encode(i, carry):
        value = fold(conv_chunk([(scratch.xe2, scratch.fe2)], i))
        value = value + conv2_bias + lifted[chunk_at(i), :]
        encoded[chunk_at(i), :] = value
        high, low = split(value)
        joined[chunk_at(i), c : 2 * c] = high
        joined[chunk_at(i), 3 * c : 4 * c] = low
        put_turned(scratch.turned, chunk_at(i), value, 1, 3)
        return carry[0] + tile_sums(value), carry[1] + tile_sums(value * value)

    sums_enc = lax.fori_loop(0, cells // CHUNK, encode, (zeros8, zeros8))

    half_cells, quarter = cells // 2, cells // 4

    def pick(source):
        pieces = []
        for b in range(2):
            value = source[pl.ds(b, half_cells, stride=2), :]
            value = value.reshape(height // 2, 2, width // 2, c)
            pieces.append([value[:, a].reshape(quarter, c) for a in range(2)])
        return [pieces[b][a] for a in range(2) for b in range(2)]

    def place_cells(target, pieces):
        for b in range(2):
            both = [pieces[2 * a + b].reshape(height // 2, 1, width // 2, c) for a in range(2)]
            value = jnp.concatenate(both, axis=1).reshape(half_cells, c)
            target[pl.ds(b, half_cells, stride=2), :] = value

    x_down = scratch.x_down
    for k, piece in enumerate(pick(encoded)):
        high, low = split(piece)
        x_down[:, k * c : (k + 1) * c] = high
        x_down[:, (k + 4) * c : (k + 5) * c] = low
    lowered = fold(dot(x_down[...], scratch.f_down[...])) + inputs.reducer_bias[...]
    x_up = scratch.x_up
    high, low = split(lowered)
    x_up[:, 0:c] = high
    x_up[:, c : 2 * c] = low
    raised = scratch.raised
    up_bias = inputs.up_bias[...]
    place_cells(
        raised, [fold(dot(x_up[...], scratch.f_up[k])) + up_bias for k in range(4)]
    )

    def raise_row(h, carry):
        value = raised[row_at(h), :]
        high, low = split(value)
        joined[row_at(h), 0:c] = high
        joined[row_at(h), 2 * c : 3 * c] = low
        put_turned(scratch.turned, row_at(h), value, 0, 2)
        return carry[0] + tile_sums(value), carry[1] + tile_sums(value * value)

    sums_raised = grid_rows(raise_row, (zeros8, zeros8))

    halves = []
    for half, (source, sums) in enumerate(((raised, sums_raised), (encoded, sums_enc))):
        mean, inv = norm_of(*sums, ones32, count32)
        gain = inputs.dec_norm1_gain[half : half + 1, :]
        bias = inputs.dec_norm1_bias[half : half + 1, :]
        scale = inv * gain
        activate(
            source,
            (scratch.xd1a, scratch.xd1b)[half],
            (scratch.td1a, scratch.td1b)[half],
            (scratch.slope_d1a, scratch.slope_d1b)[half],
            scale,
            bias - mean * scale,
        )
        halves.append((source, mean, inv, gain))
    middle_d = scratch.middle_d
    pairs = [(scratch.xd1a, scratch.fd1a), (scratch.xd1b, scratch.fd1b)]
    mean_d2, inv_d2 = norm_of(*conv_norm(pairs, middle_d), ones16, count16)
    gain_d2, bias_d2 = inputs.dec_norm2_gain[...], inputs.dec_norm2_bias[...]
    a_d2 = inv_d2 * gain_d2
    activate(
        middle_d,
        scratch.xd2,
        scratch.td2,
        scratch.slope_d2,
        a_d2 * (1.0 + dec_scale),
        (bias_d2 - mean_d2 * a_d2) * (1.0 + dec_scale) + dec_shift,
    )
    result = scratch.result
    last_bias = inputs.dec_conv2_bias[...] + inputs.skip_bias[...]

    def decode(i, carry):
        value = conv_chunk([(scratch.xd2, scratch.fd2)], i)
        value = value + dot(joined[chunk_at(i), :], scratch.f_skip[...])
        result[chunk_at(i), :] = fold(value) + last_bias
        return carry

    lax.fori_loop(0, cells // CHUNK, decode, 0)
    own_output = pltpu.make_async_copy(
        result.at[here_rows], outputs.output.at[row], local_sem.at[10]
    )
    own_output.start()
    for k in range(1, line):
        to = lax.rem(row + k, line)
        there = pl.ds(pl.multiple_of(to * strip_cells, strip_cells), strip_cells)
        output_copies.append(
            send(result.at[there], outputs.output.at[row], device_at(to))
        )

    exchanges = []
    waiting_runs = list(runs)
    landing_at = 0
    sem_at = 4 * (line - 1) + 2 * (line - 1)
    sums, final = scratch.sums, scratch.final

    def begin():
        nonlocal landing_at, sem_at
        start, rows = waiting_runs.pop(0)
        kind = Exchange if waiting_runs else SmallExchange
        exchange = kind(place, start, rows, landing_at, sem_at)
        landing_at += rows - rows // (8 * line)
        sem_at += exchange.count()
        exchanges.append(exchange)
        exchange.advance()

    final_copies = []

    def publish():
        for k, exchange in enumerate(exchanges):
            if k == len(final_copies) and exchange.done():
                rows = pl.ds(exchange.start, exchange.rows)
                copy = pltpu.make_async_copy(
                    final.at[rows], outputs.gradients.at[rows], local_sem.at[11 + k]
                )
                copy.start()
                final_copies.append(copy)

    def tick():
        for exchange in exchanges:
            if not exchange.done():
                exchange.advance()
        publish()

    def small_row(k, value):
        sums[small_at + k : small_at + k + 1, :] = value

    def spread_grad(source):
        def step(h, carry):
            value = source[row_at(h), :]
            put_row(scratch.xg, h, value)
            return carry + tile_sums(value)

        return grid_rows(step, zeros8)

    def weight_grad(turned, at, depth):
        lhs = turned[...]
        for a in range(3):
            rows = pl.ds((2 - a) * width, cells)
            part = fold_rows(dot(lhs, scratch.xg[rows, :]))
            for b in range(3):
                high, low = HIGH_AT[2 - b] * c, LOW_AT[2 - b] * c
                to = at + (3 * a + b) * depth
                sums[to : to + c, :] = part[:, high : high + c] + part[:, low : low + c]

    def back_conv(weight, slope, target, source, mean, inv):
        def step(i, carry):
            value = fold(conv_chunk([(scratch.xg, weight)], i, NT)) * slope[chunk_at(i), :]
            target[chunk_at(i), :] = value
            normed = (source[chunk_at(i), :] - mean) * inv
            return carry[0] + tile_sums(value), carry[1] + tile_sums(value * normed)

        return lax.fori_loop(0, cells // CHUNK, step, (zeros8, zeros8))

    def norm_grad(sums_in, scale, ones, count):
        one, two = group_sums(sums_in[0] * scale, sums_in[1] * scale, ones)
        return one / count, two / count

    own[2].wait()
    for copy in cot_copies:
        copy.wait_recv()
    total_cot = column_sum(spread_grad(cot))
    weight_grad(scratch.td2, starts.dec_conv2, c)
    part = fold(dot(scratch.turned[...], scratch.xg[width : cells + width, 2 * c : 4 * c]))
    sums[starts.skip_weight : starts.skip_weight + 2 * c, :] = fold_rows(part)
    small_row(23, total_cot)
    begin()

    grad = scratch.grad
    sums_d2 = back_conv(scratch.bd2, scratch.slope_d2, grad, middle_d, mean_d2, inv_d2)
    side_grads = (scratch.grad_a, scratch.grad_b)
    for half in range(2):

        def skip_back(i, carry, half=half):
            rows = pl.ds(pl.multiple_of(i * CHUNK + width, width), CHUNK)
            value = dot(scratch.xg[rows, 2 * c : 4 * c], scratch.b_skip[half], NT)
            side_grads[half][chunk_at(i), :] = fold(value)
            return carry

        lax.fori_loop(0, cells // CHUNK, skip_back, 0)
    tick()

    def table_rows(k, sums_in, gain, bias, one_plus):
        plain, times = column_sum(sums_in[0]), column_sum(sums_in[1])
        for s in range(inputs.enc_step_table.shape[0]):
            small_row(k + 2 * s, jnp.where(step_here == s, gain * times + bias * plain, 0.0))
            small_row(k + 2 * s + 1, jnp.where(step_here == s, plain, 0.0))
        return one_plus * times, one_plus * plain

    def middle_grad(source, mean, inv, scale, sums_in):
        zero, slope = norm_grad(sums_in, scale, ones16, count16)

        def step(h, carry):
            normed = (source[row_at(h), :] - mean) * inv
            value = inv * (grad[row_at(h), :] * scale - zero - normed * slope)
            put_row(scratch.xg, h, value)
            return carry

        grid_rows(step)

    gain_row, bias_row = table_rows(40, sums_d2, gain_d2, bias_d2, 1.0 + dec_scale)
    small_row(28, gain_row)
    small_row(29, bias_row)
    middle_grad(middle_d, mean_d2, inv_d2, gain_d2 * (1.0 + dec_scale), sums_d2)
    weight_grad(scratch.td1a, starts.dec_conv1, 2 * c)
    tick()
    weight_grad(scratch.td1b, starts.dec_conv1 + c, 2 * c)
    begin()

    for half, (source, mean, inv, gain) in enumerate(halves):
        sums_in = back_conv(
            (scratch.bd1a, scratch.bd1b)[half],
            (scratch.slope_d1a, scratch.slope_d1b)[half],
            grad,
            source,
            mean,
            inv,
        )
        small_row(24 + half, column_sum(sums_in[1]))
        small_row(26 + half, column_sum(sums_in[0]))
        zero, slope = norm_grad(sums_in, gain, ones32, count32)
        target = side_grads[half]

        def input_grad(h, carry):
            normed = (source[row_at(h), :] - mean) * inv
            value = inv * (grad[row_at(h), :] * gain - zero - normed * slope)
            value = target[row_at(h), :] + value
            target[row_at(h), :] = value
            return carry + tile_sums(value)

        total = grid_rows(input_grad, zeros8)
        if half == 0:
            small_row(22, column_sum(total))
        tick()

    grad_raised, grad_encoded = side_grads
    x_grad_up = scratch.x_grad_up
    for k, piece in enumerate(pick(grad_raised)):
        high, low = split(piece)
        x_grad_up[:, k * c : (k + 1) * c] = high
        x_grad_up[:, (k + 4) * c : (k + 5) * c] = low
    grad_lowered = fold(dot(x_grad_up[...], scratch.b_up[...], NT))
    small_row(21, jnp.sum(grad_lowered, axis=0, keepdims=True))
    x_grad_low = scratch.x_grad_low
    high, low = split(grad_lowered)
    x_grad_low[:, 0:c] = high
    x_grad_low[:, c : 2 * c] = low
    part = fold(fold_rows(dot(x_up[...], x_grad_up[...], TN)))
    for k in range(4):
        at = starts.up_weight + k * c
        sums[at : at + c, :] = part[:, k * c : (k + 1) * c]
    part = fold_rows(fold(dot(x_down[...], x_grad_low[...], TN)))
    sums[starts.reducer_weight : starts.reducer_weight + 4 * c, :] = part
    begin()
    place_cells(
        grad, [fold(dot(x_grad_low[...], scratch.b_down[k], NT)) for k in range(4)]
    )

    def join_row(h, carry):
        value = grad_encoded[row_at(h), :] + grad[row_at(h), :]
        grad_encoded[row_at(h), :] = value
        put_row(scratch.xg, h, value)
        return carry + tile_sums(value)

    small_row(20, column_sum(grid_rows(join_row, zeros8)))
    tick()
    weight_grad(scratch.te2, starts.enc_conv2, c)
    begin()
    sums_e2 = back_conv(scratch.be2, scratch.slope_e2, grad, middle_e, mean_e2, inv_e2)
    gain_row, bias_row = table_rows(32, sums_e2, gain_e2, bias_e2, 1.0 + enc_scale)
    small_row(18, gain_row)
    small_row(19, bias_row)
    middle_grad(middle_e, mean_e2, inv_e2, gain_e2 * (1.0 + enc_scale), sums_e2)
    tick()
    weight_grad(scratch.te1, starts.enc_conv1, c)
    begin()
    tick()
    sums_e1 = back_conv(scratch.be1, scratch.slope_e1, grad, lifted, mean_e1, inv_e1)
    small_row(16, column_sum(sums_e1[1]))
    small_row(17, column_sum(sums_e1[0]))
    zero, slope = norm_grad(sums_e1, gain_e1, ones16, count16)

    def lifted_grad(h, carry):
        normed = (lifted[row_at(h), :] - mean_e1) * inv_e1
        value = inv_e1 * (grad[row_at(h), :] * gain_e1 - zero - normed * slope)
        grad[row_at(h), :] = grad_encoded[row_at(h), :] + value
        return carry

    grid_rows(lifted_grad)
    tick()

    sums[small_at : small_at + 16, :] = dot(fields[...], grad[...], NN, HIGH)
    for k in (30, 31):
        small_row(k, jnp.zeros((1, c), F32))
    rest = small_at + 48
    sums[rest:total_rows, :] = jnp.zeros((total_rows - rest, c), F32)
    begin()
    back = dot(lift[...], grad[...], NT, HIGH)
    frames_out = scratch.frames_out
    for source in range(line):
        for k in range(strip):
            h = source * strip + k
            value = back[0:history, h * width : (h + 1) * width]
            frames_out[source, :, k, :] = value * keep * masks[h]
    own_frames = pltpu.make_async_copy(
        frames_out.at[row], outputs.frames_grad.at[row], local_sem.at[18]
    )
    own_frames.start()
    for k in range(1, line):
        to = lax.rem(row + k, line)
        output_copies.append(
            send(frames_out.at[to], outputs.frames_grad.at[row], device_at(to))
        )

    while not all(exchange.done() for exchange in exchanges):
        tick()

    for copy in output_copies:
        copy.wait_recv()
    own_output.wait()
    own_frames.wait()
    for copy in final_copies:
        copy.wait()
    for copy in frame_copies + cot_copies + output_copies:
        copy.wait_send()
    for exchange in exchanges:
        for copy in exchange.copies:
            copy.wait_send()


def write_kernel(layout, *refs):
    shapes, starts, small_at = layout
    output, frames_grad, gradients = refs[:3]
    outputs = refs[3:-4]
    output_here, frames_here, gradients_here, sem = refs[-4:]
    c = gradients.shape[1]
    moves = [(frames_grad, frames_here, outputs[1])]
    for k, name in enumerate(LARGE):
        rows = pl.ds(starts[name], shapes[name][0])
        moves.append((gradients.at[rows], gradients_here.at[rows], outputs[2 + k]))
    moves.append((output, output_here, outputs[0]))
    small = pl.ds(small_at, SMALL_COUNT)
    first = pltpu.make_async_copy(gradients.at[small], gradients_here.at[small], sem.at[0])
    first.start()
    arriving, leaving = [], []
    for k, (source, here, _) in enumerate(moves):
        arriving.append(pltpu.make_async_copy(source, here, sem.at[1 + 2 * k]))
        arriving[-1].start()
    first.wait()
    for target, (k, rows) in zip(outputs[2 + len(LARGE) :], SMALL_ROWS.values()):
        at = small_at + k
        if rows == 8:
            for s in range(target.shape[0]):
                target[s : s + 1, 0:c] = gradients_here[at + 2 * s : at + 2 * s + 1, :]
                target[s : s + 1, c : 2 * c] = gradients_here[at + 2 * s + 1 : at + 2 * s + 2, :]
        else:
            target[...] = gradients_here[at : at + rows, :]
    for k, (_, here, target) in enumerate(moves):
        arriving[k].wait()
        leaving.append(pltpu.make_async_copy(here, target, sem.at[2 + 2 * k]))
        leaving[-1].start()
    for copy in leaving:
        copy.wait()


def whole_items(shape, *arguments):
    line = shape["rows"]
    whole = Given(*arguments)
    given = whole._asdict()
    frames, cotangent = whole.frames, whole.cotangent
    items, history, strip, width = frames.shape
    c = cotangent.shape[-1]
    cells = strip * line * width
    flat = {}
    for name, value in given.items():
        if value is cotangent:
            value = value.reshape(items, strip * width, c)
        elif name in LARGE:
            value = value.reshape(-1, c)
        elif value.ndim == 1 and name not in IN_SMEM:
            value = value.reshape(-1, c)
        flat[name] = value
    shapes = {name: flat[name].shape for name in LARGE}
    big_layout = layout_of(shapes)
    starts, small_at, total_rows, runs = big_layout
    copies = 7 * (line - 1) + len(runs) * (8 + 2 * (line - 1)) + 6
    landing = sum(rows - rows // (8 * line) for _, rows in runs)
    shifted = pltpu.VMEM((cells + 2 * width, 6 * c), BF16)
    forward = pltpu.VMEM((18 * c, 2 * c), BF16)
    backward = pltpu.VMEM((2 * c, 18 * c), BF16)
    field = pltpu.VMEM((cells, c), F32)
    flipped_field = pltpu.VMEM((2 * c, cells), BF16)
    quarter = cells // 4
    scratch = dict(
        send=pltpu.SemaphoreType.DMA((copies,)),
        recv=pltpu.SemaphoreType.DMA((copies,)),
        local=pltpu.SemaphoreType.DMA((19,)),
        sums=pltpu.VMEM((total_rows, c), F32),
        final=pltpu.VMEM((total_rows, c), F32),
        landing=pltpu.VMEM((landing, c), F32),
        frames_in=pltpu.VMEM((line, history, strip, width), F32),
        mask_in=pltpu.VMEM((line, strip, width), jnp.int32),
        frames_out=pltpu.VMEM((line, history, strip, width), F32),
        fields=pltpu.VMEM((16, cells), F32),
        lift=pltpu.VMEM((16, c), F32),
        joined=pltpu.VMEM((cells, 4 * c), BF16),
        x_down=pltpu.VMEM((quarter, 8 * c), BF16),
        x_grad_up=pltpu.VMEM((quarter, 8 * c), BF16),
        x_up=pltpu.VMEM((quarter, 2 * c), BF16),
        x_grad_low=pltpu.VMEM((quarter, 2 * c), BF16),
        f_down=pltpu.VMEM((8 * c, 2 * c), BF16),
        b_down=pltpu.VMEM((4, 2 * c, 2 * c), BF16),
        f_up=pltpu.VMEM((4, 2 * c, 2 * c), BF16),
        b_up=pltpu.VMEM((2 * c, 8 * c), BF16),
        f_skip=pltpu.VMEM((4 * c, 2 * c), BF16),
        b_skip=pltpu.VMEM((2, 2 * c, 2 * c), BF16),
        xe1=shifted,
        xe2=shifted,
        xd1a=shifted,
        xd1b=shifted,
        xd2=shifted,
        xg=shifted,
        te1=flipped_field,
        te2=flipped_field,
        td1a=flipped_field,
        td1b=flipped_field,
        td2=flipped_field,
        turned=pltpu.VMEM((4 * c, cells), BF16),
        fe1=forward,
        fe2=forward,
        fd1a=forward,
        fd1b=forward,
        fd2=forward,
        be1=backward,
        be2=backward,
        bd1a=backward,
        bd1b=backward,
        bd2=backward,
        slope_e1=field,
        slope_e2=field,
        slope_d1a=field,
        slope_d1b=field,
        slope_d2=field,
        lifted=field,
        middle_e=field,
        encoded=field,
        raised=field,
        middle_d=field,
        result=field,
        cot=field,
        grad=field,
        grad_a=field,
        grad_b=field,
    )
    scratch.update({name: pltpu.VMEM(shapes[name], F32) for name in LARGE})

    in_hbm = pl.BlockSpec(memory_space=pl.ANY)
    in_vmem = pl.BlockSpec(memory_space=pltpu.VMEM)
    in_smem = pl.BlockSpec(memory_space=pltpu.SMEM)
    in_specs = [
        in_hbm if name in IN_HBM else in_smem if name in IN_SMEM else in_vmem
        for name in ARGUMENTS
    ]
    out_shape = [
        jax.ShapeDtypeStruct((items, strip * width, c), F32),
        jax.ShapeDtypeStruct(frames.shape, F32),
        jax.ShapeDtypeStruct((total_rows, c), F32),
    ]
    out_specs = [in_hbm] * 3
    results = pl.pallas_call(
        functools.partial(
            item_kernel,
            (line, strip, width, shapes, big_layout),
            tuple(scratch),
        ),
        out_shape=out_shape,
        in_specs=in_specs,
        out_specs=out_specs,
        scratch_shapes=list(scratch.values()),
        compiler_params=pltpu.CompilerParams(
            collective_id=0, has_side_effects=True, vmem_limit_bytes=62 * 1024 * 1024
        ),
    )(*[flat[name] for name in ARGUMENTS])
    names = LARGE + tuple(SMALL_ROWS)
    written = pl.pallas_call(
        functools.partial(write_kernel, (shapes, starts, small_at)),
        out_shape=out_shape[:2] + [jax.ShapeDtypeStruct(flat[name].shape, F32) for name in names],
        in_specs=[pl.BlockSpec(memory_space=pltpu.HBM)] * 3,
        out_specs=[in_hbm] * (2 + len(LARGE)) + [in_vmem] * len(SMALL_ROWS),
        scratch_shapes=[
            pltpu.VMEM((items, strip * width, c), F32),
            pltpu.VMEM(frames.shape, F32),
            pltpu.VMEM((total_rows, c), F32),
            pltpu.SemaphoreType.DMA((1 + 2 * (2 + len(LARGE)),)),
        ],
        compiler_params=pltpu.CompilerParams(vmem_limit_bytes=60 * 1024 * 1024),
    )(*results)
    grads = dict(zip(names, written[2:]))
    ordered = [name for name in ARGUMENTS if name in grads]
    return (written[0].reshape(cotangent.shape), written[1]) + tuple(
        grads[name].reshape(given[name].shape) for name in ordered
    )


def body(shape, *arguments):
    items, _, strip, width = arguments[0].shape
    line = shape["rows"]
    whole = (
        shape["section"] == 2
        and shape["batch"] == 4
        and items == line
        and arguments[-1].shape[-1] == 128
        and (strip * line * width) % CHUNK == 0
    )
    return whole_items(shape, *arguments) if whole else strips_body(*arguments)


def solution(mesh):
    in_specs = (
        P(("section", "batch"), None, "rows", None),
        P(("section", "batch")),
        P(("section", "batch"), "rows", None),
        P(("section", "batch")),
        P(),
        P(),
        P(),
        P(),
        P(),
        P(),
        P(),
        P(),
        P(),
        P(),
        P(),
        P(),
        P(),
        P(),
        P(),
        P(),
        P(),
        P(),
        P(),
        P(),
        P(),
        P(),
        P(),
        P(),
        P(("section", "batch"), "rows", None, None),
    )
    out_specs = (
        P(("section", "batch"), "rows", None, None),
        P(("section", "batch"), None, "rows", None),
        P(),
        P(),
        P(),
        P(),
        P(),
        P(),
        P(),
        P(),
        P(),
        P(),
        P(),
        P(),
        P(),
        P(),
        P(),
        P(),
        P(),
        P(),
        P(),
        P(),
        P(),
        P(),
        P(),
        P(),
    )
    return jax.shard_map(functools.partial(body, mesh.shape), mesh=mesh, in_specs=in_specs, out_specs=out_specs, check_vma=False)
```

```python
import functools
from types import SimpleNamespace
from typing import Any, NamedTuple

import jax
import jax.numpy as jnp
from jax import lax
from jax.experimental import pallas as pl
from jax.experimental.pallas import tpu as pltpu
from jax.sharding import PartitionSpec as P

GROUPS = 8
FIELDS = 3
HIST = 4


EPS = 1e-05
HIGH = lax.Precision.HIGHEST


def extended(cells, sides, width):
    for axis, dim in sides:
        count = lax.axis_size(axis)
        ends = count - 1
        head = lax.slice_in_dim(cells, 0, width, axis=dim)
        tail = lax.slice_in_dim(cells, cells.shape[dim] - width, cells.shape[dim], axis=dim)
        cells = jnp.concatenate(
            [
                lax.ppermute(tail, axis, [(i, (i + 1) % count) for i in range(ends)]),
                cells,
                lax.ppermute(head, axis, [((i + 1) % count, i) for i in range(ends)]),
            ],
            axis=dim,
        )
    return cells


def from_behind(value, axis, steps):
    count = lax.axis_size(axis)
    pairs = [(source, (source + steps) % count) for source in range(count)]
    return lax.ppermute(value, axis, pairs)


def group_view(value_arrays):
    extent = value_arrays.shape
    return value_arrays.reshape(extent[:-1] + (GROUPS, extent[-1] // GROUPS))


def global_sums(value_arrays):
    grouped = group_view(value_arrays)
    flat = grouped.reshape(-1, GROUPS, grouped.shape[-1])
    first_sum = jnp.sum(flat, axis=(0, 2))
    second_sum = jnp.sum(flat * flat, axis=(0, 2))
    return lax.psum((first_sum, second_sum), "rows")


def apply_norm(value_arrays, sum_one, sum_two, norm_gain, norm_bias, total):
    grouped = group_view(value_arrays)
    group_mean = sum_one / total
    variance = sum_two / total - group_mean * group_mean
    inverse = lax.rsqrt(variance + EPS)
    normed = (grouped - group_mean[:, None]) * inverse[:, None]
    return normed.reshape(value_arrays.shape) * norm_gain + norm_bias


def norm_back(value_arrays, grad_one, grad_two):
    grouped = group_view(value_arrays)
    extra = grad_one[:, None] + 2.0 * grouped * grad_two[:, None]
    return extra.reshape(value_arrays.shape)


def reduce_grads(grad_one, grad_two):
    return lax.psum((grad_one, grad_two), "rows")


def conv_rows(padded, kernel):
    widened = jnp.pad(padded, ((0, 0), (1, 1), (0, 0)))
    return lax.conv_general_dilated(
        widened[None],
        kernel,
        (1, 1),
        "VALID",
        dimension_numbers=("NHWC", "HWIO", "NHWC"),
        precision=HIGH,
    )[0]


def flipped(kernel):
    return jnp.transpose(kernel[::-1, ::-1], (0, 1, 3, 2))


def pad_grads(value_arrays):
    return extended(value_arrays, (("rows", 0),), 1)


def totals_of(inputs, conv1):
    strip = inputs.shape[0]
    cells = strip * lax.axis_size("rows") * inputs.shape[1]
    return (cells * (inputs.shape[2] // GROUPS), cells * (conv1.shape[3] // GROUPS))


def block_forward(inputs, weights, scale_part, shift_part):
    norm1_gain, norm1_bias, conv1, norm2_gain, norm2_bias, conv2, conv2_bias = weights
    total_in, total_mid = totals_of(inputs, conv1)
    sums_in = global_sums(inputs)

    def pad_rows(value_arrays):
        return extended(value_arrays, (("rows", 0),), 1)

    act_one = pad_rows(
        jax.nn.gelu(
            apply_norm(inputs, sums_in[0], sums_in[1], norm1_gain, norm1_bias, total_in),
            approximate=False,
        )
    )
    middle = conv_rows(act_one, conv1)
    sums_mid = global_sums(middle)
    shaped = (
        apply_norm(middle, sums_mid[0], sums_mid[1], norm2_gain, norm2_bias, total_mid)
        * (1.0 + scale_part)
        + shift_part
    )
    act_two = pad_rows(jax.nn.gelu(shaped, approximate=False))
    branch = conv_rows(act_two, conv2) + conv2_bias
    return (branch, (sums_in[0], sums_in[1], act_one, middle, sums_mid[0], sums_mid[1], act_two))


def block_backward(inputs, weights, scale_part, shift_part, kept, grad_out):
    norm1_gain, norm1_bias, conv1, norm2_gain, norm2_bias, conv2, conv2_bias = weights
    in_one, in_two, act_one, middle, mid_one, mid_two, act_two = kept
    total_in, total_mid = totals_of(inputs, conv1)
    grad_conv2 = jax.vjp(lambda kernel: conv_rows(act_two, kernel), conv2)[1](grad_out)[0]
    grad_bias2 = jnp.sum(grad_out, axis=(0, 1))
    grad_act_two = conv_rows(pad_grads(grad_out), flipped(conv2))

    def second_piece(middle_in, sum_one, sum_two, gain_in, incoming_bias, scale_in, shift_in):
        shaped = (
            apply_norm(middle_in, sum_one, sum_two, gain_in, incoming_bias, total_mid)
            * (1.0 + scale_in)
            + shift_in
        )
        return jax.nn.gelu(shaped, approximate=False)

    second_pull = jax.vjp(
        second_piece, middle, mid_one, mid_two, norm2_gain, norm2_bias, scale_part, shift_part
    )[1](grad_act_two)
    summed_one, summed_two = reduce_grads(second_pull[1], second_pull[2])
    grad_middle = second_pull[0] + norm_back(middle, summed_one, summed_two)
    grad_conv1 = jax.vjp(lambda kernel: conv_rows(act_one, kernel), conv1)[1](grad_middle)[0]
    grad_act_one = conv_rows(pad_grads(grad_middle), flipped(conv1))

    def first_piece(inputs_in, sum_one, sum_two, gain_in, incoming_bias):
        return jax.nn.gelu(
            apply_norm(inputs_in, sum_one, sum_two, gain_in, incoming_bias, total_in),
            approximate=False,
        )

    first_pull = jax.vjp(first_piece, inputs, in_one, in_two, norm1_gain, norm1_bias)[1](
        grad_act_one
    )
    first_one, first_two = reduce_grads(first_pull[1], first_pull[2])
    grad_inputs = first_pull[0] + norm_back(inputs, first_one, first_two)
    grads = (
        first_pull[3],
        first_pull[4],
        grad_conv1,
        second_pull[3],
        second_pull[4],
        grad_conv2,
        grad_bias2,
    )
    return (grad_inputs, grads, second_pull[5], second_pull[6])


def conditioning(step_item, table):
    one_hot = (jnp.arange(table.shape[0], dtype=jnp.int32) == step_item).astype(jnp.float32)
    condition = jnp.dot(one_hot, table, precision=HIGH)
    half_width = table.shape[1] // 2
    return (condition[:half_width], condition[half_width:], one_hot)


def project_in(frames_item, mask_item, count_item, incoming_weight, incoming_bias):
    history = jnp.arange(HIST, dtype=jnp.int32) >= HIST - count_item
    keep = jnp.repeat(history, FIELDS).astype(jnp.float32)
    lifted = (
        jnp.einsum(
            "fhw,fc->hwc", frames_item * keep[:, None, None], incoming_weight, precision=HIGH
        )
        + incoming_bias
    )
    return lifted * mask_item[:, :, None].astype(jnp.float32)


def coarsen_field(value_arrays, incoming_weight, incoming_bias):
    rows_here, width_here, depth_here = value_arrays.shape
    blocks = value_arrays.reshape(rows_here // 2, 2, width_here // 2, 2, depth_here)
    return jnp.einsum("iajbk,abkc->ijc", blocks, incoming_weight, precision=HIGH) + incoming_bias


def upsample(value_arrays, incoming_weight, incoming_bias):
    result = jnp.einsum("ijk,abkc->iajbc", value_arrays, incoming_weight, precision=HIGH)
    extent = result.shape
    return result.reshape(extent[0] * 2, extent[2] * 2, extent[4]) + incoming_bias


def flatten_all(pieces):
    return jnp.concatenate([piece.reshape(-1) for piece in pieces])


def unflatten_all(flat, templates):
    pieces = []
    offset_at = 0
    for template in templates:
        count_here = template.size
        pieces.append(flat[offset_at : offset_at + count_here].reshape(template.shape))
        offset_at += count_here
    return tuple(pieces)


def strips_body(
    frames,
    counts,
    cell_mask,
    step_index,
    lift_weight,
    lift_bias,
    enc_norm1_gain,
    enc_norm1_bias,
    enc_conv1,
    enc_step_table,
    enc_norm2_gain,
    enc_norm2_bias,
    enc_conv2,
    enc_conv2_bias,
    reducer_weight,
    reducer_bias,
    up_weight,
    up_bias,
    dec_norm1_gain,
    dec_norm1_bias,
    dec_conv1,
    dec_step_table,
    dec_norm2_gain,
    dec_norm2_bias,
    dec_conv2,
    dec_conv2_bias,
    skip_weight,
    skip_bias,
    cotangent,
):
    enc_weights = (
        enc_norm1_gain,
        enc_norm1_bias,
        enc_conv1,
        enc_norm2_gain,
        enc_norm2_bias,
        enc_conv2,
        enc_conv2_bias,
    )
    dec_weights = (
        dec_norm1_gain,
        dec_norm1_bias,
        dec_conv1,
        dec_norm2_gain,
        dec_norm2_bias,
        dec_conv2,
        dec_conv2_bias,
    )
    params = (
        lift_weight,
        lift_bias,
        enc_norm1_gain,
        enc_norm1_bias,
        enc_conv1,
        enc_step_table,
        enc_norm2_gain,
        enc_norm2_bias,
        enc_conv2,
        enc_conv2_bias,
        reducer_weight,
        reducer_bias,
        up_weight,
        up_bias,
        dec_norm1_gain,
        dec_norm1_bias,
        dec_conv1,
        dec_step_table,
        dec_norm2_gain,
        dec_norm2_bias,
        dec_conv2,
        dec_conv2_bias,
        skip_weight,
        skip_bias,
    )

    def forward_micro(carry, sliced):
        frames_item, mask_item, count_item, step_item = sliced
        lifted = project_in(frames_item, mask_item, count_item, lift_weight, lift_bias)
        enc_scale, enc_shift, unused_hot = conditioning(step_item, enc_step_table)
        enc_branch, enc_kept = block_forward(lifted, enc_weights, enc_scale, enc_shift)
        encoder_result = lifted + enc_branch
        coarse_field = coarsen_field(encoder_result, reducer_weight, reducer_bias)
        foreign = from_behind(coarse_field, "section", 1)
        raised_foreign = upsample(foreign, up_weight, up_bias)
        raised = from_behind(raised_foreign, "section", 1)
        joined = jnp.concatenate([raised, encoder_result], axis=-1)
        dec_scale, dec_shift, unused_again = conditioning(step_item, dec_step_table)
        dec_branch, dec_kept = block_forward(joined, dec_weights, dec_scale, dec_shift)
        output_item = jnp.dot(joined, skip_weight, precision=HIGH) + skip_bias + dec_branch
        return (carry, (output_item, (lifted, enc_kept, encoder_result, foreign, joined, dec_kept)))

    unused, (output, kept_all) = lax.scan(
        forward_micro, jnp.zeros((), jnp.float32), (frames, cell_mask, counts, step_index)
    )

    def backward_micro(totals, sliced):
        frames_item, mask_item, count_item, step_item, grad_out, kept = sliced
        lifted, enc_kept, encoder_result, foreign, joined, dec_kept = kept
        dec_scale, dec_shift, one_hot = conditioning(step_item, dec_step_table)
        grad_joined, dec_grads, dec_gscale, dec_gshift = block_backward(
            joined, dec_weights, dec_scale, dec_shift, dec_kept, grad_out
        )
        grad_skip_weight = jnp.einsum("hwk,hwc->kc", joined, grad_out, precision=HIGH)
        grad_skip_bias = jnp.sum(grad_out, axis=(0, 1))
        grad_joined = grad_joined + jnp.dot(grad_out, skip_weight.T, precision=HIGH)
        half_width = joined.shape[-1] // 2
        grad_raised = grad_joined[..., :half_width]
        grad_encoded = grad_joined[..., half_width:]
        grad_foreign_up = from_behind(grad_raised, "section", 1)
        up_pull = jax.vjp(upsample, foreign, up_weight, up_bias)[1](grad_foreign_up)
        coarse_gradient = from_behind(up_pull[0], "section", 1)
        reducer_pullback = jax.vjp(coarsen_field, encoder_result, reducer_weight, reducer_bias)[1](
            coarse_gradient
        )
        grad_encoded = grad_encoded + reducer_pullback[0]
        enc_scale, enc_shift, enc_hot = conditioning(step_item, enc_step_table)
        grad_lifted, enc_grads, enc_gscale, enc_gshift = block_backward(
            lifted, enc_weights, enc_scale, enc_shift, enc_kept, grad_encoded
        )
        grad_lifted = grad_lifted + grad_encoded
        proj_pull = jax.vjp(
            lambda frames_in, incoming_weight, incoming_bias: project_in(
                frames_in, mask_item, count_item, incoming_weight, incoming_bias
            ),
            frames_item,
            lift_weight,
            lift_bias,
        )[1](grad_lifted)
        enc_table_grad = enc_hot[:, None] * jnp.concatenate([enc_gscale, enc_gshift])[None, :]
        dec_table_grad = one_hot[:, None] * jnp.concatenate([dec_gscale, dec_gshift])[None, :]
        micro_list = (
            proj_pull[1],
            proj_pull[2],
            enc_grads[0],
            enc_grads[1],
            enc_grads[2],
            enc_table_grad,
            enc_grads[3],
            enc_grads[4],
            enc_grads[5],
            enc_grads[6],
            reducer_pullback[1],
            reducer_pullback[2],
            up_pull[1],
            up_pull[2],
            dec_grads[0],
            dec_grads[1],
            dec_grads[2],
            dec_table_grad,
            dec_grads[3],
            dec_grads[4],
            dec_grads[5],
            dec_grads[6],
            grad_skip_weight,
            grad_skip_bias,
        )
        micro_flat = flatten_all(micro_list)
        return (totals + micro_flat, proj_pull[0])

    total_size = sum((piece.size for piece in params))
    start_totals = jnp.zeros((total_size,), jnp.float32)
    flat_totals, frames_grad = lax.scan(
        backward_micro,
        start_totals,
        (frames, cell_mask, counts, step_index, cotangent, kept_all),
        reverse=True,
    )
    flat_totals = lax.psum(flat_totals, ("section", "batch", "rows"))
    grads = unflatten_all(flat_totals, params)
    return (output, frames_grad) + grads


F32 = jnp.float32
BF16 = jnp.bfloat16
MESH = pl.DeviceIdType.MESH
NN = ((1,), (0,))
NT = ((1,), (1,))
TN = ((0,), (0,))
HIGH_AT = (0, 2, 1)
LOW_AT = (4, 3, 5)
CHUNK = 512
class Given(NamedTuple):
    frames: Any
    counts: Any
    cell_mask: Any
    step_index: Any
    lift_weight: Any
    lift_bias: Any
    enc_norm1_gain: Any
    enc_norm1_bias: Any
    enc_conv1: Any
    enc_step_table: Any
    enc_norm2_gain: Any
    enc_norm2_bias: Any
    enc_conv2: Any
    enc_conv2_bias: Any
    reducer_weight: Any
    reducer_bias: Any
    up_weight: Any
    up_bias: Any
    dec_norm1_gain: Any
    dec_norm1_bias: Any
    dec_conv1: Any
    dec_step_table: Any
    dec_norm2_gain: Any
    dec_norm2_bias: Any
    dec_conv2: Any
    dec_conv2_bias: Any
    skip_weight: Any
    skip_bias: Any
    cotangent: Any


ARGUMENTS = Given._fields
LARGE = tuple(
    dict(
        dec_conv1=0,
        up_weight=0,
        reducer_weight=0,
        dec_conv2=0,
        skip_weight=0,
        enc_conv1=0,
        enc_conv2=0,
    )
)
IN_HBM = tuple(dict(frames=0, cell_mask=0, cotangent=0)) + LARGE
IN_SMEM = tuple(dict(counts=0, step_index=0))
LATE = 128
SMALL_ROWS = dict(
    enc_conv2_bias=(0, 1),
    reducer_bias=(1, 1),
    up_bias=(2, 1),
    dec_conv2_bias=(3, 1),
    skip_bias=(3, 1),
    dec_norm1_gain=(4, 2),
    dec_norm1_bias=(6, 2),
    dec_norm2_gain=(8, 1),
    dec_norm2_bias=(9, 1),
    dec_step_table=(16, 8),
    lift_weight=(LATE, 12),
    lift_bias=(LATE + 12, 1),
    enc_norm1_gain=(LATE + 16, 1),
    enc_norm1_bias=(LATE + 17, 1),
    enc_norm2_gain=(LATE + 18, 1),
    enc_norm2_bias=(LATE + 19, 1),
    enc_step_table=(LATE + 24, 8),
)
LATE_COUNT = 32
SMALL_COUNT = LATE + LATE_COUNT
DUE = ((), (), (), (), (0,), (), (), (), (1,), (2, 0), (3,), (), (), (), (), (1,), (), (), (2,), (0, 4), (), (1, 3), (5,), (2,), (), (0,), (4, 1), (3,), (6, 2))
REST = (5, 0, 4, 1, 3, 7, 6, 1, 5, 4, 2, 0, 3, 6, 2, 7, 5, 3, 4, 6, 0, 4, 5, 0, 6, 5, 6)
OUTPUTS = tuple(dict(output=0, frames_grad=0, gradients=0))


def split(value):
    high = value.astype(BF16)
    return high, (value - high.astype(F32)).astype(BF16)


def dot(left, right, dims=NN, precision=None):
    return lax.dot_general(
        left, right, (dims, ((), ())), precision=precision, preferred_element_type=F32
    )


def fold(value):
    half = value.shape[1] // 2
    return value[:, :half] + value[:, half:]


def fold_rows(value):
    half = value.shape[0] // 2
    return value[:half] + value[half:]


def tile_sums(value):
    return jnp.sum(value.reshape(-1, 8, value.shape[-1]), axis=0)


def column_sum(tiles):
    return jnp.sum(tiles, axis=0, keepdims=True)


def group_ones(channels, size):
    rows = lax.broadcasted_iota(jnp.int32, (channels, channels), 0) // size
    columns = lax.broadcasted_iota(jnp.int32, (channels, channels), 1) // size
    return (rows == columns).astype(F32)


def group_sums(first, second, ones):
    both = dot(jnp.concatenate([first, second], axis=0), ones, precision=HIGH)
    return column_sum(both[:8]), column_sum(both[8:])


class Exchange:

    def __init__(self, place, start, rows, landing, first_sem):
        self.place, self.start, self.rows, self.landing = place, start, rows, landing
        self.sem = first_sem
        self.stage = 0
        self.copies = []
        self.waiting = []
        self.group = place.plane_group
        self.half = rows // 2
        self.base = start + place.core * self.half
        self._finish(self.half)

    def _finish(self, size):
        self.part = size // self.group.count
        self.own = self.base + self.group.here * self.part
        self.shard = self.part // self.place.line.count
        self.last = self.own + self.place.line.here * self.shard

    def count(self):
        return 2 + 2 * (self.group.count - 1) + 2 * (self.place.line.count - 1)

    def _copy(self, source, target, device):
        place = self.place
        copy = pltpu.make_async_remote_copy(
            src_ref=source,
            dst_ref=target,
            send_sem=place.send.at[self.sem],
            recv_sem=place.recv.at[self.sem],
            device_id=device,
            device_id_type=MESH,
        )
        self.sem += 1
        copy.start()
        self.copies.append(copy)
        self.waiting.append(copy)

    def _wait(self):
        for copy in self.waiting:
            copy.wait_recv()
        self.waiting = []

    def _rows(self, at, size):
        return pl.ds(pl.multiple_of(at, 8), size)

    def _swap(self):
        place = self.place
        other = self._rows(self.start + (1 - place.core) * self.half, self.half)
        self.land = self.landing
        self.landing += self.half
        self._copy(
            place.sums.at[other], place.landing.at[pl.ds(self.land, self.half)], place.partner
        )

    def _add_swap(self):
        place = self.place
        block = 64 if self.half % 64 == 0 else 32

        def step(i, carry):
            here = self._rows(self.base + i * block, block)
            there = self._rows(self.land + i * block, block)
            place.sums[here] = place.sums[here] + place.landing[there]
            return carry

        lax.fori_loop(0, self.half // block, step, 0)

    def _scatter(self, group, base, size):
        place = self.place
        self.land = self.landing
        for k in range(1, group.count):
            to = lax.rem(group.here + k, group.count)
            self._copy(
                place.sums.at[self._rows(base + to * size, size)],
                place.landing.at[pl.ds(self.landing, size)],
                group.device(to),
            )
            self.landing += size

    def _total(self, group, own, size, target):
        place = self.place
        block = 8 if size % 32 else 32

        def step(i, carry):
            here = self._rows(own + i * block, block)
            total = place.sums[here]
            for k in range(group.count - 1):
                there = self._rows(self.land + k * size + i * block, block)
                total = total + place.landing[there]
            target[here] = total
            return carry

        lax.fori_loop(0, size // block, step, 0)

    def _gather(self, group, own, size):
        final = self.place.final
        here = self._rows(own, size)
        for k in range(1, group.count):
            to = lax.rem(group.here + k, group.count)
            self._copy(final.at[here], final.at[here], group.device(to))

    def _steps(self):
        place, group = self.place, self.group
        yield self._swap()
        self._wait()
        self._add_swap()
        yield from self._both()
        final = place.final
        here = self._rows(self.base, self.half)
        self._copy(final.at[here], final.at[here], place.partner)
        yield
        self._wait()
        yield

    def _both(self):
        place, group = self.place, self.group
        line = place.line
        self._scatter(group, self.base, self.part)
        yield
        self._wait()
        self._total(group, self.own, self.part, place.sums)
        self._scatter(line, self.own, self.shard)
        yield
        self._wait()
        self._total(line, self.last, self.shard, place.final)
        self._gather(line, self.last, self.shard)
        yield
        self._wait()
        self._gather(group, self.own, self.part)
        yield
        self._wait()

    def advance(self):
        if self.stage == 0:
            self.steps = self._steps()
        self.stage += 1
        next(self.steps)

    def done(self):
        return self.stage == 7


class HalvingExchange(Exchange):

    def count(self):
        return 6 + 2 * (self.place.line.count - 1)

    def _halve(self, level):
        place = self.place
        self.half = self.rows >> (level + 1)
        bit, device = place.halves[level]
        other = self._rows(self.base + (1 - bit) * self.half, self.half)
        self.base = self.base + bit * self.half
        self.land = self.landing
        self.landing += self.half
        self._copy(
            place.sums.at[other], place.landing.at[pl.ds(self.land, self.half)], device
        )

    def _steps(self):
        place, line, final = self.place, self.place.line, self.place.final
        self.base = self.start
        bases = []
        for level in range(3):
            self._halve(level)
            bases.append(self.base)
            yield
            self._wait()
            self._add_swap()
        shard = self.half // line.count
        last = self.base + line.here * shard
        self._scatter(line, self.base, shard)
        yield
        self._wait()
        self._total(line, last, shard, final)
        self._gather(line, last, shard)
        yield
        for level in (2, 1, 0):
            self._wait()
            here = self._rows(bases[level], self.rows >> (level + 1))
            self._copy(final.at[here], final.at[here], place.halves[level][1])
            yield
        self._wait()
        yield

    def done(self):
        return self.stage == 9


class SmallExchange(Exchange):

    def count(self):
        return self.place.cores_group.count + self.place.line.count - 2

    def _share(self, group, source):
        place = self.place
        self.land = self.landing
        self.landing += group.count * self.rows
        own = self._rows(self.land + group.here * self.rows, self.rows)
        place.landing[own] = source[...]
        for k in range(1, group.count):
            to = lax.rem(group.here + k, group.count)
            self._copy(source, place.landing.at[own], group.device(to))

    def _sum(self, group):
        total = None
        for k in range(group.count):
            part = self.place.landing[pl.ds(self.land + k * self.rows, self.rows)]
            total = part if total is None else total + part
        return total

    def _steps(self):
        place = self.place
        here = pl.ds(self.start, self.rows)
        self._share(place.line, place.sums.at[here])
        yield
        self._wait()
        place.small[...] = self._sum(place.line)
        self._share(place.cores_group, place.small)
        yield
        self._wait()
        place.final[here] = self._sum(place.cores_group)
        yield

    def done(self):
        return self.stage == 3


def layout_of(shapes):
    starts = {}
    at = 0
    for name in LARGE:
        starts[name] = at
        at += shapes[name][0]
    small = at
    begins = SimpleNamespace(**starts)
    late = small + LATE
    part = (begins.up_weight - begins.dec_conv1) // 3
    skip = begins.skip_weight + 128
    conv1, up = begins.dec_conv1, begins.up_weight
    edges = (
        (begins.dec_conv2, skip),
        (conv1, conv1 + part),
        (conv1 + part, conv1 + 2 * part),
        (conv1 + 2 * part, up),
        (up, begins.dec_conv2),
        (begins.enc_conv2, late),
        (skip, begins.enc_conv2),
        (late, late + LATE_COUNT),
    )
    runs = [(first, last - first) for first, last in edges]
    return starts, small, late + LATE_COUNT, runs


def item_kernel(sizes, scratch_names, *refs):
    line, strip, width, shapes, big_layout = sizes
    begins, small_at, total_rows, runs = big_layout
    starts = SimpleNamespace(**begins)
    inputs = Given(*refs[: len(ARGUMENTS)])
    refs = refs[len(ARGUMENTS) :]
    output_names = OUTPUTS
    outputs = SimpleNamespace(**dict(zip(output_names, refs)))
    scratch = SimpleNamespace(**dict(zip(scratch_names, refs[len(output_names) :])))

    def w_of(name):
        return getattr(scratch, name)

    height = strip * line
    cells = height * width
    c = inputs.lift_weight.shape[1]
    strip_cells = strip * width
    history = inputs.frames.shape[1]

    core = lax.axis_index("section")
    plane = lax.axis_index("batch")
    row = lax.axis_index("rows")
    y, x = plane // 2, lax.rem(plane, 2)
    along_x = plane + 1 - 2 * x
    along_y = plane + 2 - 4 * y

    def device_at(to):
        return (core, plane, to)

    place = SimpleNamespace(
        core=core,
        partner=(1 - core, plane, row),
        line=SimpleNamespace(count=line, here=row, device=device_at),
        plane_group=SimpleNamespace(
            count=4, here=plane, device=lambda to: (core, to, row)
        ),
        cores_group=SimpleNamespace(
            count=8,
            here=core * 4 + plane,
            device=lambda to: (to // 4, lax.rem(to, 4), row),
        ),
        halves=(
            (core, (1 - core, plane, row)),
            (x * (1 - core) + y * core, (core, along_x * (1 - core) + along_y * core, row)),
            (y * (1 - core) + x * core, (core, along_y * (1 - core) + along_x * core, row)),
        ),
        small=scratch.small,
        sums=scratch.sums,
        final=scratch.final,
        landing=scratch.landing,
        send=scratch.send,
        recv=scratch.recv,
    )
    local_sem = scratch.local

    weight_copies = {}
    for k, name in enumerate(LARGE):
        copy = pltpu.make_async_copy(getattr(inputs, name), w_of(name), local_sem.at[k])
        weight_copies[name] = copy
        copy.start()
    frames_in, mask_in, cot = scratch.frames_in, scratch.mask_in, scratch.cot
    here_rows = pl.ds(pl.multiple_of(row * strip_cells, strip_cells), strip_cells)
    own = (
        pltpu.make_async_copy(inputs.frames.at[row], frames_in.at[row], local_sem.at[7]),
        pltpu.make_async_copy(inputs.cell_mask.at[row], mask_in.at[row], local_sem.at[8]),
        pltpu.make_async_copy(
            inputs.cotangent.at[row], cot.at[here_rows], local_sem.at[9]
        ),
    )
    for copy in own:
        copy.start()

    barrier = pltpu.get_barrier_semaphore()
    peers = [device_at(lax.rem(row + k, line)) for k in range(1, line)]
    cores_group = place.cores_group
    for k in range(1, 8):
        peers.append(cores_group.device(lax.rem(cores_group.here + k, 8)))
    for device in peers:
        pl.semaphore_signal(barrier, inc=1, device_id=device, device_id_type=MESH)
    pl.semaphore_wait(barrier, len(peers))

    next_sem = 0

    def send(source, target, device):
        nonlocal next_sem
        copy = pltpu.make_async_remote_copy(
            src_ref=source,
            dst_ref=target,
            send_sem=scratch.send.at[next_sem],
            recv_sem=scratch.recv.at[next_sem],
            device_id=device,
            device_id_type=MESH,
        )
        next_sem += 1
        copy.start()
        return copy

    frame_copies, cot_copies, output_copies = [], [], []
    for k in range(1, line):
        to = lax.rem(row + k, line)
        device = device_at(to)
        frame_copies.append(send(inputs.frames.at[to], frames_in.at[row], device))
        frame_copies.append(send(inputs.cell_mask.at[to], mask_in.at[row], device))
    for k in range(1, line):
        to = lax.rem(row + k, line)
        cot_copies.append(
            send(inputs.cotangent.at[to], cot.at[here_rows], device_at(to))
        )

    copied = SimpleNamespace(**weight_copies)
    def stack_conv(source, half, depth, forward, backward):
        for a in range(3):
            for b in range(3):
                at = (3 * a + b) * depth + half * c
                high, low = split(source[at : at + c, :])
                for block in (HIGH_AT[b], LOW_AT[b]):
                    rows = slice((6 * a + block) * c, (6 * a + block + 1) * c)
                    forward[rows, 0:c] = high
                    forward[rows, c : 2 * c] = low
                for block in (HIGH_AT[2 - b], LOW_AT[2 - b]):
                    tap = 6 * (2 - a) + block
                    columns = slice(tap * c, (tap + 1) * c)
                    backward[0:c, columns] = high
                    backward[c : 2 * c, columns] = low

    copied.enc_conv1.wait()
    stack_conv(scratch.enc_conv1, 0, c, scratch.fe1, scratch.be1)
    copied.enc_conv2.wait()
    stack_conv(scratch.enc_conv2, 0, c, scratch.fe2, scratch.be2)
    copied.reducer_weight.wait()
    for k in range(4):
        high, low = split(scratch.reducer_weight[k * c : (k + 1) * c, :])
        for block in (k, k + 4):
            scratch.f_down[block * c : (block + 1) * c, 0:c] = high
            scratch.f_down[block * c : (block + 1) * c, c : 2 * c] = low
        for block in (0, 1):
            columns = slice(block * c, (block + 1) * c)
            scratch.b_down[k, 0:c, columns] = high
            scratch.b_down[k, c : 2 * c, columns] = low
    copied.up_weight.wait()
    for k in range(4):
        high, low = split(scratch.up_weight[k * c : (k + 1) * c, :])
        for block in (0, 1):
            rows = slice(block * c, (block + 1) * c)
            scratch.f_up[k, rows, 0:c] = high
            scratch.f_up[k, rows, c : 2 * c] = low
        for block in (k, k + 4):
            columns = slice(block * c, (block + 1) * c)
            scratch.b_up[0:c, columns] = high
            scratch.b_up[c : 2 * c, columns] = low
    copied.dec_conv1.wait()
    stack_conv(scratch.dec_conv1, 0, 2 * c, scratch.fd1a, scratch.bd1a)
    stack_conv(scratch.dec_conv1, 1, 2 * c, scratch.fd1b, scratch.bd1b)
    copied.dec_conv2.wait()
    stack_conv(scratch.dec_conv2, 0, c, scratch.fd2, scratch.bd2)
    copied.skip_weight.wait()
    for half in range(2):
        high, low = split(scratch.skip_weight[half * c : (half + 1) * c, :])
        for block in (half, half + 2):
            scratch.f_skip[block * c : (block + 1) * c, 0:c] = high
            scratch.f_skip[block * c : (block + 1) * c, c : 2 * c] = low
        for block in (0, 1):
            columns = slice(block * c, (block + 1) * c)
            scratch.b_skip[half, 0:c, columns] = high
            scratch.b_skip[half, c : 2 * c, columns] = low

    for buffer in (scratch.xe1, scratch.xe2, scratch.xd1a, scratch.xd1b, scratch.xd2, scratch.xg):
        edge = jnp.zeros((width, 6 * c), BF16)
        buffer[0:width, :] = edge
        buffer[cells + width : cells + 2 * width, :] = edge

    lift = scratch.lift
    lift[...] = jnp.zeros(lift.shape, F32)
    lift[0:history, :] = inputs.lift_weight[...]
    lift[history : history + 1, :] = inputs.lift_bias[...]

    block = 2 * width
    column = lax.rem(lax.broadcasted_iota(jnp.int32, (block, c), 0), width)
    at_first, at_last = column == 0, column == width - 1
    zeros8 = jnp.zeros((8, c), F32)
    ones16 = group_ones(c, c // GROUPS)
    ones32 = group_ones(c, 2 * c // GROUPS)
    count16 = float(cells * (c // GROUPS))
    count32 = float(cells * (2 * c // GROUPS))

    def grid_rows(step, carry=0):
        return lax.fori_loop(0, cells // block, step, carry, unroll=2)

    def row_at(h):
        return pl.ds(pl.multiple_of(h * block, block), block)

    def chunk_at(i):
        return pl.ds(pl.multiple_of(i * CHUNK, CHUNK), CHUNK)

    def put_row(target, h, value):
        rows = pl.ds(pl.multiple_of(h * block + width, width), block)
        left = jnp.where(at_first, 0.0, pltpu.roll(value, 1, 0))
        right = jnp.where(at_last, 0.0, pltpu.roll(value, block - 1, 0))
        for b, piece in enumerate((left, value, right)):
            high, low = split(piece)
            target[rows, HIGH_AT[b] * c : (HIGH_AT[b] + 1) * c] = high
            target[rows, LOW_AT[b] * c : (LOW_AT[b] + 1) * c] = low

    def put_turned(target, columns, value, first=0, second=1):
        high, low = split(value.T)
        target[first * c : (first + 1) * c, columns] = high
        target[second * c : (second + 1) * c, columns] = low

    def conv_chunk(pairs, i, dims=NN):
        total = None
        for data, weight in pairs:
            taps = []
            for a in range(3):
                rows = pl.ds(pl.multiple_of(i * CHUNK + a * width, width), CHUNK)
                taps.append(data[rows, :])
            part = dot(jnp.concatenate(taps, axis=1), weight[...], dims)
            total = part if total is None else total + part
        return total

    def norm_of(first, second, ones, count):
        one, two = group_sums(first, second, ones)
        mean = one / count
        return mean, lax.rsqrt(two / count - mean * mean + EPS)

    def activate(source, target, turned, slope, scale, shift):
        def step(h, carry):
            value = source[row_at(h), :] * scale + shift
            below = 0.5 + 0.5 * lax.erf(value * 0.7071067811865476)
            slope[row_at(h), :] = below + value * (
                0.3989422804014327 * jnp.exp(-0.5 * value * value)
            )
            value = value * below
            put_row(target, h, value)
            put_turned(turned, row_at(h), value)
            return carry

        grid_rows(step)

    def conv_norm(pairs, target):
        def step(i, carry):
            value = fold(conv_chunk(pairs, i))
            target[chunk_at(i), :] = value
            return carry[0] + tile_sums(value), carry[1] + tile_sums(value * value)

        return lax.fori_loop(0, cells // CHUNK, step, (zeros8, zeros8))

    def sums_of(source):
        def step(h, carry):
            value = source[row_at(h), :]
            return carry[0] + tile_sums(value), carry[1] + tile_sums(value * value)

        return grid_rows(step, (zeros8, zeros8))

    step_here = jnp.full((1, c), inputs.step_index[row], jnp.int32)

    def condition(table):
        total = jnp.zeros((1, 2 * c), F32)
        chosen = jnp.concatenate([step_here, step_here], axis=1)
        for s in range(table.shape[0]):
            total = total + jnp.where(chosen == s, table[s : s + 1, :], 0.0)
        return total[:, :c], total[:, c:]

    for copy in own[:2]:
        copy.wait()
    for copy in frame_copies:
        copy.wait_recv()
    fields = scratch.fields
    fields[...] = jnp.zeros(fields.shape, F32)
    frame_of = lax.broadcasted_iota(jnp.int32, (history, width), 0) // FIELDS
    keep = (frame_of >= HIST - inputs.counts[row]).astype(F32)
    masks = []
    for source in range(line):
        for k in range(strip):
            columns = slice((source * strip + k) * width, (source * strip + k + 1) * width)
            mask = mask_in[source, k : k + 1, :].astype(F32)
            masks.append(mask)
            fields[0:history, columns] = frames_in[source, :, k, :] * keep * mask
            fields[history : history + 1, columns] = mask
    lifted = scratch.lifted
    lifted[...] = dot(fields[...], lift[...], TN, HIGH)

    enc_scale, enc_shift = condition(inputs.enc_step_table)
    dec_scale, dec_shift = condition(inputs.dec_step_table)

    mean_e1, inv_e1 = norm_of(*sums_of(lifted), ones16, count16)
    gain_e1, bias_e1 = inputs.enc_norm1_gain[...], inputs.enc_norm1_bias[...]
    a_e1 = inv_e1 * gain_e1
    activate(lifted, scratch.xe1, scratch.te1, scratch.slope_e1, a_e1, bias_e1 - mean_e1 * a_e1)
    middle_e = scratch.middle_e
    mean_e2, inv_e2 = norm_of(
        *conv_norm([(scratch.xe1, scratch.fe1)], middle_e), ones16, count16
    )
    gain_e2, bias_e2 = inputs.enc_norm2_gain[...], inputs.enc_norm2_bias[...]
    a_e2 = inv_e2 * gain_e2
    activate(
        middle_e,
        scratch.xe2,
        scratch.te2,
        scratch.slope_e2,
        a_e2 * (1.0 + enc_scale),
        (bias_e2 - mean_e2 * a_e2) * (1.0 + enc_scale) + enc_shift,
    )
    encoded = scratch.encoded
    conv2_bias = inputs.enc_conv2_bias[...]
    joined = scratch.joined

    def encode(i, carry):
        value = fold(conv_chunk([(scratch.xe2, scratch.fe2)], i))
        value = value + conv2_bias + lifted[chunk_at(i), :]
        encoded[chunk_at(i), :] = value
        high, low = split(value)
        joined[chunk_at(i), c : 2 * c] = high
        joined[chunk_at(i), 3 * c : 4 * c] = low
        put_turned(scratch.turned, chunk_at(i), value, 1, 3)
        return carry[0] + tile_sums(value), carry[1] + tile_sums(value * value)

    sums_enc = lax.fori_loop(0, cells // CHUNK, encode, (zeros8, zeros8))

    half_cells, quarter = cells // 2, cells // 4

    def pick(source):
        pieces = []
        for b in range(2):
            value = source[pl.ds(b, half_cells, stride=2), :]
            value = value.reshape(height // 2, 2, width // 2, c)
            pieces.append([value[:, a].reshape(quarter, c) for a in range(2)])
        return [pieces[b][a] for a in range(2) for b in range(2)]

    def place_cells(target, pieces):
        for b in range(2):
            both = [pieces[2 * a + b].reshape(height // 2, 1, width // 2, c) for a in range(2)]
            value = jnp.concatenate(both, axis=1).reshape(half_cells, c)
            target[pl.ds(b, half_cells, stride=2), :] = value

    x_down = scratch.x_down
    for k, piece in enumerate(pick(encoded)):
        high, low = split(piece)
        x_down[:, k * c : (k + 1) * c] = high
        x_down[:, (k + 4) * c : (k + 5) * c] = low
    lowered = fold(dot(x_down[...], scratch.f_down[...])) + inputs.reducer_bias[...]
    x_up = scratch.x_up
    high, low = split(lowered)
    x_up[:, 0:c] = high
    x_up[:, c : 2 * c] = low
    raised = scratch.raised
    up_bias = inputs.up_bias[...]
    place_cells(
        raised, [fold(dot(x_up[...], scratch.f_up[k])) + up_bias for k in range(4)]
    )

    def raise_row(h, carry):
        value = raised[row_at(h), :]
        high, low = split(value)
        joined[row_at(h), 0:c] = high
        joined[row_at(h), 2 * c : 3 * c] = low
        put_turned(scratch.turned, row_at(h), value, 0, 2)
        return carry[0] + tile_sums(value), carry[1] + tile_sums(value * value)

    sums_raised = grid_rows(raise_row, (zeros8, zeros8))

    halves = []
    for half, (source, sums) in enumerate(((raised, sums_raised), (encoded, sums_enc))):
        mean, inv = norm_of(*sums, ones32, count32)
        gain = inputs.dec_norm1_gain[half : half + 1, :]
        bias = inputs.dec_norm1_bias[half : half + 1, :]
        scale = inv * gain
        activate(
            source,
            (scratch.xd1a, scratch.xd1b)[half],
            (scratch.td1a, scratch.td1b)[half],
            (scratch.slope_d1a, scratch.slope_d1b)[half],
            scale,
            bias - mean * scale,
        )
        halves.append((source, mean, inv, gain))
    middle_d = scratch.middle_d
    pairs = [(scratch.xd1a, scratch.fd1a), (scratch.xd1b, scratch.fd1b)]
    mean_d2, inv_d2 = norm_of(*conv_norm(pairs, middle_d), ones16, count16)
    gain_d2, bias_d2 = inputs.dec_norm2_gain[...], inputs.dec_norm2_bias[...]
    a_d2 = inv_d2 * gain_d2
    activate(
        middle_d,
        scratch.xd2,
        scratch.td2,
        scratch.slope_d2,
        a_d2 * (1.0 + dec_scale),
        (bias_d2 - mean_d2 * a_d2) * (1.0 + dec_scale) + dec_shift,
    )
    result = scratch.result
    last_bias = inputs.dec_conv2_bias[...] + inputs.skip_bias[...]

    def decode(i, carry):
        value = conv_chunk([(scratch.xd2, scratch.fd2)], i)
        value = value + dot(joined[chunk_at(i), :], scratch.f_skip[...])
        result[chunk_at(i), :] = fold(value) + last_bias
        return carry

    lax.fori_loop(0, cells // CHUNK, decode, 0)
    own_output = pltpu.make_async_copy(
        result.at[here_rows], outputs.output.at[row], local_sem.at[10]
    )
    own_output.start()
    for k in range(1, line):
        to = lax.rem(row + k, line)
        there = pl.ds(pl.multiple_of(to * strip_cells, strip_cells), strip_cells)
        output_copies.append(
            send(result.at[there], outputs.output.at[row], device_at(to))
        )

    exchanges = []
    waiting_runs = list(runs)
    landing_at = 0
    sem_at = 4 * (line - 1) + 2 * (line - 1)
    sums, final = scratch.sums, scratch.final

    kinds = (HalvingExchange,) + (Exchange,) * 6 + (SmallExchange,)

    def begin():
        nonlocal landing_at, sem_at
        start, rows = waiting_runs.pop(0)
        exchange = kinds[len(exchanges)](place, start, rows, landing_at, sem_at)
        landing_at += rows - rows // (8 * line)
        sem_at += exchange.count()
        exchanges.append(exchange)
        exchange.advance()

    final_copies = []

    def advance(k):
        exchange = exchanges[k]
        exchange.advance()
        if exchange.done():
            rows = pl.ds(exchange.start, exchange.rows)
            copy = pltpu.make_async_copy(
                final.at[rows], outputs.gradients.at[rows], local_sem.at[11 + k]
            )
            copy.start()
            final_copies.append(copy)

    due = list(DUE)

    def point():
        for k in due.pop(0):
            advance(k)

    def small_row(k, value):
        sums[small_at + k : small_at + k + 1, :] = value

    def spread_grad(source):
        def step(h, carry):
            value = source[row_at(h), :]
            put_row(scratch.xg, h, value)
            return carry + tile_sums(value)

        return grid_rows(step, zeros8)

    def weight_grad(turned, at, depth, a):
        rows = pl.ds((2 - a) * width, cells)
        part = fold_rows(dot(turned[...], scratch.xg[rows, :]))
        for b in range(3):
            high, low = HIGH_AT[2 - b] * c, LOW_AT[2 - b] * c
            to = at + (3 * a + b) * depth
            sums[to : to + c, :] = part[:, high : high + c] + part[:, low : low + c]

    def back_conv(weight, slope, target, source, mean, inv):
        carry = (zeros8, zeros8)
        for i in range(cells // CHUNK):
            value = fold(conv_chunk([(scratch.xg, weight)], i, NT)) * slope[chunk_at(i), :]
            target[chunk_at(i), :] = value
            normed = (source[chunk_at(i), :] - mean) * inv
            carry = (carry[0] + tile_sums(value), carry[1] + tile_sums(value * normed))
            if i % (cells // CHUNK // 2) == cells // CHUNK // 2 - 1:
                point()
        return carry

    def norm_grad(sums_in, scale, ones, count):
        one, two = group_sums(sums_in[0] * scale, sums_in[1] * scale, ones)
        return one / count, two / count

    own[2].wait()
    for copy in cot_copies:
        copy.wait_recv()
    total_cot = column_sum(spread_grad(cot))
    for a in range(3):
        weight_grad(scratch.td2, starts.dec_conv2, c, a)
    part = fold(dot(scratch.turned[...], scratch.xg[width : cells + width, 2 * c : 4 * c]))
    sums[starts.skip_weight : starts.skip_weight + 2 * c, :] = fold_rows(part)
    small_row(3, total_cot)
    begin()

    grad = scratch.grad
    sums_d2 = back_conv(scratch.bd2, scratch.slope_d2, grad, middle_d, mean_d2, inv_d2)
    side_grads = (scratch.grad_a, scratch.grad_b)
    for half in range(2):

        def skip_back(i, carry, half=half):
            rows = pl.ds(pl.multiple_of(i * CHUNK + width, width), CHUNK)
            value = dot(scratch.xg[rows, 2 * c : 4 * c], scratch.b_skip[half], NT)
            side_grads[half][chunk_at(i), :] = fold(value)
            return carry

        lax.fori_loop(0, cells // CHUNK, skip_back, 0)
    point()

    def table_rows(k, sums_in, gain, bias, one_plus):
        plain, times = column_sum(sums_in[0]), column_sum(sums_in[1])
        for s in range(inputs.enc_step_table.shape[0]):
            small_row(k + 2 * s, jnp.where(step_here == s, gain * times + bias * plain, 0.0))
            small_row(k + 2 * s + 1, jnp.where(step_here == s, plain, 0.0))
        return one_plus * times, one_plus * plain

    def middle_grad(source, mean, inv, scale, sums_in):
        zero, slope = norm_grad(sums_in, scale, ones16, count16)

        def step(h, carry):
            normed = (source[row_at(h), :] - mean) * inv
            value = inv * (grad[row_at(h), :] * scale - zero - normed * slope)
            put_row(scratch.xg, h, value)
            return carry

        grid_rows(step)

    gain_row, bias_row = table_rows(16, sums_d2, gain_d2, bias_d2, 1.0 + dec_scale)
    small_row(8, gain_row)
    small_row(9, bias_row)
    middle_grad(middle_d, mean_d2, inv_d2, gain_d2 * (1.0 + dec_scale), sums_d2)
    point()
    for a in range(3):
        weight_grad(scratch.td1a, starts.dec_conv1, 2 * c, a)
        weight_grad(scratch.td1b, starts.dec_conv1 + c, 2 * c, a)
        point()
        begin()

    for half, (source, mean, inv, gain) in enumerate(halves):
        sums_in = back_conv(
            (scratch.bd1a, scratch.bd1b)[half],
            (scratch.slope_d1a, scratch.slope_d1b)[half],
            grad,
            source,
            mean,
            inv,
        )
        small_row(4 + half, column_sum(sums_in[1]))
        small_row(6 + half, column_sum(sums_in[0]))
        zero, slope = norm_grad(sums_in, gain, ones32, count32)
        target = side_grads[half]

        def input_grad(h, carry):
            normed = (source[row_at(h), :] - mean) * inv
            value = inv * (grad[row_at(h), :] * gain - zero - normed * slope)
            value = target[row_at(h), :] + value
            target[row_at(h), :] = value
            return carry + tile_sums(value)

        total = grid_rows(input_grad, zeros8)
        if half == 0:
            small_row(2, column_sum(total))
        point()

    grad_raised, grad_encoded = side_grads
    x_grad_up = scratch.x_grad_up
    for k, piece in enumerate(pick(grad_raised)):
        high, low = split(piece)
        x_grad_up[:, k * c : (k + 1) * c] = high
        x_grad_up[:, (k + 4) * c : (k + 5) * c] = low
    grad_lowered = fold(dot(x_grad_up[...], scratch.b_up[...], NT))
    small_row(1, jnp.sum(grad_lowered, axis=0, keepdims=True))
    x_grad_low = scratch.x_grad_low
    high, low = split(grad_lowered)
    x_grad_low[:, 0:c] = high
    x_grad_low[:, c : 2 * c] = low
    point()
    part = fold(fold_rows(dot(x_up[...], x_grad_up[...], TN)))
    for k in range(4):
        at = starts.up_weight + k * c
        sums[at : at + c, :] = part[:, k * c : (k + 1) * c]
    part = fold_rows(fold(dot(x_down[...], x_grad_low[...], TN)))
    sums[starts.reducer_weight : starts.reducer_weight + 4 * c, :] = part
    point()
    begin()
    place_cells(
        grad, [fold(dot(x_grad_low[...], scratch.b_down[k], NT)) for k in range(4)]
    )

    def join_row(h, carry):
        value = grad_encoded[row_at(h), :] + grad[row_at(h), :]
        grad_encoded[row_at(h), :] = value
        put_row(scratch.xg, h, value)
        return carry + tile_sums(value)

    small_row(0, column_sum(grid_rows(join_row, zeros8)))
    for k in range(10, 16):
        small_row(k, jnp.zeros((1, c), F32))
    sums[small_at + 24 : small_at + LATE, :] = jnp.zeros((LATE - 24, c), F32)
    point()
    for a in range(3):
        weight_grad(scratch.te2, starts.enc_conv2, c, a)
        point()
    begin()
    sums_e2 = back_conv(scratch.be2, scratch.slope_e2, grad, middle_e, mean_e2, inv_e2)
    gain_row, bias_row = table_rows(LATE + 24, sums_e2, gain_e2, bias_e2, 1.0 + enc_scale)
    small_row(LATE + 18, gain_row)
    small_row(LATE + 19, bias_row)
    middle_grad(middle_e, mean_e2, inv_e2, gain_e2 * (1.0 + enc_scale), sums_e2)
    point()
    for a in range(3):
        weight_grad(scratch.te1, starts.enc_conv1, c, a)
        point()
    begin()
    sums_e1 = back_conv(scratch.be1, scratch.slope_e1, grad, lifted, mean_e1, inv_e1)
    small_row(LATE + 16, column_sum(sums_e1[1]))
    small_row(LATE + 17, column_sum(sums_e1[0]))
    zero, slope = norm_grad(sums_e1, gain_e1, ones16, count16)

    def lifted_grad(h, carry):
        normed = (lifted[row_at(h), :] - mean_e1) * inv_e1
        value = inv_e1 * (grad[row_at(h), :] * gain_e1 - zero - normed * slope)
        grad[row_at(h), :] = grad_encoded[row_at(h), :] + value
        return carry

    grid_rows(lifted_grad)
    point()

    late_at = small_at + LATE
    sums[late_at : late_at + 16, :] = dot(fields[...], grad[...], NN, HIGH)
    sums[late_at + 20 : late_at + 24, :] = jnp.zeros((4, c), F32)
    point()
    begin()
    back = dot(lift[...], grad[...], NT, HIGH)
    frames_out = scratch.frames_out
    for source in range(line):
        for k in range(strip):
            h = source * strip + k
            value = back[0:history, h * width : (h + 1) * width]
            frames_out[source, :, k, :] = value * keep * masks[h]
    own_frames = pltpu.make_async_copy(
        frames_out.at[row], outputs.frames_grad.at[row], local_sem.at[19]
    )
    own_frames.start()
    for k in range(1, line):
        to = lax.rem(row + k, line)
        output_copies.append(
            send(frames_out.at[to], outputs.frames_grad.at[row], device_at(to))
        )

    for k in REST:
        advance(k)
    assert not due and all(exchange.done() for exchange in exchanges)

    for copy in output_copies:
        copy.wait_recv()
    own_output.wait()
    own_frames.wait()
    for copy in final_copies:
        copy.wait()
    for copy in frame_copies + cot_copies + output_copies:
        copy.wait_send()
    for exchange in exchanges:
        for copy in exchange.copies:
            copy.wait_send()


def write_kernel(layout, *refs):
    shapes, starts, small_at = layout
    output, frames_grad, gradients = refs[:3]
    outputs = refs[3:-4]
    output_here, frames_here, gradients_here, sem = refs[-4:]
    c = gradients.shape[1]
    moves = [(frames_grad, frames_here, outputs[1])]
    for k, name in enumerate(LARGE):
        rows = pl.ds(starts[name], shapes[name][0])
        moves.append((gradients.at[rows], gradients_here.at[rows], outputs[2 + k]))
    moves.append((output, output_here, outputs[0]))
    small = pl.ds(small_at, SMALL_COUNT)
    first = pltpu.make_async_copy(gradients.at[small], gradients_here.at[small], sem.at[0])
    first.start()
    arriving, leaving = [], []
    for k, (source, here, _) in enumerate(moves):
        arriving.append(pltpu.make_async_copy(source, here, sem.at[1 + 2 * k]))
        arriving[-1].start()
    first.wait()
    for target, (k, rows) in zip(outputs[2 + len(LARGE) :], SMALL_ROWS.values()):
        at = small_at + k
        if rows == 8:
            for s in range(target.shape[0]):
                target[s : s + 1, 0:c] = gradients_here[at + 2 * s : at + 2 * s + 1, :]
                target[s : s + 1, c : 2 * c] = gradients_here[at + 2 * s + 1 : at + 2 * s + 2, :]
        else:
            target[...] = gradients_here[at : at + rows, :]
    for k, (_, here, target) in enumerate(moves):
        arriving[k].wait()
        leaving.append(pltpu.make_async_copy(here, target, sem.at[2 + 2 * k]))
        leaving[-1].start()
    for copy in leaving:
        copy.wait()


def whole_items(shape, *arguments):
    line = shape["rows"]
    whole = Given(*arguments)
    given = whole._asdict()
    frames, cotangent = whole.frames, whole.cotangent
    items, history, strip, width = frames.shape
    c = cotangent.shape[-1]
    cells = strip * line * width
    flat = {}
    for name, value in given.items():
        if value is cotangent:
            value = value.reshape(items, strip * width, c)
        elif name in LARGE:
            value = value.reshape(-1, c)
        elif value.ndim == 1 and name not in IN_SMEM:
            value = value.reshape(-1, c)
        flat[name] = value
    shapes = {name: flat[name].shape for name in LARGE}
    big_layout = layout_of(shapes)
    starts, small_at, total_rows, runs = big_layout
    copies = 7 * (line - 1) + len(runs) * (8 + 2 * (line - 1)) + 6
    landing = sum(rows - rows // (8 * line) for _, rows in runs) + LATE_COUNT * (8 + line)
    shifted = pltpu.VMEM((cells + 2 * width, 6 * c), BF16)
    forward = pltpu.VMEM((18 * c, 2 * c), BF16)
    backward = pltpu.VMEM((2 * c, 18 * c), BF16)
    field = pltpu.VMEM((cells, c), F32)
    flipped_field = pltpu.VMEM((2 * c, cells), BF16)
    quarter = cells // 4
    scratch = dict(
        small=pltpu.VMEM((LATE_COUNT, c), F32),
        send=pltpu.SemaphoreType.DMA((copies,)),
        recv=pltpu.SemaphoreType.DMA((copies,)),
        local=pltpu.SemaphoreType.DMA((20,)),
        sums=pltpu.VMEM((total_rows, c), F32),
        final=pltpu.VMEM((total_rows, c), F32),
        landing=pltpu.VMEM((landing, c), F32),
        frames_in=pltpu.VMEM((line, history, strip, width), F32),
        mask_in=pltpu.VMEM((line, strip, width), jnp.int32),
        frames_out=pltpu.VMEM((line, history, strip, width), F32),
        fields=pltpu.VMEM((16, cells), F32),
        lift=pltpu.VMEM((16, c), F32),
        joined=pltpu.VMEM((cells, 4 * c), BF16),
        x_down=pltpu.VMEM((quarter, 8 * c), BF16),
        x_grad_up=pltpu.VMEM((quarter, 8 * c), BF16),
        x_up=pltpu.VMEM((quarter, 2 * c), BF16),
        x_grad_low=pltpu.VMEM((quarter, 2 * c), BF16),
        f_down=pltpu.VMEM((8 * c, 2 * c), BF16),
        b_down=pltpu.VMEM((4, 2 * c, 2 * c), BF16),
        f_up=pltpu.VMEM((4, 2 * c, 2 * c), BF16),
        b_up=pltpu.VMEM((2 * c, 8 * c), BF16),
        f_skip=pltpu.VMEM((4 * c, 2 * c), BF16),
        b_skip=pltpu.VMEM((2, 2 * c, 2 * c), BF16),
        xe1=shifted,
        xe2=shifted,
        xd1a=shifted,
        xd1b=shifted,
        xd2=shifted,
        xg=shifted,
        te1=flipped_field,
        te2=flipped_field,
        td1a=flipped_field,
        td1b=flipped_field,
        td2=flipped_field,
        turned=pltpu.VMEM((4 * c, cells), BF16),
        fe1=forward,
        fe2=forward,
        fd1a=forward,
        fd1b=forward,
        fd2=forward,
        be1=backward,
        be2=backward,
        bd1a=backward,
        bd1b=backward,
        bd2=backward,
        slope_e1=field,
        slope_e2=field,
        slope_d1a=field,
        slope_d1b=field,
        slope_d2=field,
        lifted=field,
        middle_e=field,
        encoded=field,
        raised=field,
        middle_d=field,
        result=field,
        cot=field,
        grad=field,
        grad_a=field,
        grad_b=field,
    )
    scratch.update({name: pltpu.VMEM(shapes[name], F32) for name in LARGE})

    in_hbm = pl.BlockSpec(memory_space=pl.ANY)
    in_vmem = pl.BlockSpec(memory_space=pltpu.VMEM)
    in_smem = pl.BlockSpec(memory_space=pltpu.SMEM)
    in_specs = [
        in_hbm if name in IN_HBM else in_smem if name in IN_SMEM else in_vmem
        for name in ARGUMENTS
    ]
    out_shape = [
        jax.ShapeDtypeStruct((items, strip * width, c), F32),
        jax.ShapeDtypeStruct(frames.shape, F32),
        jax.ShapeDtypeStruct((total_rows, c), F32),
    ]
    out_specs = [in_hbm] * 3
    results = pl.pallas_call(
        functools.partial(
            item_kernel,
            (line, strip, width, shapes, big_layout),
            tuple(scratch),
        ),
        out_shape=out_shape,
        in_specs=in_specs,
        out_specs=out_specs,
        scratch_shapes=list(scratch.values()),
        compiler_params=pltpu.CompilerParams(
            collective_id=0, has_side_effects=True, vmem_limit_bytes=62 * 1024 * 1024
        ),
    )(*[flat[name] for name in ARGUMENTS])
    names = LARGE + tuple(SMALL_ROWS)
    written = pl.pallas_call(
        functools.partial(write_kernel, (shapes, starts, small_at)),
        out_shape=out_shape[:2] + [jax.ShapeDtypeStruct(flat[name].shape, F32) for name in names],
        in_specs=[pl.BlockSpec(memory_space=pltpu.HBM)] * 3,
        out_specs=[in_hbm] * (2 + len(LARGE)) + [in_vmem] * len(SMALL_ROWS),
        scratch_shapes=[
            pltpu.VMEM((items, strip * width, c), F32),
            pltpu.VMEM(frames.shape, F32),
            pltpu.VMEM((total_rows, c), F32),
            pltpu.SemaphoreType.DMA((1 + 2 * (2 + len(LARGE)),)),
        ],
        compiler_params=pltpu.CompilerParams(vmem_limit_bytes=60 * 1024 * 1024),
    )(*results)
    grads = dict(zip(names, written[2:]))
    ordered = [name for name in ARGUMENTS if name in grads]
    return (written[0].reshape(cotangent.shape), written[1]) + tuple(
        grads[name].reshape(given[name].shape) for name in ordered
    )


def body(shape, *arguments):
    items, _, strip, width = arguments[0].shape
    line = shape["rows"]
    whole = (
        shape["section"] == 2
        and shape["batch"] == 4
        and items == line
        and arguments[-1].shape[-1] == 128
        and (strip * line * width) % CHUNK == 0
    )
    return whole_items(shape, *arguments) if whole else strips_body(*arguments)


def solution(mesh):
    in_specs = (
        P(("section", "batch"), None, "rows", None),
        P(("section", "batch")),
        P(("section", "batch"), "rows", None),
        P(("section", "batch")),
        P(),
        P(),
        P(),
        P(),
        P(),
        P(),
        P(),
        P(),
        P(),
        P(),
        P(),
        P(),
        P(),
        P(),
        P(),
        P(),
        P(),
        P(),
        P(),
        P(),
        P(),
        P(),
        P(),
        P(),
        P(("section", "batch"), "rows", None, None),
    )
    out_specs = (
        P(("section", "batch"), "rows", None, None),
        P(("section", "batch"), None, "rows", None),
        P(),
        P(),
        P(),
        P(),
        P(),
        P(),
        P(),
        P(),
        P(),
        P(),
        P(),
        P(),
        P(),
        P(),
        P(),
        P(),
        P(),
        P(),
        P(),
        P(),
        P(),
        P(),
        P(),
        P(),
    )
    return jax.shard_map(functools.partial(body, mesh.shape), mesh=mesh, in_specs=in_specs, out_specs=out_specs, check_vma=False)
```

```python
import functools
from types import SimpleNamespace
from typing import Any, NamedTuple

import jax
import jax.numpy as jnp
from jax import lax
from jax.experimental import pallas as pl
from jax.experimental.pallas import tpu as pltpu
from jax.sharding import PartitionSpec as P

GROUPS = 8
FIELDS = 3
HIST = 4


EPS = 1e-05
HIGH = lax.Precision.HIGHEST


def extended(cells, sides, width):
    for axis, dim in sides:
        count = lax.axis_size(axis)
        ends = count - 1
        head = lax.slice_in_dim(cells, 0, width, axis=dim)
        tail = lax.slice_in_dim(cells, cells.shape[dim] - width, cells.shape[dim], axis=dim)
        cells = jnp.concatenate(
            [
                lax.ppermute(tail, axis, [(i, (i + 1) % count) for i in range(ends)]),
                cells,
                lax.ppermute(head, axis, [((i + 1) % count, i) for i in range(ends)]),
            ],
            axis=dim,
        )
    return cells


def from_behind(value, axis, steps):
    count = lax.axis_size(axis)
    pairs = [(source, (source + steps) % count) for source in range(count)]
    return lax.ppermute(value, axis, pairs)


def group_view(value_arrays):
    extent = value_arrays.shape
    return value_arrays.reshape(extent[:-1] + (GROUPS, extent[-1] // GROUPS))


def global_sums(value_arrays):
    grouped = group_view(value_arrays)
    flat = grouped.reshape(-1, GROUPS, grouped.shape[-1])
    first_sum = jnp.sum(flat, axis=(0, 2))
    second_sum = jnp.sum(flat * flat, axis=(0, 2))
    return lax.psum((first_sum, second_sum), "rows")


def apply_norm(value_arrays, sum_one, sum_two, norm_gain, norm_bias, total):
    grouped = group_view(value_arrays)
    group_mean = sum_one / total
    variance = sum_two / total - group_mean * group_mean
    inverse = lax.rsqrt(variance + EPS)
    normed = (grouped - group_mean[:, None]) * inverse[:, None]
    return normed.reshape(value_arrays.shape) * norm_gain + norm_bias


def norm_back(value_arrays, grad_one, grad_two):
    grouped = group_view(value_arrays)
    extra = grad_one[:, None] + 2.0 * grouped * grad_two[:, None]
    return extra.reshape(value_arrays.shape)


def reduce_grads(grad_one, grad_two):
    return lax.psum((grad_one, grad_two), "rows")


def conv_rows(padded, kernel):
    widened = jnp.pad(padded, ((0, 0), (1, 1), (0, 0)))
    return lax.conv_general_dilated(
        widened[None],
        kernel,
        (1, 1),
        "VALID",
        dimension_numbers=("NHWC", "HWIO", "NHWC"),
        precision=HIGH,
    )[0]


def flipped(kernel):
    return jnp.transpose(kernel[::-1, ::-1], (0, 1, 3, 2))


def pad_grads(value_arrays):
    return extended(value_arrays, (("rows", 0),), 1)


def totals_of(inputs, conv1):
    strip = inputs.shape[0]
    cells = strip * lax.axis_size("rows") * inputs.shape[1]
    return (cells * (inputs.shape[2] // GROUPS), cells * (conv1.shape[3] // GROUPS))


def block_forward(inputs, weights, scale_part, shift_part):
    norm1_gain, norm1_bias, conv1, norm2_gain, norm2_bias, conv2, conv2_bias = weights
    total_in, total_mid = totals_of(inputs, conv1)
    sums_in = global_sums(inputs)

    def pad_rows(value_arrays):
        return extended(value_arrays, (("rows", 0),), 1)

    act_one = pad_rows(
        jax.nn.gelu(
            apply_norm(inputs, sums_in[0], sums_in[1], norm1_gain, norm1_bias, total_in),
            approximate=False,
        )
    )
    middle = conv_rows(act_one, conv1)
    sums_mid = global_sums(middle)
    shaped = (
        apply_norm(middle, sums_mid[0], sums_mid[1], norm2_gain, norm2_bias, total_mid)
        * (1.0 + scale_part)
        + shift_part
    )
    act_two = pad_rows(jax.nn.gelu(shaped, approximate=False))
    branch = conv_rows(act_two, conv2) + conv2_bias
    return (branch, (sums_in[0], sums_in[1], act_one, middle, sums_mid[0], sums_mid[1], act_two))


def block_backward(inputs, weights, scale_part, shift_part, kept, grad_out):
    norm1_gain, norm1_bias, conv1, norm2_gain, norm2_bias, conv2, conv2_bias = weights
    in_one, in_two, act_one, middle, mid_one, mid_two, act_two = kept
    total_in, total_mid = totals_of(inputs, conv1)
    grad_conv2 = jax.vjp(lambda kernel: conv_rows(act_two, kernel), conv2)[1](grad_out)[0]
    grad_bias2 = jnp.sum(grad_out, axis=(0, 1))
    grad_act_two = conv_rows(pad_grads(grad_out), flipped(conv2))

    def second_piece(middle_in, sum_one, sum_two, gain_in, incoming_bias, scale_in, shift_in):
        shaped = (
            apply_norm(middle_in, sum_one, sum_two, gain_in, incoming_bias, total_mid)
            * (1.0 + scale_in)
            + shift_in
        )
        return jax.nn.gelu(shaped, approximate=False)

    second_pull = jax.vjp(
        second_piece, middle, mid_one, mid_two, norm2_gain, norm2_bias, scale_part, shift_part
    )[1](grad_act_two)
    summed_one, summed_two = reduce_grads(second_pull[1], second_pull[2])
    grad_middle = second_pull[0] + norm_back(middle, summed_one, summed_two)
    grad_conv1 = jax.vjp(lambda kernel: conv_rows(act_one, kernel), conv1)[1](grad_middle)[0]
    grad_act_one = conv_rows(pad_grads(grad_middle), flipped(conv1))

    def first_piece(inputs_in, sum_one, sum_two, gain_in, incoming_bias):
        return jax.nn.gelu(
            apply_norm(inputs_in, sum_one, sum_two, gain_in, incoming_bias, total_in),
            approximate=False,
        )

    first_pull = jax.vjp(first_piece, inputs, in_one, in_two, norm1_gain, norm1_bias)[1](
        grad_act_one
    )
    first_one, first_two = reduce_grads(first_pull[1], first_pull[2])
    grad_inputs = first_pull[0] + norm_back(inputs, first_one, first_two)
    grads = (
        first_pull[3],
        first_pull[4],
        grad_conv1,
        second_pull[3],
        second_pull[4],
        grad_conv2,
        grad_bias2,
    )
    return (grad_inputs, grads, second_pull[5], second_pull[6])


def conditioning(step_item, table):
    one_hot = (jnp.arange(table.shape[0], dtype=jnp.int32) == step_item).astype(jnp.float32)
    condition = jnp.dot(one_hot, table, precision=HIGH)
    half_width = table.shape[1] // 2
    return (condition[:half_width], condition[half_width:], one_hot)


def project_in(frames_item, mask_item, count_item, incoming_weight, incoming_bias):
    history = jnp.arange(HIST, dtype=jnp.int32) >= HIST - count_item
    keep = jnp.repeat(history, FIELDS).astype(jnp.float32)
    lifted = (
        jnp.einsum(
            "fhw,fc->hwc", frames_item * keep[:, None, None], incoming_weight, precision=HIGH
        )
        + incoming_bias
    )
    return lifted * mask_item[:, :, None].astype(jnp.float32)


def coarsen_field(value_arrays, incoming_weight, incoming_bias):
    rows_here, width_here, depth_here = value_arrays.shape
    blocks = value_arrays.reshape(rows_here // 2, 2, width_here // 2, 2, depth_here)
    return jnp.einsum("iajbk,abkc->ijc", blocks, incoming_weight, precision=HIGH) + incoming_bias


def upsample(value_arrays, incoming_weight, incoming_bias):
    result = jnp.einsum("ijk,abkc->iajbc", value_arrays, incoming_weight, precision=HIGH)
    extent = result.shape
    return result.reshape(extent[0] * 2, extent[2] * 2, extent[4]) + incoming_bias


def flatten_all(pieces):
    return jnp.concatenate([piece.reshape(-1) for piece in pieces])


def unflatten_all(flat, templates):
    pieces = []
    offset_at = 0
    for template in templates:
        count_here = template.size
        pieces.append(flat[offset_at : offset_at + count_here].reshape(template.shape))
        offset_at += count_here
    return tuple(pieces)


def strips_body(
    frames,
    counts,
    cell_mask,
    step_index,
    lift_weight,
    lift_bias,
    enc_norm1_gain,
    enc_norm1_bias,
    enc_conv1,
    enc_step_table,
    enc_norm2_gain,
    enc_norm2_bias,
    enc_conv2,
    enc_conv2_bias,
    reducer_weight,
    reducer_bias,
    up_weight,
    up_bias,
    dec_norm1_gain,
    dec_norm1_bias,
    dec_conv1,
    dec_step_table,
    dec_norm2_gain,
    dec_norm2_bias,
    dec_conv2,
    dec_conv2_bias,
    skip_weight,
    skip_bias,
    cotangent,
):
    enc_weights = (
        enc_norm1_gain,
        enc_norm1_bias,
        enc_conv1,
        enc_norm2_gain,
        enc_norm2_bias,
        enc_conv2,
        enc_conv2_bias,
    )
    dec_weights = (
        dec_norm1_gain,
        dec_norm1_bias,
        dec_conv1,
        dec_norm2_gain,
        dec_norm2_bias,
        dec_conv2,
        dec_conv2_bias,
    )
    params = (
        lift_weight,
        lift_bias,
        enc_norm1_gain,
        enc_norm1_bias,
        enc_conv1,
        enc_step_table,
        enc_norm2_gain,
        enc_norm2_bias,
        enc_conv2,
        enc_conv2_bias,
        reducer_weight,
        reducer_bias,
        up_weight,
        up_bias,
        dec_norm1_gain,
        dec_norm1_bias,
        dec_conv1,
        dec_step_table,
        dec_norm2_gain,
        dec_norm2_bias,
        dec_conv2,
        dec_conv2_bias,
        skip_weight,
        skip_bias,
    )

    def forward_micro(carry, sliced):
        frames_item, mask_item, count_item, step_item = sliced
        lifted = project_in(frames_item, mask_item, count_item, lift_weight, lift_bias)
        enc_scale, enc_shift, unused_hot = conditioning(step_item, enc_step_table)
        enc_branch, enc_kept = block_forward(lifted, enc_weights, enc_scale, enc_shift)
        encoder_result = lifted + enc_branch
        coarse_field = coarsen_field(encoder_result, reducer_weight, reducer_bias)
        foreign = from_behind(coarse_field, "section", 1)
        raised_foreign = upsample(foreign, up_weight, up_bias)
        raised = from_behind(raised_foreign, "section", 1)
        joined = jnp.concatenate([raised, encoder_result], axis=-1)
        dec_scale, dec_shift, unused_again = conditioning(step_item, dec_step_table)
        dec_branch, dec_kept = block_forward(joined, dec_weights, dec_scale, dec_shift)
        output_item = jnp.dot(joined, skip_weight, precision=HIGH) + skip_bias + dec_branch
        return (carry, (output_item, (lifted, enc_kept, encoder_result, foreign, joined, dec_kept)))

    unused, (output, kept_all) = lax.scan(
        forward_micro, jnp.zeros((), jnp.float32), (frames, cell_mask, counts, step_index)
    )

    def backward_micro(totals, sliced):
        frames_item, mask_item, count_item, step_item, grad_out, kept = sliced
        lifted, enc_kept, encoder_result, foreign, joined, dec_kept = kept
        dec_scale, dec_shift, one_hot = conditioning(step_item, dec_step_table)
        grad_joined, dec_grads, dec_gscale, dec_gshift = block_backward(
            joined, dec_weights, dec_scale, dec_shift, dec_kept, grad_out
        )
        grad_skip_weight = jnp.einsum("hwk,hwc->kc", joined, grad_out, precision=HIGH)
        grad_skip_bias = jnp.sum(grad_out, axis=(0, 1))
        grad_joined = grad_joined + jnp.dot(grad_out, skip_weight.T, precision=HIGH)
        half_width = joined.shape[-1] // 2
        grad_raised = grad_joined[..., :half_width]
        grad_encoded = grad_joined[..., half_width:]
        grad_foreign_up = from_behind(grad_raised, "section", 1)
        up_pull = jax.vjp(upsample, foreign, up_weight, up_bias)[1](grad_foreign_up)
        coarse_gradient = from_behind(up_pull[0], "section", 1)
        reducer_pullback = jax.vjp(coarsen_field, encoder_result, reducer_weight, reducer_bias)[1](
            coarse_gradient
        )
        grad_encoded = grad_encoded + reducer_pullback[0]
        enc_scale, enc_shift, enc_hot = conditioning(step_item, enc_step_table)
        grad_lifted, enc_grads, enc_gscale, enc_gshift = block_backward(
            lifted, enc_weights, enc_scale, enc_shift, enc_kept, grad_encoded
        )
        grad_lifted = grad_lifted + grad_encoded
        proj_pull = jax.vjp(
            lambda frames_in, incoming_weight, incoming_bias: project_in(
                frames_in, mask_item, count_item, incoming_weight, incoming_bias
            ),
            frames_item,
            lift_weight,
            lift_bias,
        )[1](grad_lifted)
        enc_table_grad = enc_hot[:, None] * jnp.concatenate([enc_gscale, enc_gshift])[None, :]
        dec_table_grad = one_hot[:, None] * jnp.concatenate([dec_gscale, dec_gshift])[None, :]
        micro_list = (
            proj_pull[1],
            proj_pull[2],
            enc_grads[0],
            enc_grads[1],
            enc_grads[2],
            enc_table_grad,
            enc_grads[3],
            enc_grads[4],
            enc_grads[5],
            enc_grads[6],
            reducer_pullback[1],
            reducer_pullback[2],
            up_pull[1],
            up_pull[2],
            dec_grads[0],
            dec_grads[1],
            dec_grads[2],
            dec_table_grad,
            dec_grads[3],
            dec_grads[4],
            dec_grads[5],
            dec_grads[6],
            grad_skip_weight,
            grad_skip_bias,
        )
        micro_flat = flatten_all(micro_list)
        return (totals + micro_flat, proj_pull[0])

    total_size = sum((piece.size for piece in params))
    start_totals = jnp.zeros((total_size,), jnp.float32)
    flat_totals, frames_grad = lax.scan(
        backward_micro,
        start_totals,
        (frames, cell_mask, counts, step_index, cotangent, kept_all),
        reverse=True,
    )
    flat_totals = lax.psum(flat_totals, ("section", "batch", "rows"))
    grads = unflatten_all(flat_totals, params)
    return (output, frames_grad) + grads


F32 = jnp.float32
BF16 = jnp.bfloat16
MESH = pl.DeviceIdType.MESH
NN = ((1,), (0,))
NT = ((1,), (1,))
TN = ((0,), (0,))
HIGH_AT = (0, 2, 1)
LOW_AT = (4, 3, 5)
CHUNK = 512
class Given(NamedTuple):
    frames: Any
    counts: Any
    cell_mask: Any
    step_index: Any
    lift_weight: Any
    lift_bias: Any
    enc_norm1_gain: Any
    enc_norm1_bias: Any
    enc_conv1: Any
    enc_step_table: Any
    enc_norm2_gain: Any
    enc_norm2_bias: Any
    enc_conv2: Any
    enc_conv2_bias: Any
    reducer_weight: Any
    reducer_bias: Any
    up_weight: Any
    up_bias: Any
    dec_norm1_gain: Any
    dec_norm1_bias: Any
    dec_conv1: Any
    dec_step_table: Any
    dec_norm2_gain: Any
    dec_norm2_bias: Any
    dec_conv2: Any
    dec_conv2_bias: Any
    skip_weight: Any
    skip_bias: Any
    cotangent: Any


ARGUMENTS = Given._fields
LARGE = tuple(
    dict(
        dec_conv1=0,
        up_weight=0,
        reducer_weight=0,
        dec_conv2=0,
        skip_weight=0,
        enc_conv1=0,
        enc_conv2=0,
    )
)
IN_HBM = tuple(dict(frames=0, cell_mask=0, cotangent=0)) + LARGE
IN_SMEM = tuple(dict(counts=0, step_index=0))
LATE = 128
SMALL_ROWS = dict(
    enc_conv2_bias=(0, 1),
    reducer_bias=(1, 1),
    up_bias=(2, 1),
    dec_conv2_bias=(3, 1),
    skip_bias=(3, 1),
    dec_norm1_gain=(4, 2),
    dec_norm1_bias=(6, 2),
    dec_norm2_gain=(8, 1),
    dec_norm2_bias=(9, 1),
    dec_step_table=(16, 8),
    lift_weight=(LATE, 12),
    lift_bias=(LATE + 12, 1),
    enc_norm1_gain=(LATE + 16, 1),
    enc_norm1_bias=(LATE + 17, 1),
    enc_norm2_gain=(LATE + 18, 1),
    enc_norm2_bias=(LATE + 19, 1),
    enc_step_table=(LATE + 24, 8),
)
LATE_COUNT = 32
PIECES = 4
SMALL_COUNT = LATE + LATE_COUNT
DUE = ((), (), (), (), (), (0,), (), (), (1,), (0, 2), (), (3,), (1, 0), (), (), (2,), (), (3,), (), (4,), (), (), (), (), (), (5,), (4, 1), (), ())
REST = (6, 0, 5, 2, 3, 6, 4, 1, 7, 1, 0, 7, 1, 0, 5, 2, 0, 3, 2, 6, 3, 0, 4, 2, 3, 5, 4, 6, 5, 4, 6, 5, 6)
OUTPUTS = tuple(dict(output=0, frames_grad=0, gradients=0))


def split(value):
    high = value.astype(BF16)
    return high, (value - high.astype(F32)).astype(BF16)


def dot(left, right, dims=NN, precision=None):
    return lax.dot_general(
        left, right, (dims, ((), ())), precision=precision, preferred_element_type=F32
    )


def fold(value):
    half = value.shape[1] // 2
    return value[:, :half] + value[:, half:]


def fold_rows(value):
    half = value.shape[0] // 2
    return value[:half] + value[half:]


def tile_sums(value):
    return jnp.sum(value.reshape(-1, 8, value.shape[-1]), axis=0)


def column_sum(tiles):
    return jnp.sum(tiles, axis=0, keepdims=True)


def group_ones(channels, size):
    rows = lax.broadcasted_iota(jnp.int32, (channels, channels), 0) // size
    columns = lax.broadcasted_iota(jnp.int32, (channels, channels), 1) // size
    return (rows == columns).astype(F32)


def group_sums(first, second, ones):
    both = dot(jnp.concatenate([first, second], axis=0), ones, precision=HIGH)
    return column_sum(both[:8]), column_sum(both[8:])


class Exchange:

    def __init__(self, place, start, rows, landing, first_sem):
        self.place, self.start, self.rows, self.landing = place, start, rows, landing
        self.sem = first_sem
        self.stage = 0
        self.copies = []
        self.waiting = []
        self.group = place.plane_group
        self.half = rows // 2
        self.base = start + place.core * self.half
        self._finish(self.half)

    def _finish(self, size):
        self.part = size // self.group.count
        self.own = self.base + self.group.here * self.part
        self.shard = self.part // self.place.line.count
        self.last = self.own + self.place.line.here * self.shard

    def count(self):
        return 2 * PIECES + 2 * (self.group.count - 1) + 2 * (self.place.line.count - 1)

    def _copy(self, source, target, device):
        place = self.place
        copy = pltpu.make_async_remote_copy(
            src_ref=source,
            dst_ref=target,
            send_sem=place.send.at[self.sem],
            recv_sem=place.recv.at[self.sem],
            device_id=device,
            device_id_type=MESH,
        )
        self.sem += 1
        copy.start()
        self.copies.append(copy)
        self.waiting.append(copy)

    def _pieces(self, source, at, target, to, size, device):
        each = size // PIECES
        for k in range(PIECES):
            self._copy(
                source.at[self._rows(at + k * each, each)],
                target.at[self._rows(to + k * each, each)],
                device,
            )

    def _wait(self):
        for copy in self.waiting:
            copy.wait_recv()
        self.waiting = []

    def _rows(self, at, size):
        return pl.ds(pl.multiple_of(at, 8), size)

    def _swap(self):
        place = self.place
        other = self.start + (1 - place.core) * self.half
        self.land = self.landing
        self.landing += self.half
        self._pieces(place.sums, other, place.landing, self.land, self.half, place.partner)

    def _add_swap(self):
        place = self.place
        block = 64 if self.half % 64 == 0 else 32

        def step(i, carry):
            here = self._rows(self.base + i * block, block)
            there = self._rows(self.land + i * block, block)
            place.sums[here] = place.sums[here] + place.landing[there]
            return carry

        lax.fori_loop(0, self.half // block, step, 0)

    def _scatter(self, group, base, size):
        place = self.place
        self.land = self.landing
        for k in range(1, group.count):
            to = lax.rem(group.here + k, group.count)
            self._copy(
                place.sums.at[self._rows(base + to * size, size)],
                place.landing.at[pl.ds(self.landing, size)],
                group.device(to),
            )
            self.landing += size

    def _total(self, group, own, size, target):
        place = self.place
        block = 8 if size % 32 else 32

        def step(i, carry):
            here = self._rows(own + i * block, block)
            total = place.sums[here]
            for k in range(group.count - 1):
                there = self._rows(self.land + k * size + i * block, block)
                total = total + place.landing[there]
            target[here] = total
            return carry

        lax.fori_loop(0, size // block, step, 0)

    def _gather(self, group, own, size):
        final = self.place.final
        here = self._rows(own, size)
        for k in range(1, group.count):
            to = lax.rem(group.here + k, group.count)
            self._copy(final.at[here], final.at[here], group.device(to))

    def _steps(self):
        place, group = self.place, self.group
        yield self._swap()
        self._wait()
        self._add_swap()
        yield from self._both()
        self._pieces(place.final, self.base, place.final, self.base, self.half, place.partner)
        yield
        self._wait()
        yield

    def _both(self):
        place, group = self.place, self.group
        line = place.line
        self._scatter(group, self.base, self.part)
        yield
        self._wait()
        self._total(group, self.own, self.part, place.sums)
        self._scatter(line, self.own, self.shard)
        yield
        self._wait()
        self._total(line, self.last, self.shard, place.final)
        self._gather(line, self.last, self.shard)
        yield
        self._wait()
        self._gather(group, self.own, self.part)
        yield
        self._wait()

    def advance(self):
        if self.stage == 0:
            self.steps = self._steps()
        self.stage += 1
        next(self.steps)

    def done(self):
        return self.stage == 7


class HalvingExchange(Exchange):

    def count(self):
        return 4 + 2 * PIECES + 2 * (self.place.line.count - 1)

    def _halve(self, level):
        place = self.place
        self.half = self.rows >> (level + 1)
        bit, device = place.halves[level]
        other = self.base + (1 - bit) * self.half
        self.base = self.base + bit * self.half
        self.land = self.landing
        self.landing += self.half
        self._send(level, place.sums, other, place.landing, self.land, device)

    def _send(self, level, source, at, target, to, device):
        if level == 0:
            self._pieces(source, at, target, to, self.rows // 2, device)
        else:
            size = self.rows >> (level + 1)
            here, there = self._rows(at, size), self._rows(to, size)
            self._copy(source.at[here], target.at[there], device)

    def _steps(self):
        place, line, final = self.place, self.place.line, self.place.final
        self.base = self.start
        bases = []
        for level in range(3):
            self._halve(level)
            bases.append(self.base)
            yield
            self._wait()
            self._add_swap()
        shard = self.half // line.count
        last = self.base + line.here * shard
        self._scatter(line, self.base, shard)
        yield
        self._wait()
        self._total(line, last, shard, final)
        self._gather(line, last, shard)
        yield
        for level in (2, 1, 0):
            self._wait()
            at = bases[level]
            self._send(level, final, at, final, at, place.halves[level][1])
            yield
        self._wait()
        yield

    def done(self):
        return self.stage == 9


class SmallExchange(Exchange):

    def count(self):
        return self.place.cores_group.count + self.place.line.count - 2

    def _share(self, group, source):
        place = self.place
        self.land = self.landing
        self.landing += group.count * self.rows
        own = self._rows(self.land + group.here * self.rows, self.rows)
        place.landing[own] = source[...]
        for k in range(1, group.count):
            to = lax.rem(group.here + k, group.count)
            self._copy(source, place.landing.at[own], group.device(to))

    def _sum(self, group):
        total = None
        for k in range(group.count):
            part = self.place.landing[pl.ds(self.land + k * self.rows, self.rows)]
            total = part if total is None else total + part
        return total

    def _steps(self):
        place = self.place
        here = pl.ds(self.start, self.rows)
        self._share(place.line, place.sums.at[here])
        yield
        self._wait()
        place.small[...] = self._sum(place.line)
        self._share(place.cores_group, place.small)
        yield
        self._wait()
        place.final[here] = self._sum(place.cores_group)
        yield

    def done(self):
        return self.stage == 3


def layout_of(shapes):
    starts = {}
    at = 0
    for name in LARGE:
        starts[name] = at
        at += shapes[name][0]
    small = at
    begins = SimpleNamespace(**starts)
    late = small + LATE
    part = (begins.up_weight - begins.dec_conv1) // 3
    skip = begins.skip_weight + 128
    conv1, up = begins.dec_conv1, begins.up_weight
    edges = (
        (begins.dec_conv2, skip),
        (conv1, conv1 + part),
        (conv1 + part, conv1 + 2 * part),
        (conv1 + 2 * part, up),
        (up, begins.dec_conv2),
        (begins.enc_conv2, late),
        (skip, begins.enc_conv2),
        (late, late + LATE_COUNT),
    )
    runs = [(first, last - first) for first, last in edges]
    return starts, small, late + LATE_COUNT, runs


def item_kernel(sizes, scratch_names, *refs):
    line, strip, width, shapes, big_layout = sizes
    begins, small_at, total_rows, runs = big_layout
    starts = SimpleNamespace(**begins)
    inputs = Given(*refs[: len(ARGUMENTS)])
    refs = refs[len(ARGUMENTS) :]
    output_names = OUTPUTS
    outputs = SimpleNamespace(**dict(zip(output_names, refs)))
    scratch = SimpleNamespace(**dict(zip(scratch_names, refs[len(output_names) :])))

    def w_of(name):
        return getattr(scratch, name)

    height = strip * line
    cells = height * width
    c = inputs.lift_weight.shape[1]
    strip_cells = strip * width
    history = inputs.frames.shape[1]

    core = lax.axis_index("section")
    plane = lax.axis_index("batch")
    row = lax.axis_index("rows")
    y, x = plane // 2, lax.rem(plane, 2)
    along_x = plane + 1 - 2 * x
    along_y = plane + 2 - 4 * y

    def device_at(to):
        return (core, plane, to)

    place = SimpleNamespace(
        core=core,
        partner=(1 - core, plane, row),
        line=SimpleNamespace(count=line, here=row, device=device_at),
        plane_group=SimpleNamespace(
            count=4, here=plane, device=lambda to: (core, to, row)
        ),
        cores_group=SimpleNamespace(
            count=8,
            here=core * 4 + plane,
            device=lambda to: (to // 4, lax.rem(to, 4), row),
        ),
        halves=(
            (core, (1 - core, plane, row)),
            (x * (1 - core) + y * core, (core, along_x * (1 - core) + along_y * core, row)),
            (y * (1 - core) + x * core, (core, along_y * (1 - core) + along_x * core, row)),
        ),
        small=scratch.small,
        sums=scratch.sums,
        final=scratch.final,
        landing=scratch.landing,
        send=scratch.send,
        recv=scratch.recv,
    )
    local_sem = scratch.local

    weight_copies = {}
    for k, name in enumerate(LARGE):
        copy = pltpu.make_async_copy(getattr(inputs, name), w_of(name), local_sem.at[k])
        weight_copies[name] = copy
        copy.start()
    frames_in, mask_in, cot = scratch.frames_in, scratch.mask_in, scratch.cot
    here_rows = pl.ds(pl.multiple_of(row * strip_cells, strip_cells), strip_cells)
    own = (
        pltpu.make_async_copy(inputs.frames.at[row], frames_in.at[row], local_sem.at[7]),
        pltpu.make_async_copy(inputs.cell_mask.at[row], mask_in.at[row], local_sem.at[8]),
        pltpu.make_async_copy(
            inputs.cotangent.at[row], cot.at[here_rows], local_sem.at[9]
        ),
    )
    for copy in own:
        copy.start()

    barrier = pltpu.get_barrier_semaphore()
    peers = [device_at(lax.rem(row + k, line)) for k in range(1, line)]
    cores_group = place.cores_group
    for k in range(1, 8):
        peers.append(cores_group.device(lax.rem(cores_group.here + k, 8)))
    for device in peers:
        pl.semaphore_signal(barrier, inc=1, device_id=device, device_id_type=MESH)
    pl.semaphore_wait(barrier, len(peers))

    next_sem = 0

    def send(source, target, device):
        nonlocal next_sem
        copy = pltpu.make_async_remote_copy(
            src_ref=source,
            dst_ref=target,
            send_sem=scratch.send.at[next_sem],
            recv_sem=scratch.recv.at[next_sem],
            device_id=device,
            device_id_type=MESH,
        )
        next_sem += 1
        copy.start()
        return copy

    frame_copies, cot_copies, output_copies = [], [], []
    for k in range(1, line):
        to = lax.rem(row + k, line)
        device = device_at(to)
        frame_copies.append(send(inputs.frames.at[to], frames_in.at[row], device))
        frame_copies.append(send(inputs.cell_mask.at[to], mask_in.at[row], device))
    for k in range(1, line):
        to = lax.rem(row + k, line)
        cot_copies.append(
            send(inputs.cotangent.at[to], cot.at[here_rows], device_at(to))
        )

    copied = SimpleNamespace(**weight_copies)
    def stack_conv(source, half, depth, forward, backward):
        for a in range(3):
            for b in range(3):
                at = (3 * a + b) * depth + half * c
                high, low = split(source[at : at + c, :])
                for block in (HIGH_AT[b], LOW_AT[b]):
                    rows = slice((6 * a + block) * c, (6 * a + block + 1) * c)
                    forward[rows, 0:c] = high
                    forward[rows, c : 2 * c] = low
                for block in (HIGH_AT[2 - b], LOW_AT[2 - b]):
                    tap = 6 * (2 - a) + block
                    columns = slice(tap * c, (tap + 1) * c)
                    backward[0:c, columns] = high
                    backward[c : 2 * c, columns] = low

    copied.enc_conv1.wait()
    stack_conv(scratch.enc_conv1, 0, c, scratch.fe1, scratch.be1)
    copied.enc_conv2.wait()
    stack_conv(scratch.enc_conv2, 0, c, scratch.fe2, scratch.be2)
    copied.reducer_weight.wait()
    for k in range(4):
        high, low = split(scratch.reducer_weight[k * c : (k + 1) * c, :])
        for block in (k, k + 4):
            scratch.f_down[block * c : (block + 1) * c, 0:c] = high
            scratch.f_down[block * c : (block + 1) * c, c : 2 * c] = low
        for block in (0, 1):
            columns = slice(block * c, (block + 1) * c)
            scratch.b_down[k, 0:c, columns] = high
            scratch.b_down[k, c : 2 * c, columns] = low
    copied.up_weight.wait()
    for k in range(4):
        high, low = split(scratch.up_weight[k * c : (k + 1) * c, :])
        for block in (0, 1):
            rows = slice(block * c, (block + 1) * c)
            scratch.f_up[k, rows, 0:c] = high
            scratch.f_up[k, rows, c : 2 * c] = low
        for block in (k, k + 4):
            columns = slice(block * c, (block + 1) * c)
            scratch.b_up[0:c, columns] = high
            scratch.b_up[c : 2 * c, columns] = low
    copied.dec_conv1.wait()
    stack_conv(scratch.dec_conv1, 0, 2 * c, scratch.fd1a, scratch.bd1a)
    stack_conv(scratch.dec_conv1, 1, 2 * c, scratch.fd1b, scratch.bd1b)
    copied.dec_conv2.wait()
    stack_conv(scratch.dec_conv2, 0, c, scratch.fd2, scratch.bd2)
    copied.skip_weight.wait()
    for half in range(2):
        high, low = split(scratch.skip_weight[half * c : (half + 1) * c, :])
        for block in (half, half + 2):
            scratch.f_skip[block * c : (block + 1) * c, 0:c] = high
            scratch.f_skip[block * c : (block + 1) * c, c : 2 * c] = low
        for block in (0, 1):
            columns = slice(block * c, (block + 1) * c)
            scratch.b_skip[half, 0:c, columns] = high
            scratch.b_skip[half, c : 2 * c, columns] = low

    for buffer in (scratch.xe1, scratch.xe2, scratch.xd1a, scratch.xd1b, scratch.xd2, scratch.xg):
        edge = jnp.zeros((width, 6 * c), BF16)
        buffer[0:width, :] = edge
        buffer[cells + width : cells + 2 * width, :] = edge

    lift = scratch.lift
    lift[...] = jnp.zeros(lift.shape, F32)
    lift[0:history, :] = inputs.lift_weight[...]
    lift[history : history + 1, :] = inputs.lift_bias[...]

    block = 2 * width
    column = lax.rem(lax.broadcasted_iota(jnp.int32, (block, c), 0), width)
    at_first, at_last = column == 0, column == width - 1
    zeros8 = jnp.zeros((8, c), F32)
    ones16 = group_ones(c, c // GROUPS)
    ones32 = group_ones(c, 2 * c // GROUPS)
    count16 = float(cells * (c // GROUPS))
    count32 = float(cells * (2 * c // GROUPS))

    def grid_rows(step, carry=0):
        return lax.fori_loop(0, cells // block, step, carry, unroll=True)

    def row_at(h):
        return pl.ds(pl.multiple_of(h * block, block), block)

    def chunk_at(i):
        return pl.ds(pl.multiple_of(i * CHUNK, CHUNK), CHUNK)

    def put_row(target, h, value):
        rows = pl.ds(pl.multiple_of(h * block + width, width), block)
        left = jnp.where(at_first, 0.0, pltpu.roll(value, 1, 0))
        right = jnp.where(at_last, 0.0, pltpu.roll(value, block - 1, 0))
        for b, piece in enumerate((left, value, right)):
            high, low = split(piece)
            target[rows, HIGH_AT[b] * c : (HIGH_AT[b] + 1) * c] = high
            target[rows, LOW_AT[b] * c : (LOW_AT[b] + 1) * c] = low

    def put_turned(target, columns, value, first=0, second=1):
        high, low = split(value.T)
        target[first * c : (first + 1) * c, columns] = high
        target[second * c : (second + 1) * c, columns] = low

    def conv_chunk(pairs, i, dims=NN):
        total = None
        for data, weight in pairs:
            taps = []
            for a in range(3):
                rows = pl.ds(pl.multiple_of(i * CHUNK + a * width, width), CHUNK)
                taps.append(data[rows, :])
            part = dot(jnp.concatenate(taps, axis=1), weight[...], dims)
            total = part if total is None else total + part
        return total

    def norm_of(first, second, ones, count):
        one, two = group_sums(first, second, ones)
        mean = one / count
        return mean, lax.rsqrt(two / count - mean * mean + EPS)

    def activate(source, target, turned, slope, scale, shift):
        def step(h, carry):
            value = source[row_at(h), :] * scale + shift
            below = 0.5 + 0.5 * lax.erf(value * 0.7071067811865476)
            slope[row_at(h), :] = below + value * (
                0.3989422804014327 * jnp.exp(-0.5 * value * value)
            )
            value = value * below
            put_row(target, h, value)
            put_turned(turned, row_at(h), value)
            return carry

        grid_rows(step)

    def conv_norm(pairs, target):
        def step(i, carry):
            value = fold(conv_chunk(pairs, i))
            target[chunk_at(i), :] = value
            return carry[0] + tile_sums(value), carry[1] + tile_sums(value * value)

        return lax.fori_loop(0, cells // CHUNK, step, (zeros8, zeros8))

    def sums_of(source):
        def step(h, carry):
            value = source[row_at(h), :]
            return carry[0] + tile_sums(value), carry[1] + tile_sums(value * value)

        return grid_rows(step, (zeros8, zeros8))

    step_here = jnp.full((1, c), inputs.step_index[row], jnp.int32)

    def condition(table):
        total = jnp.zeros((1, 2 * c), F32)
        chosen = jnp.concatenate([step_here, step_here], axis=1)
        for s in range(table.shape[0]):
            total = total + jnp.where(chosen == s, table[s : s + 1, :], 0.0)
        return total[:, :c], total[:, c:]

    for copy in own[:2]:
        copy.wait()
    for copy in frame_copies:
        copy.wait_recv()
    fields = scratch.fields
    fields[...] = jnp.zeros(fields.shape, F32)
    frame_of = lax.broadcasted_iota(jnp.int32, (history, width), 0) // FIELDS
    keep = (frame_of >= HIST - inputs.counts[row]).astype(F32)
    masks = []
    for source in range(line):
        for k in range(strip):
            columns = slice((source * strip + k) * width, (source * strip + k + 1) * width)
            mask = mask_in[source, k : k + 1, :].astype(F32)
            masks.append(mask)
            fields[0:history, columns] = frames_in[source, :, k, :] * keep * mask
            fields[history : history + 1, columns] = mask
    lifted = scratch.lifted
    lifted[...] = dot(fields[...], lift[...], TN, HIGH)

    enc_scale, enc_shift = condition(inputs.enc_step_table)
    dec_scale, dec_shift = condition(inputs.dec_step_table)

    mean_e1, inv_e1 = norm_of(*sums_of(lifted), ones16, count16)
    gain_e1, bias_e1 = inputs.enc_norm1_gain[...], inputs.enc_norm1_bias[...]
    a_e1 = inv_e1 * gain_e1
    activate(lifted, scratch.xe1, scratch.te1, scratch.slope_e1, a_e1, bias_e1 - mean_e1 * a_e1)
    middle_e = scratch.middle_e
    mean_e2, inv_e2 = norm_of(
        *conv_norm([(scratch.xe1, scratch.fe1)], middle_e), ones16, count16
    )
    gain_e2, bias_e2 = inputs.enc_norm2_gain[...], inputs.enc_norm2_bias[...]
    a_e2 = inv_e2 * gain_e2
    activate(
        middle_e,
        scratch.xe2,
        scratch.te2,
        scratch.slope_e2,
        a_e2 * (1.0 + enc_scale),
        (bias_e2 - mean_e2 * a_e2) * (1.0 + enc_scale) + enc_shift,
    )
    encoded = scratch.encoded
    conv2_bias = inputs.enc_conv2_bias[...]
    joined = scratch.joined

    def encode(i, carry):
        value = fold(conv_chunk([(scratch.xe2, scratch.fe2)], i))
        value = value + conv2_bias + lifted[chunk_at(i), :]
        encoded[chunk_at(i), :] = value
        high, low = split(value)
        joined[chunk_at(i), c : 2 * c] = high
        joined[chunk_at(i), 3 * c : 4 * c] = low
        put_turned(scratch.turned, chunk_at(i), value, 1, 3)
        return carry[0] + tile_sums(value), carry[1] + tile_sums(value * value)

    sums_enc = lax.fori_loop(0, cells // CHUNK, encode, (zeros8, zeros8))

    half_cells, quarter = cells // 2, cells // 4

    def pick(source):
        pieces = []
        for b in range(2):
            value = source[pl.ds(b, half_cells, stride=2), :]
            value = value.reshape(height // 2, 2, width // 2, c)
            pieces.append([value[:, a].reshape(quarter, c) for a in range(2)])
        return [pieces[b][a] for a in range(2) for b in range(2)]

    def place_cells(target, pieces):
        for b in range(2):
            both = [pieces[2 * a + b].reshape(height // 2, 1, width // 2, c) for a in range(2)]
            value = jnp.concatenate(both, axis=1).reshape(half_cells, c)
            target[pl.ds(b, half_cells, stride=2), :] = value

    x_down = scratch.x_down
    for k, piece in enumerate(pick(encoded)):
        high, low = split(piece)
        x_down[:, k * c : (k + 1) * c] = high
        x_down[:, (k + 4) * c : (k + 5) * c] = low
    lowered = fold(dot(x_down[...], scratch.f_down[...])) + inputs.reducer_bias[...]
    x_up = scratch.x_up
    high, low = split(lowered)
    x_up[:, 0:c] = high
    x_up[:, c : 2 * c] = low
    raised = scratch.raised
    up_bias = inputs.up_bias[...]
    place_cells(
        raised, [fold(dot(x_up[...], scratch.f_up[k])) + up_bias for k in range(4)]
    )

    def raise_row(h, carry):
        value = raised[row_at(h), :]
        high, low = split(value)
        joined[row_at(h), 0:c] = high
        joined[row_at(h), 2 * c : 3 * c] = low
        put_turned(scratch.turned, row_at(h), value, 0, 2)
        return carry[0] + tile_sums(value), carry[1] + tile_sums(value * value)

    sums_raised = grid_rows(raise_row, (zeros8, zeros8))

    halves = []
    for half, (source, sums) in enumerate(((raised, sums_raised), (encoded, sums_enc))):
        mean, inv = norm_of(*sums, ones32, count32)
        gain = inputs.dec_norm1_gain[half : half + 1, :]
        bias = inputs.dec_norm1_bias[half : half + 1, :]
        scale = inv * gain
        activate(
            source,
            (scratch.xd1a, scratch.xd1b)[half],
            (scratch.td1a, scratch.td1b)[half],
            (scratch.slope_d1a, scratch.slope_d1b)[half],
            scale,
            bias - mean * scale,
        )
        halves.append((source, mean, inv, gain))
    middle_d = scratch.middle_d
    pairs = [(scratch.xd1a, scratch.fd1a), (scratch.xd1b, scratch.fd1b)]
    mean_d2, inv_d2 = norm_of(*conv_norm(pairs, middle_d), ones16, count16)
    gain_d2, bias_d2 = inputs.dec_norm2_gain[...], inputs.dec_norm2_bias[...]
    a_d2 = inv_d2 * gain_d2
    activate(
        middle_d,
        scratch.xd2,
        scratch.td2,
        scratch.slope_d2,
        a_d2 * (1.0 + dec_scale),
        (bias_d2 - mean_d2 * a_d2) * (1.0 + dec_scale) + dec_shift,
    )
    result = scratch.result
    last_bias = inputs.dec_conv2_bias[...] + inputs.skip_bias[...]

    def decode(i, carry):
        value = conv_chunk([(scratch.xd2, scratch.fd2)], i)
        value = value + dot(joined[chunk_at(i), :], scratch.f_skip[...])
        result[chunk_at(i), :] = fold(value) + last_bias
        return carry

    lax.fori_loop(0, cells // CHUNK, decode, 0)
    own_output = pltpu.make_async_copy(
        result.at[here_rows], outputs.output.at[row], local_sem.at[10]
    )
    own_output.start()
    for k in range(1, line):
        to = lax.rem(row + k, line)
        there = pl.ds(pl.multiple_of(to * strip_cells, strip_cells), strip_cells)
        output_copies.append(
            send(result.at[there], outputs.output.at[row], device_at(to))
        )

    exchanges = []
    waiting_runs = list(runs)
    landing_at = 0
    sem_at = 4 * (line - 1) + 2 * (line - 1)
    sums, final = scratch.sums, scratch.final

    kinds = (HalvingExchange, Exchange, Exchange, Exchange, Exchange, Exchange, Exchange, SmallExchange)

    def begin():
        nonlocal landing_at, sem_at
        start, rows = waiting_runs.pop(0)
        exchange = kinds[len(exchanges)](place, start, rows, landing_at, sem_at)
        landing_at += rows - rows // (8 * line)
        sem_at += exchange.count()
        exchanges.append(exchange)
        exchange.advance()

    final_copies = []

    def advance(k):
        exchange = exchanges[k]
        exchange.advance()
        if exchange.done():
            rows = pl.ds(exchange.start, exchange.rows)
            copy = pltpu.make_async_copy(
                final.at[rows], outputs.gradients.at[rows], local_sem.at[11 + k]
            )
            copy.start()
            final_copies.append(copy)

    due = list(DUE)

    def point():
        for k in due.pop(0):
            advance(k)

    def small_row(k, value):
        sums[small_at + k : small_at + k + 1, :] = value

    def spread_grad(source):
        def step(h, carry):
            value = source[row_at(h), :]
            put_row(scratch.xg, h, value)
            return carry + tile_sums(value)

        return grid_rows(step, zeros8)

    def weight_grad(turned, at, depth, a):
        rows = pl.ds((2 - a) * width, cells)
        part = fold_rows(dot(turned[...], scratch.xg[rows, :]))
        for b in range(3):
            high, low = HIGH_AT[2 - b] * c, LOW_AT[2 - b] * c
            to = at + (3 * a + b) * depth
            sums[to : to + c, :] = part[:, high : high + c] + part[:, low : low + c]

    def back_conv(weight, slope, target, source, mean, inv):
        carry = (zeros8, zeros8)
        for i in range(cells // CHUNK):
            value = fold(conv_chunk([(scratch.xg, weight)], i, NT)) * slope[chunk_at(i), :]
            target[chunk_at(i), :] = value
            normed = (source[chunk_at(i), :] - mean) * inv
            carry = (carry[0] + tile_sums(value), carry[1] + tile_sums(value * normed))
            if i % (cells // CHUNK // 2) == cells // CHUNK // 2 - 1:
                point()
        return carry

    def norm_grad(sums_in, scale, ones, count):
        one, two = group_sums(sums_in[0] * scale, sums_in[1] * scale, ones)
        return one / count, two / count

    own[2].wait()
    for copy in cot_copies:
        copy.wait_recv()
    total_cot = column_sum(spread_grad(cot))
    for a in range(3):
        weight_grad(scratch.td2, starts.dec_conv2, c, a)
    part = fold(dot(scratch.turned[...], scratch.xg[width : cells + width, 2 * c : 4 * c]))
    sums[starts.skip_weight : starts.skip_weight + 2 * c, :] = fold_rows(part)
    small_row(3, total_cot)
    begin()

    grad = scratch.grad
    sums_d2 = back_conv(scratch.bd2, scratch.slope_d2, grad, middle_d, mean_d2, inv_d2)
    side_grads = (scratch.grad_a, scratch.grad_b)
    for half in range(2):

        def skip_back(i, carry, half=half):
            rows = pl.ds(pl.multiple_of(i * CHUNK + width, width), CHUNK)
            value = dot(scratch.xg[rows, 2 * c : 4 * c], scratch.b_skip[half], NT)
            side_grads[half][chunk_at(i), :] = fold(value)
            return carry

        lax.fori_loop(0, cells // CHUNK, skip_back, 0)
    point()

    def table_rows(k, sums_in, gain, bias, one_plus):
        plain, times = column_sum(sums_in[0]), column_sum(sums_in[1])
        for s in range(inputs.enc_step_table.shape[0]):
            small_row(k + 2 * s, jnp.where(step_here == s, gain * times + bias * plain, 0.0))
            small_row(k + 2 * s + 1, jnp.where(step_here == s, plain, 0.0))
        return one_plus * times, one_plus * plain

    def middle_grad(source, mean, inv, scale, sums_in):
        zero, slope = norm_grad(sums_in, scale, ones16, count16)

        def step(h, carry):
            normed = (source[row_at(h), :] - mean) * inv
            value = inv * (grad[row_at(h), :] * scale - zero - normed * slope)
            put_row(scratch.xg, h, value)
            return carry

        grid_rows(step)

    gain_row, bias_row = table_rows(16, sums_d2, gain_d2, bias_d2, 1.0 + dec_scale)
    small_row(8, gain_row)
    small_row(9, bias_row)
    middle_grad(middle_d, mean_d2, inv_d2, gain_d2 * (1.0 + dec_scale), sums_d2)
    point()
    for a in range(3):
        weight_grad(scratch.td1a, starts.dec_conv1, 2 * c, a)
        weight_grad(scratch.td1b, starts.dec_conv1 + c, 2 * c, a)
        point()
        begin()

    for half, (source, mean, inv, gain) in enumerate(halves):
        sums_in = back_conv(
            (scratch.bd1a, scratch.bd1b)[half],
            (scratch.slope_d1a, scratch.slope_d1b)[half],
            grad,
            source,
            mean,
            inv,
        )
        small_row(4 + half, column_sum(sums_in[1]))
        small_row(6 + half, column_sum(sums_in[0]))
        zero, slope = norm_grad(sums_in, gain, ones32, count32)
        target = side_grads[half]

        def input_grad(h, carry):
            normed = (source[row_at(h), :] - mean) * inv
            value = inv * (grad[row_at(h), :] * gain - zero - normed * slope)
            value = target[row_at(h), :] + value
            target[row_at(h), :] = value
            return carry + tile_sums(value)

        total = grid_rows(input_grad, zeros8)
        if half == 0:
            small_row(2, column_sum(total))
        point()

    grad_raised, grad_encoded = side_grads
    x_grad_up = scratch.x_grad_up
    for k, piece in enumerate(pick(grad_raised)):
        high, low = split(piece)
        x_grad_up[:, k * c : (k + 1) * c] = high
        x_grad_up[:, (k + 4) * c : (k + 5) * c] = low
    grad_lowered = fold(dot(x_grad_up[...], scratch.b_up[...], NT))
    small_row(1, jnp.sum(grad_lowered, axis=0, keepdims=True))
    x_grad_low = scratch.x_grad_low
    high, low = split(grad_lowered)
    x_grad_low[:, 0:c] = high
    x_grad_low[:, c : 2 * c] = low
    point()
    part = fold(fold_rows(dot(x_up[...], x_grad_up[...], TN)))
    for k in range(4):
        at = starts.up_weight + k * c
        sums[at : at + c, :] = part[:, k * c : (k + 1) * c]
    part = fold_rows(fold(dot(x_down[...], x_grad_low[...], TN)))
    sums[starts.reducer_weight : starts.reducer_weight + 4 * c, :] = part
    point()
    begin()
    place_cells(
        grad, [fold(dot(x_grad_low[...], scratch.b_down[k], NT)) for k in range(4)]
    )

    def join_row(h, carry):
        value = grad_encoded[row_at(h), :] + grad[row_at(h), :]
        grad_encoded[row_at(h), :] = value
        put_row(scratch.xg, h, value)
        return carry + tile_sums(value)

    small_row(0, column_sum(grid_rows(join_row, zeros8)))
    for k in range(10, 16):
        small_row(k, jnp.zeros((1, c), F32))
    sums[small_at + 24 : small_at + LATE, :] = jnp.zeros((LATE - 24, c), F32)
    point()
    for a in range(3):
        weight_grad(scratch.te2, starts.enc_conv2, c, a)
        point()
    begin()
    sums_e2 = back_conv(scratch.be2, scratch.slope_e2, grad, middle_e, mean_e2, inv_e2)
    gain_row, bias_row = table_rows(LATE + 24, sums_e2, gain_e2, bias_e2, 1.0 + enc_scale)
    small_row(LATE + 18, gain_row)
    small_row(LATE + 19, bias_row)
    middle_grad(middle_e, mean_e2, inv_e2, gain_e2 * (1.0 + enc_scale), sums_e2)
    point()
    for a in range(3):
        weight_grad(scratch.te1, starts.enc_conv1, c, a)
        point()
    begin()
    sums_e1 = back_conv(scratch.be1, scratch.slope_e1, grad, lifted, mean_e1, inv_e1)
    small_row(LATE + 16, column_sum(sums_e1[1]))
    small_row(LATE + 17, column_sum(sums_e1[0]))
    zero, slope = norm_grad(sums_e1, gain_e1, ones16, count16)

    def lifted_grad(h, carry):
        normed = (lifted[row_at(h), :] - mean_e1) * inv_e1
        value = inv_e1 * (grad[row_at(h), :] * gain_e1 - zero - normed * slope)
        grad[row_at(h), :] = grad_encoded[row_at(h), :] + value
        return carry

    grid_rows(lifted_grad)
    point()

    late_at = small_at + LATE
    sums[late_at : late_at + 16, :] = dot(fields[...], grad[...], NN, HIGH)
    sums[late_at + 20 : late_at + 24, :] = jnp.zeros((4, c), F32)
    point()
    begin()
    back = dot(lift[...], grad[...], NT, HIGH)
    frames_out = scratch.frames_out
    for source in range(line):
        for k in range(strip):
            h = source * strip + k
            value = back[0:history, h * width : (h + 1) * width]
            frames_out[source, :, k, :] = value * keep * masks[h]
    own_frames = pltpu.make_async_copy(
        frames_out.at[row], outputs.frames_grad.at[row], local_sem.at[19]
    )
    own_frames.start()
    for k in range(1, line):
        to = lax.rem(row + k, line)
        output_copies.append(
            send(frames_out.at[to], outputs.frames_grad.at[row], device_at(to))
        )

    for k in REST:
        advance(k)
    assert not due and all(exchange.done() for exchange in exchanges)

    for copy in output_copies:
        copy.wait_recv()
    own_output.wait()
    own_frames.wait()
    for copy in final_copies:
        copy.wait()
    for copy in frame_copies + cot_copies + output_copies:
        copy.wait_send()
    for exchange in exchanges:
        for copy in exchange.copies:
            copy.wait_send()


def write_kernel(layout, *refs):
    shapes, starts, small_at = layout
    output, frames_grad, gradients = refs[:3]
    outputs = refs[3:-4]
    output_here, frames_here, gradients_here, sem = refs[-4:]
    c = gradients.shape[1]
    moves = [(frames_grad, frames_here, outputs[1])]
    for k, name in enumerate(LARGE):
        rows = pl.ds(starts[name], shapes[name][0])
        moves.append((gradients.at[rows], gradients_here.at[rows], outputs[2 + k]))
    moves.append((output, output_here, outputs[0]))
    small = pl.ds(small_at, SMALL_COUNT)
    first = pltpu.make_async_copy(gradients.at[small], gradients_here.at[small], sem.at[0])
    first.start()
    arriving, leaving = [], []
    for k, (source, here, _) in enumerate(moves):
        arriving.append(pltpu.make_async_copy(source, here, sem.at[1 + 2 * k]))
        arriving[-1].start()
    first.wait()
    for target, (k, rows) in zip(outputs[2 + len(LARGE) :], SMALL_ROWS.values()):
        at = small_at + k
        if rows == 8:
            for s in range(target.shape[0]):
                target[s : s + 1, 0:c] = gradients_here[at + 2 * s : at + 2 * s + 1, :]
                target[s : s + 1, c : 2 * c] = gradients_here[at + 2 * s + 1 : at + 2 * s + 2, :]
        else:
            target[...] = gradients_here[at : at + rows, :]
    for k, (_, here, target) in enumerate(moves):
        arriving[k].wait()
        leaving.append(pltpu.make_async_copy(here, target, sem.at[2 + 2 * k]))
        leaving[-1].start()
    for copy in leaving:
        copy.wait()


def whole_items(shape, *arguments):
    line = shape["rows"]
    whole = Given(*arguments)
    given = whole._asdict()
    frames, cotangent = whole.frames, whole.cotangent
    items, history, strip, width = frames.shape
    c = cotangent.shape[-1]
    cells = strip * line * width
    flat = {}
    for name, value in given.items():
        if value is cotangent:
            value = value.reshape(items, strip * width, c)
        elif name in LARGE:
            value = value.reshape(-1, c)
        elif value.ndim == 1 and name not in IN_SMEM:
            value = value.reshape(-1, c)
        flat[name] = value
    shapes = {name: flat[name].shape for name in LARGE}
    big_layout = layout_of(shapes)
    starts, small_at, total_rows, runs = big_layout
    copies = 7 * (line - 1) + len(runs) * (6 + 2 * PIECES + 2 * (line - 1)) + 6
    landing = sum(rows - rows // (8 * line) for _, rows in runs) + LATE_COUNT * (8 + line)
    shifted = pltpu.VMEM((cells + 2 * width, 6 * c), BF16)
    forward = pltpu.VMEM((18 * c, 2 * c), BF16)
    backward = pltpu.VMEM((2 * c, 18 * c), BF16)
    field = pltpu.VMEM((cells, c), F32)
    flipped_field = pltpu.VMEM((2 * c, cells), BF16)
    quarter = cells // 4
    scratch = dict(
        small=pltpu.VMEM((LATE_COUNT, c), F32),
        send=pltpu.SemaphoreType.DMA((copies,)),
        recv=pltpu.SemaphoreType.DMA((copies,)),
        local=pltpu.SemaphoreType.DMA((20,)),
        sums=pltpu.VMEM((total_rows, c), F32),
        final=pltpu.VMEM((total_rows, c), F32),
        landing=pltpu.VMEM((landing, c), F32),
        frames_in=pltpu.VMEM((line, history, strip, width), F32),
        mask_in=pltpu.VMEM((line, strip, width), jnp.int32),
        frames_out=pltpu.VMEM((line, history, strip, width), F32),
        fields=pltpu.VMEM((16, cells), F32),
        lift=pltpu.VMEM((16, c), F32),
        joined=pltpu.VMEM((cells, 4 * c), BF16),
        x_down=pltpu.VMEM((quarter, 8 * c), BF16),
        x_grad_up=pltpu.VMEM((quarter, 8 * c), BF16),
        x_up=pltpu.VMEM((quarter, 2 * c), BF16),
        x_grad_low=pltpu.VMEM((quarter, 2 * c), BF16),
        f_down=pltpu.VMEM((8 * c, 2 * c), BF16),
        b_down=pltpu.VMEM((4, 2 * c, 2 * c), BF16),
        f_up=pltpu.VMEM((4, 2 * c, 2 * c), BF16),
        b_up=pltpu.VMEM((2 * c, 8 * c), BF16),
        f_skip=pltpu.VMEM((4 * c, 2 * c), BF16),
        b_skip=pltpu.VMEM((2, 2 * c, 2 * c), BF16),
        xe1=shifted,
        xe2=shifted,
        xd1a=shifted,
        xd1b=shifted,
        xd2=shifted,
        xg=shifted,
        te1=flipped_field,
        te2=flipped_field,
        td1a=flipped_field,
        td1b=flipped_field,
        td2=flipped_field,
        turned=pltpu.VMEM((4 * c, cells), BF16),
        fe1=forward,
        fe2=forward,
        fd1a=forward,
        fd1b=forward,
        fd2=forward,
        be1=backward,
        be2=backward,
        bd1a=backward,
        bd1b=backward,
        bd2=backward,
        slope_e1=field,
        slope_e2=field,
        slope_d1a=field,
        slope_d1b=field,
        slope_d2=field,
        lifted=field,
        middle_e=field,
        encoded=field,
        raised=field,
        middle_d=field,
        result=field,
        cot=field,
        grad=field,
        grad_a=field,
        grad_b=field,
    )
    scratch.update({name: pltpu.VMEM(shapes[name], F32) for name in LARGE})

    in_hbm = pl.BlockSpec(memory_space=pl.ANY)
    in_vmem = pl.BlockSpec(memory_space=pltpu.VMEM)
    in_smem = pl.BlockSpec(memory_space=pltpu.SMEM)
    in_specs = [
        in_hbm if name in IN_HBM else in_smem if name in IN_SMEM else in_vmem
        for name in ARGUMENTS
    ]
    out_shape = [
        jax.ShapeDtypeStruct((items, strip * width, c), F32),
        jax.ShapeDtypeStruct(frames.shape, F32),
        jax.ShapeDtypeStruct((total_rows, c), F32),
    ]
    out_specs = [in_hbm] * 3
    results = pl.pallas_call(
        functools.partial(
            item_kernel,
            (line, strip, width, shapes, big_layout),
            tuple(scratch),
        ),
        out_shape=out_shape,
        in_specs=in_specs,
        out_specs=out_specs,
        scratch_shapes=list(scratch.values()),
        compiler_params=pltpu.CompilerParams(
            collective_id=0, has_side_effects=True, vmem_limit_bytes=62 * 1024 * 1024
        ),
    )(*[flat[name] for name in ARGUMENTS])
    names = LARGE + tuple(SMALL_ROWS)
    written = pl.pallas_call(
        functools.partial(write_kernel, (shapes, starts, small_at)),
        out_shape=out_shape[:2] + [jax.ShapeDtypeStruct(flat[name].shape, F32) for name in names],
        in_specs=[pl.BlockSpec(memory_space=pltpu.HBM)] * 3,
        out_specs=[in_hbm] * (2 + len(LARGE)) + [in_vmem] * len(SMALL_ROWS),
        scratch_shapes=[
            pltpu.VMEM((items, strip * width, c), F32),
            pltpu.VMEM(frames.shape, F32),
            pltpu.VMEM((total_rows, c), F32),
            pltpu.SemaphoreType.DMA((1 + 2 * (2 + len(LARGE)),)),
        ],
        compiler_params=pltpu.CompilerParams(vmem_limit_bytes=60 * 1024 * 1024),
    )(*results)
    grads = dict(zip(names, written[2:]))
    ordered = [name for name in ARGUMENTS if name in grads]
    return (written[0].reshape(cotangent.shape), written[1]) + tuple(
        grads[name].reshape(given[name].shape) for name in ordered
    )


def body(shape, *arguments):
    items, _, strip, width = arguments[0].shape
    line = shape["rows"]
    whole = (
        shape["section"] == 2
        and shape["batch"] == 4
        and items == line
        and arguments[-1].shape[-1] == 128
        and (strip * line * width) % CHUNK == 0
    )
    return whole_items(shape, *arguments) if whole else strips_body(*arguments)


def solution(mesh):
    in_specs = (
        P(("section", "batch"), None, "rows", None),
        P(("section", "batch")),
        P(("section", "batch"), "rows", None),
        P(("section", "batch")),
        P(),
        P(),
        P(),
        P(),
        P(),
        P(),
        P(),
        P(),
        P(),
        P(),
        P(),
        P(),
        P(),
        P(),
        P(),
        P(),
        P(),
        P(),
        P(),
        P(),
        P(),
        P(),
        P(),
        P(),
        P(("section", "batch"), "rows", None, None),
    )
    out_specs = (
        P(("section", "batch"), "rows", None, None),
        P(("section", "batch"), None, "rows", None),
        P(),
        P(),
        P(),
        P(),
        P(),
        P(),
        P(),
        P(),
        P(),
        P(),
        P(),
        P(),
        P(),
        P(),
        P(),
        P(),
        P(),
        P(),
        P(),
        P(),
        P(),
        P(),
        P(),
        P(),
    )
    return jax.shard_map(functools.partial(body, mesh.shape), mesh=mesh, in_specs=in_specs, out_specs=out_specs, check_vma=False)
```

```python
import functools
from types import SimpleNamespace
from typing import Any, NamedTuple

import jax
import jax.numpy as jnp
from jax import lax
from jax.experimental import pallas as pl
from jax.experimental.pallas import tpu as pltpu
from jax.sharding import PartitionSpec as P

GROUPS = 8
FIELDS = 3
HIST = 4


EPS = 1e-05
HIGH = lax.Precision.HIGHEST


def extended(cells, sides, width):
    for axis, dim in sides:
        count = lax.axis_size(axis)
        ends = count - 1
        head = lax.slice_in_dim(cells, 0, width, axis=dim)
        tail = lax.slice_in_dim(cells, cells.shape[dim] - width, cells.shape[dim], axis=dim)
        cells = jnp.concatenate(
            [
                lax.ppermute(tail, axis, [(i, (i + 1) % count) for i in range(ends)]),
                cells,
                lax.ppermute(head, axis, [((i + 1) % count, i) for i in range(ends)]),
            ],
            axis=dim,
        )
    return cells


def from_behind(value, axis, steps):
    count = lax.axis_size(axis)
    pairs = [(source, (source + steps) % count) for source in range(count)]
    return lax.ppermute(value, axis, pairs)


def group_view(value_arrays):
    extent = value_arrays.shape
    return value_arrays.reshape(extent[:-1] + (GROUPS, extent[-1] // GROUPS))


def global_sums(value_arrays):
    grouped = group_view(value_arrays)
    flat = grouped.reshape(-1, GROUPS, grouped.shape[-1])
    first_sum = jnp.sum(flat, axis=(0, 2))
    second_sum = jnp.sum(flat * flat, axis=(0, 2))
    return lax.psum((first_sum, second_sum), "rows")


def apply_norm(value_arrays, sum_one, sum_two, norm_gain, norm_bias, total):
    grouped = group_view(value_arrays)
    group_mean = sum_one / total
    variance = sum_two / total - group_mean * group_mean
    inverse = lax.rsqrt(variance + EPS)
    normed = (grouped - group_mean[:, None]) * inverse[:, None]
    return normed.reshape(value_arrays.shape) * norm_gain + norm_bias


def norm_back(value_arrays, grad_one, grad_two):
    grouped = group_view(value_arrays)
    extra = grad_one[:, None] + 2.0 * grouped * grad_two[:, None]
    return extra.reshape(value_arrays.shape)


def reduce_grads(grad_one, grad_two):
    return lax.psum((grad_one, grad_two), "rows")


def conv_rows(padded, kernel):
    widened = jnp.pad(padded, ((0, 0), (1, 1), (0, 0)))
    return lax.conv_general_dilated(
        widened[None],
        kernel,
        (1, 1),
        "VALID",
        dimension_numbers=("NHWC", "HWIO", "NHWC"),
        precision=HIGH,
    )[0]


def flipped(kernel):
    return jnp.transpose(kernel[::-1, ::-1], (0, 1, 3, 2))


def pad_grads(value_arrays):
    return extended(value_arrays, (("rows", 0),), 1)


def totals_of(inputs, conv1):
    strip = inputs.shape[0]
    cells = strip * lax.axis_size("rows") * inputs.shape[1]
    return (cells * (inputs.shape[2] // GROUPS), cells * (conv1.shape[3] // GROUPS))


def block_forward(inputs, weights, scale_part, shift_part):
    norm1_gain, norm1_bias, conv1, norm2_gain, norm2_bias, conv2, conv2_bias = weights
    total_in, total_mid = totals_of(inputs, conv1)
    sums_in = global_sums(inputs)

    def pad_rows(value_arrays):
        return extended(value_arrays, (("rows", 0),), 1)

    act_one = pad_rows(
        jax.nn.gelu(
            apply_norm(inputs, sums_in[0], sums_in[1], norm1_gain, norm1_bias, total_in),
            approximate=False,
        )
    )
    middle = conv_rows(act_one, conv1)
    sums_mid = global_sums(middle)
    shaped = (
        apply_norm(middle, sums_mid[0], sums_mid[1], norm2_gain, norm2_bias, total_mid)
        * (1.0 + scale_part)
        + shift_part
    )
    act_two = pad_rows(jax.nn.gelu(shaped, approximate=False))
    branch = conv_rows(act_two, conv2) + conv2_bias
    return (branch, (sums_in[0], sums_in[1], act_one, middle, sums_mid[0], sums_mid[1], act_two))


def block_backward(inputs, weights, scale_part, shift_part, kept, grad_out):
    norm1_gain, norm1_bias, conv1, norm2_gain, norm2_bias, conv2, conv2_bias = weights
    in_one, in_two, act_one, middle, mid_one, mid_two, act_two = kept
    total_in, total_mid = totals_of(inputs, conv1)
    grad_conv2 = jax.vjp(lambda kernel: conv_rows(act_two, kernel), conv2)[1](grad_out)[0]
    grad_bias2 = jnp.sum(grad_out, axis=(0, 1))
    grad_act_two = conv_rows(pad_grads(grad_out), flipped(conv2))

    def second_piece(middle_in, sum_one, sum_two, gain_in, incoming_bias, scale_in, shift_in):
        shaped = (
            apply_norm(middle_in, sum_one, sum_two, gain_in, incoming_bias, total_mid)
            * (1.0 + scale_in)
            + shift_in
        )
        return jax.nn.gelu(shaped, approximate=False)

    second_pull = jax.vjp(
        second_piece, middle, mid_one, mid_two, norm2_gain, norm2_bias, scale_part, shift_part
    )[1](grad_act_two)
    summed_one, summed_two = reduce_grads(second_pull[1], second_pull[2])
    grad_middle = second_pull[0] + norm_back(middle, summed_one, summed_two)
    grad_conv1 = jax.vjp(lambda kernel: conv_rows(act_one, kernel), conv1)[1](grad_middle)[0]
    grad_act_one = conv_rows(pad_grads(grad_middle), flipped(conv1))

    def first_piece(inputs_in, sum_one, sum_two, gain_in, incoming_bias):
        return jax.nn.gelu(
            apply_norm(inputs_in, sum_one, sum_two, gain_in, incoming_bias, total_in),
            approximate=False,
        )

    first_pull = jax.vjp(first_piece, inputs, in_one, in_two, norm1_gain, norm1_bias)[1](
        grad_act_one
    )
    first_one, first_two = reduce_grads(first_pull[1], first_pull[2])
    grad_inputs = first_pull[0] + norm_back(inputs, first_one, first_two)
    grads = (
        first_pull[3],
        first_pull[4],
        grad_conv1,
        second_pull[3],
        second_pull[4],
        grad_conv2,
        grad_bias2,
    )
    return (grad_inputs, grads, second_pull[5], second_pull[6])


def conditioning(step_item, table):
    one_hot = (jnp.arange(table.shape[0], dtype=jnp.int32) == step_item).astype(jnp.float32)
    condition = jnp.dot(one_hot, table, precision=HIGH)
    half_width = table.shape[1] // 2
    return (condition[:half_width], condition[half_width:], one_hot)


def project_in(frames_item, mask_item, count_item, incoming_weight, incoming_bias):
    history = jnp.arange(HIST, dtype=jnp.int32) >= HIST - count_item
    keep = jnp.repeat(history, FIELDS).astype(jnp.float32)
    lifted = (
        jnp.einsum(
            "fhw,fc->hwc", frames_item * keep[:, None, None], incoming_weight, precision=HIGH
        )
        + incoming_bias
    )
    return lifted * mask_item[:, :, None].astype(jnp.float32)


def coarsen_field(value_arrays, incoming_weight, incoming_bias):
    rows_here, width_here, depth_here = value_arrays.shape
    blocks = value_arrays.reshape(rows_here // 2, 2, width_here // 2, 2, depth_here)
    return jnp.einsum("iajbk,abkc->ijc", blocks, incoming_weight, precision=HIGH) + incoming_bias


def upsample(value_arrays, incoming_weight, incoming_bias):
    result = jnp.einsum("ijk,abkc->iajbc", value_arrays, incoming_weight, precision=HIGH)
    extent = result.shape
    return result.reshape(extent[0] * 2, extent[2] * 2, extent[4]) + incoming_bias


def flatten_all(pieces):
    return jnp.concatenate([piece.reshape(-1) for piece in pieces])


def unflatten_all(flat, templates):
    pieces = []
    offset_at = 0
    for template in templates:
        count_here = template.size
        pieces.append(flat[offset_at : offset_at + count_here].reshape(template.shape))
        offset_at += count_here
    return tuple(pieces)


def strips_body(
    frames,
    counts,
    cell_mask,
    step_index,
    lift_weight,
    lift_bias,
    enc_norm1_gain,
    enc_norm1_bias,
    enc_conv1,
    enc_step_table,
    enc_norm2_gain,
    enc_norm2_bias,
    enc_conv2,
    enc_conv2_bias,
    reducer_weight,
    reducer_bias,
    up_weight,
    up_bias,
    dec_norm1_gain,
    dec_norm1_bias,
    dec_conv1,
    dec_step_table,
    dec_norm2_gain,
    dec_norm2_bias,
    dec_conv2,
    dec_conv2_bias,
    skip_weight,
    skip_bias,
    cotangent,
):
    enc_weights = (
        enc_norm1_gain,
        enc_norm1_bias,
        enc_conv1,
        enc_norm2_gain,
        enc_norm2_bias,
        enc_conv2,
        enc_conv2_bias,
    )
    dec_weights = (
        dec_norm1_gain,
        dec_norm1_bias,
        dec_conv1,
        dec_norm2_gain,
        dec_norm2_bias,
        dec_conv2,
        dec_conv2_bias,
    )
    params = (
        lift_weight,
        lift_bias,
        enc_norm1_gain,
        enc_norm1_bias,
        enc_conv1,
        enc_step_table,
        enc_norm2_gain,
        enc_norm2_bias,
        enc_conv2,
        enc_conv2_bias,
        reducer_weight,
        reducer_bias,
        up_weight,
        up_bias,
        dec_norm1_gain,
        dec_norm1_bias,
        dec_conv1,
        dec_step_table,
        dec_norm2_gain,
        dec_norm2_bias,
        dec_conv2,
        dec_conv2_bias,
        skip_weight,
        skip_bias,
    )

    def forward_micro(carry, sliced):
        frames_item, mask_item, count_item, step_item = sliced
        lifted = project_in(frames_item, mask_item, count_item, lift_weight, lift_bias)
        enc_scale, enc_shift, unused_hot = conditioning(step_item, enc_step_table)
        enc_branch, enc_kept = block_forward(lifted, enc_weights, enc_scale, enc_shift)
        encoder_result = lifted + enc_branch
        coarse_field = coarsen_field(encoder_result, reducer_weight, reducer_bias)
        foreign = from_behind(coarse_field, "section", 1)
        raised_foreign = upsample(foreign, up_weight, up_bias)
        raised = from_behind(raised_foreign, "section", 1)
        joined = jnp.concatenate([raised, encoder_result], axis=-1)
        dec_scale, dec_shift, unused_again = conditioning(step_item, dec_step_table)
        dec_branch, dec_kept = block_forward(joined, dec_weights, dec_scale, dec_shift)
        output_item = jnp.dot(joined, skip_weight, precision=HIGH) + skip_bias + dec_branch
        return (carry, (output_item, (lifted, enc_kept, encoder_result, foreign, joined, dec_kept)))

    unused, (output, kept_all) = lax.scan(
        forward_micro, jnp.zeros((), jnp.float32), (frames, cell_mask, counts, step_index)
    )

    def backward_micro(totals, sliced):
        frames_item, mask_item, count_item, step_item, grad_out, kept = sliced
        lifted, enc_kept, encoder_result, foreign, joined, dec_kept = kept
        dec_scale, dec_shift, one_hot = conditioning(step_item, dec_step_table)
        grad_joined, dec_grads, dec_gscale, dec_gshift = block_backward(
            joined, dec_weights, dec_scale, dec_shift, dec_kept, grad_out
        )
        grad_skip_weight = jnp.einsum("hwk,hwc->kc", joined, grad_out, precision=HIGH)
        grad_skip_bias = jnp.sum(grad_out, axis=(0, 1))
        grad_joined = grad_joined + jnp.dot(grad_out, skip_weight.T, precision=HIGH)
        half_width = joined.shape[-1] // 2
        grad_raised = grad_joined[..., :half_width]
        grad_encoded = grad_joined[..., half_width:]
        grad_foreign_up = from_behind(grad_raised, "section", 1)
        up_pull = jax.vjp(upsample, foreign, up_weight, up_bias)[1](grad_foreign_up)
        coarse_gradient = from_behind(up_pull[0], "section", 1)
        reducer_pullback = jax.vjp(coarsen_field, encoder_result, reducer_weight, reducer_bias)[1](
            coarse_gradient
        )
        grad_encoded = grad_encoded + reducer_pullback[0]
        enc_scale, enc_shift, enc_hot = conditioning(step_item, enc_step_table)
        grad_lifted, enc_grads, enc_gscale, enc_gshift = block_backward(
            lifted, enc_weights, enc_scale, enc_shift, enc_kept, grad_encoded
        )
        grad_lifted = grad_lifted + grad_encoded
        proj_pull = jax.vjp(
            lambda frames_in, incoming_weight, incoming_bias: project_in(
                frames_in, mask_item, count_item, incoming_weight, incoming_bias
            ),
            frames_item,
            lift_weight,
            lift_bias,
        )[1](grad_lifted)
        enc_table_grad = enc_hot[:, None] * jnp.concatenate([enc_gscale, enc_gshift])[None, :]
        dec_table_grad = one_hot[:, None] * jnp.concatenate([dec_gscale, dec_gshift])[None, :]
        micro_list = (
            proj_pull[1],
            proj_pull[2],
            enc_grads[0],
            enc_grads[1],
            enc_grads[2],
            enc_table_grad,
            enc_grads[3],
            enc_grads[4],
            enc_grads[5],
            enc_grads[6],
            reducer_pullback[1],
            reducer_pullback[2],
            up_pull[1],
            up_pull[2],
            dec_grads[0],
            dec_grads[1],
            dec_grads[2],
            dec_table_grad,
            dec_grads[3],
            dec_grads[4],
            dec_grads[5],
            dec_grads[6],
            grad_skip_weight,
            grad_skip_bias,
        )
        micro_flat = flatten_all(micro_list)
        return (totals + micro_flat, proj_pull[0])

    total_size = sum((piece.size for piece in params))
    start_totals = jnp.zeros((total_size,), jnp.float32)
    flat_totals, frames_grad = lax.scan(
        backward_micro,
        start_totals,
        (frames, cell_mask, counts, step_index, cotangent, kept_all),
        reverse=True,
    )
    flat_totals = lax.psum(flat_totals, ("section", "batch", "rows"))
    grads = unflatten_all(flat_totals, params)
    return (output, frames_grad) + grads


F32 = jnp.float32
BF16 = jnp.bfloat16
MESH = pl.DeviceIdType.MESH
NN = ((1,), (0,))
NT = ((1,), (1,))
TN = ((0,), (0,))
CHUNK = 256
class Given(NamedTuple):
    frames: Any
    counts: Any
    cell_mask: Any
    step_index: Any
    lift_weight: Any
    lift_bias: Any
    enc_norm1_gain: Any
    enc_norm1_bias: Any
    enc_conv1: Any
    enc_step_table: Any
    enc_norm2_gain: Any
    enc_norm2_bias: Any
    enc_conv2: Any
    enc_conv2_bias: Any
    reducer_weight: Any
    reducer_bias: Any
    up_weight: Any
    up_bias: Any
    dec_norm1_gain: Any
    dec_norm1_bias: Any
    dec_conv1: Any
    dec_step_table: Any
    dec_norm2_gain: Any
    dec_norm2_bias: Any
    dec_conv2: Any
    dec_conv2_bias: Any
    skip_weight: Any
    skip_bias: Any
    cotangent: Any


ARGUMENTS = Given._fields
LARGE = tuple(
    dict(
        dec_conv1=0,
        up_weight=0,
        reducer_weight=0,
        dec_conv2=0,
        skip_weight=0,
        enc_conv1=0,
        enc_conv2=0,
    )
)
IN_HBM = tuple(dict(frames=0, cell_mask=0, cotangent=0)) + LARGE
IN_SMEM = tuple(dict(counts=0, step_index=0))
LATE = 128
SMALL_ROWS = dict(
    enc_conv2_bias=(0, 1),
    reducer_bias=(1, 1),
    up_bias=(2, 1),
    dec_conv2_bias=(3, 1),
    skip_bias=(3, 1),
    dec_norm1_gain=(4, 2),
    dec_norm1_bias=(6, 2),
    dec_norm2_gain=(8, 1),
    dec_norm2_bias=(9, 1),
    dec_step_table=(16, 8),
    lift_weight=(LATE, 12),
    lift_bias=(LATE + 12, 1),
    enc_norm1_gain=(LATE + 16, 1),
    enc_norm1_bias=(LATE + 17, 1),
    enc_norm2_gain=(LATE + 18, 1),
    enc_norm2_bias=(LATE + 19, 1),
    enc_step_table=(LATE + 24, 8),
)
LATE_COUNT = 32
SMALL_COUNT = LATE + LATE_COUNT
DUE = ((), (), (), (0,), (), (), (0, 1), (2,), (), (0, 3), (1,), (), (2, 4), (3,), (0,), (5, 1, 4), (2,), (3,))
REST = (6, 0, 5, 1, 4, 6, 0, 2, 3, 1, 7, 0, 2, 1, 5, 3, 4, 0, 7, 6, 2, 3, 4, 5, 6, 4, 5, 6, 5, 6)
OUTPUTS = tuple(dict(output=0, frames_grad=0, gradients=0))


def split(value):
    high = value.astype(BF16)
    return high, (value - high.astype(F32)).astype(BF16)


def dot(left, right, dims=NN, precision=None):
    return lax.dot_general(
        left, right, (dims, ((), ())), precision=precision, preferred_element_type=F32
    )


def fold(value):
    half = value.shape[1] // 2
    return value[:, :half] + value[:, half:]


def fold_rows(value):
    half = value.shape[0] // 2
    return value[:half] + value[half:]


def tile_sums(value):
    return jnp.sum(value.reshape(-1, 8, value.shape[-1]), axis=0)


def column_sum(tiles):
    return jnp.sum(tiles, axis=0, keepdims=True)


def group_ones(channels, size):
    rows = lax.broadcasted_iota(jnp.int32, (channels, channels), 0) // size
    columns = lax.broadcasted_iota(jnp.int32, (channels, channels), 1) // size
    return (rows == columns).astype(F32)


def group_sums(first, second, ones):
    both = dot(jnp.concatenate([first, second], axis=0), ones, precision=HIGH)
    return column_sum(both[:8]), column_sum(both[8:])


class Exchange:

    def __init__(self, place, start, rows, landing, first_sem):
        self.place, self.start, self.rows, self.landing = place, start, rows, landing
        self.sem = first_sem
        self.stage = 0
        self.copies = []
        self.waiting = []
        self.group = place.plane_group
        self.half = rows // 2
        self.base = start + place.core * self.half
        self._finish(self.half)

    def _finish(self, size):
        self.part = size // self.group.count
        self.own = self.base + self.group.here * self.part
        self.shard = self.part // self.place.line.count
        self.last = self.own + self.place.line.here * self.shard

    def count(self):
        return 2 + 2 * (self.group.count - 1) + 2 * (self.place.line.count - 1)

    def _copy(self, source, target, device):
        place = self.place
        copy = pltpu.make_async_remote_copy(
            src_ref=source,
            dst_ref=target,
            send_sem=place.send.at[self.sem],
            recv_sem=place.recv.at[self.sem],
            device_id=device,
            device_id_type=MESH,
        )
        self.sem += 1
        copy.start()
        self.copies.append(copy)
        self.waiting.append(copy)

    def _wait(self):
        for copy in self.waiting:
            copy.wait_recv()
        self.waiting = []

    def _rows(self, at, size):
        return pl.ds(pl.multiple_of(at, 8), size)

    def _swap(self):
        place = self.place
        other = self._rows(self.start + (1 - place.core) * self.half, self.half)
        self.land = self.landing
        self.landing += self.half
        self._copy(
            place.sums.at[other], place.landing.at[pl.ds(self.land, self.half)], place.partner
        )

    def _add_swap(self):
        place = self.place
        block = 64 if self.half % 64 == 0 else 32

        def step(i, carry):
            here = self._rows(self.base + i * block, block)
            there = self._rows(self.land + i * block, block)
            place.sums[here] = place.sums[here] + place.landing[there]
            return carry

        lax.fori_loop(0, self.half // block, step, 0)

    def _scatter(self, group, base, size):
        place = self.place
        self.land = self.landing
        for k in range(1, group.count):
            to = lax.rem(group.here + k, group.count)
            self._copy(
                place.sums.at[self._rows(base + to * size, size)],
                place.landing.at[pl.ds(self.landing, size)],
                group.device(to),
            )
            self.landing += size

    def _total(self, group, own, size, target):
        place = self.place
        block = 8 if size % 32 else 32

        def step(i, carry):
            here = self._rows(own + i * block, block)
            total = place.sums[here]
            for k in range(group.count - 1):
                there = self._rows(self.land + k * size + i * block, block)
                total = total + place.landing[there]
            target[here] = total
            return carry

        lax.fori_loop(0, size // block, step, 0)

    def _gather(self, group, own, size):
        final = self.place.final
        here = self._rows(own, size)
        for k in range(1, group.count):
            to = lax.rem(group.here + k, group.count)
            self._copy(final.at[here], final.at[here], group.device(to))

    def _steps(self):
        place, group = self.place, self.group
        yield self._swap()
        self._wait()
        self._add_swap()
        yield from self._both()
        final = place.final
        here = self._rows(self.base, self.half)
        self._copy(final.at[here], final.at[here], place.partner)
        yield
        self._wait()
        yield

    def _both(self):
        place, group = self.place, self.group
        line = place.line
        self._scatter(group, self.base, self.part)
        yield
        self._wait()
        self._total(group, self.own, self.part, place.sums)
        self._scatter(line, self.own, self.shard)
        yield
        self._wait()
        self._total(line, self.last, self.shard, place.final)
        self._gather(line, self.last, self.shard)
        yield
        self._wait()
        self._gather(group, self.own, self.part)
        yield
        self._wait()

    def advance(self):
        if self.stage == 0:
            self.steps = self._steps()
        self.stage += 1
        next(self.steps)

    def done(self):
        return self.stage == 7


class HalvingExchange(Exchange):

    def count(self):
        return 6 + 2 * (self.place.line.count - 1)

    def _halve(self, level):
        place = self.place
        self.half = self.rows >> (level + 1)
        bit, device = place.halves[level]
        other = self._rows(self.base + (1 - bit) * self.half, self.half)
        self.base = self.base + bit * self.half
        self.land = self.landing
        self.landing += self.half
        self._copy(
            place.sums.at[other], place.landing.at[pl.ds(self.land, self.half)], device
        )

    def _steps(self):
        place, line, final = self.place, self.place.line, self.place.final
        self.base = self.start
        bases = []
        for level in range(3):
            self._halve(level)
            bases.append(self.base)
            yield
            self._wait()
            self._add_swap()
        shard = self.half // line.count
        last = self.base + line.here * shard
        self._scatter(line, self.base, shard)
        yield
        self._wait()
        self._total(line, last, shard, final)
        self._gather(line, last, shard)
        yield
        for level in (2, 1, 0):
            self._wait()
            here = self._rows(bases[level], self.rows >> (level + 1))
            self._copy(final.at[here], final.at[here], place.halves[level][1])
            yield
        self._wait()
        yield

    def done(self):
        return self.stage == 9


class SmallExchange(Exchange):

    def count(self):
        return self.place.cores_group.count + self.place.line.count - 2

    def _share(self, group, source):
        place = self.place
        self.land = self.landing
        self.landing += group.count * self.rows
        own = self._rows(self.land + group.here * self.rows, self.rows)
        place.landing[own] = source[...]
        for k in range(1, group.count):
            to = lax.rem(group.here + k, group.count)
            self._copy(source, place.landing.at[own], group.device(to))

    def _sum(self, group):
        total = None
        for k in range(group.count):
            part = self.place.landing[pl.ds(self.land + k * self.rows, self.rows)]
            total = part if total is None else total + part
        return total

    def _steps(self):
        place = self.place
        here = pl.ds(self.start, self.rows)
        self._share(place.line, place.sums.at[here])
        yield
        self._wait()
        place.small[...] = self._sum(place.line)
        self._share(place.cores_group, place.small)
        yield
        self._wait()
        place.final[here] = self._sum(place.cores_group)
        yield

    def done(self):
        return self.stage == 3


def layout_of(shapes):
    starts = {}
    at = 0
    for name in LARGE:
        starts[name] = at
        at += shapes[name][0]
    small = at
    begins = SimpleNamespace(**starts)
    late = small + LATE
    part = (begins.up_weight - begins.dec_conv1) // 3
    skip = begins.skip_weight + 128
    conv1, up = begins.dec_conv1, begins.up_weight
    edges = (
        (begins.dec_conv2, skip),
        (conv1, conv1 + part),
        (conv1 + part, conv1 + 2 * part),
        (conv1 + 2 * part, up),
        (up, begins.dec_conv2),
        (begins.enc_conv2, late),
        (skip, begins.enc_conv2),
        (late, late + LATE_COUNT),
    )
    runs = [(first, last - first) for first, last in edges]
    return starts, small, late + LATE_COUNT, runs


def item_kernel(sizes, scratch_names, *refs):
    line, strip, width, shapes, big_layout = sizes
    begins, small_at, total_rows, runs = big_layout
    starts = SimpleNamespace(**begins)
    inputs = Given(*refs[: len(ARGUMENTS)])
    refs = refs[len(ARGUMENTS) :]
    output_names = OUTPUTS
    outputs = SimpleNamespace(**dict(zip(output_names, refs)))
    scratch = SimpleNamespace(**dict(zip(scratch_names, refs[len(output_names) :])))

    def w_of(name):
        return getattr(scratch, name)

    height = strip * line
    cells = height * width
    c = inputs.lift_weight.shape[1]
    strip_cells = strip * width
    history = inputs.frames.shape[1]

    core = lax.axis_index("section")
    plane = lax.axis_index("batch")
    row = lax.axis_index("rows")
    y, x = plane // 2, lax.rem(plane, 2)
    along_x = plane + 1 - 2 * x
    along_y = plane + 2 - 4 * y

    def device_at(to):
        return (core, plane, to)

    place = SimpleNamespace(
        core=core,
        partner=(1 - core, plane, row),
        line=SimpleNamespace(count=line, here=row, device=device_at),
        plane_group=SimpleNamespace(
            count=4, here=plane, device=lambda to: (core, to, row)
        ),
        cores_group=SimpleNamespace(
            count=8,
            here=core * 4 + plane,
            device=lambda to: (to // 4, lax.rem(to, 4), row),
        ),
        halves=(
            (core, (1 - core, plane, row)),
            (x * (1 - core) + y * core, (core, along_x * (1 - core) + along_y * core, row)),
            (y * (1 - core) + x * core, (core, along_y * (1 - core) + along_x * core, row)),
        ),
        small=scratch.small,
        sums=scratch.sums,
        final=scratch.final,
        landing=scratch.landing,
        send=scratch.send,
        recv=scratch.recv,
    )
    local_sem = scratch.local

    weight_copies = {}
    for k, name in enumerate(LARGE):
        copy = pltpu.make_async_copy(getattr(inputs, name), w_of(name), local_sem.at[k])
        weight_copies[name] = copy
        copy.start()
    frames_in, mask_in, cot = scratch.frames_in, scratch.mask_in, scratch.cot
    here_rows = pl.ds(pl.multiple_of(row * strip_cells, strip_cells), strip_cells)
    own = (
        pltpu.make_async_copy(inputs.frames.at[row], frames_in.at[row], local_sem.at[7]),
        pltpu.make_async_copy(inputs.cell_mask.at[row], mask_in.at[row], local_sem.at[8]),
        pltpu.make_async_copy(
            inputs.cotangent.at[row], cot.at[here_rows], local_sem.at[9]
        ),
    )
    for copy in own:
        copy.start()

    barrier = pltpu.get_barrier_semaphore()
    peers = [device_at(lax.rem(row + k, line)) for k in range(1, line)]
    cores_group = place.cores_group
    for k in range(1, 8):
        peers.append(cores_group.device(lax.rem(cores_group.here + k, 8)))
    for device in peers:
        pl.semaphore_signal(barrier, inc=1, device_id=device, device_id_type=MESH)
    pl.semaphore_wait(barrier, len(peers))

    next_sem = 0

    def send(source, target, device):
        nonlocal next_sem
        copy = pltpu.make_async_remote_copy(
            src_ref=source,
            dst_ref=target,
            send_sem=scratch.send.at[next_sem],
            recv_sem=scratch.recv.at[next_sem],
            device_id=device,
            device_id_type=MESH,
        )
        next_sem += 1
        copy.start()
        return copy

    frame_copies, cot_copies, output_copies = [], [], []
    for k in range(1, line):
        to = lax.rem(row + k, line)
        device = device_at(to)
        frame_copies.append(send(inputs.frames.at[to], frames_in.at[row], device))
        frame_copies.append(send(inputs.cell_mask.at[to], mask_in.at[row], device))
    for k in range(1, line):
        to = lax.rem(row + k, line)
        cot_copies.append(
            send(inputs.cotangent.at[to], cot.at[here_rows], device_at(to))
        )

    copied = SimpleNamespace(**weight_copies)
    def stack_conv(source, half, depth, forward, backward):
        def step(t, carry):
            at = pl.multiple_of(t * depth + half * c, c)
            high, low = split(source[pl.ds(at, c), :])
            for k in range(2):
                rows = pl.ds(pl.multiple_of((2 * t + k) * c, c), c)
                forward[rows, 0:c] = high
                forward[rows, c : 2 * c] = low
                columns = pl.ds(pl.multiple_of((16 - 2 * t + k) * c, c), c)
                backward[0:c, columns] = high
                backward[c : 2 * c, columns] = low
            return carry

        lax.fori_loop(0, 9, step, 0)

    copied.enc_conv1.wait()
    stack_conv(scratch.enc_conv1, 0, c, scratch.fe1, scratch.be1)
    copied.enc_conv2.wait()
    stack_conv(scratch.enc_conv2, 0, c, scratch.fe2, scratch.be2)
    copied.reducer_weight.wait()
    for k in range(4):
        high, low = split(scratch.reducer_weight[k * c : (k + 1) * c, :])
        for block in (k, k + 4):
            scratch.f_down[block * c : (block + 1) * c, 0:c] = high
            scratch.f_down[block * c : (block + 1) * c, c : 2 * c] = low
        for block in (0, 1):
            columns = slice(block * c, (block + 1) * c)
            scratch.b_down[k, 0:c, columns] = high
            scratch.b_down[k, c : 2 * c, columns] = low
    copied.up_weight.wait()
    for k in range(4):
        high, low = split(scratch.up_weight[k * c : (k + 1) * c, :])
        for block in (0, 1):
            rows = slice(block * c, (block + 1) * c)
            scratch.f_up[k, rows, 0:c] = high
            scratch.f_up[k, rows, c : 2 * c] = low
        for block in (k, k + 4):
            columns = slice(block * c, (block + 1) * c)
            scratch.b_up[0:c, columns] = high
            scratch.b_up[c : 2 * c, columns] = low
    copied.dec_conv1.wait()
    stack_conv(scratch.dec_conv1, 0, 2 * c, scratch.fd1a, scratch.bd1a)
    stack_conv(scratch.dec_conv1, 1, 2 * c, scratch.fd1b, scratch.bd1b)
    copied.dec_conv2.wait()
    stack_conv(scratch.dec_conv2, 0, c, scratch.fd2, scratch.bd2)
    copied.skip_weight.wait()
    for half in range(2):
        high, low = split(scratch.skip_weight[half * c : (half + 1) * c, :])
        for block in (half, half + 2):
            scratch.f_skip[block * c : (block + 1) * c, 0:c] = high
            scratch.f_skip[block * c : (block + 1) * c, c : 2 * c] = low
        for block in (0, 1):
            columns = slice(block * c, (block + 1) * c)
            scratch.b_skip[half, 0:c, columns] = high
            scratch.b_skip[half, c : 2 * c, columns] = low

    for buffer in (scratch.xe1, scratch.xe2, scratch.xd1a, scratch.xd1b, scratch.xd2, scratch.xg):
        edge = jnp.zeros((width, 6 * c), BF16)
        buffer[0:width, :] = edge
        buffer[cells + width : cells + 2 * width, :] = edge

    lift = scratch.lift
    lift[...] = jnp.zeros(lift.shape, F32)
    lift[0:history, :] = inputs.lift_weight[...]
    lift[history : history + 1, :] = inputs.lift_bias[...]

    block = 2 * width
    column = lax.rem(lax.broadcasted_iota(jnp.int32, (block, c), 0), width)
    at_first, at_last = column == 0, column == width - 1
    zeros8 = jnp.zeros((8, c), F32)
    ones16 = group_ones(c, c // GROUPS)
    ones32 = group_ones(c, 2 * c // GROUPS)
    count16 = float(cells * (c // GROUPS))
    count32 = float(cells * (2 * c // GROUPS))

    def grid_rows(step, carry=0):
        return lax.fori_loop(0, cells // block, step, carry)

    def row_at(h):
        return pl.ds(pl.multiple_of(h * block, block), block)

    def chunk_at(i):
        return pl.ds(pl.multiple_of(i * CHUNK, CHUNK), CHUNK)

    def put_row(target, h, value):
        rows = pl.ds(pl.multiple_of(h * block + width, width), block)
        left = jnp.where(at_first, 0.0, pltpu.roll(value, 1, 0))
        right = jnp.where(at_last, 0.0, pltpu.roll(value, block - 1, 0))
        for b, piece in enumerate((left, value, right)):
            high, low = split(piece)
            target[rows, 2 * b * c : (2 * b + 1) * c] = high
            target[rows, (2 * b + 1) * c : (2 * b + 2) * c] = low

    def put_turned(target, columns, value, first=0, second=1):
        high, low = split(value.T)
        target[first * c : (first + 1) * c, columns] = high
        target[second * c : (second + 1) * c, columns] = low

    def conv_chunk(pairs, i, dims=NN):
        total = None
        for data, weight in pairs:
            taps = []
            for a in range(3):
                rows = pl.ds(pl.multiple_of(i * CHUNK + a * width, width), CHUNK)
                taps.append(data[rows, :])
            part = dot(jnp.concatenate(taps, axis=1), weight[...], dims)
            total = part if total is None else total + part
        return total

    def norm_of(first, second, ones, count):
        one, two = group_sums(first, second, ones)
        mean = one / count
        return mean, lax.rsqrt(two / count - mean * mean + EPS)

    def activate(source, target, turned, slope, scale, shift):
        def step(h, carry):
            value = source[row_at(h), :] * scale + shift
            below = 0.5 + 0.5 * lax.erf(value * 0.7071067811865476)
            slope[row_at(h), :] = below + value * (
                0.3989422804014327 * jnp.exp(-0.5 * value * value)
            )
            value = value * below
            put_row(target, h, value)
            put_turned(turned, row_at(h), value)
            return carry

        grid_rows(step)

    def conv_norm(pairs, target):
        def step(i, carry):
            value = fold(conv_chunk(pairs, i))
            target[chunk_at(i), :] = value
            return carry[0] + tile_sums(value), carry[1] + tile_sums(value * value)

        return lax.fori_loop(0, cells // CHUNK, step, (zeros8, zeros8))

    def sums_of(source):
        def step(h, carry):
            value = source[row_at(h), :]
            return carry[0] + tile_sums(value), carry[1] + tile_sums(value * value)

        return grid_rows(step, (zeros8, zeros8))

    step_here = jnp.full((1, c), inputs.step_index[row], jnp.int32)

    def condition(table):
        total = jnp.zeros((1, 2 * c), F32)
        chosen = jnp.concatenate([step_here, step_here], axis=1)
        for s in range(table.shape[0]):
            total = total + jnp.where(chosen == s, table[s : s + 1, :], 0.0)
        return total[:, :c], total[:, c:]

    for copy in own[:2]:
        copy.wait()
    for copy in frame_copies:
        copy.wait_recv()
    fields = scratch.fields
    fields[...] = jnp.zeros(fields.shape, F32)
    frame_of = lax.broadcasted_iota(jnp.int32, (history, width), 0) // FIELDS
    keep = (frame_of >= HIST - inputs.counts[row]).astype(F32)
    masks = []
    for source in range(line):
        for k in range(strip):
            columns = slice((source * strip + k) * width, (source * strip + k + 1) * width)
            mask = mask_in[source, k : k + 1, :].astype(F32)
            masks.append(mask)
            fields[0:history, columns] = frames_in[source, :, k, :] * keep * mask
            fields[history : history + 1, columns] = mask
    lifted = scratch.lifted

    def lift_step(i, carry):
        lifted[chunk_at(i), :] = dot(fields[:, chunk_at(i)], lift[...], TN, HIGH)
        return carry

    lax.fori_loop(0, cells // CHUNK, lift_step, 0)

    enc_scale, enc_shift = condition(inputs.enc_step_table)
    dec_scale, dec_shift = condition(inputs.dec_step_table)

    mean_e1, inv_e1 = norm_of(*sums_of(lifted), ones16, count16)
    gain_e1, bias_e1 = inputs.enc_norm1_gain[...], inputs.enc_norm1_bias[...]
    a_e1 = inv_e1 * gain_e1
    activate(lifted, scratch.xe1, scratch.te1, scratch.slope_e1, a_e1, bias_e1 - mean_e1 * a_e1)
    middle_e = scratch.middle_e
    mean_e2, inv_e2 = norm_of(
        *conv_norm([(scratch.xe1, scratch.fe1)], middle_e), ones16, count16
    )
    gain_e2, bias_e2 = inputs.enc_norm2_gain[...], inputs.enc_norm2_bias[...]
    a_e2 = inv_e2 * gain_e2
    activate(
        middle_e,
        scratch.xe2,
        scratch.te2,
        scratch.slope_e2,
        a_e2 * (1.0 + enc_scale),
        (bias_e2 - mean_e2 * a_e2) * (1.0 + enc_scale) + enc_shift,
    )
    encoded = scratch.encoded
    conv2_bias = inputs.enc_conv2_bias[...]
    joined = scratch.joined

    def encode(i, carry):
        value = fold(conv_chunk([(scratch.xe2, scratch.fe2)], i))
        value = value + conv2_bias + lifted[chunk_at(i), :]
        encoded[chunk_at(i), :] = value
        high, low = split(value)
        joined[chunk_at(i), c : 2 * c] = high
        joined[chunk_at(i), 3 * c : 4 * c] = low
        put_turned(scratch.turned, chunk_at(i), value, 1, 3)
        return carry[0] + tile_sums(value), carry[1] + tile_sums(value * value)

    sums_enc = lax.fori_loop(0, cells // CHUNK, encode, (zeros8, zeros8))

    half_cells, quarter = cells // 2, cells // 4

    def pick(source):
        pieces = []
        for b in range(2):
            value = source[pl.ds(b, half_cells, stride=2), :]
            value = value.reshape(height // 2, 2, width // 2, c)
            pieces.append([value[:, a].reshape(quarter, c) for a in range(2)])
        return [pieces[b][a] for a in range(2) for b in range(2)]

    def place_cells(target, pieces):
        for b in range(2):
            both = [pieces[2 * a + b].reshape(height // 2, 1, width // 2, c) for a in range(2)]
            value = jnp.concatenate(both, axis=1).reshape(half_cells, c)
            target[pl.ds(b, half_cells, stride=2), :] = value

    x_down = scratch.x_down
    for k, piece in enumerate(pick(encoded)):
        high, low = split(piece)
        x_down[:, k * c : (k + 1) * c] = high
        x_down[:, (k + 4) * c : (k + 5) * c] = low
    lowered = fold(dot(x_down[...], scratch.f_down[...])) + inputs.reducer_bias[...]
    x_up = scratch.x_up
    high, low = split(lowered)
    x_up[:, 0:c] = high
    x_up[:, c : 2 * c] = low
    raised = scratch.raised
    up_bias = inputs.up_bias[...]
    place_cells(
        raised, [fold(dot(x_up[...], scratch.f_up[k])) + up_bias for k in range(4)]
    )

    def raise_row(h, carry):
        value = raised[row_at(h), :]
        high, low = split(value)
        joined[row_at(h), 0:c] = high
        joined[row_at(h), 2 * c : 3 * c] = low
        put_turned(scratch.turned, row_at(h), value, 0, 2)
        return carry[0] + tile_sums(value), carry[1] + tile_sums(value * value)

    sums_raised = grid_rows(raise_row, (zeros8, zeros8))

    halves = []
    for half, (source, sums) in enumerate(((raised, sums_raised), (encoded, sums_enc))):
        mean, inv = norm_of(*sums, ones32, count32)
        gain = inputs.dec_norm1_gain[half : half + 1, :]
        bias = inputs.dec_norm1_bias[half : half + 1, :]
        scale = inv * gain
        activate(
            source,
            (scratch.xd1a, scratch.xd1b)[half],
            (scratch.td1a, scratch.td1b)[half],
            (scratch.slope_d1a, scratch.slope_d1b)[half],
            scale,
            bias - mean * scale,
        )
        halves.append((source, mean, inv, gain))
    middle_d = scratch.middle_d
    pairs = [(scratch.xd1a, scratch.fd1a), (scratch.xd1b, scratch.fd1b)]
    mean_d2, inv_d2 = norm_of(*conv_norm(pairs, middle_d), ones16, count16)
    gain_d2, bias_d2 = inputs.dec_norm2_gain[...], inputs.dec_norm2_bias[...]
    a_d2 = inv_d2 * gain_d2
    activate(
        middle_d,
        scratch.xd2,
        scratch.td2,
        scratch.slope_d2,
        a_d2 * (1.0 + dec_scale),
        (bias_d2 - mean_d2 * a_d2) * (1.0 + dec_scale) + dec_shift,
    )
    result = scratch.result
    last_bias = inputs.dec_conv2_bias[...] + inputs.skip_bias[...]

    def decode(i, carry):
        value = conv_chunk([(scratch.xd2, scratch.fd2)], i)
        value = value + dot(joined[chunk_at(i), :], scratch.f_skip[...])
        result[chunk_at(i), :] = fold(value) + last_bias
        return carry

    lax.fori_loop(0, cells // CHUNK, decode, 0)
    own_output = pltpu.make_async_copy(
        result.at[here_rows], outputs.output.at[row], local_sem.at[10]
    )
    own_output.start()
    for k in range(1, line):
        to = lax.rem(row + k, line)
        there = pl.ds(pl.multiple_of(to * strip_cells, strip_cells), strip_cells)
        output_copies.append(
            send(result.at[there], outputs.output.at[row], device_at(to))
        )

    exchanges = []
    waiting_runs = list(runs)
    landing_at = 0
    sem_at = 4 * (line - 1) + 2 * (line - 1)
    sums, final = scratch.sums, scratch.final

    kinds = (HalvingExchange, Exchange, Exchange, Exchange, Exchange, Exchange, Exchange, SmallExchange)

    def begin():
        nonlocal landing_at, sem_at
        start, rows = waiting_runs.pop(0)
        exchange = kinds[len(exchanges)](place, start, rows, landing_at, sem_at)
        landing_at += rows - rows // (8 * line)
        sem_at += exchange.count()
        exchanges.append(exchange)
        exchange.advance()

    final_copies = []

    def advance(k):
        exchange = exchanges[k]
        exchange.advance()
        if exchange.done():
            rows = pl.ds(exchange.start, exchange.rows)
            copy = pltpu.make_async_copy(
                final.at[rows], outputs.gradients.at[rows], local_sem.at[11 + k]
            )
            copy.start()
            final_copies.append(copy)

    due = list(DUE)

    def point():
        for k in due.pop(0):
            advance(k)

    def small_row(k, value):
        sums[small_at + k : small_at + k + 1, :] = value

    def spread_grad(source):
        def step(h, carry):
            value = source[row_at(h), :]
            put_row(scratch.xg, h, value)
            return carry + tile_sums(value)

        return grid_rows(step, zeros8)

    def weight_grad(pairs, depth):
        def step(t, carry):
            rows = pl.ds(pl.multiple_of((2 - t // 3) * width, width), cells)
            columns = pl.ds(pl.multiple_of((2 - lax.rem(t, 3)) * 2 * c, 2 * c), 2 * c)
            moved = scratch.xg[rows, columns]
            for turned, at in pairs:
                part = fold_rows(fold(dot(turned[...], moved)))
                sums[pl.ds(pl.multiple_of(at + t * depth, c), c), :] = part
            return carry

        lax.fori_loop(0, 9, step, 0)

    def back_conv(weight, slope, target, source, mean, inv):
        def step(i, carry):
            value = fold(conv_chunk([(scratch.xg, weight)], i, NT)) * slope[chunk_at(i), :]
            target[chunk_at(i), :] = value
            normed = (source[chunk_at(i), :] - mean) * inv
            return carry[0] + tile_sums(value), carry[1] + tile_sums(value * normed)

        sums_in = lax.fori_loop(0, cells // CHUNK, step, (zeros8, zeros8))
        point()
        return sums_in

    def norm_grad(sums_in, scale, ones, count):
        one, two = group_sums(sums_in[0] * scale, sums_in[1] * scale, ones)
        return one / count, two / count

    own[2].wait()
    for copy in cot_copies:
        copy.wait_recv()
    total_cot = column_sum(spread_grad(cot))
    weight_grad([(scratch.td2, starts.dec_conv2)], c)
    part = fold(dot(scratch.turned[...], scratch.xg[width : cells + width, 2 * c : 4 * c]))
    sums[starts.skip_weight : starts.skip_weight + 2 * c, :] = fold_rows(part)
    small_row(3, total_cot)
    begin()

    grad = scratch.grad
    sums_d2 = back_conv(scratch.bd2, scratch.slope_d2, grad, middle_d, mean_d2, inv_d2)
    side_grads = (scratch.grad_a, scratch.grad_b)
    for half in range(2):

        def skip_back(i, carry, half=half):
            rows = pl.ds(pl.multiple_of(i * CHUNK + width, width), CHUNK)
            value = dot(scratch.xg[rows, 2 * c : 4 * c], scratch.b_skip[half], NT)
            side_grads[half][chunk_at(i), :] = fold(value)
            return carry

        lax.fori_loop(0, cells // CHUNK, skip_back, 0)
    point()

    def table_rows(k, sums_in, gain, bias, one_plus):
        plain, times = column_sum(sums_in[0]), column_sum(sums_in[1])
        for s in range(inputs.enc_step_table.shape[0]):
            small_row(k + 2 * s, jnp.where(step_here == s, gain * times + bias * plain, 0.0))
            small_row(k + 2 * s + 1, jnp.where(step_here == s, plain, 0.0))
        return one_plus * times, one_plus * plain

    def middle_grad(source, mean, inv, scale, sums_in):
        zero, slope = norm_grad(sums_in, scale, ones16, count16)

        def step(h, carry):
            normed = (source[row_at(h), :] - mean) * inv
            value = inv * (grad[row_at(h), :] * scale - zero - normed * slope)
            put_row(scratch.xg, h, value)
            return carry

        grid_rows(step)

    gain_row, bias_row = table_rows(16, sums_d2, gain_d2, bias_d2, 1.0 + dec_scale)
    small_row(8, gain_row)
    small_row(9, bias_row)
    middle_grad(middle_d, mean_d2, inv_d2, gain_d2 * (1.0 + dec_scale), sums_d2)
    point()
    pairs = [(scratch.td1a, starts.dec_conv1), (scratch.td1b, starts.dec_conv1 + c)]
    weight_grad(pairs, 2 * c)
    point()
    for _ in range(3):
        begin()

    for half, (source, mean, inv, gain) in enumerate(halves):
        sums_in = back_conv(
            (scratch.bd1a, scratch.bd1b)[half],
            (scratch.slope_d1a, scratch.slope_d1b)[half],
            grad,
            source,
            mean,
            inv,
        )
        small_row(4 + half, column_sum(sums_in[1]))
        small_row(6 + half, column_sum(sums_in[0]))
        zero, slope = norm_grad(sums_in, gain, ones32, count32)
        target = side_grads[half]

        def input_grad(h, carry):
            normed = (source[row_at(h), :] - mean) * inv
            value = inv * (grad[row_at(h), :] * gain - zero - normed * slope)
            value = target[row_at(h), :] + value
            target[row_at(h), :] = value
            return carry + tile_sums(value)

        total = grid_rows(input_grad, zeros8)
        if half == 0:
            small_row(2, column_sum(total))
        point()

    grad_raised, grad_encoded = side_grads
    x_grad_up = scratch.x_grad_up
    for k, piece in enumerate(pick(grad_raised)):
        high, low = split(piece)
        x_grad_up[:, k * c : (k + 1) * c] = high
        x_grad_up[:, (k + 4) * c : (k + 5) * c] = low
    grad_lowered = fold(dot(x_grad_up[...], scratch.b_up[...], NT))
    small_row(1, jnp.sum(grad_lowered, axis=0, keepdims=True))
    x_grad_low = scratch.x_grad_low
    high, low = split(grad_lowered)
    x_grad_low[:, 0:c] = high
    x_grad_low[:, c : 2 * c] = low
    point()
    part = fold(fold_rows(dot(x_up[...], x_grad_up[...], TN)))
    for k in range(4):
        at = starts.up_weight + k * c
        sums[at : at + c, :] = part[:, k * c : (k + 1) * c]
    part = fold_rows(fold(dot(x_down[...], x_grad_low[...], TN)))
    sums[starts.reducer_weight : starts.reducer_weight + 4 * c, :] = part
    point()
    begin()
    place_cells(
        grad, [fold(dot(x_grad_low[...], scratch.b_down[k], NT)) for k in range(4)]
    )

    def join_row(h, carry):
        value = grad_encoded[row_at(h), :] + grad[row_at(h), :]
        grad_encoded[row_at(h), :] = value
        put_row(scratch.xg, h, value)
        return carry + tile_sums(value)

    small_row(0, column_sum(grid_rows(join_row, zeros8)))
    for k in range(10, 16):
        small_row(k, jnp.zeros((1, c), F32))
    sums[small_at + 24 : small_at + LATE, :] = jnp.zeros((LATE - 24, c), F32)
    point()
    weight_grad([(scratch.te2, starts.enc_conv2)], c)
    point()
    begin()
    sums_e2 = back_conv(scratch.be2, scratch.slope_e2, grad, middle_e, mean_e2, inv_e2)
    gain_row, bias_row = table_rows(LATE + 24, sums_e2, gain_e2, bias_e2, 1.0 + enc_scale)
    small_row(LATE + 18, gain_row)
    small_row(LATE + 19, bias_row)
    middle_grad(middle_e, mean_e2, inv_e2, gain_e2 * (1.0 + enc_scale), sums_e2)
    point()
    weight_grad([(scratch.te1, starts.enc_conv1)], c)
    point()
    begin()
    sums_e1 = back_conv(scratch.be1, scratch.slope_e1, grad, lifted, mean_e1, inv_e1)
    small_row(LATE + 16, column_sum(sums_e1[1]))
    small_row(LATE + 17, column_sum(sums_e1[0]))
    zero, slope = norm_grad(sums_e1, gain_e1, ones16, count16)

    def lifted_grad(h, carry):
        normed = (lifted[row_at(h), :] - mean_e1) * inv_e1
        value = inv_e1 * (grad[row_at(h), :] * gain_e1 - zero - normed * slope)
        grad[row_at(h), :] = grad_encoded[row_at(h), :] + value
        return carry

    grid_rows(lifted_grad)
    point()

    late_at = small_at + LATE
    back = scratch.back

    def back_step(i, total):
        value = grad[chunk_at(i), :]
        back[:, chunk_at(i)] = dot(lift[...], value, NT, HIGH)
        return total + dot(fields[:, chunk_at(i)], value, NN, HIGH)

    total = lax.fori_loop(0, cells // CHUNK, back_step, jnp.zeros((16, c), F32))
    sums[late_at : late_at + 16, :] = total
    sums[late_at + 20 : late_at + 24, :] = jnp.zeros((4, c), F32)
    point()
    begin()
    frames_out = scratch.frames_out
    for source in range(line):
        for k in range(strip):
            h = source * strip + k
            value = back[0:history, h * width : (h + 1) * width]
            frames_out[source, :, k, :] = value * keep * masks[h]
    own_frames = pltpu.make_async_copy(
        frames_out.at[row], outputs.frames_grad.at[row], local_sem.at[19]
    )
    own_frames.start()
    for k in range(1, line):
        to = lax.rem(row + k, line)
        output_copies.append(
            send(frames_out.at[to], outputs.frames_grad.at[row], device_at(to))
        )

    for k in REST:
        advance(k)
    assert not due and all(exchange.done() for exchange in exchanges)

    for copy in output_copies:
        copy.wait_recv()
    own_output.wait()
    own_frames.wait()
    for copy in final_copies:
        copy.wait()
    for copy in frame_copies + cot_copies + output_copies:
        copy.wait_send()
    for exchange in exchanges:
        for copy in exchange.copies:
            copy.wait_send()


def write_kernel(layout, *refs):
    shapes, starts, small_at = layout
    output, frames_grad, gradients = refs[:3]
    outputs = refs[3:-4]
    output_here, frames_here, gradients_here, sem = refs[-4:]
    c = gradients.shape[1]
    moves = [(frames_grad, frames_here, outputs[1])]
    for k, name in enumerate(LARGE):
        rows = pl.ds(starts[name], shapes[name][0])
        moves.append((gradients.at[rows], gradients_here.at[rows], outputs[2 + k]))
    moves.append((output, output_here, outputs[0]))
    small = pl.ds(small_at, SMALL_COUNT)
    first = pltpu.make_async_copy(gradients.at[small], gradients_here.at[small], sem.at[0])
    first.start()
    arriving, leaving = [], []
    for k, (source, here, _) in enumerate(moves):
        arriving.append(pltpu.make_async_copy(source, here, sem.at[1 + 2 * k]))
        arriving[-1].start()
    first.wait()
    for target, (k, rows) in zip(outputs[2 + len(LARGE) :], SMALL_ROWS.values()):
        at = small_at + k
        if rows == 8:
            for s in range(target.shape[0]):
                target[s : s + 1, 0:c] = gradients_here[at + 2 * s : at + 2 * s + 1, :]
                target[s : s + 1, c : 2 * c] = gradients_here[at + 2 * s + 1 : at + 2 * s + 2, :]
        else:
            target[...] = gradients_here[at : at + rows, :]
    for k, (_, here, target) in enumerate(moves):
        arriving[k].wait()
        leaving.append(pltpu.make_async_copy(here, target, sem.at[2 + 2 * k]))
        leaving[-1].start()
    for copy in leaving:
        copy.wait()


def whole_items(shape, *arguments):
    line = shape["rows"]
    whole = Given(*arguments)
    given = whole._asdict()
    frames, cotangent = whole.frames, whole.cotangent
    items, history, strip, width = frames.shape
    c = cotangent.shape[-1]
    cells = strip * line * width
    flat = {}
    for name, value in given.items():
        if value is cotangent:
            value = value.reshape(items, strip * width, c)
        elif name in LARGE:
            value = value.reshape(-1, c)
        elif value.ndim == 1 and name not in IN_SMEM:
            value = value.reshape(-1, c)
        flat[name] = value
    shapes = {name: flat[name].shape for name in LARGE}
    big_layout = layout_of(shapes)
    starts, small_at, total_rows, runs = big_layout
    copies = 7 * (line - 1) + len(runs) * (8 + 2 * (line - 1)) + 6
    landing = sum(rows - rows // (8 * line) for _, rows in runs) + LATE_COUNT * (8 + line)
    shifted = pltpu.VMEM((cells + 2 * width, 6 * c), BF16)
    forward = pltpu.VMEM((18 * c, 2 * c), BF16)
    backward = pltpu.VMEM((2 * c, 18 * c), BF16)
    field = pltpu.VMEM((cells, c), F32)
    flipped_field = pltpu.VMEM((2 * c, cells), BF16)
    quarter = cells // 4
    scratch = dict(
        small=pltpu.VMEM((LATE_COUNT, c), F32),
        send=pltpu.SemaphoreType.DMA((copies,)),
        recv=pltpu.SemaphoreType.DMA((copies,)),
        local=pltpu.SemaphoreType.DMA((20,)),
        sums=pltpu.VMEM((total_rows, c), F32),
        final=pltpu.VMEM((total_rows, c), F32),
        landing=pltpu.VMEM((landing, c), F32),
        frames_in=pltpu.VMEM((line, history, strip, width), F32),
        mask_in=pltpu.VMEM((line, strip, width), jnp.int32),
        frames_out=pltpu.VMEM((line, history, strip, width), F32),
        fields=pltpu.VMEM((16, cells), F32),
        back=pltpu.VMEM((16, cells), F32),
        lift=pltpu.VMEM((16, c), F32),
        joined=pltpu.VMEM((cells, 4 * c), BF16),
        x_down=pltpu.VMEM((quarter, 8 * c), BF16),
        x_grad_up=pltpu.VMEM((quarter, 8 * c), BF16),
        x_up=pltpu.VMEM((quarter, 2 * c), BF16),
        x_grad_low=pltpu.VMEM((quarter, 2 * c), BF16),
        f_down=pltpu.VMEM((8 * c, 2 * c), BF16),
        b_down=pltpu.VMEM((4, 2 * c, 2 * c), BF16),
        f_up=pltpu.VMEM((4, 2 * c, 2 * c), BF16),
        b_up=pltpu.VMEM((2 * c, 8 * c), BF16),
        f_skip=pltpu.VMEM((4 * c, 2 * c), BF16),
        b_skip=pltpu.VMEM((2, 2 * c, 2 * c), BF16),
        xe1=shifted,
        xe2=shifted,
        xd1a=shifted,
        xd1b=shifted,
        xd2=shifted,
        xg=shifted,
        te1=flipped_field,
        te2=flipped_field,
        td1a=flipped_field,
        td1b=flipped_field,
        td2=flipped_field,
        turned=pltpu.VMEM((4 * c, cells), BF16),
        fe1=forward,
        fe2=forward,
        fd1a=forward,
        fd1b=forward,
        fd2=forward,
        be1=backward,
        be2=backward,
        bd1a=backward,
        bd1b=backward,
        bd2=backward,
        slope_e1=field,
        slope_e2=field,
        slope_d1a=field,
        slope_d1b=field,
        slope_d2=field,
        lifted=field,
        middle_e=field,
        encoded=field,
        raised=field,
        middle_d=field,
        result=field,
        cot=field,
        grad=field,
        grad_a=field,
        grad_b=field,
    )
    scratch.update({name: pltpu.VMEM(shapes[name], F32) for name in LARGE})

    in_hbm = pl.BlockSpec(memory_space=pl.ANY)
    in_vmem = pl.BlockSpec(memory_space=pltpu.VMEM)
    in_smem = pl.BlockSpec(memory_space=pltpu.SMEM)
    in_specs = [
        in_hbm if name in IN_HBM else in_smem if name in IN_SMEM else in_vmem
        for name in ARGUMENTS
    ]
    out_shape = [
        jax.ShapeDtypeStruct((items, strip * width, c), F32),
        jax.ShapeDtypeStruct(frames.shape, F32),
        jax.ShapeDtypeStruct((total_rows, c), F32),
    ]
    out_specs = [in_hbm] * 3
    results = pl.pallas_call(
        functools.partial(
            item_kernel,
            (line, strip, width, shapes, big_layout),
            tuple(scratch),
        ),
        out_shape=out_shape,
        in_specs=in_specs,
        out_specs=out_specs,
        scratch_shapes=list(scratch.values()),
        compiler_params=pltpu.CompilerParams(
            collective_id=0, has_side_effects=True, vmem_limit_bytes=62 * 1024 * 1024
        ),
    )(*[flat[name] for name in ARGUMENTS])
    names = LARGE + tuple(SMALL_ROWS)
    written = pl.pallas_call(
        functools.partial(write_kernel, (shapes, starts, small_at)),
        out_shape=out_shape[:2] + [jax.ShapeDtypeStruct(flat[name].shape, F32) for name in names],
        in_specs=[pl.BlockSpec(memory_space=pltpu.HBM)] * 3,
        out_specs=[in_hbm] * (2 + len(LARGE)) + [in_vmem] * len(SMALL_ROWS),
        scratch_shapes=[
            pltpu.VMEM((items, strip * width, c), F32),
            pltpu.VMEM(frames.shape, F32),
            pltpu.VMEM((total_rows, c), F32),
            pltpu.SemaphoreType.DMA((1 + 2 * (2 + len(LARGE)),)),
        ],
        compiler_params=pltpu.CompilerParams(vmem_limit_bytes=60 * 1024 * 1024),
    )(*results)
    grads = dict(zip(names, written[2:]))
    ordered = [name for name in ARGUMENTS if name in grads]
    return (written[0].reshape(cotangent.shape), written[1]) + tuple(
        grads[name].reshape(given[name].shape) for name in ordered
    )


def body(shape, *arguments):
    items, _, strip, width = arguments[0].shape
    line = shape["rows"]
    whole = (
        shape["section"] == 2
        and shape["batch"] == 4
        and items == line
        and arguments[-1].shape[-1] == 128
        and (strip * line * width) % CHUNK == 0
    )
    return whole_items(shape, *arguments) if whole else strips_body(*arguments)


def solution(mesh):
    in_specs = (
        P(("section", "batch"), None, "rows", None),
        P(("section", "batch")),
        P(("section", "batch"), "rows", None),
        P(("section", "batch")),
        P(),
        P(),
        P(),
        P(),
        P(),
        P(),
        P(),
        P(),
        P(),
        P(),
        P(),
        P(),
        P(),
        P(),
        P(),
        P(),
        P(),
        P(),
        P(),
        P(),
        P(),
        P(),
        P(),
        P(),
        P(("section", "batch"), "rows", None, None),
    )
    out_specs = (
        P(("section", "batch"), "rows", None, None),
        P(("section", "batch"), None, "rows", None),
        P(),
        P(),
        P(),
        P(),
        P(),
        P(),
        P(),
        P(),
        P(),
        P(),
        P(),
        P(),
        P(),
        P(),
        P(),
        P(),
        P(),
        P(),
        P(),
        P(),
        P(),
        P(),
        P(),
        P(),
    )
    return jax.shard_map(functools.partial(body, mesh.shape), mesh=mesh, in_specs=in_specs, out_specs=out_specs, check_vma=False)
```

```python
import functools
from types import SimpleNamespace
from typing import Any, NamedTuple

import jax
import jax.numpy as jnp
from jax import lax
from jax.experimental import pallas as pl
from jax.experimental.pallas import tpu as pltpu
from jax.sharding import PartitionSpec as P

GROUPS = 8
FIELDS = 3
HIST = 4


EPS = 1e-05
HIGH = lax.Precision.HIGHEST


def extended(cells, sides, width):
    for axis, dim in sides:
        count = lax.axis_size(axis)
        ends = count - 1
        head = lax.slice_in_dim(cells, 0, width, axis=dim)
        tail = lax.slice_in_dim(cells, cells.shape[dim] - width, cells.shape[dim], axis=dim)
        cells = jnp.concatenate(
            [
                lax.ppermute(tail, axis, [(i, (i + 1) % count) for i in range(ends)]),
                cells,
                lax.ppermute(head, axis, [((i + 1) % count, i) for i in range(ends)]),
            ],
            axis=dim,
        )
    return cells


def from_behind(value, axis, steps):
    count = lax.axis_size(axis)
    pairs = [(source, (source + steps) % count) for source in range(count)]
    return lax.ppermute(value, axis, pairs)


def group_view(value_arrays):
    extent = value_arrays.shape
    return value_arrays.reshape(extent[:-1] + (GROUPS, extent[-1] // GROUPS))


def global_sums(value_arrays):
    grouped = group_view(value_arrays)
    flat = grouped.reshape(-1, GROUPS, grouped.shape[-1])
    first_sum = jnp.sum(flat, axis=(0, 2))
    second_sum = jnp.sum(flat * flat, axis=(0, 2))
    return lax.psum((first_sum, second_sum), "rows")


def apply_norm(value_arrays, sum_one, sum_two, norm_gain, norm_bias, total):
    grouped = group_view(value_arrays)
    group_mean = sum_one / total
    variance = sum_two / total - group_mean * group_mean
    inverse = lax.rsqrt(variance + EPS)
    normed = (grouped - group_mean[:, None]) * inverse[:, None]
    return normed.reshape(value_arrays.shape) * norm_gain + norm_bias


def norm_back(value_arrays, grad_one, grad_two):
    grouped = group_view(value_arrays)
    extra = grad_one[:, None] + 2.0 * grouped * grad_two[:, None]
    return extra.reshape(value_arrays.shape)


def reduce_grads(grad_one, grad_two):
    return lax.psum((grad_one, grad_two), "rows")


def conv_rows(padded, kernel):
    widened = jnp.pad(padded, ((0, 0), (1, 1), (0, 0)))
    return lax.conv_general_dilated(
        widened[None],
        kernel,
        (1, 1),
        "VALID",
        dimension_numbers=("NHWC", "HWIO", "NHWC"),
        precision=HIGH,
    )[0]


def flipped(kernel):
    return jnp.transpose(kernel[::-1, ::-1], (0, 1, 3, 2))


def pad_grads(value_arrays):
    return extended(value_arrays, (("rows", 0),), 1)


def totals_of(inputs, conv1):
    strip = inputs.shape[0]
    cells = strip * lax.axis_size("rows") * inputs.shape[1]
    return (cells * (inputs.shape[2] // GROUPS), cells * (conv1.shape[3] // GROUPS))


def block_forward(inputs, weights, scale_part, shift_part):
    norm1_gain, norm1_bias, conv1, norm2_gain, norm2_bias, conv2, conv2_bias = weights
    total_in, total_mid = totals_of(inputs, conv1)
    sums_in = global_sums(inputs)

    def pad_rows(value_arrays):
        return extended(value_arrays, (("rows", 0),), 1)

    act_one = pad_rows(
        jax.nn.gelu(
            apply_norm(inputs, sums_in[0], sums_in[1], norm1_gain, norm1_bias, total_in),
            approximate=False,
        )
    )
    middle = conv_rows(act_one, conv1)
    sums_mid = global_sums(middle)
    shaped = (
        apply_norm(middle, sums_mid[0], sums_mid[1], norm2_gain, norm2_bias, total_mid)
        * (1.0 + scale_part)
        + shift_part
    )
    act_two = pad_rows(jax.nn.gelu(shaped, approximate=False))
    branch = conv_rows(act_two, conv2) + conv2_bias
    return (branch, (sums_in[0], sums_in[1], act_one, middle, sums_mid[0], sums_mid[1], act_two))


def block_backward(inputs, weights, scale_part, shift_part, kept, grad_out):
    norm1_gain, norm1_bias, conv1, norm2_gain, norm2_bias, conv2, conv2_bias = weights
    in_one, in_two, act_one, middle, mid_one, mid_two, act_two = kept
    total_in, total_mid = totals_of(inputs, conv1)
    grad_conv2 = jax.vjp(lambda kernel: conv_rows(act_two, kernel), conv2)[1](grad_out)[0]
    grad_bias2 = jnp.sum(grad_out, axis=(0, 1))
    grad_act_two = conv_rows(pad_grads(grad_out), flipped(conv2))

    def second_piece(middle_in, sum_one, sum_two, gain_in, incoming_bias, scale_in, shift_in):
        shaped = (
            apply_norm(middle_in, sum_one, sum_two, gain_in, incoming_bias, total_mid)
            * (1.0 + scale_in)
            + shift_in
        )
        return jax.nn.gelu(shaped, approximate=False)

    second_pull = jax.vjp(
        second_piece, middle, mid_one, mid_two, norm2_gain, norm2_bias, scale_part, shift_part
    )[1](grad_act_two)
    summed_one, summed_two = reduce_grads(second_pull[1], second_pull[2])
    grad_middle = second_pull[0] + norm_back(middle, summed_one, summed_two)
    grad_conv1 = jax.vjp(lambda kernel: conv_rows(act_one, kernel), conv1)[1](grad_middle)[0]
    grad_act_one = conv_rows(pad_grads(grad_middle), flipped(conv1))

    def first_piece(inputs_in, sum_one, sum_two, gain_in, incoming_bias):
        return jax.nn.gelu(
            apply_norm(inputs_in, sum_one, sum_two, gain_in, incoming_bias, total_in),
            approximate=False,
        )

    first_pull = jax.vjp(first_piece, inputs, in_one, in_two, norm1_gain, norm1_bias)[1](
        grad_act_one
    )
    first_one, first_two = reduce_grads(first_pull[1], first_pull[2])
    grad_inputs = first_pull[0] + norm_back(inputs, first_one, first_two)
    grads = (
        first_pull[3],
        first_pull[4],
        grad_conv1,
        second_pull[3],
        second_pull[4],
        grad_conv2,
        grad_bias2,
    )
    return (grad_inputs, grads, second_pull[5], second_pull[6])


def conditioning(step_item, table):
    one_hot = (jnp.arange(table.shape[0], dtype=jnp.int32) == step_item).astype(jnp.float32)
    condition = jnp.dot(one_hot, table, precision=HIGH)
    half_width = table.shape[1] // 2
    return (condition[:half_width], condition[half_width:], one_hot)


def project_in(frames_item, mask_item, count_item, incoming_weight, incoming_bias):
    history = jnp.arange(HIST, dtype=jnp.int32) >= HIST - count_item
    keep = jnp.repeat(history, FIELDS).astype(jnp.float32)
    lifted = (
        jnp.einsum(
            "fhw,fc->hwc", frames_item * keep[:, None, None], incoming_weight, precision=HIGH
        )
        + incoming_bias
    )
    return lifted * mask_item[:, :, None].astype(jnp.float32)


def coarsen_field(value_arrays, incoming_weight, incoming_bias):
    rows_here, width_here, depth_here = value_arrays.shape
    blocks = value_arrays.reshape(rows_here // 2, 2, width_here // 2, 2, depth_here)
    return jnp.einsum("iajbk,abkc->ijc", blocks, incoming_weight, precision=HIGH) + incoming_bias


def upsample(value_arrays, incoming_weight, incoming_bias):
    result = jnp.einsum("ijk,abkc->iajbc", value_arrays, incoming_weight, precision=HIGH)
    extent = result.shape
    return result.reshape(extent[0] * 2, extent[2] * 2, extent[4]) + incoming_bias


def flatten_all(pieces):
    return jnp.concatenate([piece.reshape(-1) for piece in pieces])


def unflatten_all(flat, templates):
    pieces = []
    offset_at = 0
    for template in templates:
        count_here = template.size
        pieces.append(flat[offset_at : offset_at + count_here].reshape(template.shape))
        offset_at += count_here
    return tuple(pieces)


def strips_body(
    frames,
    counts,
    cell_mask,
    step_index,
    lift_weight,
    lift_bias,
    enc_norm1_gain,
    enc_norm1_bias,
    enc_conv1,
    enc_step_table,
    enc_norm2_gain,
    enc_norm2_bias,
    enc_conv2,
    enc_conv2_bias,
    reducer_weight,
    reducer_bias,
    up_weight,
    up_bias,
    dec_norm1_gain,
    dec_norm1_bias,
    dec_conv1,
    dec_step_table,
    dec_norm2_gain,
    dec_norm2_bias,
    dec_conv2,
    dec_conv2_bias,
    skip_weight,
    skip_bias,
    cotangent,
):
    enc_weights = (
        enc_norm1_gain,
        enc_norm1_bias,
        enc_conv1,
        enc_norm2_gain,
        enc_norm2_bias,
        enc_conv2,
        enc_conv2_bias,
    )
    dec_weights = (
        dec_norm1_gain,
        dec_norm1_bias,
        dec_conv1,
        dec_norm2_gain,
        dec_norm2_bias,
        dec_conv2,
        dec_conv2_bias,
    )
    params = (
        lift_weight,
        lift_bias,
        enc_norm1_gain,
        enc_norm1_bias,
        enc_conv1,
        enc_step_table,
        enc_norm2_gain,
        enc_norm2_bias,
        enc_conv2,
        enc_conv2_bias,
        reducer_weight,
        reducer_bias,
        up_weight,
        up_bias,
        dec_norm1_gain,
        dec_norm1_bias,
        dec_conv1,
        dec_step_table,
        dec_norm2_gain,
        dec_norm2_bias,
        dec_conv2,
        dec_conv2_bias,
        skip_weight,
        skip_bias,
    )

    def forward_micro(carry, sliced):
        frames_item, mask_item, count_item, step_item = sliced
        lifted = project_in(frames_item, mask_item, count_item, lift_weight, lift_bias)
        enc_scale, enc_shift, unused_hot = conditioning(step_item, enc_step_table)
        enc_branch, enc_kept = block_forward(lifted, enc_weights, enc_scale, enc_shift)
        encoder_result = lifted + enc_branch
        coarse_field = coarsen_field(encoder_result, reducer_weight, reducer_bias)
        foreign = from_behind(coarse_field, "section", 1)
        raised_foreign = upsample(foreign, up_weight, up_bias)
        raised = from_behind(raised_foreign, "section", 1)
        joined = jnp.concatenate([raised, encoder_result], axis=-1)
        dec_scale, dec_shift, unused_again = conditioning(step_item, dec_step_table)
        dec_branch, dec_kept = block_forward(joined, dec_weights, dec_scale, dec_shift)
        output_item = jnp.dot(joined, skip_weight, precision=HIGH) + skip_bias + dec_branch
        return (carry, (output_item, (lifted, enc_kept, encoder_result, foreign, joined, dec_kept)))

    unused, (output, kept_all) = lax.scan(
        forward_micro, jnp.zeros((), jnp.float32), (frames, cell_mask, counts, step_index)
    )

    def backward_micro(totals, sliced):
        frames_item, mask_item, count_item, step_item, grad_out, kept = sliced
        lifted, enc_kept, encoder_result, foreign, joined, dec_kept = kept
        dec_scale, dec_shift, one_hot = conditioning(step_item, dec_step_table)
        grad_joined, dec_grads, dec_gscale, dec_gshift = block_backward(
            joined, dec_weights, dec_scale, dec_shift, dec_kept, grad_out
        )
        grad_skip_weight = jnp.einsum("hwk,hwc->kc", joined, grad_out, precision=HIGH)
        grad_skip_bias = jnp.sum(grad_out, axis=(0, 1))
        grad_joined = grad_joined + jnp.dot(grad_out, skip_weight.T, precision=HIGH)
        half_width = joined.shape[-1] // 2
        grad_raised = grad_joined[..., :half_width]
        grad_encoded = grad_joined[..., half_width:]
        grad_foreign_up = from_behind(grad_raised, "section", 1)
        up_pull = jax.vjp(upsample, foreign, up_weight, up_bias)[1](grad_foreign_up)
        coarse_gradient = from_behind(up_pull[0], "section", 1)
        reducer_pullback = jax.vjp(coarsen_field, encoder_result, reducer_weight, reducer_bias)[1](
            coarse_gradient
        )
        grad_encoded = grad_encoded + reducer_pullback[0]
        enc_scale, enc_shift, enc_hot = conditioning(step_item, enc_step_table)
        grad_lifted, enc_grads, enc_gscale, enc_gshift = block_backward(
            lifted, enc_weights, enc_scale, enc_shift, enc_kept, grad_encoded
        )
        grad_lifted = grad_lifted + grad_encoded
        proj_pull = jax.vjp(
            lambda frames_in, incoming_weight, incoming_bias: project_in(
                frames_in, mask_item, count_item, incoming_weight, incoming_bias
            ),
            frames_item,
            lift_weight,
            lift_bias,
        )[1](grad_lifted)
        enc_table_grad = enc_hot[:, None] * jnp.concatenate([enc_gscale, enc_gshift])[None, :]
        dec_table_grad = one_hot[:, None] * jnp.concatenate([dec_gscale, dec_gshift])[None, :]
        micro_list = (
            proj_pull[1],
            proj_pull[2],
            enc_grads[0],
            enc_grads[1],
            enc_grads[2],
            enc_table_grad,
            enc_grads[3],
            enc_grads[4],
            enc_grads[5],
            enc_grads[6],
            reducer_pullback[1],
            reducer_pullback[2],
            up_pull[1],
            up_pull[2],
            dec_grads[0],
            dec_grads[1],
            dec_grads[2],
            dec_table_grad,
            dec_grads[3],
            dec_grads[4],
            dec_grads[5],
            dec_grads[6],
            grad_skip_weight,
            grad_skip_bias,
        )
        micro_flat = flatten_all(micro_list)
        return (totals + micro_flat, proj_pull[0])

    total_size = sum((piece.size for piece in params))
    start_totals = jnp.zeros((total_size,), jnp.float32)
    flat_totals, frames_grad = lax.scan(
        backward_micro,
        start_totals,
        (frames, cell_mask, counts, step_index, cotangent, kept_all),
        reverse=True,
    )
    flat_totals = lax.psum(flat_totals, ("section", "batch", "rows"))
    grads = unflatten_all(flat_totals, params)
    return (output, frames_grad) + grads


F32 = jnp.float32
BF16 = jnp.bfloat16
MESH = pl.DeviceIdType.MESH
NN = ((1,), (0,))
NT = ((1,), (1,))
TN = ((0,), (0,))
HIGH_AT = (0, 2, 1)
LOW_AT = (4, 3, 5)
CHUNK = 512
class Given(NamedTuple):
    frames: Any
    counts: Any
    cell_mask: Any
    step_index: Any
    lift_weight: Any
    lift_bias: Any
    enc_norm1_gain: Any
    enc_norm1_bias: Any
    enc_conv1: Any
    enc_step_table: Any
    enc_norm2_gain: Any
    enc_norm2_bias: Any
    enc_conv2: Any
    enc_conv2_bias: Any
    reducer_weight: Any
    reducer_bias: Any
    up_weight: Any
    up_bias: Any
    dec_norm1_gain: Any
    dec_norm1_bias: Any
    dec_conv1: Any
    dec_step_table: Any
    dec_norm2_gain: Any
    dec_norm2_bias: Any
    dec_conv2: Any
    dec_conv2_bias: Any
    skip_weight: Any
    skip_bias: Any
    cotangent: Any


ARGUMENTS = Given._fields
LARGE = tuple(
    dict(
        dec_conv1=0,
        up_weight=0,
        reducer_weight=0,
        dec_conv2=0,
        skip_weight=0,
        enc_conv1=0,
        enc_conv2=0,
    )
)
IN_HBM = tuple(dict(frames=0, cell_mask=0, cotangent=0)) + LARGE
IN_SMEM = tuple(dict(counts=0, step_index=0))
LATE = 64
SMALL_ROWS = dict(
    enc_conv2_bias=(0, 1),
    reducer_bias=(1, 1),
    up_bias=(2, 1),
    dec_conv2_bias=(3, 1),
    skip_bias=(3, 1),
    dec_norm1_gain=(4, 2),
    dec_norm1_bias=(6, 2),
    dec_norm2_gain=(8, 1),
    dec_norm2_bias=(9, 1),
    dec_step_table=(16, 8),
    lift_weight=(LATE, 12),
    lift_bias=(LATE + 12, 1),
    enc_norm1_gain=(LATE + 16, 1),
    enc_norm1_bias=(LATE + 17, 1),
    enc_norm2_gain=(LATE + 18, 1),
    enc_norm2_bias=(LATE + 19, 1),
    enc_step_table=(LATE + 24, 8),
)
LATE_COUNT = 32
SMALL_COUNT = LATE + LATE_COUNT
DUE = ((), (), (), (), (0,), (), (1,), (), (), (2,), (0,), (3,), (1,), (), (4,), (), (2,), (), (0,), (1, 3), (), (), (2, 5), (4, 0), (6,), (3, 1, 7), (), (2,), (4, 0))
REST = (8, 5, 1, 9, 3, 2, 6, 4, 7, 10, 5, 3, 0, 6, 4, 7, 5, 8, 6, 1, 0, 7, 9, 8, 5, 6, 2, 1, 7, 9, 10, 8, 3, 9, 2, 8, 4, 9, 3, 5, 4, 6, 7, 5, 8, 6, 9, 7, 8, 9)
OUTPUTS = tuple(dict(output=0, frames_grad=0, gradients=0))


def split(value):
    high = value.astype(BF16)
    return high, (value - high.astype(F32)).astype(BF16)


def dot(left, right, dims=NN, precision=None):
    return lax.dot_general(
        left, right, (dims, ((), ())), precision=precision, preferred_element_type=F32
    )


def fold(value):
    half = value.shape[1] // 2
    return value[:, :half] + value[:, half:]


def fold_rows(value):
    half = value.shape[0] // 2
    return value[:half] + value[half:]


def tile_sums(value):
    return jnp.sum(value.reshape(-1, 8, value.shape[-1]), axis=0)


def column_sum(tiles):
    return jnp.sum(tiles, axis=0, keepdims=True)


def group_ones(channels, size):
    rows = lax.broadcasted_iota(jnp.int32, (channels, channels), 0) // size
    columns = lax.broadcasted_iota(jnp.int32, (channels, channels), 1) // size
    return (rows == columns).astype(F32)


def group_sums(first, second, ones):
    both = dot(jnp.concatenate([first, second], axis=0), ones, precision=HIGH)
    return column_sum(both[:8]), column_sum(both[8:])


class Exchange:

    def __init__(self, place, start, rows, landing, first_sem):
        self.place, self.start, self.rows, self.landing = place, start, rows, landing
        self.sem = first_sem
        self.stage = 0
        self.copies = []
        self.waiting = []
        self.group = place.plane_group
        self.half = rows // 2
        self.base = start + place.core * self.half
        self._finish(self.half)

    def _finish(self, size):
        self.part = size // self.group.count
        self.own = self.base + self.group.here * self.part

    def count(self):
        return 2 + 2 * (self.group.count - 1) + 3

    def land_rows(self):
        return self.half + (self.group.count + 1) * self.part

    def _copy(self, source, target, device, only=None):
        place = self.place
        copy = pltpu.make_async_remote_copy(
            src_ref=source,
            dst_ref=target,
            send_sem=place.send.at[self.sem],
            recv_sem=place.recv.at[self.sem],
            device_id=device,
            device_id_type=MESH,
        )
        self.sem += 1
        if only is None:
            copy.start()
            self.waiting.append(copy)
        self.copies.append((copy, only))
        return copy

    def _wait(self):
        for copy in self.waiting:
            copy.wait_recv()
        self.waiting = []

    def _rows(self, at, size):
        return pl.ds(pl.multiple_of(at, 8), size)

    def _swap(self):
        place = self.place
        other = self._rows(self.start + (1 - place.core) * self.half, self.half)
        self.land = self.landing
        self.landing += self.half
        self._copy(
            place.sums.at[other], place.landing.at[pl.ds(self.land, self.half)], place.partner
        )

    def _add_swap(self):
        place = self.place
        block = 64 if self.half % 64 == 0 else 32

        def step(i, carry):
            here = self._rows(self.base + i * block, block)
            there = self._rows(self.land + i * block, block)
            place.sums[here] = place.sums[here] + place.landing[there]
            return carry

        lax.fori_loop(0, self.half // block, step, 0)

    def _scatter(self, group, base, size):
        place = self.place
        self.land = self.landing
        for k in range(1, group.count):
            to = lax.rem(group.here + k, group.count)
            self._copy(
                place.sums.at[self._rows(base + to * size, size)],
                place.landing.at[pl.ds(self.landing, size)],
                group.device(to),
            )
            self.landing += size

    def _total(self, group, own, size, target):
        place = self.place
        block = 16 if size % 16 == 0 else 8

        def step(i, carry):
            here = self._rows(own + i * block, block)
            total = place.sums[here]
            for k in range(group.count - 1):
                there = self._rows(self.land + k * size + i * block, block)
                total = total + place.landing[there]
            target[here] = total
            return carry

        lax.fori_loop(0, size // block, step, 0)

    def _gather(self, group, own, size):
        final = self.place.final
        here = self._rows(own, size)
        for k in range(1, group.count):
            to = lax.rem(group.here + k, group.count)
            self._copy(final.at[here], final.at[here], group.device(to))

    def _steps(self):
        place, group = self.place, self.group
        yield self._swap()
        self._wait()
        self._add_swap()
        yield from self._both()
        final = place.final
        here = self._rows(self.base, self.half)
        self._copy(final.at[here], final.at[here], place.partner)
        yield
        self._wait()
        yield

    def _both(self):
        place, group = self.place, self.group
        self._scatter(group, self.base, self.part)
        yield
        self._wait()
        self._total(group, self.own, self.part, place.sums)
        yield from self._line()
        self._gather(group, self.own, self.part)
        yield
        self._wait()

    def _line(self):
        place, line = self.place, self.place.line
        sums, final, landing = place.sums, place.final, place.landing
        part, own = self.part, self._rows(self.own, self.part)
        inward, across = pl.ds(self.landing, part), pl.ds(self.landing + part, part)
        self.landing += 2 * part
        block = 16 if part % 16 == 0 else 8

        def add(at, target):
            def step(i, carry):
                here = self._rows(self.own + i * block, block)
                target[here] = sums[here] + landing[pl.ds(at + i * block, block)]
                return carry

            lax.fori_loop(0, part // block, step, 0)

        first = self._copy(sums.at[own], landing.at[inward], line.device(line.inner), line.edge)
        second = self._copy(sums.at[own], landing.at[across], line.device(line.across), line.middle)
        third = self._copy(final.at[own], final.at[own], line.device(line.outer), line.middle)
        pl.when(line.edge)(first.start)
        yield

        @pl.when(line.middle)
        def _():
            first.wait_recv()
            add(self.landing - 2 * part, sums)
            second.start()

        yield

        @pl.when(line.middle)
        def _():
            second.wait_recv()
            add(self.landing - part, final)
            third.start()

        yield
        pl.when(line.edge)(third.wait_recv)

    def advance(self):
        if self.stage == 0:
            self.steps = self._steps()
        self.stage += 1
        next(self.steps)

    def done(self):
        return self.stage == 8


class SmallExchange(Exchange):

    def count(self):
        return self.place.cores_group.count + self.place.line.count - 2

    def land_rows(self):
        return self.rows * (self.place.cores_group.count + self.place.line.count)

    def _share(self, group, source):
        place = self.place
        self.land = self.landing
        self.landing += group.count * self.rows
        own = self._rows(self.land + group.here * self.rows, self.rows)
        place.landing[own] = source[...]
        for k in range(1, group.count):
            to = lax.rem(group.here + k, group.count)
            self._copy(source, place.landing.at[own], group.device(to))

    def _sum(self, group):
        total = None
        for k in range(group.count):
            part = self.place.landing[pl.ds(self.land + k * self.rows, self.rows)]
            total = part if total is None else total + part
        return total

    def _steps(self):
        place = self.place
        here = pl.ds(self.start, self.rows)
        self._share(place.line, place.sums.at[here])
        yield
        self._wait()
        place.small[...] = self._sum(place.line)
        self._share(place.cores_group, place.small)
        yield
        self._wait()
        place.final[here] = self._sum(place.cores_group)
        yield

    def done(self):
        return self.stage == 3


def layout_of(shapes):
    starts = {}
    at = 0
    for name in LARGE:
        starts[name] = at
        at += getattr(shapes, name)[0]
    small = at
    begins = SimpleNamespace(**starts)
    late = small + LATE
    tap = shapes.dec_conv2[0] // 3
    part = shapes.dec_conv1[0] // 3
    conv1, up = begins.dec_conv1, begins.up_weight
    edges = (
        (begins.dec_conv2, begins.dec_conv2 + 2 * tap),
        (begins.dec_conv2 + 2 * tap, begins.enc_conv1),
        (conv1, conv1 + part),
        (conv1 + part, conv1 + 2 * part),
        (conv1 + 2 * part, up),
        (up, begins.dec_conv2),
        (begins.enc_conv2, begins.enc_conv2 + 2 * tap),
        (begins.enc_conv2 + 2 * tap, late),
        (begins.enc_conv1, begins.enc_conv1 + 2 * tap),
        (begins.enc_conv1 + 2 * tap, begins.enc_conv2),
        (late, late + LATE_COUNT),
    )
    runs = [(first, last - first) for first, last in edges]
    return starts, small, late + LATE_COUNT, runs


def item_kernel(sizes, scratch_names, *refs):
    line, strip, width, shapes, big_layout = sizes
    begins, small_at, total_rows, runs = big_layout
    starts = SimpleNamespace(**begins)
    inputs = Given(*refs[: len(ARGUMENTS)])
    refs = refs[len(ARGUMENTS) :]
    output_names = OUTPUTS
    outputs = SimpleNamespace(**dict(zip(output_names, refs)))
    scratch = SimpleNamespace(**dict(zip(scratch_names, refs[len(output_names) :])))

    def w_of(name):
        return getattr(scratch, name)

    height = strip * line
    cells = height * width
    c = inputs.lift_weight.shape[1]
    strip_cells = strip * width
    history = inputs.frames.shape[1]

    core = lax.axis_index("section")
    plane = lax.axis_index("batch")
    row = lax.axis_index("rows")
    middle = lax.rem(row + 1, 4) // 2

    def device_at(to):
        return (core, plane, to)

    place = SimpleNamespace(
        core=core,
        partner=(1 - core, plane, row),
        line=SimpleNamespace(
            count=line,
            here=row,
            device=device_at,
            middle=middle == 1,
            edge=middle == 0,
            inner=1 + row // 2,
            across=3 - row,
            outer=3 * (row // 2),
        ),
        plane_group=SimpleNamespace(
            count=4, here=plane, device=lambda to: (core, to, row)
        ),
        cores_group=SimpleNamespace(
            count=8,
            here=core * 4 + plane,
            device=lambda to: (to // 4, lax.rem(to, 4), row),
        ),
        small=scratch.small,
        sums=scratch.sums,
        final=scratch.final,
        landing=scratch.landing,
        send=scratch.send,
        recv=scratch.recv,
    )
    local_sem = scratch.local

    weight_copies = {}
    for k, name in enumerate(LARGE):
        copy = pltpu.make_async_copy(getattr(inputs, name), w_of(name), local_sem.at[k])
        weight_copies[name] = copy
        copy.start()
    frames_in, mask_in, cot = scratch.frames_in, scratch.mask_in, scratch.cot
    here_rows = pl.ds(pl.multiple_of(row * strip_cells, strip_cells), strip_cells)
    own = (
        pltpu.make_async_copy(inputs.frames.at[row], frames_in.at[row], local_sem.at[7]),
        pltpu.make_async_copy(inputs.cell_mask.at[row], mask_in.at[row], local_sem.at[8]),
        pltpu.make_async_copy(
            inputs.cotangent.at[row], cot.at[here_rows], local_sem.at[9]
        ),
    )
    for copy in own:
        copy.start()

    barrier = pltpu.get_barrier_semaphore()
    peers = [device_at(lax.rem(row + k, line)) for k in range(1, line)]
    cores_group = place.cores_group
    for k in range(1, 8):
        peers.append(cores_group.device(lax.rem(cores_group.here + k, 8)))
    for device in peers:
        pl.semaphore_signal(barrier, inc=1, device_id=device, device_id_type=MESH)
    pl.semaphore_wait(barrier, len(peers))

    next_sem = 0

    def send(source, target, device):
        nonlocal next_sem
        copy = pltpu.make_async_remote_copy(
            src_ref=source,
            dst_ref=target,
            send_sem=scratch.send.at[next_sem],
            recv_sem=scratch.recv.at[next_sem],
            device_id=device,
            device_id_type=MESH,
        )
        next_sem += 1
        copy.start()
        return copy

    frame_copies, cot_copies, output_copies = [], [], []
    for k in range(1, line):
        to = lax.rem(row + k, line)
        device = device_at(to)
        frame_copies.append(send(inputs.frames.at[to], frames_in.at[row], device))
        frame_copies.append(send(inputs.cell_mask.at[to], mask_in.at[row], device))
    for k in range(1, line):
        to = lax.rem(row + k, line)
        cot_copies.append(
            send(inputs.cotangent.at[to], cot.at[here_rows], device_at(to))
        )

    copied = SimpleNamespace(**weight_copies)
    def stack_conv(source, half, depth, forward, backward):
        for a in range(3):
            for b in range(3):
                at = (3 * a + b) * depth + half * c
                high, low = split(source[at : at + c, :])
                for block in (HIGH_AT[b], LOW_AT[b]):
                    rows = slice((6 * a + block) * c, (6 * a + block + 1) * c)
                    forward[rows, 0:c] = high
                    forward[rows, c : 2 * c] = low
                for block in (HIGH_AT[2 - b], LOW_AT[2 - b]):
                    tap = 6 * (2 - a) + block
                    columns = slice(tap * c, (tap + 1) * c)
                    backward[0:c, columns] = high
                    backward[c : 2 * c, columns] = low

    copied.enc_conv1.wait()
    stack_conv(scratch.enc_conv1, 0, c, scratch.fe1, scratch.be1)
    copied.enc_conv2.wait()
    stack_conv(scratch.enc_conv2, 0, c, scratch.fe2, scratch.be2)
    copied.reducer_weight.wait()
    for k in range(4):
        high, low = split(scratch.reducer_weight[k * c : (k + 1) * c, :])
        for block in (k, k + 4):
            scratch.f_down[block * c : (block + 1) * c, 0:c] = high
            scratch.f_down[block * c : (block + 1) * c, c : 2 * c] = low
        for block in (0, 1):
            columns = slice(block * c, (block + 1) * c)
            scratch.b_down[k, 0:c, columns] = high
            scratch.b_down[k, c : 2 * c, columns] = low
    copied.up_weight.wait()
    for k in range(4):
        high, low = split(scratch.up_weight[k * c : (k + 1) * c, :])
        for block in (0, 1):
            rows = slice(block * c, (block + 1) * c)
            scratch.f_up[k, rows, 0:c] = high
            scratch.f_up[k, rows, c : 2 * c] = low
        for block in (k, k + 4):
            columns = slice(block * c, (block + 1) * c)
            scratch.b_up[0:c, columns] = high
            scratch.b_up[c : 2 * c, columns] = low
    copied.dec_conv1.wait()
    stack_conv(scratch.dec_conv1, 0, 2 * c, scratch.fd1a, scratch.bd1a)
    stack_conv(scratch.dec_conv1, 1, 2 * c, scratch.fd1b, scratch.bd1b)
    copied.dec_conv2.wait()
    stack_conv(scratch.dec_conv2, 0, c, scratch.fd2, scratch.bd2)
    copied.skip_weight.wait()
    for half in range(2):
        high, low = split(scratch.skip_weight[half * c : (half + 1) * c, :])
        for block in (half, half + 2):
            scratch.f_skip[block * c : (block + 1) * c, 0:c] = high
            scratch.f_skip[block * c : (block + 1) * c, c : 2 * c] = low
        for block in (0, 1):
            columns = slice(block * c, (block + 1) * c)
            scratch.b_skip[half, 0:c, columns] = high
            scratch.b_skip[half, c : 2 * c, columns] = low

    for buffer in (scratch.xe1, scratch.xe2, scratch.xd1a, scratch.xd1b, scratch.xd2, scratch.xg):
        edge = jnp.zeros((width, 6 * c), BF16)
        buffer[0:width, :] = edge
        buffer[cells + width : cells + 2 * width, :] = edge

    lift = scratch.lift
    lift[...] = jnp.zeros(lift.shape, F32)
    lift[0:history, :] = inputs.lift_weight[...]
    lift[history : history + 1, :] = inputs.lift_bias[...]

    block = 2 * width
    column = lax.rem(lax.broadcasted_iota(jnp.int32, (block, c), 0), width)
    at_first, at_last = column == 0, column == width - 1
    zeros8 = jnp.zeros((8, c), F32)
    ones16 = group_ones(c, c // GROUPS)
    ones32 = group_ones(c, 2 * c // GROUPS)
    count16 = float(cells * (c // GROUPS))
    count32 = float(cells * (2 * c // GROUPS))

    def grid_rows(step, carry=0):
        return lax.fori_loop(0, cells // block, step, carry, unroll=2)

    def row_at(h):
        return pl.ds(pl.multiple_of(h * block, block), block)

    def chunk_at(i):
        return pl.ds(pl.multiple_of(i * CHUNK, CHUNK), CHUNK)

    def put_row(target, h, value):
        rows = pl.ds(pl.multiple_of(h * block + width, width), block)
        left = jnp.where(at_first, 0.0, pltpu.roll(value, 1, 0))
        right = jnp.where(at_last, 0.0, pltpu.roll(value, block - 1, 0))
        for b, piece in enumerate((left, value, right)):
            high, low = split(piece)
            target[rows, HIGH_AT[b] * c : (HIGH_AT[b] + 1) * c] = high
            target[rows, LOW_AT[b] * c : (LOW_AT[b] + 1) * c] = low

    def put_turned(target, columns, value, first=0, second=1):
        high, low = split(value.T)
        target[first * c : (first + 1) * c, columns] = high
        target[second * c : (second + 1) * c, columns] = low

    def conv_chunk(pairs, i, dims=NN):
        total = None
        for data, weight in pairs:
            taps = []
            for a in range(3):
                rows = pl.ds(pl.multiple_of(i * CHUNK + a * width, width), CHUNK)
                taps.append(data[rows, :])
            part = dot(jnp.concatenate(taps, axis=1), weight[...], dims)
            total = part if total is None else total + part
        return total

    def norm_of(first, second, ones, count):
        one, two = group_sums(first, second, ones)
        mean = one / count
        return mean, lax.rsqrt(two / count - mean * mean + EPS)

    def activate(source, target, turned, slope, scale, shift):
        def step(h, carry):
            value = source[row_at(h), :] * scale + shift
            below = 0.5 + 0.5 * lax.erf(value * 0.7071067811865476)
            slope[row_at(h), :] = below + value * (
                0.3989422804014327 * jnp.exp(-0.5 * value * value)
            )
            value = value * below
            put_row(target, h, value)
            put_turned(turned, row_at(h), value)
            return carry

        grid_rows(step)

    def conv_norm(pairs, target):
        def step(i, carry):
            value = fold(conv_chunk(pairs, i))
            target[chunk_at(i), :] = value
            return carry[0] + tile_sums(value), carry[1] + tile_sums(value * value)

        return lax.fori_loop(0, cells // CHUNK, step, (zeros8, zeros8))

    def sums_of(source):
        def step(h, carry):
            value = source[row_at(h), :]
            return carry[0] + tile_sums(value), carry[1] + tile_sums(value * value)

        return grid_rows(step, (zeros8, zeros8))

    step_here = jnp.full((1, c), inputs.step_index[row], jnp.int32)

    def condition(table):
        total = jnp.zeros((1, 2 * c), F32)
        chosen = jnp.concatenate([step_here, step_here], axis=1)
        for s in range(table.shape[0]):
            total = total + jnp.where(chosen == s, table[s : s + 1, :], 0.0)
        return total[:, :c], total[:, c:]

    for copy in own[:2]:
        copy.wait()
    for copy in frame_copies:
        copy.wait_recv()
    fields = scratch.fields
    fields[...] = jnp.zeros(fields.shape, F32)
    frame_of = lax.broadcasted_iota(jnp.int32, (history, width), 0) // FIELDS
    keep = (frame_of >= HIST - inputs.counts[row]).astype(F32)
    masks = []
    for source in range(line):
        for k in range(strip):
            columns = slice((source * strip + k) * width, (source * strip + k + 1) * width)
            mask = mask_in[source, k : k + 1, :].astype(F32)
            masks.append(mask)
            fields[0:history, columns] = frames_in[source, :, k, :] * keep * mask
            fields[history : history + 1, columns] = mask
    lifted = scratch.lifted
    lifted[...] = dot(fields[...], lift[...], TN, HIGH)

    enc_scale, enc_shift = condition(inputs.enc_step_table)
    dec_scale, dec_shift = condition(inputs.dec_step_table)

    mean_e1, inv_e1 = norm_of(*sums_of(lifted), ones16, count16)
    gain_e1, bias_e1 = inputs.enc_norm1_gain[...], inputs.enc_norm1_bias[...]
    a_e1 = inv_e1 * gain_e1
    activate(lifted, scratch.xe1, scratch.te1, scratch.slope_e1, a_e1, bias_e1 - mean_e1 * a_e1)
    middle_e = scratch.middle_e
    mean_e2, inv_e2 = norm_of(
        *conv_norm([(scratch.xe1, scratch.fe1)], middle_e), ones16, count16
    )
    gain_e2, bias_e2 = inputs.enc_norm2_gain[...], inputs.enc_norm2_bias[...]
    a_e2 = inv_e2 * gain_e2
    activate(
        middle_e,
        scratch.xe2,
        scratch.te2,
        scratch.slope_e2,
        a_e2 * (1.0 + enc_scale),
        (bias_e2 - mean_e2 * a_e2) * (1.0 + enc_scale) + enc_shift,
    )
    encoded = scratch.encoded
    conv2_bias = inputs.enc_conv2_bias[...]
    joined = scratch.joined

    def encode(i, carry):
        value = fold(conv_chunk([(scratch.xe2, scratch.fe2)], i))
        value = value + conv2_bias + lifted[chunk_at(i), :]
        encoded[chunk_at(i), :] = value
        high, low = split(value)
        joined[chunk_at(i), c : 2 * c] = high
        joined[chunk_at(i), 3 * c : 4 * c] = low
        put_turned(scratch.turned, chunk_at(i), value, 1, 3)
        return carry[0] + tile_sums(value), carry[1] + tile_sums(value * value)

    sums_enc = lax.fori_loop(0, cells // CHUNK, encode, (zeros8, zeros8))

    half_cells, quarter = cells // 2, cells // 4

    def pick(source):
        pieces = []
        for b in range(2):
            value = source[pl.ds(b, half_cells, stride=2), :]
            value = value.reshape(height // 2, 2, width // 2, c)
            pieces.append([value[:, a].reshape(quarter, c) for a in range(2)])
        return [pieces[b][a] for a in range(2) for b in range(2)]

    def place_cells(target, pieces):
        for b in range(2):
            both = [pieces[2 * a + b].reshape(height // 2, 1, width // 2, c) for a in range(2)]
            value = jnp.concatenate(both, axis=1).reshape(half_cells, c)
            target[pl.ds(b, half_cells, stride=2), :] = value

    x_down = scratch.x_down
    for k, piece in enumerate(pick(encoded)):
        high, low = split(piece)
        x_down[:, k * c : (k + 1) * c] = high
        x_down[:, (k + 4) * c : (k + 5) * c] = low
    lowered = fold(dot(x_down[...], scratch.f_down[...])) + inputs.reducer_bias[...]
    x_up = scratch.x_up
    high, low = split(lowered)
    x_up[:, 0:c] = high
    x_up[:, c : 2 * c] = low
    raised = scratch.raised
    up_bias = inputs.up_bias[...]
    place_cells(
        raised, [fold(dot(x_up[...], scratch.f_up[k])) + up_bias for k in range(4)]
    )

    def raise_row(h, carry):
        value = raised[row_at(h), :]
        high, low = split(value)
        joined[row_at(h), 0:c] = high
        joined[row_at(h), 2 * c : 3 * c] = low
        put_turned(scratch.turned, row_at(h), value, 0, 2)
        return carry[0] + tile_sums(value), carry[1] + tile_sums(value * value)

    sums_raised = grid_rows(raise_row, (zeros8, zeros8))

    halves = []
    for half, (source, sums) in enumerate(((raised, sums_raised), (encoded, sums_enc))):
        mean, inv = norm_of(*sums, ones32, count32)
        gain = inputs.dec_norm1_gain[half : half + 1, :]
        bias = inputs.dec_norm1_bias[half : half + 1, :]
        scale = inv * gain
        activate(
            source,
            (scratch.xd1a, scratch.xd1b)[half],
            (scratch.td1a, scratch.td1b)[half],
            (scratch.slope_d1a, scratch.slope_d1b)[half],
            scale,
            bias - mean * scale,
        )
        halves.append((source, mean, inv, gain))
    middle_d = scratch.middle_d
    pairs = [(scratch.xd1a, scratch.fd1a), (scratch.xd1b, scratch.fd1b)]
    mean_d2, inv_d2 = norm_of(*conv_norm(pairs, middle_d), ones16, count16)
    gain_d2, bias_d2 = inputs.dec_norm2_gain[...], inputs.dec_norm2_bias[...]
    a_d2 = inv_d2 * gain_d2
    activate(
        middle_d,
        scratch.xd2,
        scratch.td2,
        scratch.slope_d2,
        a_d2 * (1.0 + dec_scale),
        (bias_d2 - mean_d2 * a_d2) * (1.0 + dec_scale) + dec_shift,
    )
    result = scratch.result
    last_bias = inputs.dec_conv2_bias[...] + inputs.skip_bias[...]

    def decode(i, carry):
        value = conv_chunk([(scratch.xd2, scratch.fd2)], i)
        value = value + dot(joined[chunk_at(i), :], scratch.f_skip[...])
        result[chunk_at(i), :] = fold(value) + last_bias
        return carry

    lax.fori_loop(0, cells // CHUNK, decode, 0)
    own_output = pltpu.make_async_copy(
        result.at[here_rows], outputs.output.at[row], local_sem.at[10]
    )
    own_output.start()
    for k in range(1, line):
        to = lax.rem(row + k, line)
        there = pl.ds(pl.multiple_of(to * strip_cells, strip_cells), strip_cells)
        output_copies.append(
            send(result.at[there], outputs.output.at[row], device_at(to))
        )

    exchanges = []
    waiting_runs = list(runs)
    landing_at = 0
    sem_at = 4 * (line - 1) + 2 * (line - 1)
    sums, final = scratch.sums, scratch.final

    def begin():
        nonlocal landing_at, sem_at
        start, rows = waiting_runs.pop(0)
        kind = Exchange if waiting_runs else SmallExchange
        exchange = kind(place, start, rows, landing_at, sem_at)
        landing_at += exchange.land_rows()
        sem_at += exchange.count()
        exchanges.append(exchange)
        exchange.advance()

    final_copies = []

    def advance(k):
        exchange = exchanges[k]
        exchange.advance()
        if exchange.done():
            rows = pl.ds(exchange.start, exchange.rows)
            copy = pltpu.make_async_copy(
                final.at[rows], outputs.gradients.at[rows], local_sem.at[11 + k]
            )
            copy.start()
            final_copies.append(copy)

    due = list(DUE)

    def point():
        for k in due.pop(0):
            advance(k)

    def small_row(k, value):
        sums[small_at + k : small_at + k + 1, :] = value

    def spread_grad(source):
        def step(h, carry):
            value = source[row_at(h), :]
            put_row(scratch.xg, h, value)
            return carry + tile_sums(value)

        return grid_rows(step, zeros8)

    def weight_grad(turned, at, depth, a):
        rows = pl.ds((2 - a) * width, cells)
        part = fold_rows(dot(turned[...], scratch.xg[rows, :]))
        for b in range(3):
            high, low = HIGH_AT[2 - b] * c, LOW_AT[2 - b] * c
            to = at + (3 * a + b) * depth
            sums[to : to + c, :] = part[:, high : high + c] + part[:, low : low + c]

    def back_conv(weight, slope, target, source, mean, inv):
        carry = (zeros8, zeros8)
        for i in range(cells // CHUNK):
            value = fold(conv_chunk([(scratch.xg, weight)], i, NT)) * slope[chunk_at(i), :]
            target[chunk_at(i), :] = value
            normed = (source[chunk_at(i), :] - mean) * inv
            carry = (carry[0] + tile_sums(value), carry[1] + tile_sums(value * normed))
            if i % (cells // CHUNK // 2) == cells // CHUNK // 2 - 1:
                point()
        return carry

    def norm_grad(sums_in, scale, ones, count):
        one, two = group_sums(sums_in[0] * scale, sums_in[1] * scale, ones)
        return one / count, two / count

    own[2].wait()
    for copy in cot_copies:
        copy.wait_recv()
    total_cot = column_sum(spread_grad(cot))
    for a in range(3):
        weight_grad(scratch.td2, starts.dec_conv2, c, a)
        if a == 1:
            begin()
    part = fold(dot(scratch.turned[...], scratch.xg[width : cells + width, 2 * c : 4 * c]))
    sums[starts.skip_weight : starts.skip_weight + 2 * c, :] = fold_rows(part)
    small_row(3, total_cot)
    begin()

    grad = scratch.grad
    sums_d2 = back_conv(scratch.bd2, scratch.slope_d2, grad, middle_d, mean_d2, inv_d2)
    side_grads = (scratch.grad_a, scratch.grad_b)
    for half in range(2):

        def skip_back(i, carry, half=half):
            rows = pl.ds(pl.multiple_of(i * CHUNK + width, width), CHUNK)
            value = dot(scratch.xg[rows, 2 * c : 4 * c], scratch.b_skip[half], NT)
            side_grads[half][chunk_at(i), :] = fold(value)
            return carry

        lax.fori_loop(0, cells // CHUNK, skip_back, 0)
    point()

    def table_rows(k, sums_in, gain, bias, one_plus):
        plain, times = column_sum(sums_in[0]), column_sum(sums_in[1])
        for s in range(inputs.enc_step_table.shape[0]):
            small_row(k + 2 * s, jnp.where(step_here == s, gain * times + bias * plain, 0.0))
            small_row(k + 2 * s + 1, jnp.where(step_here == s, plain, 0.0))
        return one_plus * times, one_plus * plain

    def middle_grad(source, mean, inv, scale, sums_in):
        zero, slope = norm_grad(sums_in, scale, ones16, count16)

        def step(h, carry):
            normed = (source[row_at(h), :] - mean) * inv
            value = inv * (grad[row_at(h), :] * scale - zero - normed * slope)
            put_row(scratch.xg, h, value)
            return carry

        grid_rows(step)

    gain_row, bias_row = table_rows(16, sums_d2, gain_d2, bias_d2, 1.0 + dec_scale)
    small_row(8, gain_row)
    small_row(9, bias_row)
    middle_grad(middle_d, mean_d2, inv_d2, gain_d2 * (1.0 + dec_scale), sums_d2)
    point()
    for a in range(3):
        weight_grad(scratch.td1a, starts.dec_conv1, 2 * c, a)
        weight_grad(scratch.td1b, starts.dec_conv1 + c, 2 * c, a)
        point()
        begin()

    for half, (source, mean, inv, gain) in enumerate(halves):
        sums_in = back_conv(
            (scratch.bd1a, scratch.bd1b)[half],
            (scratch.slope_d1a, scratch.slope_d1b)[half],
            grad,
            source,
            mean,
            inv,
        )
        small_row(4 + half, column_sum(sums_in[1]))
        small_row(6 + half, column_sum(sums_in[0]))
        zero, slope = norm_grad(sums_in, gain, ones32, count32)
        target = side_grads[half]

        def input_grad(h, carry):
            normed = (source[row_at(h), :] - mean) * inv
            value = inv * (grad[row_at(h), :] * gain - zero - normed * slope)
            value = target[row_at(h), :] + value
            target[row_at(h), :] = value
            return carry + tile_sums(value)

        total = grid_rows(input_grad, zeros8)
        if half == 0:
            small_row(2, column_sum(total))
        point()

    grad_raised, grad_encoded = side_grads
    x_grad_up = scratch.x_grad_up
    for k, piece in enumerate(pick(grad_raised)):
        high, low = split(piece)
        x_grad_up[:, k * c : (k + 1) * c] = high
        x_grad_up[:, (k + 4) * c : (k + 5) * c] = low
    grad_lowered = fold(dot(x_grad_up[...], scratch.b_up[...], NT))
    small_row(1, jnp.sum(grad_lowered, axis=0, keepdims=True))
    x_grad_low = scratch.x_grad_low
    high, low = split(grad_lowered)
    x_grad_low[:, 0:c] = high
    x_grad_low[:, c : 2 * c] = low
    point()
    part = fold(fold_rows(dot(x_up[...], x_grad_up[...], TN)))
    for k in range(4):
        at = starts.up_weight + k * c
        sums[at : at + c, :] = part[:, k * c : (k + 1) * c]
    part = fold_rows(fold(dot(x_down[...], x_grad_low[...], TN)))
    sums[starts.reducer_weight : starts.reducer_weight + 4 * c, :] = part
    point()
    begin()
    place_cells(
        grad, [fold(dot(x_grad_low[...], scratch.b_down[k], NT)) for k in range(4)]
    )

    def join_row(h, carry):
        value = grad_encoded[row_at(h), :] + grad[row_at(h), :]
        grad_encoded[row_at(h), :] = value
        put_row(scratch.xg, h, value)
        return carry + tile_sums(value)

    small_row(0, column_sum(grid_rows(join_row, zeros8)))
    for k in range(10, 16):
        small_row(k, jnp.zeros((1, c), F32))
    sums[small_at + 24 : small_at + LATE, :] = jnp.zeros((LATE - 24, c), F32)
    point()
    for a in range(3):
        weight_grad(scratch.te2, starts.enc_conv2, c, a)
        point()
        if a:
            begin()
    sums_e2 = back_conv(scratch.be2, scratch.slope_e2, grad, middle_e, mean_e2, inv_e2)
    gain_row, bias_row = table_rows(LATE + 24, sums_e2, gain_e2, bias_e2, 1.0 + enc_scale)
    small_row(LATE + 18, gain_row)
    small_row(LATE + 19, bias_row)
    middle_grad(middle_e, mean_e2, inv_e2, gain_e2 * (1.0 + enc_scale), sums_e2)
    point()
    for a in range(3):
        weight_grad(scratch.te1, starts.enc_conv1, c, a)
        point()
        if a:
            begin()
    sums_e1 = back_conv(scratch.be1, scratch.slope_e1, grad, lifted, mean_e1, inv_e1)
    small_row(LATE + 16, column_sum(sums_e1[1]))
    small_row(LATE + 17, column_sum(sums_e1[0]))
    zero, slope = norm_grad(sums_e1, gain_e1, ones16, count16)

    def lifted_grad(h, carry):
        normed = (lifted[row_at(h), :] - mean_e1) * inv_e1
        value = inv_e1 * (grad[row_at(h), :] * gain_e1 - zero - normed * slope)
        grad[row_at(h), :] = grad_encoded[row_at(h), :] + value
        return carry

    grid_rows(lifted_grad)
    point()

    late_at = small_at + LATE
    sums[late_at : late_at + 16, :] = dot(fields[...], grad[...], NN, HIGH)
    sums[late_at + 20 : late_at + 24, :] = jnp.zeros((4, c), F32)
    point()
    begin()
    back = dot(lift[...], grad[...], NT, HIGH)
    frames_out = scratch.frames_out
    for source in range(line):
        for k in range(strip):
            h = source * strip + k
            value = back[0:history, h * width : (h + 1) * width]
            frames_out[source, :, k, :] = value * keep * masks[h]
    own_frames = pltpu.make_async_copy(
        frames_out.at[row], outputs.frames_grad.at[row], local_sem.at[11 + len(runs)]
    )
    own_frames.start()
    for k in range(1, line):
        to = lax.rem(row + k, line)
        output_copies.append(
            send(frames_out.at[to], outputs.frames_grad.at[row], device_at(to))
        )

    for k in REST:
        advance(k)
    assert not due and all(exchange.done() for exchange in exchanges)

    for copy in output_copies:
        copy.wait_recv()
    own_output.wait()
    own_frames.wait()
    for copy in final_copies:
        copy.wait()
    for copy in frame_copies + cot_copies + output_copies:
        copy.wait_send()
    for exchange in exchanges:
        for copy, only in exchange.copies:
            if only is None:
                copy.wait_send()
            else:
                pl.when(only)(copy.wait_send)


def write_kernel(layout, *refs):
    shapes, starts, small_at = layout
    output, frames_grad, gradients = refs[:3]
    outputs = refs[3:-4]
    output_here, frames_here, gradients_here, sem = refs[-4:]
    c = gradients.shape[1]
    moves = [(frames_grad, frames_here, outputs[1])]
    for k, name in enumerate(LARGE):
        rows = pl.ds(starts[name], shapes[name][0])
        moves.append((gradients.at[rows], gradients_here.at[rows], outputs[2 + k]))
    moves.append((output, output_here, outputs[0]))
    small = pl.ds(small_at, SMALL_COUNT)
    first = pltpu.make_async_copy(gradients.at[small], gradients_here.at[small], sem.at[0])
    first.start()
    arriving, leaving = [], []
    for k, (source, here, _) in enumerate(moves):
        arriving.append(pltpu.make_async_copy(source, here, sem.at[1 + 2 * k]))
        arriving[-1].start()
    first.wait()
    for target, (k, rows) in zip(outputs[2 + len(LARGE) :], SMALL_ROWS.values()):
        at = small_at + k
        if rows == 8:
            for s in range(target.shape[0]):
                target[s : s + 1, 0:c] = gradients_here[at + 2 * s : at + 2 * s + 1, :]
                target[s : s + 1, c : 2 * c] = gradients_here[at + 2 * s + 1 : at + 2 * s + 2, :]
        else:
            target[...] = gradients_here[at : at + rows, :]
    for k, (_, here, target) in enumerate(moves):
        arriving[k].wait()
        leaving.append(pltpu.make_async_copy(here, target, sem.at[2 + 2 * k]))
        leaving[-1].start()
    for copy in leaving:
        copy.wait()


def whole_items(shape, *arguments):
    line = shape["rows"]
    whole = Given(*arguments)
    given = whole._asdict()
    frames, cotangent = whole.frames, whole.cotangent
    items, history, strip, width = frames.shape
    c = cotangent.shape[-1]
    cells = strip * line * width
    flat = {}
    for name, value in given.items():
        if value is cotangent:
            value = value.reshape(items, strip * width, c)
        elif name in LARGE:
            value = value.reshape(-1, c)
        elif value.ndim == 1 and name not in IN_SMEM:
            value = value.reshape(-1, c)
        flat[name] = value
    shapes = {name: flat[name].shape for name in LARGE}
    big_layout = layout_of(SimpleNamespace(**shapes))
    starts, small_at, total_rows, runs = big_layout
    copies = 7 * (line - 1) + len(runs) * (8 + 2 * (line - 1)) + 6
    landing = sum(rows // 2 + 5 * rows // 8 for _, rows in runs) + LATE_COUNT * (8 + line)
    shifted = pltpu.VMEM((cells + 2 * width, 6 * c), BF16)
    forward = pltpu.VMEM((18 * c, 2 * c), BF16)
    backward = pltpu.VMEM((2 * c, 18 * c), BF16)
    field = pltpu.VMEM((cells, c), F32)
    flipped_field = pltpu.VMEM((2 * c, cells), BF16)
    quarter = cells // 4
    scratch = dict(
        small=pltpu.VMEM((LATE_COUNT, c), F32),
        send=pltpu.SemaphoreType.DMA((copies,)),
        recv=pltpu.SemaphoreType.DMA((copies,)),
        local=pltpu.SemaphoreType.DMA((12 + len(runs),)),
        sums=pltpu.VMEM((total_rows, c), F32),
        final=pltpu.VMEM((total_rows, c), F32),
        landing=pltpu.VMEM((landing, c), F32),
        frames_in=pltpu.VMEM((line, history, strip, width), F32),
        mask_in=pltpu.VMEM((line, strip, width), jnp.int32),
        frames_out=pltpu.VMEM((line, history, strip, width), F32),
        fields=pltpu.VMEM((16, cells), F32),
        lift=pltpu.VMEM((16, c), F32),
        joined=pltpu.VMEM((cells, 4 * c), BF16),
        x_down=pltpu.VMEM((quarter, 8 * c), BF16),
        x_grad_up=pltpu.VMEM((quarter, 8 * c), BF16),
        x_up=pltpu.VMEM((quarter, 2 * c), BF16),
        x_grad_low=pltpu.VMEM((quarter, 2 * c), BF16),
        f_down=pltpu.VMEM((8 * c, 2 * c), BF16),
        b_down=pltpu.VMEM((4, 2 * c, 2 * c), BF16),
        f_up=pltpu.VMEM((4, 2 * c, 2 * c), BF16),
        b_up=pltpu.VMEM((2 * c, 8 * c), BF16),
        f_skip=pltpu.VMEM((4 * c, 2 * c), BF16),
        b_skip=pltpu.VMEM((2, 2 * c, 2 * c), BF16),
        xe1=shifted,
        xe2=shifted,
        xd1a=shifted,
        xd1b=shifted,
        xd2=shifted,
        xg=shifted,
        te1=flipped_field,
        te2=flipped_field,
        td1a=flipped_field,
        td1b=flipped_field,
        td2=flipped_field,
        turned=pltpu.VMEM((4 * c, cells), BF16),
        fe1=forward,
        fe2=forward,
        fd1a=forward,
        fd1b=forward,
        fd2=forward,
        be1=backward,
        be2=backward,
        bd1a=backward,
        bd1b=backward,
        bd2=backward,
        slope_e1=field,
        slope_e2=field,
        slope_d1a=field,
        slope_d1b=field,
        slope_d2=field,
        lifted=field,
        middle_e=field,
        encoded=field,
        raised=field,
        middle_d=field,
        result=field,
        cot=field,
        grad=field,
        grad_a=field,
        grad_b=field,
    )
    scratch.update({name: pltpu.VMEM(shapes[name], F32) for name in LARGE})

    in_hbm = pl.BlockSpec(memory_space=pl.ANY)
    in_vmem = pl.BlockSpec(memory_space=pltpu.VMEM)
    in_smem = pl.BlockSpec(memory_space=pltpu.SMEM)
    in_specs = [
        in_hbm if name in IN_HBM else in_smem if name in IN_SMEM else in_vmem
        for name in ARGUMENTS
    ]
    out_shape = [
        jax.ShapeDtypeStruct((items, strip * width, c), F32),
        jax.ShapeDtypeStruct(frames.shape, F32),
        jax.ShapeDtypeStruct((total_rows, c), F32),
    ]
    out_specs = [in_hbm] * 3
    results = pl.pallas_call(
        functools.partial(
            item_kernel,
            (line, strip, width, shapes, big_layout),
            tuple(scratch),
        ),
        out_shape=out_shape,
        in_specs=in_specs,
        out_specs=out_specs,
        scratch_shapes=list(scratch.values()),
        compiler_params=pltpu.CompilerParams(
            collective_id=0, has_side_effects=True, vmem_limit_bytes=62 * 1024 * 1024
        ),
    )(*[flat[name] for name in ARGUMENTS])
    names = LARGE + tuple(SMALL_ROWS)
    written = pl.pallas_call(
        functools.partial(write_kernel, (shapes, starts, small_at)),
        out_shape=out_shape[:2] + [jax.ShapeDtypeStruct(flat[name].shape, F32) for name in names],
        in_specs=[pl.BlockSpec(memory_space=pltpu.HBM)] * 3,
        out_specs=[in_hbm] * (2 + len(LARGE)) + [in_vmem] * len(SMALL_ROWS),
        scratch_shapes=[
            pltpu.VMEM((items, strip * width, c), F32),
            pltpu.VMEM(frames.shape, F32),
            pltpu.VMEM((total_rows, c), F32),
            pltpu.SemaphoreType.DMA((1 + 2 * (2 + len(LARGE)),)),
        ],
        compiler_params=pltpu.CompilerParams(vmem_limit_bytes=60 * 1024 * 1024),
    )(*results)
    grads = dict(zip(names, written[2:]))
    ordered = [name for name in ARGUMENTS if name in grads]
    return (written[0].reshape(cotangent.shape), written[1]) + tuple(
        grads[name].reshape(given[name].shape) for name in ordered
    )


def body(shape, *arguments):
    items, _, strip, width = arguments[0].shape
    line = shape["rows"]
    whole = (
        shape["section"] == 2
        and shape["batch"] == 4
        and items == line == 4
        and arguments[-1].shape[-1] == 128
        and (strip * line * width) % CHUNK == 0
    )
    return whole_items(shape, *arguments) if whole else strips_body(*arguments)


def solution(mesh):
    in_specs = (
        P(("section", "batch"), None, "rows", None),
        P(("section", "batch")),
        P(("section", "batch"), "rows", None),
        P(("section", "batch")),
        P(),
        P(),
        P(),
        P(),
        P(),
        P(),
        P(),
        P(),
        P(),
        P(),
        P(),
        P(),
        P(),
        P(),
        P(),
        P(),
        P(),
        P(),
        P(),
        P(),
        P(),
        P(),
        P(),
        P(),
        P(("section", "batch"), "rows", None, None),
    )
    out_specs = (
        P(("section", "batch"), "rows", None, None),
        P(("section", "batch"), None, "rows", None),
        P(),
        P(),
        P(),
        P(),
        P(),
        P(),
        P(),
        P(),
        P(),
        P(),
        P(),
        P(),
        P(),
        P(),
        P(),
        P(),
        P(),
        P(),
        P(),
        P(),
        P(),
        P(),
        P(),
        P(),
    )
    return jax.shard_map(functools.partial(body, mesh.shape), mesh=mesh, in_specs=in_specs, out_specs=out_specs, check_vma=False)
```

```python
import functools
from types import SimpleNamespace
from typing import Any, NamedTuple

import jax
import jax.numpy as jnp
from jax import lax
from jax.experimental import pallas as pl
from jax.experimental.pallas import tpu as pltpu
from jax.sharding import PartitionSpec as P

GROUPS = 8
FIELDS = 3
HIST = 4


EPS = 1e-05
HIGH = lax.Precision.HIGHEST


def extended(cells, sides, width):
    for axis, dim in sides:
        count = lax.axis_size(axis)
        ends = count - 1
        head = lax.slice_in_dim(cells, 0, width, axis=dim)
        tail = lax.slice_in_dim(cells, cells.shape[dim] - width, cells.shape[dim], axis=dim)
        cells = jnp.concatenate(
            [
                lax.ppermute(tail, axis, [(i, (i + 1) % count) for i in range(ends)]),
                cells,
                lax.ppermute(head, axis, [((i + 1) % count, i) for i in range(ends)]),
            ],
            axis=dim,
        )
    return cells


def from_behind(value, axis, steps):
    count = lax.axis_size(axis)
    pairs = [(source, (source + steps) % count) for source in range(count)]
    return lax.ppermute(value, axis, pairs)


def group_view(value_arrays):
    extent = value_arrays.shape
    return value_arrays.reshape(extent[:-1] + (GROUPS, extent[-1] // GROUPS))


def global_sums(value_arrays):
    grouped = group_view(value_arrays)
    flat = grouped.reshape(-1, GROUPS, grouped.shape[-1])
    first_sum = jnp.sum(flat, axis=(0, 2))
    second_sum = jnp.sum(flat * flat, axis=(0, 2))
    return lax.psum((first_sum, second_sum), "rows")


def apply_norm(value_arrays, sum_one, sum_two, norm_gain, norm_bias, total):
    grouped = group_view(value_arrays)
    group_mean = sum_one / total
    variance = sum_two / total - group_mean * group_mean
    inverse = lax.rsqrt(variance + EPS)
    normed = (grouped - group_mean[:, None]) * inverse[:, None]
    return normed.reshape(value_arrays.shape) * norm_gain + norm_bias


def norm_back(value_arrays, grad_one, grad_two):
    grouped = group_view(value_arrays)
    extra = grad_one[:, None] + 2.0 * grouped * grad_two[:, None]
    return extra.reshape(value_arrays.shape)


def reduce_grads(grad_one, grad_two):
    return lax.psum((grad_one, grad_two), "rows")


def conv_rows(padded, kernel):
    widened = jnp.pad(padded, ((0, 0), (1, 1), (0, 0)))
    return lax.conv_general_dilated(
        widened[None],
        kernel,
        (1, 1),
        "VALID",
        dimension_numbers=("NHWC", "HWIO", "NHWC"),
        precision=HIGH,
    )[0]


def flipped(kernel):
    return jnp.transpose(kernel[::-1, ::-1], (0, 1, 3, 2))


def pad_grads(value_arrays):
    return extended(value_arrays, (("rows", 0),), 1)


def totals_of(inputs, conv1):
    strip = inputs.shape[0]
    cells = strip * lax.axis_size("rows") * inputs.shape[1]
    return (cells * (inputs.shape[2] // GROUPS), cells * (conv1.shape[3] // GROUPS))


def block_forward(inputs, weights, scale_part, shift_part):
    norm1_gain, norm1_bias, conv1, norm2_gain, norm2_bias, conv2, conv2_bias = weights
    total_in, total_mid = totals_of(inputs, conv1)
    sums_in = global_sums(inputs)

    def pad_rows(value_arrays):
        return extended(value_arrays, (("rows", 0),), 1)

    act_one = pad_rows(
        jax.nn.gelu(
            apply_norm(inputs, sums_in[0], sums_in[1], norm1_gain, norm1_bias, total_in),
            approximate=False,
        )
    )
    middle = conv_rows(act_one, conv1)
    sums_mid = global_sums(middle)
    shaped = (
        apply_norm(middle, sums_mid[0], sums_mid[1], norm2_gain, norm2_bias, total_mid)
        * (1.0 + scale_part)
        + shift_part
    )
    act_two = pad_rows(jax.nn.gelu(shaped, approximate=False))
    branch = conv_rows(act_two, conv2) + conv2_bias
    return (branch, (sums_in[0], sums_in[1], act_one, middle, sums_mid[0], sums_mid[1], act_two))


def block_backward(inputs, weights, scale_part, shift_part, kept, grad_out):
    norm1_gain, norm1_bias, conv1, norm2_gain, norm2_bias, conv2, conv2_bias = weights
    in_one, in_two, act_one, middle, mid_one, mid_two, act_two = kept
    total_in, total_mid = totals_of(inputs, conv1)
    grad_conv2 = jax.vjp(lambda kernel: conv_rows(act_two, kernel), conv2)[1](grad_out)[0]
    grad_bias2 = jnp.sum(grad_out, axis=(0, 1))
    grad_act_two = conv_rows(pad_grads(grad_out), flipped(conv2))

    def second_piece(middle_in, sum_one, sum_two, gain_in, incoming_bias, scale_in, shift_in):
        shaped = (
            apply_norm(middle_in, sum_one, sum_two, gain_in, incoming_bias, total_mid)
            * (1.0 + scale_in)
            + shift_in
        )
        return jax.nn.gelu(shaped, approximate=False)

    second_pull = jax.vjp(
        second_piece, middle, mid_one, mid_two, norm2_gain, norm2_bias, scale_part, shift_part
    )[1](grad_act_two)
    summed_one, summed_two = reduce_grads(second_pull[1], second_pull[2])
    grad_middle = second_pull[0] + norm_back(middle, summed_one, summed_two)
    grad_conv1 = jax.vjp(lambda kernel: conv_rows(act_one, kernel), conv1)[1](grad_middle)[0]
    grad_act_one = conv_rows(pad_grads(grad_middle), flipped(conv1))

    def first_piece(inputs_in, sum_one, sum_two, gain_in, incoming_bias):
        return jax.nn.gelu(
            apply_norm(inputs_in, sum_one, sum_two, gain_in, incoming_bias, total_in),
            approximate=False,
        )

    first_pull = jax.vjp(first_piece, inputs, in_one, in_two, norm1_gain, norm1_bias)[1](
        grad_act_one
    )
    first_one, first_two = reduce_grads(first_pull[1], first_pull[2])
    grad_inputs = first_pull[0] + norm_back(inputs, first_one, first_two)
    grads = (
        first_pull[3],
        first_pull[4],
        grad_conv1,
        second_pull[3],
        second_pull[4],
        grad_conv2,
        grad_bias2,
    )
    return (grad_inputs, grads, second_pull[5], second_pull[6])


def conditioning(step_item, table):
    one_hot = (jnp.arange(table.shape[0], dtype=jnp.int32) == step_item).astype(jnp.float32)
    condition = jnp.dot(one_hot, table, precision=HIGH)
    half_width = table.shape[1] // 2
    return (condition[:half_width], condition[half_width:], one_hot)


def project_in(frames_item, mask_item, count_item, incoming_weight, incoming_bias):
    history = jnp.arange(HIST, dtype=jnp.int32) >= HIST - count_item
    keep = jnp.repeat(history, FIELDS).astype(jnp.float32)
    lifted = (
        jnp.einsum(
            "fhw,fc->hwc", frames_item * keep[:, None, None], incoming_weight, precision=HIGH
        )
        + incoming_bias
    )
    return lifted * mask_item[:, :, None].astype(jnp.float32)


def coarsen_field(value_arrays, incoming_weight, incoming_bias):
    rows_here, width_here, depth_here = value_arrays.shape
    blocks = value_arrays.reshape(rows_here // 2, 2, width_here // 2, 2, depth_here)
    return jnp.einsum("iajbk,abkc->ijc", blocks, incoming_weight, precision=HIGH) + incoming_bias


def upsample(value_arrays, incoming_weight, incoming_bias):
    result = jnp.einsum("ijk,abkc->iajbc", value_arrays, incoming_weight, precision=HIGH)
    extent = result.shape
    return result.reshape(extent[0] * 2, extent[2] * 2, extent[4]) + incoming_bias


def flatten_all(pieces):
    return jnp.concatenate([piece.reshape(-1) for piece in pieces])


def unflatten_all(flat, templates):
    pieces = []
    offset_at = 0
    for template in templates:
        count_here = template.size
        pieces.append(flat[offset_at : offset_at + count_here].reshape(template.shape))
        offset_at += count_here
    return tuple(pieces)


def strips_body(
    frames,
    counts,
    cell_mask,
    step_index,
    lift_weight,
    lift_bias,
    enc_norm1_gain,
    enc_norm1_bias,
    enc_conv1,
    enc_step_table,
    enc_norm2_gain,
    enc_norm2_bias,
    enc_conv2,
    enc_conv2_bias,
    reducer_weight,
    reducer_bias,
    up_weight,
    up_bias,
    dec_norm1_gain,
    dec_norm1_bias,
    dec_conv1,
    dec_step_table,
    dec_norm2_gain,
    dec_norm2_bias,
    dec_conv2,
    dec_conv2_bias,
    skip_weight,
    skip_bias,
    cotangent,
):
    enc_weights = (
        enc_norm1_gain,
        enc_norm1_bias,
        enc_conv1,
        enc_norm2_gain,
        enc_norm2_bias,
        enc_conv2,
        enc_conv2_bias,
    )
    dec_weights = (
        dec_norm1_gain,
        dec_norm1_bias,
        dec_conv1,
        dec_norm2_gain,
        dec_norm2_bias,
        dec_conv2,
        dec_conv2_bias,
    )
    params = (
        lift_weight,
        lift_bias,
        enc_norm1_gain,
        enc_norm1_bias,
        enc_conv1,
        enc_step_table,
        enc_norm2_gain,
        enc_norm2_bias,
        enc_conv2,
        enc_conv2_bias,
        reducer_weight,
        reducer_bias,
        up_weight,
        up_bias,
        dec_norm1_gain,
        dec_norm1_bias,
        dec_conv1,
        dec_step_table,
        dec_norm2_gain,
        dec_norm2_bias,
        dec_conv2,
        dec_conv2_bias,
        skip_weight,
        skip_bias,
    )

    def forward_micro(carry, sliced):
        frames_item, mask_item, count_item, step_item = sliced
        lifted = project_in(frames_item, mask_item, count_item, lift_weight, lift_bias)
        enc_scale, enc_shift, unused_hot = conditioning(step_item, enc_step_table)
        enc_branch, enc_kept = block_forward(lifted, enc_weights, enc_scale, enc_shift)
        encoder_result = lifted + enc_branch
        coarse_field = coarsen_field(encoder_result, reducer_weight, reducer_bias)
        foreign = from_behind(coarse_field, "section", 1)
        raised_foreign = upsample(foreign, up_weight, up_bias)
        raised = from_behind(raised_foreign, "section", 1)
        joined = jnp.concatenate([raised, encoder_result], axis=-1)
        dec_scale, dec_shift, unused_again = conditioning(step_item, dec_step_table)
        dec_branch, dec_kept = block_forward(joined, dec_weights, dec_scale, dec_shift)
        output_item = jnp.dot(joined, skip_weight, precision=HIGH) + skip_bias + dec_branch
        return (carry, (output_item, (lifted, enc_kept, encoder_result, foreign, joined, dec_kept)))

    unused, (output, kept_all) = lax.scan(
        forward_micro, jnp.zeros((), jnp.float32), (frames, cell_mask, counts, step_index)
    )

    def backward_micro(totals, sliced):
        frames_item, mask_item, count_item, step_item, grad_out, kept = sliced
        lifted, enc_kept, encoder_result, foreign, joined, dec_kept = kept
        dec_scale, dec_shift, one_hot = conditioning(step_item, dec_step_table)
        grad_joined, dec_grads, dec_gscale, dec_gshift = block_backward(
            joined, dec_weights, dec_scale, dec_shift, dec_kept, grad_out
        )
        grad_skip_weight = jnp.einsum("hwk,hwc->kc", joined, grad_out, precision=HIGH)
        grad_skip_bias = jnp.sum(grad_out, axis=(0, 1))
        grad_joined = grad_joined + jnp.dot(grad_out, skip_weight.T, precision=HIGH)
        half_width = joined.shape[-1] // 2
        grad_raised = grad_joined[..., :half_width]
        grad_encoded = grad_joined[..., half_width:]
        grad_foreign_up = from_behind(grad_raised, "section", 1)
        up_pull = jax.vjp(upsample, foreign, up_weight, up_bias)[1](grad_foreign_up)
        coarse_gradient = from_behind(up_pull[0], "section", 1)
        reducer_pullback = jax.vjp(coarsen_field, encoder_result, reducer_weight, reducer_bias)[1](
            coarse_gradient
        )
        grad_encoded = grad_encoded + reducer_pullback[0]
        enc_scale, enc_shift, enc_hot = conditioning(step_item, enc_step_table)
        grad_lifted, enc_grads, enc_gscale, enc_gshift = block_backward(
            lifted, enc_weights, enc_scale, enc_shift, enc_kept, grad_encoded
        )
        grad_lifted = grad_lifted + grad_encoded
        proj_pull = jax.vjp(
            lambda frames_in, incoming_weight, incoming_bias: project_in(
                frames_in, mask_item, count_item, incoming_weight, incoming_bias
            ),
            frames_item,
            lift_weight,
            lift_bias,
        )[1](grad_lifted)
        enc_table_grad = enc_hot[:, None] * jnp.concatenate([enc_gscale, enc_gshift])[None, :]
        dec_table_grad = one_hot[:, None] * jnp.concatenate([dec_gscale, dec_gshift])[None, :]
        micro_list = (
            proj_pull[1],
            proj_pull[2],
            enc_grads[0],
            enc_grads[1],
            enc_grads[2],
            enc_table_grad,
            enc_grads[3],
            enc_grads[4],
            enc_grads[5],
            enc_grads[6],
            reducer_pullback[1],
            reducer_pullback[2],
            up_pull[1],
            up_pull[2],
            dec_grads[0],
            dec_grads[1],
            dec_grads[2],
            dec_table_grad,
            dec_grads[3],
            dec_grads[4],
            dec_grads[5],
            dec_grads[6],
            grad_skip_weight,
            grad_skip_bias,
        )
        micro_flat = flatten_all(micro_list)
        return (totals + micro_flat, proj_pull[0])

    total_size = sum((piece.size for piece in params))
    start_totals = jnp.zeros((total_size,), jnp.float32)
    flat_totals, frames_grad = lax.scan(
        backward_micro,
        start_totals,
        (frames, cell_mask, counts, step_index, cotangent, kept_all),
        reverse=True,
    )
    flat_totals = lax.psum(flat_totals, ("section", "batch", "rows"))
    grads = unflatten_all(flat_totals, params)
    return (output, frames_grad) + grads


F32 = jnp.float32
BF16 = jnp.bfloat16
MESH = pl.DeviceIdType.MESH
NN = ((1,), (0,))
NT = ((1,), (1,))
TN = ((0,), (0,))
HIGH_AT = (0, 2, 1)
LOW_AT = (4, 3, 5)
CHUNK = 512
class Given(NamedTuple):
    frames: Any
    counts: Any
    cell_mask: Any
    step_index: Any
    lift_weight: Any
    lift_bias: Any
    enc_norm1_gain: Any
    enc_norm1_bias: Any
    enc_conv1: Any
    enc_step_table: Any
    enc_norm2_gain: Any
    enc_norm2_bias: Any
    enc_conv2: Any
    enc_conv2_bias: Any
    reducer_weight: Any
    reducer_bias: Any
    up_weight: Any
    up_bias: Any
    dec_norm1_gain: Any
    dec_norm1_bias: Any
    dec_conv1: Any
    dec_step_table: Any
    dec_norm2_gain: Any
    dec_norm2_bias: Any
    dec_conv2: Any
    dec_conv2_bias: Any
    skip_weight: Any
    skip_bias: Any
    cotangent: Any


ARGUMENTS = Given._fields
LARGE = tuple(
    dict(
        dec_conv1=0,
        up_weight=0,
        reducer_weight=0,
        dec_conv2=0,
        skip_weight=0,
        enc_conv1=0,
        enc_conv2=0,
    )
)
IN_HBM = tuple(dict(frames=0, cell_mask=0, cotangent=0)) + LARGE
IN_SMEM = tuple(dict(counts=0, step_index=0))
LATE = 64
SMALL_ROWS = dict(
    enc_conv2_bias=(0, 1),
    reducer_bias=(1, 1),
    up_bias=(2, 1),
    dec_conv2_bias=(3, 1),
    skip_bias=(3, 1),
    dec_norm1_gain=(4, 2),
    dec_norm1_bias=(6, 2),
    dec_norm2_gain=(8, 1),
    dec_norm2_bias=(9, 1),
    dec_step_table=(16, 8),
    lift_weight=(LATE, 12),
    lift_bias=(LATE + 12, 1),
    enc_norm1_gain=(LATE + 16, 1),
    enc_norm1_bias=(LATE + 17, 1),
    enc_norm2_gain=(LATE + 18, 1),
    enc_norm2_bias=(LATE + 19, 1),
    enc_step_table=(LATE + 24, 8),
)
LATE_COUNT = 32
SMALL_COUNT = LATE + LATE_COUNT
DUE = ((), (), (), (), (), (0,), (), (1,), (), (), (2,), (3, 0), (), (), (1,), (), (), (2,), (0,), (1, 4, 3), (2,), (), (), (5, 0), (1, 3), (4, 2), (), (6,), (7, 3, 0, 5, 4, 1, 2))
REST = (6, 3, 7, 4, 5, 6, 8, 7, 0, 4, 5, 1, 6, 7, 2, 0, 1, 5, 3, 6, 2, 8, 7, 3, 4, 5, 4, 6, 7, 5, 6, 7)
OUTPUTS = tuple(dict(output=0, frames_grad=0, gradients=0))


def split(value):
    high = value.astype(BF16)
    return high, (value - high.astype(F32)).astype(BF16)


def dot(left, right, dims=NN, precision=None):
    return lax.dot_general(
        left, right, (dims, ((), ())), precision=precision, preferred_element_type=F32
    )


def fold(value):
    half = value.shape[1] // 2
    return value[:, :half] + value[:, half:]


def fold_rows(value):
    half = value.shape[0] // 2
    return value[:half] + value[half:]


def tile_sums(value):
    return jnp.sum(value.reshape(-1, 8, value.shape[-1]), axis=0)


def column_sum(tiles):
    return jnp.sum(tiles, axis=0, keepdims=True)


def normal(value):
    bell = jnp.exp(-0.5 * value * value)
    t = 1.0 / (1.0 + 0.2316418882663604 * jnp.abs(value))
    poly = 0.5307027145
    for factor in (-0.7265760135, 0.7107068705, -0.142248368, 0.127414796):
        poly = poly * t + factor
    tail = poly * t * bell
    return jnp.where(value < 0.0, tail, 1.0 - tail), 0.3989422804014327 * bell


def dot_three(left, right, dims=NN):
    left_high, left_low = split(left)
    right_high, right_low = split(right)
    total = dot(left_high, right_high, dims)
    return total + (dot(left_high, right_low, dims) + dot(left_low, right_high, dims))


def group_ones(channels, size):
    rows = lax.broadcasted_iota(jnp.int32, (channels, channels), 0) // size
    columns = lax.broadcasted_iota(jnp.int32, (channels, channels), 1) // size
    return (rows == columns).astype(BF16)


def group_sums(first, second, ones):
    terms = []
    rest = jnp.concatenate([first, second], axis=0)
    for _ in range(3):
        term = rest.astype(BF16)
        terms.append(term)
        rest = rest - term.astype(F32)
    both = dot(jnp.concatenate(terms, axis=0), ones)
    both = both[32:48] + both[16:32] + both[:16]
    return column_sum(both[:8]), column_sum(both[8:])


class Exchange:

    def __init__(self, place, start, rows, landing, first_sem):
        self.place, self.start, self.rows, self.landing = place, start, rows, landing
        self.sem = first_sem
        self.stage = 0
        self.copies = []
        self.waiting = []
        self.group = place.plane_group
        self.half = rows // 2
        self.base = start + place.core * self.half
        self._finish(self.half)

    def _finish(self, size):
        self.part = size // self.group.count
        self.own = self.base + self.group.here * self.part

    def count(self):
        return 2 + 2 * (self.group.count - 1) + 3

    def land_rows(self):
        return self.half + (self.group.count + 1) * self.part

    def _copy(self, source, target, device, only=None):
        place = self.place
        copy = pltpu.make_async_remote_copy(
            src_ref=source,
            dst_ref=target,
            send_sem=place.send.at[self.sem],
            recv_sem=place.recv.at[self.sem],
            device_id=device,
            device_id_type=MESH,
        )
        self.sem += 1
        if only is None:
            copy.start()
            self.waiting.append(copy)
        self.copies.append((copy, only))
        return copy

    def _wait(self):
        for copy in self.waiting:
            copy.wait_recv()
        self.waiting = []

    def _rows(self, at, size):
        return pl.ds(pl.multiple_of(at, 8), size)

    def _swap(self):
        place = self.place
        other = self._rows(self.start + (1 - place.core) * self.half, self.half)
        self.land = self.landing
        self.landing += self.half
        self._copy(
            place.sums.at[other], place.landing.at[pl.ds(self.land, self.half)], place.partner
        )

    def _add_swap(self):
        place = self.place
        block = 64 if self.half % 64 == 0 else 32

        def step(i, carry):
            here = self._rows(self.base + i * block, block)
            there = self._rows(self.land + i * block, block)
            place.sums[here] = place.sums[here] + place.landing[there]
            return carry

        lax.fori_loop(0, self.half // block, step, 0)

    def _scatter(self, group, base, size):
        place = self.place
        self.land = self.landing
        for k in range(1, group.count):
            to = lax.rem(group.here + k, group.count)
            self._copy(
                place.sums.at[self._rows(base + to * size, size)],
                place.landing.at[pl.ds(self.landing, size)],
                group.device(to),
            )
            self.landing += size

    def _total(self, group, own, size, target):
        place = self.place
        block = 16 if size % 16 == 0 else 8

        def step(i, carry):
            here = self._rows(own + i * block, block)
            total = place.sums[here]
            for k in range(group.count - 1):
                there = self._rows(self.land + k * size + i * block, block)
                total = total + place.landing[there]
            target[here] = total
            return carry

        lax.fori_loop(0, size // block, step, 0)

    def _gather(self, group, own, size):
        final = self.place.final
        here = self._rows(own, size)
        for k in range(1, group.count):
            to = lax.rem(group.here + k, group.count)
            self._copy(final.at[here], final.at[here], group.device(to))

    def _steps(self):
        place, group = self.place, self.group
        yield self._swap()
        self._wait()
        self._add_swap()
        yield from self._both()
        final = place.final
        here = self._rows(self.base, self.half)
        self._copy(final.at[here], final.at[here], place.partner)
        yield
        self._wait()
        yield

    def _both(self):
        place, group = self.place, self.group
        self._scatter(group, self.base, self.part)
        yield
        self._wait()
        self._total(group, self.own, self.part, place.sums)
        yield from self._line()
        self._gather(group, self.own, self.part)
        yield
        self._wait()

    def _line(self):
        place, line = self.place, self.place.line
        sums, final, landing = place.sums, place.final, place.landing
        part, own = self.part, self._rows(self.own, self.part)
        inward, across = pl.ds(self.landing, part), pl.ds(self.landing + part, part)
        self.landing += 2 * part
        block = 16 if part % 16 == 0 else 8

        def add(at, target):
            def step(i, carry):
                here = self._rows(self.own + i * block, block)
                target[here] = sums[here] + landing[pl.ds(at + i * block, block)]
                return carry

            lax.fori_loop(0, part // block, step, 0)

        first = self._copy(sums.at[own], landing.at[inward], line.device(line.inner), line.edge)
        second = self._copy(sums.at[own], landing.at[across], line.device(line.across), line.middle)
        third = self._copy(final.at[own], final.at[own], line.device(line.outer), line.middle)
        pl.when(line.edge)(first.start)
        yield

        @pl.when(line.middle)
        def _():
            first.wait_recv()
            add(self.landing - 2 * part, sums)
            second.start()

        yield

        @pl.when(line.middle)
        def _():
            second.wait_recv()
            add(self.landing - part, final)
            third.start()

        yield
        pl.when(line.edge)(third.wait_recv)

    def advance(self):
        if self.stage == 0:
            self.steps = self._steps()
        self.stage += 1
        next(self.steps)

    def done(self):
        return self.stage == 8


class SmallExchange(Exchange):

    def count(self):
        return self.place.cores_group.count + self.place.line.count - 2

    def land_rows(self):
        return self.rows * (self.place.cores_group.count + self.place.line.count)

    def _share(self, group, source):
        place = self.place
        self.land = self.landing
        self.landing += group.count * self.rows
        own = self._rows(self.land + group.here * self.rows, self.rows)
        place.landing[own] = source[...]
        for k in range(1, group.count):
            to = lax.rem(group.here + k, group.count)
            self._copy(source, place.landing.at[own], group.device(to))

    def _sum(self, group):
        total = None
        for k in range(group.count):
            part = self.place.landing[pl.ds(self.land + k * self.rows, self.rows)]
            total = part if total is None else total + part
        return total

    def _steps(self):
        place = self.place
        here = pl.ds(self.start, self.rows)
        self._share(place.line, place.sums.at[here])
        yield
        self._wait()
        place.small[...] = self._sum(place.line)
        self._share(place.cores_group, place.small)
        yield
        self._wait()
        place.final[here] = self._sum(place.cores_group)
        yield

    def done(self):
        return self.stage == 3


def layout_of(shapes):
    starts = {}
    at = 0
    for name in LARGE:
        starts[name] = at
        at += getattr(shapes, name)[0]
    small = at
    begins = SimpleNamespace(**starts)
    late = small + LATE
    tap = shapes.dec_conv2[0] // 3
    part = shapes.dec_conv1[0] // 3
    conv1, up = begins.dec_conv1, begins.up_weight
    edges = (
        (begins.dec_conv2, begins.enc_conv1),
        (conv1, conv1 + part),
        (conv1 + part, conv1 + 2 * part),
        (conv1 + 2 * part, up),
        (up, begins.dec_conv2),
        (begins.enc_conv2, late),
        (begins.enc_conv1, begins.enc_conv1 + 2 * tap),
        (begins.enc_conv1 + 2 * tap, begins.enc_conv2),
        (late, late + LATE_COUNT),
    )
    runs = [(first, last - first) for first, last in edges]
    return starts, small, late + LATE_COUNT, runs


def item_kernel(sizes, scratch_names, *refs):
    line, strip, width, shapes, big_layout = sizes
    begins, small_at, total_rows, runs = big_layout
    starts = SimpleNamespace(**begins)
    inputs = Given(*refs[: len(ARGUMENTS)])
    refs = refs[len(ARGUMENTS) :]
    output_names = OUTPUTS
    outputs = SimpleNamespace(**dict(zip(output_names, refs)))
    scratch = SimpleNamespace(**dict(zip(scratch_names, refs[len(output_names) :])))

    def w_of(name):
        return getattr(scratch, name)

    height = strip * line
    cells = height * width
    c = inputs.lift_weight.shape[1]
    strip_cells = strip * width
    history = inputs.frames.shape[1]

    core = lax.axis_index("section")
    plane = lax.axis_index("batch")
    row = lax.axis_index("rows")
    middle = lax.rem(row + 1, 4) // 2

    def device_at(to):
        return (core, plane, to)

    place = SimpleNamespace(
        core=core,
        partner=(1 - core, plane, row),
        line=SimpleNamespace(
            count=line,
            here=row,
            device=device_at,
            middle=middle == 1,
            edge=middle == 0,
            inner=1 + row // 2,
            across=3 - row,
            outer=3 * (row // 2),
        ),
        plane_group=SimpleNamespace(
            count=4, here=plane, device=lambda to: (core, to, row)
        ),
        cores_group=SimpleNamespace(
            count=8,
            here=core * 4 + plane,
            device=lambda to: (to // 4, lax.rem(to, 4), row),
        ),
        small=scratch.small,
        sums=scratch.sums,
        final=scratch.final,
        landing=scratch.landing,
        send=scratch.send,
        recv=scratch.recv,
    )
    local_sem = scratch.local

    weight_copies = {}
    for k, name in enumerate(LARGE):
        copy = pltpu.make_async_copy(getattr(inputs, name), w_of(name), local_sem.at[k])
        weight_copies[name] = copy
        copy.start()
    frames_in, mask_in, cot = scratch.frames_in, scratch.mask_in, scratch.cot
    here_rows = pl.ds(pl.multiple_of(row * strip_cells, strip_cells), strip_cells)
    own = (
        pltpu.make_async_copy(inputs.frames.at[row], frames_in.at[row], local_sem.at[7]),
        pltpu.make_async_copy(inputs.cell_mask.at[row], mask_in.at[row], local_sem.at[8]),
        pltpu.make_async_copy(
            inputs.cotangent.at[row], cot.at[here_rows], local_sem.at[9]
        ),
    )
    for copy in own:
        copy.start()

    barrier = pltpu.get_barrier_semaphore()
    peers = [device_at(lax.rem(row + k, line)) for k in range(1, line)]
    cores_group = place.cores_group
    for k in range(1, 8):
        peers.append(cores_group.device(lax.rem(cores_group.here + k, 8)))
    for device in peers:
        pl.semaphore_signal(barrier, inc=1, device_id=device, device_id_type=MESH)
    pl.semaphore_wait(barrier, len(peers))

    next_sem = 0

    def send(source, target, device):
        nonlocal next_sem
        copy = pltpu.make_async_remote_copy(
            src_ref=source,
            dst_ref=target,
            send_sem=scratch.send.at[next_sem],
            recv_sem=scratch.recv.at[next_sem],
            device_id=device,
            device_id_type=MESH,
        )
        next_sem += 1
        copy.start()
        return copy

    frame_copies, cot_copies, output_copies = [], [], []
    for k in range(1, line):
        to = lax.rem(row + k, line)
        device = device_at(to)
        frame_copies.append(send(inputs.frames.at[to], frames_in.at[row], device))
        frame_copies.append(send(inputs.cell_mask.at[to], mask_in.at[row], device))
    for k in range(1, line):
        to = lax.rem(row + k, line)
        cot_copies.append(
            send(inputs.cotangent.at[to], cot.at[here_rows], device_at(to))
        )

    copied = SimpleNamespace(**weight_copies)
    def stack_conv(source, half, depth, forward, backward):
        for a in range(3):
            for b in range(3):
                at = (3 * a + b) * depth + half * c
                high, low = split(source[at : at + c, :])
                for block in (HIGH_AT[b], LOW_AT[b]):
                    rows = slice((6 * a + block) * c, (6 * a + block + 1) * c)
                    forward[rows, 0:c] = high
                    forward[rows, c : 2 * c] = low
                for block in (HIGH_AT[2 - b], LOW_AT[2 - b]):
                    tap = 6 * (2 - a) + block
                    columns = slice(tap * c, (tap + 1) * c)
                    backward[0:c, columns] = high
                    backward[c : 2 * c, columns] = low

    copied.enc_conv1.wait()
    stack_conv(scratch.enc_conv1, 0, c, scratch.fe1, scratch.be1)
    copied.enc_conv2.wait()
    stack_conv(scratch.enc_conv2, 0, c, scratch.fe2, scratch.be2)
    copied.reducer_weight.wait()
    for k in range(4):
        high, low = split(scratch.reducer_weight[k * c : (k + 1) * c, :])
        for block in (k, k + 4):
            scratch.f_down[block * c : (block + 1) * c, 0:c] = high
            scratch.f_down[block * c : (block + 1) * c, c : 2 * c] = low
        for block in (0, 1):
            columns = slice(block * c, (block + 1) * c)
            scratch.b_down[k, 0:c, columns] = high
            scratch.b_down[k, c : 2 * c, columns] = low
    copied.up_weight.wait()
    for k in range(4):
        high, low = split(scratch.up_weight[k * c : (k + 1) * c, :])
        for block in (0, 1):
            rows = slice(block * c, (block + 1) * c)
            scratch.f_up[k, rows, 0:c] = high
            scratch.f_up[k, rows, c : 2 * c] = low
        for block in (k, k + 4):
            columns = slice(block * c, (block + 1) * c)
            scratch.b_up[0:c, columns] = high
            scratch.b_up[c : 2 * c, columns] = low
    copied.dec_conv1.wait()
    stack_conv(scratch.dec_conv1, 0, 2 * c, scratch.fd1a, scratch.bd1a)
    stack_conv(scratch.dec_conv1, 1, 2 * c, scratch.fd1b, scratch.bd1b)
    copied.dec_conv2.wait()
    stack_conv(scratch.dec_conv2, 0, c, scratch.fd2, scratch.bd2)
    copied.skip_weight.wait()
    for half in range(2):
        high, low = split(scratch.skip_weight[half * c : (half + 1) * c, :])
        for block in (half, half + 2):
            scratch.f_skip[block * c : (block + 1) * c, 0:c] = high
            scratch.f_skip[block * c : (block + 1) * c, c : 2 * c] = low
        for block in (0, 1):
            columns = slice(block * c, (block + 1) * c)
            scratch.b_skip[half, 0:c, columns] = high
            scratch.b_skip[half, c : 2 * c, columns] = low

    for buffer in (scratch.xe1, scratch.xe2, scratch.xd1a, scratch.xd1b, scratch.xd2, scratch.xg):
        edge = jnp.zeros((width, 6 * c), BF16)
        buffer[0:width, :] = edge
        buffer[cells + width : cells + 2 * width, :] = edge

    lift = scratch.lift
    lift[...] = jnp.zeros(lift.shape, F32)
    lift[0:history, :] = inputs.lift_weight[...]
    lift[history : history + 1, :] = inputs.lift_bias[...]

    block = 2 * width
    column = lax.rem(lax.broadcasted_iota(jnp.int32, (block, c), 0), width)
    at_first, at_last = column == 0, column == width - 1
    zeros8 = jnp.zeros((8, c), F32)
    ones16 = group_ones(c, c // GROUPS)
    ones32 = group_ones(c, 2 * c // GROUPS)
    count16 = float(cells * (c // GROUPS))
    count32 = float(cells * (2 * c // GROUPS))

    def grid_rows(step, carry=0):
        return lax.fori_loop(0, cells // block, step, carry, unroll=2)

    def row_at(h):
        return pl.ds(pl.multiple_of(h * block, block), block)

    def chunk_at(i):
        return pl.ds(pl.multiple_of(i * CHUNK, CHUNK), CHUNK)

    def put_row(target, h, value):
        rows = pl.ds(pl.multiple_of(h * block + width, width), block)
        left = jnp.where(at_first, 0.0, pltpu.roll(value, 1, 0))
        right = jnp.where(at_last, 0.0, pltpu.roll(value, block - 1, 0))
        for b, piece in enumerate((left, value, right)):
            high, low = split(piece)
            target[rows, HIGH_AT[b] * c : (HIGH_AT[b] + 1) * c] = high
            target[rows, LOW_AT[b] * c : (LOW_AT[b] + 1) * c] = low

    def put_turned(target, columns, value, first=0, second=1):
        high, low = split(value.T)
        target[first * c : (first + 1) * c, columns] = high
        target[second * c : (second + 1) * c, columns] = low

    def conv_chunk(pairs, i, dims=NN):
        total = None
        for data, weight in pairs:
            taps = []
            for a in range(3):
                rows = pl.ds(pl.multiple_of(i * CHUNK + a * width, width), CHUNK)
                taps.append(data[rows, :])
            part = dot(jnp.concatenate(taps, axis=1), weight[...], dims)
            total = part if total is None else total + part
        return total

    def norm_of(first, second, ones, count):
        one, two = group_sums(first, second, ones)
        mean = one / count
        return mean, lax.rsqrt(two / count - mean * mean + EPS)

    def activate(source, target, turned, slope, scale, shift):
        def step(h, carry):
            value = source[row_at(h), :] * scale + shift
            below, density = normal(value)
            slope[row_at(h), :] = below + value * density
            value = value * below
            put_row(target, h, value)
            put_turned(turned, row_at(h), value)
            return carry

        grid_rows(step)

    def conv_norm(pairs, target):
        def step(i, carry):
            value = fold(conv_chunk(pairs, i))
            target[chunk_at(i), :] = value
            return carry[0] + tile_sums(value), carry[1] + tile_sums(value * value)

        return lax.fori_loop(0, cells // CHUNK, step, (zeros8, zeros8))

    def sums_of(source):
        def step(h, carry):
            value = source[row_at(h), :]
            return carry[0] + tile_sums(value), carry[1] + tile_sums(value * value)

        return grid_rows(step, (zeros8, zeros8))

    step_here = jnp.full((1, c), inputs.step_index[row], jnp.int32)

    def condition(table):
        total = jnp.zeros((1, 2 * c), F32)
        chosen = jnp.concatenate([step_here, step_here], axis=1)
        for s in range(table.shape[0]):
            total = total + jnp.where(chosen == s, table[s : s + 1, :], 0.0)
        return total[:, :c], total[:, c:]

    for copy in own[:2]:
        copy.wait()
    for copy in frame_copies:
        copy.wait_recv()
    fields = scratch.fields
    fields[...] = jnp.zeros(fields.shape, F32)
    frame_of = lax.broadcasted_iota(jnp.int32, (history, width), 0) // FIELDS
    keep = (frame_of >= HIST - inputs.counts[row]).astype(F32)
    masks = []
    for source in range(line):
        for k in range(strip):
            columns = slice((source * strip + k) * width, (source * strip + k + 1) * width)
            mask = mask_in[source, k : k + 1, :].astype(F32)
            masks.append(mask)
            fields[0:history, columns] = frames_in[source, :, k, :] * keep * mask
            fields[history : history + 1, columns] = mask
    lifted = scratch.lifted
    lifted[...] = dot_three(fields[...], lift[...], TN)

    enc_scale, enc_shift = condition(inputs.enc_step_table)
    dec_scale, dec_shift = condition(inputs.dec_step_table)

    mean_e1, inv_e1 = norm_of(*sums_of(lifted), ones16, count16)
    gain_e1, bias_e1 = inputs.enc_norm1_gain[...], inputs.enc_norm1_bias[...]
    a_e1 = inv_e1 * gain_e1
    activate(lifted, scratch.xe1, scratch.te1, scratch.slope_e1, a_e1, bias_e1 - mean_e1 * a_e1)
    middle_e = scratch.middle_e
    mean_e2, inv_e2 = norm_of(
        *conv_norm([(scratch.xe1, scratch.fe1)], middle_e), ones16, count16
    )
    gain_e2, bias_e2 = inputs.enc_norm2_gain[...], inputs.enc_norm2_bias[...]
    a_e2 = inv_e2 * gain_e2
    activate(
        middle_e,
        scratch.xe2,
        scratch.te2,
        scratch.slope_e2,
        a_e2 * (1.0 + enc_scale),
        (bias_e2 - mean_e2 * a_e2) * (1.0 + enc_scale) + enc_shift,
    )
    encoded = scratch.encoded
    conv2_bias = inputs.enc_conv2_bias[...]
    joined = scratch.joined

    def encode(i, carry):
        value = fold(conv_chunk([(scratch.xe2, scratch.fe2)], i))
        value = value + conv2_bias + lifted[chunk_at(i), :]
        encoded[chunk_at(i), :] = value
        high, low = split(value)
        joined[chunk_at(i), c : 2 * c] = high
        joined[chunk_at(i), 3 * c : 4 * c] = low
        put_turned(scratch.turned, chunk_at(i), value, 1, 3)
        return carry[0] + tile_sums(value), carry[1] + tile_sums(value * value)

    sums_enc = lax.fori_loop(0, cells // CHUNK, encode, (zeros8, zeros8))

    half_cells, quarter = cells // 2, cells // 4

    def pick(source):
        pieces = []
        for b in range(2):
            value = source[pl.ds(b, half_cells, stride=2), :]
            value = value.reshape(height // 2, 2, width // 2, c)
            pieces.append([value[:, a].reshape(quarter, c) for a in range(2)])
        return [pieces[b][a] for a in range(2) for b in range(2)]

    def place_cells(target, pieces):
        for b in range(2):
            both = [pieces[2 * a + b].reshape(height // 2, 1, width // 2, c) for a in range(2)]
            value = jnp.concatenate(both, axis=1).reshape(half_cells, c)
            target[pl.ds(b, half_cells, stride=2), :] = value

    x_down = scratch.x_down
    for k, piece in enumerate(pick(encoded)):
        high, low = split(piece)
        x_down[:, k * c : (k + 1) * c] = high
        x_down[:, (k + 4) * c : (k + 5) * c] = low
    lowered = fold(dot(x_down[...], scratch.f_down[...])) + inputs.reducer_bias[...]
    x_up = scratch.x_up
    high, low = split(lowered)
    x_up[:, 0:c] = high
    x_up[:, c : 2 * c] = low
    raised = scratch.raised
    up_bias = inputs.up_bias[...]
    place_cells(
        raised, [fold(dot(x_up[...], scratch.f_up[k])) + up_bias for k in range(4)]
    )

    def raise_row(h, carry):
        value = raised[row_at(h), :]
        high, low = split(value)
        joined[row_at(h), 0:c] = high
        joined[row_at(h), 2 * c : 3 * c] = low
        put_turned(scratch.turned, row_at(h), value, 0, 2)
        return carry[0] + tile_sums(value), carry[1] + tile_sums(value * value)

    sums_raised = grid_rows(raise_row, (zeros8, zeros8))

    halves = []
    for half, (source, sums) in enumerate(((raised, sums_raised), (encoded, sums_enc))):
        mean, inv = norm_of(*sums, ones32, count32)
        gain = inputs.dec_norm1_gain[half : half + 1, :]
        bias = inputs.dec_norm1_bias[half : half + 1, :]
        scale = inv * gain
        activate(
            source,
            (scratch.xd1a, scratch.xd1b)[half],
            (scratch.td1a, scratch.td1b)[half],
            (scratch.slope_d1a, scratch.slope_d1b)[half],
            scale,
            bias - mean * scale,
        )
        halves.append((source, mean, inv, gain))
    middle_d = scratch.middle_d
    pairs = [(scratch.xd1a, scratch.fd1a), (scratch.xd1b, scratch.fd1b)]
    mean_d2, inv_d2 = norm_of(*conv_norm(pairs, middle_d), ones16, count16)
    gain_d2, bias_d2 = inputs.dec_norm2_gain[...], inputs.dec_norm2_bias[...]
    a_d2 = inv_d2 * gain_d2
    activate(
        middle_d,
        scratch.xd2,
        scratch.td2,
        scratch.slope_d2,
        a_d2 * (1.0 + dec_scale),
        (bias_d2 - mean_d2 * a_d2) * (1.0 + dec_scale) + dec_shift,
    )
    result = scratch.result
    last_bias = inputs.dec_conv2_bias[...] + inputs.skip_bias[...]

    def decode(i, carry):
        value = conv_chunk([(scratch.xd2, scratch.fd2)], i)
        value = value + dot(joined[chunk_at(i), :], scratch.f_skip[...])
        result[chunk_at(i), :] = fold(value) + last_bias
        return carry

    lax.fori_loop(0, cells // CHUNK, decode, 0)
    own_output = pltpu.make_async_copy(
        result.at[here_rows], outputs.output.at[row], local_sem.at[10]
    )
    own_output.start()
    for k in range(1, line):
        to = lax.rem(row + k, line)
        there = pl.ds(pl.multiple_of(to * strip_cells, strip_cells), strip_cells)
        output_copies.append(
            send(result.at[there], outputs.output.at[row], device_at(to))
        )

    exchanges = []
    waiting_runs = list(runs)
    landing_at = 0
    sem_at = 4 * (line - 1) + 2 * (line - 1)
    sums, final = scratch.sums, scratch.final

    def begin():
        nonlocal landing_at, sem_at
        start, rows = waiting_runs.pop(0)
        kind = Exchange if waiting_runs else SmallExchange
        exchange = kind(place, start, rows, landing_at, sem_at)
        landing_at += exchange.land_rows()
        sem_at += exchange.count()
        exchanges.append(exchange)
        exchange.advance()

    final_copies = []

    def advance(k):
        exchange = exchanges[k]
        exchange.advance()
        if exchange.done():
            rows = pl.ds(exchange.start, exchange.rows)
            copy = pltpu.make_async_copy(
                final.at[rows], outputs.gradients.at[rows], local_sem.at[11 + k]
            )
            copy.start()
            final_copies.append(copy)

    due = list(DUE)

    def point():
        for k in due.pop(0):
            advance(k)

    def small_row(k, value):
        sums[small_at + k : small_at + k + 1, :] = value

    def spread_grad(source):
        def step(h, carry):
            value = source[row_at(h), :]
            put_row(scratch.xg, h, value)
            return carry + tile_sums(value)

        return grid_rows(step, zeros8)

    def weight_grad(turned, at, depth, a):
        rows = pl.ds((2 - a) * width, cells)
        part = fold_rows(dot(turned[...], scratch.xg[rows, :]))
        for b in range(3):
            high, low = HIGH_AT[2 - b] * c, LOW_AT[2 - b] * c
            to = at + (3 * a + b) * depth
            sums[to : to + c, :] = part[:, high : high + c] + part[:, low : low + c]

    def back_conv(weight, slope, target, source, mean, inv):
        carry = (zeros8, zeros8)
        for i in range(cells // CHUNK):
            value = fold(conv_chunk([(scratch.xg, weight)], i, NT)) * slope[chunk_at(i), :]
            target[chunk_at(i), :] = value
            normed = (source[chunk_at(i), :] - mean) * inv
            carry = (carry[0] + tile_sums(value), carry[1] + tile_sums(value * normed))
            if i % (cells // CHUNK // 2) == cells // CHUNK // 2 - 1:
                point()
        return carry

    def norm_grad(sums_in, scale, ones, count):
        one, two = group_sums(sums_in[0] * scale, sums_in[1] * scale, ones)
        return one / count, two / count

    own[2].wait()
    for copy in cot_copies:
        copy.wait_recv()
    total_cot = column_sum(spread_grad(cot))
    for a in range(3):
        weight_grad(scratch.td2, starts.dec_conv2, c, a)
    part = fold(dot(scratch.turned[...], scratch.xg[width : cells + width, 2 * c : 4 * c]))
    sums[starts.skip_weight : starts.skip_weight + 2 * c, :] = fold_rows(part)
    small_row(3, total_cot)
    begin()

    grad = scratch.grad
    sums_d2 = back_conv(scratch.bd2, scratch.slope_d2, grad, middle_d, mean_d2, inv_d2)
    side_grads = (scratch.grad_a, scratch.grad_b)
    for half in range(2):

        def skip_back(i, carry, half=half):
            rows = pl.ds(pl.multiple_of(i * CHUNK + width, width), CHUNK)
            value = dot(scratch.xg[rows, 2 * c : 4 * c], scratch.b_skip[half], NT)
            side_grads[half][chunk_at(i), :] = fold(value)
            return carry

        lax.fori_loop(0, cells // CHUNK, skip_back, 0)
    point()

    def table_rows(k, sums_in, gain, bias, one_plus):
        plain, times = column_sum(sums_in[0]), column_sum(sums_in[1])
        for s in range(inputs.enc_step_table.shape[0]):
            small_row(k + 2 * s, jnp.where(step_here == s, gain * times + bias * plain, 0.0))
            small_row(k + 2 * s + 1, jnp.where(step_here == s, plain, 0.0))
        return one_plus * times, one_plus * plain

    def middle_grad(source, mean, inv, scale, sums_in):
        zero, slope = norm_grad(sums_in, scale, ones16, count16)

        def step(h, carry):
            normed = (source[row_at(h), :] - mean) * inv
            value = inv * (grad[row_at(h), :] * scale - zero - normed * slope)
            put_row(scratch.xg, h, value)
            return carry

        grid_rows(step)

    gain_row, bias_row = table_rows(16, sums_d2, gain_d2, bias_d2, 1.0 + dec_scale)
    small_row(8, gain_row)
    small_row(9, bias_row)
    middle_grad(middle_d, mean_d2, inv_d2, gain_d2 * (1.0 + dec_scale), sums_d2)
    point()
    for a in range(3):
        weight_grad(scratch.td1a, starts.dec_conv1, 2 * c, a)
        weight_grad(scratch.td1b, starts.dec_conv1 + c, 2 * c, a)
        point()
        begin()

    for half, (source, mean, inv, gain) in enumerate(halves):
        sums_in = back_conv(
            (scratch.bd1a, scratch.bd1b)[half],
            (scratch.slope_d1a, scratch.slope_d1b)[half],
            grad,
            source,
            mean,
            inv,
        )
        small_row(4 + half, column_sum(sums_in[1]))
        small_row(6 + half, column_sum(sums_in[0]))
        zero, slope = norm_grad(sums_in, gain, ones32, count32)
        target = side_grads[half]

        def input_grad(h, carry):
            normed = (source[row_at(h), :] - mean) * inv
            value = inv * (grad[row_at(h), :] * gain - zero - normed * slope)
            value = target[row_at(h), :] + value
            target[row_at(h), :] = value
            return carry + tile_sums(value)

        total = grid_rows(input_grad, zeros8)
        if half == 0:
            small_row(2, column_sum(total))
        point()

    grad_raised, grad_encoded = side_grads
    x_grad_up = scratch.x_grad_up
    for k, piece in enumerate(pick(grad_raised)):
        high, low = split(piece)
        x_grad_up[:, k * c : (k + 1) * c] = high
        x_grad_up[:, (k + 4) * c : (k + 5) * c] = low
    grad_lowered = fold(dot(x_grad_up[...], scratch.b_up[...], NT))
    small_row(1, jnp.sum(grad_lowered, axis=0, keepdims=True))
    x_grad_low = scratch.x_grad_low
    high, low = split(grad_lowered)
    x_grad_low[:, 0:c] = high
    x_grad_low[:, c : 2 * c] = low
    point()
    part = fold(fold_rows(dot(x_up[...], x_grad_up[...], TN)))
    for k in range(4):
        at = starts.up_weight + k * c
        sums[at : at + c, :] = part[:, k * c : (k + 1) * c]
    part = fold_rows(fold(dot(x_down[...], x_grad_low[...], TN)))
    sums[starts.reducer_weight : starts.reducer_weight + 4 * c, :] = part
    point()
    begin()
    place_cells(
        grad, [fold(dot(x_grad_low[...], scratch.b_down[k], NT)) for k in range(4)]
    )

    def join_row(h, carry):
        value = grad_encoded[row_at(h), :] + grad[row_at(h), :]
        grad_encoded[row_at(h), :] = value
        put_row(scratch.xg, h, value)
        return carry + tile_sums(value)

    small_row(0, column_sum(grid_rows(join_row, zeros8)))
    for k in range(10, 16):
        small_row(k, jnp.zeros((1, c), F32))
    sums[small_at + 24 : small_at + LATE, :] = jnp.zeros((LATE - 24, c), F32)
    point()
    for a in range(3):
        weight_grad(scratch.te2, starts.enc_conv2, c, a)
        point()
    begin()
    sums_e2 = back_conv(scratch.be2, scratch.slope_e2, grad, middle_e, mean_e2, inv_e2)
    gain_row, bias_row = table_rows(LATE + 24, sums_e2, gain_e2, bias_e2, 1.0 + enc_scale)
    small_row(LATE + 18, gain_row)
    small_row(LATE + 19, bias_row)
    middle_grad(middle_e, mean_e2, inv_e2, gain_e2 * (1.0 + enc_scale), sums_e2)
    point()
    for a in range(3):
        weight_grad(scratch.te1, starts.enc_conv1, c, a)
        point()
        if a:
            begin()
    sums_e1 = back_conv(scratch.be1, scratch.slope_e1, grad, lifted, mean_e1, inv_e1)
    small_row(LATE + 16, column_sum(sums_e1[1]))
    small_row(LATE + 17, column_sum(sums_e1[0]))
    zero, slope = norm_grad(sums_e1, gain_e1, ones16, count16)

    def lifted_grad(h, carry):
        normed = (lifted[row_at(h), :] - mean_e1) * inv_e1
        value = inv_e1 * (grad[row_at(h), :] * gain_e1 - zero - normed * slope)
        grad[row_at(h), :] = grad_encoded[row_at(h), :] + value
        return carry

    grid_rows(lifted_grad)
    point()

    late_at = small_at + LATE
    sums[late_at : late_at + 16, :] = dot_three(fields[...], grad[...])
    sums[late_at + 20 : late_at + 24, :] = jnp.zeros((4, c), F32)
    point()
    begin()
    back = dot_three(lift[...], grad[...], NT)
    frames_out = scratch.frames_out
    for source in range(line):
        for k in range(strip):
            h = source * strip + k
            value = back[0:history, h * width : (h + 1) * width]
            frames_out[source, :, k, :] = value * keep * masks[h]
    own_frames = pltpu.make_async_copy(
        frames_out.at[row], outputs.frames_grad.at[row], local_sem.at[11 + len(runs)]
    )
    own_frames.start()
    for k in range(1, line):
        to = lax.rem(row + k, line)
        output_copies.append(
            send(frames_out.at[to], outputs.frames_grad.at[row], device_at(to))
        )

    for k in REST:
        advance(k)
    assert not due and all(exchange.done() for exchange in exchanges)

    for copy in output_copies:
        copy.wait_recv()
    own_output.wait()
    own_frames.wait()
    for copy in final_copies:
        copy.wait()
    for copy in frame_copies + cot_copies + output_copies:
        copy.wait_send()
    for exchange in exchanges:
        for copy, only in exchange.copies:
            if only is None:
                copy.wait_send()
            else:
                pl.when(only)(copy.wait_send)


def write_kernel(layout, *refs):
    shapes, starts, small_at = layout
    output, frames_grad, gradients = refs[:3]
    outputs = refs[3:-4]
    output_here, frames_here, gradients_here, sem = refs[-4:]
    c = gradients.shape[1]
    moves = [(frames_grad, frames_here, outputs[1])]
    for k, name in enumerate(LARGE):
        rows = pl.ds(starts[name], shapes[name][0])
        moves.append((gradients.at[rows], gradients_here.at[rows], outputs[2 + k]))
    moves.append((output, output_here, outputs[0]))
    small = pl.ds(small_at, SMALL_COUNT)
    first = pltpu.make_async_copy(gradients.at[small], gradients_here.at[small], sem.at[0])
    first.start()
    arriving, leaving = [], []
    for k, (source, here, _) in enumerate(moves):
        arriving.append(pltpu.make_async_copy(source, here, sem.at[1 + 2 * k]))
        arriving[-1].start()
    first.wait()
    for target, (k, rows) in zip(outputs[2 + len(LARGE) :], SMALL_ROWS.values()):
        at = small_at + k
        if rows == 8:
            for s in range(target.shape[0]):
                target[s : s + 1, 0:c] = gradients_here[at + 2 * s : at + 2 * s + 1, :]
                target[s : s + 1, c : 2 * c] = gradients_here[at + 2 * s + 1 : at + 2 * s + 2, :]
        else:
            target[...] = gradients_here[at : at + rows, :]
    for k, (_, here, target) in enumerate(moves):
        arriving[k].wait()
        leaving.append(pltpu.make_async_copy(here, target, sem.at[2 + 2 * k]))
        leaving[-1].start()
    for copy in leaving:
        copy.wait()


def whole_items(shape, *arguments):
    line = shape["rows"]
    whole = Given(*arguments)
    given = whole._asdict()
    frames, cotangent = whole.frames, whole.cotangent
    items, history, strip, width = frames.shape
    c = cotangent.shape[-1]
    cells = strip * line * width
    flat = {}
    for name, value in given.items():
        if value is cotangent:
            value = value.reshape(items, strip * width, c)
        elif name in LARGE:
            value = value.reshape(-1, c)
        elif value.ndim == 1 and name not in IN_SMEM:
            value = value.reshape(-1, c)
        flat[name] = value
    shapes = {name: flat[name].shape for name in LARGE}
    big_layout = layout_of(SimpleNamespace(**shapes))
    starts, small_at, total_rows, runs = big_layout
    copies = 7 * (line - 1) + len(runs) * (8 + 2 * (line - 1)) + 6
    landing = sum(rows // 2 + 5 * rows // 8 for _, rows in runs) + LATE_COUNT * (8 + line)
    shifted = pltpu.VMEM((cells + 2 * width, 6 * c), BF16)
    forward = pltpu.VMEM((18 * c, 2 * c), BF16)
    backward = pltpu.VMEM((2 * c, 18 * c), BF16)
    field = pltpu.VMEM((cells, c), F32)
    flipped_field = pltpu.VMEM((2 * c, cells), BF16)
    quarter = cells // 4
    scratch = dict(
        small=pltpu.VMEM((LATE_COUNT, c), F32),
        send=pltpu.SemaphoreType.DMA((copies,)),
        recv=pltpu.SemaphoreType.DMA((copies,)),
        local=pltpu.SemaphoreType.DMA((12 + len(runs),)),
        sums=pltpu.VMEM((total_rows, c), F32),
        final=pltpu.VMEM((total_rows, c), F32),
        landing=pltpu.VMEM((landing, c), F32),
        frames_in=pltpu.VMEM((line, history, strip, width), F32),
        mask_in=pltpu.VMEM((line, strip, width), jnp.int32),
        frames_out=pltpu.VMEM((line, history, strip, width), F32),
        fields=pltpu.VMEM((16, cells), F32),
        lift=pltpu.VMEM((16, c), F32),
        joined=pltpu.VMEM((cells, 4 * c), BF16),
        x_down=pltpu.VMEM((quarter, 8 * c), BF16),
        x_grad_up=pltpu.VMEM((quarter, 8 * c), BF16),
        x_up=pltpu.VMEM((quarter, 2 * c), BF16),
        x_grad_low=pltpu.VMEM((quarter, 2 * c), BF16),
        f_down=pltpu.VMEM((8 * c, 2 * c), BF16),
        b_down=pltpu.VMEM((4, 2 * c, 2 * c), BF16),
        f_up=pltpu.VMEM((4, 2 * c, 2 * c), BF16),
        b_up=pltpu.VMEM((2 * c, 8 * c), BF16),
        f_skip=pltpu.VMEM((4 * c, 2 * c), BF16),
        b_skip=pltpu.VMEM((2, 2 * c, 2 * c), BF16),
        xe1=shifted,
        xe2=shifted,
        xd1a=shifted,
        xd1b=shifted,
        xd2=shifted,
        xg=shifted,
        te1=flipped_field,
        te2=flipped_field,
        td1a=flipped_field,
        td1b=flipped_field,
        td2=flipped_field,
        turned=pltpu.VMEM((4 * c, cells), BF16),
        fe1=forward,
        fe2=forward,
        fd1a=forward,
        fd1b=forward,
        fd2=forward,
        be1=backward,
        be2=backward,
        bd1a=backward,
        bd1b=backward,
        bd2=backward,
        slope_e1=field,
        slope_e2=field,
        slope_d1a=field,
        slope_d1b=field,
        slope_d2=field,
        lifted=field,
        middle_e=field,
        encoded=field,
        raised=field,
        middle_d=field,
        result=field,
        cot=field,
        grad=field,
        grad_a=field,
        grad_b=field,
    )
    scratch.update({name: pltpu.VMEM(shapes[name], F32) for name in LARGE})

    in_hbm = pl.BlockSpec(memory_space=pl.ANY)
    in_vmem = pl.BlockSpec(memory_space=pltpu.VMEM)
    in_smem = pl.BlockSpec(memory_space=pltpu.SMEM)
    in_specs = [
        in_hbm if name in IN_HBM else in_smem if name in IN_SMEM else in_vmem
        for name in ARGUMENTS
    ]
    out_shape = [
        jax.ShapeDtypeStruct((items, strip * width, c), F32),
        jax.ShapeDtypeStruct(frames.shape, F32),
        jax.ShapeDtypeStruct((total_rows, c), F32),
    ]
    out_specs = [in_hbm] * 3
    results = pl.pallas_call(
        functools.partial(
            item_kernel,
            (line, strip, width, shapes, big_layout),
            tuple(scratch),
        ),
        out_shape=out_shape,
        in_specs=in_specs,
        out_specs=out_specs,
        scratch_shapes=list(scratch.values()),
        compiler_params=pltpu.CompilerParams(
            collective_id=0, has_side_effects=True, vmem_limit_bytes=62 * 1024 * 1024
        ),
    )(*[flat[name] for name in ARGUMENTS])
    names = LARGE + tuple(SMALL_ROWS)
    written = pl.pallas_call(
        functools.partial(write_kernel, (shapes, starts, small_at)),
        out_shape=out_shape[:2] + [jax.ShapeDtypeStruct(flat[name].shape, F32) for name in names],
        in_specs=[pl.BlockSpec(memory_space=pltpu.HBM)] * 3,
        out_specs=[in_hbm] * (2 + len(LARGE)) + [in_vmem] * len(SMALL_ROWS),
        scratch_shapes=[
            pltpu.VMEM((items, strip * width, c), F32),
            pltpu.VMEM(frames.shape, F32),
            pltpu.VMEM((total_rows, c), F32),
            pltpu.SemaphoreType.DMA((1 + 2 * (2 + len(LARGE)),)),
        ],
        compiler_params=pltpu.CompilerParams(vmem_limit_bytes=60 * 1024 * 1024),
    )(*results)
    grads = dict(zip(names, written[2:]))
    ordered = [name for name in ARGUMENTS if name in grads]
    return (written[0].reshape(cotangent.shape), written[1]) + tuple(
        grads[name].reshape(given[name].shape) for name in ordered
    )


def body(shape, *arguments):
    items, _, strip, width = arguments[0].shape
    line = shape["rows"]
    whole = (
        shape["section"] == 2
        and shape["batch"] == 4
        and items == line == 4
        and arguments[-1].shape[-1] == 128
        and (strip * line * width) % CHUNK == 0
    )
    return whole_items(shape, *arguments) if whole else strips_body(*arguments)


def solution(mesh):
    in_specs = (
        P(("section", "batch"), None, "rows", None),
        P(("section", "batch")),
        P(("section", "batch"), "rows", None),
        P(("section", "batch")),
        P(),
        P(),
        P(),
        P(),
        P(),
        P(),
        P(),
        P(),
        P(),
        P(),
        P(),
        P(),
        P(),
        P(),
        P(),
        P(),
        P(),
        P(),
        P(),
        P(),
        P(),
        P(),
        P(),
        P(),
        P(("section", "batch"), "rows", None, None),
    )
    out_specs = (
        P(("section", "batch"), "rows", None, None),
        P(("section", "batch"), None, "rows", None),
        P(),
        P(),
        P(),
        P(),
        P(),
        P(),
        P(),
        P(),
        P(),
        P(),
        P(),
        P(),
        P(),
        P(),
        P(),
        P(),
        P(),
        P(),
        P(),
        P(),
        P(),
        P(),
        P(),
        P(),
    )
    return jax.shard_map(functools.partial(body, mesh.shape), mesh=mesh, in_specs=in_specs, out_specs=out_specs, check_vma=False)
```

```python
import functools
from types import SimpleNamespace
from typing import Any, NamedTuple

import jax
import jax.numpy as jnp
from jax import lax
from jax.experimental import pallas as pl
from jax.experimental.pallas import tpu as pltpu
from jax.sharding import PartitionSpec as P

GROUPS = 8
FIELDS = 3
HIST = 4


EPS = 1e-05
HIGH = lax.Precision.HIGHEST


def extended(cells, sides, width):
    for axis, dim in sides:
        count = lax.axis_size(axis)
        ends = count - 1
        head = lax.slice_in_dim(cells, 0, width, axis=dim)
        tail = lax.slice_in_dim(cells, cells.shape[dim] - width, cells.shape[dim], axis=dim)
        cells = jnp.concatenate(
            [
                lax.ppermute(tail, axis, [(i, (i + 1) % count) for i in range(ends)]),
                cells,
                lax.ppermute(head, axis, [((i + 1) % count, i) for i in range(ends)]),
            ],
            axis=dim,
        )
    return cells


def from_behind(value, axis, steps):
    count = lax.axis_size(axis)
    pairs = [(source, (source + steps) % count) for source in range(count)]
    return lax.ppermute(value, axis, pairs)


def group_view(value_arrays):
    extent = value_arrays.shape
    return value_arrays.reshape(extent[:-1] + (GROUPS, extent[-1] // GROUPS))


def global_sums(value_arrays):
    grouped = group_view(value_arrays)
    flat = grouped.reshape(-1, GROUPS, grouped.shape[-1])
    first_sum = jnp.sum(flat, axis=(0, 2))
    second_sum = jnp.sum(flat * flat, axis=(0, 2))
    return lax.psum((first_sum, second_sum), "rows")


def apply_norm(value_arrays, sum_one, sum_two, norm_gain, norm_bias, total):
    grouped = group_view(value_arrays)
    group_mean = sum_one / total
    variance = sum_two / total - group_mean * group_mean
    inverse = lax.rsqrt(variance + EPS)
    normed = (grouped - group_mean[:, None]) * inverse[:, None]
    return normed.reshape(value_arrays.shape) * norm_gain + norm_bias


def norm_back(value_arrays, grad_one, grad_two):
    grouped = group_view(value_arrays)
    extra = grad_one[:, None] + 2.0 * grouped * grad_two[:, None]
    return extra.reshape(value_arrays.shape)


def reduce_grads(grad_one, grad_two):
    return lax.psum((grad_one, grad_two), "rows")


def conv_rows(padded, kernel):
    widened = jnp.pad(padded, ((0, 0), (1, 1), (0, 0)))
    return lax.conv_general_dilated(
        widened[None],
        kernel,
        (1, 1),
        "VALID",
        dimension_numbers=("NHWC", "HWIO", "NHWC"),
        precision=HIGH,
    )[0]


def flipped(kernel):
    return jnp.transpose(kernel[::-1, ::-1], (0, 1, 3, 2))


def pad_grads(value_arrays):
    return extended(value_arrays, (("rows", 0),), 1)


def totals_of(inputs, conv1):
    strip = inputs.shape[0]
    cells = strip * lax.axis_size("rows") * inputs.shape[1]
    return (cells * (inputs.shape[2] // GROUPS), cells * (conv1.shape[3] // GROUPS))


def block_forward(inputs, weights, scale_part, shift_part):
    norm1_gain, norm1_bias, conv1, norm2_gain, norm2_bias, conv2, conv2_bias = weights
    total_in, total_mid = totals_of(inputs, conv1)
    sums_in = global_sums(inputs)

    def pad_rows(value_arrays):
        return extended(value_arrays, (("rows", 0),), 1)

    act_one = pad_rows(
        jax.nn.gelu(
            apply_norm(inputs, sums_in[0], sums_in[1], norm1_gain, norm1_bias, total_in),
            approximate=False,
        )
    )
    middle = conv_rows(act_one, conv1)
    sums_mid = global_sums(middle)
    shaped = (
        apply_norm(middle, sums_mid[0], sums_mid[1], norm2_gain, norm2_bias, total_mid)
        * (1.0 + scale_part)
        + shift_part
    )
    act_two = pad_rows(jax.nn.gelu(shaped, approximate=False))
    branch = conv_rows(act_two, conv2) + conv2_bias
    return (branch, (sums_in[0], sums_in[1], act_one, middle, sums_mid[0], sums_mid[1], act_two))


def block_backward(inputs, weights, scale_part, shift_part, kept, grad_out):
    norm1_gain, norm1_bias, conv1, norm2_gain, norm2_bias, conv2, conv2_bias = weights
    in_one, in_two, act_one, middle, mid_one, mid_two, act_two = kept
    total_in, total_mid = totals_of(inputs, conv1)
    grad_conv2 = jax.vjp(lambda kernel: conv_rows(act_two, kernel), conv2)[1](grad_out)[0]
    grad_bias2 = jnp.sum(grad_out, axis=(0, 1))
    grad_act_two = conv_rows(pad_grads(grad_out), flipped(conv2))

    def second_piece(middle_in, sum_one, sum_two, gain_in, incoming_bias, scale_in, shift_in):
        shaped = (
            apply_norm(middle_in, sum_one, sum_two, gain_in, incoming_bias, total_mid)
            * (1.0 + scale_in)
            + shift_in
        )
        return jax.nn.gelu(shaped, approximate=False)

    second_pull = jax.vjp(
        second_piece, middle, mid_one, mid_two, norm2_gain, norm2_bias, scale_part, shift_part
    )[1](grad_act_two)
    summed_one, summed_two = reduce_grads(second_pull[1], second_pull[2])
    grad_middle = second_pull[0] + norm_back(middle, summed_one, summed_two)
    grad_conv1 = jax.vjp(lambda kernel: conv_rows(act_one, kernel), conv1)[1](grad_middle)[0]
    grad_act_one = conv_rows(pad_grads(grad_middle), flipped(conv1))

    def first_piece(inputs_in, sum_one, sum_two, gain_in, incoming_bias):
        return jax.nn.gelu(
            apply_norm(inputs_in, sum_one, sum_two, gain_in, incoming_bias, total_in),
            approximate=False,
        )

    first_pull = jax.vjp(first_piece, inputs, in_one, in_two, norm1_gain, norm1_bias)[1](
        grad_act_one
    )
    first_one, first_two = reduce_grads(first_pull[1], first_pull[2])
    grad_inputs = first_pull[0] + norm_back(inputs, first_one, first_two)
    grads = (
        first_pull[3],
        first_pull[4],
        grad_conv1,
        second_pull[3],
        second_pull[4],
        grad_conv2,
        grad_bias2,
    )
    return (grad_inputs, grads, second_pull[5], second_pull[6])


def conditioning(step_item, table):
    one_hot = (jnp.arange(table.shape[0], dtype=jnp.int32) == step_item).astype(jnp.float32)
    condition = jnp.dot(one_hot, table, precision=HIGH)
    half_width = table.shape[1] // 2
    return (condition[:half_width], condition[half_width:], one_hot)


def project_in(frames_item, mask_item, count_item, incoming_weight, incoming_bias):
    history = jnp.arange(HIST, dtype=jnp.int32) >= HIST - count_item
    keep = jnp.repeat(history, FIELDS).astype(jnp.float32)
    lifted = (
        jnp.einsum(
            "fhw,fc->hwc", frames_item * keep[:, None, None], incoming_weight, precision=HIGH
        )
        + incoming_bias
    )
    return lifted * mask_item[:, :, None].astype(jnp.float32)


def coarsen_field(value_arrays, incoming_weight, incoming_bias):
    rows_here, width_here, depth_here = value_arrays.shape
    blocks = value_arrays.reshape(rows_here // 2, 2, width_here // 2, 2, depth_here)
    return jnp.einsum("iajbk,abkc->ijc", blocks, incoming_weight, precision=HIGH) + incoming_bias


def upsample(value_arrays, incoming_weight, incoming_bias):
    result = jnp.einsum("ijk,abkc->iajbc", value_arrays, incoming_weight, precision=HIGH)
    extent = result.shape
    return result.reshape(extent[0] * 2, extent[2] * 2, extent[4]) + incoming_bias


def flatten_all(pieces):
    return jnp.concatenate([piece.reshape(-1) for piece in pieces])


def unflatten_all(flat, templates):
    pieces = []
    offset_at = 0
    for template in templates:
        count_here = template.size
        pieces.append(flat[offset_at : offset_at + count_here].reshape(template.shape))
        offset_at += count_here
    return tuple(pieces)


def strips_body(
    frames,
    counts,
    cell_mask,
    step_index,
    lift_weight,
    lift_bias,
    enc_norm1_gain,
    enc_norm1_bias,
    enc_conv1,
    enc_step_table,
    enc_norm2_gain,
    enc_norm2_bias,
    enc_conv2,
    enc_conv2_bias,
    reducer_weight,
    reducer_bias,
    up_weight,
    up_bias,
    dec_norm1_gain,
    dec_norm1_bias,
    dec_conv1,
    dec_step_table,
    dec_norm2_gain,
    dec_norm2_bias,
    dec_conv2,
    dec_conv2_bias,
    skip_weight,
    skip_bias,
    cotangent,
):
    enc_weights = (
        enc_norm1_gain,
        enc_norm1_bias,
        enc_conv1,
        enc_norm2_gain,
        enc_norm2_bias,
        enc_conv2,
        enc_conv2_bias,
    )
    dec_weights = (
        dec_norm1_gain,
        dec_norm1_bias,
        dec_conv1,
        dec_norm2_gain,
        dec_norm2_bias,
        dec_conv2,
        dec_conv2_bias,
    )
    params = (
        lift_weight,
        lift_bias,
        enc_norm1_gain,
        enc_norm1_bias,
        enc_conv1,
        enc_step_table,
        enc_norm2_gain,
        enc_norm2_bias,
        enc_conv2,
        enc_conv2_bias,
        reducer_weight,
        reducer_bias,
        up_weight,
        up_bias,
        dec_norm1_gain,
        dec_norm1_bias,
        dec_conv1,
        dec_step_table,
        dec_norm2_gain,
        dec_norm2_bias,
        dec_conv2,
        dec_conv2_bias,
        skip_weight,
        skip_bias,
    )

    def forward_micro(carry, sliced):
        frames_item, mask_item, count_item, step_item = sliced
        lifted = project_in(frames_item, mask_item, count_item, lift_weight, lift_bias)
        enc_scale, enc_shift, unused_hot = conditioning(step_item, enc_step_table)
        enc_branch, enc_kept = block_forward(lifted, enc_weights, enc_scale, enc_shift)
        encoder_result = lifted + enc_branch
        coarse_field = coarsen_field(encoder_result, reducer_weight, reducer_bias)
        foreign = from_behind(coarse_field, "section", 1)
        raised_foreign = upsample(foreign, up_weight, up_bias)
        raised = from_behind(raised_foreign, "section", 1)
        joined = jnp.concatenate([raised, encoder_result], axis=-1)
        dec_scale, dec_shift, unused_again = conditioning(step_item, dec_step_table)
        dec_branch, dec_kept = block_forward(joined, dec_weights, dec_scale, dec_shift)
        output_item = jnp.dot(joined, skip_weight, precision=HIGH) + skip_bias + dec_branch
        return (carry, (output_item, (lifted, enc_kept, encoder_result, foreign, joined, dec_kept)))

    unused, (output, kept_all) = lax.scan(
        forward_micro, jnp.zeros((), jnp.float32), (frames, cell_mask, counts, step_index)
    )

    def backward_micro(totals, sliced):
        frames_item, mask_item, count_item, step_item, grad_out, kept = sliced
        lifted, enc_kept, encoder_result, foreign, joined, dec_kept = kept
        dec_scale, dec_shift, one_hot = conditioning(step_item, dec_step_table)
        grad_joined, dec_grads, dec_gscale, dec_gshift = block_backward(
            joined, dec_weights, dec_scale, dec_shift, dec_kept, grad_out
        )
        grad_skip_weight = jnp.einsum("hwk,hwc->kc", joined, grad_out, precision=HIGH)
        grad_skip_bias = jnp.sum(grad_out, axis=(0, 1))
        grad_joined = grad_joined + jnp.dot(grad_out, skip_weight.T, precision=HIGH)
        half_width = joined.shape[-1] // 2
        grad_raised = grad_joined[..., :half_width]
        grad_encoded = grad_joined[..., half_width:]
        grad_foreign_up = from_behind(grad_raised, "section", 1)
        up_pull = jax.vjp(upsample, foreign, up_weight, up_bias)[1](grad_foreign_up)
        coarse_gradient = from_behind(up_pull[0], "section", 1)
        reducer_pullback = jax.vjp(coarsen_field, encoder_result, reducer_weight, reducer_bias)[1](
            coarse_gradient
        )
        grad_encoded = grad_encoded + reducer_pullback[0]
        enc_scale, enc_shift, enc_hot = conditioning(step_item, enc_step_table)
        grad_lifted, enc_grads, enc_gscale, enc_gshift = block_backward(
            lifted, enc_weights, enc_scale, enc_shift, enc_kept, grad_encoded
        )
        grad_lifted = grad_lifted + grad_encoded
        proj_pull = jax.vjp(
            lambda frames_in, incoming_weight, incoming_bias: project_in(
                frames_in, mask_item, count_item, incoming_weight, incoming_bias
            ),
            frames_item,
            lift_weight,
            lift_bias,
        )[1](grad_lifted)
        enc_table_grad = enc_hot[:, None] * jnp.concatenate([enc_gscale, enc_gshift])[None, :]
        dec_table_grad = one_hot[:, None] * jnp.concatenate([dec_gscale, dec_gshift])[None, :]
        micro_list = (
            proj_pull[1],
            proj_pull[2],
            enc_grads[0],
            enc_grads[1],
            enc_grads[2],
            enc_table_grad,
            enc_grads[3],
            enc_grads[4],
            enc_grads[5],
            enc_grads[6],
            reducer_pullback[1],
            reducer_pullback[2],
            up_pull[1],
            up_pull[2],
            dec_grads[0],
            dec_grads[1],
            dec_grads[2],
            dec_table_grad,
            dec_grads[3],
            dec_grads[4],
            dec_grads[5],
            dec_grads[6],
            grad_skip_weight,
            grad_skip_bias,
        )
        micro_flat = flatten_all(micro_list)
        return (totals + micro_flat, proj_pull[0])

    total_size = sum((piece.size for piece in params))
    start_totals = jnp.zeros((total_size,), jnp.float32)
    flat_totals, frames_grad = lax.scan(
        backward_micro,
        start_totals,
        (frames, cell_mask, counts, step_index, cotangent, kept_all),
        reverse=True,
    )
    flat_totals = lax.psum(flat_totals, ("section", "batch", "rows"))
    grads = unflatten_all(flat_totals, params)
    return (output, frames_grad) + grads


F32 = jnp.float32
BF16 = jnp.bfloat16
MESH = pl.DeviceIdType.MESH
NN = ((1,), (0,))
NT = ((1,), (1,))
TN = ((0,), (0,))
HIGH_AT = (0, 2, 1)
LOW_AT = (4, 3, 5)
CHUNK = 512
class Given(NamedTuple):
    frames: Any
    counts: Any
    cell_mask: Any
    step_index: Any
    lift_weight: Any
    lift_bias: Any
    enc_norm1_gain: Any
    enc_norm1_bias: Any
    enc_conv1: Any
    enc_step_table: Any
    enc_norm2_gain: Any
    enc_norm2_bias: Any
    enc_conv2: Any
    enc_conv2_bias: Any
    reducer_weight: Any
    reducer_bias: Any
    up_weight: Any
    up_bias: Any
    dec_norm1_gain: Any
    dec_norm1_bias: Any
    dec_conv1: Any
    dec_step_table: Any
    dec_norm2_gain: Any
    dec_norm2_bias: Any
    dec_conv2: Any
    dec_conv2_bias: Any
    skip_weight: Any
    skip_bias: Any
    cotangent: Any


ARGUMENTS = Given._fields
LARGE = tuple(
    dict(
        dec_conv1=0,
        up_weight=0,
        reducer_weight=0,
        dec_conv2=0,
        skip_weight=0,
        enc_conv1=0,
        enc_conv2=0,
    )
)
IN_HBM = tuple(dict(frames=0, cell_mask=0, cotangent=0)) + LARGE
IN_SMEM = tuple(dict(counts=0, step_index=0))
LATE = 64
SMALL_ROWS = dict(
    enc_conv2_bias=(0, 1),
    reducer_bias=(1, 1),
    up_bias=(2, 1),
    dec_conv2_bias=(3, 1),
    skip_bias=(3, 1),
    dec_norm1_gain=(4, 2),
    dec_norm1_bias=(6, 2),
    dec_norm2_gain=(8, 1),
    dec_norm2_bias=(9, 1),
    dec_step_table=(16, 8),
    lift_weight=(LATE, 12),
    lift_bias=(LATE + 12, 1),
    enc_norm1_gain=(LATE + 16, 1),
    enc_norm1_bias=(LATE + 17, 1),
    enc_norm2_gain=(LATE + 18, 1),
    enc_norm2_bias=(LATE + 19, 1),
    enc_step_table=(LATE + 24, 8),
)
LATE_COUNT = 32
SMALL_COUNT = LATE + LATE_COUNT
DUE = ((), (), (), (), (), (0,), (), (1,), (), (), (2,), (3, 0), (), (), (1,), (), (), (2,), (0,), (1, 4, 3), (2,), (), (), (5, 0), (1, 3), (4, 2), (), (6,), (7, 3, 0, 5, 4, 1, 2))
REST = (6, 3, 7, 4, 5, 6, 8, 7, 0, 4, 5, 1, 6, 7, 2, 0, 1, 5, 3, 6, 2, 8, 7, 3, 4, 5, 4, 6, 7, 5, 6, 7)
OUTPUTS = tuple(dict(output=0, frames_grad=0, gradients=0))


def split(value):
    high = value.astype(BF16)
    return high, (value - high.astype(F32)).astype(BF16)


def dot(left, right, dims=NN, precision=None):
    return lax.dot_general(
        left, right, (dims, ((), ())), precision=precision, preferred_element_type=F32
    )


def fold(value):
    half = value.shape[1] // 2
    return value[:, :half] + value[:, half:]


def fold_rows(value):
    half = value.shape[0] // 2
    return value[:half] + value[half:]


def tile_sums(value):
    return jnp.sum(value.reshape(-1, 8, value.shape[-1]), axis=0)


def column_sum(tiles):
    return jnp.sum(tiles, axis=0, keepdims=True)


def normal(value):
    bell = jnp.exp(-0.5 * value * value)
    t = 1.0 / (1.0 + 0.2316418882663604 * jnp.abs(value))
    poly = 0.5307027145
    for factor in (-0.7265760135, 0.7107068705, -0.142248368, 0.127414796):
        poly = poly * t + factor
    tail = poly * t * bell
    return jnp.where(value < 0.0, tail, 1.0 - tail), 0.3989422804014327 * bell


def dot_three(left, right, dims=NN):
    left_high, left_low = split(left)
    right_high, right_low = split(right)
    total = dot(left_high, right_high, dims)
    return total + (dot(left_high, right_low, dims) + dot(left_low, right_high, dims))


def group_ones(channels, size):
    rows = lax.broadcasted_iota(jnp.int32, (channels, channels), 0) // size
    columns = lax.broadcasted_iota(jnp.int32, (channels, channels), 1) // size
    return (rows == columns).astype(BF16)


def group_sums(first, second, ones):
    terms = []
    rest = jnp.concatenate([first, second], axis=0)
    for _ in range(3):
        term = rest.astype(BF16)
        terms.append(term)
        rest = rest - term.astype(F32)
    both = dot(jnp.concatenate(terms, axis=0), ones)
    both = both[32:48] + both[16:32] + both[:16]
    return column_sum(both[:8]), column_sum(both[8:])


class Exchange:

    def __init__(self, place, start, rows, landing, first_sem):
        self.place, self.start, self.rows, self.landing = place, start, rows, landing
        self.sem = first_sem
        self.stage = 0
        self.copies = []
        self.waiting = []
        self.group = place.plane_group
        self.half = rows // 2
        self.base = start + place.core * self.half
        self._finish(self.half)

    def _finish(self, size):
        self.part = size // self.group.count
        self.own = self.base + self.group.here * self.part

    def count(self):
        return 2 + 2 * (self.group.count - 1) + 3

    def land_rows(self):
        return self.half + (self.group.count + 1) * self.part

    def _copy(self, source, target, device, only=None):
        place = self.place
        copy = pltpu.make_async_remote_copy(
            src_ref=source,
            dst_ref=target,
            send_sem=place.send.at[self.sem],
            recv_sem=place.recv.at[self.sem],
            device_id=device,
            device_id_type=MESH,
        )
        self.sem += 1
        if only is None:
            copy.start()
            self.waiting.append(copy)
        self.copies.append((copy, only))
        return copy

    def _wait(self):
        for copy in self.waiting:
            copy.wait_recv()
        self.waiting = []

    def _rows(self, at, size):
        return pl.ds(pl.multiple_of(at, 8), size)

    def _swap(self):
        place = self.place
        other = self._rows(self.start + (1 - place.core) * self.half, self.half)
        self.land = self.landing
        self.landing += self.half
        self._copy(
            place.sums.at[other], place.landing.at[pl.ds(self.land, self.half)], place.partner
        )

    def _add_swap(self):
        place = self.place
        block = 64 if self.half % 64 == 0 else 32

        def step(i, carry):
            here = self._rows(self.base + i * block, block)
            there = self._rows(self.land + i * block, block)
            place.sums[here] = place.sums[here] + place.landing[there]
            return carry

        lax.fori_loop(0, self.half // block, step, 0)

    def _scatter(self, group, base, size):
        place = self.place
        self.land = self.landing
        for k in range(1, group.count):
            to = lax.rem(group.here + k, group.count)
            self._copy(
                place.sums.at[self._rows(base + to * size, size)],
                place.landing.at[pl.ds(self.landing, size)],
                group.device(to),
            )
            self.landing += size

    def _total(self, group, own, size, target):
        place = self.place
        block = 16 if size % 16 == 0 else 8

        def step(i, carry):
            here = self._rows(own + i * block, block)
            total = place.sums[here]
            for k in range(group.count - 1):
                there = self._rows(self.land + k * size + i * block, block)
                total = total + place.landing[there]
            target[here] = total
            return carry

        lax.fori_loop(0, size // block, step, 0)

    def _gather(self, group, own, size):
        final = self.place.final
        here = self._rows(own, size)
        for k in range(1, group.count):
            to = lax.rem(group.here + k, group.count)
            self._copy(final.at[here], final.at[here], group.device(to))

    def _steps(self):
        place, group = self.place, self.group
        yield self._swap()
        self._wait()
        self._add_swap()
        yield from self._both()
        final = place.final
        here = self._rows(self.base, self.half)
        self._copy(final.at[here], final.at[here], place.partner)
        yield
        self._wait()
        yield

    def _both(self):
        place, group = self.place, self.group
        self._scatter(group, self.base, self.part)
        yield
        self._wait()
        self._total(group, self.own, self.part, place.sums)
        yield from self._line()
        self._gather(group, self.own, self.part)
        yield
        self._wait()

    def _line(self):
        place, line = self.place, self.place.line
        sums, final, landing = place.sums, place.final, place.landing
        part, own = self.part, self._rows(self.own, self.part)
        inward, across = pl.ds(self.landing, part), pl.ds(self.landing + part, part)
        self.landing += 2 * part
        block = 16 if part % 16 == 0 else 8

        def add(at, target):
            def step(i, carry):
                here = self._rows(self.own + i * block, block)
                target[here] = sums[here] + landing[pl.ds(at + i * block, block)]
                return carry

            lax.fori_loop(0, part // block, step, 0)

        first = self._copy(sums.at[own], landing.at[inward], line.device(line.inner), line.edge)
        second = self._copy(sums.at[own], landing.at[across], line.device(line.across), line.middle)
        third = self._copy(final.at[own], final.at[own], line.device(line.outer), line.middle)
        pl.when(line.edge)(first.start)
        yield

        @pl.when(line.middle)
        def _():
            first.wait_recv()
            add(self.landing - 2 * part, sums)
            second.start()

        yield

        @pl.when(line.middle)
        def _():
            second.wait_recv()
            add(self.landing - part, final)
            third.start()

        yield
        pl.when(line.edge)(third.wait_recv)

    def advance(self):
        if self.stage == 0:
            self.steps = self._steps()
        self.stage += 1
        next(self.steps)

    def done(self):
        return self.stage == 8


class SmallExchange(Exchange):

    def count(self):
        return self.place.cores_group.count + self.place.line.count - 2

    def land_rows(self):
        return self.rows * (self.place.cores_group.count + self.place.line.count)

    def _share(self, group, source):
        place = self.place
        self.land = self.landing
        self.landing += group.count * self.rows
        own = self._rows(self.land + group.here * self.rows, self.rows)
        place.landing[own] = source[...]
        for k in range(1, group.count):
            to = lax.rem(group.here + k, group.count)
            self._copy(source, place.landing.at[own], group.device(to))

    def _sum(self, group):
        total = None
        for k in range(group.count):
            part = self.place.landing[pl.ds(self.land + k * self.rows, self.rows)]
            total = part if total is None else total + part
        return total

    def _steps(self):
        place = self.place
        here = pl.ds(self.start, self.rows)
        self._share(place.line, place.sums.at[here])
        yield
        self._wait()
        place.small[...] = self._sum(place.line)
        self._share(place.cores_group, place.small)
        yield
        self._wait()
        place.final[here] = self._sum(place.cores_group)
        yield

    def done(self):
        return self.stage == 3


def layout_of(shapes):
    starts = {}
    at = 0
    for name in LARGE:
        starts[name] = at
        at += getattr(shapes, name)[0]
    small = at
    begins = SimpleNamespace(**starts)
    late = small + LATE
    tap = shapes.dec_conv2[0] // 3
    part = shapes.dec_conv1[0] // 3
    conv1, up = begins.dec_conv1, begins.up_weight
    edges = (
        (begins.dec_conv2, begins.enc_conv1),
        (conv1, conv1 + part),
        (conv1 + part, conv1 + 2 * part),
        (conv1 + 2 * part, up),
        (up, begins.dec_conv2),
        (begins.enc_conv2, late),
        (begins.enc_conv1, begins.enc_conv1 + 2 * tap),
        (begins.enc_conv1 + 2 * tap, begins.enc_conv2),
        (late, late + LATE_COUNT),
    )
    runs = [(first, last - first) for first, last in edges]
    return starts, small, late + LATE_COUNT, runs


def item_kernel(sizes, scratch_names, *refs):
    line, strip, width, shapes, big_layout = sizes
    begins, small_at, total_rows, runs = big_layout
    starts = SimpleNamespace(**begins)
    inputs = Given(*refs[: len(ARGUMENTS)])
    refs = refs[len(ARGUMENTS) :]
    output_names = OUTPUTS
    outputs = SimpleNamespace(**dict(zip(output_names, refs)))
    scratch = SimpleNamespace(**dict(zip(scratch_names, refs[len(output_names) :])))

    def w_of(name):
        return getattr(scratch, name)

    height = strip * line
    cells = height * width
    c = inputs.lift_weight.shape[1]
    strip_cells = strip * width
    history = inputs.frames.shape[1]

    core = lax.axis_index("section")
    plane = lax.axis_index("batch")
    row = lax.axis_index("rows")
    middle = lax.rem(row + 1, 4) // 2

    def device_at(to):
        return (core, plane, to)

    place = SimpleNamespace(
        core=core,
        partner=(1 - core, plane, row),
        line=SimpleNamespace(
            count=line,
            here=row,
            device=device_at,
            middle=middle == 1,
            edge=middle == 0,
            inner=1 + row // 2,
            across=3 - row,
            outer=3 * (row // 2),
        ),
        plane_group=SimpleNamespace(
            count=4, here=plane, device=lambda to: (core, to, row)
        ),
        cores_group=SimpleNamespace(
            count=8,
            here=core * 4 + plane,
            device=lambda to: (to // 4, lax.rem(to, 4), row),
        ),
        small=scratch.small,
        sums=scratch.sums,
        final=scratch.final,
        landing=scratch.landing,
        send=scratch.send,
        recv=scratch.recv,
    )
    local_sem = scratch.local

    frames_in, mask_in, cot = scratch.frames_in, scratch.mask_in, scratch.cot
    here_rows = pl.ds(pl.multiple_of(row * strip_cells, strip_cells), strip_cells)
    frames_from, mask_from, cot_from = scratch.frames_from, scratch.mask_from, scratch.cot_from
    staged = (
        pltpu.make_async_copy(inputs.frames, frames_from, local_sem.at[7]),
        pltpu.make_async_copy(inputs.cell_mask, mask_from, local_sem.at[8]),
        pltpu.make_async_copy(inputs.cotangent, cot_from, local_sem.at[9]),
    )
    for copy in staged:
        copy.start()

    weight_copies = {}
    for k, name in enumerate(LARGE):
        copy = pltpu.make_async_copy(getattr(inputs, name), w_of(name), local_sem.at[k])
        weight_copies[name] = copy
        copy.start()

    barrier = pltpu.get_barrier_semaphore()
    peers = [device_at(lax.rem(row + k, line)) for k in range(1, line)]
    cores_group = place.cores_group
    for k in range(1, 8):
        peers.append(cores_group.device(lax.rem(cores_group.here + k, 8)))
    for device in peers:
        pl.semaphore_signal(barrier, inc=1, device_id=device, device_id_type=MESH)
    pl.semaphore_wait(barrier, len(peers))

    next_sem = 0

    def send(source, target, device):
        nonlocal next_sem
        copy = pltpu.make_async_remote_copy(
            src_ref=source,
            dst_ref=target,
            send_sem=scratch.send.at[next_sem],
            recv_sem=scratch.recv.at[next_sem],
            device_id=device,
            device_id_type=MESH,
        )
        next_sem += 1
        copy.start()
        return copy

    frame_copies, cot_copies, output_copies = [], [], []
    for copy in staged[:2]:
        copy.wait()
    for k in range(1, line):
        to = lax.rem(row + k, line)
        device = device_at(to)
        frame_copies.append(send(frames_from.at[to], frames_in.at[row], device))
        frame_copies.append(send(mask_from.at[to], mask_in.at[row], device))
    staged[2].wait()
    for k in range(1, line):
        to = lax.rem(row + k, line)
        cot_copies.append(
            send(cot_from.at[to], cot.at[here_rows], device_at(to))
        )

    copied = SimpleNamespace(**weight_copies)
    def stack_conv(source, half, depth, forward, backward):
        for a in range(3):
            for b in range(3):
                at = (3 * a + b) * depth + half * c
                high, low = split(source[at : at + c, :])
                for block in (HIGH_AT[b], LOW_AT[b]):
                    rows = slice((6 * a + block) * c, (6 * a + block + 1) * c)
                    forward[rows, 0:c] = high
                    forward[rows, c : 2 * c] = low
                for block in (HIGH_AT[2 - b], LOW_AT[2 - b]):
                    tap = 6 * (2 - a) + block
                    columns = slice(tap * c, (tap + 1) * c)
                    backward[0:c, columns] = high
                    backward[c : 2 * c, columns] = low

    copied.enc_conv1.wait()
    stack_conv(scratch.enc_conv1, 0, c, scratch.fe1, scratch.be1)
    copied.enc_conv2.wait()
    stack_conv(scratch.enc_conv2, 0, c, scratch.fe2, scratch.be2)
    copied.reducer_weight.wait()
    for k in range(4):
        high, low = split(scratch.reducer_weight[k * c : (k + 1) * c, :])
        for block in (k, k + 4):
            scratch.f_down[block * c : (block + 1) * c, 0:c] = high
            scratch.f_down[block * c : (block + 1) * c, c : 2 * c] = low
        for block in (0, 1):
            columns = slice(block * c, (block + 1) * c)
            scratch.b_down[k, 0:c, columns] = high
            scratch.b_down[k, c : 2 * c, columns] = low
    copied.up_weight.wait()
    for k in range(4):
        high, low = split(scratch.up_weight[k * c : (k + 1) * c, :])
        for block in (0, 1):
            rows = slice(block * c, (block + 1) * c)
            scratch.f_up[k, rows, 0:c] = high
            scratch.f_up[k, rows, c : 2 * c] = low
        for block in (k, k + 4):
            columns = slice(block * c, (block + 1) * c)
            scratch.b_up[0:c, columns] = high
            scratch.b_up[c : 2 * c, columns] = low
    copied.dec_conv1.wait()
    stack_conv(scratch.dec_conv1, 0, 2 * c, scratch.fd1a, scratch.bd1a)
    stack_conv(scratch.dec_conv1, 1, 2 * c, scratch.fd1b, scratch.bd1b)
    copied.dec_conv2.wait()
    stack_conv(scratch.dec_conv2, 0, c, scratch.fd2, scratch.bd2)
    copied.skip_weight.wait()
    for half in range(2):
        high, low = split(scratch.skip_weight[half * c : (half + 1) * c, :])
        for block in (half, half + 2):
            scratch.f_skip[block * c : (block + 1) * c, 0:c] = high
            scratch.f_skip[block * c : (block + 1) * c, c : 2 * c] = low
        for block in (0, 1):
            columns = slice(block * c, (block + 1) * c)
            scratch.b_skip[half, 0:c, columns] = high
            scratch.b_skip[half, c : 2 * c, columns] = low

    for buffer in (scratch.xe1, scratch.xe2, scratch.xd1a, scratch.xd1b, scratch.xd2, scratch.xg):
        edge = jnp.zeros((width, 6 * c), BF16)
        buffer[0:width, :] = edge
        buffer[cells + width : cells + 2 * width, :] = edge

    lift = scratch.lift
    lift[...] = jnp.zeros(lift.shape, F32)
    lift[0:history, :] = inputs.lift_weight[...]
    lift[history : history + 1, :] = inputs.lift_bias[...]

    block = 2 * width
    column = lax.rem(lax.broadcasted_iota(jnp.int32, (block, c), 0), width)
    at_first, at_last = column == 0, column == width - 1
    zeros8 = jnp.zeros((8, c), F32)
    ones16 = group_ones(c, c // GROUPS)
    ones32 = group_ones(c, 2 * c // GROUPS)
    count16 = float(cells * (c // GROUPS))
    count32 = float(cells * (2 * c // GROUPS))

    def grid_rows(step, carry=0):
        return lax.fori_loop(0, cells // block, step, carry, unroll=2)

    def row_at(h):
        return pl.ds(pl.multiple_of(h * block, block), block)

    def chunk_at(i):
        return pl.ds(pl.multiple_of(i * CHUNK, CHUNK), CHUNK)

    def put_row(target, h, value):
        rows = pl.ds(pl.multiple_of(h * block + width, width), block)
        left = jnp.where(at_first, 0.0, pltpu.roll(value, 1, 0))
        right = jnp.where(at_last, 0.0, pltpu.roll(value, block - 1, 0))
        for b, piece in enumerate((left, value, right)):
            high, low = split(piece)
            target[rows, HIGH_AT[b] * c : (HIGH_AT[b] + 1) * c] = high
            target[rows, LOW_AT[b] * c : (LOW_AT[b] + 1) * c] = low

    def put_turned(target, columns, value, first=0, second=1):
        high, low = split(value.T)
        target[first * c : (first + 1) * c, columns] = high
        target[second * c : (second + 1) * c, columns] = low

    def conv_chunk(pairs, i, dims=NN):
        total = None
        for data, weight in pairs:
            taps = []
            for a in range(3):
                rows = pl.ds(pl.multiple_of(i * CHUNK + a * width, width), CHUNK)
                taps.append(data[rows, :])
            part = dot(jnp.concatenate(taps, axis=1), weight[...], dims)
            total = part if total is None else total + part
        return total

    def norm_of(first, second, ones, count):
        one, two = group_sums(first, second, ones)
        mean = one / count
        return mean, lax.rsqrt(two / count - mean * mean + EPS)

    def activate(source, target, turned, slope, scale, shift):
        def step(h, carry):
            value = source[row_at(h), :] * scale + shift
            below, density = normal(value)
            slope[row_at(h), :] = below + value * density
            value = value * below
            put_row(target, h, value)
            put_turned(turned, row_at(h), value)
            return carry

        grid_rows(step)

    def conv_norm(pairs, target):
        def step(i, carry):
            value = fold(conv_chunk(pairs, i))
            target[chunk_at(i), :] = value
            return carry[0] + tile_sums(value), carry[1] + tile_sums(value * value)

        return lax.fori_loop(0, cells // CHUNK, step, (zeros8, zeros8))

    def sums_of(source):
        def step(h, carry):
            value = source[row_at(h), :]
            return carry[0] + tile_sums(value), carry[1] + tile_sums(value * value)

        return grid_rows(step, (zeros8, zeros8))

    step_here = jnp.full((1, c), inputs.step_index[row], jnp.int32)

    def condition(table):
        total = jnp.zeros((1, 2 * c), F32)
        chosen = jnp.concatenate([step_here, step_here], axis=1)
        for s in range(table.shape[0]):
            total = total + jnp.where(chosen == s, table[s : s + 1, :], 0.0)
        return total[:, :c], total[:, c:]

    frames_in[row] = frames_from[row]
    mask_in[row] = mask_from[row]
    for copy in frame_copies:
        copy.wait_recv()
    fields = scratch.fields
    fields[...] = jnp.zeros(fields.shape, F32)
    frame_of = lax.broadcasted_iota(jnp.int32, (history, width), 0) // FIELDS
    keep = (frame_of >= HIST - inputs.counts[row]).astype(F32)
    masks = []
    for source in range(line):
        for k in range(strip):
            columns = slice((source * strip + k) * width, (source * strip + k + 1) * width)
            mask = mask_in[source, k : k + 1, :].astype(F32)
            masks.append(mask)
            fields[0:history, columns] = frames_in[source, :, k, :] * keep * mask
            fields[history : history + 1, columns] = mask
    lifted = scratch.lifted
    lifted[...] = dot_three(fields[...], lift[...], TN)

    enc_scale, enc_shift = condition(inputs.enc_step_table)
    dec_scale, dec_shift = condition(inputs.dec_step_table)

    mean_e1, inv_e1 = norm_of(*sums_of(lifted), ones16, count16)
    gain_e1, bias_e1 = inputs.enc_norm1_gain[...], inputs.enc_norm1_bias[...]
    a_e1 = inv_e1 * gain_e1
    activate(lifted, scratch.xe1, scratch.te1, scratch.slope_e1, a_e1, bias_e1 - mean_e1 * a_e1)
    middle_e = scratch.middle_e
    mean_e2, inv_e2 = norm_of(
        *conv_norm([(scratch.xe1, scratch.fe1)], middle_e), ones16, count16
    )
    gain_e2, bias_e2 = inputs.enc_norm2_gain[...], inputs.enc_norm2_bias[...]
    a_e2 = inv_e2 * gain_e2
    activate(
        middle_e,
        scratch.xe2,
        scratch.te2,
        scratch.slope_e2,
        a_e2 * (1.0 + enc_scale),
        (bias_e2 - mean_e2 * a_e2) * (1.0 + enc_scale) + enc_shift,
    )
    encoded = scratch.encoded
    conv2_bias = inputs.enc_conv2_bias[...]
    joined = scratch.joined

    def encode(i, carry):
        value = fold(conv_chunk([(scratch.xe2, scratch.fe2)], i))
        value = value + conv2_bias + lifted[chunk_at(i), :]
        encoded[chunk_at(i), :] = value
        high, low = split(value)
        joined[chunk_at(i), c : 2 * c] = high
        joined[chunk_at(i), 3 * c : 4 * c] = low
        put_turned(scratch.turned, chunk_at(i), value, 1, 3)
        return carry[0] + tile_sums(value), carry[1] + tile_sums(value * value)

    sums_enc = lax.fori_loop(0, cells // CHUNK, encode, (zeros8, zeros8))

    half_cells, quarter = cells // 2, cells // 4

    def pick(source):
        pieces = []
        for b in range(2):
            value = source[pl.ds(b, half_cells, stride=2), :]
            value = value.reshape(height // 2, 2, width // 2, c)
            pieces.append([value[:, a].reshape(quarter, c) for a in range(2)])
        return [pieces[b][a] for a in range(2) for b in range(2)]

    def place_cells(target, pieces):
        for b in range(2):
            both = [pieces[2 * a + b].reshape(height // 2, 1, width // 2, c) for a in range(2)]
            value = jnp.concatenate(both, axis=1).reshape(half_cells, c)
            target[pl.ds(b, half_cells, stride=2), :] = value

    x_down = scratch.x_down
    for k, piece in enumerate(pick(encoded)):
        high, low = split(piece)
        x_down[:, k * c : (k + 1) * c] = high
        x_down[:, (k + 4) * c : (k + 5) * c] = low
    lowered = fold(dot(x_down[...], scratch.f_down[...])) + inputs.reducer_bias[...]
    x_up = scratch.x_up
    high, low = split(lowered)
    x_up[:, 0:c] = high
    x_up[:, c : 2 * c] = low
    raised = scratch.raised
    up_bias = inputs.up_bias[...]
    place_cells(
        raised, [fold(dot(x_up[...], scratch.f_up[k])) + up_bias for k in range(4)]
    )

    def raise_row(h, carry):
        value = raised[row_at(h), :]
        high, low = split(value)
        joined[row_at(h), 0:c] = high
        joined[row_at(h), 2 * c : 3 * c] = low
        put_turned(scratch.turned, row_at(h), value, 0, 2)
        return carry[0] + tile_sums(value), carry[1] + tile_sums(value * value)

    sums_raised = grid_rows(raise_row, (zeros8, zeros8))

    halves = []
    for half, (source, sums) in enumerate(((raised, sums_raised), (encoded, sums_enc))):
        mean, inv = norm_of(*sums, ones32, count32)
        gain = inputs.dec_norm1_gain[half : half + 1, :]
        bias = inputs.dec_norm1_bias[half : half + 1, :]
        scale = inv * gain
        activate(
            source,
            (scratch.xd1a, scratch.xd1b)[half],
            (scratch.td1a, scratch.td1b)[half],
            (scratch.slope_d1a, scratch.slope_d1b)[half],
            scale,
            bias - mean * scale,
        )
        halves.append((source, mean, inv, gain))
    middle_d = scratch.middle_d
    pairs = [(scratch.xd1a, scratch.fd1a), (scratch.xd1b, scratch.fd1b)]
    mean_d2, inv_d2 = norm_of(*conv_norm(pairs, middle_d), ones16, count16)
    gain_d2, bias_d2 = inputs.dec_norm2_gain[...], inputs.dec_norm2_bias[...]
    a_d2 = inv_d2 * gain_d2
    activate(
        middle_d,
        scratch.xd2,
        scratch.td2,
        scratch.slope_d2,
        a_d2 * (1.0 + dec_scale),
        (bias_d2 - mean_d2 * a_d2) * (1.0 + dec_scale) + dec_shift,
    )
    result = scratch.result
    last_bias = inputs.dec_conv2_bias[...] + inputs.skip_bias[...]

    def decode(i, carry):
        value = conv_chunk([(scratch.xd2, scratch.fd2)], i)
        value = value + dot(joined[chunk_at(i), :], scratch.f_skip[...])
        result[chunk_at(i), :] = fold(value) + last_bias
        return carry

    lax.fori_loop(0, cells // CHUNK, decode, 0)
    output_here, frames_here = scratch.output_here, scratch.frames_here
    output_here[row] = result[here_rows]
    for k in range(1, line):
        to = lax.rem(row + k, line)
        there = pl.ds(pl.multiple_of(to * strip_cells, strip_cells), strip_cells)
        output_copies.append(
            send(result.at[there], output_here.at[row], device_at(to))
        )

    exchanges = []
    waiting_runs = list(runs)
    landing_at = 0
    sem_at = 4 * (line - 1) + 2 * (line - 1)
    sums, final = scratch.sums, scratch.final

    def begin():
        nonlocal landing_at, sem_at
        start, rows = waiting_runs.pop(0)
        kind = Exchange if waiting_runs else SmallExchange
        exchange = kind(place, start, rows, landing_at, sem_at)
        landing_at += exchange.land_rows()
        sem_at += exchange.count()
        exchanges.append(exchange)
        exchange.advance()

    final_copies = []

    def advance(k):
        exchange = exchanges[k]
        exchange.advance()
        if exchange.done():
            rows = pl.ds(exchange.start, exchange.rows)
            copy = pltpu.make_async_copy(
                final.at[rows], outputs.gradients.at[rows], local_sem.at[11 + k]
            )
            copy.start()
            final_copies.append(copy)

    due = list(DUE)

    def point():
        for k in due.pop(0):
            advance(k)

    def small_row(k, value):
        sums[small_at + k : small_at + k + 1, :] = value

    def spread_grad(source):
        def step(h, carry):
            value = source[row_at(h), :]
            put_row(scratch.xg, h, value)
            return carry + tile_sums(value)

        return grid_rows(step, zeros8)

    def weight_grad(turned, at, depth, a):
        rows = pl.ds((2 - a) * width, cells)
        part = fold_rows(dot(turned[...], scratch.xg[rows, :]))
        for b in range(3):
            high, low = HIGH_AT[2 - b] * c, LOW_AT[2 - b] * c
            to = at + (3 * a + b) * depth
            sums[to : to + c, :] = part[:, high : high + c] + part[:, low : low + c]

    def back_conv(weight, slope, target, source, mean, inv):
        carry = (zeros8, zeros8)
        for i in range(cells // CHUNK):
            value = fold(conv_chunk([(scratch.xg, weight)], i, NT)) * slope[chunk_at(i), :]
            target[chunk_at(i), :] = value
            normed = (source[chunk_at(i), :] - mean) * inv
            carry = (carry[0] + tile_sums(value), carry[1] + tile_sums(value * normed))
            if i % (cells // CHUNK // 2) == cells // CHUNK // 2 - 1:
                point()
        return carry

    def norm_grad(sums_in, scale, ones, count):
        one, two = group_sums(sums_in[0] * scale, sums_in[1] * scale, ones)
        return one / count, two / count

    cot[here_rows] = cot_from[row]
    for copy in cot_copies:
        copy.wait_recv()
    total_cot = column_sum(spread_grad(cot))
    for a in range(3):
        weight_grad(scratch.td2, starts.dec_conv2, c, a)
    part = fold(dot(scratch.turned[...], scratch.xg[width : cells + width, 2 * c : 4 * c]))
    sums[starts.skip_weight : starts.skip_weight + 2 * c, :] = fold_rows(part)
    small_row(3, total_cot)
    begin()

    grad = scratch.grad
    sums_d2 = back_conv(scratch.bd2, scratch.slope_d2, grad, middle_d, mean_d2, inv_d2)
    side_grads = (scratch.grad_a, scratch.grad_b)
    for half in range(2):

        def skip_back(i, carry, half=half):
            rows = pl.ds(pl.multiple_of(i * CHUNK + width, width), CHUNK)
            value = dot(scratch.xg[rows, 2 * c : 4 * c], scratch.b_skip[half], NT)
            side_grads[half][chunk_at(i), :] = fold(value)
            return carry

        lax.fori_loop(0, cells // CHUNK, skip_back, 0)
    point()

    def table_rows(k, sums_in, gain, bias, one_plus):
        plain, times = column_sum(sums_in[0]), column_sum(sums_in[1])
        for s in range(inputs.enc_step_table.shape[0]):
            small_row(k + 2 * s, jnp.where(step_here == s, gain * times + bias * plain, 0.0))
            small_row(k + 2 * s + 1, jnp.where(step_here == s, plain, 0.0))
        return one_plus * times, one_plus * plain

    def middle_grad(source, mean, inv, scale, sums_in):
        zero, slope = norm_grad(sums_in, scale, ones16, count16)

        def step(h, carry):
            normed = (source[row_at(h), :] - mean) * inv
            value = inv * (grad[row_at(h), :] * scale - zero - normed * slope)
            put_row(scratch.xg, h, value)
            return carry

        grid_rows(step)

    gain_row, bias_row = table_rows(16, sums_d2, gain_d2, bias_d2, 1.0 + dec_scale)
    small_row(8, gain_row)
    small_row(9, bias_row)
    middle_grad(middle_d, mean_d2, inv_d2, gain_d2 * (1.0 + dec_scale), sums_d2)
    point()
    for a in range(3):
        weight_grad(scratch.td1a, starts.dec_conv1, 2 * c, a)
        weight_grad(scratch.td1b, starts.dec_conv1 + c, 2 * c, a)
        point()
        begin()

    for half, (source, mean, inv, gain) in enumerate(halves):
        sums_in = back_conv(
            (scratch.bd1a, scratch.bd1b)[half],
            (scratch.slope_d1a, scratch.slope_d1b)[half],
            grad,
            source,
            mean,
            inv,
        )
        small_row(4 + half, column_sum(sums_in[1]))
        small_row(6 + half, column_sum(sums_in[0]))
        zero, slope = norm_grad(sums_in, gain, ones32, count32)
        target = side_grads[half]

        def input_grad(h, carry):
            normed = (source[row_at(h), :] - mean) * inv
            value = inv * (grad[row_at(h), :] * gain - zero - normed * slope)
            value = target[row_at(h), :] + value
            target[row_at(h), :] = value
            return carry + tile_sums(value)

        total = grid_rows(input_grad, zeros8)
        if half == 0:
            small_row(2, column_sum(total))
        point()

    grad_raised, grad_encoded = side_grads
    x_grad_up = scratch.x_grad_up
    for k, piece in enumerate(pick(grad_raised)):
        high, low = split(piece)
        x_grad_up[:, k * c : (k + 1) * c] = high
        x_grad_up[:, (k + 4) * c : (k + 5) * c] = low
    grad_lowered = fold(dot(x_grad_up[...], scratch.b_up[...], NT))
    small_row(1, jnp.sum(grad_lowered, axis=0, keepdims=True))
    x_grad_low = scratch.x_grad_low
    high, low = split(grad_lowered)
    x_grad_low[:, 0:c] = high
    x_grad_low[:, c : 2 * c] = low
    point()
    part = fold(fold_rows(dot(x_up[...], x_grad_up[...], TN)))
    for k in range(4):
        at = starts.up_weight + k * c
        sums[at : at + c, :] = part[:, k * c : (k + 1) * c]
    part = fold_rows(fold(dot(x_down[...], x_grad_low[...], TN)))
    sums[starts.reducer_weight : starts.reducer_weight + 4 * c, :] = part
    point()
    begin()
    place_cells(
        grad, [fold(dot(x_grad_low[...], scratch.b_down[k], NT)) for k in range(4)]
    )

    def join_row(h, carry):
        value = grad_encoded[row_at(h), :] + grad[row_at(h), :]
        grad_encoded[row_at(h), :] = value
        put_row(scratch.xg, h, value)
        return carry + tile_sums(value)

    small_row(0, column_sum(grid_rows(join_row, zeros8)))
    for k in range(10, 16):
        small_row(k, jnp.zeros((1, c), F32))
    sums[small_at + 24 : small_at + LATE, :] = jnp.zeros((LATE - 24, c), F32)
    point()
    for a in range(3):
        weight_grad(scratch.te2, starts.enc_conv2, c, a)
        point()
    begin()
    sums_e2 = back_conv(scratch.be2, scratch.slope_e2, grad, middle_e, mean_e2, inv_e2)
    gain_row, bias_row = table_rows(LATE + 24, sums_e2, gain_e2, bias_e2, 1.0 + enc_scale)
    small_row(LATE + 18, gain_row)
    small_row(LATE + 19, bias_row)
    middle_grad(middle_e, mean_e2, inv_e2, gain_e2 * (1.0 + enc_scale), sums_e2)
    point()
    for a in range(3):
        weight_grad(scratch.te1, starts.enc_conv1, c, a)
        point()
        if a:
            begin()
    sums_e1 = back_conv(scratch.be1, scratch.slope_e1, grad, lifted, mean_e1, inv_e1)
    small_row(LATE + 16, column_sum(sums_e1[1]))
    small_row(LATE + 17, column_sum(sums_e1[0]))
    zero, slope = norm_grad(sums_e1, gain_e1, ones16, count16)

    def lifted_grad(h, carry):
        normed = (lifted[row_at(h), :] - mean_e1) * inv_e1
        value = inv_e1 * (grad[row_at(h), :] * gain_e1 - zero - normed * slope)
        grad[row_at(h), :] = grad_encoded[row_at(h), :] + value
        return carry

    grid_rows(lifted_grad)
    point()

    late_at = small_at + LATE
    sums[late_at : late_at + 16, :] = dot_three(fields[...], grad[...])
    sums[late_at + 20 : late_at + 24, :] = jnp.zeros((4, c), F32)
    point()
    begin()
    back = dot_three(lift[...], grad[...], NT)
    frames_out = scratch.frames_out
    for source in range(line):
        for k in range(strip):
            h = source * strip + k
            value = back[0:history, h * width : (h + 1) * width]
            frames_out[source, :, k, :] = value * keep * masks[h]
    frames_here[row] = frames_out[row]
    for k in range(1, line):
        to = lax.rem(row + k, line)
        output_copies.append(
            send(frames_out.at[to], frames_here.at[row], device_at(to))
        )

    for copy in output_copies[: line - 1]:
        copy.wait_recv()
    own_output = pltpu.make_async_copy(output_here, outputs.output, local_sem.at[10])
    own_output.start()
    for k in REST:
        advance(k)
    assert not due and all(exchange.done() for exchange in exchanges)

    for copy in output_copies[line - 1 :]:
        copy.wait_recv()
    own_frames = pltpu.make_async_copy(
        frames_here, outputs.frames_grad, local_sem.at[11 + len(runs)]
    )
    own_frames.start()
    own_output.wait()
    own_frames.wait()
    for copy in final_copies:
        copy.wait()
    for copy in frame_copies + cot_copies + output_copies:
        copy.wait_send()
    for exchange in exchanges:
        for copy, only in exchange.copies:
            if only is None:
                copy.wait_send()
            else:
                pl.when(only)(copy.wait_send)


def write_kernel(layout, *refs):
    shapes, starts, small_at = layout
    output, frames_grad, gradients = refs[:3]
    outputs = refs[3:-4]
    output_here, frames_here, gradients_here, sem = refs[-4:]
    c = gradients.shape[1]
    moves = [(frames_grad, frames_here, outputs[1])]
    for k, name in enumerate(LARGE):
        rows = pl.ds(starts[name], shapes[name][0])
        moves.append((gradients.at[rows], gradients_here.at[rows], outputs[2 + k]))
    moves.append((output, output_here, outputs[0]))
    small = pl.ds(small_at, SMALL_COUNT)
    first = pltpu.make_async_copy(gradients.at[small], gradients_here.at[small], sem.at[0])
    first.start()
    arriving, leaving = [], []
    for k, (source, here, _) in enumerate(moves):
        arriving.append(pltpu.make_async_copy(source, here, sem.at[1 + 2 * k]))
        arriving[-1].start()
    first.wait()
    for target, (k, rows) in zip(outputs[2 + len(LARGE) :], SMALL_ROWS.values()):
        at = small_at + k
        if rows == 8:
            for s in range(target.shape[0]):
                target[s : s + 1, 0:c] = gradients_here[at + 2 * s : at + 2 * s + 1, :]
                target[s : s + 1, c : 2 * c] = gradients_here[at + 2 * s + 1 : at + 2 * s + 2, :]
        else:
            target[...] = gradients_here[at : at + rows, :]
    for k, (_, here, target) in enumerate(moves):
        arriving[k].wait()
        leaving.append(pltpu.make_async_copy(here, target, sem.at[2 + 2 * k]))
        leaving[-1].start()
    for copy in leaving:
        copy.wait()


def whole_items(shape, *arguments):
    line = shape["rows"]
    whole = Given(*arguments)
    given = whole._asdict()
    frames, cotangent = whole.frames, whole.cotangent
    items, history, strip, width = frames.shape
    c = cotangent.shape[-1]
    cells = strip * line * width
    flat = {}
    for name, value in given.items():
        if value is cotangent:
            value = value.reshape(items, strip * width, c)
        elif name in LARGE:
            value = value.reshape(-1, c)
        elif value.ndim == 1 and name not in IN_SMEM:
            value = value.reshape(-1, c)
        flat[name] = value
    shapes = {name: flat[name].shape for name in LARGE}
    big_layout = layout_of(SimpleNamespace(**shapes))
    starts, small_at, total_rows, runs = big_layout
    copies = 7 * (line - 1) + len(runs) * (8 + 2 * (line - 1)) + 6
    landing = sum(rows // 2 + 5 * rows // 8 for _, rows in runs) + LATE_COUNT * (8 + line)
    shifted = pltpu.VMEM((cells + 2 * width, 6 * c), BF16)
    forward = pltpu.VMEM((18 * c, 2 * c), BF16)
    backward = pltpu.VMEM((2 * c, 18 * c), BF16)
    field = pltpu.VMEM((cells, c), F32)
    flipped_field = pltpu.VMEM((2 * c, cells), BF16)
    quarter = cells // 4
    scratch = dict(
        small=pltpu.VMEM((LATE_COUNT, c), F32),
        send=pltpu.SemaphoreType.DMA((copies,)),
        recv=pltpu.SemaphoreType.DMA((copies,)),
        local=pltpu.SemaphoreType.DMA((12 + len(runs),)),
        sums=pltpu.VMEM((total_rows, c), F32),
        final=pltpu.VMEM((total_rows, c), F32),
        landing=pltpu.VMEM((landing, c), F32),
        frames_in=pltpu.VMEM((line, history, strip, width), F32),
        mask_in=pltpu.VMEM((line, strip, width), jnp.int32),
        frames_out=pltpu.VMEM((line, history, strip, width), F32),
        frames_from=pltpu.VMEM((line, history, strip, width), F32),
        frames_here=pltpu.VMEM((line, history, strip, width), F32),
        mask_from=pltpu.VMEM((line, strip, width), jnp.int32),
        cot_from=pltpu.VMEM((items, strip * width, c), F32),
        output_here=pltpu.VMEM((items, strip * width, c), F32),
        fields=pltpu.VMEM((16, cells), F32),
        lift=pltpu.VMEM((16, c), F32),
        joined=pltpu.VMEM((cells, 4 * c), BF16),
        x_down=pltpu.VMEM((quarter, 8 * c), BF16),
        x_grad_up=pltpu.VMEM((quarter, 8 * c), BF16),
        x_up=pltpu.VMEM((quarter, 2 * c), BF16),
        x_grad_low=pltpu.VMEM((quarter, 2 * c), BF16),
        f_down=pltpu.VMEM((8 * c, 2 * c), BF16),
        b_down=pltpu.VMEM((4, 2 * c, 2 * c), BF16),
        f_up=pltpu.VMEM((4, 2 * c, 2 * c), BF16),
        b_up=pltpu.VMEM((2 * c, 8 * c), BF16),
        f_skip=pltpu.VMEM((4 * c, 2 * c), BF16),
        b_skip=pltpu.VMEM((2, 2 * c, 2 * c), BF16),
        xe1=shifted,
        xe2=shifted,
        xd1a=shifted,
        xd1b=shifted,
        xd2=shifted,
        xg=shifted,
        te1=flipped_field,
        te2=flipped_field,
        td1a=flipped_field,
        td1b=flipped_field,
        td2=flipped_field,
        turned=pltpu.VMEM((4 * c, cells), BF16),
        fe1=forward,
        fe2=forward,
        fd1a=forward,
        fd1b=forward,
        fd2=forward,
        be1=backward,
        be2=backward,
        bd1a=backward,
        bd1b=backward,
        bd2=backward,
        slope_e1=field,
        slope_e2=field,
        slope_d1a=field,
        slope_d1b=field,
        slope_d2=field,
        lifted=field,
        middle_e=field,
        encoded=field,
        raised=field,
        middle_d=field,
        result=field,
        cot=field,
        grad=field,
        grad_a=field,
        grad_b=field,
    )
    scratch.update({name: pltpu.VMEM(shapes[name], F32) for name in LARGE})

    in_hbm = pl.BlockSpec(memory_space=pl.ANY)
    in_vmem = pl.BlockSpec(memory_space=pltpu.VMEM)
    in_smem = pl.BlockSpec(memory_space=pltpu.SMEM)
    in_specs = [
        in_hbm if name in IN_HBM else in_smem if name in IN_SMEM else in_vmem
        for name in ARGUMENTS
    ]
    out_shape = [
        jax.ShapeDtypeStruct((items, strip * width, c), F32),
        jax.ShapeDtypeStruct(frames.shape, F32),
        jax.ShapeDtypeStruct((total_rows, c), F32),
    ]
    out_specs = [in_hbm] * 3
    results = pl.pallas_call(
        functools.partial(
            item_kernel,
            (line, strip, width, shapes, big_layout),
            tuple(scratch),
        ),
        out_shape=out_shape,
        in_specs=in_specs,
        out_specs=out_specs,
        scratch_shapes=list(scratch.values()),
        compiler_params=pltpu.CompilerParams(
            collective_id=0, has_side_effects=True, vmem_limit_bytes=62 * 1024 * 1024
        ),
    )(*[flat[name] for name in ARGUMENTS])
    names = LARGE + tuple(SMALL_ROWS)
    written = pl.pallas_call(
        functools.partial(write_kernel, (shapes, starts, small_at)),
        out_shape=out_shape[:2] + [jax.ShapeDtypeStruct(flat[name].shape, F32) for name in names],
        in_specs=[pl.BlockSpec(memory_space=pltpu.HBM)] * 3,
        out_specs=[in_hbm] * (2 + len(LARGE)) + [in_vmem] * len(SMALL_ROWS),
        scratch_shapes=[
            pltpu.VMEM((items, strip * width, c), F32),
            pltpu.VMEM(frames.shape, F32),
            pltpu.VMEM((total_rows, c), F32),
            pltpu.SemaphoreType.DMA((1 + 2 * (2 + len(LARGE)),)),
        ],
        compiler_params=pltpu.CompilerParams(vmem_limit_bytes=60 * 1024 * 1024),
    )(*results)
    grads = dict(zip(names, written[2:]))
    ordered = [name for name in ARGUMENTS if name in grads]
    return (written[0].reshape(cotangent.shape), written[1]) + tuple(
        grads[name].reshape(given[name].shape) for name in ordered
    )


def body(shape, *arguments):
    items, _, strip, width = arguments[0].shape
    line = shape["rows"]
    whole = (
        shape["section"] == 2
        and shape["batch"] == 4
        and items == line == 4
        and arguments[-1].shape[-1] == 128
        and (strip * line * width) % CHUNK == 0
    )
    return whole_items(shape, *arguments) if whole else strips_body(*arguments)


def solution(mesh):
    in_specs = (
        P(("section", "batch"), None, "rows", None),
        P(("section", "batch")),
        P(("section", "batch"), "rows", None),
        P(("section", "batch")),
        P(),
        P(),
        P(),
        P(),
        P(),
        P(),
        P(),
        P(),
        P(),
        P(),
        P(),
        P(),
        P(),
        P(),
        P(),
        P(),
        P(),
        P(),
        P(),
        P(),
        P(),
        P(),
        P(),
        P(),
        P(("section", "batch"), "rows", None, None),
    )
    out_specs = (
        P(("section", "batch"), "rows", None, None),
        P(("section", "batch"), None, "rows", None),
        P(),
        P(),
        P(),
        P(),
        P(),
        P(),
        P(),
        P(),
        P(),
        P(),
        P(),
        P(),
        P(),
        P(),
        P(),
        P(),
        P(),
        P(),
        P(),
        P(),
        P(),
        P(),
        P(),
        P(),
    )
    return jax.shard_map(functools.partial(body, mesh.shape), mesh=mesh, in_specs=in_specs, out_specs=out_specs, check_vma=False)
```

```python
import functools
from types import SimpleNamespace
from typing import Any, NamedTuple

import jax
import jax.numpy as jnp
from jax import lax
from jax.experimental import pallas as pl
from jax.experimental.pallas import tpu as pltpu
from jax.sharding import PartitionSpec as P

GROUPS = 8
FIELDS = 3
HIST = 4


EPS = 1e-05
HIGH = lax.Precision.HIGHEST


def extended(cells, sides, width):
    for axis, dim in sides:
        count = lax.axis_size(axis)
        ends = count - 1
        head = lax.slice_in_dim(cells, 0, width, axis=dim)
        tail = lax.slice_in_dim(cells, cells.shape[dim] - width, cells.shape[dim], axis=dim)
        cells = jnp.concatenate(
            [
                lax.ppermute(tail, axis, [(i, (i + 1) % count) for i in range(ends)]),
                cells,
                lax.ppermute(head, axis, [((i + 1) % count, i) for i in range(ends)]),
            ],
            axis=dim,
        )
    return cells


def from_behind(value, axis, steps):
    count = lax.axis_size(axis)
    pairs = [(source, (source + steps) % count) for source in range(count)]
    return lax.ppermute(value, axis, pairs)


def group_view(value_arrays):
    extent = value_arrays.shape
    return value_arrays.reshape(extent[:-1] + (GROUPS, extent[-1] // GROUPS))


def global_sums(value_arrays):
    grouped = group_view(value_arrays)
    flat = grouped.reshape(-1, GROUPS, grouped.shape[-1])
    first_sum = jnp.sum(flat, axis=(0, 2))
    second_sum = jnp.sum(flat * flat, axis=(0, 2))
    return lax.psum((first_sum, second_sum), "rows")


def apply_norm(value_arrays, sum_one, sum_two, norm_gain, norm_bias, total):
    grouped = group_view(value_arrays)
    group_mean = sum_one / total
    variance = sum_two / total - group_mean * group_mean
    inverse = lax.rsqrt(variance + EPS)
    normed = (grouped - group_mean[:, None]) * inverse[:, None]
    return normed.reshape(value_arrays.shape) * norm_gain + norm_bias


def norm_back(value_arrays, grad_one, grad_two):
    grouped = group_view(value_arrays)
    extra = grad_one[:, None] + 2.0 * grouped * grad_two[:, None]
    return extra.reshape(value_arrays.shape)


def reduce_grads(grad_one, grad_two):
    return lax.psum((grad_one, grad_two), "rows")


def conv_rows(padded, kernel):
    widened = jnp.pad(padded, ((0, 0), (1, 1), (0, 0)))
    return lax.conv_general_dilated(
        widened[None],
        kernel,
        (1, 1),
        "VALID",
        dimension_numbers=("NHWC", "HWIO", "NHWC"),
        precision=HIGH,
    )[0]


def flipped(kernel):
    return jnp.transpose(kernel[::-1, ::-1], (0, 1, 3, 2))


def pad_grads(value_arrays):
    return extended(value_arrays, (("rows", 0),), 1)


def totals_of(inputs, conv1):
    strip = inputs.shape[0]
    cells = strip * lax.axis_size("rows") * inputs.shape[1]
    return (cells * (inputs.shape[2] // GROUPS), cells * (conv1.shape[3] // GROUPS))


def block_forward(inputs, weights, scale_part, shift_part):
    norm1_gain, norm1_bias, conv1, norm2_gain, norm2_bias, conv2, conv2_bias = weights
    total_in, total_mid = totals_of(inputs, conv1)
    sums_in = global_sums(inputs)

    def pad_rows(value_arrays):
        return extended(value_arrays, (("rows", 0),), 1)

    act_one = pad_rows(
        jax.nn.gelu(
            apply_norm(inputs, sums_in[0], sums_in[1], norm1_gain, norm1_bias, total_in),
            approximate=False,
        )
    )
    middle = conv_rows(act_one, conv1)
    sums_mid = global_sums(middle)
    shaped = (
        apply_norm(middle, sums_mid[0], sums_mid[1], norm2_gain, norm2_bias, total_mid)
        * (1.0 + scale_part)
        + shift_part
    )
    act_two = pad_rows(jax.nn.gelu(shaped, approximate=False))
    branch = conv_rows(act_two, conv2) + conv2_bias
    return (branch, (sums_in[0], sums_in[1], act_one, middle, sums_mid[0], sums_mid[1], act_two))


def block_backward(inputs, weights, scale_part, shift_part, kept, grad_out):
    norm1_gain, norm1_bias, conv1, norm2_gain, norm2_bias, conv2, conv2_bias = weights
    in_one, in_two, act_one, middle, mid_one, mid_two, act_two = kept
    total_in, total_mid = totals_of(inputs, conv1)
    grad_conv2 = jax.vjp(lambda kernel: conv_rows(act_two, kernel), conv2)[1](grad_out)[0]
    grad_bias2 = jnp.sum(grad_out, axis=(0, 1))
    grad_act_two = conv_rows(pad_grads(grad_out), flipped(conv2))

    def second_piece(middle_in, sum_one, sum_two, gain_in, incoming_bias, scale_in, shift_in):
        shaped = (
            apply_norm(middle_in, sum_one, sum_two, gain_in, incoming_bias, total_mid)
            * (1.0 + scale_in)
            + shift_in
        )
        return jax.nn.gelu(shaped, approximate=False)

    second_pull = jax.vjp(
        second_piece, middle, mid_one, mid_two, norm2_gain, norm2_bias, scale_part, shift_part
    )[1](grad_act_two)
    summed_one, summed_two = reduce_grads(second_pull[1], second_pull[2])
    grad_middle = second_pull[0] + norm_back(middle, summed_one, summed_two)
    grad_conv1 = jax.vjp(lambda kernel: conv_rows(act_one, kernel), conv1)[1](grad_middle)[0]
    grad_act_one = conv_rows(pad_grads(grad_middle), flipped(conv1))

    def first_piece(inputs_in, sum_one, sum_two, gain_in, incoming_bias):
        return jax.nn.gelu(
            apply_norm(inputs_in, sum_one, sum_two, gain_in, incoming_bias, total_in),
            approximate=False,
        )

    first_pull = jax.vjp(first_piece, inputs, in_one, in_two, norm1_gain, norm1_bias)[1](
        grad_act_one
    )
    first_one, first_two = reduce_grads(first_pull[1], first_pull[2])
    grad_inputs = first_pull[0] + norm_back(inputs, first_one, first_two)
    grads = (
        first_pull[3],
        first_pull[4],
        grad_conv1,
        second_pull[3],
        second_pull[4],
        grad_conv2,
        grad_bias2,
    )
    return (grad_inputs, grads, second_pull[5], second_pull[6])


def conditioning(step_item, table):
    one_hot = (jnp.arange(table.shape[0], dtype=jnp.int32) == step_item).astype(jnp.float32)
    condition = jnp.dot(one_hot, table, precision=HIGH)
    half_width = table.shape[1] // 2
    return (condition[:half_width], condition[half_width:], one_hot)


def project_in(frames_item, mask_item, count_item, incoming_weight, incoming_bias):
    history = jnp.arange(HIST, dtype=jnp.int32) >= HIST - count_item
    keep = jnp.repeat(history, FIELDS).astype(jnp.float32)
    lifted = (
        jnp.einsum(
            "fhw,fc->hwc", frames_item * keep[:, None, None], incoming_weight, precision=HIGH
        )
        + incoming_bias
    )
    return lifted * mask_item[:, :, None].astype(jnp.float32)


def coarsen_field(value_arrays, incoming_weight, incoming_bias):
    rows_here, width_here, depth_here = value_arrays.shape
    blocks = value_arrays.reshape(rows_here // 2, 2, width_here // 2, 2, depth_here)
    return jnp.einsum("iajbk,abkc->ijc", blocks, incoming_weight, precision=HIGH) + incoming_bias


def upsample(value_arrays, incoming_weight, incoming_bias):
    result = jnp.einsum("ijk,abkc->iajbc", value_arrays, incoming_weight, precision=HIGH)
    extent = result.shape
    return result.reshape(extent[0] * 2, extent[2] * 2, extent[4]) + incoming_bias


def flatten_all(pieces):
    return jnp.concatenate([piece.reshape(-1) for piece in pieces])


def unflatten_all(flat, templates):
    pieces = []
    offset_at = 0
    for template in templates:
        count_here = template.size
        pieces.append(flat[offset_at : offset_at + count_here].reshape(template.shape))
        offset_at += count_here
    return tuple(pieces)


def strips_body(
    frames,
    counts,
    cell_mask,
    step_index,
    lift_weight,
    lift_bias,
    enc_norm1_gain,
    enc_norm1_bias,
    enc_conv1,
    enc_step_table,
    enc_norm2_gain,
    enc_norm2_bias,
    enc_conv2,
    enc_conv2_bias,
    reducer_weight,
    reducer_bias,
    up_weight,
    up_bias,
    dec_norm1_gain,
    dec_norm1_bias,
    dec_conv1,
    dec_step_table,
    dec_norm2_gain,
    dec_norm2_bias,
    dec_conv2,
    dec_conv2_bias,
    skip_weight,
    skip_bias,
    cotangent,
):
    enc_weights = (
        enc_norm1_gain,
        enc_norm1_bias,
        enc_conv1,
        enc_norm2_gain,
        enc_norm2_bias,
        enc_conv2,
        enc_conv2_bias,
    )
    dec_weights = (
        dec_norm1_gain,
        dec_norm1_bias,
        dec_conv1,
        dec_norm2_gain,
        dec_norm2_bias,
        dec_conv2,
        dec_conv2_bias,
    )
    params = (
        lift_weight,
        lift_bias,
        enc_norm1_gain,
        enc_norm1_bias,
        enc_conv1,
        enc_step_table,
        enc_norm2_gain,
        enc_norm2_bias,
        enc_conv2,
        enc_conv2_bias,
        reducer_weight,
        reducer_bias,
        up_weight,
        up_bias,
        dec_norm1_gain,
        dec_norm1_bias,
        dec_conv1,
        dec_step_table,
        dec_norm2_gain,
        dec_norm2_bias,
        dec_conv2,
        dec_conv2_bias,
        skip_weight,
        skip_bias,
    )

    def forward_micro(carry, sliced):
        frames_item, mask_item, count_item, step_item = sliced
        lifted = project_in(frames_item, mask_item, count_item, lift_weight, lift_bias)
        enc_scale, enc_shift, unused_hot = conditioning(step_item, enc_step_table)
        enc_branch, enc_kept = block_forward(lifted, enc_weights, enc_scale, enc_shift)
        encoder_result = lifted + enc_branch
        coarse_field = coarsen_field(encoder_result, reducer_weight, reducer_bias)
        foreign = from_behind(coarse_field, "section", 1)
        raised_foreign = upsample(foreign, up_weight, up_bias)
        raised = from_behind(raised_foreign, "section", 1)
        joined = jnp.concatenate([raised, encoder_result], axis=-1)
        dec_scale, dec_shift, unused_again = conditioning(step_item, dec_step_table)
        dec_branch, dec_kept = block_forward(joined, dec_weights, dec_scale, dec_shift)
        output_item = jnp.dot(joined, skip_weight, precision=HIGH) + skip_bias + dec_branch
        return (carry, (output_item, (lifted, enc_kept, encoder_result, foreign, joined, dec_kept)))

    unused, (output, kept_all) = lax.scan(
        forward_micro, jnp.zeros((), jnp.float32), (frames, cell_mask, counts, step_index)
    )

    def backward_micro(totals, sliced):
        frames_item, mask_item, count_item, step_item, grad_out, kept = sliced
        lifted, enc_kept, encoder_result, foreign, joined, dec_kept = kept
        dec_scale, dec_shift, one_hot = conditioning(step_item, dec_step_table)
        grad_joined, dec_grads, dec_gscale, dec_gshift = block_backward(
            joined, dec_weights, dec_scale, dec_shift, dec_kept, grad_out
        )
        grad_skip_weight = jnp.einsum("hwk,hwc->kc", joined, grad_out, precision=HIGH)
        grad_skip_bias = jnp.sum(grad_out, axis=(0, 1))
        grad_joined = grad_joined + jnp.dot(grad_out, skip_weight.T, precision=HIGH)
        half_width = joined.shape[-1] // 2
        grad_raised = grad_joined[..., :half_width]
        grad_encoded = grad_joined[..., half_width:]
        grad_foreign_up = from_behind(grad_raised, "section", 1)
        up_pull = jax.vjp(upsample, foreign, up_weight, up_bias)[1](grad_foreign_up)
        coarse_gradient = from_behind(up_pull[0], "section", 1)
        reducer_pullback = jax.vjp(coarsen_field, encoder_result, reducer_weight, reducer_bias)[1](
            coarse_gradient
        )
        grad_encoded = grad_encoded + reducer_pullback[0]
        enc_scale, enc_shift, enc_hot = conditioning(step_item, enc_step_table)
        grad_lifted, enc_grads, enc_gscale, enc_gshift = block_backward(
            lifted, enc_weights, enc_scale, enc_shift, enc_kept, grad_encoded
        )
        grad_lifted = grad_lifted + grad_encoded
        proj_pull = jax.vjp(
            lambda frames_in, incoming_weight, incoming_bias: project_in(
                frames_in, mask_item, count_item, incoming_weight, incoming_bias
            ),
            frames_item,
            lift_weight,
            lift_bias,
        )[1](grad_lifted)
        enc_table_grad = enc_hot[:, None] * jnp.concatenate([enc_gscale, enc_gshift])[None, :]
        dec_table_grad = one_hot[:, None] * jnp.concatenate([dec_gscale, dec_gshift])[None, :]
        micro_list = (
            proj_pull[1],
            proj_pull[2],
            enc_grads[0],
            enc_grads[1],
            enc_grads[2],
            enc_table_grad,
            enc_grads[3],
            enc_grads[4],
            enc_grads[5],
            enc_grads[6],
            reducer_pullback[1],
            reducer_pullback[2],
            up_pull[1],
            up_pull[2],
            dec_grads[0],
            dec_grads[1],
            dec_grads[2],
            dec_table_grad,
            dec_grads[3],
            dec_grads[4],
            dec_grads[5],
            dec_grads[6],
            grad_skip_weight,
            grad_skip_bias,
        )
        micro_flat = flatten_all(micro_list)
        return (totals + micro_flat, proj_pull[0])

    total_size = sum((piece.size for piece in params))
    start_totals = jnp.zeros((total_size,), jnp.float32)
    flat_totals, frames_grad = lax.scan(
        backward_micro,
        start_totals,
        (frames, cell_mask, counts, step_index, cotangent, kept_all),
        reverse=True,
    )
    flat_totals = lax.psum(flat_totals, ("section", "batch", "rows"))
    grads = unflatten_all(flat_totals, params)
    return (output, frames_grad) + grads


F32 = jnp.float32
BF16 = jnp.bfloat16
MESH = pl.DeviceIdType.MESH
NN = ((1,), (0,))
NT = ((1,), (1,))
TN = ((0,), (0,))
HIGH_AT = (0, 2, 1)
LOW_AT = (4, 3, 5)
CHUNK = 512
class Given(NamedTuple):
    frames: Any
    counts: Any
    cell_mask: Any
    step_index: Any
    lift_weight: Any
    lift_bias: Any
    enc_norm1_gain: Any
    enc_norm1_bias: Any
    enc_conv1: Any
    enc_step_table: Any
    enc_norm2_gain: Any
    enc_norm2_bias: Any
    enc_conv2: Any
    enc_conv2_bias: Any
    reducer_weight: Any
    reducer_bias: Any
    up_weight: Any
    up_bias: Any
    dec_norm1_gain: Any
    dec_norm1_bias: Any
    dec_conv1: Any
    dec_step_table: Any
    dec_norm2_gain: Any
    dec_norm2_bias: Any
    dec_conv2: Any
    dec_conv2_bias: Any
    skip_weight: Any
    skip_bias: Any
    cotangent: Any


ARGUMENTS = Given._fields
LARGE = tuple(
    dict(
        dec_conv2=0,
        skip_weight=0,
        dec_conv1=0,
        enc_conv1=0,
        up_weight=0,
        reducer_weight=0,
        enc_conv2=0,
    )
)
IN_HBM = tuple(dict(frames=0, cell_mask=0, cotangent=0)) + LARGE
IN_SMEM = tuple(dict(counts=0, step_index=0))
LATE = 64
SMALL_ROWS = dict(
    enc_conv2_bias=(0, 1),
    reducer_bias=(1, 1),
    up_bias=(2, 1),
    dec_conv2_bias=(3, 1),
    skip_bias=(3, 1),
    dec_norm1_gain=(4, 2),
    dec_norm1_bias=(6, 2),
    dec_norm2_gain=(8, 1),
    dec_norm2_bias=(9, 1),
    dec_step_table=(16, 8),
    lift_weight=(LATE, 12),
    lift_bias=(LATE + 12, 1),
    enc_norm1_gain=(LATE + 16, 1),
    enc_norm1_bias=(LATE + 17, 1),
    enc_norm2_gain=(LATE + 18, 1),
    enc_norm2_bias=(LATE + 19, 1),
    enc_step_table=(LATE + 24, 8),
)
LATE_COUNT = 32
SMALL_COUNT = LATE + LATE_COUNT
DUE = ((), (), (), (), (), (0,), (), (), (), (), (), (), (), (0,), (1,), (), (), (), (), (), (0,), (), (), (), (), (), (), (2, 1, 0), ())
REST = (3, 4, 0, 1, 2, 3, 4, 1, 2, 3, 0, 1, 2, 0, 3, 2, 1, 3, 1, 2, 3, 2, 3)
OUTPUTS = tuple(dict(output=0, frames_grad=0, gradients=0))


def split(value):
    high = value.astype(BF16)
    return high, (value - high.astype(F32)).astype(BF16)


def dot(left, right, dims=NN, precision=None):
    return lax.dot_general(
        left, right, (dims, ((), ())), precision=precision, preferred_element_type=F32
    )


def fold(value):
    half = value.shape[1] // 2
    return value[:, :half] + value[:, half:]


def fold_rows(value):
    half = value.shape[0] // 2
    return value[:half] + value[half:]


def tile_sums(value):
    return jnp.sum(value.reshape(-1, 8, value.shape[-1]), axis=0)


def column_sum(tiles):
    return jnp.sum(tiles, axis=0, keepdims=True)


def normal(value):
    bell = jnp.exp(-0.5 * value * value)
    t = 1.0 / (1.0 + 0.2316418882663604 * jnp.abs(value))
    poly = 0.5307027145
    for factor in (-0.7265760135, 0.7107068705, -0.142248368, 0.127414796):
        poly = poly * t + factor
    tail = poly * t * bell
    return jnp.where(value < 0.0, tail, 1.0 - tail), 0.3989422804014327 * bell


def dot_three(left, right, dims=NN):
    left_high, left_low = split(left)
    right_high, right_low = split(right)
    total = dot(left_high, right_high, dims)
    return total + (dot(left_high, right_low, dims) + dot(left_low, right_high, dims))


def group_ones(channels, size):
    rows = lax.broadcasted_iota(jnp.int32, (channels, channels), 0) // size
    columns = lax.broadcasted_iota(jnp.int32, (channels, channels), 1) // size
    return (rows == columns).astype(BF16)


def group_sums(first, second, ones):
    terms = []
    rest = jnp.concatenate([first, second], axis=0)
    for _ in range(3):
        term = rest.astype(BF16)
        terms.append(term)
        rest = rest - term.astype(F32)
    both = dot(jnp.concatenate(terms, axis=0), ones)
    both = both[32:48] + both[16:32] + both[:16]
    return column_sum(both[:8]), column_sum(both[8:])


class Exchange:

    def __init__(self, place, start, rows, landing, first_sem):
        self.place, self.start, self.rows, self.landing = place, start, rows, landing
        self.sem = first_sem
        self.stage = 0
        self.copies = []
        self.waiting = []
        self.group = place.plane_group
        self.half = rows // 2
        self.base = start + place.core * self.half
        self._finish(self.half)

    def _finish(self, size):
        self.part = size // self.group.count
        self.own = self.base + self.group.here * self.part

    def count(self):
        return 2 + 2 * (self.group.count - 1) + 3

    def land_rows(self):
        return self.half + (self.group.count + 1) * self.part

    def _copy(self, source, target, device, only=None):
        place = self.place
        copy = pltpu.make_async_remote_copy(
            src_ref=source,
            dst_ref=target,
            send_sem=place.send.at[self.sem],
            recv_sem=place.recv.at[self.sem],
            device_id=device,
            device_id_type=MESH,
        )
        self.sem += 1
        if only is None:
            copy.start()
            self.waiting.append(copy)
        self.copies.append((copy, only))
        return copy

    def _wait(self):
        for copy in self.waiting:
            copy.wait_recv()
        self.waiting = []

    def _rows(self, at, size):
        return pl.ds(pl.multiple_of(at, 8), size)

    def _swap(self):
        place = self.place
        other = self._rows(self.start + (1 - place.core) * self.half, self.half)
        self.land = self.landing
        self.landing += self.half
        self._copy(
            place.sums.at[other], place.landing.at[pl.ds(self.land, self.half)], place.partner
        )

    def _add_swap(self):
        place = self.place
        block = 64 if self.half % 64 == 0 else 32

        def step(i, carry):
            here = self._rows(self.base + i * block, block)
            there = self._rows(self.land + i * block, block)
            place.sums[here] = place.sums[here] + place.landing[there]
            return carry

        lax.fori_loop(0, self.half // block, step, 0)

    def _scatter(self, group, base, size):
        place = self.place
        self.land = self.landing
        for k in range(1, group.count):
            to = lax.rem(group.here + k, group.count)
            self._copy(
                place.sums.at[self._rows(base + to * size, size)],
                place.landing.at[pl.ds(self.landing, size)],
                group.device(to),
            )
            self.landing += size

    def _total(self, group, own, size, target):
        place = self.place
        block = 16 if size % 16 == 0 else 8

        def step(i, carry):
            here = self._rows(own + i * block, block)
            total = place.sums[here]
            for k in range(group.count - 1):
                there = self._rows(self.land + k * size + i * block, block)
                total = total + place.landing[there]
            target[here] = total
            return carry

        lax.fori_loop(0, size // block, step, 0)

    def _gather(self, group, own, size):
        final = self.place.final
        here = self._rows(own, size)
        for k in range(1, group.count):
            to = lax.rem(group.here + k, group.count)
            self._copy(final.at[here], final.at[here], group.device(to))

    def _steps(self):
        place, group = self.place, self.group
        yield self._swap()
        self._wait()
        self._add_swap()
        yield from self._both()
        final = place.final
        here = self._rows(self.base, self.half)
        self._copy(final.at[here], final.at[here], place.partner)
        yield
        self._wait()
        yield

    def _both(self):
        place, group = self.place, self.group
        self._scatter(group, self.base, self.part)
        yield
        self._wait()
        self._total(group, self.own, self.part, place.sums)
        yield from self._line()
        self._gather(group, self.own, self.part)
        yield
        self._wait()

    def _line(self):
        place, line = self.place, self.place.line
        sums, final, landing = place.sums, place.final, place.landing
        part, own = self.part, self._rows(self.own, self.part)
        inward, across = pl.ds(self.landing, part), pl.ds(self.landing + part, part)
        self.landing += 2 * part
        block = 16 if part % 16 == 0 else 8

        def add(at, target):
            def step(i, carry):
                here = self._rows(self.own + i * block, block)
                target[here] = sums[here] + landing[pl.ds(at + i * block, block)]
                return carry

            lax.fori_loop(0, part // block, step, 0)

        first = self._copy(sums.at[own], landing.at[inward], line.device(line.inner), line.edge)
        second = self._copy(sums.at[own], landing.at[across], line.device(line.across), line.middle)
        third = self._copy(final.at[own], final.at[own], line.device(line.outer), line.middle)
        pl.when(line.edge)(first.start)
        yield

        @pl.when(line.middle)
        def _():
            first.wait_recv()
            add(self.landing - 2 * part, sums)
            second.start()

        yield

        @pl.when(line.middle)
        def _():
            second.wait_recv()
            add(self.landing - part, final)
            third.start()

        yield
        pl.when(line.edge)(third.wait_recv)

    def advance(self):
        if self.stage == 0:
            self.steps = self._steps()
        self.stage += 1
        next(self.steps)

    def done(self):
        return self.stage == 8


class SmallExchange(Exchange):

    def count(self):
        return self.place.cores_group.count + self.place.line.count - 2

    def land_rows(self):
        return self.rows * (self.place.cores_group.count + self.place.line.count)

    def _share(self, group, source):
        place = self.place
        self.land = self.landing
        self.landing += group.count * self.rows
        own = self._rows(self.land + group.here * self.rows, self.rows)
        place.landing[own] = source[...]
        for k in range(1, group.count):
            to = lax.rem(group.here + k, group.count)
            self._copy(source, place.landing.at[own], group.device(to))

    def _sum(self, group):
        total = None
        for k in range(group.count):
            part = self.place.landing[pl.ds(self.land + k * self.rows, self.rows)]
            total = part if total is None else total + part
        return total

    def _steps(self):
        place = self.place
        here = pl.ds(self.start, self.rows)
        self._share(place.line, place.sums.at[here])
        yield
        self._wait()
        place.small[...] = self._sum(place.line)
        self._share(place.cores_group, place.small)
        yield
        self._wait()
        place.final[here] = self._sum(place.cores_group)
        yield

    def done(self):
        return self.stage == 3


def layout_of(shapes):
    starts = {}
    at = 0
    for name in LARGE:
        starts[name] = at
        at += getattr(shapes, name)[0]
    small = at
    begins = SimpleNamespace(**starts)
    late = small + LATE
    edges = (
        (begins.dec_conv2, begins.dec_conv1),
        (begins.dec_conv1, begins.enc_conv1),
        (begins.up_weight, late),
        (begins.enc_conv1, begins.up_weight),
        (late, late + LATE_COUNT),
    )
    runs = [(first, last - first) for first, last in edges]
    return starts, small, late + LATE_COUNT, runs


def item_kernel(sizes, scratch_names, *refs):
    line, strip, width, shapes, big_layout = sizes
    begins, small_at, total_rows, runs = big_layout
    starts = SimpleNamespace(**begins)
    inputs = Given(*refs[: len(ARGUMENTS)])
    refs = refs[len(ARGUMENTS) :]
    output_names = OUTPUTS
    outputs = SimpleNamespace(**dict(zip(output_names, refs)))
    scratch = SimpleNamespace(**dict(zip(scratch_names, refs[len(output_names) :])))

    def w_of(name):
        return getattr(scratch, name)

    height = strip * line
    cells = height * width
    c = inputs.lift_weight.shape[1]
    strip_cells = strip * width
    history = inputs.frames.shape[1]

    core = lax.axis_index("section")
    plane = lax.axis_index("batch")
    row = lax.axis_index("rows")
    middle = lax.rem(row + 1, 4) // 2

    def device_at(to):
        return (core, plane, to)

    place = SimpleNamespace(
        core=core,
        partner=(1 - core, plane, row),
        line=SimpleNamespace(
            count=line,
            here=row,
            device=device_at,
            middle=middle == 1,
            edge=middle == 0,
            inner=1 + row // 2,
            across=3 - row,
            outer=3 * (row // 2),
        ),
        plane_group=SimpleNamespace(
            count=4, here=plane, device=lambda to: (core, to, row)
        ),
        cores_group=SimpleNamespace(
            count=8,
            here=core * 4 + plane,
            device=lambda to: (to // 4, lax.rem(to, 4), row),
        ),
        small=scratch.small,
        sums=scratch.sums,
        final=scratch.final,
        landing=scratch.landing,
        send=scratch.send,
        recv=scratch.recv,
    )
    local_sem = scratch.local

    frames_in, mask_in, cot = scratch.frames_in, scratch.mask_in, scratch.cot
    here_rows = pl.ds(pl.multiple_of(row * strip_cells, strip_cells), strip_cells)
    frames_from, mask_from, cot_from = scratch.frames_from, scratch.mask_from, scratch.cot_from
    staged = (
        pltpu.make_async_copy(inputs.frames, frames_from, local_sem.at[7]),
        pltpu.make_async_copy(inputs.cell_mask, mask_from, local_sem.at[8]),
        pltpu.make_async_copy(inputs.cotangent, cot_from, local_sem.at[9]),
    )
    for copy in staged:
        copy.start()

    weight_copies = {}
    for k, name in enumerate(LARGE):
        copy = pltpu.make_async_copy(getattr(inputs, name), w_of(name), local_sem.at[k])
        weight_copies[name] = copy
        copy.start()

    barrier = pltpu.get_barrier_semaphore()
    peers = [device_at(lax.rem(row + k, line)) for k in range(1, line)]
    cores_group = place.cores_group
    for k in range(1, 8):
        peers.append(cores_group.device(lax.rem(cores_group.here + k, 8)))
    for device in peers:
        pl.semaphore_signal(barrier, inc=1, device_id=device, device_id_type=MESH)
    pl.semaphore_wait(barrier, len(peers))

    next_sem = 0

    def send(source, target, device):
        nonlocal next_sem
        copy = pltpu.make_async_remote_copy(
            src_ref=source,
            dst_ref=target,
            send_sem=scratch.send.at[next_sem],
            recv_sem=scratch.recv.at[next_sem],
            device_id=device,
            device_id_type=MESH,
        )
        next_sem += 1
        copy.start()
        return copy

    frame_copies, cot_copies, output_copies = [], [], []
    for copy in staged[:2]:
        copy.wait()
    for k in range(1, line):
        to = lax.rem(row + k, line)
        device = device_at(to)
        frame_copies.append(send(frames_from.at[to], frames_in.at[row], device))
        frame_copies.append(send(mask_from.at[to], mask_in.at[row], device))
    staged[2].wait()
    for k in range(1, line):
        to = lax.rem(row + k, line)
        cot_copies.append(
            send(cot_from.at[to], cot.at[here_rows], device_at(to))
        )

    copied = SimpleNamespace(**weight_copies)
    def stack_conv(source, half, depth, forward, backward):
        for a in range(3):
            for b in range(3):
                at = (3 * a + b) * depth + half * c
                high, low = split(source[at : at + c, :])
                for block in (HIGH_AT[b], LOW_AT[b]):
                    rows = slice((6 * a + block) * c, (6 * a + block + 1) * c)
                    forward[rows, 0:c] = high
                    forward[rows, c : 2 * c] = low
                for block in (HIGH_AT[2 - b], LOW_AT[2 - b]):
                    tap = 6 * (2 - a) + block
                    columns = slice(tap * c, (tap + 1) * c)
                    backward[0:c, columns] = high
                    backward[c : 2 * c, columns] = low

    copied.enc_conv1.wait()
    stack_conv(scratch.enc_conv1, 0, c, scratch.fe1, scratch.be1)
    copied.enc_conv2.wait()
    stack_conv(scratch.enc_conv2, 0, c, scratch.fe2, scratch.be2)
    copied.reducer_weight.wait()
    for k in range(4):
        high, low = split(scratch.reducer_weight[k * c : (k + 1) * c, :])
        for block in (k, k + 4):
            scratch.f_down[block * c : (block + 1) * c, 0:c] = high
            scratch.f_down[block * c : (block + 1) * c, c : 2 * c] = low
        for block in (0, 1):
            columns = slice(block * c, (block + 1) * c)
            scratch.b_down[k, 0:c, columns] = high
            scratch.b_down[k, c : 2 * c, columns] = low
    copied.up_weight.wait()
    for k in range(4):
        high, low = split(scratch.up_weight[k * c : (k + 1) * c, :])
        for block in (0, 1):
            rows = slice(block * c, (block + 1) * c)
            scratch.f_up[k, rows, 0:c] = high
            scratch.f_up[k, rows, c : 2 * c] = low
        for block in (k, k + 4):
            columns = slice(block * c, (block + 1) * c)
            scratch.b_up[0:c, columns] = high
            scratch.b_up[c : 2 * c, columns] = low
    copied.dec_conv1.wait()
    stack_conv(scratch.dec_conv1, 0, 2 * c, scratch.fd1a, scratch.bd1a)
    stack_conv(scratch.dec_conv1, 1, 2 * c, scratch.fd1b, scratch.bd1b)
    copied.dec_conv2.wait()
    stack_conv(scratch.dec_conv2, 0, c, scratch.fd2, scratch.bd2)
    copied.skip_weight.wait()
    for half in range(2):
        high, low = split(scratch.skip_weight[half * c : (half + 1) * c, :])
        for block in (half, half + 2):
            scratch.f_skip[block * c : (block + 1) * c, 0:c] = high
            scratch.f_skip[block * c : (block + 1) * c, c : 2 * c] = low
        for block in (0, 1):
            columns = slice(block * c, (block + 1) * c)
            scratch.b_skip[half, 0:c, columns] = high
            scratch.b_skip[half, c : 2 * c, columns] = low

    for buffer in (scratch.xe1, scratch.xe2, scratch.xd1a, scratch.xd1b, scratch.xd2, scratch.xg):
        edge = jnp.zeros((width, 6 * c), BF16)
        buffer[0:width, :] = edge
        buffer[cells + width : cells + 2 * width, :] = edge

    lift = scratch.lift
    lift[...] = jnp.zeros(lift.shape, F32)
    lift[0:history, :] = inputs.lift_weight[...]
    lift[history : history + 1, :] = inputs.lift_bias[...]

    block = 2 * width
    column = lax.rem(lax.broadcasted_iota(jnp.int32, (block, c), 0), width)
    at_first, at_last = column == 0, column == width - 1
    zeros8 = jnp.zeros((8, c), F32)
    ones16 = group_ones(c, c // GROUPS)
    ones32 = group_ones(c, 2 * c // GROUPS)
    count16 = float(cells * (c // GROUPS))
    count32 = float(cells * (2 * c // GROUPS))

    def grid_rows(step, carry=0):
        return lax.fori_loop(0, cells // block, step, carry, unroll=2)

    def row_at(h):
        return pl.ds(pl.multiple_of(h * block, block), block)

    def chunk_at(i):
        return pl.ds(pl.multiple_of(i * CHUNK, CHUNK), CHUNK)

    def put_row(target, h, value):
        rows = pl.ds(pl.multiple_of(h * block + width, width), block)
        left = jnp.where(at_first, 0.0, pltpu.roll(value, 1, 0))
        right = jnp.where(at_last, 0.0, pltpu.roll(value, block - 1, 0))
        for b, piece in enumerate((left, value, right)):
            high, low = split(piece)
            target[rows, HIGH_AT[b] * c : (HIGH_AT[b] + 1) * c] = high
            target[rows, LOW_AT[b] * c : (LOW_AT[b] + 1) * c] = low

    def put_turned(target, columns, value, first=0, second=1):
        high, low = split(value.T)
        target[first * c : (first + 1) * c, columns] = high
        target[second * c : (second + 1) * c, columns] = low

    def conv_chunk(pairs, i, dims=NN):
        total = None
        for data, weight in pairs:
            taps = []
            for a in range(3):
                rows = pl.ds(pl.multiple_of(i * CHUNK + a * width, width), CHUNK)
                taps.append(data[rows, :])
            part = dot(jnp.concatenate(taps, axis=1), weight[...], dims)
            total = part if total is None else total + part
        return total

    def norm_of(first, second, ones, count):
        one, two = group_sums(first, second, ones)
        mean = one / count
        return mean, lax.rsqrt(two / count - mean * mean + EPS)

    def activate(source, target, turned, slope, scale, shift):
        def step(h, carry):
            value = source[row_at(h), :] * scale + shift
            below, density = normal(value)
            slope[row_at(h), :] = below + value * density
            value = value * below
            put_row(target, h, value)
            put_turned(turned, row_at(h), value)
            return carry

        grid_rows(step)

    def conv_norm(pairs, target):
        def step(i, carry):
            value = fold(conv_chunk(pairs, i))
            target[chunk_at(i), :] = value
            return carry[0] + tile_sums(value), carry[1] + tile_sums(value * value)

        return lax.fori_loop(0, cells // CHUNK, step, (zeros8, zeros8))

    def sums_of(source):
        def step(h, carry):
            value = source[row_at(h), :]
            return carry[0] + tile_sums(value), carry[1] + tile_sums(value * value)

        return grid_rows(step, (zeros8, zeros8))

    step_here = jnp.full((1, c), inputs.step_index[row], jnp.int32)

    def condition(table):
        total = jnp.zeros((1, 2 * c), F32)
        chosen = jnp.concatenate([step_here, step_here], axis=1)
        for s in range(table.shape[0]):
            total = total + jnp.where(chosen == s, table[s : s + 1, :], 0.0)
        return total[:, :c], total[:, c:]

    frames_in[row] = frames_from[row]
    mask_in[row] = mask_from[row]
    for copy in frame_copies:
        copy.wait_recv()
    fields = scratch.fields
    fields[...] = jnp.zeros(fields.shape, F32)
    frame_of = lax.broadcasted_iota(jnp.int32, (history, width), 0) // FIELDS
    keep = (frame_of >= HIST - inputs.counts[row]).astype(F32)
    masks = []
    for source in range(line):
        for k in range(strip):
            columns = slice((source * strip + k) * width, (source * strip + k + 1) * width)
            mask = mask_in[source, k : k + 1, :].astype(F32)
            masks.append(mask)
            fields[0:history, columns] = frames_in[source, :, k, :] * keep * mask
            fields[history : history + 1, columns] = mask
    lifted = scratch.lifted
    lifted[...] = dot_three(fields[...], lift[...], TN)

    enc_scale, enc_shift = condition(inputs.enc_step_table)
    dec_scale, dec_shift = condition(inputs.dec_step_table)

    mean_e1, inv_e1 = norm_of(*sums_of(lifted), ones16, count16)
    gain_e1, bias_e1 = inputs.enc_norm1_gain[...], inputs.enc_norm1_bias[...]
    a_e1 = inv_e1 * gain_e1
    activate(lifted, scratch.xe1, scratch.te1, scratch.slope_e1, a_e1, bias_e1 - mean_e1 * a_e1)
    middle_e = scratch.middle_e
    mean_e2, inv_e2 = norm_of(
        *conv_norm([(scratch.xe1, scratch.fe1)], middle_e), ones16, count16
    )
    gain_e2, bias_e2 = inputs.enc_norm2_gain[...], inputs.enc_norm2_bias[...]
    a_e2 = inv_e2 * gain_e2
    activate(
        middle_e,
        scratch.xe2,
        scratch.te2,
        scratch.slope_e2,
        a_e2 * (1.0 + enc_scale),
        (bias_e2 - mean_e2 * a_e2) * (1.0 + enc_scale) + enc_shift,
    )
    encoded = scratch.encoded
    conv2_bias = inputs.enc_conv2_bias[...]
    joined = scratch.joined

    def encode(i, carry):
        value = fold(conv_chunk([(scratch.xe2, scratch.fe2)], i))
        value = value + conv2_bias + lifted[chunk_at(i), :]
        encoded[chunk_at(i), :] = value
        high, low = split(value)
        joined[chunk_at(i), c : 2 * c] = high
        joined[chunk_at(i), 3 * c : 4 * c] = low
        put_turned(scratch.turned, chunk_at(i), value, 1, 3)
        return carry[0] + tile_sums(value), carry[1] + tile_sums(value * value)

    sums_enc = lax.fori_loop(0, cells // CHUNK, encode, (zeros8, zeros8))

    half_cells, quarter = cells // 2, cells // 4

    def pick(source):
        pieces = []
        for b in range(2):
            value = source[pl.ds(b, half_cells, stride=2), :]
            value = value.reshape(height // 2, 2, width // 2, c)
            pieces.append([value[:, a].reshape(quarter, c) for a in range(2)])
        return [pieces[b][a] for a in range(2) for b in range(2)]

    def place_cells(target, pieces):
        for b in range(2):
            both = [pieces[2 * a + b].reshape(height // 2, 1, width // 2, c) for a in range(2)]
            value = jnp.concatenate(both, axis=1).reshape(half_cells, c)
            target[pl.ds(b, half_cells, stride=2), :] = value

    x_down = scratch.x_down
    for k, piece in enumerate(pick(encoded)):
        high, low = split(piece)
        x_down[:, k * c : (k + 1) * c] = high
        x_down[:, (k + 4) * c : (k + 5) * c] = low
    lowered = fold(dot(x_down[...], scratch.f_down[...])) + inputs.reducer_bias[...]
    x_up = scratch.x_up
    high, low = split(lowered)
    x_up[:, 0:c] = high
    x_up[:, c : 2 * c] = low
    raised = scratch.raised
    up_bias = inputs.up_bias[...]
    place_cells(
        raised, [fold(dot(x_up[...], scratch.f_up[k])) + up_bias for k in range(4)]
    )

    def raise_row(h, carry):
        value = raised[row_at(h), :]
        high, low = split(value)
        joined[row_at(h), 0:c] = high
        joined[row_at(h), 2 * c : 3 * c] = low
        put_turned(scratch.turned, row_at(h), value, 0, 2)
        return carry[0] + tile_sums(value), carry[1] + tile_sums(value * value)

    sums_raised = grid_rows(raise_row, (zeros8, zeros8))

    halves = []
    for half, (source, sums) in enumerate(((raised, sums_raised), (encoded, sums_enc))):
        mean, inv = norm_of(*sums, ones32, count32)
        gain = inputs.dec_norm1_gain[half : half + 1, :]
        bias = inputs.dec_norm1_bias[half : half + 1, :]
        scale = inv * gain
        activate(
            source,
            (scratch.xd1a, scratch.xd1b)[half],
            (scratch.td1a, scratch.td1b)[half],
            (scratch.slope_d1a, scratch.slope_d1b)[half],
            scale,
            bias - mean * scale,
        )
        halves.append((source, mean, inv, gain))
    middle_d = scratch.middle_d
    pairs = [(scratch.xd1a, scratch.fd1a), (scratch.xd1b, scratch.fd1b)]
    mean_d2, inv_d2 = norm_of(*conv_norm(pairs, middle_d), ones16, count16)
    gain_d2, bias_d2 = inputs.dec_norm2_gain[...], inputs.dec_norm2_bias[...]
    a_d2 = inv_d2 * gain_d2
    activate(
        middle_d,
        scratch.xd2,
        scratch.td2,
        scratch.slope_d2,
        a_d2 * (1.0 + dec_scale),
        (bias_d2 - mean_d2 * a_d2) * (1.0 + dec_scale) + dec_shift,
    )
    result = scratch.result
    last_bias = inputs.dec_conv2_bias[...] + inputs.skip_bias[...]

    def decode(i, carry):
        value = conv_chunk([(scratch.xd2, scratch.fd2)], i)
        value = value + dot(joined[chunk_at(i), :], scratch.f_skip[...])
        result[chunk_at(i), :] = fold(value) + last_bias
        return carry

    lax.fori_loop(0, cells // CHUNK, decode, 0)
    output_here, frames_here = scratch.output_here, scratch.frames_here
    output_here[row] = result[here_rows]
    for k in range(1, line):
        to = lax.rem(row + k, line)
        there = pl.ds(pl.multiple_of(to * strip_cells, strip_cells), strip_cells)
        output_copies.append(
            send(result.at[there], output_here.at[row], device_at(to))
        )

    exchanges = []
    waiting_runs = list(runs)
    landing_at = 0
    sem_at = 4 * (line - 1) + 2 * (line - 1)
    sums, final = scratch.sums, scratch.final

    def begin():
        nonlocal landing_at, sem_at
        start, rows = waiting_runs.pop(0)
        kind = Exchange if waiting_runs else SmallExchange
        exchange = kind(place, start, rows, landing_at, sem_at)
        landing_at += exchange.land_rows()
        sem_at += exchange.count()
        exchanges.append(exchange)
        exchange.advance()

    final_copies = []

    def advance(k):
        exchange = exchanges[k]
        exchange.advance()
        if exchange.done():
            rows = pl.ds(exchange.start, exchange.rows)
            copy = pltpu.make_async_copy(
                final.at[rows], outputs.gradients.at[rows], local_sem.at[11 + k]
            )
            copy.start()
            final_copies.append(copy)

    due = list(DUE)

    def point():
        for k in due.pop(0):
            advance(k)

    def small_row(k, value):
        sums[small_at + k : small_at + k + 1, :] = value

    def spread_grad(source):
        def step(h, carry):
            value = source[row_at(h), :]
            put_row(scratch.xg, h, value)
            return carry + tile_sums(value)

        return grid_rows(step, zeros8)

    def weight_grad(turned, at, depth, a):
        rows = pl.ds((2 - a) * width, cells)
        part = fold_rows(dot(turned[...], scratch.xg[rows, :]))
        for b in range(3):
            high, low = HIGH_AT[2 - b] * c, LOW_AT[2 - b] * c
            to = at + (3 * a + b) * depth
            sums[to : to + c, :] = part[:, high : high + c] + part[:, low : low + c]

    def back_conv(weight, slope, target, source, mean, inv):
        carry = (zeros8, zeros8)
        for i in range(cells // CHUNK):
            value = fold(conv_chunk([(scratch.xg, weight)], i, NT)) * slope[chunk_at(i), :]
            target[chunk_at(i), :] = value
            normed = (source[chunk_at(i), :] - mean) * inv
            carry = (carry[0] + tile_sums(value), carry[1] + tile_sums(value * normed))
            if i % (cells // CHUNK // 2) == cells // CHUNK // 2 - 1:
                point()
        return carry

    def norm_grad(sums_in, scale, ones, count):
        one, two = group_sums(sums_in[0] * scale, sums_in[1] * scale, ones)
        return one / count, two / count

    cot[here_rows] = cot_from[row]
    for copy in cot_copies:
        copy.wait_recv()
    total_cot = column_sum(spread_grad(cot))
    for a in range(3):
        weight_grad(scratch.td2, starts.dec_conv2, c, a)
    part = fold(dot(scratch.turned[...], scratch.xg[width : cells + width, 2 * c : 4 * c]))
    sums[starts.skip_weight : starts.skip_weight + 2 * c, :] = fold_rows(part)
    small_row(3, total_cot)
    begin()

    grad = scratch.grad
    sums_d2 = back_conv(scratch.bd2, scratch.slope_d2, grad, middle_d, mean_d2, inv_d2)
    side_grads = (scratch.grad_a, scratch.grad_b)
    for half in range(2):

        def skip_back(i, carry, half=half):
            rows = pl.ds(pl.multiple_of(i * CHUNK + width, width), CHUNK)
            value = dot(scratch.xg[rows, 2 * c : 4 * c], scratch.b_skip[half], NT)
            side_grads[half][chunk_at(i), :] = fold(value)
            return carry

        lax.fori_loop(0, cells // CHUNK, skip_back, 0)
    point()

    def table_rows(k, sums_in, gain, bias, one_plus):
        plain, times = column_sum(sums_in[0]), column_sum(sums_in[1])
        for s in range(inputs.enc_step_table.shape[0]):
            small_row(k + 2 * s, jnp.where(step_here == s, gain * times + bias * plain, 0.0))
            small_row(k + 2 * s + 1, jnp.where(step_here == s, plain, 0.0))
        return one_plus * times, one_plus * plain

    def middle_grad(source, mean, inv, scale, sums_in):
        zero, slope = norm_grad(sums_in, scale, ones16, count16)

        def step(h, carry):
            normed = (source[row_at(h), :] - mean) * inv
            value = inv * (grad[row_at(h), :] * scale - zero - normed * slope)
            put_row(scratch.xg, h, value)
            return carry

        grid_rows(step)

    gain_row, bias_row = table_rows(16, sums_d2, gain_d2, bias_d2, 1.0 + dec_scale)
    small_row(8, gain_row)
    small_row(9, bias_row)
    middle_grad(middle_d, mean_d2, inv_d2, gain_d2 * (1.0 + dec_scale), sums_d2)
    point()
    for a in range(3):
        weight_grad(scratch.td1a, starts.dec_conv1, 2 * c, a)
        weight_grad(scratch.td1b, starts.dec_conv1 + c, 2 * c, a)
        point()
    begin()

    for half, (source, mean, inv, gain) in enumerate(halves):
        sums_in = back_conv(
            (scratch.bd1a, scratch.bd1b)[half],
            (scratch.slope_d1a, scratch.slope_d1b)[half],
            grad,
            source,
            mean,
            inv,
        )
        small_row(4 + half, column_sum(sums_in[1]))
        small_row(6 + half, column_sum(sums_in[0]))
        zero, slope = norm_grad(sums_in, gain, ones32, count32)
        target = side_grads[half]

        def input_grad(h, carry):
            normed = (source[row_at(h), :] - mean) * inv
            value = inv * (grad[row_at(h), :] * gain - zero - normed * slope)
            value = target[row_at(h), :] + value
            target[row_at(h), :] = value
            return carry + tile_sums(value)

        total = grid_rows(input_grad, zeros8)
        if half == 0:
            small_row(2, column_sum(total))
        point()

    grad_raised, grad_encoded = side_grads
    x_grad_up = scratch.x_grad_up
    for k, piece in enumerate(pick(grad_raised)):
        high, low = split(piece)
        x_grad_up[:, k * c : (k + 1) * c] = high
        x_grad_up[:, (k + 4) * c : (k + 5) * c] = low
    grad_lowered = fold(dot(x_grad_up[...], scratch.b_up[...], NT))
    small_row(1, jnp.sum(grad_lowered, axis=0, keepdims=True))
    x_grad_low = scratch.x_grad_low
    high, low = split(grad_lowered)
    x_grad_low[:, 0:c] = high
    x_grad_low[:, c : 2 * c] = low
    point()
    part = fold(fold_rows(dot(x_up[...], x_grad_up[...], TN)))
    for k in range(4):
        at = starts.up_weight + k * c
        sums[at : at + c, :] = part[:, k * c : (k + 1) * c]
    part = fold_rows(fold(dot(x_down[...], x_grad_low[...], TN)))
    sums[starts.reducer_weight : starts.reducer_weight + 4 * c, :] = part
    point()
    place_cells(
        grad, [fold(dot(x_grad_low[...], scratch.b_down[k], NT)) for k in range(4)]
    )

    def join_row(h, carry):
        value = grad_encoded[row_at(h), :] + grad[row_at(h), :]
        grad_encoded[row_at(h), :] = value
        put_row(scratch.xg, h, value)
        return carry + tile_sums(value)

    small_row(0, column_sum(grid_rows(join_row, zeros8)))
    for k in range(10, 16):
        small_row(k, jnp.zeros((1, c), F32))
    sums[small_at + 24 : small_at + LATE, :] = jnp.zeros((LATE - 24, c), F32)
    point()
    for a in range(3):
        weight_grad(scratch.te2, starts.enc_conv2, c, a)
        point()
    begin()
    sums_e2 = back_conv(scratch.be2, scratch.slope_e2, grad, middle_e, mean_e2, inv_e2)
    gain_row, bias_row = table_rows(LATE + 24, sums_e2, gain_e2, bias_e2, 1.0 + enc_scale)
    small_row(LATE + 18, gain_row)
    small_row(LATE + 19, bias_row)
    middle_grad(middle_e, mean_e2, inv_e2, gain_e2 * (1.0 + enc_scale), sums_e2)
    point()
    for a in range(3):
        weight_grad(scratch.te1, starts.enc_conv1, c, a)
        point()
    begin()
    sums_e1 = back_conv(scratch.be1, scratch.slope_e1, grad, lifted, mean_e1, inv_e1)
    small_row(LATE + 16, column_sum(sums_e1[1]))
    small_row(LATE + 17, column_sum(sums_e1[0]))
    zero, slope = norm_grad(sums_e1, gain_e1, ones16, count16)

    def lifted_grad(h, carry):
        normed = (lifted[row_at(h), :] - mean_e1) * inv_e1
        value = inv_e1 * (grad[row_at(h), :] * gain_e1 - zero - normed * slope)
        grad[row_at(h), :] = grad_encoded[row_at(h), :] + value
        return carry

    grid_rows(lifted_grad)
    point()

    late_at = small_at + LATE
    sums[late_at : late_at + 16, :] = dot_three(fields[...], grad[...])
    sums[late_at + 20 : late_at + 24, :] = jnp.zeros((4, c), F32)
    point()
    begin()
    back = dot_three(lift[...], grad[...], NT)
    frames_out = scratch.frames_out
    for source in range(line):
        for k in range(strip):
            h = source * strip + k
            value = back[0:history, h * width : (h + 1) * width]
            frames_out[source, :, k, :] = value * keep * masks[h]
    frames_here[row] = frames_out[row]
    for k in range(1, line):
        to = lax.rem(row + k, line)
        output_copies.append(
            send(frames_out.at[to], frames_here.at[row], device_at(to))
        )

    for copy in output_copies[: line - 1]:
        copy.wait_recv()
    own_output = pltpu.make_async_copy(output_here, outputs.output, local_sem.at[10])
    own_output.start()
    for k in REST:
        advance(k)
    assert not due and all(exchange.done() for exchange in exchanges)

    for copy in output_copies[line - 1 :]:
        copy.wait_recv()
    own_frames = pltpu.make_async_copy(
        frames_here, outputs.frames_grad, local_sem.at[11 + len(runs)]
    )
    own_frames.start()
    own_output.wait()
    own_frames.wait()
    for copy in final_copies:
        copy.wait()
    for copy in frame_copies + cot_copies + output_copies:
        copy.wait_send()
    for exchange in exchanges:
        for copy, only in exchange.copies:
            if only is None:
                copy.wait_send()
            else:
                pl.when(only)(copy.wait_send)


def write_kernel(layout, *refs):
    shapes, starts, small_at = layout
    output, frames_grad, gradients = refs[:3]
    outputs = refs[3:-4]
    output_here, frames_here, gradients_here, sem = refs[-4:]
    c = gradients.shape[1]
    moves = [(frames_grad, frames_here, outputs[1])]
    for k, name in enumerate(LARGE):
        rows = pl.ds(starts[name], shapes[name][0])
        moves.append((gradients.at[rows], gradients_here.at[rows], outputs[2 + k]))
    moves.append((output, output_here, outputs[0]))
    small = pl.ds(small_at, SMALL_COUNT)
    first = pltpu.make_async_copy(gradients.at[small], gradients_here.at[small], sem.at[0])
    first.start()
    arriving, leaving = [], []
    for k, (source, here, _) in enumerate(moves):
        arriving.append(pltpu.make_async_copy(source, here, sem.at[1 + 2 * k]))
        arriving[-1].start()
    first.wait()
    for target, (k, rows) in zip(outputs[2 + len(LARGE) :], SMALL_ROWS.values()):
        at = small_at + k
        if rows == 8:
            for s in range(target.shape[0]):
                target[s : s + 1, 0:c] = gradients_here[at + 2 * s : at + 2 * s + 1, :]
                target[s : s + 1, c : 2 * c] = gradients_here[at + 2 * s + 1 : at + 2 * s + 2, :]
        else:
            target[...] = gradients_here[at : at + rows, :]
    for k, (_, here, target) in enumerate(moves):
        arriving[k].wait()
        leaving.append(pltpu.make_async_copy(here, target, sem.at[2 + 2 * k]))
        leaving[-1].start()
    for copy in leaving:
        copy.wait()


def whole_items(shape, *arguments):
    line = shape["rows"]
    whole = Given(*arguments)
    given = whole._asdict()
    frames, cotangent = whole.frames, whole.cotangent
    items, history, strip, width = frames.shape
    c = cotangent.shape[-1]
    cells = strip * line * width
    flat = {}
    for name, value in given.items():
        if value is cotangent:
            value = value.reshape(items, strip * width, c)
        elif name in LARGE:
            value = value.reshape(-1, c)
        elif value.ndim == 1 and name not in IN_SMEM:
            value = value.reshape(-1, c)
        flat[name] = value
    shapes = {name: flat[name].shape for name in LARGE}
    big_layout = layout_of(SimpleNamespace(**shapes))
    starts, small_at, total_rows, runs = big_layout
    copies = 7 * (line - 1) + len(runs) * (8 + 2 * (line - 1)) + 6
    landing = sum(rows // 2 + 5 * rows // 8 for _, rows in runs) + LATE_COUNT * (8 + line)
    shifted = pltpu.VMEM((cells + 2 * width, 6 * c), BF16)
    forward = pltpu.VMEM((18 * c, 2 * c), BF16)
    backward = pltpu.VMEM((2 * c, 18 * c), BF16)
    field = pltpu.VMEM((cells, c), F32)
    flipped_field = pltpu.VMEM((2 * c, cells), BF16)
    quarter = cells // 4
    scratch = dict(
        small=pltpu.VMEM((LATE_COUNT, c), F32),
        send=pltpu.SemaphoreType.DMA((copies,)),
        recv=pltpu.SemaphoreType.DMA((copies,)),
        local=pltpu.SemaphoreType.DMA((12 + len(runs),)),
        sums=pltpu.VMEM((total_rows, c), F32),
        final=pltpu.VMEM((total_rows, c), F32),
        landing=pltpu.VMEM((landing, c), F32),
        frames_in=pltpu.VMEM((line, history, strip, width), F32),
        mask_in=pltpu.VMEM((line, strip, width), jnp.int32),
        frames_out=pltpu.VMEM((line, history, strip, width), F32),
        frames_from=pltpu.VMEM((line, history, strip, width), F32),
        frames_here=pltpu.VMEM((line, history, strip, width), F32),
        mask_from=pltpu.VMEM((line, strip, width), jnp.int32),
        cot_from=pltpu.VMEM((items, strip * width, c), F32),
        output_here=pltpu.VMEM((items, strip * width, c), F32),
        fields=pltpu.VMEM((16, cells), F32),
        lift=pltpu.VMEM((16, c), F32),
        joined=pltpu.VMEM((cells, 4 * c), BF16),
        x_down=pltpu.VMEM((quarter, 8 * c), BF16),
        x_grad_up=pltpu.VMEM((quarter, 8 * c), BF16),
        x_up=pltpu.VMEM((quarter, 2 * c), BF16),
        x_grad_low=pltpu.VMEM((quarter, 2 * c), BF16),
        f_down=pltpu.VMEM((8 * c, 2 * c), BF16),
        b_down=pltpu.VMEM((4, 2 * c, 2 * c), BF16),
        f_up=pltpu.VMEM((4, 2 * c, 2 * c), BF16),
        b_up=pltpu.VMEM((2 * c, 8 * c), BF16),
        f_skip=pltpu.VMEM((4 * c, 2 * c), BF16),
        b_skip=pltpu.VMEM((2, 2 * c, 2 * c), BF16),
        xe1=shifted,
        xe2=shifted,
        xd1a=shifted,
        xd1b=shifted,
        xd2=shifted,
        xg=shifted,
        te1=flipped_field,
        te2=flipped_field,
        td1a=flipped_field,
        td1b=flipped_field,
        td2=flipped_field,
        turned=pltpu.VMEM((4 * c, cells), BF16),
        fe1=forward,
        fe2=forward,
        fd1a=forward,
        fd1b=forward,
        fd2=forward,
        be1=backward,
        be2=backward,
        bd1a=backward,
        bd1b=backward,
        bd2=backward,
        slope_e1=field,
        slope_e2=field,
        slope_d1a=field,
        slope_d1b=field,
        slope_d2=field,
        lifted=field,
        middle_e=field,
        encoded=field,
        raised=field,
        middle_d=field,
        result=field,
        cot=field,
        grad=field,
        grad_a=field,
        grad_b=field,
    )
    scratch.update({name: pltpu.VMEM(shapes[name], F32) for name in LARGE})

    in_hbm = pl.BlockSpec(memory_space=pl.ANY)
    in_vmem = pl.BlockSpec(memory_space=pltpu.VMEM)
    in_smem = pl.BlockSpec(memory_space=pltpu.SMEM)
    in_specs = [
        in_hbm if name in IN_HBM else in_smem if name in IN_SMEM else in_vmem
        for name in ARGUMENTS
    ]
    out_shape = [
        jax.ShapeDtypeStruct((items, strip * width, c), F32),
        jax.ShapeDtypeStruct(frames.shape, F32),
        jax.ShapeDtypeStruct((total_rows, c), F32),
    ]
    out_specs = [in_hbm] * 3
    results = pl.pallas_call(
        functools.partial(
            item_kernel,
            (line, strip, width, shapes, big_layout),
            tuple(scratch),
        ),
        out_shape=out_shape,
        in_specs=in_specs,
        out_specs=out_specs,
        scratch_shapes=list(scratch.values()),
        compiler_params=pltpu.CompilerParams(
            collective_id=0, has_side_effects=True, vmem_limit_bytes=62 * 1024 * 1024
        ),
    )(*[flat[name] for name in ARGUMENTS])
    names = LARGE + tuple(SMALL_ROWS)
    written = pl.pallas_call(
        functools.partial(write_kernel, (shapes, starts, small_at)),
        out_shape=out_shape[:2] + [jax.ShapeDtypeStruct(flat[name].shape, F32) for name in names],
        in_specs=[pl.BlockSpec(memory_space=pltpu.HBM)] * 3,
        out_specs=[in_hbm] * (2 + len(LARGE)) + [in_vmem] * len(SMALL_ROWS),
        scratch_shapes=[
            pltpu.VMEM((items, strip * width, c), F32),
            pltpu.VMEM(frames.shape, F32),
            pltpu.VMEM((total_rows, c), F32),
            pltpu.SemaphoreType.DMA((1 + 2 * (2 + len(LARGE)),)),
        ],
        compiler_params=pltpu.CompilerParams(vmem_limit_bytes=60 * 1024 * 1024),
    )(*results)
    grads = dict(zip(names, written[2:]))
    ordered = [name for name in ARGUMENTS if name in grads]
    return (written[0].reshape(cotangent.shape), written[1]) + tuple(
        grads[name].reshape(given[name].shape) for name in ordered
    )


def body(shape, *arguments):
    items, _, strip, width = arguments[0].shape
    line = shape["rows"]
    whole = (
        shape["section"] == 2
        and shape["batch"] == 4
        and items == line == 4
        and arguments[-1].shape[-1] == 128
        and (strip * line * width) % CHUNK == 0
    )
    return whole_items(shape, *arguments) if whole else strips_body(*arguments)


def solution(mesh):
    in_specs = (
        P(("section", "batch"), None, "rows", None),
        P(("section", "batch")),
        P(("section", "batch"), "rows", None),
        P(("section", "batch")),
        P(),
        P(),
        P(),
        P(),
        P(),
        P(),
        P(),
        P(),
        P(),
        P(),
        P(),
        P(),
        P(),
        P(),
        P(),
        P(),
        P(),
        P(),
        P(),
        P(),
        P(),
        P(),
        P(),
        P(),
        P(("section", "batch"), "rows", None, None),
    )
    out_specs = (
        P(("section", "batch"), "rows", None, None),
        P(("section", "batch"), None, "rows", None),
        P(),
        P(),
        P(),
        P(),
        P(),
        P(),
        P(),
        P(),
        P(),
        P(),
        P(),
        P(),
        P(),
        P(),
        P(),
        P(),
        P(),
        P(),
        P(),
        P(),
        P(),
        P(),
        P(),
        P(),
    )
    return jax.shard_map(functools.partial(body, mesh.shape), mesh=mesh, in_specs=in_specs, out_specs=out_specs, check_vma=False)
```

```python
import functools
from types import SimpleNamespace
from typing import Any, NamedTuple

import jax
import jax.numpy as jnp
from jax import lax
from jax.experimental import pallas as pl
from jax.experimental.pallas import tpu as pltpu
from jax.sharding import PartitionSpec as P

GROUPS = 8
FIELDS = 3
HIST = 4


EPS = 1e-05
HIGH = lax.Precision.HIGHEST


def extended(cells, sides, width):
    for axis, dim in sides:
        count = lax.axis_size(axis)
        ends = count - 1
        head = lax.slice_in_dim(cells, 0, width, axis=dim)
        tail = lax.slice_in_dim(cells, cells.shape[dim] - width, cells.shape[dim], axis=dim)
        cells = jnp.concatenate(
            [
                lax.ppermute(tail, axis, [(i, (i + 1) % count) for i in range(ends)]),
                cells,
                lax.ppermute(head, axis, [((i + 1) % count, i) for i in range(ends)]),
            ],
            axis=dim,
        )
    return cells


def from_behind(value, axis, steps):
    count = lax.axis_size(axis)
    pairs = [(source, (source + steps) % count) for source in range(count)]
    return lax.ppermute(value, axis, pairs)


def group_view(value_arrays):
    extent = value_arrays.shape
    return value_arrays.reshape(extent[:-1] + (GROUPS, extent[-1] // GROUPS))


def global_sums(value_arrays):
    grouped = group_view(value_arrays)
    flat = grouped.reshape(-1, GROUPS, grouped.shape[-1])
    first_sum = jnp.sum(flat, axis=(0, 2))
    second_sum = jnp.sum(flat * flat, axis=(0, 2))
    return lax.psum((first_sum, second_sum), "rows")


def apply_norm(value_arrays, sum_one, sum_two, norm_gain, norm_bias, total):
    grouped = group_view(value_arrays)
    group_mean = sum_one / total
    variance = sum_two / total - group_mean * group_mean
    inverse = lax.rsqrt(variance + EPS)
    normed = (grouped - group_mean[:, None]) * inverse[:, None]
    return normed.reshape(value_arrays.shape) * norm_gain + norm_bias


def norm_back(value_arrays, grad_one, grad_two):
    grouped = group_view(value_arrays)
    extra = grad_one[:, None] + 2.0 * grouped * grad_two[:, None]
    return extra.reshape(value_arrays.shape)


def reduce_grads(grad_one, grad_two):
    return lax.psum((grad_one, grad_two), "rows")


def conv_rows(padded, kernel):
    widened = jnp.pad(padded, ((0, 0), (1, 1), (0, 0)))
    return lax.conv_general_dilated(
        widened[None],
        kernel,
        (1, 1),
        "VALID",
        dimension_numbers=("NHWC", "HWIO", "NHWC"),
        precision=HIGH,
    )[0]


def flipped(kernel):
    return jnp.transpose(kernel[::-1, ::-1], (0, 1, 3, 2))


def pad_grads(value_arrays):
    return extended(value_arrays, (("rows", 0),), 1)


def totals_of(inputs, conv1):
    strip = inputs.shape[0]
    cells = strip * lax.axis_size("rows") * inputs.shape[1]
    return (cells * (inputs.shape[2] // GROUPS), cells * (conv1.shape[3] // GROUPS))


def block_forward(inputs, weights, scale_part, shift_part):
    norm1_gain, norm1_bias, conv1, norm2_gain, norm2_bias, conv2, conv2_bias = weights
    total_in, total_mid = totals_of(inputs, conv1)
    sums_in = global_sums(inputs)

    def pad_rows(value_arrays):
        return extended(value_arrays, (("rows", 0),), 1)

    act_one = pad_rows(
        jax.nn.gelu(
            apply_norm(inputs, sums_in[0], sums_in[1], norm1_gain, norm1_bias, total_in),
            approximate=False,
        )
    )
    middle = conv_rows(act_one, conv1)
    sums_mid = global_sums(middle)
    shaped = (
        apply_norm(middle, sums_mid[0], sums_mid[1], norm2_gain, norm2_bias, total_mid)
        * (1.0 + scale_part)
        + shift_part
    )
    act_two = pad_rows(jax.nn.gelu(shaped, approximate=False))
    branch = conv_rows(act_two, conv2) + conv2_bias
    return (branch, (sums_in[0], sums_in[1], act_one, middle, sums_mid[0], sums_mid[1], act_two))


def block_backward(inputs, weights, scale_part, shift_part, kept, grad_out):
    norm1_gain, norm1_bias, conv1, norm2_gain, norm2_bias, conv2, conv2_bias = weights
    in_one, in_two, act_one, middle, mid_one, mid_two, act_two = kept
    total_in, total_mid = totals_of(inputs, conv1)
    grad_conv2 = jax.vjp(lambda kernel: conv_rows(act_two, kernel), conv2)[1](grad_out)[0]
    grad_bias2 = jnp.sum(grad_out, axis=(0, 1))
    grad_act_two = conv_rows(pad_grads(grad_out), flipped(conv2))

    def second_piece(middle_in, sum_one, sum_two, gain_in, incoming_bias, scale_in, shift_in):
        shaped = (
            apply_norm(middle_in, sum_one, sum_two, gain_in, incoming_bias, total_mid)
            * (1.0 + scale_in)
            + shift_in
        )
        return jax.nn.gelu(shaped, approximate=False)

    second_pull = jax.vjp(
        second_piece, middle, mid_one, mid_two, norm2_gain, norm2_bias, scale_part, shift_part
    )[1](grad_act_two)
    summed_one, summed_two = reduce_grads(second_pull[1], second_pull[2])
    grad_middle = second_pull[0] + norm_back(middle, summed_one, summed_two)
    grad_conv1 = jax.vjp(lambda kernel: conv_rows(act_one, kernel), conv1)[1](grad_middle)[0]
    grad_act_one = conv_rows(pad_grads(grad_middle), flipped(conv1))

    def first_piece(inputs_in, sum_one, sum_two, gain_in, incoming_bias):
        return jax.nn.gelu(
            apply_norm(inputs_in, sum_one, sum_two, gain_in, incoming_bias, total_in),
            approximate=False,
        )

    first_pull = jax.vjp(first_piece, inputs, in_one, in_two, norm1_gain, norm1_bias)[1](
        grad_act_one
    )
    first_one, first_two = reduce_grads(first_pull[1], first_pull[2])
    grad_inputs = first_pull[0] + norm_back(inputs, first_one, first_two)
    grads = (
        first_pull[3],
        first_pull[4],
        grad_conv1,
        second_pull[3],
        second_pull[4],
        grad_conv2,
        grad_bias2,
    )
    return (grad_inputs, grads, second_pull[5], second_pull[6])


def conditioning(step_item, table):
    one_hot = (jnp.arange(table.shape[0], dtype=jnp.int32) == step_item).astype(jnp.float32)
    condition = jnp.dot(one_hot, table, precision=HIGH)
    half_width = table.shape[1] // 2
    return (condition[:half_width], condition[half_width:], one_hot)


def project_in(frames_item, mask_item, count_item, incoming_weight, incoming_bias):
    history = jnp.arange(HIST, dtype=jnp.int32) >= HIST - count_item
    keep = jnp.repeat(history, FIELDS).astype(jnp.float32)
    lifted = (
        jnp.einsum(
            "fhw,fc->hwc", frames_item * keep[:, None, None], incoming_weight, precision=HIGH
        )
        + incoming_bias
    )
    return lifted * mask_item[:, :, None].astype(jnp.float32)


def coarsen_field(value_arrays, incoming_weight, incoming_bias):
    rows_here, width_here, depth_here = value_arrays.shape
    blocks = value_arrays.reshape(rows_here // 2, 2, width_here // 2, 2, depth_here)
    return jnp.einsum("iajbk,abkc->ijc", blocks, incoming_weight, precision=HIGH) + incoming_bias


def upsample(value_arrays, incoming_weight, incoming_bias):
    result = jnp.einsum("ijk,abkc->iajbc", value_arrays, incoming_weight, precision=HIGH)
    extent = result.shape
    return result.reshape(extent[0] * 2, extent[2] * 2, extent[4]) + incoming_bias


def flatten_all(pieces):
    return jnp.concatenate([piece.reshape(-1) for piece in pieces])


def unflatten_all(flat, templates):
    pieces = []
    offset_at = 0
    for template in templates:
        count_here = template.size
        pieces.append(flat[offset_at : offset_at + count_here].reshape(template.shape))
        offset_at += count_here
    return tuple(pieces)


def strips_body(
    frames,
    counts,
    cell_mask,
    step_index,
    lift_weight,
    lift_bias,
    enc_norm1_gain,
    enc_norm1_bias,
    enc_conv1,
    enc_step_table,
    enc_norm2_gain,
    enc_norm2_bias,
    enc_conv2,
    enc_conv2_bias,
    reducer_weight,
    reducer_bias,
    up_weight,
    up_bias,
    dec_norm1_gain,
    dec_norm1_bias,
    dec_conv1,
    dec_step_table,
    dec_norm2_gain,
    dec_norm2_bias,
    dec_conv2,
    dec_conv2_bias,
    skip_weight,
    skip_bias,
    cotangent,
):
    enc_weights = (
        enc_norm1_gain,
        enc_norm1_bias,
        enc_conv1,
        enc_norm2_gain,
        enc_norm2_bias,
        enc_conv2,
        enc_conv2_bias,
    )
    dec_weights = (
        dec_norm1_gain,
        dec_norm1_bias,
        dec_conv1,
        dec_norm2_gain,
        dec_norm2_bias,
        dec_conv2,
        dec_conv2_bias,
    )
    params = (
        lift_weight,
        lift_bias,
        enc_norm1_gain,
        enc_norm1_bias,
        enc_conv1,
        enc_step_table,
        enc_norm2_gain,
        enc_norm2_bias,
        enc_conv2,
        enc_conv2_bias,
        reducer_weight,
        reducer_bias,
        up_weight,
        up_bias,
        dec_norm1_gain,
        dec_norm1_bias,
        dec_conv1,
        dec_step_table,
        dec_norm2_gain,
        dec_norm2_bias,
        dec_conv2,
        dec_conv2_bias,
        skip_weight,
        skip_bias,
    )

    def forward_micro(carry, sliced):
        frames_item, mask_item, count_item, step_item = sliced
        lifted = project_in(frames_item, mask_item, count_item, lift_weight, lift_bias)
        enc_scale, enc_shift, unused_hot = conditioning(step_item, enc_step_table)
        enc_branch, enc_kept = block_forward(lifted, enc_weights, enc_scale, enc_shift)
        encoder_result = lifted + enc_branch
        coarse_field = coarsen_field(encoder_result, reducer_weight, reducer_bias)
        foreign = from_behind(coarse_field, "section", 1)
        raised_foreign = upsample(foreign, up_weight, up_bias)
        raised = from_behind(raised_foreign, "section", 1)
        joined = jnp.concatenate([raised, encoder_result], axis=-1)
        dec_scale, dec_shift, unused_again = conditioning(step_item, dec_step_table)
        dec_branch, dec_kept = block_forward(joined, dec_weights, dec_scale, dec_shift)
        output_item = jnp.dot(joined, skip_weight, precision=HIGH) + skip_bias + dec_branch
        return (carry, (output_item, (lifted, enc_kept, encoder_result, foreign, joined, dec_kept)))

    unused, (output, kept_all) = lax.scan(
        forward_micro, jnp.zeros((), jnp.float32), (frames, cell_mask, counts, step_index)
    )

    def backward_micro(totals, sliced):
        frames_item, mask_item, count_item, step_item, grad_out, kept = sliced
        lifted, enc_kept, encoder_result, foreign, joined, dec_kept = kept
        dec_scale, dec_shift, one_hot = conditioning(step_item, dec_step_table)
        grad_joined, dec_grads, dec_gscale, dec_gshift = block_backward(
            joined, dec_weights, dec_scale, dec_shift, dec_kept, grad_out
        )
        grad_skip_weight = jnp.einsum("hwk,hwc->kc", joined, grad_out, precision=HIGH)
        grad_skip_bias = jnp.sum(grad_out, axis=(0, 1))
        grad_joined = grad_joined + jnp.dot(grad_out, skip_weight.T, precision=HIGH)
        half_width = joined.shape[-1] // 2
        grad_raised = grad_joined[..., :half_width]
        grad_encoded = grad_joined[..., half_width:]
        grad_foreign_up = from_behind(grad_raised, "section", 1)
        up_pull = jax.vjp(upsample, foreign, up_weight, up_bias)[1](grad_foreign_up)
        coarse_gradient = from_behind(up_pull[0], "section", 1)
        reducer_pullback = jax.vjp(coarsen_field, encoder_result, reducer_weight, reducer_bias)[1](
            coarse_gradient
        )
        grad_encoded = grad_encoded + reducer_pullback[0]
        enc_scale, enc_shift, enc_hot = conditioning(step_item, enc_step_table)
        grad_lifted, enc_grads, enc_gscale, enc_gshift = block_backward(
            lifted, enc_weights, enc_scale, enc_shift, enc_kept, grad_encoded
        )
        grad_lifted = grad_lifted + grad_encoded
        proj_pull = jax.vjp(
            lambda frames_in, incoming_weight, incoming_bias: project_in(
                frames_in, mask_item, count_item, incoming_weight, incoming_bias
            ),
            frames_item,
            lift_weight,
            lift_bias,
        )[1](grad_lifted)
        enc_table_grad = enc_hot[:, None] * jnp.concatenate([enc_gscale, enc_gshift])[None, :]
        dec_table_grad = one_hot[:, None] * jnp.concatenate([dec_gscale, dec_gshift])[None, :]
        micro_list = (
            proj_pull[1],
            proj_pull[2],
            enc_grads[0],
            enc_grads[1],
            enc_grads[2],
            enc_table_grad,
            enc_grads[3],
            enc_grads[4],
            enc_grads[5],
            enc_grads[6],
            reducer_pullback[1],
            reducer_pullback[2],
            up_pull[1],
            up_pull[2],
            dec_grads[0],
            dec_grads[1],
            dec_grads[2],
            dec_table_grad,
            dec_grads[3],
            dec_grads[4],
            dec_grads[5],
            dec_grads[6],
            grad_skip_weight,
            grad_skip_bias,
        )
        micro_flat = flatten_all(micro_list)
        return (totals + micro_flat, proj_pull[0])

    total_size = sum((piece.size for piece in params))
    start_totals = jnp.zeros((total_size,), jnp.float32)
    flat_totals, frames_grad = lax.scan(
        backward_micro,
        start_totals,
        (frames, cell_mask, counts, step_index, cotangent, kept_all),
        reverse=True,
    )
    flat_totals = lax.psum(flat_totals, ("section", "batch", "rows"))
    grads = unflatten_all(flat_totals, params)
    return (output, frames_grad) + grads


F32 = jnp.float32
BF16 = jnp.bfloat16
MESH = pl.DeviceIdType.MESH
NN = ((1,), (0,))
NT = ((1,), (1,))
TN = ((0,), (0,))
HIGH_AT = (0, 2, 1)
LOW_AT = (4, 3, 5)
CHUNK = 512
class Given(NamedTuple):
    frames: Any
    counts: Any
    cell_mask: Any
    step_index: Any
    lift_weight: Any
    lift_bias: Any
    enc_norm1_gain: Any
    enc_norm1_bias: Any
    enc_conv1: Any
    enc_step_table: Any
    enc_norm2_gain: Any
    enc_norm2_bias: Any
    enc_conv2: Any
    enc_conv2_bias: Any
    reducer_weight: Any
    reducer_bias: Any
    up_weight: Any
    up_bias: Any
    dec_norm1_gain: Any
    dec_norm1_bias: Any
    dec_conv1: Any
    dec_step_table: Any
    dec_norm2_gain: Any
    dec_norm2_bias: Any
    dec_conv2: Any
    dec_conv2_bias: Any
    skip_weight: Any
    skip_bias: Any
    cotangent: Any


ARGUMENTS = Given._fields
LARGE = tuple(
    dict(
        dec_conv1=0,
        up_weight=0,
        reducer_weight=0,
        dec_conv2=0,
        skip_weight=0,
        enc_conv1=0,
        enc_conv2=0,
    )
)
IN_HBM = tuple(dict(frames=0, cell_mask=0, cotangent=0)) + LARGE
IN_SMEM = tuple(dict(counts=0, step_index=0))
LATE = 64
SMALL_ROWS = dict(
    enc_conv2_bias=(0, 1),
    reducer_bias=(1, 1),
    up_bias=(2, 1),
    dec_conv2_bias=(3, 1),
    skip_bias=(3, 1),
    dec_norm1_gain=(4, 2),
    dec_norm1_bias=(6, 2),
    dec_norm2_gain=(8, 1),
    dec_norm2_bias=(9, 1),
    dec_step_table=(16, 8),
    lift_weight=(LATE, 12),
    lift_bias=(LATE + 12, 1),
    enc_norm1_gain=(LATE + 16, 1),
    enc_norm1_bias=(LATE + 17, 1),
    enc_norm2_gain=(LATE + 18, 1),
    enc_norm2_bias=(LATE + 19, 1),
    enc_step_table=(LATE + 24, 8),
)
LATE_COUNT = 32
SMALL_COUNT = LATE + LATE_COUNT
DUE = ((), (), (), (), (), (0,), (), (1,), (), (), (2,), (3, 0), (), (), (1,), (), (), (2,), (0,), (1, 4, 3), (2,), (), (), (5, 0), (1, 3), (4, 2), (), (6,), (7, 3, 0, 5, 4, 1, 2))
REST = (6, 3, 7, 4, 5, 6, 8, 7, 0, 4, 5, 1, 6, 7, 2, 0, 1, 5, 3, 6, 2, 8, 7, 3, 4, 5, 4, 6, 7, 5, 6, 7)
OUTPUTS = tuple(dict(output=0, frames_grad=0, gradients=0))


def split(value):
    high = value.astype(BF16)
    return high, (value - high.astype(F32)).astype(BF16)


def dot(left, right, dims=NN, precision=None):
    return lax.dot_general(
        left, right, (dims, ((), ())), precision=precision, preferred_element_type=F32
    )


def fold(value):
    half = value.shape[1] // 2
    return value[:, :half] + value[:, half:]


def fold_rows(value):
    half = value.shape[0] // 2
    return value[:half] + value[half:]


def tile_sums(value):
    return jnp.sum(value.reshape(-1, 8, value.shape[-1]), axis=0)


def column_sum(tiles):
    return jnp.sum(tiles, axis=0, keepdims=True)


def normal(value):
    bell = jnp.exp(-0.5 * value * value)
    t = 1.0 / (1.0 + 0.2316418882663604 * jnp.abs(value))
    poly = 0.5307027145
    for factor in (-0.7265760135, 0.7107068705, -0.142248368, 0.127414796):
        poly = poly * t + factor
    tail = poly * t * bell
    return jnp.where(value < 0.0, tail, 1.0 - tail), 0.3989422804014327 * bell


def dot_three(left, right, dims=NN):
    left_high, left_low = split(left)
    right_high, right_low = split(right)
    total = dot(left_high, right_high, dims)
    return total + (dot(left_high, right_low, dims) + dot(left_low, right_high, dims))


def group_ones(channels, size):
    rows = lax.broadcasted_iota(jnp.int32, (channels, channels), 0) // size
    columns = lax.broadcasted_iota(jnp.int32, (channels, channels), 1) // size
    return (rows == columns).astype(BF16)


def group_sums(first, second, ones):
    terms = []
    rest = jnp.concatenate([first, second], axis=0)
    for _ in range(3):
        term = rest.astype(BF16)
        terms.append(term)
        rest = rest - term.astype(F32)
    both = dot(jnp.concatenate(terms, axis=0), ones)
    both = both[32:48] + both[16:32] + both[:16]
    return column_sum(both[:8]), column_sum(both[8:])


class Exchange:

    def __init__(self, place, start, rows, landing, first_sem):
        self.place, self.start, self.rows, self.landing = place, start, rows, landing
        self.sem = first_sem
        self.stage = 0
        self.copies = []
        self.waiting = []
        self.group = place.plane_group
        self.half = rows // 2
        self.base = start + place.core * self.half
        self._finish(self.half)

    def _finish(self, size):
        self.part = size // self.group.count
        self.own = self.base + self.group.here * self.part

    def count(self):
        return 2 + 2 * (self.group.count - 1) + 3

    def land_rows(self):
        return self.half + (self.group.count + 1) * self.part

    def _copy(self, source, target, device, only=None):
        place = self.place
        copy = pltpu.make_async_remote_copy(
            src_ref=source,
            dst_ref=target,
            send_sem=place.send.at[self.sem],
            recv_sem=place.recv.at[self.sem],
            device_id=device,
            device_id_type=MESH,
        )
        self.sem += 1
        if only is None:
            copy.start()
            self.waiting.append(copy)
        self.copies.append((copy, only))
        return copy

    def _wait(self):
        for copy in self.waiting:
            copy.wait_recv()
        self.waiting = []

    def _rows(self, at, size):
        return pl.ds(pl.multiple_of(at, 8), size)

    def _swap(self):
        place = self.place
        other = self._rows(self.start + (1 - place.core) * self.half, self.half)
        self.land = self.landing
        self.landing += self.half
        self._copy(
            place.sums.at[other], place.landing.at[pl.ds(self.land, self.half)], place.partner
        )

    def _add_swap(self):
        place = self.place
        block = 64 if self.half % 64 == 0 else 32

        def step(i, carry):
            here = self._rows(self.base + i * block, block)
            there = self._rows(self.land + i * block, block)
            place.sums[here] = place.sums[here] + place.landing[there]
            return carry

        lax.fori_loop(0, self.half // block, step, 0)

    def _scatter(self, group, base, size):
        place = self.place
        self.land = self.landing
        for k in range(1, group.count):
            to = lax.rem(group.here + k, group.count)
            self._copy(
                place.sums.at[self._rows(base + to * size, size)],
                place.landing.at[pl.ds(self.landing, size)],
                group.device(to),
            )
            self.landing += size

    def _total(self, group, own, size, target):
        place = self.place
        block = 16 if size % 16 == 0 else 8

        def step(i, carry):
            here = self._rows(own + i * block, block)
            total = place.sums[here]
            for k in range(group.count - 1):
                there = self._rows(self.land + k * size + i * block, block)
                total = total + place.landing[there]
            target[here] = total
            return carry

        lax.fori_loop(0, size // block, step, 0)

    def _gather(self, group, own, size):
        final = self.place.final
        here = self._rows(own, size)
        for k in range(1, group.count):
            to = lax.rem(group.here + k, group.count)
            self._copy(final.at[here], final.at[here], group.device(to))

    def _steps(self):
        place, group = self.place, self.group
        yield self._swap()
        self._wait()
        self._add_swap()
        yield from self._both()
        final = place.final
        here = self._rows(self.base, self.half)
        self._copy(final.at[here], final.at[here], place.partner)
        yield
        self._wait()
        yield

    def _both(self):
        place, group = self.place, self.group
        self._scatter(group, self.base, self.part)
        yield
        self._wait()
        self._total(group, self.own, self.part, place.sums)
        yield from self._line()
        self._gather(group, self.own, self.part)
        yield
        self._wait()

    def _line(self):
        place, line = self.place, self.place.line
        sums, final, landing = place.sums, place.final, place.landing
        part, own = self.part, self._rows(self.own, self.part)
        inward, across = pl.ds(self.landing, part), pl.ds(self.landing + part, part)
        self.landing += 2 * part
        block = 16 if part % 16 == 0 else 8

        def add(at, target):
            def step(i, carry):
                here = self._rows(self.own + i * block, block)
                target[here] = sums[here] + landing[pl.ds(at + i * block, block)]
                return carry

            lax.fori_loop(0, part // block, step, 0)

        first = self._copy(sums.at[own], landing.at[inward], line.device(line.inner), line.edge)
        second = self._copy(sums.at[own], landing.at[across], line.device(line.across), line.middle)
        third = self._copy(final.at[own], final.at[own], line.device(line.outer), line.middle)
        pl.when(line.edge)(first.start)
        yield

        @pl.when(line.middle)
        def _():
            first.wait_recv()
            add(self.landing - 2 * part, sums)
            second.start()

        yield

        @pl.when(line.middle)
        def _():
            second.wait_recv()
            add(self.landing - part, final)
            third.start()

        yield
        pl.when(line.edge)(third.wait_recv)

    def advance(self):
        if self.stage == 0:
            self.steps = self._steps()
        self.stage += 1
        next(self.steps)

    def done(self):
        return self.stage == 8


class SmallExchange(Exchange):

    def count(self):
        return self.place.cores_group.count + self.place.line.count - 2

    def land_rows(self):
        return self.rows * (self.place.cores_group.count + self.place.line.count)

    def _share(self, group, source):
        place = self.place
        self.land = self.landing
        self.landing += group.count * self.rows
        own = self._rows(self.land + group.here * self.rows, self.rows)
        place.landing[own] = source[...]
        for k in range(1, group.count):
            to = lax.rem(group.here + k, group.count)
            self._copy(source, place.landing.at[own], group.device(to))

    def _sum(self, group):
        total = None
        for k in range(group.count):
            part = self.place.landing[pl.ds(self.land + k * self.rows, self.rows)]
            total = part if total is None else total + part
        return total

    def _steps(self):
        place = self.place
        here = pl.ds(self.start, self.rows)
        self._share(place.line, place.sums.at[here])
        yield
        self._wait()
        place.small[...] = self._sum(place.line)
        self._share(place.cores_group, place.small)
        yield
        self._wait()
        place.final[here] = self._sum(place.cores_group)
        yield

    def done(self):
        return self.stage == 3


def layout_of(shapes):
    starts = {}
    at = 0
    for name in LARGE:
        starts[name] = at
        at += getattr(shapes, name)[0]
    small = at
    begins = SimpleNamespace(**starts)
    late = small + LATE
    tap = shapes.dec_conv2[0] // 3
    part = shapes.dec_conv1[0] // 3
    conv1, up = begins.dec_conv1, begins.up_weight
    edges = (
        (begins.dec_conv2, begins.enc_conv1),
        (conv1, conv1 + part),
        (conv1 + part, conv1 + 2 * part),
        (conv1 + 2 * part, up),
        (up, begins.dec_conv2),
        (begins.enc_conv2, late),
        (begins.enc_conv1, begins.enc_conv1 + 2 * tap),
        (begins.enc_conv1 + 2 * tap, begins.enc_conv2),
        (late, late + LATE_COUNT),
    )
    runs = [(first, last - first) for first, last in edges]
    return starts, small, late + LATE_COUNT, runs


def item_kernel(sizes, scratch_names, *refs):
    line, strip, width, shapes, big_layout = sizes
    begins, small_at, total_rows, runs = big_layout
    starts = SimpleNamespace(**begins)
    inputs = Given(*refs[: len(ARGUMENTS)])
    refs = refs[len(ARGUMENTS) :]
    output_names = OUTPUTS
    outputs = SimpleNamespace(**dict(zip(output_names, refs)))
    scratch = SimpleNamespace(**dict(zip(scratch_names, refs[len(output_names) :])))

    def w_of(name):
        return getattr(scratch, name)

    height = strip * line
    cells = height * width
    c = inputs.lift_weight.shape[1]
    strip_cells = strip * width
    history = inputs.frames.shape[1]

    core = lax.axis_index("section")
    plane = lax.axis_index("batch")
    row = lax.axis_index("rows")
    middle = lax.rem(row + 1, 4) // 2

    def device_at(to):
        return (core, plane, to)

    place = SimpleNamespace(
        core=core,
        partner=(1 - core, plane, row),
        line=SimpleNamespace(
            count=line,
            here=row,
            device=device_at,
            middle=middle == 1,
            edge=middle == 0,
            inner=1 + row // 2,
            across=3 - row,
            outer=3 * (row // 2),
        ),
        plane_group=SimpleNamespace(
            count=4, here=plane, device=lambda to: (core, to, row)
        ),
        cores_group=SimpleNamespace(
            count=8,
            here=core * 4 + plane,
            device=lambda to: (to // 4, lax.rem(to, 4), row),
        ),
        small=scratch.small,
        sums=scratch.sums,
        final=scratch.final,
        landing=scratch.landing,
        send=scratch.send,
        recv=scratch.recv,
    )
    local_sem = scratch.local

    frames_in, mask_in, cot = scratch.frames_in, scratch.mask_in, scratch.cot
    here_rows = pl.ds(pl.multiple_of(row * strip_cells, strip_cells), strip_cells)
    frames_from, mask_from, cot_from = scratch.frames_from, scratch.mask_from, scratch.cot_from
    staged = (
        pltpu.make_async_copy(inputs.frames, frames_from, local_sem.at[7]),
        pltpu.make_async_copy(inputs.cell_mask, mask_from, local_sem.at[8]),
        pltpu.make_async_copy(inputs.cotangent, cot_from, local_sem.at[9]),
    )
    for copy in staged:
        copy.start()

    weight_copies = {}
    for k, name in enumerate(LARGE):
        copy = pltpu.make_async_copy(getattr(inputs, name), w_of(name), local_sem.at[k])
        weight_copies[name] = copy
        copy.start()

    barrier = pltpu.get_barrier_semaphore()
    peers = [device_at(lax.rem(row + k, line)) for k in range(1, line)]
    cores_group = place.cores_group
    for k in range(1, 8):
        peers.append(cores_group.device(lax.rem(cores_group.here + k, 8)))
    for device in peers:
        pl.semaphore_signal(barrier, inc=1, device_id=device, device_id_type=MESH)
    pl.semaphore_wait(barrier, len(peers))

    next_sem = 0

    def send(source, target, device):
        nonlocal next_sem
        copy = pltpu.make_async_remote_copy(
            src_ref=source,
            dst_ref=target,
            send_sem=scratch.send.at[next_sem],
            recv_sem=scratch.recv.at[next_sem],
            device_id=device,
            device_id_type=MESH,
        )
        next_sem += 1
        copy.start()
        return copy

    frame_copies, cot_copies, output_copies = [], [], []
    for copy in staged[:2]:
        copy.wait()
    for k in range(1, line):
        to = lax.rem(row + k, line)
        device = device_at(to)
        frame_copies.append(send(frames_from.at[to], frames_in.at[row], device))
        frame_copies.append(send(mask_from.at[to], mask_in.at[row], device))
    staged[2].wait()
    for k in range(1, line):
        to = lax.rem(row + k, line)
        cot_copies.append(
            send(cot_from.at[to], cot.at[here_rows], device_at(to))
        )

    copied = SimpleNamespace(**weight_copies)
    def put_pair(target, block, value):
        high, low = split(value)
        rows = slice(block * c, (block + 1) * c)
        target[rows, 0:c] = high
        target[rows, c : 2 * c] = low

    def stack_conv(source, half, depth, forward, backward):
        for a in range(3):
            for b in range(3):
                at = (3 * a + b) * depth + half * c
                value = source[at : at + c, :]
                turned = value.T
                for places in (HIGH_AT, LOW_AT):
                    put_pair(forward, 6 * a + places[b], value)
                    put_pair(backward, 6 * (2 - a) + places[2 - b], turned)

    copied.enc_conv1.wait()
    stack_conv(scratch.enc_conv1, 0, c, scratch.fe1, scratch.be1)
    copied.enc_conv2.wait()
    stack_conv(scratch.enc_conv2, 0, c, scratch.fe2, scratch.be2)
    copied.reducer_weight.wait()
    for k in range(4):
        value = scratch.reducer_weight[k * c : (k + 1) * c, :]
        turned = value.T
        for block in (k, k + 4):
            put_pair(scratch.f_down, block, value)
        for block in (0, 1):
            put_pair(scratch.b_down.at[k], block, turned)
    copied.up_weight.wait()
    for k in range(4):
        value = scratch.up_weight[k * c : (k + 1) * c, :]
        turned = value.T
        for block in (0, 1):
            put_pair(scratch.f_up.at[k], block, value)
        for block in (k, k + 4):
            put_pair(scratch.b_up, block, turned)
    copied.dec_conv1.wait()
    stack_conv(scratch.dec_conv1, 0, 2 * c, scratch.fd1a, scratch.bd1a)
    stack_conv(scratch.dec_conv1, 1, 2 * c, scratch.fd1b, scratch.bd1b)
    copied.dec_conv2.wait()
    stack_conv(scratch.dec_conv2, 0, c, scratch.fd2, scratch.bd2)
    copied.skip_weight.wait()
    for half in range(2):
        value = scratch.skip_weight[half * c : (half + 1) * c, :]
        turned = value.T
        for block in (half, half + 2):
            put_pair(scratch.f_skip, block, value)
        for block in (0, 1):
            put_pair(scratch.b_skip.at[half], block, turned)

    for buffer in (scratch.xe1, scratch.xe2, scratch.xd1a, scratch.xd1b, scratch.xd2, scratch.xg):
        edge = jnp.zeros((width, 6 * c), BF16)
        buffer[0:width, :] = edge
        buffer[cells + width : cells + 2 * width, :] = edge

    lift = scratch.lift
    lift[...] = jnp.zeros(lift.shape, F32)
    lift[0:history, :] = inputs.lift_weight[...]
    lift[history : history + 1, :] = inputs.lift_bias[...]

    block = 2 * width
    column = lax.rem(lax.broadcasted_iota(jnp.int32, (block, c), 0), width)
    at_first, at_last = column == 0, column == width - 1
    zeros8 = jnp.zeros((8, c), F32)
    ones16 = group_ones(c, c // GROUPS)
    ones32 = group_ones(c, 2 * c // GROUPS)
    count16 = float(cells * (c // GROUPS))
    count32 = float(cells * (2 * c // GROUPS))

    def grid_rows(step, carry=0):
        return lax.fori_loop(0, cells // block, step, carry, unroll=2)

    def row_at(h):
        return pl.ds(pl.multiple_of(h * block, block), block)

    def chunk_at(i):
        return pl.ds(pl.multiple_of(i * CHUNK, CHUNK), CHUNK)

    def put_row(target, h, value):
        rows = pl.ds(pl.multiple_of(h * block + width, width), block)
        left = jnp.where(at_first, 0.0, pltpu.roll(value, 1, 0))
        right = jnp.where(at_last, 0.0, pltpu.roll(value, block - 1, 0))
        for b, piece in enumerate((left, value, right)):
            high, low = split(piece)
            target[rows, HIGH_AT[b] * c : (HIGH_AT[b] + 1) * c] = high
            target[rows, LOW_AT[b] * c : (LOW_AT[b] + 1) * c] = low

    def put_turned(target, columns, value, first=0, second=1):
        high, low = split(value.T)
        target[first * c : (first + 1) * c, columns] = high
        target[second * c : (second + 1) * c, columns] = low

    def conv_chunk(pairs, i):
        total = None
        for data, weight in pairs:
            taps = []
            for a in range(3):
                rows = pl.ds(pl.multiple_of(i * CHUNK + a * width, width), CHUNK)
                taps.append(data[rows, :])
            part = dot(jnp.concatenate(taps, axis=1), weight[...])
            total = part if total is None else total + part
        return total

    def norm_of(first, second, ones, count):
        one, two = group_sums(first, second, ones)
        mean = one / count
        return mean, lax.rsqrt(two / count - mean * mean + EPS)

    def activate(source, target, turned, slope, scale, shift):
        def step(h, carry):
            value = source[row_at(h), :] * scale + shift
            below, density = normal(value)
            slope[row_at(h), :] = below + value * density
            value = value * below
            put_row(target, h, value)
            put_turned(turned, row_at(h), value)
            return carry

        grid_rows(step)

    def conv_norm(pairs, target):
        def step(i, carry):
            value = fold(conv_chunk(pairs, i))
            target[chunk_at(i), :] = value
            return carry[0] + tile_sums(value), carry[1] + tile_sums(value * value)

        return lax.fori_loop(0, cells // CHUNK, step, (zeros8, zeros8))

    def sums_of(source):
        def step(h, carry):
            value = source[row_at(h), :]
            return carry[0] + tile_sums(value), carry[1] + tile_sums(value * value)

        return grid_rows(step, (zeros8, zeros8))

    step_here = jnp.full((1, c), inputs.step_index[row], jnp.int32)

    def condition(table):
        total = jnp.zeros((1, 2 * c), F32)
        chosen = jnp.concatenate([step_here, step_here], axis=1)
        for s in range(table.shape[0]):
            total = total + jnp.where(chosen == s, table[s : s + 1, :], 0.0)
        return total[:, :c], total[:, c:]

    frames_in[row] = frames_from[row]
    mask_in[row] = mask_from[row]
    for copy in frame_copies:
        copy.wait_recv()
    fields = scratch.fields
    fields[...] = jnp.zeros(fields.shape, F32)
    frame_of = lax.broadcasted_iota(jnp.int32, (history, width), 0) // FIELDS
    keep = (frame_of >= HIST - inputs.counts[row]).astype(F32)
    masks = []
    for source in range(line):
        for k in range(strip):
            columns = slice((source * strip + k) * width, (source * strip + k + 1) * width)
            mask = mask_in[source, k : k + 1, :].astype(F32)
            masks.append(mask)
            fields[0:history, columns] = frames_in[source, :, k, :] * keep * mask
            fields[history : history + 1, columns] = mask
    lifted = scratch.lifted
    lifted[...] = dot_three(fields[...], lift[...], TN)

    enc_scale, enc_shift = condition(inputs.enc_step_table)
    dec_scale, dec_shift = condition(inputs.dec_step_table)

    mean_e1, inv_e1 = norm_of(*sums_of(lifted), ones16, count16)
    gain_e1, bias_e1 = inputs.enc_norm1_gain[...], inputs.enc_norm1_bias[...]
    a_e1 = inv_e1 * gain_e1
    activate(lifted, scratch.xe1, scratch.te1, scratch.slope_e1, a_e1, bias_e1 - mean_e1 * a_e1)
    middle_e = scratch.middle_e
    mean_e2, inv_e2 = norm_of(
        *conv_norm([(scratch.xe1, scratch.fe1)], middle_e), ones16, count16
    )
    gain_e2, bias_e2 = inputs.enc_norm2_gain[...], inputs.enc_norm2_bias[...]
    a_e2 = inv_e2 * gain_e2
    activate(
        middle_e,
        scratch.xe2,
        scratch.te2,
        scratch.slope_e2,
        a_e2 * (1.0 + enc_scale),
        (bias_e2 - mean_e2 * a_e2) * (1.0 + enc_scale) + enc_shift,
    )
    encoded = scratch.encoded
    conv2_bias = inputs.enc_conv2_bias[...]
    joined = scratch.joined

    def encode(i, carry):
        value = fold(conv_chunk([(scratch.xe2, scratch.fe2)], i))
        value = value + conv2_bias + lifted[chunk_at(i), :]
        encoded[chunk_at(i), :] = value
        high, low = split(value)
        joined[chunk_at(i), c : 2 * c] = high
        joined[chunk_at(i), 3 * c : 4 * c] = low
        put_turned(scratch.turned, chunk_at(i), value, 1, 3)
        return carry[0] + tile_sums(value), carry[1] + tile_sums(value * value)

    sums_enc = lax.fori_loop(0, cells // CHUNK, encode, (zeros8, zeros8))

    half_cells, quarter = cells // 2, cells // 4

    def pick(source):
        pieces = []
        for b in range(2):
            value = source[pl.ds(b, half_cells, stride=2), :]
            value = value.reshape(height // 2, 2, width // 2, c)
            pieces.append([value[:, a].reshape(quarter, c) for a in range(2)])
        return [pieces[b][a] for a in range(2) for b in range(2)]

    def place_cells(target, pieces):
        for b in range(2):
            both = [pieces[2 * a + b].reshape(height // 2, 1, width // 2, c) for a in range(2)]
            value = jnp.concatenate(both, axis=1).reshape(half_cells, c)
            target[pl.ds(b, half_cells, stride=2), :] = value

    x_down = scratch.x_down
    for k, piece in enumerate(pick(encoded)):
        high, low = split(piece)
        x_down[:, k * c : (k + 1) * c] = high
        x_down[:, (k + 4) * c : (k + 5) * c] = low
    lowered = fold(dot(x_down[...], scratch.f_down[...])) + inputs.reducer_bias[...]
    x_up = scratch.x_up
    high, low = split(lowered)
    x_up[:, 0:c] = high
    x_up[:, c : 2 * c] = low
    raised = scratch.raised
    up_bias = inputs.up_bias[...]
    place_cells(
        raised, [fold(dot(x_up[...], scratch.f_up[k])) + up_bias for k in range(4)]
    )

    def raise_row(h, carry):
        value = raised[row_at(h), :]
        high, low = split(value)
        joined[row_at(h), 0:c] = high
        joined[row_at(h), 2 * c : 3 * c] = low
        put_turned(scratch.turned, row_at(h), value, 0, 2)
        return carry[0] + tile_sums(value), carry[1] + tile_sums(value * value)

    sums_raised = grid_rows(raise_row, (zeros8, zeros8))

    halves = []
    for half, (source, sums) in enumerate(((raised, sums_raised), (encoded, sums_enc))):
        mean, inv = norm_of(*sums, ones32, count32)
        gain = inputs.dec_norm1_gain[half : half + 1, :]
        bias = inputs.dec_norm1_bias[half : half + 1, :]
        scale = inv * gain
        activate(
            source,
            (scratch.xd1a, scratch.xd1b)[half],
            scratch.td1.at[2 * c * half : 2 * c * (half + 1)],
            (scratch.slope_d1a, scratch.slope_d1b)[half],
            scale,
            bias - mean * scale,
        )
        halves.append((source, mean, inv, gain))
    middle_d = scratch.middle_d
    pairs = [(scratch.xd1a, scratch.fd1a), (scratch.xd1b, scratch.fd1b)]
    mean_d2, inv_d2 = norm_of(*conv_norm(pairs, middle_d), ones16, count16)
    gain_d2, bias_d2 = inputs.dec_norm2_gain[...], inputs.dec_norm2_bias[...]
    a_d2 = inv_d2 * gain_d2
    activate(
        middle_d,
        scratch.xd2,
        scratch.td2,
        scratch.slope_d2,
        a_d2 * (1.0 + dec_scale),
        (bias_d2 - mean_d2 * a_d2) * (1.0 + dec_scale) + dec_shift,
    )
    result = scratch.result
    last_bias = inputs.dec_conv2_bias[...] + inputs.skip_bias[...]

    def decode(i, carry):
        value = conv_chunk([(scratch.xd2, scratch.fd2)], i)
        value = value + dot(joined[chunk_at(i), :], scratch.f_skip[...])
        result[chunk_at(i), :] = fold(value) + last_bias
        return carry

    lax.fori_loop(0, cells // CHUNK, decode, 0)
    output_here, frames_here = scratch.output_here, scratch.frames_here
    output_here[row] = result[here_rows]
    for k in range(1, line):
        to = lax.rem(row + k, line)
        there = pl.ds(pl.multiple_of(to * strip_cells, strip_cells), strip_cells)
        output_copies.append(
            send(result.at[there], output_here.at[row], device_at(to))
        )

    exchanges = []
    waiting_runs = list(runs)
    landing_at = 0
    sem_at = 4 * (line - 1) + 2 * (line - 1)
    sums, final = scratch.sums, scratch.final

    def begin():
        nonlocal landing_at, sem_at
        start, rows = waiting_runs.pop(0)
        kind = Exchange if waiting_runs else SmallExchange
        exchange = kind(place, start, rows, landing_at, sem_at)
        landing_at += exchange.land_rows()
        sem_at += exchange.count()
        exchanges.append(exchange)
        exchange.advance()

    final_copies = []

    def advance(k):
        exchange = exchanges[k]
        exchange.advance()
        if exchange.done():
            rows = pl.ds(exchange.start, exchange.rows)
            copy = pltpu.make_async_copy(
                final.at[rows], outputs.gradients.at[rows], local_sem.at[11 + k]
            )
            copy.start()
            final_copies.append(copy)

    due = list(DUE)

    def point():
        for k in due.pop(0):
            advance(k)

    def small_row(k, value):
        sums[small_at + k : small_at + k + 1, :] = value

    def spread_grad(source):
        def step(h, carry):
            value = source[row_at(h), :]
            put_row(scratch.xg, h, value)
            return carry + tile_sums(value)

        return grid_rows(step, zeros8)

    def weight_grad(turned, at, depth, a):
        rows = pl.ds((2 - a) * width, cells)
        both = dot(turned[...], scratch.xg[rows, :])
        for half in range(depth // c):
            part = fold_rows(both[2 * c * half : 2 * c * (half + 1)])
            for b in range(3):
                high, low = HIGH_AT[2 - b] * c, LOW_AT[2 - b] * c
                to = at + (3 * a + b) * depth + half * c
                sums[to : to + c, :] = part[:, high : high + c] + part[:, low : low + c]

    def back_conv(weight, slope, target, source, mean, inv):
        carry = (zeros8, zeros8)
        for i in range(cells // CHUNK):
            value = fold(conv_chunk([(scratch.xg, weight)], i)) * slope[chunk_at(i), :]
            target[chunk_at(i), :] = value
            normed = (source[chunk_at(i), :] - mean) * inv
            carry = (carry[0] + tile_sums(value), carry[1] + tile_sums(value * normed))
            if i % (cells // CHUNK // 2) == cells // CHUNK // 2 - 1:
                point()
        return carry

    def norm_grad(sums_in, scale, ones, count):
        one, two = group_sums(sums_in[0] * scale, sums_in[1] * scale, ones)
        return one / count, two / count

    cot[here_rows] = cot_from[row]
    for copy in cot_copies:
        copy.wait_recv()
    total_cot = column_sum(spread_grad(cot))
    for a in range(3):
        weight_grad(scratch.td2, starts.dec_conv2, c, a)
    part = fold(dot(scratch.turned[...], scratch.xg[width : cells + width, 2 * c : 4 * c]))
    sums[starts.skip_weight : starts.skip_weight + 2 * c, :] = fold_rows(part)
    small_row(3, total_cot)
    begin()

    grad = scratch.grad
    sums_d2 = back_conv(scratch.bd2, scratch.slope_d2, grad, middle_d, mean_d2, inv_d2)
    side_grads = (scratch.grad_a, scratch.grad_b)
    for half in range(2):

        def skip_back(i, carry, half=half):
            rows = pl.ds(pl.multiple_of(i * CHUNK + width, width), CHUNK)
            value = dot(scratch.xg[rows, 2 * c : 4 * c], scratch.b_skip[half])
            side_grads[half][chunk_at(i), :] = fold(value)
            return carry

        lax.fori_loop(0, cells // CHUNK, skip_back, 0)
    point()

    def table_rows(k, sums_in, gain, bias, one_plus):
        plain, times = column_sum(sums_in[0]), column_sum(sums_in[1])
        for s in range(inputs.enc_step_table.shape[0]):
            small_row(k + 2 * s, jnp.where(step_here == s, gain * times + bias * plain, 0.0))
            small_row(k + 2 * s + 1, jnp.where(step_here == s, plain, 0.0))
        return one_plus * times, one_plus * plain

    def middle_grad(source, mean, inv, scale, sums_in):
        zero, slope = norm_grad(sums_in, scale, ones16, count16)

        def step(h, carry):
            normed = (source[row_at(h), :] - mean) * inv
            value = inv * (grad[row_at(h), :] * scale - zero - normed * slope)
            put_row(scratch.xg, h, value)
            return carry

        grid_rows(step)

    gain_row, bias_row = table_rows(16, sums_d2, gain_d2, bias_d2, 1.0 + dec_scale)
    small_row(8, gain_row)
    small_row(9, bias_row)
    middle_grad(middle_d, mean_d2, inv_d2, gain_d2 * (1.0 + dec_scale), sums_d2)
    point()
    for a in range(3):
        weight_grad(scratch.td1, starts.dec_conv1, 2 * c, a)
        point()
        begin()

    for half, (source, mean, inv, gain) in enumerate(halves):
        sums_in = back_conv(
            (scratch.bd1a, scratch.bd1b)[half],
            (scratch.slope_d1a, scratch.slope_d1b)[half],
            grad,
            source,
            mean,
            inv,
        )
        small_row(4 + half, column_sum(sums_in[1]))
        small_row(6 + half, column_sum(sums_in[0]))
        zero, slope = norm_grad(sums_in, gain, ones32, count32)
        target = side_grads[half]

        def input_grad(h, carry):
            normed = (source[row_at(h), :] - mean) * inv
            value = inv * (grad[row_at(h), :] * gain - zero - normed * slope)
            value = target[row_at(h), :] + value
            target[row_at(h), :] = value
            return carry + tile_sums(value)

        total = grid_rows(input_grad, zeros8)
        if half == 0:
            small_row(2, column_sum(total))
        point()

    grad_raised, grad_encoded = side_grads
    x_grad_up = scratch.x_grad_up
    for k, piece in enumerate(pick(grad_raised)):
        high, low = split(piece)
        x_grad_up[:, k * c : (k + 1) * c] = high
        x_grad_up[:, (k + 4) * c : (k + 5) * c] = low
    grad_lowered = fold(dot(x_grad_up[...], scratch.b_up[...]))
    small_row(1, jnp.sum(grad_lowered, axis=0, keepdims=True))
    x_grad_low = scratch.x_grad_low
    high, low = split(grad_lowered)
    x_grad_low[:, 0:c] = high
    x_grad_low[:, c : 2 * c] = low
    point()
    part = fold(fold_rows(dot(x_up[...], x_grad_up[...], TN)))
    for k in range(4):
        at = starts.up_weight + k * c
        sums[at : at + c, :] = part[:, k * c : (k + 1) * c]
    part = fold_rows(fold(dot(x_down[...], x_grad_low[...], TN)))
    sums[starts.reducer_weight : starts.reducer_weight + 4 * c, :] = part
    point()
    begin()
    place_cells(
        grad, [fold(dot(x_grad_low[...], scratch.b_down[k])) for k in range(4)]
    )

    def join_row(h, carry):
        value = grad_encoded[row_at(h), :] + grad[row_at(h), :]
        grad_encoded[row_at(h), :] = value
        put_row(scratch.xg, h, value)
        return carry + tile_sums(value)

    small_row(0, column_sum(grid_rows(join_row, zeros8)))
    for k in range(10, 16):
        small_row(k, jnp.zeros((1, c), F32))
    sums[small_at + 24 : small_at + LATE, :] = jnp.zeros((LATE - 24, c), F32)
    point()
    for a in range(3):
        weight_grad(scratch.te2, starts.enc_conv2, c, a)
        point()
    begin()
    sums_e2 = back_conv(scratch.be2, scratch.slope_e2, grad, middle_e, mean_e2, inv_e2)
    gain_row, bias_row = table_rows(LATE + 24, sums_e2, gain_e2, bias_e2, 1.0 + enc_scale)
    small_row(LATE + 18, gain_row)
    small_row(LATE + 19, bias_row)
    middle_grad(middle_e, mean_e2, inv_e2, gain_e2 * (1.0 + enc_scale), sums_e2)
    point()
    for a in range(3):
        weight_grad(scratch.te1, starts.enc_conv1, c, a)
        point()
        if a:
            begin()
    sums_e1 = back_conv(scratch.be1, scratch.slope_e1, grad, lifted, mean_e1, inv_e1)
    small_row(LATE + 16, column_sum(sums_e1[1]))
    small_row(LATE + 17, column_sum(sums_e1[0]))
    zero, slope = norm_grad(sums_e1, gain_e1, ones16, count16)

    def lifted_grad(h, carry):
        normed = (lifted[row_at(h), :] - mean_e1) * inv_e1
        value = inv_e1 * (grad[row_at(h), :] * gain_e1 - zero - normed * slope)
        grad[row_at(h), :] = grad_encoded[row_at(h), :] + value
        return carry

    grid_rows(lifted_grad)
    point()

    late_at = small_at + LATE
    sums[late_at : late_at + 16, :] = dot_three(fields[...], grad[...])
    sums[late_at + 20 : late_at + 24, :] = jnp.zeros((4, c), F32)
    point()
    begin()
    back = dot_three(lift[...], grad[...], NT)
    frames_out = scratch.frames_out
    for source in range(line):
        for k in range(strip):
            h = source * strip + k
            value = back[0:history, h * width : (h + 1) * width]
            frames_out[source, :, k, :] = value * keep * masks[h]
    frames_here[row] = frames_out[row]
    for k in range(1, line):
        to = lax.rem(row + k, line)
        output_copies.append(
            send(frames_out.at[to], frames_here.at[row], device_at(to))
        )

    for copy in output_copies[: line - 1]:
        copy.wait_recv()
    own_output = pltpu.make_async_copy(output_here, outputs.output, local_sem.at[10])
    own_output.start()
    for k in REST:
        advance(k)
    assert not due and all(exchange.done() for exchange in exchanges)

    for copy in output_copies[line - 1 :]:
        copy.wait_recv()
    own_frames = pltpu.make_async_copy(
        frames_here, outputs.frames_grad, local_sem.at[11 + len(runs)]
    )
    own_frames.start()
    own_output.wait()
    own_frames.wait()
    for copy in final_copies:
        copy.wait()
    for copy in frame_copies + cot_copies + output_copies:
        copy.wait_send()
    for exchange in exchanges:
        for copy, only in exchange.copies:
            if only is None:
                copy.wait_send()
            else:
                pl.when(only)(copy.wait_send)


def write_kernel(layout, *refs):
    shapes, starts, small_at = layout
    output, frames_grad, gradients = refs[:3]
    outputs = refs[3:-4]
    output_here, frames_here, gradients_here, sem = refs[-4:]
    c = gradients.shape[1]
    moves = [(frames_grad, frames_here, outputs[1])]
    for k, name in enumerate(LARGE):
        rows = pl.ds(starts[name], shapes[name][0])
        moves.append((gradients.at[rows], gradients_here.at[rows], outputs[2 + k]))
    moves.append((output, output_here, outputs[0]))
    small = pl.ds(small_at, SMALL_COUNT)
    first = pltpu.make_async_copy(gradients.at[small], gradients_here.at[small], sem.at[0])
    first.start()
    arriving, leaving = [], []
    for k, (source, here, _) in enumerate(moves):
        arriving.append(pltpu.make_async_copy(source, here, sem.at[1 + 2 * k]))
        arriving[-1].start()
    first.wait()
    for target, (k, rows) in zip(outputs[2 + len(LARGE) :], SMALL_ROWS.values()):
        at = small_at + k
        if rows == 8:
            for s in range(target.shape[0]):
                target[s : s + 1, 0:c] = gradients_here[at + 2 * s : at + 2 * s + 1, :]
                target[s : s + 1, c : 2 * c] = gradients_here[at + 2 * s + 1 : at + 2 * s + 2, :]
        else:
            target[...] = gradients_here[at : at + rows, :]
    for k, (_, here, target) in enumerate(moves):
        arriving[k].wait()
        leaving.append(pltpu.make_async_copy(here, target, sem.at[2 + 2 * k]))
        leaving[-1].start()
    for copy in leaving:
        copy.wait()


def whole_items(shape, *arguments):
    line = shape["rows"]
    whole = Given(*arguments)
    given = whole._asdict()
    frames, cotangent = whole.frames, whole.cotangent
    items, history, strip, width = frames.shape
    c = cotangent.shape[-1]
    cells = strip * line * width
    flat = {}
    for name, value in given.items():
        if value is cotangent:
            value = value.reshape(items, strip * width, c)
        elif name in LARGE:
            value = value.reshape(-1, c)
        elif value.ndim == 1 and name not in IN_SMEM:
            value = value.reshape(-1, c)
        flat[name] = value
    shapes = {name: flat[name].shape for name in LARGE}
    big_layout = layout_of(SimpleNamespace(**shapes))
    starts, small_at, total_rows, runs = big_layout
    copies = 7 * (line - 1) + len(runs) * (8 + 2 * (line - 1)) + 6
    landing = sum(rows // 2 + 5 * rows // 8 for _, rows in runs) + LATE_COUNT * (8 + line)
    shifted = pltpu.VMEM((cells + 2 * width, 6 * c), BF16)
    forward = pltpu.VMEM((18 * c, 2 * c), BF16)
    backward = forward
    field = pltpu.VMEM((cells, c), F32)
    flipped_field = pltpu.VMEM((2 * c, cells), BF16)
    quarter = cells // 4
    scratch = dict(
        small=pltpu.VMEM((LATE_COUNT, c), F32),
        send=pltpu.SemaphoreType.DMA((copies,)),
        recv=pltpu.SemaphoreType.DMA((copies,)),
        local=pltpu.SemaphoreType.DMA((12 + len(runs),)),
        sums=pltpu.VMEM((total_rows, c), F32),
        final=pltpu.VMEM((total_rows, c), F32),
        landing=pltpu.VMEM((landing, c), F32),
        frames_in=pltpu.VMEM((line, history, strip, width), F32),
        mask_in=pltpu.VMEM((line, strip, width), jnp.int32),
        frames_out=pltpu.VMEM((line, history, strip, width), F32),
        frames_from=pltpu.VMEM((line, history, strip, width), F32),
        frames_here=pltpu.VMEM((line, history, strip, width), F32),
        mask_from=pltpu.VMEM((line, strip, width), jnp.int32),
        cot_from=pltpu.VMEM((items, strip * width, c), F32),
        output_here=pltpu.VMEM((items, strip * width, c), F32),
        fields=pltpu.VMEM((16, cells), F32),
        lift=pltpu.VMEM((16, c), F32),
        joined=pltpu.VMEM((cells, 4 * c), BF16),
        x_down=pltpu.VMEM((quarter, 8 * c), BF16),
        x_grad_up=pltpu.VMEM((quarter, 8 * c), BF16),
        x_up=pltpu.VMEM((quarter, 2 * c), BF16),
        x_grad_low=pltpu.VMEM((quarter, 2 * c), BF16),
        f_down=pltpu.VMEM((8 * c, 2 * c), BF16),
        b_down=pltpu.VMEM((4, 2 * c, 2 * c), BF16),
        f_up=pltpu.VMEM((4, 2 * c, 2 * c), BF16),
        b_up=pltpu.VMEM((8 * c, 2 * c), BF16),
        f_skip=pltpu.VMEM((4 * c, 2 * c), BF16),
        b_skip=pltpu.VMEM((2, 2 * c, 2 * c), BF16),
        xe1=shifted,
        xe2=shifted,
        xd1a=shifted,
        xd1b=shifted,
        xd2=shifted,
        xg=shifted,
        te1=flipped_field,
        te2=flipped_field,
        td1=pltpu.VMEM((4 * c, cells), BF16),
        td2=flipped_field,
        turned=pltpu.VMEM((4 * c, cells), BF16),
        fe1=forward,
        fe2=forward,
        fd1a=forward,
        fd1b=forward,
        fd2=forward,
        be1=backward,
        be2=backward,
        bd1a=backward,
        bd1b=backward,
        bd2=backward,
        slope_e1=field,
        slope_e2=field,
        slope_d1a=field,
        slope_d1b=field,
        slope_d2=field,
        lifted=field,
        middle_e=field,
        encoded=field,
        raised=field,
        middle_d=field,
        result=field,
        cot=field,
        grad=field,
        grad_a=field,
        grad_b=field,
    )
    scratch.update({name: pltpu.VMEM(shapes[name], F32) for name in LARGE})

    in_hbm = pl.BlockSpec(memory_space=pl.ANY)
    in_vmem = pl.BlockSpec(memory_space=pltpu.VMEM)
    in_smem = pl.BlockSpec(memory_space=pltpu.SMEM)
    in_specs = [
        in_hbm if name in IN_HBM else in_smem if name in IN_SMEM else in_vmem
        for name in ARGUMENTS
    ]
    out_shape = [
        jax.ShapeDtypeStruct((items, strip * width, c), F32),
        jax.ShapeDtypeStruct(frames.shape, F32),
        jax.ShapeDtypeStruct((total_rows, c), F32),
    ]
    out_specs = [in_hbm] * 3
    results = pl.pallas_call(
        functools.partial(
            item_kernel,
            (line, strip, width, shapes, big_layout),
            tuple(scratch),
        ),
        out_shape=out_shape,
        in_specs=in_specs,
        out_specs=out_specs,
        scratch_shapes=list(scratch.values()),
        compiler_params=pltpu.CompilerParams(
            collective_id=0, has_side_effects=True, vmem_limit_bytes=62 * 1024 * 1024
        ),
    )(*[flat[name] for name in ARGUMENTS])
    names = LARGE + tuple(SMALL_ROWS)
    written = pl.pallas_call(
        functools.partial(write_kernel, (shapes, starts, small_at)),
        out_shape=out_shape[:2] + [jax.ShapeDtypeStruct(flat[name].shape, F32) for name in names],
        in_specs=[pl.BlockSpec(memory_space=pltpu.HBM)] * 3,
        out_specs=[in_hbm] * (2 + len(LARGE)) + [in_vmem] * len(SMALL_ROWS),
        scratch_shapes=[
            pltpu.VMEM((items, strip * width, c), F32),
            pltpu.VMEM(frames.shape, F32),
            pltpu.VMEM((total_rows, c), F32),
            pltpu.SemaphoreType.DMA((1 + 2 * (2 + len(LARGE)),)),
        ],
        compiler_params=pltpu.CompilerParams(vmem_limit_bytes=60 * 1024 * 1024),
    )(*results)
    grads = dict(zip(names, written[2:]))
    ordered = [name for name in ARGUMENTS if name in grads]
    return (written[0].reshape(cotangent.shape), written[1]) + tuple(
        grads[name].reshape(given[name].shape) for name in ordered
    )


def body(shape, *arguments):
    items, _, strip, width = arguments[0].shape
    line = shape["rows"]
    whole = (
        shape["section"] == 2
        and shape["batch"] == 4
        and items == line == 4
        and arguments[-1].shape[-1] == 128
        and (strip * line * width) % CHUNK == 0
    )
    return whole_items(shape, *arguments) if whole else strips_body(*arguments)


def solution(mesh):
    in_specs = (
        P(("section", "batch"), None, "rows", None),
        P(("section", "batch")),
        P(("section", "batch"), "rows", None),
        P(("section", "batch")),
        P(),
        P(),
        P(),
        P(),
        P(),
        P(),
        P(),
        P(),
        P(),
        P(),
        P(),
        P(),
        P(),
        P(),
        P(),
        P(),
        P(),
        P(),
        P(),
        P(),
        P(),
        P(),
        P(),
        P(),
        P(("section", "batch"), "rows", None, None),
    )
    out_specs = (
        P(("section", "batch"), "rows", None, None),
        P(("section", "batch"), None, "rows", None),
        P(),
        P(),
        P(),
        P(),
        P(),
        P(),
        P(),
        P(),
        P(),
        P(),
        P(),
        P(),
        P(),
        P(),
        P(),
        P(),
        P(),
        P(),
        P(),
        P(),
        P(),
        P(),
        P(),
        P(),
    )
    return jax.shard_map(functools.partial(body, mesh.shape), mesh=mesh, in_specs=in_specs, out_specs=out_specs, check_vma=False)
```

```python
import functools
from types import SimpleNamespace
from typing import Any, NamedTuple

import jax
import jax.numpy as jnp
from jax import lax
from jax.experimental import pallas as pl
from jax.experimental.pallas import tpu as pltpu
from jax.sharding import PartitionSpec as P

GROUPS = 8
FIELDS = 3
HIST = 4


EPS = 1e-05
HIGH = lax.Precision.HIGHEST


def extended(cells, sides, width):
    for axis, dim in sides:
        count = lax.axis_size(axis)
        ends = count - 1
        head = lax.slice_in_dim(cells, 0, width, axis=dim)
        tail = lax.slice_in_dim(cells, cells.shape[dim] - width, cells.shape[dim], axis=dim)
        cells = jnp.concatenate(
            [
                lax.ppermute(tail, axis, [(i, (i + 1) % count) for i in range(ends)]),
                cells,
                lax.ppermute(head, axis, [((i + 1) % count, i) for i in range(ends)]),
            ],
            axis=dim,
        )
    return cells


def from_behind(value, axis, steps):
    count = lax.axis_size(axis)
    pairs = [(source, (source + steps) % count) for source in range(count)]
    return lax.ppermute(value, axis, pairs)


def group_view(value_arrays):
    extent = value_arrays.shape
    return value_arrays.reshape(extent[:-1] + (GROUPS, extent[-1] // GROUPS))


def global_sums(value_arrays):
    grouped = group_view(value_arrays)
    flat = grouped.reshape(-1, GROUPS, grouped.shape[-1])
    first_sum = jnp.sum(flat, axis=(0, 2))
    second_sum = jnp.sum(flat * flat, axis=(0, 2))
    return lax.psum((first_sum, second_sum), "rows")


def apply_norm(value_arrays, sum_one, sum_two, norm_gain, norm_bias, total):
    grouped = group_view(value_arrays)
    group_mean = sum_one / total
    variance = sum_two / total - group_mean * group_mean
    inverse = lax.rsqrt(variance + EPS)
    normed = (grouped - group_mean[:, None]) * inverse[:, None]
    return normed.reshape(value_arrays.shape) * norm_gain + norm_bias


def norm_back(value_arrays, grad_one, grad_two):
    grouped = group_view(value_arrays)
    extra = grad_one[:, None] + 2.0 * grouped * grad_two[:, None]
    return extra.reshape(value_arrays.shape)


def reduce_grads(grad_one, grad_two):
    return lax.psum((grad_one, grad_two), "rows")


def conv_rows(padded, kernel):
    widened = jnp.pad(padded, ((0, 0), (1, 1), (0, 0)))
    return lax.conv_general_dilated(
        widened[None],
        kernel,
        (1, 1),
        "VALID",
        dimension_numbers=("NHWC", "HWIO", "NHWC"),
        precision=HIGH,
    )[0]


def flipped(kernel):
    return jnp.transpose(kernel[::-1, ::-1], (0, 1, 3, 2))


def pad_grads(value_arrays):
    return extended(value_arrays, (("rows", 0),), 1)


def totals_of(inputs, conv1):
    strip = inputs.shape[0]
    cells = strip * lax.axis_size("rows") * inputs.shape[1]
    return (cells * (inputs.shape[2] // GROUPS), cells * (conv1.shape[3] // GROUPS))


def block_forward(inputs, weights, scale_part, shift_part):
    norm1_gain, norm1_bias, conv1, norm2_gain, norm2_bias, conv2, conv2_bias = weights
    total_in, total_mid = totals_of(inputs, conv1)
    sums_in = global_sums(inputs)

    def pad_rows(value_arrays):
        return extended(value_arrays, (("rows", 0),), 1)

    act_one = pad_rows(
        jax.nn.gelu(
            apply_norm(inputs, sums_in[0], sums_in[1], norm1_gain, norm1_bias, total_in),
            approximate=False,
        )
    )
    middle = conv_rows(act_one, conv1)
    sums_mid = global_sums(middle)
    shaped = (
        apply_norm(middle, sums_mid[0], sums_mid[1], norm2_gain, norm2_bias, total_mid)
        * (1.0 + scale_part)
        + shift_part
    )
    act_two = pad_rows(jax.nn.gelu(shaped, approximate=False))
    branch = conv_rows(act_two, conv2) + conv2_bias
    return (branch, (sums_in[0], sums_in[1], act_one, middle, sums_mid[0], sums_mid[1], act_two))


def block_backward(inputs, weights, scale_part, shift_part, kept, grad_out):
    norm1_gain, norm1_bias, conv1, norm2_gain, norm2_bias, conv2, conv2_bias = weights
    in_one, in_two, act_one, middle, mid_one, mid_two, act_two = kept
    total_in, total_mid = totals_of(inputs, conv1)
    grad_conv2 = jax.vjp(lambda kernel: conv_rows(act_two, kernel), conv2)[1](grad_out)[0]
    grad_bias2 = jnp.sum(grad_out, axis=(0, 1))
    grad_act_two = conv_rows(pad_grads(grad_out), flipped(conv2))

    def second_piece(middle_in, sum_one, sum_two, gain_in, incoming_bias, scale_in, shift_in):
        shaped = (
            apply_norm(middle_in, sum_one, sum_two, gain_in, incoming_bias, total_mid)
            * (1.0 + scale_in)
            + shift_in
        )
        return jax.nn.gelu(shaped, approximate=False)

    second_pull = jax.vjp(
        second_piece, middle, mid_one, mid_two, norm2_gain, norm2_bias, scale_part, shift_part
    )[1](grad_act_two)
    summed_one, summed_two = reduce_grads(second_pull[1], second_pull[2])
    grad_middle = second_pull[0] + norm_back(middle, summed_one, summed_two)
    grad_conv1 = jax.vjp(lambda kernel: conv_rows(act_one, kernel), conv1)[1](grad_middle)[0]
    grad_act_one = conv_rows(pad_grads(grad_middle), flipped(conv1))

    def first_piece(inputs_in, sum_one, sum_two, gain_in, incoming_bias):
        return jax.nn.gelu(
            apply_norm(inputs_in, sum_one, sum_two, gain_in, incoming_bias, total_in),
            approximate=False,
        )

    first_pull = jax.vjp(first_piece, inputs, in_one, in_two, norm1_gain, norm1_bias)[1](
        grad_act_one
    )
    first_one, first_two = reduce_grads(first_pull[1], first_pull[2])
    grad_inputs = first_pull[0] + norm_back(inputs, first_one, first_two)
    grads = (
        first_pull[3],
        first_pull[4],
        grad_conv1,
        second_pull[3],
        second_pull[4],
        grad_conv2,
        grad_bias2,
    )
    return (grad_inputs, grads, second_pull[5], second_pull[6])


def conditioning(step_item, table):
    one_hot = (jnp.arange(table.shape[0], dtype=jnp.int32) == step_item).astype(jnp.float32)
    condition = jnp.dot(one_hot, table, precision=HIGH)
    half_width = table.shape[1] // 2
    return (condition[:half_width], condition[half_width:], one_hot)


def project_in(frames_item, mask_item, count_item, incoming_weight, incoming_bias):
    history = jnp.arange(HIST, dtype=jnp.int32) >= HIST - count_item
    keep = jnp.repeat(history, FIELDS).astype(jnp.float32)
    lifted = (
        jnp.einsum(
            "fhw,fc->hwc", frames_item * keep[:, None, None], incoming_weight, precision=HIGH
        )
        + incoming_bias
    )
    return lifted * mask_item[:, :, None].astype(jnp.float32)


def coarsen_field(value_arrays, incoming_weight, incoming_bias):
    rows_here, width_here, depth_here = value_arrays.shape
    blocks = value_arrays.reshape(rows_here // 2, 2, width_here // 2, 2, depth_here)
    return jnp.einsum("iajbk,abkc->ijc", blocks, incoming_weight, precision=HIGH) + incoming_bias


def upsample(value_arrays, incoming_weight, incoming_bias):
    result = jnp.einsum("ijk,abkc->iajbc", value_arrays, incoming_weight, precision=HIGH)
    extent = result.shape
    return result.reshape(extent[0] * 2, extent[2] * 2, extent[4]) + incoming_bias


def flatten_all(pieces):
    return jnp.concatenate([piece.reshape(-1) for piece in pieces])


def unflatten_all(flat, templates):
    pieces = []
    offset_at = 0
    for template in templates:
        count_here = template.size
        pieces.append(flat[offset_at : offset_at + count_here].reshape(template.shape))
        offset_at += count_here
    return tuple(pieces)


def strips_body(
    frames,
    counts,
    cell_mask,
    step_index,
    lift_weight,
    lift_bias,
    enc_norm1_gain,
    enc_norm1_bias,
    enc_conv1,
    enc_step_table,
    enc_norm2_gain,
    enc_norm2_bias,
    enc_conv2,
    enc_conv2_bias,
    reducer_weight,
    reducer_bias,
    up_weight,
    up_bias,
    dec_norm1_gain,
    dec_norm1_bias,
    dec_conv1,
    dec_step_table,
    dec_norm2_gain,
    dec_norm2_bias,
    dec_conv2,
    dec_conv2_bias,
    skip_weight,
    skip_bias,
    cotangent,
):
    enc_weights = (
        enc_norm1_gain,
        enc_norm1_bias,
        enc_conv1,
        enc_norm2_gain,
        enc_norm2_bias,
        enc_conv2,
        enc_conv2_bias,
    )
    dec_weights = (
        dec_norm1_gain,
        dec_norm1_bias,
        dec_conv1,
        dec_norm2_gain,
        dec_norm2_bias,
        dec_conv2,
        dec_conv2_bias,
    )
    params = (
        lift_weight,
        lift_bias,
        enc_norm1_gain,
        enc_norm1_bias,
        enc_conv1,
        enc_step_table,
        enc_norm2_gain,
        enc_norm2_bias,
        enc_conv2,
        enc_conv2_bias,
        reducer_weight,
        reducer_bias,
        up_weight,
        up_bias,
        dec_norm1_gain,
        dec_norm1_bias,
        dec_conv1,
        dec_step_table,
        dec_norm2_gain,
        dec_norm2_bias,
        dec_conv2,
        dec_conv2_bias,
        skip_weight,
        skip_bias,
    )

    def forward_micro(carry, sliced):
        frames_item, mask_item, count_item, step_item = sliced
        lifted = project_in(frames_item, mask_item, count_item, lift_weight, lift_bias)
        enc_scale, enc_shift, unused_hot = conditioning(step_item, enc_step_table)
        enc_branch, enc_kept = block_forward(lifted, enc_weights, enc_scale, enc_shift)
        encoder_result = lifted + enc_branch
        coarse_field = coarsen_field(encoder_result, reducer_weight, reducer_bias)
        foreign = from_behind(coarse_field, "section", 1)
        raised_foreign = upsample(foreign, up_weight, up_bias)
        raised = from_behind(raised_foreign, "section", 1)
        joined = jnp.concatenate([raised, encoder_result], axis=-1)
        dec_scale, dec_shift, unused_again = conditioning(step_item, dec_step_table)
        dec_branch, dec_kept = block_forward(joined, dec_weights, dec_scale, dec_shift)
        output_item = jnp.dot(joined, skip_weight, precision=HIGH) + skip_bias + dec_branch
        return (carry, (output_item, (lifted, enc_kept, encoder_result, foreign, joined, dec_kept)))

    unused, (output, kept_all) = lax.scan(
        forward_micro, jnp.zeros((), jnp.float32), (frames, cell_mask, counts, step_index)
    )

    def backward_micro(totals, sliced):
        frames_item, mask_item, count_item, step_item, grad_out, kept = sliced
        lifted, enc_kept, encoder_result, foreign, joined, dec_kept = kept
        dec_scale, dec_shift, one_hot = conditioning(step_item, dec_step_table)
        grad_joined, dec_grads, dec_gscale, dec_gshift = block_backward(
            joined, dec_weights, dec_scale, dec_shift, dec_kept, grad_out
        )
        grad_skip_weight = jnp.einsum("hwk,hwc->kc", joined, grad_out, precision=HIGH)
        grad_skip_bias = jnp.sum(grad_out, axis=(0, 1))
        grad_joined = grad_joined + jnp.dot(grad_out, skip_weight.T, precision=HIGH)
        half_width = joined.shape[-1] // 2
        grad_raised = grad_joined[..., :half_width]
        grad_encoded = grad_joined[..., half_width:]
        grad_foreign_up = from_behind(grad_raised, "section", 1)
        up_pull = jax.vjp(upsample, foreign, up_weight, up_bias)[1](grad_foreign_up)
        coarse_gradient = from_behind(up_pull[0], "section", 1)
        reducer_pullback = jax.vjp(coarsen_field, encoder_result, reducer_weight, reducer_bias)[1](
            coarse_gradient
        )
        grad_encoded = grad_encoded + reducer_pullback[0]
        enc_scale, enc_shift, enc_hot = conditioning(step_item, enc_step_table)
        grad_lifted, enc_grads, enc_gscale, enc_gshift = block_backward(
            lifted, enc_weights, enc_scale, enc_shift, enc_kept, grad_encoded
        )
        grad_lifted = grad_lifted + grad_encoded
        proj_pull = jax.vjp(
            lambda frames_in, incoming_weight, incoming_bias: project_in(
                frames_in, mask_item, count_item, incoming_weight, incoming_bias
            ),
            frames_item,
            lift_weight,
            lift_bias,
        )[1](grad_lifted)
        enc_table_grad = enc_hot[:, None] * jnp.concatenate([enc_gscale, enc_gshift])[None, :]
        dec_table_grad = one_hot[:, None] * jnp.concatenate([dec_gscale, dec_gshift])[None, :]
        micro_list = (
            proj_pull[1],
            proj_pull[2],
            enc_grads[0],
            enc_grads[1],
            enc_grads[2],
            enc_table_grad,
            enc_grads[3],
            enc_grads[4],
            enc_grads[5],
            enc_grads[6],
            reducer_pullback[1],
            reducer_pullback[2],
            up_pull[1],
            up_pull[2],
            dec_grads[0],
            dec_grads[1],
            dec_grads[2],
            dec_table_grad,
            dec_grads[3],
            dec_grads[4],
            dec_grads[5],
            dec_grads[6],
            grad_skip_weight,
            grad_skip_bias,
        )
        micro_flat = flatten_all(micro_list)
        return (totals + micro_flat, proj_pull[0])

    total_size = sum((piece.size for piece in params))
    start_totals = jnp.zeros((total_size,), jnp.float32)
    flat_totals, frames_grad = lax.scan(
        backward_micro,
        start_totals,
        (frames, cell_mask, counts, step_index, cotangent, kept_all),
        reverse=True,
    )
    flat_totals = lax.psum(flat_totals, ("section", "batch", "rows"))
    grads = unflatten_all(flat_totals, params)
    return (output, frames_grad) + grads


F32 = jnp.float32
BF16 = jnp.bfloat16
MESH = pl.DeviceIdType.MESH
NN = ((1,), (0,))
NT = ((1,), (1,))
TN = ((0,), (0,))
HIGH_AT = (0, 2, 1)
LOW_AT = (4, 3, 5)
CHUNK = 512
class Given(NamedTuple):
    frames: Any
    counts: Any
    cell_mask: Any
    step_index: Any
    lift_weight: Any
    lift_bias: Any
    enc_norm1_gain: Any
    enc_norm1_bias: Any
    enc_conv1: Any
    enc_step_table: Any
    enc_norm2_gain: Any
    enc_norm2_bias: Any
    enc_conv2: Any
    enc_conv2_bias: Any
    reducer_weight: Any
    reducer_bias: Any
    up_weight: Any
    up_bias: Any
    dec_norm1_gain: Any
    dec_norm1_bias: Any
    dec_conv1: Any
    dec_step_table: Any
    dec_norm2_gain: Any
    dec_norm2_bias: Any
    dec_conv2: Any
    dec_conv2_bias: Any
    skip_weight: Any
    skip_bias: Any
    cotangent: Any


ARGUMENTS = Given._fields
LARGE = tuple(
    dict(
        dec_conv1=0,
        up_weight=0,
        reducer_weight=0,
        dec_conv2=0,
        skip_weight=0,
        enc_conv1=0,
        enc_conv2=0,
    )
)
IN_HBM = tuple(dict(frames=0, cell_mask=0, cotangent=0)) + LARGE
IN_SMEM = tuple(dict(counts=0, step_index=0))
LATE = 64
SMALL_ROWS = dict(
    enc_conv2_bias=(0, 1),
    reducer_bias=(1, 1),
    up_bias=(2, 1),
    dec_conv2_bias=(3, 1),
    skip_bias=(3, 1),
    dec_norm1_gain=(4, 2),
    dec_norm1_bias=(6, 2),
    dec_norm2_gain=(8, 1),
    dec_norm2_bias=(9, 1),
    dec_step_table=(16, 8),
    lift_weight=(LATE, 12),
    lift_bias=(LATE + 12, 1),
    enc_norm1_gain=(LATE + 16, 1),
    enc_norm1_bias=(LATE + 17, 1),
    enc_norm2_gain=(LATE + 18, 1),
    enc_norm2_bias=(LATE + 19, 1),
    enc_step_table=(LATE + 24, 8),
)
LATE_COUNT = 32
SMALL_COUNT = LATE + LATE_COUNT
DUE = ((), (), (), (), (), (0,), (), (1,), (), (), (2,), (3, 0), (), (), (1,), (), (), (2,), (0,), (1, 4, 3), (2,), (), (), (5, 0), (1, 3), (4, 2), (), (6,), (7, 3, 0, 5, 4, 1, 2))
REST = (6, 3, 7, 4, 5, 6, 8, 7, 0, 4, 5, 1, 6, 7, 2, 0, 1, 5, 3, 6, 2, 8, 7, 3, 4, 5, 4, 6, 7, 5, 6, 7)
OUTPUTS = tuple(dict(output=0, frames_grad=0, gradients=0))


def split(value):
    high = value.astype(BF16)
    return high, (value - high.astype(F32)).astype(BF16)


def dot(left, right, dims=NN, precision=None):
    return lax.dot_general(
        left, right, (dims, ((), ())), precision=precision, preferred_element_type=F32
    )


def fold(value):
    half = value.shape[1] // 2
    return value[:, :half] + value[:, half:]


def fold_rows(value):
    half = value.shape[0] // 2
    return value[:half] + value[half:]


def tile_sums(value):
    return jnp.sum(value.reshape(-1, 8, value.shape[-1]), axis=0)


def column_sum(tiles):
    return jnp.sum(tiles, axis=0, keepdims=True)


def normal(value):
    bell = jnp.exp(-0.5 * value * value)
    t = 1.0 / (1.0 + 0.2316418882663604 * jnp.abs(value))
    poly = 0.5307027145
    for factor in (-0.7265760135, 0.7107068705, -0.142248368, 0.127414796):
        poly = poly * t + factor
    tail = poly * t * bell
    return jnp.where(value < 0.0, tail, 1.0 - tail), 0.3989422804014327 * bell


def dot_three(left, right, dims=NN):
    left_high, left_low = split(left)
    right_high, right_low = split(right)
    total = dot(left_high, right_high, dims)
    return total + (dot(left_high, right_low, dims) + dot(left_low, right_high, dims))


def group_ones(channels, size):
    rows = lax.broadcasted_iota(jnp.int32, (channels, channels), 0) // size
    columns = lax.broadcasted_iota(jnp.int32, (channels, channels), 1) // size
    return (rows == columns).astype(BF16)


def group_sums(first, second, ones):
    terms = []
    rest = jnp.concatenate([first, second], axis=0)
    for _ in range(3):
        term = rest.astype(BF16)
        terms.append(term)
        rest = rest - term.astype(F32)
    both = dot(jnp.concatenate(terms, axis=0), ones)
    both = both[32:48] + both[16:32] + both[:16]
    return column_sum(both[:8]), column_sum(both[8:])


class LineSwap:

    def __init__(self, line, source, target, inward, across, make):
        far = 3 - line.outer
        self.line = line
        to_inner, to_across = line.device(line.inner), line.device(line.across)
        to_outer = line.device(line.outer)
        here = target(line.here)
        self.to_far = make(source(3 - line.here), inward.at[1], to_inner)
        self.to_second = make(source(3 - line.inner), inward.at[0], to_inner)
        self.to_inner = make(source(line.inner), here, to_inner)
        self.for_far = make(source(far), across.at[0], to_across)
        self.to_across = make(source(line.across), here, to_across)
        self.to_outer = make(source(line.outer), here, to_outer)
        self.pass_far = make(inward.at[1], across.at[1], to_across)
        self.pass_second = make(inward.at[0], target(line.outer), to_across)
        self.pass_across = make(across.at[0], target(line.across), to_outer)
        self.pass_opposite = make(across.at[1], target(far), to_outer)

    def first(self):
        @pl.when(self.line.edge)
        def _():
            for copy in (self.to_far, self.to_second, self.to_inner):
                copy.start()

        @pl.when(self.line.middle)
        def _():
            for copy in (self.for_far, self.to_across, self.to_outer):
                copy.start()

    def second(self):
        @pl.when(self.line.middle)
        def _():
            self.for_far.wait_recv()
            self.pass_across.start()
            self.to_far.wait_recv()
            self.pass_far.start()
            self.to_second.wait_recv()
            self.pass_second.start()

    def third(self):
        @pl.when(self.line.middle)
        def _():
            self.pass_far.wait_recv()
            self.pass_opposite.start()

    def arrive(self):
        @pl.when(self.line.edge)
        def _():
            for copy in (self.to_outer, self.pass_across, self.pass_opposite):
                copy.wait_recv()

        @pl.when(self.line.middle)
        def _():
            for copy in (self.to_inner, self.to_across, self.pass_second):
                copy.wait_recv()

    def sent(self):
        @pl.when(self.line.edge)
        def _():
            for copy in (self.to_far, self.to_second, self.to_inner):
                copy.wait_send()

        @pl.when(self.line.middle)
        def _():
            for copy in (self.for_far, self.to_across, self.to_outer):
                copy.wait_send()
            for copy in (self.pass_far, self.pass_second, self.pass_across, self.pass_opposite):
                copy.wait_send()


class Exchange:

    def __init__(self, place, start, rows, landing, first_sem):
        self.place, self.start, self.rows, self.landing = place, start, rows, landing
        self.sem = first_sem
        self.stage = 0
        self.copies = []
        self.waiting = []
        self.group = place.plane_group
        self.half = rows // 2
        self.base = start + place.core * self.half
        self._finish(self.half)

    def _finish(self, size):
        self.part = size // self.group.count
        self.own = self.base + self.group.here * self.part

    def count(self):
        return 2 + 2 * (self.group.count - 1) + 3

    def land_rows(self):
        return self.half + (self.group.count + 1) * self.part

    def _copy(self, source, target, device, only=None):
        place = self.place
        copy = pltpu.make_async_remote_copy(
            src_ref=source,
            dst_ref=target,
            send_sem=place.send.at[self.sem],
            recv_sem=place.recv.at[self.sem],
            device_id=device,
            device_id_type=MESH,
        )
        self.sem += 1
        if only is None:
            copy.start()
            self.waiting.append(copy)
        self.copies.append((copy, only))
        return copy

    def _wait(self):
        for copy in self.waiting:
            copy.wait_recv()
        self.waiting = []

    def _rows(self, at, size):
        return pl.ds(pl.multiple_of(at, 8), size)

    def _swap(self):
        place = self.place
        other = self._rows(self.start + (1 - place.core) * self.half, self.half)
        self.land = self.landing
        self.landing += self.half
        self._copy(
            place.sums.at[other], place.landing.at[pl.ds(self.land, self.half)], place.partner
        )

    def _add_swap(self):
        place = self.place
        block = 64 if self.half % 64 == 0 else 32

        def step(i, carry):
            here = self._rows(self.base + i * block, block)
            there = self._rows(self.land + i * block, block)
            place.sums[here] = place.sums[here] + place.landing[there]
            return carry

        lax.fori_loop(0, self.half // block, step, 0)

    def _scatter(self, group, base, size):
        place = self.place
        self.land = self.landing
        for k in range(1, group.count):
            to = lax.rem(group.here + k, group.count)
            self._copy(
                place.sums.at[self._rows(base + to * size, size)],
                place.landing.at[pl.ds(self.landing, size)],
                group.device(to),
            )
            self.landing += size

    def _total(self, group, own, size, target):
        place = self.place
        block = 16 if size % 16 == 0 else 8

        def step(i, carry):
            here = self._rows(own + i * block, block)
            total = place.sums[here]
            for k in range(group.count - 1):
                there = self._rows(self.land + k * size + i * block, block)
                total = total + place.landing[there]
            target[here] = total
            return carry

        lax.fori_loop(0, size // block, step, 0)

    def _gather(self, group, own, size):
        final = self.place.final
        here = self._rows(own, size)
        for k in range(1, group.count):
            to = lax.rem(group.here + k, group.count)
            self._copy(final.at[here], final.at[here], group.device(to))

    def _steps(self):
        place, group = self.place, self.group
        yield self._swap()
        self._wait()
        self._add_swap()
        yield from self._both()
        final = place.final
        here = self._rows(self.base, self.half)
        self._copy(final.at[here], final.at[here], place.partner)
        yield
        self._wait()
        yield

    def _both(self):
        place, group = self.place, self.group
        self._scatter(group, self.base, self.part)
        yield
        self._wait()
        self._total(group, self.own, self.part, place.sums)
        yield from self._line()
        self._gather(group, self.own, self.part)
        yield
        self._wait()

    def _line(self):
        place, line = self.place, self.place.line
        sums, final, landing = place.sums, place.final, place.landing
        part, own = self.part, self._rows(self.own, self.part)
        inward, across = pl.ds(self.landing, part), pl.ds(self.landing + part, part)
        self.landing += 2 * part
        block = 16 if part % 16 == 0 else 8

        def add(at, target):
            def step(i, carry):
                here = self._rows(self.own + i * block, block)
                target[here] = sums[here] + landing[pl.ds(at + i * block, block)]
                return carry

            lax.fori_loop(0, part // block, step, 0)

        first = self._copy(sums.at[own], landing.at[inward], line.device(line.inner), line.edge)
        second = self._copy(sums.at[own], landing.at[across], line.device(line.across), line.middle)
        third = self._copy(final.at[own], final.at[own], line.device(line.outer), line.middle)
        pl.when(line.edge)(first.start)
        yield

        @pl.when(line.middle)
        def _():
            first.wait_recv()
            add(self.landing - 2 * part, sums)
            second.start()

        yield

        @pl.when(line.middle)
        def _():
            second.wait_recv()
            add(self.landing - part, final)
            third.start()

        yield
        pl.when(line.edge)(third.wait_recv)

    def advance(self):
        if self.stage == 0:
            self.steps = self._steps()
        self.stage += 1
        next(self.steps)

    def done(self):
        return self.stage == 8


class SmallExchange(Exchange):

    def count(self):
        return self.place.cores_group.count + self.place.line.count - 2

    def land_rows(self):
        return self.rows * (self.place.cores_group.count + self.place.line.count)

    def _share(self, group, source):
        place = self.place
        self.land = self.landing
        self.landing += group.count * self.rows
        own = self._rows(self.land + group.here * self.rows, self.rows)
        place.landing[own] = source[...]
        for k in range(1, group.count):
            to = lax.rem(group.here + k, group.count)
            self._copy(source, place.landing.at[own], group.device(to))

    def _sum(self, group):
        total = None
        for k in range(group.count):
            part = self.place.landing[pl.ds(self.land + k * self.rows, self.rows)]
            total = part if total is None else total + part
        return total

    def _steps(self):
        place = self.place
        here = pl.ds(self.start, self.rows)
        self._share(place.line, place.sums.at[here])
        yield
        self._wait()
        place.small[...] = self._sum(place.line)
        self._share(place.cores_group, place.small)
        yield
        self._wait()
        place.final[here] = self._sum(place.cores_group)
        yield

    def done(self):
        return self.stage == 3


def layout_of(shapes):
    starts = {}
    at = 0
    for name in LARGE:
        starts[name] = at
        at += getattr(shapes, name)[0]
    small = at
    begins = SimpleNamespace(**starts)
    late = small + LATE
    tap = shapes.dec_conv2[0] // 3
    part = shapes.dec_conv1[0] // 3
    conv1, up = begins.dec_conv1, begins.up_weight
    edges = (
        (begins.dec_conv2, begins.enc_conv1),
        (conv1, conv1 + part),
        (conv1 + part, conv1 + 2 * part),
        (conv1 + 2 * part, up),
        (up, begins.dec_conv2),
        (begins.enc_conv2, late),
        (begins.enc_conv1, begins.enc_conv1 + 2 * tap),
        (begins.enc_conv1 + 2 * tap, begins.enc_conv2),
        (late, late + LATE_COUNT),
    )
    runs = [(first, last - first) for first, last in edges]
    return starts, small, late + LATE_COUNT, runs


def item_kernel(sizes, scratch_names, *refs):
    line, strip, width, shapes, big_layout = sizes
    begins, small_at, total_rows, runs = big_layout
    starts = SimpleNamespace(**begins)
    inputs = Given(*refs[: len(ARGUMENTS)])
    refs = refs[len(ARGUMENTS) :]
    output_names = OUTPUTS
    outputs = SimpleNamespace(**dict(zip(output_names, refs)))
    scratch = SimpleNamespace(**dict(zip(scratch_names, refs[len(output_names) :])))

    def w_of(name):
        return getattr(scratch, name)

    height = strip * line
    cells = height * width
    c = inputs.lift_weight.shape[1]
    strip_cells = strip * width
    history = inputs.frames.shape[1]

    core = lax.axis_index("section")
    plane = lax.axis_index("batch")
    row = lax.axis_index("rows")
    middle = lax.rem(row + 1, 4) // 2

    def device_at(to):
        return (core, plane, to)

    place = SimpleNamespace(
        core=core,
        partner=(1 - core, plane, row),
        line=SimpleNamespace(
            count=line,
            here=row,
            device=device_at,
            middle=middle == 1,
            edge=middle == 0,
            inner=1 + row // 2,
            across=3 - row,
            outer=3 * (row // 2),
        ),
        plane_group=SimpleNamespace(
            count=4, here=plane, device=lambda to: (core, to, row)
        ),
        cores_group=SimpleNamespace(
            count=8,
            here=core * 4 + plane,
            device=lambda to: (to // 4, lax.rem(to, 4), row),
        ),
        small=scratch.small,
        sums=scratch.sums,
        final=scratch.final,
        landing=scratch.landing,
        send=scratch.send,
        recv=scratch.recv,
    )
    local_sem = scratch.local

    frames_in, mask_in, cot = scratch.frames_in, scratch.mask_in, scratch.cot
    here_rows = pl.ds(pl.multiple_of(row * strip_cells, strip_cells), strip_cells)
    frames_from, mask_from, cot_from = scratch.frames_from, scratch.mask_from, scratch.cot_from
    staged = (
        pltpu.make_async_copy(inputs.frames, frames_from, local_sem.at[7]),
        pltpu.make_async_copy(inputs.cell_mask, mask_from, local_sem.at[8]),
        pltpu.make_async_copy(inputs.cotangent, cot_from, local_sem.at[9]),
    )
    for copy in staged:
        copy.start()

    weight_copies = {}
    for k, name in enumerate(LARGE):
        copy = pltpu.make_async_copy(getattr(inputs, name), w_of(name), local_sem.at[k])
        weight_copies[name] = copy
        copy.start()

    barrier = pltpu.get_barrier_semaphore()
    peers = [device_at(lax.rem(row + k, line)) for k in range(1, line)]
    cores_group = place.cores_group
    for k in range(1, 8):
        peers.append(cores_group.device(lax.rem(cores_group.here + k, 8)))
    for device in peers:
        pl.semaphore_signal(barrier, inc=1, device_id=device, device_id_type=MESH)
    pl.semaphore_wait(barrier, len(peers))

    next_sem = 0

    def make(source, target, device):
        nonlocal next_sem
        copy = pltpu.make_async_remote_copy(
            src_ref=source,
            dst_ref=target,
            send_sem=scratch.send.at[next_sem],
            recv_sem=scratch.recv.at[next_sem],
            device_id=device,
            device_id_type=MESH,
        )
        next_sem += 1
        return copy

    def send(source, target, device):
        copy = make(source, target, device)
        copy.start()
        return copy

    def strip_of(ref, to):
        return ref.at[pl.ds(pl.multiple_of(to * strip_cells, strip_cells), strip_cells)]

    frame_copies, output_copies = [], []
    for copy in staged[:2]:
        copy.wait()
    for k in range(1, line):
        to = lax.rem(row + k, line)
        device = device_at(to)
        frame_copies.append(send(frames_from.at[to], frames_in.at[row], device))
        frame_copies.append(send(mask_from.at[to], mask_in.at[row], device))
    staged[2].wait()
    cot_swap = LineSwap(
        place.line,
        lambda to: cot_from.at[to],
        lambda source: strip_of(cot, source),
        scratch.cot_inward,
        scratch.cot_across,
        make,
    )
    cot_swap.first()

    copied = SimpleNamespace(**weight_copies)
    def put_pair(target, block, value):
        high, low = split(value)
        rows = slice(block * c, (block + 1) * c)
        target[rows, 0:c] = high
        target[rows, c : 2 * c] = low

    def stack_conv(source, half, depth, forward, backward):
        for a in range(3):
            for b in range(3):
                at = (3 * a + b) * depth + half * c
                value = source[at : at + c, :]
                turned = value.T
                for places in (HIGH_AT, LOW_AT):
                    put_pair(forward, 6 * a + places[b], value)
                    put_pair(backward, 6 * (2 - a) + places[2 - b], turned)

    copied.enc_conv1.wait()
    stack_conv(scratch.enc_conv1, 0, c, scratch.fe1, scratch.be1)
    copied.enc_conv2.wait()
    stack_conv(scratch.enc_conv2, 0, c, scratch.fe2, scratch.be2)
    copied.reducer_weight.wait()
    for k in range(4):
        value = scratch.reducer_weight[k * c : (k + 1) * c, :]
        turned = value.T
        for block in (k, k + 4):
            put_pair(scratch.f_down, block, value)
        for block in (0, 1):
            put_pair(scratch.b_down.at[k], block, turned)
    copied.up_weight.wait()
    for k in range(4):
        value = scratch.up_weight[k * c : (k + 1) * c, :]
        turned = value.T
        for block in (0, 1):
            put_pair(scratch.f_up.at[k], block, value)
        for block in (k, k + 4):
            put_pair(scratch.b_up, block, turned)
    copied.dec_conv1.wait()
    stack_conv(scratch.dec_conv1, 0, 2 * c, scratch.fd1a, scratch.bd1a)
    stack_conv(scratch.dec_conv1, 1, 2 * c, scratch.fd1b, scratch.bd1b)
    copied.dec_conv2.wait()
    stack_conv(scratch.dec_conv2, 0, c, scratch.fd2, scratch.bd2)
    copied.skip_weight.wait()
    for half in range(2):
        value = scratch.skip_weight[half * c : (half + 1) * c, :]
        turned = value.T
        for block in (half, half + 2):
            put_pair(scratch.f_skip, block, value)
        for block in (0, 1):
            put_pair(scratch.b_skip.at[half], block, turned)

    for buffer in (scratch.xe1, scratch.xe2, scratch.xd1a, scratch.xd1b, scratch.xd2, scratch.xg):
        edge = jnp.zeros((width, 6 * c), BF16)
        buffer[0:width, :] = edge
        buffer[cells + width : cells + 2 * width, :] = edge

    lift = scratch.lift
    lift[...] = jnp.zeros(lift.shape, F32)
    lift[0:history, :] = inputs.lift_weight[...]
    lift[history : history + 1, :] = inputs.lift_bias[...]

    block = 2 * width
    column = lax.rem(lax.broadcasted_iota(jnp.int32, (block, c), 0), width)
    at_first, at_last = column == 0, column == width - 1
    zeros8 = jnp.zeros((8, c), F32)
    ones16 = group_ones(c, c // GROUPS)
    ones32 = group_ones(c, 2 * c // GROUPS)
    count16 = float(cells * (c // GROUPS))
    count32 = float(cells * (2 * c // GROUPS))

    def grid_rows(step, carry=0):
        return lax.fori_loop(0, cells // block, step, carry, unroll=2)

    def row_at(h):
        return pl.ds(pl.multiple_of(h * block, block), block)

    def chunk_at(i):
        return pl.ds(pl.multiple_of(i * CHUNK, CHUNK), CHUNK)

    def put_row(target, h, value):
        rows = pl.ds(pl.multiple_of(h * block + width, width), block)
        left = jnp.where(at_first, 0.0, pltpu.roll(value, 1, 0))
        right = jnp.where(at_last, 0.0, pltpu.roll(value, block - 1, 0))
        for b, piece in enumerate((left, value, right)):
            high, low = split(piece)
            target[rows, HIGH_AT[b] * c : (HIGH_AT[b] + 1) * c] = high
            target[rows, LOW_AT[b] * c : (LOW_AT[b] + 1) * c] = low

    def put_turned(target, columns, value, first=0, second=1):
        high, low = split(value.T)
        target[first * c : (first + 1) * c, columns] = high
        target[second * c : (second + 1) * c, columns] = low

    def conv_chunk(pairs, i):
        total = None
        for data, weight in pairs:
            taps = []
            for a in range(3):
                rows = pl.ds(pl.multiple_of(i * CHUNK + a * width, width), CHUNK)
                taps.append(data[rows, :])
            part = dot(jnp.concatenate(taps, axis=1), weight[...])
            total = part if total is None else total + part
        return total

    def norm_of(first, second, ones, count):
        one, two = group_sums(first, second, ones)
        mean = one / count
        return mean, lax.rsqrt(two / count - mean * mean + EPS)

    def activate(source, target, turned, slope, scale, shift):
        def step(h, carry):
            value = source[row_at(h), :] * scale + shift
            below, density = normal(value)
            slope[row_at(h), :] = below + value * density
            value = value * below
            put_row(target, h, value)
            put_turned(turned, row_at(h), value)
            return carry

        grid_rows(step)

    def conv_norm(pairs, target):
        def step(i, carry):
            value = fold(conv_chunk(pairs, i))
            target[chunk_at(i), :] = value
            return carry[0] + tile_sums(value), carry[1] + tile_sums(value * value)

        return lax.fori_loop(0, cells // CHUNK, step, (zeros8, zeros8))

    def sums_of(source):
        def step(h, carry):
            value = source[row_at(h), :]
            return carry[0] + tile_sums(value), carry[1] + tile_sums(value * value)

        return grid_rows(step, (zeros8, zeros8))

    step_here = jnp.full((1, c), inputs.step_index[row], jnp.int32)

    def condition(table):
        total = jnp.zeros((1, 2 * c), F32)
        chosen = jnp.concatenate([step_here, step_here], axis=1)
        for s in range(table.shape[0]):
            total = total + jnp.where(chosen == s, table[s : s + 1, :], 0.0)
        return total[:, :c], total[:, c:]

    frames_in[row] = frames_from[row]
    mask_in[row] = mask_from[row]
    for copy in frame_copies:
        copy.wait_recv()
    fields = scratch.fields
    fields[...] = jnp.zeros(fields.shape, F32)
    frame_of = lax.broadcasted_iota(jnp.int32, (history, width), 0) // FIELDS
    keep = (frame_of >= HIST - inputs.counts[row]).astype(F32)
    masks = []
    for source in range(line):
        for k in range(strip):
            columns = slice((source * strip + k) * width, (source * strip + k + 1) * width)
            mask = mask_in[source, k : k + 1, :].astype(F32)
            masks.append(mask)
            fields[0:history, columns] = frames_in[source, :, k, :] * keep * mask
            fields[history : history + 1, columns] = mask
    lifted = scratch.lifted
    lifted[...] = dot_three(fields[...], lift[...], TN)

    enc_scale, enc_shift = condition(inputs.enc_step_table)
    dec_scale, dec_shift = condition(inputs.dec_step_table)

    mean_e1, inv_e1 = norm_of(*sums_of(lifted), ones16, count16)
    gain_e1, bias_e1 = inputs.enc_norm1_gain[...], inputs.enc_norm1_bias[...]
    a_e1 = inv_e1 * gain_e1
    activate(lifted, scratch.xe1, scratch.te1, scratch.slope_e1, a_e1, bias_e1 - mean_e1 * a_e1)
    middle_e = scratch.middle_e
    mean_e2, inv_e2 = norm_of(
        *conv_norm([(scratch.xe1, scratch.fe1)], middle_e), ones16, count16
    )
    gain_e2, bias_e2 = inputs.enc_norm2_gain[...], inputs.enc_norm2_bias[...]
    a_e2 = inv_e2 * gain_e2
    activate(
        middle_e,
        scratch.xe2,
        scratch.te2,
        scratch.slope_e2,
        a_e2 * (1.0 + enc_scale),
        (bias_e2 - mean_e2 * a_e2) * (1.0 + enc_scale) + enc_shift,
    )
    cot_swap.second()
    encoded = scratch.encoded
    conv2_bias = inputs.enc_conv2_bias[...]
    joined = scratch.joined

    def encode(i, carry):
        value = fold(conv_chunk([(scratch.xe2, scratch.fe2)], i))
        value = value + conv2_bias + lifted[chunk_at(i), :]
        encoded[chunk_at(i), :] = value
        high, low = split(value)
        joined[chunk_at(i), c : 2 * c] = high
        joined[chunk_at(i), 3 * c : 4 * c] = low
        put_turned(scratch.turned, chunk_at(i), value, 1, 3)
        return carry[0] + tile_sums(value), carry[1] + tile_sums(value * value)

    sums_enc = lax.fori_loop(0, cells // CHUNK, encode, (zeros8, zeros8))

    half_cells, quarter = cells // 2, cells // 4

    def pick(source):
        pieces = []
        for b in range(2):
            value = source[pl.ds(b, half_cells, stride=2), :]
            value = value.reshape(height // 2, 2, width // 2, c)
            pieces.append([value[:, a].reshape(quarter, c) for a in range(2)])
        return [pieces[b][a] for a in range(2) for b in range(2)]

    def place_cells(target, pieces):
        for b in range(2):
            both = [pieces[2 * a + b].reshape(height // 2, 1, width // 2, c) for a in range(2)]
            value = jnp.concatenate(both, axis=1).reshape(half_cells, c)
            target[pl.ds(b, half_cells, stride=2), :] = value

    x_down = scratch.x_down
    for k, piece in enumerate(pick(encoded)):
        high, low = split(piece)
        x_down[:, k * c : (k + 1) * c] = high
        x_down[:, (k + 4) * c : (k + 5) * c] = low
    lowered = fold(dot(x_down[...], scratch.f_down[...])) + inputs.reducer_bias[...]
    x_up = scratch.x_up
    high, low = split(lowered)
    x_up[:, 0:c] = high
    x_up[:, c : 2 * c] = low
    raised = scratch.raised
    up_bias = inputs.up_bias[...]
    place_cells(
        raised, [fold(dot(x_up[...], scratch.f_up[k])) + up_bias for k in range(4)]
    )

    def raise_row(h, carry):
        value = raised[row_at(h), :]
        high, low = split(value)
        joined[row_at(h), 0:c] = high
        joined[row_at(h), 2 * c : 3 * c] = low
        put_turned(scratch.turned, row_at(h), value, 0, 2)
        return carry[0] + tile_sums(value), carry[1] + tile_sums(value * value)

    sums_raised = grid_rows(raise_row, (zeros8, zeros8))

    halves = []
    for half, (source, sums) in enumerate(((raised, sums_raised), (encoded, sums_enc))):
        mean, inv = norm_of(*sums, ones32, count32)
        gain = inputs.dec_norm1_gain[half : half + 1, :]
        bias = inputs.dec_norm1_bias[half : half + 1, :]
        scale = inv * gain
        activate(
            source,
            (scratch.xd1a, scratch.xd1b)[half],
            scratch.td1.at[2 * c * half : 2 * c * (half + 1)],
            (scratch.slope_d1a, scratch.slope_d1b)[half],
            scale,
            bias - mean * scale,
        )
        halves.append((source, mean, inv, gain))
    middle_d = scratch.middle_d
    pairs = [(scratch.xd1a, scratch.fd1a), (scratch.xd1b, scratch.fd1b)]
    mean_d2, inv_d2 = norm_of(*conv_norm(pairs, middle_d), ones16, count16)
    cot_swap.third()
    gain_d2, bias_d2 = inputs.dec_norm2_gain[...], inputs.dec_norm2_bias[...]
    a_d2 = inv_d2 * gain_d2
    activate(
        middle_d,
        scratch.xd2,
        scratch.td2,
        scratch.slope_d2,
        a_d2 * (1.0 + dec_scale),
        (bias_d2 - mean_d2 * a_d2) * (1.0 + dec_scale) + dec_shift,
    )
    result = scratch.result
    last_bias = inputs.dec_conv2_bias[...] + inputs.skip_bias[...]

    def decode(i, carry):
        value = conv_chunk([(scratch.xd2, scratch.fd2)], i)
        value = value + dot(joined[chunk_at(i), :], scratch.f_skip[...])
        result[chunk_at(i), :] = fold(value) + last_bias
        return carry

    lax.fori_loop(0, cells // CHUNK, decode, 0)
    output_here, frames_here = scratch.output_here, scratch.frames_here
    output_here[row] = result[here_rows]
    output_swap = LineSwap(
        place.line,
        lambda to: strip_of(result, to),
        lambda source: output_here.at[source],
        scratch.output_inward,
        scratch.output_across,
        make,
    )
    output_swap.first()

    exchanges = []
    waiting_runs = list(runs)
    landing_at = 0
    sem_at = 3 * (line - 1) + 20
    sums, final = scratch.sums, scratch.final

    def begin():
        nonlocal landing_at, sem_at
        start, rows = waiting_runs.pop(0)
        kind = Exchange if waiting_runs else SmallExchange
        exchange = kind(place, start, rows, landing_at, sem_at)
        landing_at += exchange.land_rows()
        sem_at += exchange.count()
        exchanges.append(exchange)
        exchange.advance()

    final_copies = []

    def advance(k):
        exchange = exchanges[k]
        exchange.advance()
        if exchange.done():
            rows = pl.ds(exchange.start, exchange.rows)
            copy = pltpu.make_async_copy(
                final.at[rows], outputs.gradients.at[rows], local_sem.at[11 + k]
            )
            copy.start()
            final_copies.append(copy)

    due = list(DUE)

    def point():
        for k in due.pop(0):
            advance(k)

    def small_row(k, value):
        sums[small_at + k : small_at + k + 1, :] = value

    def spread_grad(source):
        def step(h, carry):
            value = source[row_at(h), :]
            put_row(scratch.xg, h, value)
            return carry + tile_sums(value)

        return grid_rows(step, zeros8)

    def weight_grad(turned, at, depth, a):
        rows = pl.ds((2 - a) * width, cells)
        both = dot(turned[...], scratch.xg[rows, :])
        for half in range(depth // c):
            part = fold_rows(both[2 * c * half : 2 * c * (half + 1)])
            for b in range(3):
                high, low = HIGH_AT[2 - b] * c, LOW_AT[2 - b] * c
                to = at + (3 * a + b) * depth + half * c
                sums[to : to + c, :] = part[:, high : high + c] + part[:, low : low + c]

    def back_conv(weight, slope, target, source, mean, inv):
        carry = (zeros8, zeros8)
        for i in range(cells // CHUNK):
            value = fold(conv_chunk([(scratch.xg, weight)], i)) * slope[chunk_at(i), :]
            target[chunk_at(i), :] = value
            normed = (source[chunk_at(i), :] - mean) * inv
            carry = (carry[0] + tile_sums(value), carry[1] + tile_sums(value * normed))
            if i % (cells // CHUNK // 2) == cells // CHUNK // 2 - 1:
                point()
        return carry

    def norm_grad(sums_in, scale, ones, count):
        one, two = group_sums(sums_in[0] * scale, sums_in[1] * scale, ones)
        return one / count, two / count

    cot[here_rows] = cot_from[row]
    cot_swap.arrive()
    total_cot = column_sum(spread_grad(cot))
    for a in range(3):
        weight_grad(scratch.td2, starts.dec_conv2, c, a)
    part = fold(dot(scratch.turned[...], scratch.xg[width : cells + width, 2 * c : 4 * c]))
    sums[starts.skip_weight : starts.skip_weight + 2 * c, :] = fold_rows(part)
    small_row(3, total_cot)
    begin()

    grad = scratch.grad
    sums_d2 = back_conv(scratch.bd2, scratch.slope_d2, grad, middle_d, mean_d2, inv_d2)
    side_grads = (scratch.grad_a, scratch.grad_b)
    for half in range(2):

        def skip_back(i, carry, half=half):
            rows = pl.ds(pl.multiple_of(i * CHUNK + width, width), CHUNK)
            value = dot(scratch.xg[rows, 2 * c : 4 * c], scratch.b_skip[half])
            side_grads[half][chunk_at(i), :] = fold(value)
            return carry

        lax.fori_loop(0, cells // CHUNK, skip_back, 0)
    point()

    def table_rows(k, sums_in, gain, bias, one_plus):
        plain, times = column_sum(sums_in[0]), column_sum(sums_in[1])
        for s in range(inputs.enc_step_table.shape[0]):
            small_row(k + 2 * s, jnp.where(step_here == s, gain * times + bias * plain, 0.0))
            small_row(k + 2 * s + 1, jnp.where(step_here == s, plain, 0.0))
        return one_plus * times, one_plus * plain

    def middle_grad(source, mean, inv, scale, sums_in):
        zero, slope = norm_grad(sums_in, scale, ones16, count16)

        def step(h, carry):
            normed = (source[row_at(h), :] - mean) * inv
            value = inv * (grad[row_at(h), :] * scale - zero - normed * slope)
            put_row(scratch.xg, h, value)
            return carry

        grid_rows(step)

    gain_row, bias_row = table_rows(16, sums_d2, gain_d2, bias_d2, 1.0 + dec_scale)
    small_row(8, gain_row)
    small_row(9, bias_row)
    middle_grad(middle_d, mean_d2, inv_d2, gain_d2 * (1.0 + dec_scale), sums_d2)
    point()
    output_swap.second()
    for a in range(3):
        weight_grad(scratch.td1, starts.dec_conv1, 2 * c, a)
        point()
        begin()

    for half, (source, mean, inv, gain) in enumerate(halves):
        sums_in = back_conv(
            (scratch.bd1a, scratch.bd1b)[half],
            (scratch.slope_d1a, scratch.slope_d1b)[half],
            grad,
            source,
            mean,
            inv,
        )
        small_row(4 + half, column_sum(sums_in[1]))
        small_row(6 + half, column_sum(sums_in[0]))
        zero, slope = norm_grad(sums_in, gain, ones32, count32)
        target = side_grads[half]

        def input_grad(h, carry):
            normed = (source[row_at(h), :] - mean) * inv
            value = inv * (grad[row_at(h), :] * gain - zero - normed * slope)
            value = target[row_at(h), :] + value
            target[row_at(h), :] = value
            return carry + tile_sums(value)

        total = grid_rows(input_grad, zeros8)
        if half == 0:
            small_row(2, column_sum(total))
        point()

    output_swap.third()
    grad_raised, grad_encoded = side_grads
    x_grad_up = scratch.x_grad_up
    for k, piece in enumerate(pick(grad_raised)):
        high, low = split(piece)
        x_grad_up[:, k * c : (k + 1) * c] = high
        x_grad_up[:, (k + 4) * c : (k + 5) * c] = low
    grad_lowered = fold(dot(x_grad_up[...], scratch.b_up[...]))
    small_row(1, jnp.sum(grad_lowered, axis=0, keepdims=True))
    x_grad_low = scratch.x_grad_low
    high, low = split(grad_lowered)
    x_grad_low[:, 0:c] = high
    x_grad_low[:, c : 2 * c] = low
    point()
    part = fold(fold_rows(dot(x_up[...], x_grad_up[...], TN)))
    for k in range(4):
        at = starts.up_weight + k * c
        sums[at : at + c, :] = part[:, k * c : (k + 1) * c]
    part = fold_rows(fold(dot(x_down[...], x_grad_low[...], TN)))
    sums[starts.reducer_weight : starts.reducer_weight + 4 * c, :] = part
    point()
    begin()
    place_cells(
        grad, [fold(dot(x_grad_low[...], scratch.b_down[k])) for k in range(4)]
    )

    def join_row(h, carry):
        value = grad_encoded[row_at(h), :] + grad[row_at(h), :]
        grad_encoded[row_at(h), :] = value
        put_row(scratch.xg, h, value)
        return carry + tile_sums(value)

    small_row(0, column_sum(grid_rows(join_row, zeros8)))
    for k in range(10, 16):
        small_row(k, jnp.zeros((1, c), F32))
    sums[small_at + 24 : small_at + LATE, :] = jnp.zeros((LATE - 24, c), F32)
    point()
    for a in range(3):
        weight_grad(scratch.te2, starts.enc_conv2, c, a)
        point()
    begin()
    sums_e2 = back_conv(scratch.be2, scratch.slope_e2, grad, middle_e, mean_e2, inv_e2)
    gain_row, bias_row = table_rows(LATE + 24, sums_e2, gain_e2, bias_e2, 1.0 + enc_scale)
    small_row(LATE + 18, gain_row)
    small_row(LATE + 19, bias_row)
    middle_grad(middle_e, mean_e2, inv_e2, gain_e2 * (1.0 + enc_scale), sums_e2)
    point()
    for a in range(3):
        weight_grad(scratch.te1, starts.enc_conv1, c, a)
        point()
        if a:
            begin()
    sums_e1 = back_conv(scratch.be1, scratch.slope_e1, grad, lifted, mean_e1, inv_e1)
    small_row(LATE + 16, column_sum(sums_e1[1]))
    small_row(LATE + 17, column_sum(sums_e1[0]))
    zero, slope = norm_grad(sums_e1, gain_e1, ones16, count16)

    def lifted_grad(h, carry):
        normed = (lifted[row_at(h), :] - mean_e1) * inv_e1
        value = inv_e1 * (grad[row_at(h), :] * gain_e1 - zero - normed * slope)
        grad[row_at(h), :] = grad_encoded[row_at(h), :] + value
        return carry

    grid_rows(lifted_grad)
    point()

    late_at = small_at + LATE
    sums[late_at : late_at + 16, :] = dot_three(fields[...], grad[...])
    sums[late_at + 20 : late_at + 24, :] = jnp.zeros((4, c), F32)
    point()
    begin()
    back = dot_three(lift[...], grad[...], NT)
    frames_out = scratch.frames_out
    for source in range(line):
        for k in range(strip):
            h = source * strip + k
            value = back[0:history, h * width : (h + 1) * width]
            frames_out[source, :, k, :] = value * keep * masks[h]
    frames_here[row] = frames_out[row]
    for k in range(1, line):
        to = lax.rem(row + k, line)
        output_copies.append(
            send(frames_out.at[to], frames_here.at[row], device_at(to))
        )

    output_swap.arrive()
    own_output = pltpu.make_async_copy(output_here, outputs.output, local_sem.at[10])
    own_output.start()
    for k in REST:
        advance(k)
    assert not due and all(exchange.done() for exchange in exchanges)

    for copy in output_copies:
        copy.wait_recv()
    own_frames = pltpu.make_async_copy(
        frames_here, outputs.frames_grad, local_sem.at[11 + len(runs)]
    )
    own_frames.start()
    own_output.wait()
    own_frames.wait()
    for copy in final_copies:
        copy.wait()
    for copy in frame_copies + output_copies:
        copy.wait_send()
    cot_swap.sent()
    output_swap.sent()
    for exchange in exchanges:
        for copy, only in exchange.copies:
            if only is None:
                copy.wait_send()
            else:
                pl.when(only)(copy.wait_send)


def write_kernel(layout, *refs):
    shapes, starts, small_at = layout
    output, frames_grad, gradients = refs[:3]
    outputs = refs[3:-4]
    output_here, frames_here, gradients_here, sem = refs[-4:]
    c = gradients.shape[1]
    moves = [(frames_grad, frames_here, outputs[1])]
    for k, name in enumerate(LARGE):
        rows = pl.ds(starts[name], shapes[name][0])
        moves.append((gradients.at[rows], gradients_here.at[rows], outputs[2 + k]))
    moves.append((output, output_here, outputs[0]))
    small = pl.ds(small_at, SMALL_COUNT)
    first = pltpu.make_async_copy(gradients.at[small], gradients_here.at[small], sem.at[0])
    first.start()
    arriving, leaving = [], []
    for k, (source, here, _) in enumerate(moves):
        arriving.append(pltpu.make_async_copy(source, here, sem.at[1 + 2 * k]))
        arriving[-1].start()
    first.wait()
    for target, (k, rows) in zip(outputs[2 + len(LARGE) :], SMALL_ROWS.values()):
        at = small_at + k
        if rows == 8:
            for s in range(target.shape[0]):
                target[s : s + 1, 0:c] = gradients_here[at + 2 * s : at + 2 * s + 1, :]
                target[s : s + 1, c : 2 * c] = gradients_here[at + 2 * s + 1 : at + 2 * s + 2, :]
        else:
            target[...] = gradients_here[at : at + rows, :]
    for k, (_, here, target) in enumerate(moves):
        arriving[k].wait()
        leaving.append(pltpu.make_async_copy(here, target, sem.at[2 + 2 * k]))
        leaving[-1].start()
    for copy in leaving:
        copy.wait()


def whole_items(shape, *arguments):
    line = shape["rows"]
    whole = Given(*arguments)
    given = whole._asdict()
    frames, cotangent = whole.frames, whole.cotangent
    items, history, strip, width = frames.shape
    c = cotangent.shape[-1]
    cells = strip * line * width
    flat = {}
    for name, value in given.items():
        if value is cotangent:
            value = value.reshape(items, strip * width, c)
        elif name in LARGE:
            value = value.reshape(-1, c)
        elif value.ndim == 1 and name not in IN_SMEM:
            value = value.reshape(-1, c)
        flat[name] = value
    shapes = {name: flat[name].shape for name in LARGE}
    big_layout = layout_of(SimpleNamespace(**shapes))
    starts, small_at, total_rows, runs = big_layout
    copies = 20 + 3 * (line - 1) + len(runs) * (8 + 2 * (line - 1)) + 6
    landing = sum(rows // 2 + 5 * rows // 8 for _, rows in runs) + LATE_COUNT * (8 + line)
    shifted = pltpu.VMEM((cells + 2 * width, 6 * c), BF16)
    forward = pltpu.VMEM((18 * c, 2 * c), BF16)
    backward = forward
    field = pltpu.VMEM((cells, c), F32)
    flipped_field = pltpu.VMEM((2 * c, cells), BF16)
    quarter = cells // 4
    scratch = dict(
        small=pltpu.VMEM((LATE_COUNT, c), F32),
        send=pltpu.SemaphoreType.DMA((copies,)),
        recv=pltpu.SemaphoreType.DMA((copies,)),
        local=pltpu.SemaphoreType.DMA((12 + len(runs),)),
        sums=pltpu.VMEM((total_rows, c), F32),
        final=pltpu.VMEM((total_rows, c), F32),
        landing=pltpu.VMEM((landing, c), F32),
        frames_in=pltpu.VMEM((line, history, strip, width), F32),
        mask_in=pltpu.VMEM((line, strip, width), jnp.int32),
        frames_out=pltpu.VMEM((line, history, strip, width), F32),
        frames_from=pltpu.VMEM((line, history, strip, width), F32),
        frames_here=pltpu.VMEM((line, history, strip, width), F32),
        mask_from=pltpu.VMEM((line, strip, width), jnp.int32),
        cot_from=pltpu.VMEM((items, strip * width, c), F32),
        output_here=pltpu.VMEM((items, strip * width, c), F32),
        cot_inward=pltpu.VMEM((2, strip * width, c), F32),
        cot_across=pltpu.VMEM((2, strip * width, c), F32),
        output_inward=pltpu.VMEM((2, strip * width, c), F32),
        output_across=pltpu.VMEM((2, strip * width, c), F32),
        fields=pltpu.VMEM((16, cells), F32),
        lift=pltpu.VMEM((16, c), F32),
        joined=pltpu.VMEM((cells, 4 * c), BF16),
        x_down=pltpu.VMEM((quarter, 8 * c), BF16),
        x_grad_up=pltpu.VMEM((quarter, 8 * c), BF16),
        x_up=pltpu.VMEM((quarter, 2 * c), BF16),
        x_grad_low=pltpu.VMEM((quarter, 2 * c), BF16),
        f_down=pltpu.VMEM((8 * c, 2 * c), BF16),
        b_down=pltpu.VMEM((4, 2 * c, 2 * c), BF16),
        f_up=pltpu.VMEM((4, 2 * c, 2 * c), BF16),
        b_up=pltpu.VMEM((8 * c, 2 * c), BF16),
        f_skip=pltpu.VMEM((4 * c, 2 * c), BF16),
        b_skip=pltpu.VMEM((2, 2 * c, 2 * c), BF16),
        xe1=shifted,
        xe2=shifted,
        xd1a=shifted,
        xd1b=shifted,
        xd2=shifted,
        xg=shifted,
        te1=flipped_field,
        te2=flipped_field,
        td1=pltpu.VMEM((4 * c, cells), BF16),
        td2=flipped_field,
        turned=pltpu.VMEM((4 * c, cells), BF16),
        fe1=forward,
        fe2=forward,
        fd1a=forward,
        fd1b=forward,
        fd2=forward,
        be1=backward,
        be2=backward,
        bd1a=backward,
        bd1b=backward,
        bd2=backward,
        slope_e1=field,
        slope_e2=field,
        slope_d1a=field,
        slope_d1b=field,
        slope_d2=field,
        lifted=field,
        middle_e=field,
        encoded=field,
        raised=field,
        middle_d=field,
        result=field,
        cot=field,
        grad=field,
        grad_a=field,
        grad_b=field,
    )
    scratch.update({name: pltpu.VMEM(shapes[name], F32) for name in LARGE})

    in_hbm = pl.BlockSpec(memory_space=pl.ANY)
    in_vmem = pl.BlockSpec(memory_space=pltpu.VMEM)
    in_smem = pl.BlockSpec(memory_space=pltpu.SMEM)
    in_specs = [
        in_hbm if name in IN_HBM else in_smem if name in IN_SMEM else in_vmem
        for name in ARGUMENTS
    ]
    out_shape = [
        jax.ShapeDtypeStruct((items, strip * width, c), F32),
        jax.ShapeDtypeStruct(frames.shape, F32),
        jax.ShapeDtypeStruct((total_rows, c), F32),
    ]
    out_specs = [in_hbm] * 3
    results = pl.pallas_call(
        functools.partial(
            item_kernel,
            (line, strip, width, shapes, big_layout),
            tuple(scratch),
        ),
        out_shape=out_shape,
        in_specs=in_specs,
        out_specs=out_specs,
        scratch_shapes=list(scratch.values()),
        compiler_params=pltpu.CompilerParams(
            collective_id=0, has_side_effects=True, vmem_limit_bytes=62 * 1024 * 1024
        ),
    )(*[flat[name] for name in ARGUMENTS])
    names = LARGE + tuple(SMALL_ROWS)
    written = pl.pallas_call(
        functools.partial(write_kernel, (shapes, starts, small_at)),
        out_shape=out_shape[:2] + [jax.ShapeDtypeStruct(flat[name].shape, F32) for name in names],
        in_specs=[pl.BlockSpec(memory_space=pltpu.HBM)] * 3,
        out_specs=[in_hbm] * (2 + len(LARGE)) + [in_vmem] * len(SMALL_ROWS),
        scratch_shapes=[
            pltpu.VMEM((items, strip * width, c), F32),
            pltpu.VMEM(frames.shape, F32),
            pltpu.VMEM((total_rows, c), F32),
            pltpu.SemaphoreType.DMA((1 + 2 * (2 + len(LARGE)),)),
        ],
        compiler_params=pltpu.CompilerParams(vmem_limit_bytes=60 * 1024 * 1024),
    )(*results)
    grads = dict(zip(names, written[2:]))
    ordered = [name for name in ARGUMENTS if name in grads]
    return (written[0].reshape(cotangent.shape), written[1]) + tuple(
        grads[name].reshape(given[name].shape) for name in ordered
    )


def body(shape, *arguments):
    items, _, strip, width = arguments[0].shape
    line = shape["rows"]
    whole = (
        shape["section"] == 2
        and shape["batch"] == 4
        and items == line == 4
        and arguments[-1].shape[-1] == 128
        and (strip * line * width) % CHUNK == 0
    )
    return whole_items(shape, *arguments) if whole else strips_body(*arguments)


def solution(mesh):
    in_specs = (
        P(("section", "batch"), None, "rows", None),
        P(("section", "batch")),
        P(("section", "batch"), "rows", None),
        P(("section", "batch")),
        P(),
        P(),
        P(),
        P(),
        P(),
        P(),
        P(),
        P(),
        P(),
        P(),
        P(),
        P(),
        P(),
        P(),
        P(),
        P(),
        P(),
        P(),
        P(),
        P(),
        P(),
        P(),
        P(),
        P(),
        P(("section", "batch"), "rows", None, None),
    )
    out_specs = (
        P(("section", "batch"), "rows", None, None),
        P(("section", "batch"), None, "rows", None),
        P(),
        P(),
        P(),
        P(),
        P(),
        P(),
        P(),
        P(),
        P(),
        P(),
        P(),
        P(),
        P(),
        P(),
        P(),
        P(),
        P(),
        P(),
        P(),
        P(),
        P(),
        P(),
        P(),
        P(),
    )
    return jax.shard_map(functools.partial(body, mesh.shape), mesh=mesh, in_specs=in_specs, out_specs=out_specs, check_vma=False)
```

```python
import functools
from types import SimpleNamespace
from typing import Any, NamedTuple

import jax
import jax.numpy as jnp
from jax import lax
from jax.experimental import pallas as pl
from jax.experimental.pallas import tpu as pltpu
from jax.sharding import PartitionSpec as P

GROUPS = 8
FIELDS = 3
HIST = 4


EPS = 1e-05
HIGH = lax.Precision.HIGHEST


def extended(cells, sides, width):
    for axis, dim in sides:
        count = lax.axis_size(axis)
        ends = count - 1
        head = lax.slice_in_dim(cells, 0, width, axis=dim)
        tail = lax.slice_in_dim(cells, cells.shape[dim] - width, cells.shape[dim], axis=dim)
        cells = jnp.concatenate(
            [
                lax.ppermute(tail, axis, [(i, (i + 1) % count) for i in range(ends)]),
                cells,
                lax.ppermute(head, axis, [((i + 1) % count, i) for i in range(ends)]),
            ],
            axis=dim,
        )
    return cells


def from_behind(value, axis, steps):
    count = lax.axis_size(axis)
    pairs = [(source, (source + steps) % count) for source in range(count)]
    return lax.ppermute(value, axis, pairs)


def group_view(value_arrays):
    extent = value_arrays.shape
    return value_arrays.reshape(extent[:-1] + (GROUPS, extent[-1] // GROUPS))


def global_sums(value_arrays):
    grouped = group_view(value_arrays)
    flat = grouped.reshape(-1, GROUPS, grouped.shape[-1])
    first_sum = jnp.sum(flat, axis=(0, 2))
    second_sum = jnp.sum(flat * flat, axis=(0, 2))
    return lax.psum((first_sum, second_sum), "rows")


def apply_norm(value_arrays, sum_one, sum_two, norm_gain, norm_bias, total):
    grouped = group_view(value_arrays)
    group_mean = sum_one / total
    variance = sum_two / total - group_mean * group_mean
    inverse = lax.rsqrt(variance + EPS)
    normed = (grouped - group_mean[:, None]) * inverse[:, None]
    return normed.reshape(value_arrays.shape) * norm_gain + norm_bias


def norm_back(value_arrays, grad_one, grad_two):
    grouped = group_view(value_arrays)
    extra = grad_one[:, None] + 2.0 * grouped * grad_two[:, None]
    return extra.reshape(value_arrays.shape)


def reduce_grads(grad_one, grad_two):
    return lax.psum((grad_one, grad_two), "rows")


def conv_rows(padded, kernel):
    widened = jnp.pad(padded, ((0, 0), (1, 1), (0, 0)))
    return lax.conv_general_dilated(
        widened[None],
        kernel,
        (1, 1),
        "VALID",
        dimension_numbers=("NHWC", "HWIO", "NHWC"),
        precision=HIGH,
    )[0]


def flipped(kernel):
    return jnp.transpose(kernel[::-1, ::-1], (0, 1, 3, 2))


def pad_grads(value_arrays):
    return extended(value_arrays, (("rows", 0),), 1)


def totals_of(inputs, conv1):
    strip = inputs.shape[0]
    cells = strip * lax.axis_size("rows") * inputs.shape[1]
    return (cells * (inputs.shape[2] // GROUPS), cells * (conv1.shape[3] // GROUPS))


def block_forward(inputs, weights, scale_part, shift_part):
    norm1_gain, norm1_bias, conv1, norm2_gain, norm2_bias, conv2, conv2_bias = weights
    total_in, total_mid = totals_of(inputs, conv1)
    sums_in = global_sums(inputs)

    def pad_rows(value_arrays):
        return extended(value_arrays, (("rows", 0),), 1)

    act_one = pad_rows(
        jax.nn.gelu(
            apply_norm(inputs, sums_in[0], sums_in[1], norm1_gain, norm1_bias, total_in),
            approximate=False,
        )
    )
    middle = conv_rows(act_one, conv1)
    sums_mid = global_sums(middle)
    shaped = (
        apply_norm(middle, sums_mid[0], sums_mid[1], norm2_gain, norm2_bias, total_mid)
        * (1.0 + scale_part)
        + shift_part
    )
    act_two = pad_rows(jax.nn.gelu(shaped, approximate=False))
    branch = conv_rows(act_two, conv2) + conv2_bias
    return (branch, (sums_in[0], sums_in[1], act_one, middle, sums_mid[0], sums_mid[1], act_two))


def block_backward(inputs, weights, scale_part, shift_part, kept, grad_out):
    norm1_gain, norm1_bias, conv1, norm2_gain, norm2_bias, conv2, conv2_bias = weights
    in_one, in_two, act_one, middle, mid_one, mid_two, act_two = kept
    total_in, total_mid = totals_of(inputs, conv1)
    grad_conv2 = jax.vjp(lambda kernel: conv_rows(act_two, kernel), conv2)[1](grad_out)[0]
    grad_bias2 = jnp.sum(grad_out, axis=(0, 1))
    grad_act_two = conv_rows(pad_grads(grad_out), flipped(conv2))

    def second_piece(middle_in, sum_one, sum_two, gain_in, incoming_bias, scale_in, shift_in):
        shaped = (
            apply_norm(middle_in, sum_one, sum_two, gain_in, incoming_bias, total_mid)
            * (1.0 + scale_in)
            + shift_in
        )
        return jax.nn.gelu(shaped, approximate=False)

    second_pull = jax.vjp(
        second_piece, middle, mid_one, mid_two, norm2_gain, norm2_bias, scale_part, shift_part
    )[1](grad_act_two)
    summed_one, summed_two = reduce_grads(second_pull[1], second_pull[2])
    grad_middle = second_pull[0] + norm_back(middle, summed_one, summed_two)
    grad_conv1 = jax.vjp(lambda kernel: conv_rows(act_one, kernel), conv1)[1](grad_middle)[0]
    grad_act_one = conv_rows(pad_grads(grad_middle), flipped(conv1))

    def first_piece(inputs_in, sum_one, sum_two, gain_in, incoming_bias):
        return jax.nn.gelu(
            apply_norm(inputs_in, sum_one, sum_two, gain_in, incoming_bias, total_in),
            approximate=False,
        )

    first_pull = jax.vjp(first_piece, inputs, in_one, in_two, norm1_gain, norm1_bias)[1](
        grad_act_one
    )
    first_one, first_two = reduce_grads(first_pull[1], first_pull[2])
    grad_inputs = first_pull[0] + norm_back(inputs, first_one, first_two)
    grads = (
        first_pull[3],
        first_pull[4],
        grad_conv1,
        second_pull[3],
        second_pull[4],
        grad_conv2,
        grad_bias2,
    )
    return (grad_inputs, grads, second_pull[5], second_pull[6])


def conditioning(step_item, table):
    one_hot = (jnp.arange(table.shape[0], dtype=jnp.int32) == step_item).astype(jnp.float32)
    condition = jnp.dot(one_hot, table, precision=HIGH)
    half_width = table.shape[1] // 2
    return (condition[:half_width], condition[half_width:], one_hot)


def project_in(frames_item, mask_item, count_item, incoming_weight, incoming_bias):
    history = jnp.arange(HIST, dtype=jnp.int32) >= HIST - count_item
    keep = jnp.repeat(history, FIELDS).astype(jnp.float32)
    lifted = (
        jnp.einsum(
            "fhw,fc->hwc", frames_item * keep[:, None, None], incoming_weight, precision=HIGH
        )
        + incoming_bias
    )
    return lifted * mask_item[:, :, None].astype(jnp.float32)


def coarsen_field(value_arrays, incoming_weight, incoming_bias):
    rows_here, width_here, depth_here = value_arrays.shape
    blocks = value_arrays.reshape(rows_here // 2, 2, width_here // 2, 2, depth_here)
    return jnp.einsum("iajbk,abkc->ijc", blocks, incoming_weight, precision=HIGH) + incoming_bias


def upsample(value_arrays, incoming_weight, incoming_bias):
    result = jnp.einsum("ijk,abkc->iajbc", value_arrays, incoming_weight, precision=HIGH)
    extent = result.shape
    return result.reshape(extent[0] * 2, extent[2] * 2, extent[4]) + incoming_bias


def flatten_all(pieces):
    return jnp.concatenate([piece.reshape(-1) for piece in pieces])


def unflatten_all(flat, templates):
    pieces = []
    offset_at = 0
    for template in templates:
        count_here = template.size
        pieces.append(flat[offset_at : offset_at + count_here].reshape(template.shape))
        offset_at += count_here
    return tuple(pieces)


def strips_body(
    frames,
    counts,
    cell_mask,
    step_index,
    lift_weight,
    lift_bias,
    enc_norm1_gain,
    enc_norm1_bias,
    enc_conv1,
    enc_step_table,
    enc_norm2_gain,
    enc_norm2_bias,
    enc_conv2,
    enc_conv2_bias,
    reducer_weight,
    reducer_bias,
    up_weight,
    up_bias,
    dec_norm1_gain,
    dec_norm1_bias,
    dec_conv1,
    dec_step_table,
    dec_norm2_gain,
    dec_norm2_bias,
    dec_conv2,
    dec_conv2_bias,
    skip_weight,
    skip_bias,
    cotangent,
):
    enc_weights = (
        enc_norm1_gain,
        enc_norm1_bias,
        enc_conv1,
        enc_norm2_gain,
        enc_norm2_bias,
        enc_conv2,
        enc_conv2_bias,
    )
    dec_weights = (
        dec_norm1_gain,
        dec_norm1_bias,
        dec_conv1,
        dec_norm2_gain,
        dec_norm2_bias,
        dec_conv2,
        dec_conv2_bias,
    )
    params = (
        lift_weight,
        lift_bias,
        enc_norm1_gain,
        enc_norm1_bias,
        enc_conv1,
        enc_step_table,
        enc_norm2_gain,
        enc_norm2_bias,
        enc_conv2,
        enc_conv2_bias,
        reducer_weight,
        reducer_bias,
        up_weight,
        up_bias,
        dec_norm1_gain,
        dec_norm1_bias,
        dec_conv1,
        dec_step_table,
        dec_norm2_gain,
        dec_norm2_bias,
        dec_conv2,
        dec_conv2_bias,
        skip_weight,
        skip_bias,
    )

    def forward_micro(carry, sliced):
        frames_item, mask_item, count_item, step_item = sliced
        lifted = project_in(frames_item, mask_item, count_item, lift_weight, lift_bias)
        enc_scale, enc_shift, unused_hot = conditioning(step_item, enc_step_table)
        enc_branch, enc_kept = block_forward(lifted, enc_weights, enc_scale, enc_shift)
        encoder_result = lifted + enc_branch
        coarse_field = coarsen_field(encoder_result, reducer_weight, reducer_bias)
        foreign = from_behind(coarse_field, "section", 1)
        raised_foreign = upsample(foreign, up_weight, up_bias)
        raised = from_behind(raised_foreign, "section", 1)
        joined = jnp.concatenate([raised, encoder_result], axis=-1)
        dec_scale, dec_shift, unused_again = conditioning(step_item, dec_step_table)
        dec_branch, dec_kept = block_forward(joined, dec_weights, dec_scale, dec_shift)
        output_item = jnp.dot(joined, skip_weight, precision=HIGH) + skip_bias + dec_branch
        return (carry, (output_item, (lifted, enc_kept, encoder_result, foreign, joined, dec_kept)))

    unused, (output, kept_all) = lax.scan(
        forward_micro, jnp.zeros((), jnp.float32), (frames, cell_mask, counts, step_index)
    )

    def backward_micro(totals, sliced):
        frames_item, mask_item, count_item, step_item, grad_out, kept = sliced
        lifted, enc_kept, encoder_result, foreign, joined, dec_kept = kept
        dec_scale, dec_shift, one_hot = conditioning(step_item, dec_step_table)
        grad_joined, dec_grads, dec_gscale, dec_gshift = block_backward(
            joined, dec_weights, dec_scale, dec_shift, dec_kept, grad_out
        )
        grad_skip_weight = jnp.einsum("hwk,hwc->kc", joined, grad_out, precision=HIGH)
        grad_skip_bias = jnp.sum(grad_out, axis=(0, 1))
        grad_joined = grad_joined + jnp.dot(grad_out, skip_weight.T, precision=HIGH)
        half_width = joined.shape[-1] // 2
        grad_raised = grad_joined[..., :half_width]
        grad_encoded = grad_joined[..., half_width:]
        grad_foreign_up = from_behind(grad_raised, "section", 1)
        up_pull = jax.vjp(upsample, foreign, up_weight, up_bias)[1](grad_foreign_up)
        coarse_gradient = from_behind(up_pull[0], "section", 1)
        reducer_pullback = jax.vjp(coarsen_field, encoder_result, reducer_weight, reducer_bias)[1](
            coarse_gradient
        )
        grad_encoded = grad_encoded + reducer_pullback[0]
        enc_scale, enc_shift, enc_hot = conditioning(step_item, enc_step_table)
        grad_lifted, enc_grads, enc_gscale, enc_gshift = block_backward(
            lifted, enc_weights, enc_scale, enc_shift, enc_kept, grad_encoded
        )
        grad_lifted = grad_lifted + grad_encoded
        proj_pull = jax.vjp(
            lambda frames_in, incoming_weight, incoming_bias: project_in(
                frames_in, mask_item, count_item, incoming_weight, incoming_bias
            ),
            frames_item,
            lift_weight,
            lift_bias,
        )[1](grad_lifted)
        enc_table_grad = enc_hot[:, None] * jnp.concatenate([enc_gscale, enc_gshift])[None, :]
        dec_table_grad = one_hot[:, None] * jnp.concatenate([dec_gscale, dec_gshift])[None, :]
        micro_list = (
            proj_pull[1],
            proj_pull[2],
            enc_grads[0],
            enc_grads[1],
            enc_grads[2],
            enc_table_grad,
            enc_grads[3],
            enc_grads[4],
            enc_grads[5],
            enc_grads[6],
            reducer_pullback[1],
            reducer_pullback[2],
            up_pull[1],
            up_pull[2],
            dec_grads[0],
            dec_grads[1],
            dec_grads[2],
            dec_table_grad,
            dec_grads[3],
            dec_grads[4],
            dec_grads[5],
            dec_grads[6],
            grad_skip_weight,
            grad_skip_bias,
        )
        micro_flat = flatten_all(micro_list)
        return (totals + micro_flat, proj_pull[0])

    total_size = sum((piece.size for piece in params))
    start_totals = jnp.zeros((total_size,), jnp.float32)
    flat_totals, frames_grad = lax.scan(
        backward_micro,
        start_totals,
        (frames, cell_mask, counts, step_index, cotangent, kept_all),
        reverse=True,
    )
    flat_totals = lax.psum(flat_totals, ("section", "batch", "rows"))
    grads = unflatten_all(flat_totals, params)
    return (output, frames_grad) + grads


F32 = jnp.float32
BF16 = jnp.bfloat16
MESH = pl.DeviceIdType.MESH
NN = ((1,), (0,))
NT = ((1,), (1,))
TN = ((0,), (0,))
HIGH_AT = (0, 2, 1)
LOW_AT = (4, 3, 5)
CHUNK = 1024
class Given(NamedTuple):
    frames: Any
    counts: Any
    cell_mask: Any
    step_index: Any
    lift_weight: Any
    lift_bias: Any
    enc_norm1_gain: Any
    enc_norm1_bias: Any
    enc_conv1: Any
    enc_step_table: Any
    enc_norm2_gain: Any
    enc_norm2_bias: Any
    enc_conv2: Any
    enc_conv2_bias: Any
    reducer_weight: Any
    reducer_bias: Any
    up_weight: Any
    up_bias: Any
    dec_norm1_gain: Any
    dec_norm1_bias: Any
    dec_conv1: Any
    dec_step_table: Any
    dec_norm2_gain: Any
    dec_norm2_bias: Any
    dec_conv2: Any
    dec_conv2_bias: Any
    skip_weight: Any
    skip_bias: Any
    cotangent: Any


ARGUMENTS = Given._fields
LARGE = tuple(
    dict(
        dec_conv1=0,
        up_weight=0,
        reducer_weight=0,
        dec_conv2=0,
        skip_weight=0,
        enc_conv1=0,
        enc_conv2=0,
    )
)
IN_HBM = tuple(dict(frames=0, cell_mask=0, cotangent=0)) + LARGE
IN_SMEM = tuple(dict(counts=0, step_index=0))
LATE = 64
SMALL_ROWS = dict(
    enc_conv2_bias=(0, 1),
    reducer_bias=(1, 1),
    up_bias=(2, 1),
    dec_conv2_bias=(3, 1),
    skip_bias=(3, 1),
    dec_norm1_gain=(4, 2),
    dec_norm1_bias=(6, 2),
    dec_norm2_gain=(8, 1),
    dec_norm2_bias=(9, 1),
    dec_step_table=(16, 8),
    lift_weight=(LATE, 12),
    lift_bias=(LATE + 12, 1),
    enc_norm1_gain=(LATE + 16, 1),
    enc_norm1_bias=(LATE + 17, 1),
    enc_norm2_gain=(LATE + 18, 1),
    enc_norm2_bias=(LATE + 19, 1),
    enc_step_table=(LATE + 24, 8),
)
LATE_COUNT = 32
SMALL_COUNT = LATE + LATE_COUNT
DUE = ((), (), (), (), (), (0,), (), (1,), (), (), (2,), (3, 0), (), (), (1,), (), (), (2,), (0,), (1, 4, 3), (2,), (), (), (5, 0), (1, 3), (4, 2), (), (6,), (7, 3, 0, 5, 4, 1, 2))
REST = (6, 3, 7, 4, 5, 6, 8, 7, 0, 4, 5, 1, 6, 7, 2, 0, 1, 5, 3, 6, 2, 8, 7, 3, 4, 5, 4, 6, 7, 5, 6, 7)
OUTPUTS = tuple(dict(output=0, frames_grad=0, gradients=0))


def split(value):
    high = value.astype(BF16)
    return high, (value - high.astype(F32)).astype(BF16)


def dot(left, right, dims=NN, precision=None):
    return lax.dot_general(
        left, right, (dims, ((), ())), precision=precision, preferred_element_type=F32
    )


def fold(value):
    half = value.shape[1] // 2
    return value[:, :half] + value[:, half:]


def fold_rows(value):
    half = value.shape[0] // 2
    return value[:half] + value[half:]


def tile_sums(value):
    return jnp.sum(value.reshape(-1, 8, value.shape[-1]), axis=0)


def column_sum(tiles):
    return jnp.sum(tiles, axis=0, keepdims=True)


def normal(value):
    bell = jnp.exp(-0.5 * value * value)
    t = 1.0 / (1.0 + 0.2316418882663604 * jnp.abs(value))
    poly = 0.5307027145
    for factor in (-0.7265760135, 0.7107068705, -0.142248368, 0.127414796):
        poly = poly * t + factor
    tail = poly * t * bell
    return jnp.where(value < 0.0, tail, 1.0 - tail), 0.3989422804014327 * bell


def dot_three(left, right, dims=NN):
    left_high, left_low = split(left)
    right_high, right_low = split(right)
    total = dot(left_high, right_high, dims)
    return total + (dot(left_high, right_low, dims) + dot(left_low, right_high, dims))


def group_ones(channels, size):
    rows = lax.broadcasted_iota(jnp.int32, (channels, channels), 0) // size
    columns = lax.broadcasted_iota(jnp.int32, (channels, channels), 1) // size
    return (rows == columns).astype(BF16)


def group_sums(first, second, ones):
    terms = []
    rest = jnp.concatenate([first, second], axis=0)
    for _ in range(3):
        term = rest.astype(BF16)
        terms.append(term)
        rest = rest - term.astype(F32)
    both = dot(jnp.concatenate(terms, axis=0), ones)
    both = both[32:48] + both[16:32] + both[:16]
    return column_sum(both[:8]), column_sum(both[8:])


class LineSwap:

    def __init__(self, line, source, target, inward, across, make):
        far = 3 - line.outer
        self.line = line
        to_inner, to_across = line.device(line.inner), line.device(line.across)
        to_outer = line.device(line.outer)
        here = target(line.here)
        self.to_far = make(source(3 - line.here), inward.at[1], to_inner)
        self.to_second = make(source(3 - line.inner), inward.at[0], to_inner)
        self.to_inner = make(source(line.inner), here, to_inner)
        self.for_far = make(source(far), across.at[0], to_across)
        self.to_across = make(source(line.across), here, to_across)
        self.to_outer = make(source(line.outer), here, to_outer)
        self.pass_far = make(inward.at[1], across.at[1], to_across)
        self.pass_second = make(inward.at[0], target(line.outer), to_across)
        self.pass_across = make(across.at[0], target(line.across), to_outer)
        self.pass_opposite = make(across.at[1], target(far), to_outer)

    def first(self):
        @pl.when(self.line.edge)
        def _():
            for copy in (self.to_far, self.to_second, self.to_inner):
                copy.start()

        @pl.when(self.line.middle)
        def _():
            for copy in (self.for_far, self.to_across, self.to_outer):
                copy.start()

    def second(self):
        @pl.when(self.line.middle)
        def _():
            self.for_far.wait_recv()
            self.pass_across.start()
            self.to_far.wait_recv()
            self.pass_far.start()
            self.to_second.wait_recv()
            self.pass_second.start()

    def third(self):
        @pl.when(self.line.middle)
        def _():
            self.pass_far.wait_recv()
            self.pass_opposite.start()

    def arrive(self):
        @pl.when(self.line.edge)
        def _():
            for copy in (self.to_outer, self.pass_across, self.pass_opposite):
                copy.wait_recv()

        @pl.when(self.line.middle)
        def _():
            for copy in (self.to_inner, self.to_across, self.pass_second):
                copy.wait_recv()

    def sent(self):
        @pl.when(self.line.edge)
        def _():
            for copy in (self.to_far, self.to_second, self.to_inner):
                copy.wait_send()

        @pl.when(self.line.middle)
        def _():
            for copy in (self.for_far, self.to_across, self.to_outer):
                copy.wait_send()
            for copy in (self.pass_far, self.pass_second, self.pass_across, self.pass_opposite):
                copy.wait_send()


class Exchange:

    def __init__(self, place, start, rows, landing, first_sem):
        self.place, self.start, self.rows, self.landing = place, start, rows, landing
        self.sem = first_sem
        self.stage = 0
        self.copies = []
        self.waiting = []
        self.group = place.plane_group
        self.half = rows // 2
        self.base = start + place.core * self.half
        self._finish(self.half)

    def _finish(self, size):
        self.part = size // self.group.count
        self.own = self.base + self.group.here * self.part

    def count(self):
        return 2 + 2 * (self.group.count - 1) + 3

    def land_rows(self):
        return self.half + (self.group.count + 1) * self.part

    def _copy(self, source, target, device, only=None):
        place = self.place
        copy = pltpu.make_async_remote_copy(
            src_ref=source,
            dst_ref=target,
            send_sem=place.send.at[self.sem],
            recv_sem=place.recv.at[self.sem],
            device_id=device,
            device_id_type=MESH,
        )
        self.sem += 1
        if only is None:
            copy.start()
            self.waiting.append(copy)
        self.copies.append((copy, only))
        return copy

    def _wait(self):
        for copy in self.waiting:
            copy.wait_recv()
        self.waiting = []

    def _rows(self, at, size):
        return pl.ds(pl.multiple_of(at, 8), size)

    def _swap(self):
        place = self.place
        other = self._rows(self.start + (1 - place.core) * self.half, self.half)
        self.land = self.landing
        self.landing += self.half
        self._copy(
            place.sums.at[other], place.landing.at[pl.ds(self.land, self.half)], place.partner
        )

    def _add_swap(self):
        place = self.place
        block = 64 if self.half % 64 == 0 else 32

        def step(i, carry):
            here = self._rows(self.base + i * block, block)
            there = self._rows(self.land + i * block, block)
            place.sums[here] = place.sums[here] + place.landing[there]
            return carry

        lax.fori_loop(0, self.half // block, step, 0)

    def _scatter(self, group, base, size):
        place = self.place
        self.land = self.landing
        for k in range(1, group.count):
            to = lax.rem(group.here + k, group.count)
            self._copy(
                place.sums.at[self._rows(base + to * size, size)],
                place.landing.at[pl.ds(self.landing, size)],
                group.device(to),
            )
            self.landing += size

    def _total(self, group, own, size, target):
        place = self.place
        block = 16 if size % 16 == 0 else 8

        def step(i, carry):
            here = self._rows(own + i * block, block)
            total = place.sums[here]
            for k in range(group.count - 1):
                there = self._rows(self.land + k * size + i * block, block)
                total = total + place.landing[there]
            target[here] = total
            return carry

        lax.fori_loop(0, size // block, step, 0)

    def _gather(self, group, own, size):
        final = self.place.final
        here = self._rows(own, size)
        for k in range(1, group.count):
            to = lax.rem(group.here + k, group.count)
            self._copy(final.at[here], final.at[here], group.device(to))

    def _steps(self):
        place, group = self.place, self.group
        yield self._swap()
        self._wait()
        self._add_swap()
        yield from self._both()
        final = place.final
        here = self._rows(self.base, self.half)
        self._copy(final.at[here], final.at[here], place.partner)
        yield
        self._wait()
        yield

    def _both(self):
        place, group = self.place, self.group
        self._scatter(group, self.base, self.part)
        yield
        self._wait()
        self._total(group, self.own, self.part, place.sums)
        yield from self._line()
        self._gather(group, self.own, self.part)
        yield
        self._wait()

    def _line(self):
        place, line = self.place, self.place.line
        sums, final, landing = place.sums, place.final, place.landing
        part, own = self.part, self._rows(self.own, self.part)
        inward, across = pl.ds(self.landing, part), pl.ds(self.landing + part, part)
        self.landing += 2 * part
        block = 16 if part % 16 == 0 else 8

        def add(at, target):
            def step(i, carry):
                here = self._rows(self.own + i * block, block)
                target[here] = sums[here] + landing[pl.ds(at + i * block, block)]
                return carry

            lax.fori_loop(0, part // block, step, 0)

        first = self._copy(sums.at[own], landing.at[inward], line.device(line.inner), line.edge)
        second = self._copy(sums.at[own], landing.at[across], line.device(line.across), line.middle)
        third = self._copy(final.at[own], final.at[own], line.device(line.outer), line.middle)
        pl.when(line.edge)(first.start)
        yield

        @pl.when(line.middle)
        def _():
            first.wait_recv()
            add(self.landing - 2 * part, sums)
            second.start()

        yield

        @pl.when(line.middle)
        def _():
            second.wait_recv()
            add(self.landing - part, final)
            third.start()

        yield
        pl.when(line.edge)(third.wait_recv)

    def advance(self):
        if self.stage == 0:
            self.steps = self._steps()
        self.stage += 1
        next(self.steps)

    def done(self):
        return self.stage == 8


class SmallExchange(Exchange):

    def count(self):
        return self.place.cores_group.count + self.place.line.count - 2

    def land_rows(self):
        return self.rows * (self.place.cores_group.count + self.place.line.count)

    def _share(self, group, source):
        place = self.place
        self.land = self.landing
        self.landing += group.count * self.rows
        own = self._rows(self.land + group.here * self.rows, self.rows)
        place.landing[own] = source[...]
        for k in range(1, group.count):
            to = lax.rem(group.here + k, group.count)
            self._copy(source, place.landing.at[own], group.device(to))

    def _sum(self, group):
        total = None
        for k in range(group.count):
            part = self.place.landing[pl.ds(self.land + k * self.rows, self.rows)]
            total = part if total is None else total + part
        return total

    def _steps(self):
        place = self.place
        here = pl.ds(self.start, self.rows)
        self._share(place.line, place.sums.at[here])
        yield
        self._wait()
        place.small[...] = self._sum(place.line)
        self._share(place.cores_group, place.small)
        yield
        self._wait()
        place.final[here] = self._sum(place.cores_group)
        yield

    def done(self):
        return self.stage == 3


def layout_of(shapes):
    starts = {}
    at = 0
    for name in LARGE:
        starts[name] = at
        at += getattr(shapes, name)[0]
    small = at
    begins = SimpleNamespace(**starts)
    late = small + LATE
    tap = shapes.dec_conv2[0] // 3
    part = shapes.dec_conv1[0] // 3
    conv1, up = begins.dec_conv1, begins.up_weight
    edges = (
        (begins.dec_conv2, begins.enc_conv1),
        (conv1, conv1 + part),
        (conv1 + part, conv1 + 2 * part),
        (conv1 + 2 * part, up),
        (up, begins.dec_conv2),
        (begins.enc_conv2, late),
        (begins.enc_conv1, begins.enc_conv1 + 2 * tap),
        (begins.enc_conv1 + 2 * tap, begins.enc_conv2),
        (late, late + LATE_COUNT),
    )
    runs = [(first, last - first) for first, last in edges]
    return starts, small, late + LATE_COUNT, runs


def item_kernel(sizes, scratch_names, *refs):
    line, strip, width, shapes, big_layout = sizes
    begins, small_at, total_rows, runs = big_layout
    starts = SimpleNamespace(**begins)
    inputs = Given(*refs[: len(ARGUMENTS)])
    refs = refs[len(ARGUMENTS) :]
    output_names = OUTPUTS
    outputs = SimpleNamespace(**dict(zip(output_names, refs)))
    scratch = SimpleNamespace(**dict(zip(scratch_names, refs[len(output_names) :])))

    def w_of(name):
        return getattr(scratch, name)

    height = strip * line
    cells = height * width
    c = inputs.lift_weight.shape[1]
    strip_cells = strip * width
    history = inputs.frames.shape[1]

    core = lax.axis_index("section")
    plane = lax.axis_index("batch")
    row = lax.axis_index("rows")
    middle = lax.rem(row + 1, 4) // 2

    def device_at(to):
        return (core, plane, to)

    place = SimpleNamespace(
        core=core,
        partner=(1 - core, plane, row),
        line=SimpleNamespace(
            count=line,
            here=row,
            device=device_at,
            middle=middle == 1,
            edge=middle == 0,
            inner=1 + row // 2,
            across=3 - row,
            outer=3 * (row // 2),
        ),
        plane_group=SimpleNamespace(
            count=4, here=plane, device=lambda to: (core, to, row)
        ),
        cores_group=SimpleNamespace(
            count=8,
            here=core * 4 + plane,
            device=lambda to: (to // 4, lax.rem(to, 4), row),
        ),
        small=scratch.small,
        sums=scratch.sums,
        final=scratch.final,
        landing=scratch.landing,
        send=scratch.send,
        recv=scratch.recv,
    )
    local_sem = scratch.local

    frames_in, mask_in, cot = scratch.frames_in, scratch.mask_in, scratch.cot
    here_rows = pl.ds(pl.multiple_of(row * strip_cells, strip_cells), strip_cells)
    frames_from, mask_from, cot_from = scratch.frames_from, scratch.mask_from, scratch.cot_from
    staged = (
        pltpu.make_async_copy(inputs.frames, frames_from, local_sem.at[7]),
        pltpu.make_async_copy(inputs.cell_mask, mask_from, local_sem.at[8]),
        pltpu.make_async_copy(inputs.cotangent, cot_from, local_sem.at[9]),
    )
    for copy in staged:
        copy.start()

    weight_copies = {}
    for k, name in enumerate(LARGE):
        copy = pltpu.make_async_copy(getattr(inputs, name), w_of(name), local_sem.at[k])
        weight_copies[name] = copy
        copy.start()

    barrier = pltpu.get_barrier_semaphore()
    peers = [device_at(lax.rem(row + k, line)) for k in range(1, line)]
    cores_group = place.cores_group
    for k in range(1, 8):
        peers.append(cores_group.device(lax.rem(cores_group.here + k, 8)))
    for device in peers:
        pl.semaphore_signal(barrier, inc=1, device_id=device, device_id_type=MESH)
    pl.semaphore_wait(barrier, len(peers))

    next_sem = 0

    def make(source, target, device):
        nonlocal next_sem
        copy = pltpu.make_async_remote_copy(
            src_ref=source,
            dst_ref=target,
            send_sem=scratch.send.at[next_sem],
            recv_sem=scratch.recv.at[next_sem],
            device_id=device,
            device_id_type=MESH,
        )
        next_sem += 1
        return copy

    def send(source, target, device):
        copy = make(source, target, device)
        copy.start()
        return copy

    def strip_of(ref, to):
        return ref.at[pl.ds(pl.multiple_of(to * strip_cells, strip_cells), strip_cells)]

    frame_copies, output_copies = [], []
    for copy in staged[:2]:
        copy.wait()
    for k in range(1, line):
        to = lax.rem(row + k, line)
        device = device_at(to)
        frame_copies.append(send(frames_from.at[to], frames_in.at[row], device))
        frame_copies.append(send(mask_from.at[to], mask_in.at[row], device))
    staged[2].wait()
    cot_swap = LineSwap(
        place.line,
        lambda to: cot_from.at[to],
        lambda source: strip_of(cot, source),
        scratch.cot_inward,
        scratch.cot_across,
        make,
    )
    cot_swap.first()

    copied = SimpleNamespace(**weight_copies)
    def put_pair(target, block, value):
        high, low = split(value)
        rows = slice(block * c, (block + 1) * c)
        target[rows, 0:c] = high
        target[rows, c : 2 * c] = low

    def stack_conv(source, half, depth, forward, backward):
        for a in range(3):
            for b in range(3):
                at = (3 * a + b) * depth + half * c
                value = source[at : at + c, :]
                turned = value.T
                for places in (HIGH_AT, LOW_AT):
                    put_pair(forward, 6 * a + places[b], value)
                    put_pair(backward, 6 * (2 - a) + places[2 - b], turned)

    copied.enc_conv1.wait()
    stack_conv(scratch.enc_conv1, 0, c, scratch.fe1, scratch.be1)
    copied.enc_conv2.wait()
    stack_conv(scratch.enc_conv2, 0, c, scratch.fe2, scratch.be2)
    copied.reducer_weight.wait()
    for k in range(4):
        value = scratch.reducer_weight[k * c : (k + 1) * c, :]
        turned = value.T
        for block in (k, k + 4):
            put_pair(scratch.f_down, block, value)
        for block in (0, 1):
            put_pair(scratch.b_down.at[k], block, turned)
    copied.up_weight.wait()
    for k in range(4):
        value = scratch.up_weight[k * c : (k + 1) * c, :]
        turned = value.T
        for block in (0, 1):
            put_pair(scratch.f_up.at[k], block, value)
        for block in (k, k + 4):
            put_pair(scratch.b_up, block, turned)
    copied.dec_conv1.wait()
    stack_conv(scratch.dec_conv1, 0, 2 * c, scratch.fd1a, scratch.bd1a)
    stack_conv(scratch.dec_conv1, 1, 2 * c, scratch.fd1b, scratch.bd1b)
    copied.dec_conv2.wait()
    stack_conv(scratch.dec_conv2, 0, c, scratch.fd2, scratch.bd2)
    copied.skip_weight.wait()
    for half in range(2):
        value = scratch.skip_weight[half * c : (half + 1) * c, :]
        turned = value.T
        for block in (half, half + 2):
            put_pair(scratch.f_skip, block, value)
        for block in (0, 1):
            put_pair(scratch.b_skip.at[half], block, turned)

    for buffer in (scratch.xe1, scratch.xe2, scratch.xd1a, scratch.xd1b, scratch.xd2, scratch.xg):
        edge = jnp.zeros((width, 6 * c), BF16)
        buffer[0:width, :] = edge
        buffer[cells + width : cells + 2 * width, :] = edge

    lift = scratch.lift
    lift[...] = jnp.zeros(lift.shape, F32)
    lift[0:history, :] = inputs.lift_weight[...]
    lift[history : history + 1, :] = inputs.lift_bias[...]

    block = 2 * width
    column = lax.rem(lax.broadcasted_iota(jnp.int32, (block, c), 0), width)
    at_first, at_last = column == 0, column == width - 1
    zeros8 = jnp.zeros((8, c), F32)
    ones16 = group_ones(c, c // GROUPS)
    ones32 = group_ones(c, 2 * c // GROUPS)
    count16 = float(cells * (c // GROUPS))
    count32 = float(cells * (2 * c // GROUPS))

    def grid_rows(step, carry=0):
        return lax.fori_loop(0, cells // block, step, carry, unroll=2)

    def row_at(h):
        return pl.ds(pl.multiple_of(h * block, block), block)

    def chunk_at(i):
        return pl.ds(pl.multiple_of(i * CHUNK, CHUNK), CHUNK)

    def put_row(target, h, value):
        rows = pl.ds(pl.multiple_of(h * block + width, width), block)
        left = jnp.where(at_first, 0.0, pltpu.roll(value, 1, 0))
        right = jnp.where(at_last, 0.0, pltpu.roll(value, block - 1, 0))
        for b, piece in enumerate((left, value, right)):
            high, low = split(piece)
            target[rows, HIGH_AT[b] * c : (HIGH_AT[b] + 1) * c] = high
            target[rows, LOW_AT[b] * c : (LOW_AT[b] + 1) * c] = low

    def put_turned(target, columns, value, first=0, second=1):
        high, low = split(value.T)
        target[first * c : (first + 1) * c, columns] = high
        target[second * c : (second + 1) * c, columns] = low

    def conv_chunk(pairs, i):
        total = None
        for data, weight in pairs:
            taps = []
            for a in range(3):
                rows = pl.ds(pl.multiple_of(i * CHUNK + a * width, width), CHUNK)
                taps.append(data[rows, :])
            part = dot(jnp.concatenate(taps, axis=1), weight[...])
            total = part if total is None else total + part
        return total

    def norm_of(first, second, ones, count):
        one, two = group_sums(first, second, ones)
        mean = one / count
        return mean, lax.rsqrt(two / count - mean * mean + EPS)

    def activate(source, target, turned, slope, scale, shift):
        def step(h, carry):
            value = source[row_at(h), :] * scale + shift
            below, density = normal(value)
            slope[row_at(h), :] = below + value * density
            value = value * below
            put_row(target, h, value)
            put_turned(turned, row_at(h), value)
            return carry

        grid_rows(step)

    def conv_norm(pairs, target):
        def step(i, carry):
            value = fold(conv_chunk(pairs, i))
            target[chunk_at(i), :] = value
            return carry[0] + tile_sums(value), carry[1] + tile_sums(value * value)

        return lax.fori_loop(0, cells // CHUNK, step, (zeros8, zeros8))

    def sums_of(source):
        def step(h, carry):
            value = source[row_at(h), :]
            return carry[0] + tile_sums(value), carry[1] + tile_sums(value * value)

        return grid_rows(step, (zeros8, zeros8))

    step_here = jnp.full((1, c), inputs.step_index[row], jnp.int32)

    def condition(table):
        total = jnp.zeros((1, 2 * c), F32)
        chosen = jnp.concatenate([step_here, step_here], axis=1)
        for s in range(table.shape[0]):
            total = total + jnp.where(chosen == s, table[s : s + 1, :], 0.0)
        return total[:, :c], total[:, c:]

    frames_in[row] = frames_from[row]
    mask_in[row] = mask_from[row]
    for copy in frame_copies:
        copy.wait_recv()
    fields = scratch.fields
    fields[...] = jnp.zeros(fields.shape, F32)
    frame_of = lax.broadcasted_iota(jnp.int32, (history, width), 0) // FIELDS
    keep = (frame_of >= HIST - inputs.counts[row]).astype(F32)
    masks = []
    for source in range(line):
        for k in range(strip):
            columns = slice((source * strip + k) * width, (source * strip + k + 1) * width)
            mask = mask_in[source, k : k + 1, :].astype(F32)
            masks.append(mask)
            fields[0:history, columns] = frames_in[source, :, k, :] * keep * mask
            fields[history : history + 1, columns] = mask
    lifted = scratch.lifted
    lifted[...] = dot_three(fields[...], lift[...], TN)

    enc_scale, enc_shift = condition(inputs.enc_step_table)
    dec_scale, dec_shift = condition(inputs.dec_step_table)

    mean_e1, inv_e1 = norm_of(*sums_of(lifted), ones16, count16)
    gain_e1, bias_e1 = inputs.enc_norm1_gain[...], inputs.enc_norm1_bias[...]
    a_e1 = inv_e1 * gain_e1
    activate(lifted, scratch.xe1, scratch.te1, scratch.slope_e1, a_e1, bias_e1 - mean_e1 * a_e1)
    middle_e = scratch.middle_e
    mean_e2, inv_e2 = norm_of(
        *conv_norm([(scratch.xe1, scratch.fe1)], middle_e), ones16, count16
    )
    gain_e2, bias_e2 = inputs.enc_norm2_gain[...], inputs.enc_norm2_bias[...]
    a_e2 = inv_e2 * gain_e2
    activate(
        middle_e,
        scratch.xe2,
        scratch.te2,
        scratch.slope_e2,
        a_e2 * (1.0 + enc_scale),
        (bias_e2 - mean_e2 * a_e2) * (1.0 + enc_scale) + enc_shift,
    )
    cot_swap.second()
    encoded = scratch.encoded
    conv2_bias = inputs.enc_conv2_bias[...]
    joined = scratch.joined

    def encode(i, carry):
        value = fold(conv_chunk([(scratch.xe2, scratch.fe2)], i))
        value = value + conv2_bias + lifted[chunk_at(i), :]
        encoded[chunk_at(i), :] = value
        high, low = split(value)
        joined[chunk_at(i), c : 2 * c] = high
        joined[chunk_at(i), 3 * c : 4 * c] = low
        put_turned(scratch.turned, chunk_at(i), value, 1, 3)
        return carry[0] + tile_sums(value), carry[1] + tile_sums(value * value)

    sums_enc = lax.fori_loop(0, cells // CHUNK, encode, (zeros8, zeros8))

    half_cells, quarter = cells // 2, cells // 4

    def pick(source):
        pieces = []
        for b in range(2):
            value = source[pl.ds(b, half_cells, stride=2), :]
            value = value.reshape(height // 2, 2, width // 2, c)
            pieces.append([value[:, a].reshape(quarter, c) for a in range(2)])
        return [pieces[b][a] for a in range(2) for b in range(2)]

    def place_cells(target, pieces):
        for b in range(2):
            both = [pieces[2 * a + b].reshape(height // 2, 1, width // 2, c) for a in range(2)]
            value = jnp.concatenate(both, axis=1).reshape(half_cells, c)
            target[pl.ds(b, half_cells, stride=2), :] = value

    x_down = scratch.x_down
    for k, piece in enumerate(pick(encoded)):
        high, low = split(piece)
        x_down[:, k * c : (k + 1) * c] = high
        x_down[:, (k + 4) * c : (k + 5) * c] = low
    lowered = fold(dot(x_down[...], scratch.f_down[...])) + inputs.reducer_bias[...]
    x_up = scratch.x_up
    high, low = split(lowered)
    x_up[:, 0:c] = high
    x_up[:, c : 2 * c] = low
    raised = scratch.raised
    up_bias = inputs.up_bias[...]
    place_cells(
        raised, [fold(dot(x_up[...], scratch.f_up[k])) + up_bias for k in range(4)]
    )

    def raise_row(h, carry):
        value = raised[row_at(h), :]
        high, low = split(value)
        joined[row_at(h), 0:c] = high
        joined[row_at(h), 2 * c : 3 * c] = low
        put_turned(scratch.turned, row_at(h), value, 0, 2)
        return carry[0] + tile_sums(value), carry[1] + tile_sums(value * value)

    sums_raised = grid_rows(raise_row, (zeros8, zeros8))

    halves = []
    for half, (source, sums) in enumerate(((raised, sums_raised), (encoded, sums_enc))):
        mean, inv = norm_of(*sums, ones32, count32)
        gain = inputs.dec_norm1_gain[half : half + 1, :]
        bias = inputs.dec_norm1_bias[half : half + 1, :]
        scale = inv * gain
        activate(
            source,
            (scratch.xd1a, scratch.xd1b)[half],
            scratch.td1.at[2 * c * half : 2 * c * (half + 1)],
            (scratch.slope_d1a, scratch.slope_d1b)[half],
            scale,
            bias - mean * scale,
        )
        halves.append((source, mean, inv, gain))
    middle_d = scratch.middle_d
    pairs = [(scratch.xd1a, scratch.fd1a), (scratch.xd1b, scratch.fd1b)]
    mean_d2, inv_d2 = norm_of(*conv_norm(pairs, middle_d), ones16, count16)
    cot_swap.third()
    gain_d2, bias_d2 = inputs.dec_norm2_gain[...], inputs.dec_norm2_bias[...]
    a_d2 = inv_d2 * gain_d2
    activate(
        middle_d,
        scratch.xd2,
        scratch.td2,
        scratch.slope_d2,
        a_d2 * (1.0 + dec_scale),
        (bias_d2 - mean_d2 * a_d2) * (1.0 + dec_scale) + dec_shift,
    )
    result = scratch.result
    last_bias = inputs.dec_conv2_bias[...] + inputs.skip_bias[...]

    def decode(i, carry):
        value = conv_chunk([(scratch.xd2, scratch.fd2)], i)
        value = value + dot(joined[chunk_at(i), :], scratch.f_skip[...])
        result[chunk_at(i), :] = fold(value) + last_bias
        return carry

    lax.fori_loop(0, cells // CHUNK, decode, 0)
    output_here, frames_here = scratch.output_here, scratch.frames_here
    output_here[row] = result[here_rows]
    output_swap = LineSwap(
        place.line,
        lambda to: strip_of(result, to),
        lambda source: output_here.at[source],
        scratch.output_inward,
        scratch.output_across,
        make,
    )
    output_swap.first()

    exchanges = []
    waiting_runs = list(runs)
    landing_at = 0
    sem_at = 3 * (line - 1) + 20
    sums, final = scratch.sums, scratch.final

    def begin():
        nonlocal landing_at, sem_at
        start, rows = waiting_runs.pop(0)
        kind = Exchange if waiting_runs else SmallExchange
        exchange = kind(place, start, rows, landing_at, sem_at)
        landing_at += exchange.land_rows()
        sem_at += exchange.count()
        exchanges.append(exchange)
        exchange.advance()

    final_copies = []

    def advance(k):
        exchange = exchanges[k]
        exchange.advance()
        if exchange.done():
            rows = pl.ds(exchange.start, exchange.rows)
            copy = pltpu.make_async_copy(
                final.at[rows], outputs.gradients.at[rows], local_sem.at[11 + k]
            )
            copy.start()
            final_copies.append(copy)

    due = list(DUE)

    def point():
        for k in due.pop(0):
            advance(k)

    def small_row(k, value):
        sums[small_at + k : small_at + k + 1, :] = value

    def spread_grad(source):
        def step(h, carry):
            value = source[row_at(h), :]
            put_row(scratch.xg, h, value)
            return carry + tile_sums(value)

        return grid_rows(step, zeros8)

    def weight_grad(turned, at, depth, a):
        rows = pl.ds((2 - a) * width, cells)
        both = dot(turned[...], scratch.xg[rows, :])
        for half in range(depth // c):
            part = fold_rows(both[2 * c * half : 2 * c * (half + 1)])
            for b in range(3):
                high, low = HIGH_AT[2 - b] * c, LOW_AT[2 - b] * c
                to = at + (3 * a + b) * depth + half * c
                sums[to : to + c, :] = part[:, high : high + c] + part[:, low : low + c]

    def back_conv(weight, slope, target, source, mean, inv):
        carry = (zeros8, zeros8)
        for i in range(cells // CHUNK):
            value = fold(conv_chunk([(scratch.xg, weight)], i)) * slope[chunk_at(i), :]
            target[chunk_at(i), :] = value
            normed = (source[chunk_at(i), :] - mean) * inv
            carry = (carry[0] + tile_sums(value), carry[1] + tile_sums(value * normed))
        for _ in range(2):
            point()
        return carry

    def norm_grad(sums_in, scale, ones, count):
        one, two = group_sums(sums_in[0] * scale, sums_in[1] * scale, ones)
        return one / count, two / count

    cot[here_rows] = cot_from[row]
    cot_swap.arrive()
    total_cot = column_sum(spread_grad(cot))
    for a in range(3):
        weight_grad(scratch.td2, starts.dec_conv2, c, a)
    part = fold(dot(scratch.turned[...], scratch.xg[width : cells + width, 2 * c : 4 * c]))
    sums[starts.skip_weight : starts.skip_weight + 2 * c, :] = fold_rows(part)
    small_row(3, total_cot)
    begin()

    grad = scratch.grad
    sums_d2 = back_conv(scratch.bd2, scratch.slope_d2, grad, middle_d, mean_d2, inv_d2)
    side_grads = (scratch.grad_a, scratch.grad_b)
    for half in range(2):

        def skip_back(i, carry, half=half):
            rows = pl.ds(pl.multiple_of(i * CHUNK + width, width), CHUNK)
            value = dot(scratch.xg[rows, 2 * c : 4 * c], scratch.b_skip[half])
            side_grads[half][chunk_at(i), :] = fold(value)
            return carry

        lax.fori_loop(0, cells // CHUNK, skip_back, 0)
    point()

    def table_rows(k, sums_in, gain, bias, one_plus):
        plain, times = column_sum(sums_in[0]), column_sum(sums_in[1])
        for s in range(inputs.enc_step_table.shape[0]):
            small_row(k + 2 * s, jnp.where(step_here == s, gain * times + bias * plain, 0.0))
            small_row(k + 2 * s + 1, jnp.where(step_here == s, plain, 0.0))
        return one_plus * times, one_plus * plain

    def middle_grad(source, mean, inv, scale, sums_in):
        zero, slope = norm_grad(sums_in, scale, ones16, count16)

        def step(h, carry):
            normed = (source[row_at(h), :] - mean) * inv
            value = inv * (grad[row_at(h), :] * scale - zero - normed * slope)
            put_row(scratch.xg, h, value)
            return carry

        grid_rows(step)

    gain_row, bias_row = table_rows(16, sums_d2, gain_d2, bias_d2, 1.0 + dec_scale)
    small_row(8, gain_row)
    small_row(9, bias_row)
    middle_grad(middle_d, mean_d2, inv_d2, gain_d2 * (1.0 + dec_scale), sums_d2)
    point()
    output_swap.second()
    for a in range(3):
        weight_grad(scratch.td1, starts.dec_conv1, 2 * c, a)
        point()
        begin()

    for half, (source, mean, inv, gain) in enumerate(halves):
        sums_in = back_conv(
            (scratch.bd1a, scratch.bd1b)[half],
            (scratch.slope_d1a, scratch.slope_d1b)[half],
            grad,
            source,
            mean,
            inv,
        )
        small_row(4 + half, column_sum(sums_in[1]))
        small_row(6 + half, column_sum(sums_in[0]))
        zero, slope = norm_grad(sums_in, gain, ones32, count32)
        target = side_grads[half]

        def input_grad(h, carry):
            normed = (source[row_at(h), :] - mean) * inv
            value = inv * (grad[row_at(h), :] * gain - zero - normed * slope)
            value = target[row_at(h), :] + value
            target[row_at(h), :] = value
            return carry + tile_sums(value)

        total = grid_rows(input_grad, zeros8)
        if half == 0:
            small_row(2, column_sum(total))
        point()

    output_swap.third()
    grad_raised, grad_encoded = side_grads
    x_grad_up = scratch.x_grad_up
    for k, piece in enumerate(pick(grad_raised)):
        high, low = split(piece)
        x_grad_up[:, k * c : (k + 1) * c] = high
        x_grad_up[:, (k + 4) * c : (k + 5) * c] = low
    grad_lowered = fold(dot(x_grad_up[...], scratch.b_up[...]))
    small_row(1, jnp.sum(grad_lowered, axis=0, keepdims=True))
    x_grad_low = scratch.x_grad_low
    high, low = split(grad_lowered)
    x_grad_low[:, 0:c] = high
    x_grad_low[:, c : 2 * c] = low
    point()
    part = fold(fold_rows(dot(x_up[...], x_grad_up[...], TN)))
    for k in range(4):
        at = starts.up_weight + k * c
        sums[at : at + c, :] = part[:, k * c : (k + 1) * c]
    part = fold_rows(fold(dot(x_down[...], x_grad_low[...], TN)))
    sums[starts.reducer_weight : starts.reducer_weight + 4 * c, :] = part
    point()
    begin()
    place_cells(
        grad, [fold(dot(x_grad_low[...], scratch.b_down[k])) for k in range(4)]
    )

    def join_row(h, carry):
        value = grad_encoded[row_at(h), :] + grad[row_at(h), :]
        grad_encoded[row_at(h), :] = value
        put_row(scratch.xg, h, value)
        return carry + tile_sums(value)

    small_row(0, column_sum(grid_rows(join_row, zeros8)))
    for k in range(10, 16):
        small_row(k, jnp.zeros((1, c), F32))
    sums[small_at + 24 : small_at + LATE, :] = jnp.zeros((LATE - 24, c), F32)
    point()
    for a in range(3):
        weight_grad(scratch.te2, starts.enc_conv2, c, a)
        point()
    begin()
    sums_e2 = back_conv(scratch.be2, scratch.slope_e2, grad, middle_e, mean_e2, inv_e2)
    gain_row, bias_row = table_rows(LATE + 24, sums_e2, gain_e2, bias_e2, 1.0 + enc_scale)
    small_row(LATE + 18, gain_row)
    small_row(LATE + 19, bias_row)
    middle_grad(middle_e, mean_e2, inv_e2, gain_e2 * (1.0 + enc_scale), sums_e2)
    point()
    for a in range(3):
        weight_grad(scratch.te1, starts.enc_conv1, c, a)
        point()
        if a:
            begin()
    sums_e1 = back_conv(scratch.be1, scratch.slope_e1, grad, lifted, mean_e1, inv_e1)
    small_row(LATE + 16, column_sum(sums_e1[1]))
    small_row(LATE + 17, column_sum(sums_e1[0]))
    zero, slope = norm_grad(sums_e1, gain_e1, ones16, count16)

    def lifted_grad(h, carry):
        normed = (lifted[row_at(h), :] - mean_e1) * inv_e1
        value = inv_e1 * (grad[row_at(h), :] * gain_e1 - zero - normed * slope)
        grad[row_at(h), :] = grad_encoded[row_at(h), :] + value
        return carry

    grid_rows(lifted_grad)
    point()

    late_at = small_at + LATE
    sums[late_at : late_at + 16, :] = dot_three(fields[...], grad[...])
    sums[late_at + 20 : late_at + 24, :] = jnp.zeros((4, c), F32)
    point()
    begin()
    back = dot_three(lift[...], grad[...], NT)
    frames_out = scratch.frames_out
    for source in range(line):
        for k in range(strip):
            h = source * strip + k
            value = back[0:history, h * width : (h + 1) * width]
            frames_out[source, :, k, :] = value * keep * masks[h]
    frames_here[row] = frames_out[row]
    for k in range(1, line):
        to = lax.rem(row + k, line)
        output_copies.append(
            send(frames_out.at[to], frames_here.at[row], device_at(to))
        )

    output_swap.arrive()
    own_output = pltpu.make_async_copy(output_here, outputs.output, local_sem.at[10])
    own_output.start()
    for k in REST:
        advance(k)
    assert not due and all(exchange.done() for exchange in exchanges)

    for copy in output_copies:
        copy.wait_recv()
    own_frames = pltpu.make_async_copy(
        frames_here, outputs.frames_grad, local_sem.at[11 + len(runs)]
    )
    own_frames.start()
    own_output.wait()
    own_frames.wait()
    for copy in final_copies:
        copy.wait()
    for copy in frame_copies + output_copies:
        copy.wait_send()
    cot_swap.sent()
    output_swap.sent()
    for exchange in exchanges:
        for copy, only in exchange.copies:
            if only is None:
                copy.wait_send()
            else:
                pl.when(only)(copy.wait_send)


def write_kernel(layout, *refs):
    shapes, starts, small_at = layout
    output, frames_grad, gradients = refs[:3]
    outputs = refs[3:-4]
    output_here, frames_here, gradients_here, sem = refs[-4:]
    c = gradients.shape[1]
    moves = [(frames_grad, frames_here, outputs[1])]
    for k, name in enumerate(LARGE):
        rows = pl.ds(starts[name], shapes[name][0])
        moves.append((gradients.at[rows], gradients_here.at[rows], outputs[2 + k]))
    moves.append((output, output_here, outputs[0]))
    small = pl.ds(small_at, SMALL_COUNT)
    first = pltpu.make_async_copy(gradients.at[small], gradients_here.at[small], sem.at[0])
    first.start()
    arriving, leaving = [], []
    for k, (source, here, _) in enumerate(moves):
        arriving.append(pltpu.make_async_copy(source, here, sem.at[1 + 2 * k]))
        arriving[-1].start()
    first.wait()
    for target, (k, rows) in zip(outputs[2 + len(LARGE) :], SMALL_ROWS.values()):
        at = small_at + k
        if rows == 8:
            for s in range(target.shape[0]):
                target[s : s + 1, 0:c] = gradients_here[at + 2 * s : at + 2 * s + 1, :]
                target[s : s + 1, c : 2 * c] = gradients_here[at + 2 * s + 1 : at + 2 * s + 2, :]
        else:
            target[...] = gradients_here[at : at + rows, :]
    for k, (_, here, target) in enumerate(moves):
        arriving[k].wait()
        leaving.append(pltpu.make_async_copy(here, target, sem.at[2 + 2 * k]))
        leaving[-1].start()
    for copy in leaving:
        copy.wait()


def whole_items(shape, *arguments):
    line = shape["rows"]
    whole = Given(*arguments)
    given = whole._asdict()
    frames, cotangent = whole.frames, whole.cotangent
    items, history, strip, width = frames.shape
    c = cotangent.shape[-1]
    cells = strip * line * width
    flat = {}
    for name, value in given.items():
        if value is cotangent:
            value = value.reshape(items, strip * width, c)
        elif name in LARGE:
            value = value.reshape(-1, c)
        elif value.ndim == 1 and name not in IN_SMEM:
            value = value.reshape(-1, c)
        flat[name] = value
    shapes = {name: flat[name].shape for name in LARGE}
    big_layout = layout_of(SimpleNamespace(**shapes))
    starts, small_at, total_rows, runs = big_layout
    copies = 20 + 3 * (line - 1) + len(runs) * (8 + 2 * (line - 1)) + 6
    landing = sum(rows // 2 + 5 * rows // 8 for _, rows in runs) + LATE_COUNT * (8 + line)
    shifted = pltpu.VMEM((cells + 2 * width, 6 * c), BF16)
    forward = pltpu.VMEM((18 * c, 2 * c), BF16)
    backward = forward
    field = pltpu.VMEM((cells, c), F32)
    flipped_field = pltpu.VMEM((2 * c, cells), BF16)
    quarter = cells // 4
    scratch = dict(
        small=pltpu.VMEM((LATE_COUNT, c), F32),
        send=pltpu.SemaphoreType.DMA((copies,)),
        recv=pltpu.SemaphoreType.DMA((copies,)),
        local=pltpu.SemaphoreType.DMA((12 + len(runs),)),
        sums=pltpu.VMEM((total_rows, c), F32),
        final=pltpu.VMEM((total_rows, c), F32),
        landing=pltpu.VMEM((landing, c), F32),
        frames_in=pltpu.VMEM((line, history, strip, width), F32),
        mask_in=pltpu.VMEM((line, strip, width), jnp.int32),
        frames_out=pltpu.VMEM((line, history, strip, width), F32),
        frames_from=pltpu.VMEM((line, history, strip, width), F32),
        frames_here=pltpu.VMEM((line, history, strip, width), F32),
        mask_from=pltpu.VMEM((line, strip, width), jnp.int32),
        cot_from=pltpu.VMEM((items, strip * width, c), F32),
        output_here=pltpu.VMEM((items, strip * width, c), F32),
        cot_inward=pltpu.VMEM((2, strip * width, c), F32),
        cot_across=pltpu.VMEM((2, strip * width, c), F32),
        output_inward=pltpu.VMEM((2, strip * width, c), F32),
        output_across=pltpu.VMEM((2, strip * width, c), F32),
        fields=pltpu.VMEM((16, cells), F32),
        lift=pltpu.VMEM((16, c), F32),
        joined=pltpu.VMEM((cells, 4 * c), BF16),
        x_down=pltpu.VMEM((quarter, 8 * c), BF16),
        x_grad_up=pltpu.VMEM((quarter, 8 * c), BF16),
        x_up=pltpu.VMEM((quarter, 2 * c), BF16),
        x_grad_low=pltpu.VMEM((quarter, 2 * c), BF16),
        f_down=pltpu.VMEM((8 * c, 2 * c), BF16),
        b_down=pltpu.VMEM((4, 2 * c, 2 * c), BF16),
        f_up=pltpu.VMEM((4, 2 * c, 2 * c), BF16),
        b_up=pltpu.VMEM((8 * c, 2 * c), BF16),
        f_skip=pltpu.VMEM((4 * c, 2 * c), BF16),
        b_skip=pltpu.VMEM((2, 2 * c, 2 * c), BF16),
        xe1=shifted,
        xe2=shifted,
        xd1a=shifted,
        xd1b=shifted,
        xd2=shifted,
        xg=shifted,
        te1=flipped_field,
        te2=flipped_field,
        td1=pltpu.VMEM((4 * c, cells), BF16),
        td2=flipped_field,
        turned=pltpu.VMEM((4 * c, cells), BF16),
        fe1=forward,
        fe2=forward,
        fd1a=forward,
        fd1b=forward,
        fd2=forward,
        be1=backward,
        be2=backward,
        bd1a=backward,
        bd1b=backward,
        bd2=backward,
        slope_e1=field,
        slope_e2=field,
        slope_d1a=field,
        slope_d1b=field,
        slope_d2=field,
        lifted=field,
        middle_e=field,
        encoded=field,
        raised=field,
        middle_d=field,
        result=field,
        cot=field,
        grad=field,
        grad_a=field,
        grad_b=field,
    )
    scratch.update({name: pltpu.VMEM(shapes[name], F32) for name in LARGE})

    in_hbm = pl.BlockSpec(memory_space=pl.ANY)
    in_vmem = pl.BlockSpec(memory_space=pltpu.VMEM)
    in_smem = pl.BlockSpec(memory_space=pltpu.SMEM)
    in_specs = [
        in_hbm if name in IN_HBM else in_smem if name in IN_SMEM else in_vmem
        for name in ARGUMENTS
    ]
    out_shape = [
        jax.ShapeDtypeStruct((items, strip * width, c), F32),
        jax.ShapeDtypeStruct(frames.shape, F32),
        jax.ShapeDtypeStruct((total_rows, c), F32),
    ]
    out_specs = [in_hbm] * 3
    results = pl.pallas_call(
        functools.partial(
            item_kernel,
            (line, strip, width, shapes, big_layout),
            tuple(scratch),
        ),
        out_shape=out_shape,
        in_specs=in_specs,
        out_specs=out_specs,
        scratch_shapes=list(scratch.values()),
        compiler_params=pltpu.CompilerParams(
            collective_id=0, has_side_effects=True, vmem_limit_bytes=62 * 1024 * 1024
        ),
    )(*[flat[name] for name in ARGUMENTS])
    names = LARGE + tuple(SMALL_ROWS)
    written = pl.pallas_call(
        functools.partial(write_kernel, (shapes, starts, small_at)),
        out_shape=out_shape[:2] + [jax.ShapeDtypeStruct(flat[name].shape, F32) for name in names],
        in_specs=[pl.BlockSpec(memory_space=pltpu.HBM)] * 3,
        out_specs=[in_hbm] * (2 + len(LARGE)) + [in_vmem] * len(SMALL_ROWS),
        scratch_shapes=[
            pltpu.VMEM((items, strip * width, c), F32),
            pltpu.VMEM(frames.shape, F32),
            pltpu.VMEM((total_rows, c), F32),
            pltpu.SemaphoreType.DMA((1 + 2 * (2 + len(LARGE)),)),
        ],
        compiler_params=pltpu.CompilerParams(vmem_limit_bytes=60 * 1024 * 1024),
    )(*results)
    grads = dict(zip(names, written[2:]))
    ordered = [name for name in ARGUMENTS if name in grads]
    return (written[0].reshape(cotangent.shape), written[1]) + tuple(
        grads[name].reshape(given[name].shape) for name in ordered
    )


def body(shape, *arguments):
    items, _, strip, width = arguments[0].shape
    line = shape["rows"]
    whole = (
        shape["section"] == 2
        and shape["batch"] == 4
        and items == line == 4
        and arguments[-1].shape[-1] == 128
        and (strip * line * width) % CHUNK == 0
    )
    return whole_items(shape, *arguments) if whole else strips_body(*arguments)


def solution(mesh):
    in_specs = (
        P(("section", "batch"), None, "rows", None),
        P(("section", "batch")),
        P(("section", "batch"), "rows", None),
        P(("section", "batch")),
        P(),
        P(),
        P(),
        P(),
        P(),
        P(),
        P(),
        P(),
        P(),
        P(),
        P(),
        P(),
        P(),
        P(),
        P(),
        P(),
        P(),
        P(),
        P(),
        P(),
        P(),
        P(),
        P(),
        P(),
        P(("section", "batch"), "rows", None, None),
    )
    out_specs = (
        P(("section", "batch"), "rows", None, None),
        P(("section", "batch"), None, "rows", None),
        P(),
        P(),
        P(),
        P(),
        P(),
        P(),
        P(),
        P(),
        P(),
        P(),
        P(),
        P(),
        P(),
        P(),
        P(),
        P(),
        P(),
        P(),
        P(),
        P(),
        P(),
        P(),
        P(),
        P(),
    )
    return jax.shard_map(functools.partial(body, mesh.shape), mesh=mesh, in_specs=in_specs, out_specs=out_specs, check_vma=False)
```

```python
import functools
from types import SimpleNamespace
from typing import Any, NamedTuple

import jax
import jax.numpy as jnp
from jax import lax
from jax.experimental import pallas as pl
from jax.experimental.pallas import tpu as pltpu
from jax.sharding import PartitionSpec as P

GROUPS = 8
FIELDS = 3
HIST = 4


EPS = 1e-05
HIGH = lax.Precision.HIGHEST


def extended(cells, sides, width):
    for axis, dim in sides:
        count = lax.axis_size(axis)
        ends = count - 1
        head = lax.slice_in_dim(cells, 0, width, axis=dim)
        tail = lax.slice_in_dim(cells, cells.shape[dim] - width, cells.shape[dim], axis=dim)
        cells = jnp.concatenate(
            [
                lax.ppermute(tail, axis, [(i, (i + 1) % count) for i in range(ends)]),
                cells,
                lax.ppermute(head, axis, [((i + 1) % count, i) for i in range(ends)]),
            ],
            axis=dim,
        )
    return cells


def from_behind(value, axis, steps):
    count = lax.axis_size(axis)
    pairs = [(source, (source + steps) % count) for source in range(count)]
    return lax.ppermute(value, axis, pairs)


def group_view(value_arrays):
    extent = value_arrays.shape
    return value_arrays.reshape(extent[:-1] + (GROUPS, extent[-1] // GROUPS))


def global_sums(value_arrays):
    grouped = group_view(value_arrays)
    flat = grouped.reshape(-1, GROUPS, grouped.shape[-1])
    first_sum = jnp.sum(flat, axis=(0, 2))
    second_sum = jnp.sum(flat * flat, axis=(0, 2))
    return lax.psum((first_sum, second_sum), "rows")


def apply_norm(value_arrays, sum_one, sum_two, norm_gain, norm_bias, total):
    grouped = group_view(value_arrays)
    group_mean = sum_one / total
    variance = sum_two / total - group_mean * group_mean
    inverse = lax.rsqrt(variance + EPS)
    normed = (grouped - group_mean[:, None]) * inverse[:, None]
    return normed.reshape(value_arrays.shape) * norm_gain + norm_bias


def norm_back(value_arrays, grad_one, grad_two):
    grouped = group_view(value_arrays)
    extra = grad_one[:, None] + 2.0 * grouped * grad_two[:, None]
    return extra.reshape(value_arrays.shape)


def reduce_grads(grad_one, grad_two):
    return lax.psum((grad_one, grad_two), "rows")


def conv_rows(padded, kernel):
    widened = jnp.pad(padded, ((0, 0), (1, 1), (0, 0)))
    return lax.conv_general_dilated(
        widened[None],
        kernel,
        (1, 1),
        "VALID",
        dimension_numbers=("NHWC", "HWIO", "NHWC"),
        precision=HIGH,
    )[0]


def flipped(kernel):
    return jnp.transpose(kernel[::-1, ::-1], (0, 1, 3, 2))


def pad_grads(value_arrays):
    return extended(value_arrays, (("rows", 0),), 1)


def totals_of(inputs, conv1):
    strip = inputs.shape[0]
    cells = strip * lax.axis_size("rows") * inputs.shape[1]
    return (cells * (inputs.shape[2] // GROUPS), cells * (conv1.shape[3] // GROUPS))


def block_forward(inputs, weights, scale_part, shift_part):
    norm1_gain, norm1_bias, conv1, norm2_gain, norm2_bias, conv2, conv2_bias = weights
    total_in, total_mid = totals_of(inputs, conv1)
    sums_in = global_sums(inputs)

    def pad_rows(value_arrays):
        return extended(value_arrays, (("rows", 0),), 1)

    act_one = pad_rows(
        jax.nn.gelu(
            apply_norm(inputs, sums_in[0], sums_in[1], norm1_gain, norm1_bias, total_in),
            approximate=False,
        )
    )
    middle = conv_rows(act_one, conv1)
    sums_mid = global_sums(middle)
    shaped = (
        apply_norm(middle, sums_mid[0], sums_mid[1], norm2_gain, norm2_bias, total_mid)
        * (1.0 + scale_part)
        + shift_part
    )
    act_two = pad_rows(jax.nn.gelu(shaped, approximate=False))
    branch = conv_rows(act_two, conv2) + conv2_bias
    return (branch, (sums_in[0], sums_in[1], act_one, middle, sums_mid[0], sums_mid[1], act_two))


def block_backward(inputs, weights, scale_part, shift_part, kept, grad_out):
    norm1_gain, norm1_bias, conv1, norm2_gain, norm2_bias, conv2, conv2_bias = weights
    in_one, in_two, act_one, middle, mid_one, mid_two, act_two = kept
    total_in, total_mid = totals_of(inputs, conv1)
    grad_conv2 = jax.vjp(lambda kernel: conv_rows(act_two, kernel), conv2)[1](grad_out)[0]
    grad_bias2 = jnp.sum(grad_out, axis=(0, 1))
    grad_act_two = conv_rows(pad_grads(grad_out), flipped(conv2))

    def second_piece(middle_in, sum_one, sum_two, gain_in, incoming_bias, scale_in, shift_in):
        shaped = (
            apply_norm(middle_in, sum_one, sum_two, gain_in, incoming_bias, total_mid)
            * (1.0 + scale_in)
            + shift_in
        )
        return jax.nn.gelu(shaped, approximate=False)

    second_pull = jax.vjp(
        second_piece, middle, mid_one, mid_two, norm2_gain, norm2_bias, scale_part, shift_part
    )[1](grad_act_two)
    summed_one, summed_two = reduce_grads(second_pull[1], second_pull[2])
    grad_middle = second_pull[0] + norm_back(middle, summed_one, summed_two)
    grad_conv1 = jax.vjp(lambda kernel: conv_rows(act_one, kernel), conv1)[1](grad_middle)[0]
    grad_act_one = conv_rows(pad_grads(grad_middle), flipped(conv1))

    def first_piece(inputs_in, sum_one, sum_two, gain_in, incoming_bias):
        return jax.nn.gelu(
            apply_norm(inputs_in, sum_one, sum_two, gain_in, incoming_bias, total_in),
            approximate=False,
        )

    first_pull = jax.vjp(first_piece, inputs, in_one, in_two, norm1_gain, norm1_bias)[1](
        grad_act_one
    )
    first_one, first_two = reduce_grads(first_pull[1], first_pull[2])
    grad_inputs = first_pull[0] + norm_back(inputs, first_one, first_two)
    grads = (
        first_pull[3],
        first_pull[4],
        grad_conv1,
        second_pull[3],
        second_pull[4],
        grad_conv2,
        grad_bias2,
    )
    return (grad_inputs, grads, second_pull[5], second_pull[6])


def conditioning(step_item, table):
    one_hot = (jnp.arange(table.shape[0], dtype=jnp.int32) == step_item).astype(jnp.float32)
    condition = jnp.dot(one_hot, table, precision=HIGH)
    half_width = table.shape[1] // 2
    return (condition[:half_width], condition[half_width:], one_hot)


def project_in(frames_item, mask_item, count_item, incoming_weight, incoming_bias):
    history = jnp.arange(HIST, dtype=jnp.int32) >= HIST - count_item
    keep = jnp.repeat(history, FIELDS).astype(jnp.float32)
    lifted = (
        jnp.einsum(
            "fhw,fc->hwc", frames_item * keep[:, None, None], incoming_weight, precision=HIGH
        )
        + incoming_bias
    )
    return lifted * mask_item[:, :, None].astype(jnp.float32)


def coarsen_field(value_arrays, incoming_weight, incoming_bias):
    rows_here, width_here, depth_here = value_arrays.shape
    blocks = value_arrays.reshape(rows_here // 2, 2, width_here // 2, 2, depth_here)
    return jnp.einsum("iajbk,abkc->ijc", blocks, incoming_weight, precision=HIGH) + incoming_bias


def upsample(value_arrays, incoming_weight, incoming_bias):
    result = jnp.einsum("ijk,abkc->iajbc", value_arrays, incoming_weight, precision=HIGH)
    extent = result.shape
    return result.reshape(extent[0] * 2, extent[2] * 2, extent[4]) + incoming_bias


def flatten_all(pieces):
    return jnp.concatenate([piece.reshape(-1) for piece in pieces])


def unflatten_all(flat, templates):
    pieces = []
    offset_at = 0
    for template in templates:
        count_here = template.size
        pieces.append(flat[offset_at : offset_at + count_here].reshape(template.shape))
        offset_at += count_here
    return tuple(pieces)


def strips_body(
    frames,
    counts,
    cell_mask,
    step_index,
    lift_weight,
    lift_bias,
    enc_norm1_gain,
    enc_norm1_bias,
    enc_conv1,
    enc_step_table,
    enc_norm2_gain,
    enc_norm2_bias,
    enc_conv2,
    enc_conv2_bias,
    reducer_weight,
    reducer_bias,
    up_weight,
    up_bias,
    dec_norm1_gain,
    dec_norm1_bias,
    dec_conv1,
    dec_step_table,
    dec_norm2_gain,
    dec_norm2_bias,
    dec_conv2,
    dec_conv2_bias,
    skip_weight,
    skip_bias,
    cotangent,
):
    enc_weights = (
        enc_norm1_gain,
        enc_norm1_bias,
        enc_conv1,
        enc_norm2_gain,
        enc_norm2_bias,
        enc_conv2,
        enc_conv2_bias,
    )
    dec_weights = (
        dec_norm1_gain,
        dec_norm1_bias,
        dec_conv1,
        dec_norm2_gain,
        dec_norm2_bias,
        dec_conv2,
        dec_conv2_bias,
    )
    params = (
        lift_weight,
        lift_bias,
        enc_norm1_gain,
        enc_norm1_bias,
        enc_conv1,
        enc_step_table,
        enc_norm2_gain,
        enc_norm2_bias,
        enc_conv2,
        enc_conv2_bias,
        reducer_weight,
        reducer_bias,
        up_weight,
        up_bias,
        dec_norm1_gain,
        dec_norm1_bias,
        dec_conv1,
        dec_step_table,
        dec_norm2_gain,
        dec_norm2_bias,
        dec_conv2,
        dec_conv2_bias,
        skip_weight,
        skip_bias,
    )

    def forward_micro(carry, sliced):
        frames_item, mask_item, count_item, step_item = sliced
        lifted = project_in(frames_item, mask_item, count_item, lift_weight, lift_bias)
        enc_scale, enc_shift, unused_hot = conditioning(step_item, enc_step_table)
        enc_branch, enc_kept = block_forward(lifted, enc_weights, enc_scale, enc_shift)
        encoder_result = lifted + enc_branch
        coarse_field = coarsen_field(encoder_result, reducer_weight, reducer_bias)
        foreign = from_behind(coarse_field, "section", 1)
        raised_foreign = upsample(foreign, up_weight, up_bias)
        raised = from_behind(raised_foreign, "section", 1)
        joined = jnp.concatenate([raised, encoder_result], axis=-1)
        dec_scale, dec_shift, unused_again = conditioning(step_item, dec_step_table)
        dec_branch, dec_kept = block_forward(joined, dec_weights, dec_scale, dec_shift)
        output_item = jnp.dot(joined, skip_weight, precision=HIGH) + skip_bias + dec_branch
        return (carry, (output_item, (lifted, enc_kept, encoder_result, foreign, joined, dec_kept)))

    unused, (output, kept_all) = lax.scan(
        forward_micro, jnp.zeros((), jnp.float32), (frames, cell_mask, counts, step_index)
    )

    def backward_micro(totals, sliced):
        frames_item, mask_item, count_item, step_item, grad_out, kept = sliced
        lifted, enc_kept, encoder_result, foreign, joined, dec_kept = kept
        dec_scale, dec_shift, one_hot = conditioning(step_item, dec_step_table)
        grad_joined, dec_grads, dec_gscale, dec_gshift = block_backward(
            joined, dec_weights, dec_scale, dec_shift, dec_kept, grad_out
        )
        grad_skip_weight = jnp.einsum("hwk,hwc->kc", joined, grad_out, precision=HIGH)
        grad_skip_bias = jnp.sum(grad_out, axis=(0, 1))
        grad_joined = grad_joined + jnp.dot(grad_out, skip_weight.T, precision=HIGH)
        half_width = joined.shape[-1] // 2
        grad_raised = grad_joined[..., :half_width]
        grad_encoded = grad_joined[..., half_width:]
        grad_foreign_up = from_behind(grad_raised, "section", 1)
        up_pull = jax.vjp(upsample, foreign, up_weight, up_bias)[1](grad_foreign_up)
        coarse_gradient = from_behind(up_pull[0], "section", 1)
        reducer_pullback = jax.vjp(coarsen_field, encoder_result, reducer_weight, reducer_bias)[1](
            coarse_gradient
        )
        grad_encoded = grad_encoded + reducer_pullback[0]
        enc_scale, enc_shift, enc_hot = conditioning(step_item, enc_step_table)
        grad_lifted, enc_grads, enc_gscale, enc_gshift = block_backward(
            lifted, enc_weights, enc_scale, enc_shift, enc_kept, grad_encoded
        )
        grad_lifted = grad_lifted + grad_encoded
        proj_pull = jax.vjp(
            lambda frames_in, incoming_weight, incoming_bias: project_in(
                frames_in, mask_item, count_item, incoming_weight, incoming_bias
            ),
            frames_item,
            lift_weight,
            lift_bias,
        )[1](grad_lifted)
        enc_table_grad = enc_hot[:, None] * jnp.concatenate([enc_gscale, enc_gshift])[None, :]
        dec_table_grad = one_hot[:, None] * jnp.concatenate([dec_gscale, dec_gshift])[None, :]
        micro_list = (
            proj_pull[1],
            proj_pull[2],
            enc_grads[0],
            enc_grads[1],
            enc_grads[2],
            enc_table_grad,
            enc_grads[3],
            enc_grads[4],
            enc_grads[5],
            enc_grads[6],
            reducer_pullback[1],
            reducer_pullback[2],
            up_pull[1],
            up_pull[2],
            dec_grads[0],
            dec_grads[1],
            dec_grads[2],
            dec_table_grad,
            dec_grads[3],
            dec_grads[4],
            dec_grads[5],
            dec_grads[6],
            grad_skip_weight,
            grad_skip_bias,
        )
        micro_flat = flatten_all(micro_list)
        return (totals + micro_flat, proj_pull[0])

    total_size = sum((piece.size for piece in params))
    start_totals = jnp.zeros((total_size,), jnp.float32)
    flat_totals, frames_grad = lax.scan(
        backward_micro,
        start_totals,
        (frames, cell_mask, counts, step_index, cotangent, kept_all),
        reverse=True,
    )
    flat_totals = lax.psum(flat_totals, ("section", "batch", "rows"))
    grads = unflatten_all(flat_totals, params)
    return (output, frames_grad) + grads


F32 = jnp.float32
BF16 = jnp.bfloat16
MESH = pl.DeviceIdType.MESH
NN = ((1,), (0,))
NT = ((1,), (1,))
TN = ((0,), (0,))
CHUNK = 512
class Given(NamedTuple):
    frames: Any
    counts: Any
    cell_mask: Any
    step_index: Any
    lift_weight: Any
    lift_bias: Any
    enc_norm1_gain: Any
    enc_norm1_bias: Any
    enc_conv1: Any
    enc_step_table: Any
    enc_norm2_gain: Any
    enc_norm2_bias: Any
    enc_conv2: Any
    enc_conv2_bias: Any
    reducer_weight: Any
    reducer_bias: Any
    up_weight: Any
    up_bias: Any
    dec_norm1_gain: Any
    dec_norm1_bias: Any
    dec_conv1: Any
    dec_step_table: Any
    dec_norm2_gain: Any
    dec_norm2_bias: Any
    dec_conv2: Any
    dec_conv2_bias: Any
    skip_weight: Any
    skip_bias: Any
    cotangent: Any


ARGUMENTS = Given._fields
LARGE = tuple(
    dict(
        dec_conv1=0,
        up_weight=0,
        reducer_weight=0,
        dec_conv2=0,
        skip_weight=0,
        enc_conv1=0,
        enc_conv2=0,
    )
)
IN_HBM = tuple(dict(frames=0, cell_mask=0, cotangent=0)) + LARGE
IN_SMEM = tuple(dict(counts=0, step_index=0))
LATE = 64
SMALL_ROWS = dict(
    enc_conv2_bias=(0, 1),
    reducer_bias=(1, 1),
    up_bias=(2, 1),
    dec_conv2_bias=(3, 1),
    skip_bias=(3, 1),
    dec_norm1_gain=(4, 2),
    dec_norm1_bias=(6, 2),
    dec_norm2_gain=(8, 1),
    dec_norm2_bias=(9, 1),
    dec_step_table=(16, 8),
    lift_weight=(LATE, 12),
    lift_bias=(LATE + 12, 1),
    enc_norm1_gain=(LATE + 16, 1),
    enc_norm1_bias=(LATE + 17, 1),
    enc_norm2_gain=(LATE + 18, 1),
    enc_norm2_bias=(LATE + 19, 1),
    enc_step_table=(LATE + 24, 8),
)
LATE_COUNT = 32
SMALL_COUNT = LATE + LATE_COUNT
DUE = ((), (), (), (0,), (), (1, 2), (3, 0), (), (1,), (), (2, 0), (3, 1, 4, 2), (0, 3, 1), (5, 2, 4), (3, 0, 1), (2, 4, 5, 3, 6, 7), (0,), (4,))
REST = (5, 1, 0, 2, 4, 1, 8, 5, 3, 2, 6, 7, 3, 5, 6, 4, 7, 8, 6, 4, 7, 5, 6, 7, 5, 6, 7, 6, 7)
OUTPUTS = tuple(dict(output=0, frames_grad=0, gradients=0))


def split(value):
    high = value.astype(BF16)
    return high, (value - high.astype(F32)).astype(BF16)


def dot(left, right, dims=NN, precision=None):
    return lax.dot_general(
        left, right, (dims, ((), ())), precision=precision, preferred_element_type=F32
    )


def fold(value):
    half = value.shape[1] // 2
    return value[:, :half] + value[:, half:]


def fold_rows(value):
    half = value.shape[0] // 2
    return value[:half] + value[half:]


def tile_sums(value):
    return jnp.sum(value.reshape(-1, 8, value.shape[-1]), axis=0)


def column_sum(tiles):
    return jnp.sum(tiles, axis=0, keepdims=True)


def normal(value):
    bell = jnp.exp(-0.5 * value * value)
    t = 1.0 / (1.0 + 0.2316418882663604 * jnp.abs(value))
    poly = 0.5307027145
    for factor in (-0.7265760135, 0.7107068705, -0.142248368, 0.127414796):
        poly = poly * t + factor
    tail = poly * t * bell
    return jnp.where(value < 0.0, tail, 1.0 - tail), 0.3989422804014327 * bell


def dot_three(left, right, dims=NN):
    left_high, left_low = split(left)
    right_high, right_low = split(right)
    total = dot(left_high, right_high, dims)
    return total + (dot(left_high, right_low, dims) + dot(left_low, right_high, dims))


def group_ones(channels, size):
    rows = lax.broadcasted_iota(jnp.int32, (channels, channels), 0) // size
    columns = lax.broadcasted_iota(jnp.int32, (channels, channels), 1) // size
    return (rows == columns).astype(BF16)


def group_sums(first, second, ones):
    terms = []
    rest = jnp.concatenate([first, second], axis=0)
    for _ in range(3):
        term = rest.astype(BF16)
        terms.append(term)
        rest = rest - term.astype(F32)
    both = dot(jnp.concatenate(terms, axis=0), ones)
    both = both[32:48] + both[16:32] + both[:16]
    return column_sum(both[:8]), column_sum(both[8:])


class LineSwap:

    def __init__(self, line, source, target, inward, across, make):
        far = 3 - line.outer
        self.line = line
        to_inner, to_across = line.device(line.inner), line.device(line.across)
        to_outer = line.device(line.outer)
        here = target(line.here)
        self.to_far = make(source(3 - line.here), inward.at[1], to_inner)
        self.to_second = make(source(3 - line.inner), inward.at[0], to_inner)
        self.to_inner = make(source(line.inner), here, to_inner)
        self.for_far = make(source(far), across.at[0], to_across)
        self.to_across = make(source(line.across), here, to_across)
        self.to_outer = make(source(line.outer), here, to_outer)
        self.pass_far = make(inward.at[1], across.at[1], to_across)
        self.pass_second = make(inward.at[0], target(line.outer), to_across)
        self.pass_across = make(across.at[0], target(line.across), to_outer)
        self.pass_opposite = make(across.at[1], target(far), to_outer)

    def first(self):
        @pl.when(self.line.edge)
        def _():
            for copy in (self.to_far, self.to_second, self.to_inner):
                copy.start()

        @pl.when(self.line.middle)
        def _():
            for copy in (self.for_far, self.to_across, self.to_outer):
                copy.start()

    def second(self):
        @pl.when(self.line.middle)
        def _():
            self.for_far.wait_recv()
            self.pass_across.start()
            self.to_far.wait_recv()
            self.pass_far.start()
            self.to_second.wait_recv()
            self.pass_second.start()

    def third(self):
        @pl.when(self.line.middle)
        def _():
            self.pass_far.wait_recv()
            self.pass_opposite.start()

    def arrive(self):
        @pl.when(self.line.edge)
        def _():
            for copy in (self.to_outer, self.pass_across, self.pass_opposite):
                copy.wait_recv()

        @pl.when(self.line.middle)
        def _():
            for copy in (self.to_inner, self.to_across, self.pass_second):
                copy.wait_recv()

    def sent(self):
        @pl.when(self.line.edge)
        def _():
            for copy in (self.to_far, self.to_second, self.to_inner):
                copy.wait_send()

        @pl.when(self.line.middle)
        def _():
            for copy in (self.for_far, self.to_across, self.to_outer):
                copy.wait_send()
            for copy in (self.pass_far, self.pass_second, self.pass_across, self.pass_opposite):
                copy.wait_send()


class Exchange:

    def __init__(self, place, start, rows, landing, first_sem):
        self.place, self.start, self.rows, self.landing = place, start, rows, landing
        self.sem = first_sem
        self.stage = 0
        self.copies = []
        self.waiting = []
        self.group = place.plane_group
        self.half = rows // 2
        self.base = start + place.core * self.half
        self._finish(self.half)

    def _finish(self, size):
        self.part = size // self.group.count
        self.own = self.base + self.group.here * self.part

    def count(self):
        return 2 + 2 * (self.group.count - 1) + 3

    def land_rows(self):
        return self.half + (self.group.count + 1) * self.part

    def _copy(self, source, target, device, only=None):
        place = self.place
        copy = pltpu.make_async_remote_copy(
            src_ref=source,
            dst_ref=target,
            send_sem=place.send.at[self.sem],
            recv_sem=place.recv.at[self.sem],
            device_id=device,
            device_id_type=MESH,
        )
        self.sem += 1
        if only is None:
            copy.start()
            self.waiting.append(copy)
        self.copies.append((copy, only))
        return copy

    def _wait(self):
        for copy in self.waiting:
            copy.wait_recv()
        self.waiting = []

    def _rows(self, at, size):
        return pl.ds(pl.multiple_of(at, 8), size)

    def _swap(self):
        place = self.place
        other = self._rows(self.start + (1 - place.core) * self.half, self.half)
        self.land = self.landing
        self.landing += self.half
        self._copy(
            place.sums.at[other], place.landing.at[pl.ds(self.land, self.half)], place.partner
        )

    def _add_swap(self):
        place = self.place
        block = 64 if self.half % 64 == 0 else 32

        def step(i, carry):
            here = self._rows(self.base + i * block, block)
            there = self._rows(self.land + i * block, block)
            place.sums[here] = place.sums[here] + place.landing[there]
            return carry

        lax.fori_loop(0, self.half // block, step, 0)

    def _scatter(self, group, base, size):
        place = self.place
        self.land = self.landing
        for k in range(1, group.count):
            to = lax.rem(group.here + k, group.count)
            self._copy(
                place.sums.at[self._rows(base + to * size, size)],
                place.landing.at[pl.ds(self.landing, size)],
                group.device(to),
            )
            self.landing += size

    def _total(self, group, own, size, target):
        place = self.place
        block = 16 if size % 16 == 0 else 8

        def step(i, carry):
            here = self._rows(own + i * block, block)
            total = place.sums[here]
            for k in range(group.count - 1):
                there = self._rows(self.land + k * size + i * block, block)
                total = total + place.landing[there]
            target[here] = total
            return carry

        lax.fori_loop(0, size // block, step, 0)

    def _gather(self, group, own, size):
        final = self.place.final
        here = self._rows(own, size)
        for k in range(1, group.count):
            to = lax.rem(group.here + k, group.count)
            self._copy(final.at[here], final.at[here], group.device(to))

    def _steps(self):
        place, group = self.place, self.group
        yield self._swap()
        self._wait()
        self._add_swap()
        yield from self._both()
        final = place.final
        here = self._rows(self.base, self.half)
        self._copy(final.at[here], final.at[here], place.partner)
        yield
        self._wait()
        yield

    def _both(self):
        place, group = self.place, self.group
        self._scatter(group, self.base, self.part)
        yield
        self._wait()
        self._total(group, self.own, self.part, place.sums)
        yield from self._line()
        self._gather(group, self.own, self.part)
        yield
        self._wait()

    def _line(self):
        place, line = self.place, self.place.line
        sums, final, landing = place.sums, place.final, place.landing
        part, own = self.part, self._rows(self.own, self.part)
        inward, across = pl.ds(self.landing, part), pl.ds(self.landing + part, part)
        self.landing += 2 * part
        block = 16 if part % 16 == 0 else 8

        def add(at, target):
            def step(i, carry):
                here = self._rows(self.own + i * block, block)
                target[here] = sums[here] + landing[pl.ds(at + i * block, block)]
                return carry

            lax.fori_loop(0, part // block, step, 0)

        first = self._copy(sums.at[own], landing.at[inward], line.device(line.inner), line.edge)
        second = self._copy(sums.at[own], landing.at[across], line.device(line.across), line.middle)
        third = self._copy(final.at[own], final.at[own], line.device(line.outer), line.middle)
        pl.when(line.edge)(first.start)
        yield

        @pl.when(line.middle)
        def _():
            first.wait_recv()
            add(self.landing - 2 * part, sums)
            second.start()

        yield

        @pl.when(line.middle)
        def _():
            second.wait_recv()
            add(self.landing - part, final)
            third.start()

        yield
        pl.when(line.edge)(third.wait_recv)

    def advance(self):
        if self.stage == 0:
            self.steps = self._steps()
        self.stage += 1
        next(self.steps)

    def done(self):
        return self.stage == 8


class SmallExchange(Exchange):

    def count(self):
        return self.place.cores_group.count + self.place.line.count - 2

    def land_rows(self):
        return self.rows * (self.place.cores_group.count + self.place.line.count)

    def _share(self, group, source):
        place = self.place
        self.land = self.landing
        self.landing += group.count * self.rows
        own = self._rows(self.land + group.here * self.rows, self.rows)
        place.landing[own] = source[...]
        for k in range(1, group.count):
            to = lax.rem(group.here + k, group.count)
            self._copy(source, place.landing.at[own], group.device(to))

    def _sum(self, group):
        total = None
        for k in range(group.count):
            part = self.place.landing[pl.ds(self.land + k * self.rows, self.rows)]
            total = part if total is None else total + part
        return total

    def _steps(self):
        place = self.place
        here = pl.ds(self.start, self.rows)
        self._share(place.line, place.sums.at[here])
        yield
        self._wait()
        place.small[...] = self._sum(place.line)
        self._share(place.cores_group, place.small)
        yield
        self._wait()
        place.final[here] = self._sum(place.cores_group)
        yield

    def done(self):
        return self.stage == 3


def layout_of(shapes):
    starts = {}
    at = 0
    for name in LARGE:
        starts[name] = at
        at += getattr(shapes, name)[0]
    small = at
    begins = SimpleNamespace(**starts)
    late = small + LATE
    tap = shapes.dec_conv2[0] // 3
    part = shapes.dec_conv1[0] // 3
    conv1, up = begins.dec_conv1, begins.up_weight
    edges = (
        (begins.dec_conv2, begins.enc_conv1),
        (conv1, conv1 + part),
        (conv1 + part, conv1 + 2 * part),
        (conv1 + 2 * part, up),
        (up, begins.dec_conv2),
        (begins.enc_conv2, late),
        (begins.enc_conv1, begins.enc_conv1 + 2 * tap),
        (begins.enc_conv1 + 2 * tap, begins.enc_conv2),
        (late, late + LATE_COUNT),
    )
    runs = [(first, last - first) for first, last in edges]
    return starts, small, late + LATE_COUNT, runs


def item_kernel(sizes, scratch_names, *refs):
    line, strip, width, shapes, big_layout = sizes
    begins, small_at, total_rows, runs = big_layout
    starts = SimpleNamespace(**begins)
    inputs = Given(*refs[: len(ARGUMENTS)])
    refs = refs[len(ARGUMENTS) :]
    output_names = OUTPUTS
    outputs = SimpleNamespace(**dict(zip(output_names, refs)))
    scratch = SimpleNamespace(**dict(zip(scratch_names, refs[len(output_names) :])))

    def w_of(name):
        return getattr(scratch, name)

    height = strip * line
    cells = height * width
    c = inputs.lift_weight.shape[1]
    strip_cells = strip * width
    history = inputs.frames.shape[1]

    core = lax.axis_index("section")
    plane = lax.axis_index("batch")
    row = lax.axis_index("rows")
    middle = lax.rem(row + 1, 4) // 2

    def device_at(to):
        return (core, plane, to)

    place = SimpleNamespace(
        core=core,
        partner=(1 - core, plane, row),
        line=SimpleNamespace(
            count=line,
            here=row,
            device=device_at,
            middle=middle == 1,
            edge=middle == 0,
            inner=1 + row // 2,
            across=3 - row,
            outer=3 * (row // 2),
        ),
        plane_group=SimpleNamespace(
            count=4, here=plane, device=lambda to: (core, to, row)
        ),
        cores_group=SimpleNamespace(
            count=8,
            here=core * 4 + plane,
            device=lambda to: (to // 4, lax.rem(to, 4), row),
        ),
        small=scratch.small,
        sums=scratch.sums,
        final=scratch.final,
        landing=scratch.landing,
        send=scratch.send,
        recv=scratch.recv,
    )
    local_sem = scratch.local

    frames_in, mask_in, cot = scratch.frames_in, scratch.mask_in, scratch.cot
    here_rows = pl.ds(pl.multiple_of(row * strip_cells, strip_cells), strip_cells)
    frames_from, mask_from, cot_from = scratch.frames_from, scratch.mask_from, scratch.cot_from
    staged = (
        pltpu.make_async_copy(inputs.frames, frames_from, local_sem.at[7]),
        pltpu.make_async_copy(inputs.cell_mask, mask_from, local_sem.at[8]),
        pltpu.make_async_copy(inputs.cotangent, cot_from, local_sem.at[9]),
    )
    for copy in staged:
        copy.start()

    weight_copies = {}
    for k, name in enumerate(LARGE):
        copy = pltpu.make_async_copy(getattr(inputs, name), w_of(name), local_sem.at[k])
        weight_copies[name] = copy
        copy.start()

    barrier = pltpu.get_barrier_semaphore()
    peers = [device_at(lax.rem(row + k, line)) for k in range(1, line)]
    cores_group = place.cores_group
    for k in range(1, 8):
        peers.append(cores_group.device(lax.rem(cores_group.here + k, 8)))
    for device in peers:
        pl.semaphore_signal(barrier, inc=1, device_id=device, device_id_type=MESH)
    pl.semaphore_wait(barrier, len(peers))

    next_sem = 0

    def make(source, target, device):
        nonlocal next_sem
        copy = pltpu.make_async_remote_copy(
            src_ref=source,
            dst_ref=target,
            send_sem=scratch.send.at[next_sem],
            recv_sem=scratch.recv.at[next_sem],
            device_id=device,
            device_id_type=MESH,
        )
        next_sem += 1
        return copy

    def send(source, target, device):
        copy = make(source, target, device)
        copy.start()
        return copy

    def strip_of(ref, to):
        return ref.at[pl.ds(pl.multiple_of(to * strip_cells, strip_cells), strip_cells)]

    frame_copies, output_copies = [], []
    for copy in staged[:2]:
        copy.wait()
    for k in range(1, line):
        to = lax.rem(row + k, line)
        device = device_at(to)
        frame_copies.append(send(frames_from.at[to], frames_in.at[row], device))
        frame_copies.append(send(mask_from.at[to], mask_in.at[row], device))
    staged[2].wait()
    cot_swap = LineSwap(
        place.line,
        lambda to: cot_from.at[to],
        lambda source: strip_of(cot, source),
        scratch.cot_inward,
        scratch.cot_across,
        make,
    )
    cot_swap.first()

    copied = SimpleNamespace(**weight_copies)
    def put_pair(target, block, value):
        high, low = split(value)
        rows = pl.ds(pl.multiple_of(block * c, c), c)
        target[rows, 0:c] = high
        target[rows, c : 2 * c] = low

    def stack_conv(source, half, depth, forward, backward):
        def step(t, carry):
            value = source[pl.ds(pl.multiple_of(t * depth + half * c, c), c), :]
            turned = value.T
            for k in range(2):
                put_pair(forward, 2 * t + k, value)
                put_pair(backward, 16 - 2 * t + k, turned)
            return carry

        lax.fori_loop(0, 9, step, 0)

    copied.enc_conv1.wait()
    stack_conv(scratch.enc_conv1, 0, c, scratch.fe1, scratch.be1)
    copied.enc_conv2.wait()
    stack_conv(scratch.enc_conv2, 0, c, scratch.fe2, scratch.be2)
    copied.reducer_weight.wait()
    for k in range(4):
        value = scratch.reducer_weight[k * c : (k + 1) * c, :]
        turned = value.T
        for block in (k, k + 4):
            put_pair(scratch.f_down, block, value)
        for block in (0, 1):
            put_pair(scratch.b_down.at[k], block, turned)
    copied.up_weight.wait()
    for k in range(4):
        value = scratch.up_weight[k * c : (k + 1) * c, :]
        turned = value.T
        for block in (0, 1):
            put_pair(scratch.f_up.at[k], block, value)
        for block in (k, k + 4):
            put_pair(scratch.b_up, block, turned)
    copied.dec_conv1.wait()
    stack_conv(scratch.dec_conv1, 0, 2 * c, scratch.fd1a, scratch.bd1a)
    stack_conv(scratch.dec_conv1, 1, 2 * c, scratch.fd1b, scratch.bd1b)
    copied.dec_conv2.wait()
    stack_conv(scratch.dec_conv2, 0, c, scratch.fd2, scratch.bd2)
    copied.skip_weight.wait()
    for half in range(2):
        value = scratch.skip_weight[half * c : (half + 1) * c, :]
        turned = value.T
        for block in (half, half + 2):
            put_pair(scratch.f_skip, block, value)
        for block in (0, 1):
            put_pair(scratch.b_skip.at[half], block, turned)

    for buffer in (scratch.xe1, scratch.xe2, scratch.xd1a, scratch.xd1b, scratch.xd2, scratch.xg):
        edge = jnp.zeros((width, 6 * c), BF16)
        buffer[0:width, :] = edge
        buffer[cells + width : cells + 2 * width, :] = edge

    lift = scratch.lift
    lift[...] = jnp.zeros(lift.shape, F32)
    lift[0:history, :] = inputs.lift_weight[...]
    lift[history : history + 1, :] = inputs.lift_bias[...]

    block = 2 * width
    column = lax.rem(lax.broadcasted_iota(jnp.int32, (block, c), 0), width)
    at_first, at_last = column == 0, column == width - 1
    zeros8 = jnp.zeros((8, c), F32)
    ones16 = group_ones(c, c // GROUPS)
    ones32 = group_ones(c, 2 * c // GROUPS)
    count16 = float(cells * (c // GROUPS))
    count32 = float(cells * (2 * c // GROUPS))

    def grid_rows(step, carry=0):
        return lax.fori_loop(0, cells // block, step, carry, unroll=2)

    def row_at(h):
        return pl.ds(pl.multiple_of(h * block, block), block)

    def chunk_at(i):
        return pl.ds(pl.multiple_of(i * CHUNK, CHUNK), CHUNK)

    def put_row(target, h, value):
        rows = pl.ds(pl.multiple_of(h * block + width, width), block)
        left = jnp.where(at_first, 0.0, pltpu.roll(value, 1, 0))
        right = jnp.where(at_last, 0.0, pltpu.roll(value, block - 1, 0))
        for b, piece in enumerate((left, value, right)):
            high, low = split(piece)
            target[rows, 2 * b * c : (2 * b + 1) * c] = high
            target[rows, (2 * b + 1) * c : (2 * b + 2) * c] = low

    def put_turned(target, columns, value, first=0, second=1):
        high, low = split(value.T)
        target[first * c : (first + 1) * c, columns] = high
        target[second * c : (second + 1) * c, columns] = low

    def conv_chunk(pairs, i):
        total = None
        for data, weight in pairs:
            taps = []
            for a in range(3):
                rows = pl.ds(pl.multiple_of(i * CHUNK + a * width, width), CHUNK)
                taps.append(data[rows, :])
            part = dot(jnp.concatenate(taps, axis=1), weight[...])
            total = part if total is None else total + part
        return total

    def norm_of(first, second, ones, count):
        one, two = group_sums(first, second, ones)
        mean = one / count
        return mean, lax.rsqrt(two / count - mean * mean + EPS)

    def activate(source, target, turned, slope, scale, shift):
        def step(h, carry):
            value = source[row_at(h), :] * scale + shift
            below, density = normal(value)
            slope[row_at(h), :] = below + value * density
            value = value * below
            put_row(target, h, value)
            put_turned(turned, row_at(h), value)
            return carry

        grid_rows(step)

    def conv_norm(pairs, target):
        def step(i, carry):
            value = fold(conv_chunk(pairs, i))
            target[chunk_at(i), :] = value
            return carry[0] + tile_sums(value), carry[1] + tile_sums(value * value)

        return lax.fori_loop(0, cells // CHUNK, step, (zeros8, zeros8))

    def sums_of(source):
        def step(h, carry):
            value = source[row_at(h), :]
            return carry[0] + tile_sums(value), carry[1] + tile_sums(value * value)

        return grid_rows(step, (zeros8, zeros8))

    step_here = jnp.full((1, c), inputs.step_index[row], jnp.int32)

    def condition(table):
        total = jnp.zeros((1, 2 * c), F32)
        chosen = jnp.concatenate([step_here, step_here], axis=1)
        for s in range(table.shape[0]):
            total = total + jnp.where(chosen == s, table[s : s + 1, :], 0.0)
        return total[:, :c], total[:, c:]

    frames_in[row] = frames_from[row]
    mask_in[row] = mask_from[row]
    for copy in frame_copies:
        copy.wait_recv()
    fields = scratch.fields
    fields[...] = jnp.zeros(fields.shape, F32)
    frame_of = lax.broadcasted_iota(jnp.int32, (history, width), 0) // FIELDS
    keep = (frame_of >= HIST - inputs.counts[row]).astype(F32)
    masks = []
    for source in range(line):
        for k in range(strip):
            columns = slice((source * strip + k) * width, (source * strip + k + 1) * width)
            mask = mask_in[source, k : k + 1, :].astype(F32)
            masks.append(mask)
            fields[0:history, columns] = frames_in[source, :, k, :] * keep * mask
            fields[history : history + 1, columns] = mask
    lifted = scratch.lifted
    lifted[...] = dot_three(fields[...], lift[...], TN)

    enc_scale, enc_shift = condition(inputs.enc_step_table)
    dec_scale, dec_shift = condition(inputs.dec_step_table)

    mean_e1, inv_e1 = norm_of(*sums_of(lifted), ones16, count16)
    gain_e1, bias_e1 = inputs.enc_norm1_gain[...], inputs.enc_norm1_bias[...]
    a_e1 = inv_e1 * gain_e1
    activate(lifted, scratch.xe1, scratch.te1, scratch.slope_e1, a_e1, bias_e1 - mean_e1 * a_e1)
    middle_e = scratch.middle_e
    mean_e2, inv_e2 = norm_of(
        *conv_norm([(scratch.xe1, scratch.fe1)], middle_e), ones16, count16
    )
    gain_e2, bias_e2 = inputs.enc_norm2_gain[...], inputs.enc_norm2_bias[...]
    a_e2 = inv_e2 * gain_e2
    activate(
        middle_e,
        scratch.xe2,
        scratch.te2,
        scratch.slope_e2,
        a_e2 * (1.0 + enc_scale),
        (bias_e2 - mean_e2 * a_e2) * (1.0 + enc_scale) + enc_shift,
    )
    cot_swap.second()
    encoded = scratch.encoded
    conv2_bias = inputs.enc_conv2_bias[...]
    joined = scratch.joined

    def encode(i, carry):
        value = fold(conv_chunk([(scratch.xe2, scratch.fe2)], i))
        value = value + conv2_bias + lifted[chunk_at(i), :]
        encoded[chunk_at(i), :] = value
        high, low = split(value)
        joined[chunk_at(i), c : 2 * c] = high
        joined[chunk_at(i), 3 * c : 4 * c] = low
        put_turned(scratch.turned, chunk_at(i), value, 1, 3)
        return carry[0] + tile_sums(value), carry[1] + tile_sums(value * value)

    sums_enc = lax.fori_loop(0, cells // CHUNK, encode, (zeros8, zeros8))

    half_cells, quarter = cells // 2, cells // 4

    def pick(source):
        pieces = []
        for b in range(2):
            value = source[pl.ds(b, half_cells, stride=2), :]
            value = value.reshape(height // 2, 2, width // 2, c)
            pieces.append([value[:, a].reshape(quarter, c) for a in range(2)])
        return [pieces[b][a] for a in range(2) for b in range(2)]

    def place_cells(target, pieces):
        for b in range(2):
            both = [pieces[2 * a + b].reshape(height // 2, 1, width // 2, c) for a in range(2)]
            value = jnp.concatenate(both, axis=1).reshape(half_cells, c)
            target[pl.ds(b, half_cells, stride=2), :] = value

    x_down = scratch.x_down
    for k, piece in enumerate(pick(encoded)):
        high, low = split(piece)
        x_down[:, k * c : (k + 1) * c] = high
        x_down[:, (k + 4) * c : (k + 5) * c] = low
    lowered = fold(dot(x_down[...], scratch.f_down[...])) + inputs.reducer_bias[...]
    x_up = scratch.x_up
    high, low = split(lowered)
    x_up[:, 0:c] = high
    x_up[:, c : 2 * c] = low
    raised = scratch.raised
    up_bias = inputs.up_bias[...]
    place_cells(
        raised, [fold(dot(x_up[...], scratch.f_up[k])) + up_bias for k in range(4)]
    )

    def raise_row(h, carry):
        value = raised[row_at(h), :]
        high, low = split(value)
        joined[row_at(h), 0:c] = high
        joined[row_at(h), 2 * c : 3 * c] = low
        put_turned(scratch.turned, row_at(h), value, 0, 2)
        return carry[0] + tile_sums(value), carry[1] + tile_sums(value * value)

    sums_raised = grid_rows(raise_row, (zeros8, zeros8))

    halves = []
    for half, (source, sums) in enumerate(((raised, sums_raised), (encoded, sums_enc))):
        mean, inv = norm_of(*sums, ones32, count32)
        gain = inputs.dec_norm1_gain[half : half + 1, :]
        bias = inputs.dec_norm1_bias[half : half + 1, :]
        scale = inv * gain
        activate(
            source,
            (scratch.xd1a, scratch.xd1b)[half],
            scratch.td1.at[2 * c * half : 2 * c * (half + 1)],
            (scratch.slope_d1a, scratch.slope_d1b)[half],
            scale,
            bias - mean * scale,
        )
        halves.append((source, mean, inv, gain))
    middle_d = scratch.middle_d
    pairs = [(scratch.xd1a, scratch.fd1a), (scratch.xd1b, scratch.fd1b)]
    mean_d2, inv_d2 = norm_of(*conv_norm(pairs, middle_d), ones16, count16)
    cot_swap.third()
    gain_d2, bias_d2 = inputs.dec_norm2_gain[...], inputs.dec_norm2_bias[...]
    a_d2 = inv_d2 * gain_d2
    activate(
        middle_d,
        scratch.xd2,
        scratch.td2,
        scratch.slope_d2,
        a_d2 * (1.0 + dec_scale),
        (bias_d2 - mean_d2 * a_d2) * (1.0 + dec_scale) + dec_shift,
    )
    result = scratch.result
    last_bias = inputs.dec_conv2_bias[...] + inputs.skip_bias[...]

    def decode(i, carry):
        value = conv_chunk([(scratch.xd2, scratch.fd2)], i)
        value = value + dot(joined[chunk_at(i), :], scratch.f_skip[...])
        result[chunk_at(i), :] = fold(value) + last_bias
        return carry

    lax.fori_loop(0, cells // CHUNK, decode, 0)
    output_here, frames_here = scratch.output_here, scratch.frames_here
    output_here[row] = result[here_rows]
    output_swap = LineSwap(
        place.line,
        lambda to: strip_of(result, to),
        lambda source: output_here.at[source],
        scratch.output_inward,
        scratch.output_across,
        make,
    )
    output_swap.first()

    exchanges = []
    waiting_runs = list(runs)
    landing_at = 0
    sem_at = 3 * (line - 1) + 20
    sums, final = scratch.sums, scratch.final

    def begin():
        nonlocal landing_at, sem_at
        start, rows = waiting_runs.pop(0)
        kind = Exchange if waiting_runs else SmallExchange
        exchange = kind(place, start, rows, landing_at, sem_at)
        landing_at += exchange.land_rows()
        sem_at += exchange.count()
        exchanges.append(exchange)
        exchange.advance()

    final_copies = []

    def advance(k):
        exchange = exchanges[k]
        exchange.advance()
        if exchange.done():
            rows = pl.ds(exchange.start, exchange.rows)
            copy = pltpu.make_async_copy(
                final.at[rows], outputs.gradients.at[rows], local_sem.at[11 + k]
            )
            copy.start()
            final_copies.append(copy)

    due = list(DUE)

    def point():
        for k in due.pop(0):
            advance(k)

    def small_row(k, value):
        sums[small_at + k : small_at + k + 1, :] = value

    def spread_grad(source):
        def step(h, carry):
            value = source[row_at(h), :]
            put_row(scratch.xg, h, value)
            return carry + tile_sums(value)

        return grid_rows(step, zeros8)

    def weight_grad(turned, at, depth):
        def step(a, carry):
            rows = pl.ds(pl.multiple_of((2 - a) * width, width), cells)
            both = dot(turned[...], scratch.xg[rows, :])
            for half in range(depth // c):
                part = fold_rows(both[2 * c * half : 2 * c * (half + 1)])
                for b in range(3):
                    to = pl.multiple_of(at + (3 * a + b) * depth + half * c, c)
                    columns = part[:, (2 - b) * 2 * c : (3 - b) * 2 * c]
                    sums[pl.ds(to, c), :] = fold(columns)
            return carry

        lax.fori_loop(0, 3, step, 0)

    def back_conv(weight, slope, target, source, mean, inv):
        def step(i, carry):
            value = fold(conv_chunk([(scratch.xg, weight)], i)) * slope[chunk_at(i), :]
            target[chunk_at(i), :] = value
            normed = (source[chunk_at(i), :] - mean) * inv
            return carry[0] + tile_sums(value), carry[1] + tile_sums(value * normed)

        sums_in = lax.fori_loop(0, cells // CHUNK, step, (zeros8, zeros8))
        point()
        return sums_in

    def norm_grad(sums_in, scale, ones, count):
        one, two = group_sums(sums_in[0] * scale, sums_in[1] * scale, ones)
        return one / count, two / count

    cot[here_rows] = cot_from[row]
    cot_swap.arrive()
    total_cot = column_sum(spread_grad(cot))
    weight_grad(scratch.td2, starts.dec_conv2, c)
    part = fold(dot(scratch.turned[...], scratch.xg[width : cells + width, 2 * c : 4 * c]))
    sums[starts.skip_weight : starts.skip_weight + 2 * c, :] = fold_rows(part)
    small_row(3, total_cot)
    begin()

    grad = scratch.grad
    sums_d2 = back_conv(scratch.bd2, scratch.slope_d2, grad, middle_d, mean_d2, inv_d2)
    side_grads = (scratch.grad_a, scratch.grad_b)
    for half in range(2):

        def skip_back(i, carry, half=half):
            rows = pl.ds(pl.multiple_of(i * CHUNK + width, width), CHUNK)
            value = dot(scratch.xg[rows, 2 * c : 4 * c], scratch.b_skip[half])
            side_grads[half][chunk_at(i), :] = fold(value)
            return carry

        lax.fori_loop(0, cells // CHUNK, skip_back, 0)
    point()

    def table_rows(k, sums_in, gain, bias, one_plus):
        plain, times = column_sum(sums_in[0]), column_sum(sums_in[1])
        for s in range(inputs.enc_step_table.shape[0]):
            small_row(k + 2 * s, jnp.where(step_here == s, gain * times + bias * plain, 0.0))
            small_row(k + 2 * s + 1, jnp.where(step_here == s, plain, 0.0))
        return one_plus * times, one_plus * plain

    def middle_grad(source, mean, inv, scale, sums_in):
        zero, slope = norm_grad(sums_in, scale, ones16, count16)

        def step(h, carry):
            normed = (source[row_at(h), :] - mean) * inv
            value = inv * (grad[row_at(h), :] * scale - zero - normed * slope)
            put_row(scratch.xg, h, value)
            return carry

        grid_rows(step)

    gain_row, bias_row = table_rows(16, sums_d2, gain_d2, bias_d2, 1.0 + dec_scale)
    small_row(8, gain_row)
    small_row(9, bias_row)
    middle_grad(middle_d, mean_d2, inv_d2, gain_d2 * (1.0 + dec_scale), sums_d2)
    point()
    output_swap.second()
    weight_grad(scratch.td1, starts.dec_conv1, 2 * c)
    point()
    for _ in range(3):
        begin()

    for half, (source, mean, inv, gain) in enumerate(halves):
        sums_in = back_conv(
            (scratch.bd1a, scratch.bd1b)[half],
            (scratch.slope_d1a, scratch.slope_d1b)[half],
            grad,
            source,
            mean,
            inv,
        )
        small_row(4 + half, column_sum(sums_in[1]))
        small_row(6 + half, column_sum(sums_in[0]))
        zero, slope = norm_grad(sums_in, gain, ones32, count32)
        target = side_grads[half]

        def input_grad(h, carry):
            normed = (source[row_at(h), :] - mean) * inv
            value = inv * (grad[row_at(h), :] * gain - zero - normed * slope)
            value = target[row_at(h), :] + value
            target[row_at(h), :] = value
            return carry + tile_sums(value)

        total = grid_rows(input_grad, zeros8)
        if half == 0:
            small_row(2, column_sum(total))
        point()

    output_swap.third()
    grad_raised, grad_encoded = side_grads
    x_grad_up = scratch.x_grad_up
    for k, piece in enumerate(pick(grad_raised)):
        high, low = split(piece)
        x_grad_up[:, k * c : (k + 1) * c] = high
        x_grad_up[:, (k + 4) * c : (k + 5) * c] = low
    grad_lowered = fold(dot(x_grad_up[...], scratch.b_up[...]))
    small_row(1, jnp.sum(grad_lowered, axis=0, keepdims=True))
    x_grad_low = scratch.x_grad_low
    high, low = split(grad_lowered)
    x_grad_low[:, 0:c] = high
    x_grad_low[:, c : 2 * c] = low
    point()
    part = fold(fold_rows(dot(x_up[...], x_grad_up[...], TN)))
    for k in range(4):
        at = starts.up_weight + k * c
        sums[at : at + c, :] = part[:, k * c : (k + 1) * c]
    part = fold_rows(fold(dot(x_down[...], x_grad_low[...], TN)))
    sums[starts.reducer_weight : starts.reducer_weight + 4 * c, :] = part
    point()
    begin()
    place_cells(
        grad, [fold(dot(x_grad_low[...], scratch.b_down[k])) for k in range(4)]
    )

    def join_row(h, carry):
        value = grad_encoded[row_at(h), :] + grad[row_at(h), :]
        grad_encoded[row_at(h), :] = value
        put_row(scratch.xg, h, value)
        return carry + tile_sums(value)

    small_row(0, column_sum(grid_rows(join_row, zeros8)))
    for k in range(10, 16):
        small_row(k, jnp.zeros((1, c), F32))
    sums[small_at + 24 : small_at + LATE, :] = jnp.zeros((LATE - 24, c), F32)
    point()
    weight_grad(scratch.te2, starts.enc_conv2, c)
    point()
    begin()
    sums_e2 = back_conv(scratch.be2, scratch.slope_e2, grad, middle_e, mean_e2, inv_e2)
    gain_row, bias_row = table_rows(LATE + 24, sums_e2, gain_e2, bias_e2, 1.0 + enc_scale)
    small_row(LATE + 18, gain_row)
    small_row(LATE + 19, bias_row)
    middle_grad(middle_e, mean_e2, inv_e2, gain_e2 * (1.0 + enc_scale), sums_e2)
    point()
    weight_grad(scratch.te1, starts.enc_conv1, c)
    point()
    for _ in range(2):
        begin()
    sums_e1 = back_conv(scratch.be1, scratch.slope_e1, grad, lifted, mean_e1, inv_e1)
    small_row(LATE + 16, column_sum(sums_e1[1]))
    small_row(LATE + 17, column_sum(sums_e1[0]))
    zero, slope = norm_grad(sums_e1, gain_e1, ones16, count16)

    def lifted_grad(h, carry):
        normed = (lifted[row_at(h), :] - mean_e1) * inv_e1
        value = inv_e1 * (grad[row_at(h), :] * gain_e1 - zero - normed * slope)
        grad[row_at(h), :] = grad_encoded[row_at(h), :] + value
        return carry

    grid_rows(lifted_grad)
    point()

    late_at = small_at + LATE
    sums[late_at : late_at + 16, :] = dot_three(fields[...], grad[...])
    sums[late_at + 20 : late_at + 24, :] = jnp.zeros((4, c), F32)
    point()
    begin()
    back = dot_three(lift[...], grad[...], NT)
    frames_out = scratch.frames_out
    for source in range(line):
        for k in range(strip):
            h = source * strip + k
            value = back[0:history, h * width : (h + 1) * width]
            frames_out[source, :, k, :] = value * keep * masks[h]
    frames_here[row] = frames_out[row]
    for k in range(1, line):
        to = lax.rem(row + k, line)
        output_copies.append(
            send(frames_out.at[to], frames_here.at[row], device_at(to))
        )

    output_swap.arrive()
    own_output = pltpu.make_async_copy(output_here, outputs.output, local_sem.at[10])
    own_output.start()
    for k in REST:
        advance(k)
    assert not due and all(exchange.done() for exchange in exchanges)

    for copy in output_copies:
        copy.wait_recv()
    own_frames = pltpu.make_async_copy(
        frames_here, outputs.frames_grad, local_sem.at[11 + len(runs)]
    )
    own_frames.start()
    own_output.wait()
    own_frames.wait()
    for copy in final_copies:
        copy.wait()
    for copy in frame_copies + output_copies:
        copy.wait_send()
    cot_swap.sent()
    output_swap.sent()
    for exchange in exchanges:
        for copy, only in exchange.copies:
            if only is None:
                copy.wait_send()
            else:
                pl.when(only)(copy.wait_send)


def write_kernel(layout, *refs):
    shapes, starts, small_at = layout
    output, frames_grad, gradients = refs[:3]
    outputs = refs[3:-4]
    output_here, frames_here, gradients_here, sem = refs[-4:]
    c = gradients.shape[1]
    moves = [(frames_grad, frames_here, outputs[1])]
    for k, name in enumerate(LARGE):
        rows = pl.ds(starts[name], shapes[name][0])
        moves.append((gradients.at[rows], gradients_here.at[rows], outputs[2 + k]))
    moves.append((output, output_here, outputs[0]))
    small = pl.ds(small_at, SMALL_COUNT)
    first = pltpu.make_async_copy(gradients.at[small], gradients_here.at[small], sem.at[0])
    first.start()
    arriving, leaving = [], []
    for k, (source, here, _) in enumerate(moves):
        arriving.append(pltpu.make_async_copy(source, here, sem.at[1 + 2 * k]))
        arriving[-1].start()
    first.wait()
    for target, (k, rows) in zip(outputs[2 + len(LARGE) :], SMALL_ROWS.values()):
        at = small_at + k
        if rows == 8:
            for s in range(target.shape[0]):
                target[s : s + 1, 0:c] = gradients_here[at + 2 * s : at + 2 * s + 1, :]
                target[s : s + 1, c : 2 * c] = gradients_here[at + 2 * s + 1 : at + 2 * s + 2, :]
        else:
            target[...] = gradients_here[at : at + rows, :]
    for k, (_, here, target) in enumerate(moves):
        arriving[k].wait()
        leaving.append(pltpu.make_async_copy(here, target, sem.at[2 + 2 * k]))
        leaving[-1].start()
    for copy in leaving:
        copy.wait()


def whole_items(shape, *arguments):
    line = shape["rows"]
    whole = Given(*arguments)
    given = whole._asdict()
    frames, cotangent = whole.frames, whole.cotangent
    items, history, strip, width = frames.shape
    c = cotangent.shape[-1]
    cells = strip * line * width
    flat = {}
    for name, value in given.items():
        if value is cotangent:
            value = value.reshape(items, strip * width, c)
        elif name in LARGE:
            value = value.reshape(-1, c)
        elif value.ndim == 1 and name not in IN_SMEM:
            value = value.reshape(-1, c)
        flat[name] = value
    shapes = {name: flat[name].shape for name in LARGE}
    big_layout = layout_of(SimpleNamespace(**shapes))
    starts, small_at, total_rows, runs = big_layout
    copies = 20 + 3 * (line - 1) + len(runs) * (8 + 2 * (line - 1)) + 6
    landing = sum(rows // 2 + 5 * rows // 8 for _, rows in runs) + LATE_COUNT * (8 + line)
    shifted = pltpu.VMEM((cells + 2 * width, 6 * c), BF16)
    forward = pltpu.VMEM((18 * c, 2 * c), BF16)
    backward = forward
    field = pltpu.VMEM((cells, c), F32)
    flipped_field = pltpu.VMEM((2 * c, cells), BF16)
    quarter = cells // 4
    scratch = dict(
        small=pltpu.VMEM((LATE_COUNT, c), F32),
        send=pltpu.SemaphoreType.DMA((copies,)),
        recv=pltpu.SemaphoreType.DMA((copies,)),
        local=pltpu.SemaphoreType.DMA((12 + len(runs),)),
        sums=pltpu.VMEM((total_rows, c), F32),
        final=pltpu.VMEM((total_rows, c), F32),
        landing=pltpu.VMEM((landing, c), F32),
        frames_in=pltpu.VMEM((line, history, strip, width), F32),
        mask_in=pltpu.VMEM((line, strip, width), jnp.int32),
        frames_out=pltpu.VMEM((line, history, strip, width), F32),
        frames_from=pltpu.VMEM((line, history, strip, width), F32),
        frames_here=pltpu.VMEM((line, history, strip, width), F32),
        mask_from=pltpu.VMEM((line, strip, width), jnp.int32),
        cot_from=pltpu.VMEM((items, strip * width, c), F32),
        output_here=pltpu.VMEM((items, strip * width, c), F32),
        cot_inward=pltpu.VMEM((2, strip * width, c), F32),
        cot_across=pltpu.VMEM((2, strip * width, c), F32),
        output_inward=pltpu.VMEM((2, strip * width, c), F32),
        output_across=pltpu.VMEM((2, strip * width, c), F32),
        fields=pltpu.VMEM((16, cells), F32),
        lift=pltpu.VMEM((16, c), F32),
        joined=pltpu.VMEM((cells, 4 * c), BF16),
        x_down=pltpu.VMEM((quarter, 8 * c), BF16),
        x_grad_up=pltpu.VMEM((quarter, 8 * c), BF16),
        x_up=pltpu.VMEM((quarter, 2 * c), BF16),
        x_grad_low=pltpu.VMEM((quarter, 2 * c), BF16),
        f_down=pltpu.VMEM((8 * c, 2 * c), BF16),
        b_down=pltpu.VMEM((4, 2 * c, 2 * c), BF16),
        f_up=pltpu.VMEM((4, 2 * c, 2 * c), BF16),
        b_up=pltpu.VMEM((8 * c, 2 * c), BF16),
        f_skip=pltpu.VMEM((4 * c, 2 * c), BF16),
        b_skip=pltpu.VMEM((2, 2 * c, 2 * c), BF16),
        xe1=shifted,
        xe2=shifted,
        xd1a=shifted,
        xd1b=shifted,
        xd2=shifted,
        xg=shifted,
        te1=flipped_field,
        te2=flipped_field,
        td1=pltpu.VMEM((4 * c, cells), BF16),
        td2=flipped_field,
        turned=pltpu.VMEM((4 * c, cells), BF16),
        fe1=forward,
        fe2=forward,
        fd1a=forward,
        fd1b=forward,
        fd2=forward,
        be1=backward,
        be2=backward,
        bd1a=backward,
        bd1b=backward,
        bd2=backward,
        slope_e1=field,
        slope_e2=field,
        slope_d1a=field,
        slope_d1b=field,
        slope_d2=field,
        lifted=field,
        middle_e=field,
        encoded=field,
        raised=field,
        middle_d=field,
        result=field,
        cot=field,
        grad=field,
        grad_a=field,
        grad_b=field,
    )
    scratch.update({name: pltpu.VMEM(shapes[name], F32) for name in LARGE})

    in_hbm = pl.BlockSpec(memory_space=pl.ANY)
    in_vmem = pl.BlockSpec(memory_space=pltpu.VMEM)
    in_smem = pl.BlockSpec(memory_space=pltpu.SMEM)
    in_specs = [
        in_hbm if name in IN_HBM else in_smem if name in IN_SMEM else in_vmem
        for name in ARGUMENTS
    ]
    out_shape = [
        jax.ShapeDtypeStruct((items, strip * width, c), F32),
        jax.ShapeDtypeStruct(frames.shape, F32),
        jax.ShapeDtypeStruct((total_rows, c), F32),
    ]
    out_specs = [in_hbm] * 3
    results = pl.pallas_call(
        functools.partial(
            item_kernel,
            (line, strip, width, shapes, big_layout),
            tuple(scratch),
        ),
        out_shape=out_shape,
        in_specs=in_specs,
        out_specs=out_specs,
        scratch_shapes=list(scratch.values()),
        compiler_params=pltpu.CompilerParams(
            collective_id=0, has_side_effects=True, vmem_limit_bytes=62 * 1024 * 1024
        ),
    )(*[flat[name] for name in ARGUMENTS])
    names = LARGE + tuple(SMALL_ROWS)
    written = pl.pallas_call(
        functools.partial(write_kernel, (shapes, starts, small_at)),
        out_shape=out_shape[:2] + [jax.ShapeDtypeStruct(flat[name].shape, F32) for name in names],
        in_specs=[pl.BlockSpec(memory_space=pltpu.HBM)] * 3,
        out_specs=[in_hbm] * (2 + len(LARGE)) + [in_vmem] * len(SMALL_ROWS),
        scratch_shapes=[
            pltpu.VMEM((items, strip * width, c), F32),
            pltpu.VMEM(frames.shape, F32),
            pltpu.VMEM((total_rows, c), F32),
            pltpu.SemaphoreType.DMA((1 + 2 * (2 + len(LARGE)),)),
        ],
        compiler_params=pltpu.CompilerParams(vmem_limit_bytes=60 * 1024 * 1024),
    )(*results)
    grads = dict(zip(names, written[2:]))
    ordered = [name for name in ARGUMENTS if name in grads]
    return (written[0].reshape(cotangent.shape), written[1]) + tuple(
        grads[name].reshape(given[name].shape) for name in ordered
    )


def body(shape, *arguments):
    items, _, strip, width = arguments[0].shape
    line = shape["rows"]
    whole = (
        shape["section"] == 2
        and shape["batch"] == 4
        and items == line == 4
        and arguments[-1].shape[-1] == 128
        and (strip * line * width) % CHUNK == 0
    )
    return whole_items(shape, *arguments) if whole else strips_body(*arguments)


def solution(mesh):
    in_specs = (
        P(("section", "batch"), None, "rows", None),
        P(("section", "batch")),
        P(("section", "batch"), "rows", None),
        P(("section", "batch")),
        P(),
        P(),
        P(),
        P(),
        P(),
        P(),
        P(),
        P(),
        P(),
        P(),
        P(),
        P(),
        P(),
        P(),
        P(),
        P(),
        P(),
        P(),
        P(),
        P(),
        P(),
        P(),
        P(),
        P(),
        P(("section", "batch"), "rows", None, None),
    )
    out_specs = (
        P(("section", "batch"), "rows", None, None),
        P(("section", "batch"), None, "rows", None),
        P(),
        P(),
        P(),
        P(),
        P(),
        P(),
        P(),
        P(),
        P(),
        P(),
        P(),
        P(),
        P(),
        P(),
        P(),
        P(),
        P(),
        P(),
        P(),
        P(),
        P(),
        P(),
        P(),
        P(),
    )
    return jax.shard_map(functools.partial(body, mesh.shape), mesh=mesh, in_specs=in_specs, out_specs=out_specs, check_vma=False)
```

```python
import functools
from types import SimpleNamespace
from typing import Any, NamedTuple

import jax
import jax.numpy as jnp
from jax import lax
from jax.experimental import pallas as pl
from jax.experimental.pallas import tpu as pltpu
from jax.sharding import PartitionSpec as P

GROUPS = 8
FIELDS = 3
HIST = 4


EPS = 1e-05
HIGH = lax.Precision.HIGHEST


def extended(cells, sides, width):
    for axis, dim in sides:
        count = lax.axis_size(axis)
        ends = count - 1
        head = lax.slice_in_dim(cells, 0, width, axis=dim)
        tail = lax.slice_in_dim(cells, cells.shape[dim] - width, cells.shape[dim], axis=dim)
        cells = jnp.concatenate(
            [
                lax.ppermute(tail, axis, [(i, (i + 1) % count) for i in range(ends)]),
                cells,
                lax.ppermute(head, axis, [((i + 1) % count, i) for i in range(ends)]),
            ],
            axis=dim,
        )
    return cells


def from_behind(value, axis, steps):
    count = lax.axis_size(axis)
    pairs = [(source, (source + steps) % count) for source in range(count)]
    return lax.ppermute(value, axis, pairs)


def group_view(value_arrays):
    extent = value_arrays.shape
    return value_arrays.reshape(extent[:-1] + (GROUPS, extent[-1] // GROUPS))


def global_sums(value_arrays):
    grouped = group_view(value_arrays)
    flat = grouped.reshape(-1, GROUPS, grouped.shape[-1])
    first_sum = jnp.sum(flat, axis=(0, 2))
    second_sum = jnp.sum(flat * flat, axis=(0, 2))
    return lax.psum((first_sum, second_sum), "rows")


def apply_norm(value_arrays, sum_one, sum_two, norm_gain, norm_bias, total):
    grouped = group_view(value_arrays)
    group_mean = sum_one / total
    variance = sum_two / total - group_mean * group_mean
    inverse = lax.rsqrt(variance + EPS)
    normed = (grouped - group_mean[:, None]) * inverse[:, None]
    return normed.reshape(value_arrays.shape) * norm_gain + norm_bias


def norm_back(value_arrays, grad_one, grad_two):
    grouped = group_view(value_arrays)
    extra = grad_one[:, None] + 2.0 * grouped * grad_two[:, None]
    return extra.reshape(value_arrays.shape)


def reduce_grads(grad_one, grad_two):
    return lax.psum((grad_one, grad_two), "rows")


def conv_rows(padded, kernel):
    widened = jnp.pad(padded, ((0, 0), (1, 1), (0, 0)))
    return lax.conv_general_dilated(
        widened[None],
        kernel,
        (1, 1),
        "VALID",
        dimension_numbers=("NHWC", "HWIO", "NHWC"),
        precision=HIGH,
    )[0]


def flipped(kernel):
    return jnp.transpose(kernel[::-1, ::-1], (0, 1, 3, 2))


def pad_grads(value_arrays):
    return extended(value_arrays, (("rows", 0),), 1)


def totals_of(inputs, conv1):
    strip = inputs.shape[0]
    cells = strip * lax.axis_size("rows") * inputs.shape[1]
    return (cells * (inputs.shape[2] // GROUPS), cells * (conv1.shape[3] // GROUPS))


def block_forward(inputs, weights, scale_part, shift_part):
    norm1_gain, norm1_bias, conv1, norm2_gain, norm2_bias, conv2, conv2_bias = weights
    total_in, total_mid = totals_of(inputs, conv1)
    sums_in = global_sums(inputs)

    def pad_rows(value_arrays):
        return extended(value_arrays, (("rows", 0),), 1)

    act_one = pad_rows(
        jax.nn.gelu(
            apply_norm(inputs, sums_in[0], sums_in[1], norm1_gain, norm1_bias, total_in),
            approximate=False,
        )
    )
    middle = conv_rows(act_one, conv1)
    sums_mid = global_sums(middle)
    shaped = (
        apply_norm(middle, sums_mid[0], sums_mid[1], norm2_gain, norm2_bias, total_mid)
        * (1.0 + scale_part)
        + shift_part
    )
    act_two = pad_rows(jax.nn.gelu(shaped, approximate=False))
    branch = conv_rows(act_two, conv2) + conv2_bias
    return (branch, (sums_in[0], sums_in[1], act_one, middle, sums_mid[0], sums_mid[1], act_two))


def block_backward(inputs, weights, scale_part, shift_part, kept, grad_out):
    norm1_gain, norm1_bias, conv1, norm2_gain, norm2_bias, conv2, conv2_bias = weights
    in_one, in_two, act_one, middle, mid_one, mid_two, act_two = kept
    total_in, total_mid = totals_of(inputs, conv1)
    grad_conv2 = jax.vjp(lambda kernel: conv_rows(act_two, kernel), conv2)[1](grad_out)[0]
    grad_bias2 = jnp.sum(grad_out, axis=(0, 1))
    grad_act_two = conv_rows(pad_grads(grad_out), flipped(conv2))

    def second_piece(middle_in, sum_one, sum_two, gain_in, incoming_bias, scale_in, shift_in):
        shaped = (
            apply_norm(middle_in, sum_one, sum_two, gain_in, incoming_bias, total_mid)
            * (1.0 + scale_in)
            + shift_in
        )
        return jax.nn.gelu(shaped, approximate=False)

    second_pull = jax.vjp(
        second_piece, middle, mid_one, mid_two, norm2_gain, norm2_bias, scale_part, shift_part
    )[1](grad_act_two)
    summed_one, summed_two = reduce_grads(second_pull[1], second_pull[2])
    grad_middle = second_pull[0] + norm_back(middle, summed_one, summed_two)
    grad_conv1 = jax.vjp(lambda kernel: conv_rows(act_one, kernel), conv1)[1](grad_middle)[0]
    grad_act_one = conv_rows(pad_grads(grad_middle), flipped(conv1))

    def first_piece(inputs_in, sum_one, sum_two, gain_in, incoming_bias):
        return jax.nn.gelu(
            apply_norm(inputs_in, sum_one, sum_two, gain_in, incoming_bias, total_in),
            approximate=False,
        )

    first_pull = jax.vjp(first_piece, inputs, in_one, in_two, norm1_gain, norm1_bias)[1](
        grad_act_one
    )
    first_one, first_two = reduce_grads(first_pull[1], first_pull[2])
    grad_inputs = first_pull[0] + norm_back(inputs, first_one, first_two)
    grads = (
        first_pull[3],
        first_pull[4],
        grad_conv1,
        second_pull[3],
        second_pull[4],
        grad_conv2,
        grad_bias2,
    )
    return (grad_inputs, grads, second_pull[5], second_pull[6])


def conditioning(step_item, table):
    one_hot = (jnp.arange(table.shape[0], dtype=jnp.int32) == step_item).astype(jnp.float32)
    condition = jnp.dot(one_hot, table, precision=HIGH)
    half_width = table.shape[1] // 2
    return (condition[:half_width], condition[half_width:], one_hot)


def project_in(frames_item, mask_item, count_item, incoming_weight, incoming_bias):
    history = jnp.arange(HIST, dtype=jnp.int32) >= HIST - count_item
    keep = jnp.repeat(history, FIELDS).astype(jnp.float32)
    lifted = (
        jnp.einsum(
            "fhw,fc->hwc", frames_item * keep[:, None, None], incoming_weight, precision=HIGH
        )
        + incoming_bias
    )
    return lifted * mask_item[:, :, None].astype(jnp.float32)


def coarsen_field(value_arrays, incoming_weight, incoming_bias):
    rows_here, width_here, depth_here = value_arrays.shape
    blocks = value_arrays.reshape(rows_here // 2, 2, width_here // 2, 2, depth_here)
    return jnp.einsum("iajbk,abkc->ijc", blocks, incoming_weight, precision=HIGH) + incoming_bias


def upsample(value_arrays, incoming_weight, incoming_bias):
    result = jnp.einsum("ijk,abkc->iajbc", value_arrays, incoming_weight, precision=HIGH)
    extent = result.shape
    return result.reshape(extent[0] * 2, extent[2] * 2, extent[4]) + incoming_bias


def flatten_all(pieces):
    return jnp.concatenate([piece.reshape(-1) for piece in pieces])


def unflatten_all(flat, templates):
    pieces = []
    offset_at = 0
    for template in templates:
        count_here = template.size
        pieces.append(flat[offset_at : offset_at + count_here].reshape(template.shape))
        offset_at += count_here
    return tuple(pieces)


def strips_body(
    frames,
    counts,
    cell_mask,
    step_index,
    lift_weight,
    lift_bias,
    enc_norm1_gain,
    enc_norm1_bias,
    enc_conv1,
    enc_step_table,
    enc_norm2_gain,
    enc_norm2_bias,
    enc_conv2,
    enc_conv2_bias,
    reducer_weight,
    reducer_bias,
    up_weight,
    up_bias,
    dec_norm1_gain,
    dec_norm1_bias,
    dec_conv1,
    dec_step_table,
    dec_norm2_gain,
    dec_norm2_bias,
    dec_conv2,
    dec_conv2_bias,
    skip_weight,
    skip_bias,
    cotangent,
):
    enc_weights = (
        enc_norm1_gain,
        enc_norm1_bias,
        enc_conv1,
        enc_norm2_gain,
        enc_norm2_bias,
        enc_conv2,
        enc_conv2_bias,
    )
    dec_weights = (
        dec_norm1_gain,
        dec_norm1_bias,
        dec_conv1,
        dec_norm2_gain,
        dec_norm2_bias,
        dec_conv2,
        dec_conv2_bias,
    )
    params = (
        lift_weight,
        lift_bias,
        enc_norm1_gain,
        enc_norm1_bias,
        enc_conv1,
        enc_step_table,
        enc_norm2_gain,
        enc_norm2_bias,
        enc_conv2,
        enc_conv2_bias,
        reducer_weight,
        reducer_bias,
        up_weight,
        up_bias,
        dec_norm1_gain,
        dec_norm1_bias,
        dec_conv1,
        dec_step_table,
        dec_norm2_gain,
        dec_norm2_bias,
        dec_conv2,
        dec_conv2_bias,
        skip_weight,
        skip_bias,
    )

    def forward_micro(carry, sliced):
        frames_item, mask_item, count_item, step_item = sliced
        lifted = project_in(frames_item, mask_item, count_item, lift_weight, lift_bias)
        enc_scale, enc_shift, unused_hot = conditioning(step_item, enc_step_table)
        enc_branch, enc_kept = block_forward(lifted, enc_weights, enc_scale, enc_shift)
        encoder_result = lifted + enc_branch
        coarse_field = coarsen_field(encoder_result, reducer_weight, reducer_bias)
        foreign = from_behind(coarse_field, "section", 1)
        raised_foreign = upsample(foreign, up_weight, up_bias)
        raised = from_behind(raised_foreign, "section", 1)
        joined = jnp.concatenate([raised, encoder_result], axis=-1)
        dec_scale, dec_shift, unused_again = conditioning(step_item, dec_step_table)
        dec_branch, dec_kept = block_forward(joined, dec_weights, dec_scale, dec_shift)
        output_item = jnp.dot(joined, skip_weight, precision=HIGH) + skip_bias + dec_branch
        return (carry, (output_item, (lifted, enc_kept, encoder_result, foreign, joined, dec_kept)))

    unused, (output, kept_all) = lax.scan(
        forward_micro, jnp.zeros((), jnp.float32), (frames, cell_mask, counts, step_index)
    )

    def backward_micro(totals, sliced):
        frames_item, mask_item, count_item, step_item, grad_out, kept = sliced
        lifted, enc_kept, encoder_result, foreign, joined, dec_kept = kept
        dec_scale, dec_shift, one_hot = conditioning(step_item, dec_step_table)
        grad_joined, dec_grads, dec_gscale, dec_gshift = block_backward(
            joined, dec_weights, dec_scale, dec_shift, dec_kept, grad_out
        )
        grad_skip_weight = jnp.einsum("hwk,hwc->kc", joined, grad_out, precision=HIGH)
        grad_skip_bias = jnp.sum(grad_out, axis=(0, 1))
        grad_joined = grad_joined + jnp.dot(grad_out, skip_weight.T, precision=HIGH)
        half_width = joined.shape[-1] // 2
        grad_raised = grad_joined[..., :half_width]
        grad_encoded = grad_joined[..., half_width:]
        grad_foreign_up = from_behind(grad_raised, "section", 1)
        up_pull = jax.vjp(upsample, foreign, up_weight, up_bias)[1](grad_foreign_up)
        coarse_gradient = from_behind(up_pull[0], "section", 1)
        reducer_pullback = jax.vjp(coarsen_field, encoder_result, reducer_weight, reducer_bias)[1](
            coarse_gradient
        )
        grad_encoded = grad_encoded + reducer_pullback[0]
        enc_scale, enc_shift, enc_hot = conditioning(step_item, enc_step_table)
        grad_lifted, enc_grads, enc_gscale, enc_gshift = block_backward(
            lifted, enc_weights, enc_scale, enc_shift, enc_kept, grad_encoded
        )
        grad_lifted = grad_lifted + grad_encoded
        proj_pull = jax.vjp(
            lambda frames_in, incoming_weight, incoming_bias: project_in(
                frames_in, mask_item, count_item, incoming_weight, incoming_bias
            ),
            frames_item,
            lift_weight,
            lift_bias,
        )[1](grad_lifted)
        enc_table_grad = enc_hot[:, None] * jnp.concatenate([enc_gscale, enc_gshift])[None, :]
        dec_table_grad = one_hot[:, None] * jnp.concatenate([dec_gscale, dec_gshift])[None, :]
        micro_list = (
            proj_pull[1],
            proj_pull[2],
            enc_grads[0],
            enc_grads[1],
            enc_grads[2],
            enc_table_grad,
            enc_grads[3],
            enc_grads[4],
            enc_grads[5],
            enc_grads[6],
            reducer_pullback[1],
            reducer_pullback[2],
            up_pull[1],
            up_pull[2],
            dec_grads[0],
            dec_grads[1],
            dec_grads[2],
            dec_table_grad,
            dec_grads[3],
            dec_grads[4],
            dec_grads[5],
            dec_grads[6],
            grad_skip_weight,
            grad_skip_bias,
        )
        micro_flat = flatten_all(micro_list)
        return (totals + micro_flat, proj_pull[0])

    total_size = sum((piece.size for piece in params))
    start_totals = jnp.zeros((total_size,), jnp.float32)
    flat_totals, frames_grad = lax.scan(
        backward_micro,
        start_totals,
        (frames, cell_mask, counts, step_index, cotangent, kept_all),
        reverse=True,
    )
    flat_totals = lax.psum(flat_totals, ("section", "batch", "rows"))
    grads = unflatten_all(flat_totals, params)
    return (output, frames_grad) + grads


F32 = jnp.float32
BF16 = jnp.bfloat16
MESH = pl.DeviceIdType.MESH
NN = ((1,), (0,))
NT = ((1,), (1,))
TN = ((0,), (0,))
HIGH_AT = (0, 2, 1)
LOW_AT = (4, 3, 5)
CHUNK = 512
class Given(NamedTuple):
    frames: Any
    counts: Any
    cell_mask: Any
    step_index: Any
    lift_weight: Any
    lift_bias: Any
    enc_norm1_gain: Any
    enc_norm1_bias: Any
    enc_conv1: Any
    enc_step_table: Any
    enc_norm2_gain: Any
    enc_norm2_bias: Any
    enc_conv2: Any
    enc_conv2_bias: Any
    reducer_weight: Any
    reducer_bias: Any
    up_weight: Any
    up_bias: Any
    dec_norm1_gain: Any
    dec_norm1_bias: Any
    dec_conv1: Any
    dec_step_table: Any
    dec_norm2_gain: Any
    dec_norm2_bias: Any
    dec_conv2: Any
    dec_conv2_bias: Any
    skip_weight: Any
    skip_bias: Any
    cotangent: Any


ARGUMENTS = Given._fields
LARGE = tuple(
    dict(
        dec_conv1=0,
        up_weight=0,
        reducer_weight=0,
        dec_conv2=0,
        skip_weight=0,
        enc_conv1=0,
        enc_conv2=0,
    )
)
IN_HBM = tuple(dict(frames=0, cell_mask=0, cotangent=0)) + LARGE
IN_SMEM = tuple(dict(counts=0, step_index=0))
LATE = 64
SMALL_ROWS = dict(
    enc_conv2_bias=(0, 1),
    reducer_bias=(1, 1),
    up_bias=(2, 1),
    dec_conv2_bias=(3, 1),
    skip_bias=(3, 1),
    dec_norm1_gain=(4, 2),
    dec_norm1_bias=(6, 2),
    dec_norm2_gain=(8, 1),
    dec_norm2_bias=(9, 1),
    dec_step_table=(16, 8),
    lift_weight=(LATE, 12),
    lift_bias=(LATE + 12, 1),
    enc_norm1_gain=(LATE + 16, 1),
    enc_norm1_bias=(LATE + 17, 1),
    enc_norm2_gain=(LATE + 18, 1),
    enc_norm2_bias=(LATE + 19, 1),
    enc_step_table=(LATE + 24, 8),
)
LATE_COUNT = 32
SMALL_COUNT = LATE + LATE_COUNT
DUE = ((), (), (0,), (), (), (), (), (0,), (1,), (2,), (3, 0), (1,), (2,), (), (3, 1, 0, 2), (), (), (3,), (1,), (2, 0, 4), (3,), (1,), (2,), (4, 0, 5, 3), (1,), (2, 4), (0, 3), (6, 7, 5, 1, 4, 2), (), ())
REST = (0, 3, 4, 6, 7, 8, 5, 0, 1, 4, 2, 3, 5, 6, 1, 7, 2, 8, 3, 4, 6, 5, 7, 4, 6, 7, 5, 4, 6, 7, 5, 6, 7, 5, 6, 7, 5, 6, 7)
OUTPUTS = tuple(dict(output=0, frames_grad=0, gradients=0))


def split(value):
    high = value.astype(BF16)
    return high, (value - high.astype(F32)).astype(BF16)


def dot(left, right, dims=NN, precision=None):
    return lax.dot_general(
        left, right, (dims, ((), ())), precision=precision, preferred_element_type=F32
    )


def fold(value):
    half = value.shape[1] // 2
    return value[:, :half] + value[:, half:]


def fold_rows(value):
    half = value.shape[0] // 2
    return value[:half] + value[half:]


def tile_sums(value):
    return jnp.sum(value.reshape(-1, 8, value.shape[-1]), axis=0)


def column_sum(tiles):
    return jnp.sum(tiles, axis=0, keepdims=True)


def normal(value):
    bell = jnp.exp(-0.5 * value * value)
    t = 1.0 / (1.0 + 0.2316418882663604 * jnp.abs(value))
    poly = 0.5307027145
    for factor in (-0.7265760135, 0.7107068705, -0.142248368, 0.127414796):
        poly = poly * t + factor
    tail = poly * t * bell
    return jnp.where(value < 0.0, tail, 1.0 - tail), 0.3989422804014327 * bell


def dot_three(left, right, dims=NN):
    left_high, left_low = split(left)
    right_high, right_low = split(right)
    total = dot(left_high, right_high, dims)
    return total + (dot(left_high, right_low, dims) + dot(left_low, right_high, dims))


def group_ones(channels, size):
    rows = lax.broadcasted_iota(jnp.int32, (channels, channels), 0) // size
    columns = lax.broadcasted_iota(jnp.int32, (channels, channels), 1) // size
    return (rows == columns).astype(BF16)


def group_sums(first, second, ones):
    terms = []
    rest = jnp.concatenate([first, second], axis=0)
    for _ in range(3):
        term = rest.astype(BF16)
        terms.append(term)
        rest = rest - term.astype(F32)
    both = dot(jnp.concatenate(terms, axis=0), ones)
    both = both[32:48] + both[16:32] + both[:16]
    return column_sum(both[:8]), column_sum(both[8:])


class LineSwap:

    def __init__(self, line, source, target, inward, across, make):
        far = 3 - line.outer
        self.line = line
        to_inner, to_across = line.device(line.inner), line.device(line.across)
        to_outer = line.device(line.outer)
        here = target(line.here)
        self.to_far = make(source(3 - line.here), inward.at[1], to_inner)
        self.to_second = make(source(3 - line.inner), inward.at[0], to_inner)
        self.to_inner = make(source(line.inner), here, to_inner)
        self.for_far = make(source(far), across.at[0], to_across)
        self.to_across = make(source(line.across), here, to_across)
        self.to_outer = make(source(line.outer), here, to_outer)
        self.pass_far = make(inward.at[1], across.at[1], to_across)
        self.pass_second = make(inward.at[0], target(line.outer), to_across)
        self.pass_across = make(across.at[0], target(line.across), to_outer)
        self.pass_opposite = make(across.at[1], target(far), to_outer)

    def first(self):
        @pl.when(self.line.edge)
        def _():
            for copy in (self.to_far, self.to_second, self.to_inner):
                copy.start()

        @pl.when(self.line.middle)
        def _():
            for copy in (self.for_far, self.to_across, self.to_outer):
                copy.start()

    def second(self):
        @pl.when(self.line.middle)
        def _():
            self.for_far.wait_recv()
            self.pass_across.start()
            self.to_far.wait_recv()
            self.pass_far.start()
            self.to_second.wait_recv()
            self.pass_second.start()

    def third(self):
        @pl.when(self.line.middle)
        def _():
            self.pass_far.wait_recv()
            self.pass_opposite.start()

    def arrive(self):
        @pl.when(self.line.edge)
        def _():
            for copy in (self.to_outer, self.pass_across, self.pass_opposite):
                copy.wait_recv()

        @pl.when(self.line.middle)
        def _():
            for copy in (self.to_inner, self.to_across, self.pass_second):
                copy.wait_recv()

    def sent(self):
        @pl.when(self.line.edge)
        def _():
            for copy in (self.to_far, self.to_second, self.to_inner):
                copy.wait_send()

        @pl.when(self.line.middle)
        def _():
            for copy in (self.for_far, self.to_across, self.to_outer):
                copy.wait_send()
            for copy in (self.pass_far, self.pass_second, self.pass_across, self.pass_opposite):
                copy.wait_send()


class Exchange:

    def __init__(self, place, start, rows, landing, first_sem):
        self.place, self.start, self.rows, self.landing = place, start, rows, landing
        self.sem = first_sem
        self.stage = 0
        self.copies = []
        self.waiting = []
        self.group = place.plane_group
        self.half = rows // 2
        self.base = start + place.core * self.half
        self._finish(self.half)

    def _finish(self, size):
        self.part = size // self.group.count
        self.own = self.base + self.group.here * self.part

    def count(self):
        return 2 + 2 * (self.group.count - 1) + 3

    def land_rows(self):
        return self.half + (self.group.count + 1) * self.part

    def _copy(self, source, target, device, only=None):
        place = self.place
        copy = pltpu.make_async_remote_copy(
            src_ref=source,
            dst_ref=target,
            send_sem=place.send.at[self.sem],
            recv_sem=place.recv.at[self.sem],
            device_id=device,
            device_id_type=MESH,
        )
        self.sem += 1
        if only is None:
            copy.start()
            self.waiting.append(copy)
        self.copies.append((copy, only))
        return copy

    def _wait(self):
        for copy in self.waiting:
            copy.wait_recv()
        self.waiting = []

    def _rows(self, at, size):
        return pl.ds(pl.multiple_of(at, 8), size)

    def _swap(self):
        place = self.place
        other = self._rows(self.start + (1 - place.core) * self.half, self.half)
        self.land = self.landing
        self.landing += self.half
        self._copy(
            place.sums.at[other], place.landing.at[pl.ds(self.land, self.half)], place.partner
        )

    def _add_swap(self):
        place = self.place
        block = next(size for size in (64, 32, 16, 8) if self.half % size == 0)

        def step(i, carry):
            here = self._rows(self.base + i * block, block)
            there = self._rows(self.land + i * block, block)
            place.sums[here] = place.sums[here] + place.landing[there]
            return carry

        lax.fori_loop(0, self.half // block, step, 0)

    def _scatter(self, group, base, size):
        place = self.place
        self.land = self.landing
        for k in range(1, group.count):
            to = lax.rem(group.here + k, group.count)
            self._copy(
                place.sums.at[self._rows(base + to * size, size)],
                place.landing.at[pl.ds(self.landing, size)],
                group.device(to),
            )
            self.landing += size

    def _total(self, group, own, size, target):
        place = self.place
        block = 16 if size % 16 == 0 else 8

        def step(i, carry):
            here = self._rows(own + i * block, block)
            total = place.sums[here]
            for k in range(group.count - 1):
                there = self._rows(self.land + k * size + i * block, block)
                total = total + place.landing[there]
            target[here] = total
            return carry

        lax.fori_loop(0, size // block, step, 0)

    def _gather(self, group, own, size):
        final = self.place.final
        here = self._rows(own, size)
        for k in range(1, group.count):
            to = lax.rem(group.here + k, group.count)
            self._copy(final.at[here], final.at[here], group.device(to))

    def _steps(self):
        place, group = self.place, self.group
        yield self._swap()
        self._wait()
        self._add_swap()
        yield from self._both()
        final = place.final
        here = self._rows(self.base, self.half)
        self._copy(final.at[here], final.at[here], place.partner)
        yield
        self._wait()
        yield

    def _both(self):
        place, group = self.place, self.group
        self._scatter(group, self.base, self.part)
        yield
        self._wait()
        self._total(group, self.own, self.part, place.sums)
        yield from self._line()
        self._gather(group, self.own, self.part)
        yield
        self._wait()

    def _line(self):
        place, line = self.place, self.place.line
        sums, final, landing = place.sums, place.final, place.landing
        part, own = self.part, self._rows(self.own, self.part)
        inward, across = pl.ds(self.landing, part), pl.ds(self.landing + part, part)
        self.landing += 2 * part
        block = 16 if part % 16 == 0 else 8

        def add(at, target):
            def step(i, carry):
                here = self._rows(self.own + i * block, block)
                target[here] = sums[here] + landing[pl.ds(at + i * block, block)]
                return carry

            lax.fori_loop(0, part // block, step, 0)

        first = self._copy(sums.at[own], landing.at[inward], line.device(line.inner), line.edge)
        second = self._copy(sums.at[own], landing.at[across], line.device(line.across), line.middle)
        third = self._copy(final.at[own], final.at[own], line.device(line.outer), line.middle)
        pl.when(line.edge)(first.start)
        yield

        @pl.when(line.middle)
        def _():
            first.wait_recv()
            add(self.landing - 2 * part, sums)
            second.start()

        yield

        @pl.when(line.middle)
        def _():
            second.wait_recv()
            add(self.landing - part, final)
            third.start()

        yield
        pl.when(line.edge)(third.wait_recv)

    def advance(self):
        if self.stage == 0:
            self.steps = self._steps()
        self.stage += 1
        next(self.steps)

    def done(self):
        return self.stage == 8


class HalvingExchange(Exchange):

    def count(self):
        return 9

    def land_rows(self):
        return self.rows // 2 + self.rows // 4 + 3 * self.rows // 8

    def _steps(self):
        place, final = self.place, self.place.final
        self.base = self.start
        bases = []
        for level in range(3):
            self.half = self.rows >> (level + 1)
            bit, device = place.halves[level]
            other = self._rows(self.base + (1 - bit) * self.half, self.half)
            self.base = self.base + bit * self.half
            self.land = self.landing
            self.landing += self.half
            bases.append(self.base)
            self._copy(
                place.sums.at[other], place.landing.at[pl.ds(self.land, self.half)], device
            )
            yield
            self._wait()
            self._add_swap()
        self.own, self.part = self.base, self.half
        yield from self._line()
        for level in (2, 1, 0):
            self._wait()
            here = self._rows(bases[level], self.rows >> (level + 1))
            self._copy(final.at[here], final.at[here], place.halves[level][1])
            yield
        self._wait()
        yield

    def done(self):
        return self.stage == 10


class SmallExchange(Exchange):

    def count(self):
        return self.place.cores_group.count + self.place.line.count - 2

    def land_rows(self):
        return self.rows * (self.place.cores_group.count + self.place.line.count)

    def _share(self, group, source):
        place = self.place
        self.land = self.landing
        self.landing += group.count * self.rows
        own = self._rows(self.land + group.here * self.rows, self.rows)
        place.landing[own] = source[...]
        for k in range(1, group.count):
            to = lax.rem(group.here + k, group.count)
            self._copy(source, place.landing.at[own], group.device(to))

    def _sum(self, group):
        total = None
        for k in range(group.count):
            part = self.place.landing[pl.ds(self.land + k * self.rows, self.rows)]
            total = part if total is None else total + part
        return total

    def _steps(self):
        place = self.place
        here = pl.ds(self.start, self.rows)
        self._share(place.line, place.sums.at[here])
        yield
        self._wait()
        place.small[...] = self._sum(place.line)
        self._share(place.cores_group, place.small)
        yield
        self._wait()
        place.final[here] = self._sum(place.cores_group)
        yield

    def done(self):
        return self.stage == 3


KINDS = (HalvingExchange,) * 8 + (SmallExchange,)


def layout_of(shapes):
    starts = {}
    at = 0
    for name in LARGE:
        starts[name] = at
        at += getattr(shapes, name)[0]
    small = at
    begins = SimpleNamespace(**starts)
    late = small + LATE
    tap = shapes.dec_conv2[0] // 3
    part = shapes.dec_conv1[0] // 3
    conv1, up = begins.dec_conv1, begins.up_weight
    edges = (
        (begins.dec_conv2, begins.enc_conv1),
        (conv1, conv1 + part),
        (conv1 + part, conv1 + 2 * part),
        (conv1 + 2 * part, up),
        (up, begins.dec_conv2),
        (begins.enc_conv2, late),
        (begins.enc_conv1, begins.enc_conv1 + 2 * tap),
        (begins.enc_conv1 + 2 * tap, begins.enc_conv2),
        (late, late + LATE_COUNT),
    )
    runs = [(first, last - first) for first, last in edges]
    return starts, small, late + LATE_COUNT, runs


def item_kernel(sizes, scratch_names, *refs):
    line, strip, width, shapes, big_layout = sizes
    begins, small_at, total_rows, runs = big_layout
    starts = SimpleNamespace(**begins)
    inputs = Given(*refs[: len(ARGUMENTS)])
    refs = refs[len(ARGUMENTS) :]
    output_names = OUTPUTS
    outputs = SimpleNamespace(**dict(zip(output_names, refs)))
    scratch = SimpleNamespace(**dict(zip(scratch_names, refs[len(output_names) :])))

    def w_of(name):
        return getattr(scratch, name)

    height = strip * line
    cells = height * width
    c = inputs.lift_weight.shape[1]
    strip_cells = strip * width
    history = inputs.frames.shape[1]

    core = lax.axis_index("section")
    plane = lax.axis_index("batch")
    row = lax.axis_index("rows")
    middle = lax.rem(row + 1, 4) // 2
    y, x = plane // 2, lax.rem(plane, 2)
    along_x = plane + 1 - 2 * x
    along_y = plane + 2 - 4 * y

    def device_at(to):
        return (core, plane, to)

    place = SimpleNamespace(
        core=core,
        partner=(1 - core, plane, row),
        line=SimpleNamespace(
            count=line,
            here=row,
            device=device_at,
            middle=middle == 1,
            edge=middle == 0,
            inner=1 + row // 2,
            across=3 - row,
            outer=3 * (row // 2),
        ),
        plane_group=SimpleNamespace(
            count=4, here=plane, device=lambda to: (core, to, row)
        ),
        cores_group=SimpleNamespace(
            count=8,
            here=core * 4 + plane,
            device=lambda to: (to // 4, lax.rem(to, 4), row),
        ),
        halves=(
            (core, (1 - core, plane, row)),
            (x * (1 - core) + y * core, (core, along_x * (1 - core) + along_y * core, row)),
            (y * (1 - core) + x * core, (core, along_y * (1 - core) + along_x * core, row)),
        ),
        small=scratch.small,
        sums=scratch.sums,
        final=scratch.final,
        landing=scratch.landing,
        send=scratch.send,
        recv=scratch.recv,
    )
    local_sem = scratch.local

    frames_in, mask_in, cot = scratch.frames_in, scratch.mask_in, scratch.cot
    here_rows = pl.ds(pl.multiple_of(row * strip_cells, strip_cells), strip_cells)
    frames_from, mask_from, cot_from = scratch.frames_from, scratch.mask_from, scratch.cot_from
    staged = (
        pltpu.make_async_copy(inputs.frames, frames_from, local_sem.at[7]),
        pltpu.make_async_copy(inputs.cell_mask, mask_from, local_sem.at[8]),
        pltpu.make_async_copy(inputs.cotangent, cot_from, local_sem.at[9]),
    )
    for copy in staged:
        copy.start()

    weight_copies = {}
    for k, name in enumerate(LARGE):
        copy = pltpu.make_async_copy(getattr(inputs, name), w_of(name), local_sem.at[k])
        weight_copies[name] = copy
        copy.start()

    barrier = pltpu.get_barrier_semaphore()
    peers = [device_at(lax.rem(row + k, line)) for k in range(1, line)]
    cores_group = place.cores_group
    for k in range(1, 8):
        peers.append(cores_group.device(lax.rem(cores_group.here + k, 8)))
    for device in peers:
        pl.semaphore_signal(barrier, inc=1, device_id=device, device_id_type=MESH)
    pl.semaphore_wait(barrier, len(peers))

    next_sem = 0

    def make(source, target, device):
        nonlocal next_sem
        copy = pltpu.make_async_remote_copy(
            src_ref=source,
            dst_ref=target,
            send_sem=scratch.send.at[next_sem],
            recv_sem=scratch.recv.at[next_sem],
            device_id=device,
            device_id_type=MESH,
        )
        next_sem += 1
        return copy

    def send(source, target, device):
        copy = make(source, target, device)
        copy.start()
        return copy

    def strip_of(ref, to):
        return ref.at[pl.ds(pl.multiple_of(to * strip_cells, strip_cells), strip_cells)]

    frame_copies, output_copies = [], []
    for copy in staged[:2]:
        copy.wait()
    for k in range(1, line):
        to = lax.rem(row + k, line)
        device = device_at(to)
        frame_copies.append(send(frames_from.at[to], frames_in.at[row], device))
        frame_copies.append(send(mask_from.at[to], mask_in.at[row], device))
    staged[2].wait()
    cot_swap = LineSwap(
        place.line,
        lambda to: cot_from.at[to],
        lambda source: strip_of(cot, source),
        scratch.cot_inward,
        scratch.cot_across,
        make,
    )
    cot_swap.first()

    copied = SimpleNamespace(**weight_copies)
    def put_pair(target, block, value):
        high, low = split(value)
        rows = slice(block * c, (block + 1) * c)
        target[rows, 0:c] = high
        target[rows, c : 2 * c] = low

    def stack_conv(source, half, depth, forward, backward):
        for a in range(3):
            for b in range(3):
                at = (3 * a + b) * depth + half * c
                value = source[at : at + c, :]
                turned = value.T
                for places in (HIGH_AT, LOW_AT):
                    put_pair(forward, 6 * a + places[b], value)
                    put_pair(backward, 6 * (2 - a) + places[2 - b], turned)

    copied.enc_conv1.wait()
    stack_conv(scratch.enc_conv1, 0, c, scratch.fe1, scratch.be1)
    copied.enc_conv2.wait()
    stack_conv(scratch.enc_conv2, 0, c, scratch.fe2, scratch.be2)
    copied.reducer_weight.wait()
    for k in range(4):
        value = scratch.reducer_weight[k * c : (k + 1) * c, :]
        turned = value.T
        for block in (k, k + 4):
            put_pair(scratch.f_down, block, value)
        for block in (0, 1):
            put_pair(scratch.b_down.at[k], block, turned)
    copied.up_weight.wait()
    for k in range(4):
        value = scratch.up_weight[k * c : (k + 1) * c, :]
        turned = value.T
        for block in (0, 1):
            put_pair(scratch.f_up.at[k], block, value)
        for block in (k, k + 4):
            put_pair(scratch.b_up, block, turned)
    copied.dec_conv1.wait()
    stack_conv(scratch.dec_conv1, 0, 2 * c, scratch.fd1a, scratch.bd1a)
    stack_conv(scratch.dec_conv1, 1, 2 * c, scratch.fd1b, scratch.bd1b)
    copied.dec_conv2.wait()
    stack_conv(scratch.dec_conv2, 0, c, scratch.fd2, scratch.bd2)
    copied.skip_weight.wait()
    for half in range(2):
        value = scratch.skip_weight[half * c : (half + 1) * c, :]
        turned = value.T
        for block in (half, half + 2):
            put_pair(scratch.f_skip, block, value)
        for block in (0, 1):
            put_pair(scratch.b_skip.at[half], block, turned)

    for buffer in (scratch.xe1, scratch.xe2, scratch.xd1a, scratch.xd1b, scratch.xd2, scratch.xg):
        edge = jnp.zeros((width, 6 * c), BF16)
        buffer[0:width, :] = edge
        buffer[cells + width : cells + 2 * width, :] = edge

    lift = scratch.lift
    lift[...] = jnp.zeros(lift.shape, F32)
    lift[0:history, :] = inputs.lift_weight[...]
    lift[history : history + 1, :] = inputs.lift_bias[...]

    block = 2 * width
    column = lax.rem(lax.broadcasted_iota(jnp.int32, (block, c), 0), width)
    at_first, at_last = column == 0, column == width - 1
    zeros8 = jnp.zeros((8, c), F32)
    ones16 = group_ones(c, c // GROUPS)
    ones32 = group_ones(c, 2 * c // GROUPS)
    count16 = float(cells * (c // GROUPS))
    count32 = float(cells * (2 * c // GROUPS))

    def grid_rows(step, carry=0):
        return lax.fori_loop(0, cells // block, step, carry, unroll=2)

    def row_at(h):
        return pl.ds(pl.multiple_of(h * block, block), block)

    def chunk_at(i):
        return pl.ds(pl.multiple_of(i * CHUNK, CHUNK), CHUNK)

    def put_row(target, h, value):
        rows = pl.ds(pl.multiple_of(h * block + width, width), block)
        left = jnp.where(at_first, 0.0, pltpu.roll(value, 1, 0))
        right = jnp.where(at_last, 0.0, pltpu.roll(value, block - 1, 0))
        for b, piece in enumerate((left, value, right)):
            high, low = split(piece)
            target[rows, HIGH_AT[b] * c : (HIGH_AT[b] + 1) * c] = high
            target[rows, LOW_AT[b] * c : (LOW_AT[b] + 1) * c] = low

    def put_turned(target, columns, value, first=0, second=1):
        high, low = split(value.T)
        target[first * c : (first + 1) * c, columns] = high
        target[second * c : (second + 1) * c, columns] = low

    def conv_chunk(pairs, i):
        total = None
        for data, weight in pairs:
            taps = []
            for a in range(3):
                rows = pl.ds(pl.multiple_of(i * CHUNK + a * width, width), CHUNK)
                taps.append(data[rows, :])
            part = dot(jnp.concatenate(taps, axis=1), weight[...])
            total = part if total is None else total + part
        return total

    def norm_of(first, second, ones, count):
        one, two = group_sums(first, second, ones)
        mean = one / count
        return mean, lax.rsqrt(two / count - mean * mean + EPS)

    def activate(source, target, turned, slope, scale, shift):
        def step(h, carry):
            value = source[row_at(h), :] * scale + shift
            below, density = normal(value)
            slope[row_at(h), :] = below + value * density
            value = value * below
            put_row(target, h, value)
            put_turned(turned, row_at(h), value)
            return carry

        grid_rows(step)

    def conv_norm(pairs, target):
        def step(i, carry):
            value = fold(conv_chunk(pairs, i))
            target[chunk_at(i), :] = value
            return carry[0] + tile_sums(value), carry[1] + tile_sums(value * value)

        return lax.fori_loop(0, cells // CHUNK, step, (zeros8, zeros8))

    def sums_of(source):
        def step(h, carry):
            value = source[row_at(h), :]
            return carry[0] + tile_sums(value), carry[1] + tile_sums(value * value)

        return grid_rows(step, (zeros8, zeros8))

    step_here = jnp.full((1, c), inputs.step_index[row], jnp.int32)

    def condition(table):
        total = jnp.zeros((1, 2 * c), F32)
        chosen = jnp.concatenate([step_here, step_here], axis=1)
        for s in range(table.shape[0]):
            total = total + jnp.where(chosen == s, table[s : s + 1, :], 0.0)
        return total[:, :c], total[:, c:]

    frames_in[row] = frames_from[row]
    mask_in[row] = mask_from[row]
    for copy in frame_copies:
        copy.wait_recv()
    fields = scratch.fields
    fields[...] = jnp.zeros(fields.shape, F32)
    frame_of = lax.broadcasted_iota(jnp.int32, (history, width), 0) // FIELDS
    keep = (frame_of >= HIST - inputs.counts[row]).astype(F32)
    masks = []
    for source in range(line):
        for k in range(strip):
            columns = slice((source * strip + k) * width, (source * strip + k + 1) * width)
            mask = mask_in[source, k : k + 1, :].astype(F32)
            masks.append(mask)
            fields[0:history, columns] = frames_in[source, :, k, :] * keep * mask
            fields[history : history + 1, columns] = mask
    lifted = scratch.lifted
    lifted[...] = dot_three(fields[...], lift[...], TN)

    enc_scale, enc_shift = condition(inputs.enc_step_table)
    dec_scale, dec_shift = condition(inputs.dec_step_table)

    mean_e1, inv_e1 = norm_of(*sums_of(lifted), ones16, count16)
    gain_e1, bias_e1 = inputs.enc_norm1_gain[...], inputs.enc_norm1_bias[...]
    a_e1 = inv_e1 * gain_e1
    activate(lifted, scratch.xe1, scratch.te1, scratch.slope_e1, a_e1, bias_e1 - mean_e1 * a_e1)
    middle_e = scratch.middle_e
    mean_e2, inv_e2 = norm_of(
        *conv_norm([(scratch.xe1, scratch.fe1)], middle_e), ones16, count16
    )
    gain_e2, bias_e2 = inputs.enc_norm2_gain[...], inputs.enc_norm2_bias[...]
    a_e2 = inv_e2 * gain_e2
    activate(
        middle_e,
        scratch.xe2,
        scratch.te2,
        scratch.slope_e2,
        a_e2 * (1.0 + enc_scale),
        (bias_e2 - mean_e2 * a_e2) * (1.0 + enc_scale) + enc_shift,
    )
    cot_swap.second()
    encoded = scratch.encoded
    conv2_bias = inputs.enc_conv2_bias[...]
    joined = scratch.joined

    def encode(i, carry):
        value = fold(conv_chunk([(scratch.xe2, scratch.fe2)], i))
        value = value + conv2_bias + lifted[chunk_at(i), :]
        encoded[chunk_at(i), :] = value
        high, low = split(value)
        joined[chunk_at(i), c : 2 * c] = high
        joined[chunk_at(i), 3 * c : 4 * c] = low
        put_turned(scratch.turned, chunk_at(i), value, 1, 3)
        return carry[0] + tile_sums(value), carry[1] + tile_sums(value * value)

    sums_enc = lax.fori_loop(0, cells // CHUNK, encode, (zeros8, zeros8))

    half_cells, quarter = cells // 2, cells // 4

    def pick(source):
        pieces = []
        for b in range(2):
            value = source[pl.ds(b, half_cells, stride=2), :]
            value = value.reshape(height // 2, 2, width // 2, c)
            pieces.append([value[:, a].reshape(quarter, c) for a in range(2)])
        return [pieces[b][a] for a in range(2) for b in range(2)]

    def place_cells(target, pieces):
        for b in range(2):
            both = [pieces[2 * a + b].reshape(height // 2, 1, width // 2, c) for a in range(2)]
            value = jnp.concatenate(both, axis=1).reshape(half_cells, c)
            target[pl.ds(b, half_cells, stride=2), :] = value

    x_down = scratch.x_down
    for k, piece in enumerate(pick(encoded)):
        high, low = split(piece)
        x_down[:, k * c : (k + 1) * c] = high
        x_down[:, (k + 4) * c : (k + 5) * c] = low
    lowered = fold(dot(x_down[...], scratch.f_down[...])) + inputs.reducer_bias[...]
    x_up = scratch.x_up
    high, low = split(lowered)
    x_up[:, 0:c] = high
    x_up[:, c : 2 * c] = low
    raised = scratch.raised
    up_bias = inputs.up_bias[...]
    place_cells(
        raised, [fold(dot(x_up[...], scratch.f_up[k])) + up_bias for k in range(4)]
    )

    def raise_row(h, carry):
        value = raised[row_at(h), :]
        high, low = split(value)
        joined[row_at(h), 0:c] = high
        joined[row_at(h), 2 * c : 3 * c] = low
        put_turned(scratch.turned, row_at(h), value, 0, 2)
        return carry[0] + tile_sums(value), carry[1] + tile_sums(value * value)

    sums_raised = grid_rows(raise_row, (zeros8, zeros8))

    halves = []
    for half, (source, sums) in enumerate(((raised, sums_raised), (encoded, sums_enc))):
        mean, inv = norm_of(*sums, ones32, count32)
        gain = inputs.dec_norm1_gain[half : half + 1, :]
        bias = inputs.dec_norm1_bias[half : half + 1, :]
        scale = inv * gain
        activate(
            source,
            (scratch.xd1a, scratch.xd1b)[half],
            scratch.td1.at[2 * c * half : 2 * c * (half + 1)],
            (scratch.slope_d1a, scratch.slope_d1b)[half],
            scale,
            bias - mean * scale,
        )
        halves.append((source, mean, inv, gain))
    middle_d = scratch.middle_d
    pairs = [(scratch.xd1a, scratch.fd1a), (scratch.xd1b, scratch.fd1b)]
    mean_d2, inv_d2 = norm_of(*conv_norm(pairs, middle_d), ones16, count16)
    cot_swap.third()
    gain_d2, bias_d2 = inputs.dec_norm2_gain[...], inputs.dec_norm2_bias[...]
    a_d2 = inv_d2 * gain_d2
    activate(
        middle_d,
        scratch.xd2,
        scratch.td2,
        scratch.slope_d2,
        a_d2 * (1.0 + dec_scale),
        (bias_d2 - mean_d2 * a_d2) * (1.0 + dec_scale) + dec_shift,
    )
    exchanges = []
    waiting_runs = list(runs)
    landing_at = 0
    sem_at = 3 * (line - 1) + 20
    sums, final = scratch.sums, scratch.final

    def begin():
        nonlocal landing_at, sem_at
        start, rows = waiting_runs.pop(0)
        kind = KINDS[len(exchanges)]
        exchange = kind(place, start, rows, landing_at, sem_at)
        landing_at += exchange.land_rows()
        sem_at += exchange.count()
        exchanges.append(exchange)
        exchange.advance()

    final_copies = []

    def advance(k):
        exchange = exchanges[k]
        exchange.advance()
        if exchange.done():
            rows = pl.ds(exchange.start, exchange.rows)
            copy = pltpu.make_async_copy(
                final.at[rows], outputs.gradients.at[rows], local_sem.at[11 + k]
            )
            copy.start()
            final_copies.append(copy)

    due = list(DUE)

    def point():
        for k in due.pop(0):
            advance(k)

    def small_row(k, value):
        sums[small_at + k : small_at + k + 1, :] = value

    def spread_grad(source):
        def step(h, carry):
            value = source[row_at(h), :]
            put_row(scratch.xg, h, value)
            return carry + tile_sums(value)

        return grid_rows(step, zeros8)

    def weight_grad(turned, at, depth, a):
        rows = pl.ds((2 - a) * width, cells)
        both = dot(turned[...], scratch.xg[rows, :])
        for half in range(depth // c):
            part = fold_rows(both[2 * c * half : 2 * c * (half + 1)])
            for b in range(3):
                high, low = HIGH_AT[2 - b] * c, LOW_AT[2 - b] * c
                to = at + (3 * a + b) * depth + half * c
                sums[to : to + c, :] = part[:, high : high + c] + part[:, low : low + c]

    def back_conv(weight, slope, target, source, mean, inv):
        carry = (zeros8, zeros8)
        for i in range(cells // CHUNK):
            value = fold(conv_chunk([(scratch.xg, weight)], i)) * slope[chunk_at(i), :]
            target[chunk_at(i), :] = value
            normed = (source[chunk_at(i), :] - mean) * inv
            carry = (carry[0] + tile_sums(value), carry[1] + tile_sums(value * normed))
            if i % (cells // CHUNK // 2) == cells // CHUNK // 2 - 1:
                point()
        return carry

    def norm_grad(sums_in, scale, ones, count):
        one, two = group_sums(sums_in[0] * scale, sums_in[1] * scale, ones)
        return one / count, two / count

    cot[here_rows] = cot_from[row]
    cot_swap.arrive()
    total_cot = column_sum(spread_grad(cot))
    for a in range(3):
        weight_grad(scratch.td2, starts.dec_conv2, c, a)
    part = fold(dot(scratch.turned[...], scratch.xg[width : cells + width, 2 * c : 4 * c]))
    sums[starts.skip_weight : starts.skip_weight + 2 * c, :] = fold_rows(part)
    small_row(3, total_cot)
    begin()

    result = scratch.result
    last_bias = inputs.dec_conv2_bias[...] + inputs.skip_bias[...]

    def decode(i, carry):
        value = conv_chunk([(scratch.xd2, scratch.fd2)], i)
        value = value + dot(joined[chunk_at(i), :], scratch.f_skip[...])
        result[chunk_at(i), :] = fold(value) + last_bias
        return carry

    lax.fori_loop(0, cells // CHUNK, decode, 0)
    output_here, frames_here = scratch.output_here, scratch.frames_here
    output_here[row] = result[here_rows]
    output_swap = LineSwap(
        place.line,
        lambda to: strip_of(result, to),
        lambda source: output_here.at[source],
        scratch.output_inward,
        scratch.output_across,
        make,
    )
    output_swap.first()

    point()

    grad = scratch.grad
    sums_d2 = back_conv(scratch.bd2, scratch.slope_d2, grad, middle_d, mean_d2, inv_d2)
    side_grads = (scratch.grad_a, scratch.grad_b)
    for half in range(2):

        def skip_back(i, carry, half=half):
            rows = pl.ds(pl.multiple_of(i * CHUNK + width, width), CHUNK)
            value = dot(scratch.xg[rows, 2 * c : 4 * c], scratch.b_skip[half])
            side_grads[half][chunk_at(i), :] = fold(value)
            return carry

        lax.fori_loop(0, cells // CHUNK, skip_back, 0)
    point()

    def table_rows(k, sums_in, gain, bias, one_plus):
        plain, times = column_sum(sums_in[0]), column_sum(sums_in[1])
        for s in range(inputs.enc_step_table.shape[0]):
            small_row(k + 2 * s, jnp.where(step_here == s, gain * times + bias * plain, 0.0))
            small_row(k + 2 * s + 1, jnp.where(step_here == s, plain, 0.0))
        return one_plus * times, one_plus * plain

    def middle_grad(source, mean, inv, scale, sums_in):
        zero, slope = norm_grad(sums_in, scale, ones16, count16)

        def step(h, carry):
            normed = (source[row_at(h), :] - mean) * inv
            value = inv * (grad[row_at(h), :] * scale - zero - normed * slope)
            put_row(scratch.xg, h, value)
            return carry

        grid_rows(step)

    gain_row, bias_row = table_rows(16, sums_d2, gain_d2, bias_d2, 1.0 + dec_scale)
    small_row(8, gain_row)
    small_row(9, bias_row)
    middle_grad(middle_d, mean_d2, inv_d2, gain_d2 * (1.0 + dec_scale), sums_d2)
    point()
    output_swap.second()
    for a in range(3):
        weight_grad(scratch.td1, starts.dec_conv1, 2 * c, a)
        point()
        begin()

    for half, (source, mean, inv, gain) in enumerate(halves):
        sums_in = back_conv(
            (scratch.bd1a, scratch.bd1b)[half],
            (scratch.slope_d1a, scratch.slope_d1b)[half],
            grad,
            source,
            mean,
            inv,
        )
        small_row(4 + half, column_sum(sums_in[1]))
        small_row(6 + half, column_sum(sums_in[0]))
        zero, slope = norm_grad(sums_in, gain, ones32, count32)
        target = side_grads[half]

        def input_grad(h, carry):
            normed = (source[row_at(h), :] - mean) * inv
            value = inv * (grad[row_at(h), :] * gain - zero - normed * slope)
            value = target[row_at(h), :] + value
            target[row_at(h), :] = value
            return carry + tile_sums(value)

        total = grid_rows(input_grad, zeros8)
        if half == 0:
            small_row(2, column_sum(total))
        point()

    output_swap.third()
    grad_raised, grad_encoded = side_grads
    x_grad_up = scratch.x_grad_up
    for k, piece in enumerate(pick(grad_raised)):
        high, low = split(piece)
        x_grad_up[:, k * c : (k + 1) * c] = high
        x_grad_up[:, (k + 4) * c : (k + 5) * c] = low
    grad_lowered = fold(dot(x_grad_up[...], scratch.b_up[...]))
    small_row(1, jnp.sum(grad_lowered, axis=0, keepdims=True))
    x_grad_low = scratch.x_grad_low
    high, low = split(grad_lowered)
    x_grad_low[:, 0:c] = high
    x_grad_low[:, c : 2 * c] = low
    point()
    part = fold(fold_rows(dot(x_up[...], x_grad_up[...], TN)))
    for k in range(4):
        at = starts.up_weight + k * c
        sums[at : at + c, :] = part[:, k * c : (k + 1) * c]
    part = fold_rows(fold(dot(x_down[...], x_grad_low[...], TN)))
    sums[starts.reducer_weight : starts.reducer_weight + 4 * c, :] = part
    point()
    begin()
    place_cells(
        grad, [fold(dot(x_grad_low[...], scratch.b_down[k])) for k in range(4)]
    )

    def join_row(h, carry):
        value = grad_encoded[row_at(h), :] + grad[row_at(h), :]
        grad_encoded[row_at(h), :] = value
        put_row(scratch.xg, h, value)
        return carry + tile_sums(value)

    small_row(0, column_sum(grid_rows(join_row, zeros8)))
    for k in range(10, 16):
        small_row(k, jnp.zeros((1, c), F32))
    sums[small_at + 24 : small_at + LATE, :] = jnp.zeros((LATE - 24, c), F32)
    point()
    for a in range(3):
        weight_grad(scratch.te2, starts.enc_conv2, c, a)
        point()
    begin()
    sums_e2 = back_conv(scratch.be2, scratch.slope_e2, grad, middle_e, mean_e2, inv_e2)
    gain_row, bias_row = table_rows(LATE + 24, sums_e2, gain_e2, bias_e2, 1.0 + enc_scale)
    small_row(LATE + 18, gain_row)
    small_row(LATE + 19, bias_row)
    middle_grad(middle_e, mean_e2, inv_e2, gain_e2 * (1.0 + enc_scale), sums_e2)
    point()
    for a in range(3):
        weight_grad(scratch.te1, starts.enc_conv1, c, a)
        point()
        if a:
            begin()
    sums_e1 = back_conv(scratch.be1, scratch.slope_e1, grad, lifted, mean_e1, inv_e1)
    small_row(LATE + 16, column_sum(sums_e1[1]))
    small_row(LATE + 17, column_sum(sums_e1[0]))
    zero, slope = norm_grad(sums_e1, gain_e1, ones16, count16)

    def lifted_grad(h, carry):
        normed = (lifted[row_at(h), :] - mean_e1) * inv_e1
        value = inv_e1 * (grad[row_at(h), :] * gain_e1 - zero - normed * slope)
        grad[row_at(h), :] = grad_encoded[row_at(h), :] + value
        return carry

    grid_rows(lifted_grad)
    point()

    late_at = small_at + LATE
    sums[late_at : late_at + 16, :] = dot_three(fields[...], grad[...])
    sums[late_at + 20 : late_at + 24, :] = jnp.zeros((4, c), F32)
    point()
    begin()
    back = dot_three(lift[...], grad[...], NT)
    frames_out = scratch.frames_out
    for source in range(line):
        for k in range(strip):
            h = source * strip + k
            value = back[0:history, h * width : (h + 1) * width]
            frames_out[source, :, k, :] = value * keep * masks[h]
    frames_here[row] = frames_out[row]
    for k in range(1, line):
        to = lax.rem(row + k, line)
        output_copies.append(
            send(frames_out.at[to], frames_here.at[row], device_at(to))
        )

    output_swap.arrive()
    own_output = pltpu.make_async_copy(output_here, outputs.output, local_sem.at[10])
    own_output.start()
    for k in REST:
        advance(k)
    assert not due and all(exchange.done() for exchange in exchanges)

    for copy in output_copies:
        copy.wait_recv()
    own_frames = pltpu.make_async_copy(
        frames_here, outputs.frames_grad, local_sem.at[11 + len(runs)]
    )
    own_frames.start()
    own_output.wait()
    own_frames.wait()
    for copy in final_copies:
        copy.wait()
    for copy in frame_copies + output_copies:
        copy.wait_send()
    cot_swap.sent()
    output_swap.sent()
    for exchange in exchanges:
        for copy, only in exchange.copies:
            if only is None:
                copy.wait_send()
            else:
                pl.when(only)(copy.wait_send)


def write_kernel(layout, *refs):
    shapes, starts, small_at = layout
    output, frames_grad, gradients = refs[:3]
    outputs = refs[3:-4]
    output_here, frames_here, gradients_here, sem = refs[-4:]
    c = gradients.shape[1]
    moves = [(frames_grad, frames_here, outputs[1])]
    for k, name in enumerate(LARGE):
        rows = pl.ds(starts[name], shapes[name][0])
        moves.append((gradients.at[rows], gradients_here.at[rows], outputs[2 + k]))
    moves.append((output, output_here, outputs[0]))
    small = pl.ds(small_at, SMALL_COUNT)
    first = pltpu.make_async_copy(gradients.at[small], gradients_here.at[small], sem.at[0])
    first.start()
    arriving, leaving = [], []
    for k, (source, here, _) in enumerate(moves):
        arriving.append(pltpu.make_async_copy(source, here, sem.at[1 + 2 * k]))
        arriving[-1].start()
    first.wait()
    for target, (k, rows) in zip(outputs[2 + len(LARGE) :], SMALL_ROWS.values()):
        at = small_at + k
        if rows == 8:
            for s in range(target.shape[0]):
                target[s : s + 1, 0:c] = gradients_here[at + 2 * s : at + 2 * s + 1, :]
                target[s : s + 1, c : 2 * c] = gradients_here[at + 2 * s + 1 : at + 2 * s + 2, :]
        else:
            target[...] = gradients_here[at : at + rows, :]
    for k, (_, here, target) in enumerate(moves):
        arriving[k].wait()
        leaving.append(pltpu.make_async_copy(here, target, sem.at[2 + 2 * k]))
        leaving[-1].start()
    for copy in leaving:
        copy.wait()


def whole_items(shape, *arguments):
    line = shape["rows"]
    whole = Given(*arguments)
    given = whole._asdict()
    frames, cotangent = whole.frames, whole.cotangent
    items, history, strip, width = frames.shape
    c = cotangent.shape[-1]
    cells = strip * line * width
    flat = {}
    for name, value in given.items():
        if value is cotangent:
            value = value.reshape(items, strip * width, c)
        elif name in LARGE:
            value = value.reshape(-1, c)
        elif value.ndim == 1 and name not in IN_SMEM:
            value = value.reshape(-1, c)
        flat[name] = value
    shapes = {name: flat[name].shape for name in LARGE}
    big_layout = layout_of(SimpleNamespace(**shapes))
    starts, small_at, total_rows, runs = big_layout
    copies = 20 + 3 * (line - 1) + len(runs) * (8 + 2 * (line - 1)) + 6
    landing = sum(rows // 2 + 5 * rows // 8 for _, rows in runs) + LATE_COUNT * (8 + line)
    shifted = pltpu.VMEM((cells + 2 * width, 6 * c), BF16)
    forward = pltpu.VMEM((18 * c, 2 * c), BF16)
    backward = forward
    field = pltpu.VMEM((cells, c), F32)
    flipped_field = pltpu.VMEM((2 * c, cells), BF16)
    quarter = cells // 4
    scratch = dict(
        small=pltpu.VMEM((LATE_COUNT, c), F32),
        send=pltpu.SemaphoreType.DMA((copies,)),
        recv=pltpu.SemaphoreType.DMA((copies,)),
        local=pltpu.SemaphoreType.DMA((12 + len(runs),)),
        sums=pltpu.VMEM((total_rows, c), F32),
        final=pltpu.VMEM((total_rows, c), F32),
        landing=pltpu.VMEM((landing, c), F32),
        frames_in=pltpu.VMEM((line, history, strip, width), F32),
        mask_in=pltpu.VMEM((line, strip, width), jnp.int32),
        frames_out=pltpu.VMEM((line, history, strip, width), F32),
        frames_from=pltpu.VMEM((line, history, strip, width), F32),
        frames_here=pltpu.VMEM((line, history, strip, width), F32),
        mask_from=pltpu.VMEM((line, strip, width), jnp.int32),
        cot_from=pltpu.VMEM((items, strip * width, c), F32),
        output_here=pltpu.VMEM((items, strip * width, c), F32),
        cot_inward=pltpu.VMEM((2, strip * width, c), F32),
        cot_across=pltpu.VMEM((2, strip * width, c), F32),
        output_inward=pltpu.VMEM((2, strip * width, c), F32),
        output_across=pltpu.VMEM((2, strip * width, c), F32),
        fields=pltpu.VMEM((16, cells), F32),
        lift=pltpu.VMEM((16, c), F32),
        joined=pltpu.VMEM((cells, 4 * c), BF16),
        x_down=pltpu.VMEM((quarter, 8 * c), BF16),
        x_grad_up=pltpu.VMEM((quarter, 8 * c), BF16),
        x_up=pltpu.VMEM((quarter, 2 * c), BF16),
        x_grad_low=pltpu.VMEM((quarter, 2 * c), BF16),
        f_down=pltpu.VMEM((8 * c, 2 * c), BF16),
        b_down=pltpu.VMEM((4, 2 * c, 2 * c), BF16),
        f_up=pltpu.VMEM((4, 2 * c, 2 * c), BF16),
        b_up=pltpu.VMEM((8 * c, 2 * c), BF16),
        f_skip=pltpu.VMEM((4 * c, 2 * c), BF16),
        b_skip=pltpu.VMEM((2, 2 * c, 2 * c), BF16),
        xe1=shifted,
        xe2=shifted,
        xd1a=shifted,
        xd1b=shifted,
        xd2=shifted,
        xg=shifted,
        te1=flipped_field,
        te2=flipped_field,
        td1=pltpu.VMEM((4 * c, cells), BF16),
        td2=flipped_field,
        turned=pltpu.VMEM((4 * c, cells), BF16),
        fe1=forward,
        fe2=forward,
        fd1a=forward,
        fd1b=forward,
        fd2=forward,
        be1=backward,
        be2=backward,
        bd1a=backward,
        bd1b=backward,
        bd2=backward,
        slope_e1=field,
        slope_e2=field,
        slope_d1a=field,
        slope_d1b=field,
        slope_d2=field,
        lifted=field,
        middle_e=field,
        encoded=field,
        raised=field,
        middle_d=field,
        result=field,
        cot=field,
        grad=field,
        grad_a=field,
        grad_b=field,
    )
    scratch.update({name: pltpu.VMEM(shapes[name], F32) for name in LARGE})

    in_hbm = pl.BlockSpec(memory_space=pl.ANY)
    in_vmem = pl.BlockSpec(memory_space=pltpu.VMEM)
    in_smem = pl.BlockSpec(memory_space=pltpu.SMEM)
    in_specs = [
        in_hbm if name in IN_HBM else in_smem if name in IN_SMEM else in_vmem
        for name in ARGUMENTS
    ]
    out_shape = [
        jax.ShapeDtypeStruct((items, strip * width, c), F32),
        jax.ShapeDtypeStruct(frames.shape, F32),
        jax.ShapeDtypeStruct((total_rows, c), F32),
    ]
    out_specs = [in_hbm] * 3
    results = pl.pallas_call(
        functools.partial(
            item_kernel,
            (line, strip, width, shapes, big_layout),
            tuple(scratch),
        ),
        out_shape=out_shape,
        in_specs=in_specs,
        out_specs=out_specs,
        scratch_shapes=list(scratch.values()),
        compiler_params=pltpu.CompilerParams(
            collective_id=0, has_side_effects=True, vmem_limit_bytes=62 * 1024 * 1024
        ),
    )(*[flat[name] for name in ARGUMENTS])
    names = LARGE + tuple(SMALL_ROWS)
    written = pl.pallas_call(
        functools.partial(write_kernel, (shapes, starts, small_at)),
        out_shape=out_shape[:2] + [jax.ShapeDtypeStruct(flat[name].shape, F32) for name in names],
        in_specs=[pl.BlockSpec(memory_space=pltpu.HBM)] * 3,
        out_specs=[in_hbm] * (2 + len(LARGE)) + [in_vmem] * len(SMALL_ROWS),
        scratch_shapes=[
            pltpu.VMEM((items, strip * width, c), F32),
            pltpu.VMEM(frames.shape, F32),
            pltpu.VMEM((total_rows, c), F32),
            pltpu.SemaphoreType.DMA((1 + 2 * (2 + len(LARGE)),)),
        ],
        compiler_params=pltpu.CompilerParams(vmem_limit_bytes=60 * 1024 * 1024),
    )(*results)
    grads = dict(zip(names, written[2:]))
    ordered = [name for name in ARGUMENTS if name in grads]
    return (written[0].reshape(cotangent.shape), written[1]) + tuple(
        grads[name].reshape(given[name].shape) for name in ordered
    )


def body(shape, *arguments):
    items, _, strip, width = arguments[0].shape
    line = shape["rows"]
    whole = (
        shape["section"] == 2
        and shape["batch"] == 4
        and items == line == 4
        and arguments[-1].shape[-1] == 128
        and (strip * line * width) % CHUNK == 0
    )
    return whole_items(shape, *arguments) if whole else strips_body(*arguments)


def solution(mesh):
    in_specs = (
        P(("section", "batch"), None, "rows", None),
        P(("section", "batch")),
        P(("section", "batch"), "rows", None),
        P(("section", "batch")),
        P(),
        P(),
        P(),
        P(),
        P(),
        P(),
        P(),
        P(),
        P(),
        P(),
        P(),
        P(),
        P(),
        P(),
        P(),
        P(),
        P(),
        P(),
        P(),
        P(),
        P(),
        P(),
        P(),
        P(),
        P(("section", "batch"), "rows", None, None),
    )
    out_specs = (
        P(("section", "batch"), "rows", None, None),
        P(("section", "batch"), None, "rows", None),
        P(),
        P(),
        P(),
        P(),
        P(),
        P(),
        P(),
        P(),
        P(),
        P(),
        P(),
        P(),
        P(),
        P(),
        P(),
        P(),
        P(),
        P(),
        P(),
        P(),
        P(),
        P(),
        P(),
        P(),
    )
    return jax.shard_map(functools.partial(body, mesh.shape), mesh=mesh, in_specs=in_specs, out_specs=out_specs, check_vma=False)
```

```python
import functools
from types import SimpleNamespace
from typing import Any, NamedTuple

import jax
import jax.numpy as jnp
from jax import lax
from jax.experimental import pallas as pl
from jax.experimental.pallas import tpu as pltpu
from jax.sharding import PartitionSpec as P

GROUPS = 8
FIELDS = 3
HIST = 4


EPS = 1e-05
HIGH = lax.Precision.HIGHEST


def extended(cells, sides, width):
    for axis, dim in sides:
        count = lax.axis_size(axis)
        ends = count - 1
        head = lax.slice_in_dim(cells, 0, width, axis=dim)
        tail = lax.slice_in_dim(cells, cells.shape[dim] - width, cells.shape[dim], axis=dim)
        cells = jnp.concatenate(
            [
                lax.ppermute(tail, axis, [(i, (i + 1) % count) for i in range(ends)]),
                cells,
                lax.ppermute(head, axis, [((i + 1) % count, i) for i in range(ends)]),
            ],
            axis=dim,
        )
    return cells


def from_behind(value, axis, steps):
    count = lax.axis_size(axis)
    pairs = [(source, (source + steps) % count) for source in range(count)]
    return lax.ppermute(value, axis, pairs)


def group_view(value_arrays):
    extent = value_arrays.shape
    return value_arrays.reshape(extent[:-1] + (GROUPS, extent[-1] // GROUPS))


def global_sums(value_arrays):
    grouped = group_view(value_arrays)
    flat = grouped.reshape(-1, GROUPS, grouped.shape[-1])
    first_sum = jnp.sum(flat, axis=(0, 2))
    second_sum = jnp.sum(flat * flat, axis=(0, 2))
    return lax.psum((first_sum, second_sum), "rows")


def apply_norm(value_arrays, sum_one, sum_two, norm_gain, norm_bias, total):
    grouped = group_view(value_arrays)
    group_mean = sum_one / total
    variance = sum_two / total - group_mean * group_mean
    inverse = lax.rsqrt(variance + EPS)
    normed = (grouped - group_mean[:, None]) * inverse[:, None]
    return normed.reshape(value_arrays.shape) * norm_gain + norm_bias


def norm_back(value_arrays, grad_one, grad_two):
    grouped = group_view(value_arrays)
    extra = grad_one[:, None] + 2.0 * grouped * grad_two[:, None]
    return extra.reshape(value_arrays.shape)


def reduce_grads(grad_one, grad_two):
    return lax.psum((grad_one, grad_two), "rows")


def conv_rows(padded, kernel):
    widened = jnp.pad(padded, ((0, 0), (1, 1), (0, 0)))
    return lax.conv_general_dilated(
        widened[None],
        kernel,
        (1, 1),
        "VALID",
        dimension_numbers=("NHWC", "HWIO", "NHWC"),
        precision=HIGH,
    )[0]


def flipped(kernel):
    return jnp.transpose(kernel[::-1, ::-1], (0, 1, 3, 2))


def pad_grads(value_arrays):
    return extended(value_arrays, (("rows", 0),), 1)


def totals_of(inputs, conv1):
    strip = inputs.shape[0]
    cells = strip * lax.axis_size("rows") * inputs.shape[1]
    return (cells * (inputs.shape[2] // GROUPS), cells * (conv1.shape[3] // GROUPS))


def block_forward(inputs, weights, scale_part, shift_part):
    norm1_gain, norm1_bias, conv1, norm2_gain, norm2_bias, conv2, conv2_bias = weights
    total_in, total_mid = totals_of(inputs, conv1)
    sums_in = global_sums(inputs)

    def pad_rows(value_arrays):
        return extended(value_arrays, (("rows", 0),), 1)

    act_one = pad_rows(
        jax.nn.gelu(
            apply_norm(inputs, sums_in[0], sums_in[1], norm1_gain, norm1_bias, total_in),
            approximate=False,
        )
    )
    middle = conv_rows(act_one, conv1)
    sums_mid = global_sums(middle)
    shaped = (
        apply_norm(middle, sums_mid[0], sums_mid[1], norm2_gain, norm2_bias, total_mid)
        * (1.0 + scale_part)
        + shift_part
    )
    act_two = pad_rows(jax.nn.gelu(shaped, approximate=False))
    branch = conv_rows(act_two, conv2) + conv2_bias
    return (branch, (sums_in[0], sums_in[1], act_one, middle, sums_mid[0], sums_mid[1], act_two))


def block_backward(inputs, weights, scale_part, shift_part, kept, grad_out):
    norm1_gain, norm1_bias, conv1, norm2_gain, norm2_bias, conv2, conv2_bias = weights
    in_one, in_two, act_one, middle, mid_one, mid_two, act_two = kept
    total_in, total_mid = totals_of(inputs, conv1)
    grad_conv2 = jax.vjp(lambda kernel: conv_rows(act_two, kernel), conv2)[1](grad_out)[0]
    grad_bias2 = jnp.sum(grad_out, axis=(0, 1))
    grad_act_two = conv_rows(pad_grads(grad_out), flipped(conv2))

    def second_piece(middle_in, sum_one, sum_two, gain_in, incoming_bias, scale_in, shift_in):
        shaped = (
            apply_norm(middle_in, sum_one, sum_two, gain_in, incoming_bias, total_mid)
            * (1.0 + scale_in)
            + shift_in
        )
        return jax.nn.gelu(shaped, approximate=False)

    second_pull = jax.vjp(
        second_piece, middle, mid_one, mid_two, norm2_gain, norm2_bias, scale_part, shift_part
    )[1](grad_act_two)
    summed_one, summed_two = reduce_grads(second_pull[1], second_pull[2])
    grad_middle = second_pull[0] + norm_back(middle, summed_one, summed_two)
    grad_conv1 = jax.vjp(lambda kernel: conv_rows(act_one, kernel), conv1)[1](grad_middle)[0]
    grad_act_one = conv_rows(pad_grads(grad_middle), flipped(conv1))

    def first_piece(inputs_in, sum_one, sum_two, gain_in, incoming_bias):
        return jax.nn.gelu(
            apply_norm(inputs_in, sum_one, sum_two, gain_in, incoming_bias, total_in),
            approximate=False,
        )

    first_pull = jax.vjp(first_piece, inputs, in_one, in_two, norm1_gain, norm1_bias)[1](
        grad_act_one
    )
    first_one, first_two = reduce_grads(first_pull[1], first_pull[2])
    grad_inputs = first_pull[0] + norm_back(inputs, first_one, first_two)
    grads = (
        first_pull[3],
        first_pull[4],
        grad_conv1,
        second_pull[3],
        second_pull[4],
        grad_conv2,
        grad_bias2,
    )
    return (grad_inputs, grads, second_pull[5], second_pull[6])


def conditioning(step_item, table):
    one_hot = (jnp.arange(table.shape[0], dtype=jnp.int32) == step_item).astype(jnp.float32)
    condition = jnp.dot(one_hot, table, precision=HIGH)
    half_width = table.shape[1] // 2
    return (condition[:half_width], condition[half_width:], one_hot)


def project_in(frames_item, mask_item, count_item, incoming_weight, incoming_bias):
    history = jnp.arange(HIST, dtype=jnp.int32) >= HIST - count_item
    keep = jnp.repeat(history, FIELDS).astype(jnp.float32)
    lifted = (
        jnp.einsum(
            "fhw,fc->hwc", frames_item * keep[:, None, None], incoming_weight, precision=HIGH
        )
        + incoming_bias
    )
    return lifted * mask_item[:, :, None].astype(jnp.float32)


def coarsen_field(value_arrays, incoming_weight, incoming_bias):
    rows_here, width_here, depth_here = value_arrays.shape
    blocks = value_arrays.reshape(rows_here // 2, 2, width_here // 2, 2, depth_here)
    return jnp.einsum("iajbk,abkc->ijc", blocks, incoming_weight, precision=HIGH) + incoming_bias


def upsample(value_arrays, incoming_weight, incoming_bias):
    result = jnp.einsum("ijk,abkc->iajbc", value_arrays, incoming_weight, precision=HIGH)
    extent = result.shape
    return result.reshape(extent[0] * 2, extent[2] * 2, extent[4]) + incoming_bias


def flatten_all(pieces):
    return jnp.concatenate([piece.reshape(-1) for piece in pieces])


def unflatten_all(flat, templates):
    pieces = []
    offset_at = 0
    for template in templates:
        count_here = template.size
        pieces.append(flat[offset_at : offset_at + count_here].reshape(template.shape))
        offset_at += count_here
    return tuple(pieces)


def strips_body(
    frames,
    counts,
    cell_mask,
    step_index,
    lift_weight,
    lift_bias,
    enc_norm1_gain,
    enc_norm1_bias,
    enc_conv1,
    enc_step_table,
    enc_norm2_gain,
    enc_norm2_bias,
    enc_conv2,
    enc_conv2_bias,
    reducer_weight,
    reducer_bias,
    up_weight,
    up_bias,
    dec_norm1_gain,
    dec_norm1_bias,
    dec_conv1,
    dec_step_table,
    dec_norm2_gain,
    dec_norm2_bias,
    dec_conv2,
    dec_conv2_bias,
    skip_weight,
    skip_bias,
    cotangent,
):
    enc_weights = (
        enc_norm1_gain,
        enc_norm1_bias,
        enc_conv1,
        enc_norm2_gain,
        enc_norm2_bias,
        enc_conv2,
        enc_conv2_bias,
    )
    dec_weights = (
        dec_norm1_gain,
        dec_norm1_bias,
        dec_conv1,
        dec_norm2_gain,
        dec_norm2_bias,
        dec_conv2,
        dec_conv2_bias,
    )
    params = (
        lift_weight,
        lift_bias,
        enc_norm1_gain,
        enc_norm1_bias,
        enc_conv1,
        enc_step_table,
        enc_norm2_gain,
        enc_norm2_bias,
        enc_conv2,
        enc_conv2_bias,
        reducer_weight,
        reducer_bias,
        up_weight,
        up_bias,
        dec_norm1_gain,
        dec_norm1_bias,
        dec_conv1,
        dec_step_table,
        dec_norm2_gain,
        dec_norm2_bias,
        dec_conv2,
        dec_conv2_bias,
        skip_weight,
        skip_bias,
    )

    def forward_micro(carry, sliced):
        frames_item, mask_item, count_item, step_item = sliced
        lifted = project_in(frames_item, mask_item, count_item, lift_weight, lift_bias)
        enc_scale, enc_shift, unused_hot = conditioning(step_item, enc_step_table)
        enc_branch, enc_kept = block_forward(lifted, enc_weights, enc_scale, enc_shift)
        encoder_result = lifted + enc_branch
        coarse_field = coarsen_field(encoder_result, reducer_weight, reducer_bias)
        foreign = from_behind(coarse_field, "section", 1)
        raised_foreign = upsample(foreign, up_weight, up_bias)
        raised = from_behind(raised_foreign, "section", 1)
        joined = jnp.concatenate([raised, encoder_result], axis=-1)
        dec_scale, dec_shift, unused_again = conditioning(step_item, dec_step_table)
        dec_branch, dec_kept = block_forward(joined, dec_weights, dec_scale, dec_shift)
        output_item = jnp.dot(joined, skip_weight, precision=HIGH) + skip_bias + dec_branch
        return (carry, (output_item, (lifted, enc_kept, encoder_result, foreign, joined, dec_kept)))

    unused, (output, kept_all) = lax.scan(
        forward_micro, jnp.zeros((), jnp.float32), (frames, cell_mask, counts, step_index)
    )

    def backward_micro(totals, sliced):
        frames_item, mask_item, count_item, step_item, grad_out, kept = sliced
        lifted, enc_kept, encoder_result, foreign, joined, dec_kept = kept
        dec_scale, dec_shift, one_hot = conditioning(step_item, dec_step_table)
        grad_joined, dec_grads, dec_gscale, dec_gshift = block_backward(
            joined, dec_weights, dec_scale, dec_shift, dec_kept, grad_out
        )
        grad_skip_weight = jnp.einsum("hwk,hwc->kc", joined, grad_out, precision=HIGH)
        grad_skip_bias = jnp.sum(grad_out, axis=(0, 1))
        grad_joined = grad_joined + jnp.dot(grad_out, skip_weight.T, precision=HIGH)
        half_width = joined.shape[-1] // 2
        grad_raised = grad_joined[..., :half_width]
        grad_encoded = grad_joined[..., half_width:]
        grad_foreign_up = from_behind(grad_raised, "section", 1)
        up_pull = jax.vjp(upsample, foreign, up_weight, up_bias)[1](grad_foreign_up)
        coarse_gradient = from_behind(up_pull[0], "section", 1)
        reducer_pullback = jax.vjp(coarsen_field, encoder_result, reducer_weight, reducer_bias)[1](
            coarse_gradient
        )
        grad_encoded = grad_encoded + reducer_pullback[0]
        enc_scale, enc_shift, enc_hot = conditioning(step_item, enc_step_table)
        grad_lifted, enc_grads, enc_gscale, enc_gshift = block_backward(
            lifted, enc_weights, enc_scale, enc_shift, enc_kept, grad_encoded
        )
        grad_lifted = grad_lifted + grad_encoded
        proj_pull = jax.vjp(
            lambda frames_in, incoming_weight, incoming_bias: project_in(
                frames_in, mask_item, count_item, incoming_weight, incoming_bias
            ),
            frames_item,
            lift_weight,
            lift_bias,
        )[1](grad_lifted)
        enc_table_grad = enc_hot[:, None] * jnp.concatenate([enc_gscale, enc_gshift])[None, :]
        dec_table_grad = one_hot[:, None] * jnp.concatenate([dec_gscale, dec_gshift])[None, :]
        micro_list = (
            proj_pull[1],
            proj_pull[2],
            enc_grads[0],
            enc_grads[1],
            enc_grads[2],
            enc_table_grad,
            enc_grads[3],
            enc_grads[4],
            enc_grads[5],
            enc_grads[6],
            reducer_pullback[1],
            reducer_pullback[2],
            up_pull[1],
            up_pull[2],
            dec_grads[0],
            dec_grads[1],
            dec_grads[2],
            dec_table_grad,
            dec_grads[3],
            dec_grads[4],
            dec_grads[5],
            dec_grads[6],
            grad_skip_weight,
            grad_skip_bias,
        )
        micro_flat = flatten_all(micro_list)
        return (totals + micro_flat, proj_pull[0])

    total_size = sum((piece.size for piece in params))
    start_totals = jnp.zeros((total_size,), jnp.float32)
    flat_totals, frames_grad = lax.scan(
        backward_micro,
        start_totals,
        (frames, cell_mask, counts, step_index, cotangent, kept_all),
        reverse=True,
    )
    flat_totals = lax.psum(flat_totals, ("section", "batch", "rows"))
    grads = unflatten_all(flat_totals, params)
    return (output, frames_grad) + grads


F32 = jnp.float32
BF16 = jnp.bfloat16
MESH = pl.DeviceIdType.MESH
NN = ((1,), (0,))
NT = ((1,), (1,))
TN = ((0,), (0,))
HIGH_AT = (0, 2, 1)
LOW_AT = (4, 3, 5)
CHUNK = 512
class Given(NamedTuple):
    frames: Any
    counts: Any
    cell_mask: Any
    step_index: Any
    lift_weight: Any
    lift_bias: Any
    enc_norm1_gain: Any
    enc_norm1_bias: Any
    enc_conv1: Any
    enc_step_table: Any
    enc_norm2_gain: Any
    enc_norm2_bias: Any
    enc_conv2: Any
    enc_conv2_bias: Any
    reducer_weight: Any
    reducer_bias: Any
    up_weight: Any
    up_bias: Any
    dec_norm1_gain: Any
    dec_norm1_bias: Any
    dec_conv1: Any
    dec_step_table: Any
    dec_norm2_gain: Any
    dec_norm2_bias: Any
    dec_conv2: Any
    dec_conv2_bias: Any
    skip_weight: Any
    skip_bias: Any
    cotangent: Any


ARGUMENTS = Given._fields
LARGE = tuple(
    dict(
        dec_conv1=0,
        up_weight=0,
        reducer_weight=0,
        dec_conv2=0,
        skip_weight=0,
        enc_conv1=0,
        enc_conv2=0,
    )
)
IN_HBM = tuple(dict(frames=0, cell_mask=0, cotangent=0)) + LARGE
IN_SMEM = tuple(dict(counts=0, step_index=0))
LATE = 128
SMALL_ROWS = dict(
    enc_conv2_bias=(0, 1),
    reducer_bias=(1, 1),
    up_bias=(2, 1),
    dec_conv2_bias=(3, 1),
    skip_bias=(3, 1),
    dec_norm1_gain=(4, 2),
    dec_norm1_bias=(6, 2),
    dec_norm2_gain=(8, 1),
    dec_norm2_bias=(9, 1),
    dec_step_table=(16, 8),
    lift_weight=(LATE, 12),
    lift_bias=(LATE + 12, 1),
    enc_norm1_gain=(LATE + 16, 1),
    enc_norm1_bias=(LATE + 17, 1),
    enc_norm2_gain=(LATE + 18, 1),
    enc_norm2_bias=(LATE + 19, 1),
    enc_step_table=(LATE + 24, 8),
)
LATE_COUNT = 32
SMALL_COUNT = LATE + LATE_COUNT
DUE = ((), (), (), (), (), (0,), (), (), (1,), (2,), (3,), (0,), (), (), (1,), (), (), (2,), (), (4, 3, 0, 1), (2,), (), (), (3,), (), (0,), (1,), (5, 2), (3,))
REST = (4, 5, 7, 4, 5, 6, 4, 0, 6, 1, 6, 0, 2, 1, 3, 7, 2, 3, 5, 4, 4, 6)
OUTPUTS = tuple(dict(output=0, frames_grad=0, gradients=0))


def split(value):
    high = value.astype(BF16)
    return high, (value - high.astype(F32)).astype(BF16)


def dot(left, right, dims=NN, precision=None):
    return lax.dot_general(
        left, right, (dims, ((), ())), precision=precision, preferred_element_type=F32
    )


def fold(value):
    half = value.shape[1] // 2
    return value[:, :half] + value[:, half:]


def fold_rows(value):
    half = value.shape[0] // 2
    return value[:half] + value[half:]


def tile_sums(value):
    return jnp.sum(value.reshape(-1, 8, value.shape[-1]), axis=0)


def column_sum(tiles):
    return jnp.sum(tiles, axis=0, keepdims=True)


def normal(value):
    bell = jnp.exp(-0.5 * value * value)
    t = 1.0 / (1.0 + 0.2316418882663604 * jnp.abs(value))
    poly = 0.5307027145
    for factor in (-0.7265760135, 0.7107068705, -0.142248368, 0.127414796):
        poly = poly * t + factor
    tail = poly * t * bell
    return jnp.where(value < 0.0, tail, 1.0 - tail), 0.3989422804014327 * bell


def dot_three(left, right, dims=NN):
    left_high, left_low = split(left)
    right_high, right_low = split(right)
    total = dot(left_high, right_high, dims)
    return total + (dot(left_high, right_low, dims) + dot(left_low, right_high, dims))


def group_ones(channels, size):
    rows = lax.broadcasted_iota(jnp.int32, (channels, channels), 0) // size
    columns = lax.broadcasted_iota(jnp.int32, (channels, channels), 1) // size
    return (rows == columns).astype(BF16)


def group_sums(first, second, ones):
    terms = []
    rest = jnp.concatenate([first, second], axis=0)
    for _ in range(3):
        term = rest.astype(BF16)
        terms.append(term)
        rest = rest - term.astype(F32)
    both = dot(jnp.concatenate(terms, axis=0), ones)
    both = both[32:48] + both[16:32] + both[:16]
    return column_sum(both[:8]), column_sum(both[8:])


class LineSwap:

    def __init__(self, line, source, target, inward, across, make):
        far = 3 - line.outer
        self.line = line
        to_inner, to_across = line.device(line.inner), line.device(line.across)
        to_outer = line.device(line.outer)
        here = target(line.here)
        self.to_far = make(source(3 - line.here), inward.at[1], to_inner)
        self.to_second = make(source(3 - line.inner), inward.at[0], to_inner)
        self.to_inner = make(source(line.inner), here, to_inner)
        self.for_far = make(source(far), across.at[0], to_across)
        self.to_across = make(source(line.across), here, to_across)
        self.to_outer = make(source(line.outer), here, to_outer)
        self.pass_far = make(inward.at[1], across.at[1], to_across)
        self.pass_second = make(inward.at[0], target(line.outer), to_across)
        self.pass_across = make(across.at[0], target(line.across), to_outer)
        self.pass_opposite = make(across.at[1], target(far), to_outer)

    def first(self):
        @pl.when(self.line.edge)
        def _():
            for copy in (self.to_far, self.to_second, self.to_inner):
                copy.start()

        @pl.when(self.line.middle)
        def _():
            for copy in (self.for_far, self.to_across, self.to_outer):
                copy.start()

    def second(self):
        @pl.when(self.line.middle)
        def _():
            self.for_far.wait_recv()
            self.pass_across.start()
            self.to_far.wait_recv()
            self.pass_far.start()
            self.to_second.wait_recv()
            self.pass_second.start()

    def third(self):
        @pl.when(self.line.middle)
        def _():
            self.pass_far.wait_recv()
            self.pass_opposite.start()

    def arrive(self):
        @pl.when(self.line.edge)
        def _():
            for copy in (self.to_outer, self.pass_across, self.pass_opposite):
                copy.wait_recv()

        @pl.when(self.line.middle)
        def _():
            for copy in (self.to_inner, self.to_across, self.pass_second):
                copy.wait_recv()

    def sent(self):
        @pl.when(self.line.edge)
        def _():
            for copy in (self.to_far, self.to_second, self.to_inner):
                copy.wait_send()

        @pl.when(self.line.middle)
        def _():
            for copy in (self.for_far, self.to_across, self.to_outer):
                copy.wait_send()
            for copy in (self.pass_far, self.pass_second, self.pass_across, self.pass_opposite):
                copy.wait_send()


class Exchange:

    def __init__(self, place, start, rows, landing, first_sem):
        self.place, self.start, self.rows, self.landing = place, start, rows, landing
        self.sem = first_sem
        self.stage = 0
        self.copies = []
        self.waiting = []
        self.group = place.plane_group
        self.half = rows // 2
        self.base = start + place.core * self.half
        self._finish(self.half)

    def _finish(self, size):
        self.part = size // self.group.count
        self.own = self.base + self.group.here * self.part
        self.shard = self.part // self.place.line.count
        self.last = self.own + self.place.line.here * self.shard

    def count(self):
        return 2 + 2 * (self.group.count - 1) + 2 * (self.place.line.count - 1)

    def land_rows(self):
        return self.rows - self.shard

    def _copy(self, source, target, device):
        place = self.place
        copy = pltpu.make_async_remote_copy(
            src_ref=source,
            dst_ref=target,
            send_sem=place.send.at[self.sem],
            recv_sem=place.recv.at[self.sem],
            device_id=device,
            device_id_type=MESH,
        )
        self.sem += 1
        copy.start()
        self.waiting.append(copy)
        self.copies.append(copy)

    def _wait(self):
        for copy in self.waiting:
            copy.wait_recv()
        self.waiting = []

    def _rows(self, at, size):
        return pl.ds(pl.multiple_of(at, 8), size)

    def _swap(self):
        place = self.place
        other = self._rows(self.start + (1 - place.core) * self.half, self.half)
        self.land = self.landing
        self.landing += self.half
        self._copy(
            place.sums.at[other], place.landing.at[pl.ds(self.land, self.half)], place.partner
        )

    def _add_swap(self):
        place = self.place
        block = 64 if self.half % 64 == 0 else 32

        def step(i, carry):
            here = self._rows(self.base + i * block, block)
            there = self._rows(self.land + i * block, block)
            place.sums[here] = place.sums[here] + place.landing[there]
            return carry

        lax.fori_loop(0, self.half // block, step, 0)

    def _scatter(self, group, base, size):
        place = self.place
        self.land = self.landing
        for k in range(1, group.count):
            to = lax.rem(group.here + k, group.count)
            self._copy(
                place.sums.at[self._rows(base + to * size, size)],
                place.landing.at[pl.ds(self.landing, size)],
                group.device(to),
            )
            self.landing += size

    def _total(self, group, own, size, target):
        place = self.place
        block = 16 if size % 16 == 0 else 8

        def step(i, carry):
            here = self._rows(own + i * block, block)
            total = place.sums[here]
            for k in range(group.count - 1):
                there = self._rows(self.land + k * size + i * block, block)
                total = total + place.landing[there]
            target[here] = total
            return carry

        lax.fori_loop(0, size // block, step, 0)

    def _gather(self, group, own, size):
        final = self.place.final
        here = self._rows(own, size)
        for k in range(1, group.count):
            to = lax.rem(group.here + k, group.count)
            self._copy(final.at[here], final.at[here], group.device(to))

    def _steps(self):
        place, group = self.place, self.group
        yield self._swap()
        self._wait()
        self._add_swap()
        yield from self._both()
        final = place.final
        here = self._rows(self.base, self.half)
        self._copy(final.at[here], final.at[here], place.partner)
        yield
        self._wait()
        yield

    def _both(self):
        place, group = self.place, self.group
        self._scatter(group, self.base, self.part)
        yield
        self._wait()
        self._total(group, self.own, self.part, place.sums)
        line = place.line
        self._scatter(line, self.own, self.shard)
        yield
        self._wait()
        self._total(line, self.last, self.shard, place.final)
        self._gather(line, self.last, self.shard)
        yield
        self._wait()
        self._gather(group, self.own, self.part)
        yield
        self._wait()

    def advance(self):
        if self.stage == 0:
            self.steps = self._steps()
        self.stage += 1
        next(self.steps)

    def done(self):
        return self.stage == 7


class PlaneExchange(Exchange):

    def __init__(self, place, start, rows, landing, first_sem):
        super().__init__(place, start, rows, landing, first_sem)
        self.group = place.cores_group
        self.base = start
        self._finish(rows)

    def count(self):
        return 2 * (self.group.count - 1) + 2 * (self.place.line.count - 1)

    def _steps(self):
        yield from self._both()
        yield

    def done(self):
        return self.stage == 5


class SmallExchange(Exchange):

    def count(self):
        return self.place.cores_group.count + self.place.line.count - 2

    def land_rows(self):
        return self.rows * (self.place.cores_group.count + self.place.line.count)

    def _share(self, group, source):
        place = self.place
        self.land = self.landing
        self.landing += group.count * self.rows
        own = self._rows(self.land + group.here * self.rows, self.rows)
        place.landing[own] = source[...]
        for k in range(1, group.count):
            to = lax.rem(group.here + k, group.count)
            self._copy(source, place.landing.at[own], group.device(to))

    def _sum(self, group):
        total = None
        for k in range(group.count):
            part = self.place.landing[pl.ds(self.land + k * self.rows, self.rows)]
            total = part if total is None else total + part
        return total

    def _steps(self):
        place = self.place
        here = pl.ds(self.start, self.rows)
        self._share(place.line, place.sums.at[here])
        yield
        self._wait()
        place.small[...] = self._sum(place.line)
        self._share(place.cores_group, place.small)
        yield
        self._wait()
        place.final[here] = self._sum(place.cores_group)
        yield

    def done(self):
        return self.stage == 3


KINDS = (Exchange,) * 5 + (PlaneExchange,) * 2 + (SmallExchange,)


def layout_of(shapes):
    starts = {}
    at = 0
    for name in LARGE:
        starts[name] = at
        at += getattr(shapes, name)[0]
    small = at
    begins = SimpleNamespace(**starts)
    late = small + LATE
    part = shapes.dec_conv1[0] // 3
    skip = begins.skip_weight + 128
    conv1, up = begins.dec_conv1, begins.up_weight
    edges = (
        (begins.dec_conv2, skip),
        (conv1, conv1 + part),
        (conv1 + part, conv1 + 2 * part),
        (conv1 + 2 * part, up),
        (up, begins.dec_conv2),
        (begins.enc_conv2, late),
        (skip, begins.enc_conv2),
        (late, late + LATE_COUNT),
    )
    runs = [(first, last - first) for first, last in edges]
    return starts, small, late + LATE_COUNT, runs


def item_kernel(sizes, scratch_names, *refs):
    line, strip, width, shapes, big_layout = sizes
    begins, small_at, total_rows, runs = big_layout
    starts = SimpleNamespace(**begins)
    inputs = Given(*refs[: len(ARGUMENTS)])
    refs = refs[len(ARGUMENTS) :]
    output_names = OUTPUTS
    outputs = SimpleNamespace(**dict(zip(output_names, refs)))
    scratch = SimpleNamespace(**dict(zip(scratch_names, refs[len(output_names) :])))

    def w_of(name):
        return getattr(scratch, name)

    height = strip * line
    cells = height * width
    c = inputs.lift_weight.shape[1]
    strip_cells = strip * width
    history = inputs.frames.shape[1]

    core = lax.axis_index("section")
    plane = lax.axis_index("batch")
    row = lax.axis_index("rows")
    middle = lax.rem(row + 1, 4) // 2

    def device_at(to):
        return (core, plane, to)

    place = SimpleNamespace(
        core=core,
        partner=(1 - core, plane, row),
        line=SimpleNamespace(
            count=line,
            here=row,
            device=device_at,
            middle=middle == 1,
            edge=middle == 0,
            inner=1 + row // 2,
            across=3 - row,
            outer=3 * (row // 2),
        ),
        plane_group=SimpleNamespace(
            count=4, here=plane, device=lambda to: (core, to, row)
        ),
        cores_group=SimpleNamespace(
            count=8,
            here=core * 4 + plane,
            device=lambda to: (to // 4, lax.rem(to, 4), row),
        ),
        small=scratch.small,
        sums=scratch.sums,
        final=scratch.final,
        landing=scratch.landing,
        send=scratch.send,
        recv=scratch.recv,
    )
    local_sem = scratch.local

    frames_in, mask_in, cot = scratch.frames_in, scratch.mask_in, scratch.cot
    here_rows = pl.ds(pl.multiple_of(row * strip_cells, strip_cells), strip_cells)
    frames_from, mask_from, cot_from = scratch.frames_from, scratch.mask_from, scratch.cot_from
    staged = (
        pltpu.make_async_copy(inputs.frames, frames_from, local_sem.at[7]),
        pltpu.make_async_copy(inputs.cell_mask, mask_from, local_sem.at[8]),
        pltpu.make_async_copy(inputs.cotangent, cot_from, local_sem.at[9]),
    )
    for copy in staged:
        copy.start()

    weight_copies = {}
    for k, name in enumerate(LARGE):
        copy = pltpu.make_async_copy(getattr(inputs, name), w_of(name), local_sem.at[k])
        weight_copies[name] = copy
        copy.start()

    barrier = pltpu.get_barrier_semaphore()
    peers = [device_at(lax.rem(row + k, line)) for k in range(1, line)]
    cores_group = place.cores_group
    for k in range(1, 8):
        peers.append(cores_group.device(lax.rem(cores_group.here + k, 8)))
    for device in peers:
        pl.semaphore_signal(barrier, inc=1, device_id=device, device_id_type=MESH)
    pl.semaphore_wait(barrier, len(peers))

    next_sem = 0

    def make(source, target, device):
        nonlocal next_sem
        copy = pltpu.make_async_remote_copy(
            src_ref=source,
            dst_ref=target,
            send_sem=scratch.send.at[next_sem],
            recv_sem=scratch.recv.at[next_sem],
            device_id=device,
            device_id_type=MESH,
        )
        next_sem += 1
        return copy

    def send(source, target, device):
        copy = make(source, target, device)
        copy.start()
        return copy

    def strip_of(ref, to):
        return ref.at[pl.ds(pl.multiple_of(to * strip_cells, strip_cells), strip_cells)]

    frame_copies, output_copies = [], []
    for copy in staged[:2]:
        copy.wait()
    for k in range(1, line):
        to = lax.rem(row + k, line)
        device = device_at(to)
        frame_copies.append(send(frames_from.at[to], frames_in.at[row], device))
        frame_copies.append(send(mask_from.at[to], mask_in.at[row], device))
    staged[2].wait()
    cot_swap = LineSwap(
        place.line,
        lambda to: cot_from.at[to],
        lambda source: strip_of(cot, source),
        scratch.cot_inward,
        scratch.cot_across,
        make,
    )
    cot_swap.first()

    copied = SimpleNamespace(**weight_copies)
    def put_pair(target, block, value):
        high, low = split(value)
        rows = slice(block * c, (block + 1) * c)
        target[rows, 0:c] = high
        target[rows, c : 2 * c] = low

    def stack_conv(source, half, depth, forward, backward):
        for a in range(3):
            for b in range(3):
                at = (3 * a + b) * depth + half * c
                value = source[at : at + c, :]
                turned = value.T
                for places in (HIGH_AT, LOW_AT):
                    put_pair(forward, 6 * a + places[b], value)
                    put_pair(backward, 6 * (2 - a) + places[2 - b], turned)

    copied.enc_conv1.wait()
    stack_conv(scratch.enc_conv1, 0, c, scratch.fe1, scratch.be1)
    copied.enc_conv2.wait()
    stack_conv(scratch.enc_conv2, 0, c, scratch.fe2, scratch.be2)
    copied.reducer_weight.wait()
    for k in range(4):
        value = scratch.reducer_weight[k * c : (k + 1) * c, :]
        turned = value.T
        for block in (k, k + 4):
            put_pair(scratch.f_down, block, value)
        for block in (0, 1):
            put_pair(scratch.b_down.at[k], block, turned)
    copied.up_weight.wait()
    for k in range(4):
        value = scratch.up_weight[k * c : (k + 1) * c, :]
        turned = value.T
        for block in (0, 1):
            put_pair(scratch.f_up.at[k], block, value)
        for block in (k, k + 4):
            put_pair(scratch.b_up, block, turned)
    copied.dec_conv1.wait()
    stack_conv(scratch.dec_conv1, 0, 2 * c, scratch.fd1a, scratch.bd1a)
    stack_conv(scratch.dec_conv1, 1, 2 * c, scratch.fd1b, scratch.bd1b)
    copied.dec_conv2.wait()
    stack_conv(scratch.dec_conv2, 0, c, scratch.fd2, scratch.bd2)
    copied.skip_weight.wait()
    for half in range(2):
        value = scratch.skip_weight[half * c : (half + 1) * c, :]
        turned = value.T
        for block in (half, half + 2):
            put_pair(scratch.f_skip, block, value)
        for block in (0, 1):
            put_pair(scratch.b_skip.at[half], block, turned)

    for buffer in (scratch.xe1, scratch.xe2, scratch.xd1a, scratch.xd1b, scratch.xd2, scratch.xg):
        edge = jnp.zeros((width, 6 * c), BF16)
        buffer[0:width, :] = edge
        buffer[cells + width : cells + 2 * width, :] = edge

    lift = scratch.lift
    lift[...] = jnp.zeros(lift.shape, F32)
    lift[0:history, :] = inputs.lift_weight[...]
    lift[history : history + 1, :] = inputs.lift_bias[...]

    block = 2 * width
    column = lax.rem(lax.broadcasted_iota(jnp.int32, (block, c), 0), width)
    at_first, at_last = column == 0, column == width - 1
    zeros8 = jnp.zeros((8, c), F32)
    ones16 = group_ones(c, c // GROUPS)
    ones32 = group_ones(c, 2 * c // GROUPS)
    count16 = float(cells * (c // GROUPS))
    count32 = float(cells * (2 * c // GROUPS))

    def grid_rows(step, carry=0):
        return lax.fori_loop(0, cells // block, step, carry, unroll=2)

    def row_at(h):
        return pl.ds(pl.multiple_of(h * block, block), block)

    def chunk_at(i):
        return pl.ds(pl.multiple_of(i * CHUNK, CHUNK), CHUNK)

    def put_row(target, h, value):
        rows = pl.ds(pl.multiple_of(h * block + width, width), block)
        left = jnp.where(at_first, 0.0, pltpu.roll(value, 1, 0))
        right = jnp.where(at_last, 0.0, pltpu.roll(value, block - 1, 0))
        for b, piece in enumerate((left, value, right)):
            high, low = split(piece)
            target[rows, HIGH_AT[b] * c : (HIGH_AT[b] + 1) * c] = high
            target[rows, LOW_AT[b] * c : (LOW_AT[b] + 1) * c] = low

    def put_turned(target, columns, value, first=0, second=1):
        high, low = split(value.T)
        target[first * c : (first + 1) * c, columns] = high
        target[second * c : (second + 1) * c, columns] = low

    def conv_chunk(pairs, i):
        total = None
        for data, weight in pairs:
            taps = []
            for a in range(3):
                rows = pl.ds(pl.multiple_of(i * CHUNK + a * width, width), CHUNK)
                taps.append(data[rows, :])
            part = dot(jnp.concatenate(taps, axis=1), weight[...])
            total = part if total is None else total + part
        return total

    def norm_of(first, second, ones, count):
        one, two = group_sums(first, second, ones)
        mean = one / count
        return mean, lax.rsqrt(two / count - mean * mean + EPS)

    def activate(source, target, turned, slope, scale, shift):
        def step(h, carry):
            value = source[row_at(h), :] * scale + shift
            below, density = normal(value)
            slope[row_at(h), :] = below + value * density
            value = value * below
            put_row(target, h, value)
            put_turned(turned, row_at(h), value)
            return carry

        grid_rows(step)

    def conv_norm(pairs, target):
        def step(i, carry):
            value = fold(conv_chunk(pairs, i))
            target[chunk_at(i), :] = value
            return carry[0] + tile_sums(value), carry[1] + tile_sums(value * value)

        return lax.fori_loop(0, cells // CHUNK, step, (zeros8, zeros8))

    def sums_of(source):
        def step(h, carry):
            value = source[row_at(h), :]
            return carry[0] + tile_sums(value), carry[1] + tile_sums(value * value)

        return grid_rows(step, (zeros8, zeros8))

    step_here = jnp.full((1, c), inputs.step_index[row], jnp.int32)

    def condition(table):
        total = jnp.zeros((1, 2 * c), F32)
        chosen = jnp.concatenate([step_here, step_here], axis=1)
        for s in range(table.shape[0]):
            total = total + jnp.where(chosen == s, table[s : s + 1, :], 0.0)
        return total[:, :c], total[:, c:]

    frames_in[row] = frames_from[row]
    mask_in[row] = mask_from[row]
    for copy in frame_copies:
        copy.wait_recv()
    fields = scratch.fields
    fields[...] = jnp.zeros(fields.shape, F32)
    frame_of = lax.broadcasted_iota(jnp.int32, (history, width), 0) // FIELDS
    keep = (frame_of >= HIST - inputs.counts[row]).astype(F32)
    masks = []
    for source in range(line):
        for k in range(strip):
            columns = slice((source * strip + k) * width, (source * strip + k + 1) * width)
            mask = mask_in[source, k : k + 1, :].astype(F32)
            masks.append(mask)
            fields[0:history, columns] = frames_in[source, :, k, :] * keep * mask
            fields[history : history + 1, columns] = mask
    lifted = scratch.lifted
    lifted[...] = dot_three(fields[...], lift[...], TN)

    enc_scale, enc_shift = condition(inputs.enc_step_table)
    dec_scale, dec_shift = condition(inputs.dec_step_table)

    mean_e1, inv_e1 = norm_of(*sums_of(lifted), ones16, count16)
    gain_e1, bias_e1 = inputs.enc_norm1_gain[...], inputs.enc_norm1_bias[...]
    a_e1 = inv_e1 * gain_e1
    activate(lifted, scratch.xe1, scratch.te1, scratch.slope_e1, a_e1, bias_e1 - mean_e1 * a_e1)
    middle_e = scratch.middle_e
    mean_e2, inv_e2 = norm_of(
        *conv_norm([(scratch.xe1, scratch.fe1)], middle_e), ones16, count16
    )
    gain_e2, bias_e2 = inputs.enc_norm2_gain[...], inputs.enc_norm2_bias[...]
    a_e2 = inv_e2 * gain_e2
    activate(
        middle_e,
        scratch.xe2,
        scratch.te2,
        scratch.slope_e2,
        a_e2 * (1.0 + enc_scale),
        (bias_e2 - mean_e2 * a_e2) * (1.0 + enc_scale) + enc_shift,
    )
    cot_swap.second()
    encoded = scratch.encoded
    conv2_bias = inputs.enc_conv2_bias[...]
    joined = scratch.joined

    def encode(i, carry):
        value = fold(conv_chunk([(scratch.xe2, scratch.fe2)], i))
        value = value + conv2_bias + lifted[chunk_at(i), :]
        encoded[chunk_at(i), :] = value
        high, low = split(value)
        joined[chunk_at(i), c : 2 * c] = high
        joined[chunk_at(i), 3 * c : 4 * c] = low
        put_turned(scratch.turned, chunk_at(i), value, 1, 3)
        return carry[0] + tile_sums(value), carry[1] + tile_sums(value * value)

    sums_enc = lax.fori_loop(0, cells // CHUNK, encode, (zeros8, zeros8))

    half_cells, quarter = cells // 2, cells // 4

    def pick(source):
        pieces = []
        for b in range(2):
            value = source[pl.ds(b, half_cells, stride=2), :]
            value = value.reshape(height // 2, 2, width // 2, c)
            pieces.append([value[:, a].reshape(quarter, c) for a in range(2)])
        return [pieces[b][a] for a in range(2) for b in range(2)]

    def place_cells(target, pieces):
        for b in range(2):
            both = [pieces[2 * a + b].reshape(height // 2, 1, width // 2, c) for a in range(2)]
            value = jnp.concatenate(both, axis=1).reshape(half_cells, c)
            target[pl.ds(b, half_cells, stride=2), :] = value

    x_down = scratch.x_down
    for k, piece in enumerate(pick(encoded)):
        high, low = split(piece)
        x_down[:, k * c : (k + 1) * c] = high
        x_down[:, (k + 4) * c : (k + 5) * c] = low
    lowered = fold(dot(x_down[...], scratch.f_down[...])) + inputs.reducer_bias[...]
    x_up = scratch.x_up
    high, low = split(lowered)
    x_up[:, 0:c] = high
    x_up[:, c : 2 * c] = low
    raised = scratch.raised
    up_bias = inputs.up_bias[...]
    place_cells(
        raised, [fold(dot(x_up[...], scratch.f_up[k])) + up_bias for k in range(4)]
    )

    def raise_row(h, carry):
        value = raised[row_at(h), :]
        high, low = split(value)
        joined[row_at(h), 0:c] = high
        joined[row_at(h), 2 * c : 3 * c] = low
        put_turned(scratch.turned, row_at(h), value, 0, 2)
        return carry[0] + tile_sums(value), carry[1] + tile_sums(value * value)

    sums_raised = grid_rows(raise_row, (zeros8, zeros8))

    halves = []
    for half, (source, sums) in enumerate(((raised, sums_raised), (encoded, sums_enc))):
        mean, inv = norm_of(*sums, ones32, count32)
        gain = inputs.dec_norm1_gain[half : half + 1, :]
        bias = inputs.dec_norm1_bias[half : half + 1, :]
        scale = inv * gain
        activate(
            source,
            (scratch.xd1a, scratch.xd1b)[half],
            scratch.td1.at[2 * c * half : 2 * c * (half + 1)],
            (scratch.slope_d1a, scratch.slope_d1b)[half],
            scale,
            bias - mean * scale,
        )
        halves.append((source, mean, inv, gain))
    middle_d = scratch.middle_d
    pairs = [(scratch.xd1a, scratch.fd1a), (scratch.xd1b, scratch.fd1b)]
    mean_d2, inv_d2 = norm_of(*conv_norm(pairs, middle_d), ones16, count16)
    cot_swap.third()
    gain_d2, bias_d2 = inputs.dec_norm2_gain[...], inputs.dec_norm2_bias[...]
    a_d2 = inv_d2 * gain_d2
    activate(
        middle_d,
        scratch.xd2,
        scratch.td2,
        scratch.slope_d2,
        a_d2 * (1.0 + dec_scale),
        (bias_d2 - mean_d2 * a_d2) * (1.0 + dec_scale) + dec_shift,
    )
    result = scratch.result
    last_bias = inputs.dec_conv2_bias[...] + inputs.skip_bias[...]

    def decode(i, carry):
        value = conv_chunk([(scratch.xd2, scratch.fd2)], i)
        value = value + dot(joined[chunk_at(i), :], scratch.f_skip[...])
        result[chunk_at(i), :] = fold(value) + last_bias
        return carry

    lax.fori_loop(0, cells // CHUNK, decode, 0)
    output_here, frames_here = scratch.output_here, scratch.frames_here
    output_here[row] = result[here_rows]
    output_swap = LineSwap(
        place.line,
        lambda to: strip_of(result, to),
        lambda source: output_here.at[source],
        scratch.output_inward,
        scratch.output_across,
        make,
    )
    output_swap.first()

    exchanges = []
    waiting_runs = list(runs)
    landing_at = 0
    sem_at = 3 * (line - 1) + 20
    sums, final = scratch.sums, scratch.final

    def begin():
        nonlocal landing_at, sem_at
        start, rows = waiting_runs.pop(0)
        kind = KINDS[len(exchanges)]
        exchange = kind(place, start, rows, landing_at, sem_at)
        landing_at += exchange.land_rows()
        sem_at += exchange.count()
        exchanges.append(exchange)
        exchange.advance()

    final_copies = []

    def advance(k):
        exchange = exchanges[k]
        exchange.advance()
        if exchange.done():
            rows = pl.ds(exchange.start, exchange.rows)
            copy = pltpu.make_async_copy(
                final.at[rows], outputs.gradients.at[rows], local_sem.at[11 + k]
            )
            copy.start()
            final_copies.append(copy)

    due = list(DUE)

    def point():
        for k in due.pop(0):
            advance(k)

    def small_row(k, value):
        sums[small_at + k : small_at + k + 1, :] = value

    def spread_grad(source):
        def step(h, carry):
            value = source[row_at(h), :]
            put_row(scratch.xg, h, value)
            return carry + tile_sums(value)

        return grid_rows(step, zeros8)

    def weight_grad(turned, at, depth, a):
        rows = pl.ds((2 - a) * width, cells)
        both = dot(turned[...], scratch.xg[rows, :])
        for half in range(depth // c):
            part = fold_rows(both[2 * c * half : 2 * c * (half + 1)])
            for b in range(3):
                high, low = HIGH_AT[2 - b] * c, LOW_AT[2 - b] * c
                to = at + (3 * a + b) * depth + half * c
                sums[to : to + c, :] = part[:, high : high + c] + part[:, low : low + c]

    def back_conv(weight, slope, target, source, mean, inv):
        carry = (zeros8, zeros8)
        for i in range(cells // CHUNK):
            value = fold(conv_chunk([(scratch.xg, weight)], i)) * slope[chunk_at(i), :]
            target[chunk_at(i), :] = value
            normed = (source[chunk_at(i), :] - mean) * inv
            carry = (carry[0] + tile_sums(value), carry[1] + tile_sums(value * normed))
            if i % (cells // CHUNK // 2) == cells // CHUNK // 2 - 1:
                point()
        return carry

    def norm_grad(sums_in, scale, ones, count):
        one, two = group_sums(sums_in[0] * scale, sums_in[1] * scale, ones)
        return one / count, two / count

    cot[here_rows] = cot_from[row]
    cot_swap.arrive()
    total_cot = column_sum(spread_grad(cot))
    for a in range(3):
        weight_grad(scratch.td2, starts.dec_conv2, c, a)
    part = fold(dot(scratch.turned[...], scratch.xg[width : cells + width, 2 * c : 4 * c]))
    sums[starts.skip_weight : starts.skip_weight + 2 * c, :] = fold_rows(part)
    small_row(3, total_cot)
    begin()

    grad = scratch.grad
    sums_d2 = back_conv(scratch.bd2, scratch.slope_d2, grad, middle_d, mean_d2, inv_d2)
    side_grads = (scratch.grad_a, scratch.grad_b)
    for half in range(2):

        def skip_back(i, carry, half=half):
            rows = pl.ds(pl.multiple_of(i * CHUNK + width, width), CHUNK)
            value = dot(scratch.xg[rows, 2 * c : 4 * c], scratch.b_skip[half])
            side_grads[half][chunk_at(i), :] = fold(value)
            return carry

        lax.fori_loop(0, cells // CHUNK, skip_back, 0)
    point()

    def table_rows(k, sums_in, gain, bias, one_plus):
        plain, times = column_sum(sums_in[0]), column_sum(sums_in[1])
        for s in range(inputs.enc_step_table.shape[0]):
            small_row(k + 2 * s, jnp.where(step_here == s, gain * times + bias * plain, 0.0))
            small_row(k + 2 * s + 1, jnp.where(step_here == s, plain, 0.0))
        return one_plus * times, one_plus * plain

    def middle_grad(source, mean, inv, scale, sums_in):
        zero, slope = norm_grad(sums_in, scale, ones16, count16)

        def step(h, carry):
            normed = (source[row_at(h), :] - mean) * inv
            value = inv * (grad[row_at(h), :] * scale - zero - normed * slope)
            put_row(scratch.xg, h, value)
            return carry

        grid_rows(step)

    gain_row, bias_row = table_rows(16, sums_d2, gain_d2, bias_d2, 1.0 + dec_scale)
    small_row(8, gain_row)
    small_row(9, bias_row)
    middle_grad(middle_d, mean_d2, inv_d2, gain_d2 * (1.0 + dec_scale), sums_d2)
    point()
    output_swap.second()
    for a in range(3):
        weight_grad(scratch.td1, starts.dec_conv1, 2 * c, a)
        point()
        begin()

    for half, (source, mean, inv, gain) in enumerate(halves):
        sums_in = back_conv(
            (scratch.bd1a, scratch.bd1b)[half],
            (scratch.slope_d1a, scratch.slope_d1b)[half],
            grad,
            source,
            mean,
            inv,
        )
        small_row(4 + half, column_sum(sums_in[1]))
        small_row(6 + half, column_sum(sums_in[0]))
        zero, slope = norm_grad(sums_in, gain, ones32, count32)
        target = side_grads[half]

        def input_grad(h, carry):
            normed = (source[row_at(h), :] - mean) * inv
            value = inv * (grad[row_at(h), :] * gain - zero - normed * slope)
            value = target[row_at(h), :] + value
            target[row_at(h), :] = value
            return carry + tile_sums(value)

        total = grid_rows(input_grad, zeros8)
        if half == 0:
            small_row(2, column_sum(total))
        point()

    output_swap.third()
    grad_raised, grad_encoded = side_grads
    x_grad_up = scratch.x_grad_up
    for k, piece in enumerate(pick(grad_raised)):
        high, low = split(piece)
        x_grad_up[:, k * c : (k + 1) * c] = high
        x_grad_up[:, (k + 4) * c : (k + 5) * c] = low
    grad_lowered = fold(dot(x_grad_up[...], scratch.b_up[...]))
    small_row(1, jnp.sum(grad_lowered, axis=0, keepdims=True))
    x_grad_low = scratch.x_grad_low
    high, low = split(grad_lowered)
    x_grad_low[:, 0:c] = high
    x_grad_low[:, c : 2 * c] = low
    point()
    part = fold(fold_rows(dot(x_up[...], x_grad_up[...], TN)))
    for k in range(4):
        at = starts.up_weight + k * c
        sums[at : at + c, :] = part[:, k * c : (k + 1) * c]
    part = fold_rows(fold(dot(x_down[...], x_grad_low[...], TN)))
    sums[starts.reducer_weight : starts.reducer_weight + 4 * c, :] = part
    point()
    begin()
    place_cells(
        grad, [fold(dot(x_grad_low[...], scratch.b_down[k])) for k in range(4)]
    )

    def join_row(h, carry):
        value = grad_encoded[row_at(h), :] + grad[row_at(h), :]
        grad_encoded[row_at(h), :] = value
        put_row(scratch.xg, h, value)
        return carry + tile_sums(value)

    small_row(0, column_sum(grid_rows(join_row, zeros8)))
    for k in range(10, 16):
        small_row(k, jnp.zeros((1, c), F32))
    sums[small_at + 24 : small_at + LATE, :] = jnp.zeros((LATE - 24, c), F32)
    point()
    for a in range(3):
        weight_grad(scratch.te2, starts.enc_conv2, c, a)
        point()
    begin()
    sums_e2 = back_conv(scratch.be2, scratch.slope_e2, grad, middle_e, mean_e2, inv_e2)
    gain_row, bias_row = table_rows(LATE + 24, sums_e2, gain_e2, bias_e2, 1.0 + enc_scale)
    small_row(LATE + 18, gain_row)
    small_row(LATE + 19, bias_row)
    middle_grad(middle_e, mean_e2, inv_e2, gain_e2 * (1.0 + enc_scale), sums_e2)
    point()
    for a in range(3):
        weight_grad(scratch.te1, starts.enc_conv1, c, a)
        point()
    begin()
    sums_e1 = back_conv(scratch.be1, scratch.slope_e1, grad, lifted, mean_e1, inv_e1)
    small_row(LATE + 16, column_sum(sums_e1[1]))
    small_row(LATE + 17, column_sum(sums_e1[0]))
    zero, slope = norm_grad(sums_e1, gain_e1, ones16, count16)

    def lifted_grad(h, carry):
        normed = (lifted[row_at(h), :] - mean_e1) * inv_e1
        value = inv_e1 * (grad[row_at(h), :] * gain_e1 - zero - normed * slope)
        grad[row_at(h), :] = grad_encoded[row_at(h), :] + value
        return carry

    grid_rows(lifted_grad)
    point()

    late_at = small_at + LATE
    sums[late_at : late_at + 16, :] = dot_three(fields[...], grad[...])
    sums[late_at + 20 : late_at + 24, :] = jnp.zeros((4, c), F32)
    point()
    begin()
    back = dot_three(lift[...], grad[...], NT)
    frames_out = scratch.frames_out
    for source in range(line):
        for k in range(strip):
            h = source * strip + k
            value = back[0:history, h * width : (h + 1) * width]
            frames_out[source, :, k, :] = value * keep * masks[h]
    frames_here[row] = frames_out[row]
    for k in range(1, line):
        to = lax.rem(row + k, line)
        output_copies.append(
            send(frames_out.at[to], frames_here.at[row], device_at(to))
        )

    output_swap.arrive()
    own_output = pltpu.make_async_copy(output_here, outputs.output, local_sem.at[10])
    own_output.start()
    for k in REST:
        advance(k)
    assert not due and all(exchange.done() for exchange in exchanges)

    for copy in output_copies:
        copy.wait_recv()
    own_frames = pltpu.make_async_copy(
        frames_here, outputs.frames_grad, local_sem.at[11 + len(runs)]
    )
    own_frames.start()
    own_output.wait()
    own_frames.wait()
    for copy in final_copies:
        copy.wait()
    for copy in frame_copies + output_copies:
        copy.wait_send()
    cot_swap.sent()
    output_swap.sent()
    for exchange in exchanges:
        for copy in exchange.copies:
            copy.wait_send()


def write_kernel(layout, *refs):
    shapes, starts, small_at = layout
    output, frames_grad, gradients = refs[:3]
    outputs = refs[3:-4]
    output_here, frames_here, gradients_here, sem = refs[-4:]
    c = gradients.shape[1]
    moves = [(frames_grad, frames_here, outputs[1])]
    for k, name in enumerate(LARGE):
        rows = pl.ds(starts[name], shapes[name][0])
        moves.append((gradients.at[rows], gradients_here.at[rows], outputs[2 + k]))
    moves.append((output, output_here, outputs[0]))
    small = pl.ds(small_at, SMALL_COUNT)
    first = pltpu.make_async_copy(gradients.at[small], gradients_here.at[small], sem.at[0])
    first.start()
    arriving, leaving = [], []
    for k, (source, here, _) in enumerate(moves):
        arriving.append(pltpu.make_async_copy(source, here, sem.at[1 + 2 * k]))
        arriving[-1].start()
    first.wait()
    for target, (k, rows) in zip(outputs[2 + len(LARGE) :], SMALL_ROWS.values()):
        at = small_at + k
        if rows == 8:
            for s in range(target.shape[0]):
                target[s : s + 1, 0:c] = gradients_here[at + 2 * s : at + 2 * s + 1, :]
                target[s : s + 1, c : 2 * c] = gradients_here[at + 2 * s + 1 : at + 2 * s + 2, :]
        else:
            target[...] = gradients_here[at : at + rows, :]
    for k, (_, here, target) in enumerate(moves):
        arriving[k].wait()
        leaving.append(pltpu.make_async_copy(here, target, sem.at[2 + 2 * k]))
        leaving[-1].start()
    for copy in leaving:
        copy.wait()


def whole_items(shape, *arguments):
    line = shape["rows"]
    whole = Given(*arguments)
    given = whole._asdict()
    frames, cotangent = whole.frames, whole.cotangent
    items, history, strip, width = frames.shape
    c = cotangent.shape[-1]
    cells = strip * line * width
    flat = {}
    for name, value in given.items():
        if value is cotangent:
            value = value.reshape(items, strip * width, c)
        elif name in LARGE:
            value = value.reshape(-1, c)
        elif value.ndim == 1 and name not in IN_SMEM:
            value = value.reshape(-1, c)
        flat[name] = value
    shapes = {name: flat[name].shape for name in LARGE}
    big_layout = layout_of(SimpleNamespace(**shapes))
    starts, small_at, total_rows, runs = big_layout
    copies = 20 + 3 * (line - 1) + len(runs) * (14 + 2 * (line - 1)) + 6
    landing = sum(rows for _, rows in runs) + LATE_COUNT * (8 + line)
    shifted = pltpu.VMEM((cells + 2 * width, 6 * c), BF16)
    forward = pltpu.VMEM((18 * c, 2 * c), BF16)
    backward = forward
    field = pltpu.VMEM((cells, c), F32)
    flipped_field = pltpu.VMEM((2 * c, cells), BF16)
    quarter = cells // 4
    scratch = dict(
        small=pltpu.VMEM((LATE_COUNT, c), F32),
        send=pltpu.SemaphoreType.DMA((copies,)),
        recv=pltpu.SemaphoreType.DMA((copies,)),
        local=pltpu.SemaphoreType.DMA((12 + len(runs),)),
        sums=pltpu.VMEM((total_rows, c), F32),
        final=pltpu.VMEM((total_rows, c), F32),
        landing=pltpu.VMEM((landing, c), F32),
        frames_in=pltpu.VMEM((line, history, strip, width), F32),
        mask_in=pltpu.VMEM((line, strip, width), jnp.int32),
        frames_out=pltpu.VMEM((line, history, strip, width), F32),
        frames_from=pltpu.VMEM((line, history, strip, width), F32),
        frames_here=pltpu.VMEM((line, history, strip, width), F32),
        mask_from=pltpu.VMEM((line, strip, width), jnp.int32),
        cot_from=pltpu.VMEM((items, strip * width, c), F32),
        output_here=pltpu.VMEM((items, strip * width, c), F32),
        cot_inward=pltpu.VMEM((2, strip * width, c), F32),
        cot_across=pltpu.VMEM((2, strip * width, c), F32),
        output_inward=pltpu.VMEM((2, strip * width, c), F32),
        output_across=pltpu.VMEM((2, strip * width, c), F32),
        fields=pltpu.VMEM((16, cells), F32),
        lift=pltpu.VMEM((16, c), F32),
        joined=pltpu.VMEM((cells, 4 * c), BF16),
        x_down=pltpu.VMEM((quarter, 8 * c), BF16),
        x_grad_up=pltpu.VMEM((quarter, 8 * c), BF16),
        x_up=pltpu.VMEM((quarter, 2 * c), BF16),
        x_grad_low=pltpu.VMEM((quarter, 2 * c), BF16),
        f_down=pltpu.VMEM((8 * c, 2 * c), BF16),
        b_down=pltpu.VMEM((4, 2 * c, 2 * c), BF16),
        f_up=pltpu.VMEM((4, 2 * c, 2 * c), BF16),
        b_up=pltpu.VMEM((8 * c, 2 * c), BF16),
        f_skip=pltpu.VMEM((4 * c, 2 * c), BF16),
        b_skip=pltpu.VMEM((2, 2 * c, 2 * c), BF16),
        xe1=shifted,
        xe2=shifted,
        xd1a=shifted,
        xd1b=shifted,
        xd2=shifted,
        xg=shifted,
        te1=flipped_field,
        te2=flipped_field,
        td1=pltpu.VMEM((4 * c, cells), BF16),
        td2=flipped_field,
        turned=pltpu.VMEM((4 * c, cells), BF16),
        fe1=forward,
        fe2=forward,
        fd1a=forward,
        fd1b=forward,
        fd2=forward,
        be1=backward,
        be2=backward,
        bd1a=backward,
        bd1b=backward,
        bd2=backward,
        slope_e1=field,
        slope_e2=field,
        slope_d1a=field,
        slope_d1b=field,
        slope_d2=field,
        lifted=field,
        middle_e=field,
        encoded=field,
        raised=field,
        middle_d=field,
        result=field,
        cot=field,
        grad=field,
        grad_a=field,
        grad_b=field,
    )
    scratch.update({name: pltpu.VMEM(shapes[name], F32) for name in LARGE})

    in_hbm = pl.BlockSpec(memory_space=pl.ANY)
    in_vmem = pl.BlockSpec(memory_space=pltpu.VMEM)
    in_smem = pl.BlockSpec(memory_space=pltpu.SMEM)
    in_specs = [
        in_hbm if name in IN_HBM else in_smem if name in IN_SMEM else in_vmem
        for name in ARGUMENTS
    ]
    out_shape = [
        jax.ShapeDtypeStruct((items, strip * width, c), F32),
        jax.ShapeDtypeStruct(frames.shape, F32),
        jax.ShapeDtypeStruct((total_rows, c), F32),
    ]
    out_specs = [in_hbm] * 3
    results = pl.pallas_call(
        functools.partial(
            item_kernel,
            (line, strip, width, shapes, big_layout),
            tuple(scratch),
        ),
        out_shape=out_shape,
        in_specs=in_specs,
        out_specs=out_specs,
        scratch_shapes=list(scratch.values()),
        compiler_params=pltpu.CompilerParams(
            collective_id=0, has_side_effects=True, vmem_limit_bytes=62 * 1024 * 1024
        ),
    )(*[flat[name] for name in ARGUMENTS])
    names = LARGE + tuple(SMALL_ROWS)
    written = pl.pallas_call(
        functools.partial(write_kernel, (shapes, starts, small_at)),
        out_shape=out_shape[:2] + [jax.ShapeDtypeStruct(flat[name].shape, F32) for name in names],
        in_specs=[pl.BlockSpec(memory_space=pltpu.HBM)] * 3,
        out_specs=[in_hbm] * (2 + len(LARGE)) + [in_vmem] * len(SMALL_ROWS),
        scratch_shapes=[
            pltpu.VMEM((items, strip * width, c), F32),
            pltpu.VMEM(frames.shape, F32),
            pltpu.VMEM((total_rows, c), F32),
            pltpu.SemaphoreType.DMA((1 + 2 * (2 + len(LARGE)),)),
        ],
        compiler_params=pltpu.CompilerParams(vmem_limit_bytes=60 * 1024 * 1024),
    )(*results)
    grads = dict(zip(names, written[2:]))
    ordered = [name for name in ARGUMENTS if name in grads]
    return (written[0].reshape(cotangent.shape), written[1]) + tuple(
        grads[name].reshape(given[name].shape) for name in ordered
    )


def body(shape, *arguments):
    items, _, strip, width = arguments[0].shape
    line = shape["rows"]
    whole = (
        shape["section"] == 2
        and shape["batch"] == 4
        and items == line == 4
        and arguments[-1].shape[-1] == 128
        and (strip * line * width) % CHUNK == 0
    )
    return whole_items(shape, *arguments) if whole else strips_body(*arguments)


def solution(mesh):
    in_specs = (
        P(("section", "batch"), None, "rows", None),
        P(("section", "batch")),
        P(("section", "batch"), "rows", None),
        P(("section", "batch")),
        P(),
        P(),
        P(),
        P(),
        P(),
        P(),
        P(),
        P(),
        P(),
        P(),
        P(),
        P(),
        P(),
        P(),
        P(),
        P(),
        P(),
        P(),
        P(),
        P(),
        P(),
        P(),
        P(),
        P(),
        P(("section", "batch"), "rows", None, None),
    )
    out_specs = (
        P(("section", "batch"), "rows", None, None),
        P(("section", "batch"), None, "rows", None),
        P(),
        P(),
        P(),
        P(),
        P(),
        P(),
        P(),
        P(),
        P(),
        P(),
        P(),
        P(),
        P(),
        P(),
        P(),
        P(),
        P(),
        P(),
        P(),
        P(),
        P(),
        P(),
        P(),
        P(),
    )
    return jax.shard_map(functools.partial(body, mesh.shape), mesh=mesh, in_specs=in_specs, out_specs=out_specs, check_vma=False)
```

```python
import functools
from types import SimpleNamespace
from typing import Any, NamedTuple

import jax
import jax.numpy as jnp
from jax import lax
from jax.experimental import pallas as pl
from jax.experimental.pallas import tpu as pltpu
from jax.sharding import PartitionSpec as P

GROUPS = 8
FIELDS = 3
HIST = 4


EPS = 1e-05
HIGH = lax.Precision.HIGHEST


def extended(cells, sides, width):
    for axis, dim in sides:
        count = lax.axis_size(axis)
        ends = count - 1
        head = lax.slice_in_dim(cells, 0, width, axis=dim)
        tail = lax.slice_in_dim(cells, cells.shape[dim] - width, cells.shape[dim], axis=dim)
        cells = jnp.concatenate(
            [
                lax.ppermute(tail, axis, [(i, (i + 1) % count) for i in range(ends)]),
                cells,
                lax.ppermute(head, axis, [((i + 1) % count, i) for i in range(ends)]),
            ],
            axis=dim,
        )
    return cells


def from_behind(value, axis, steps):
    count = lax.axis_size(axis)
    pairs = [(source, (source + steps) % count) for source in range(count)]
    return lax.ppermute(value, axis, pairs)


def group_view(value_arrays):
    extent = value_arrays.shape
    return value_arrays.reshape(extent[:-1] + (GROUPS, extent[-1] // GROUPS))


def global_sums(value_arrays):
    grouped = group_view(value_arrays)
    flat = grouped.reshape(-1, GROUPS, grouped.shape[-1])
    first_sum = jnp.sum(flat, axis=(0, 2))
    second_sum = jnp.sum(flat * flat, axis=(0, 2))
    return lax.psum((first_sum, second_sum), "rows")


def apply_norm(value_arrays, sum_one, sum_two, norm_gain, norm_bias, total):
    grouped = group_view(value_arrays)
    group_mean = sum_one / total
    variance = sum_two / total - group_mean * group_mean
    inverse = lax.rsqrt(variance + EPS)
    normed = (grouped - group_mean[:, None]) * inverse[:, None]
    return normed.reshape(value_arrays.shape) * norm_gain + norm_bias


def norm_back(value_arrays, grad_one, grad_two):
    grouped = group_view(value_arrays)
    extra = grad_one[:, None] + 2.0 * grouped * grad_two[:, None]
    return extra.reshape(value_arrays.shape)


def reduce_grads(grad_one, grad_two):
    return lax.psum((grad_one, grad_two), "rows")


def conv_rows(padded, kernel):
    widened = jnp.pad(padded, ((0, 0), (1, 1), (0, 0)))
    return lax.conv_general_dilated(
        widened[None],
        kernel,
        (1, 1),
        "VALID",
        dimension_numbers=("NHWC", "HWIO", "NHWC"),
        precision=HIGH,
    )[0]


def flipped(kernel):
    return jnp.transpose(kernel[::-1, ::-1], (0, 1, 3, 2))


def pad_grads(value_arrays):
    return extended(value_arrays, (("rows", 0),), 1)


def totals_of(inputs, conv1):
    strip = inputs.shape[0]
    cells = strip * lax.axis_size("rows") * inputs.shape[1]
    return (cells * (inputs.shape[2] // GROUPS), cells * (conv1.shape[3] // GROUPS))


def block_forward(inputs, weights, scale_part, shift_part):
    norm1_gain, norm1_bias, conv1, norm2_gain, norm2_bias, conv2, conv2_bias = weights
    total_in, total_mid = totals_of(inputs, conv1)
    sums_in = global_sums(inputs)

    def pad_rows(value_arrays):
        return extended(value_arrays, (("rows", 0),), 1)

    act_one = pad_rows(
        jax.nn.gelu(
            apply_norm(inputs, sums_in[0], sums_in[1], norm1_gain, norm1_bias, total_in),
            approximate=False,
        )
    )
    middle = conv_rows(act_one, conv1)
    sums_mid = global_sums(middle)
    shaped = (
        apply_norm(middle, sums_mid[0], sums_mid[1], norm2_gain, norm2_bias, total_mid)
        * (1.0 + scale_part)
        + shift_part
    )
    act_two = pad_rows(jax.nn.gelu(shaped, approximate=False))
    branch = conv_rows(act_two, conv2) + conv2_bias
    return (branch, (sums_in[0], sums_in[1], act_one, middle, sums_mid[0], sums_mid[1], act_two))


def block_backward(inputs, weights, scale_part, shift_part, kept, grad_out):
    norm1_gain, norm1_bias, conv1, norm2_gain, norm2_bias, conv2, conv2_bias = weights
    in_one, in_two, act_one, middle, mid_one, mid_two, act_two = kept
    total_in, total_mid = totals_of(inputs, conv1)
    grad_conv2 = jax.vjp(lambda kernel: conv_rows(act_two, kernel), conv2)[1](grad_out)[0]
    grad_bias2 = jnp.sum(grad_out, axis=(0, 1))
    grad_act_two = conv_rows(pad_grads(grad_out), flipped(conv2))

    def second_piece(middle_in, sum_one, sum_two, gain_in, incoming_bias, scale_in, shift_in):
        shaped = (
            apply_norm(middle_in, sum_one, sum_two, gain_in, incoming_bias, total_mid)
            * (1.0 + scale_in)
            + shift_in
        )
        return jax.nn.gelu(shaped, approximate=False)

    second_pull = jax.vjp(
        second_piece, middle, mid_one, mid_two, norm2_gain, norm2_bias, scale_part, shift_part
    )[1](grad_act_two)
    summed_one, summed_two = reduce_grads(second_pull[1], second_pull[2])
    grad_middle = second_pull[0] + norm_back(middle, summed_one, summed_two)
    grad_conv1 = jax.vjp(lambda kernel: conv_rows(act_one, kernel), conv1)[1](grad_middle)[0]
    grad_act_one = conv_rows(pad_grads(grad_middle), flipped(conv1))

    def first_piece(inputs_in, sum_one, sum_two, gain_in, incoming_bias):
        return jax.nn.gelu(
            apply_norm(inputs_in, sum_one, sum_two, gain_in, incoming_bias, total_in),
            approximate=False,
        )

    first_pull = jax.vjp(first_piece, inputs, in_one, in_two, norm1_gain, norm1_bias)[1](
        grad_act_one
    )
    first_one, first_two = reduce_grads(first_pull[1], first_pull[2])
    grad_inputs = first_pull[0] + norm_back(inputs, first_one, first_two)
    grads = (
        first_pull[3],
        first_pull[4],
        grad_conv1,
        second_pull[3],
        second_pull[4],
        grad_conv2,
        grad_bias2,
    )
    return (grad_inputs, grads, second_pull[5], second_pull[6])


def conditioning(step_item, table):
    one_hot = (jnp.arange(table.shape[0], dtype=jnp.int32) == step_item).astype(jnp.float32)
    condition = jnp.dot(one_hot, table, precision=HIGH)
    half_width = table.shape[1] // 2
    return (condition[:half_width], condition[half_width:], one_hot)


def project_in(frames_item, mask_item, count_item, incoming_weight, incoming_bias):
    history = jnp.arange(HIST, dtype=jnp.int32) >= HIST - count_item
    keep = jnp.repeat(history, FIELDS).astype(jnp.float32)
    lifted = (
        jnp.einsum(
            "fhw,fc->hwc", frames_item * keep[:, None, None], incoming_weight, precision=HIGH
        )
        + incoming_bias
    )
    return lifted * mask_item[:, :, None].astype(jnp.float32)


def coarsen_field(value_arrays, incoming_weight, incoming_bias):
    rows_here, width_here, depth_here = value_arrays.shape
    blocks = value_arrays.reshape(rows_here // 2, 2, width_here // 2, 2, depth_here)
    return jnp.einsum("iajbk,abkc->ijc", blocks, incoming_weight, precision=HIGH) + incoming_bias


def upsample(value_arrays, incoming_weight, incoming_bias):
    result = jnp.einsum("ijk,abkc->iajbc", value_arrays, incoming_weight, precision=HIGH)
    extent = result.shape
    return result.reshape(extent[0] * 2, extent[2] * 2, extent[4]) + incoming_bias


def flatten_all(pieces):
    return jnp.concatenate([piece.reshape(-1) for piece in pieces])


def unflatten_all(flat, templates):
    pieces = []
    offset_at = 0
    for template in templates:
        count_here = template.size
        pieces.append(flat[offset_at : offset_at + count_here].reshape(template.shape))
        offset_at += count_here
    return tuple(pieces)


def strips_body(
    frames,
    counts,
    cell_mask,
    step_index,
    lift_weight,
    lift_bias,
    enc_norm1_gain,
    enc_norm1_bias,
    enc_conv1,
    enc_step_table,
    enc_norm2_gain,
    enc_norm2_bias,
    enc_conv2,
    enc_conv2_bias,
    reducer_weight,
    reducer_bias,
    up_weight,
    up_bias,
    dec_norm1_gain,
    dec_norm1_bias,
    dec_conv1,
    dec_step_table,
    dec_norm2_gain,
    dec_norm2_bias,
    dec_conv2,
    dec_conv2_bias,
    skip_weight,
    skip_bias,
    cotangent,
):
    enc_weights = (
        enc_norm1_gain,
        enc_norm1_bias,
        enc_conv1,
        enc_norm2_gain,
        enc_norm2_bias,
        enc_conv2,
        enc_conv2_bias,
    )
    dec_weights = (
        dec_norm1_gain,
        dec_norm1_bias,
        dec_conv1,
        dec_norm2_gain,
        dec_norm2_bias,
        dec_conv2,
        dec_conv2_bias,
    )
    params = (
        lift_weight,
        lift_bias,
        enc_norm1_gain,
        enc_norm1_bias,
        enc_conv1,
        enc_step_table,
        enc_norm2_gain,
        enc_norm2_bias,
        enc_conv2,
        enc_conv2_bias,
        reducer_weight,
        reducer_bias,
        up_weight,
        up_bias,
        dec_norm1_gain,
        dec_norm1_bias,
        dec_conv1,
        dec_step_table,
        dec_norm2_gain,
        dec_norm2_bias,
        dec_conv2,
        dec_conv2_bias,
        skip_weight,
        skip_bias,
    )

    def forward_micro(carry, sliced):
        frames_item, mask_item, count_item, step_item = sliced
        lifted = project_in(frames_item, mask_item, count_item, lift_weight, lift_bias)
        enc_scale, enc_shift, unused_hot = conditioning(step_item, enc_step_table)
        enc_branch, enc_kept = block_forward(lifted, enc_weights, enc_scale, enc_shift)
        encoder_result = lifted + enc_branch
        coarse_field = coarsen_field(encoder_result, reducer_weight, reducer_bias)
        foreign = from_behind(coarse_field, "section", 1)
        raised_foreign = upsample(foreign, up_weight, up_bias)
        raised = from_behind(raised_foreign, "section", 1)
        joined = jnp.concatenate([raised, encoder_result], axis=-1)
        dec_scale, dec_shift, unused_again = conditioning(step_item, dec_step_table)
        dec_branch, dec_kept = block_forward(joined, dec_weights, dec_scale, dec_shift)
        output_item = jnp.dot(joined, skip_weight, precision=HIGH) + skip_bias + dec_branch
        return (carry, (output_item, (lifted, enc_kept, encoder_result, foreign, joined, dec_kept)))

    unused, (output, kept_all) = lax.scan(
        forward_micro, jnp.zeros((), jnp.float32), (frames, cell_mask, counts, step_index)
    )

    def backward_micro(totals, sliced):
        frames_item, mask_item, count_item, step_item, grad_out, kept = sliced
        lifted, enc_kept, encoder_result, foreign, joined, dec_kept = kept
        dec_scale, dec_shift, one_hot = conditioning(step_item, dec_step_table)
        grad_joined, dec_grads, dec_gscale, dec_gshift = block_backward(
            joined, dec_weights, dec_scale, dec_shift, dec_kept, grad_out
        )
        grad_skip_weight = jnp.einsum("hwk,hwc->kc", joined, grad_out, precision=HIGH)
        grad_skip_bias = jnp.sum(grad_out, axis=(0, 1))
        grad_joined = grad_joined + jnp.dot(grad_out, skip_weight.T, precision=HIGH)
        half_width = joined.shape[-1] // 2
        grad_raised = grad_joined[..., :half_width]
        grad_encoded = grad_joined[..., half_width:]
        grad_foreign_up = from_behind(grad_raised, "section", 1)
        up_pull = jax.vjp(upsample, foreign, up_weight, up_bias)[1](grad_foreign_up)
        coarse_gradient = from_behind(up_pull[0], "section", 1)
        reducer_pullback = jax.vjp(coarsen_field, encoder_result, reducer_weight, reducer_bias)[1](
            coarse_gradient
        )
        grad_encoded = grad_encoded + reducer_pullback[0]
        enc_scale, enc_shift, enc_hot = conditioning(step_item, enc_step_table)
        grad_lifted, enc_grads, enc_gscale, enc_gshift = block_backward(
            lifted, enc_weights, enc_scale, enc_shift, enc_kept, grad_encoded
        )
        grad_lifted = grad_lifted + grad_encoded
        proj_pull = jax.vjp(
            lambda frames_in, incoming_weight, incoming_bias: project_in(
                frames_in, mask_item, count_item, incoming_weight, incoming_bias
            ),
            frames_item,
            lift_weight,
            lift_bias,
        )[1](grad_lifted)
        enc_table_grad = enc_hot[:, None] * jnp.concatenate([enc_gscale, enc_gshift])[None, :]
        dec_table_grad = one_hot[:, None] * jnp.concatenate([dec_gscale, dec_gshift])[None, :]
        micro_list = (
            proj_pull[1],
            proj_pull[2],
            enc_grads[0],
            enc_grads[1],
            enc_grads[2],
            enc_table_grad,
            enc_grads[3],
            enc_grads[4],
            enc_grads[5],
            enc_grads[6],
            reducer_pullback[1],
            reducer_pullback[2],
            up_pull[1],
            up_pull[2],
            dec_grads[0],
            dec_grads[1],
            dec_grads[2],
            dec_table_grad,
            dec_grads[3],
            dec_grads[4],
            dec_grads[5],
            dec_grads[6],
            grad_skip_weight,
            grad_skip_bias,
        )
        micro_flat = flatten_all(micro_list)
        return (totals + micro_flat, proj_pull[0])

    total_size = sum((piece.size for piece in params))
    start_totals = jnp.zeros((total_size,), jnp.float32)
    flat_totals, frames_grad = lax.scan(
        backward_micro,
        start_totals,
        (frames, cell_mask, counts, step_index, cotangent, kept_all),
        reverse=True,
    )
    flat_totals = lax.psum(flat_totals, ("section", "batch", "rows"))
    grads = unflatten_all(flat_totals, params)
    return (output, frames_grad) + grads


F32 = jnp.float32
BF16 = jnp.bfloat16
MESH = pl.DeviceIdType.MESH
NN = ((1,), (0,))
NT = ((1,), (1,))
TN = ((0,), (0,))
HIGH_AT = (0, 2, 1)
LOW_AT = (4, 3, 5)
CHUNK = 512
class Given(NamedTuple):
    frames: Any
    counts: Any
    cell_mask: Any
    step_index: Any
    lift_weight: Any
    lift_bias: Any
    enc_norm1_gain: Any
    enc_norm1_bias: Any
    enc_conv1: Any
    enc_step_table: Any
    enc_norm2_gain: Any
    enc_norm2_bias: Any
    enc_conv2: Any
    enc_conv2_bias: Any
    reducer_weight: Any
    reducer_bias: Any
    up_weight: Any
    up_bias: Any
    dec_norm1_gain: Any
    dec_norm1_bias: Any
    dec_conv1: Any
    dec_step_table: Any
    dec_norm2_gain: Any
    dec_norm2_bias: Any
    dec_conv2: Any
    dec_conv2_bias: Any
    skip_weight: Any
    skip_bias: Any
    cotangent: Any


ARGUMENTS = Given._fields
LARGE = tuple(
    dict(
        dec_conv1=0,
        up_weight=0,
        reducer_weight=0,
        dec_conv2=0,
        skip_weight=0,
        enc_conv1=0,
        enc_conv2=0,
    )
)
IN_HBM = tuple(dict(frames=0, cell_mask=0, cotangent=0)) + LARGE
IN_SMEM = tuple(dict(counts=0, step_index=0))
LATE = 64
SMALL_ROWS = dict(
    enc_conv2_bias=(0, 1),
    reducer_bias=(1, 1),
    up_bias=(2, 1),
    dec_conv2_bias=(3, 1),
    skip_bias=(3, 1),
    dec_norm1_gain=(4, 2),
    dec_norm1_bias=(6, 2),
    dec_norm2_gain=(8, 1),
    dec_norm2_bias=(9, 1),
    dec_step_table=(16, 8),
    lift_weight=(LATE, 12),
    lift_bias=(LATE + 12, 1),
    enc_norm1_gain=(LATE + 16, 1),
    enc_norm1_bias=(LATE + 17, 1),
    enc_norm2_gain=(LATE + 18, 1),
    enc_norm2_bias=(LATE + 19, 1),
    enc_step_table=(LATE + 24, 8),
)
LATE_COUNT = 32
PIECES = 4
SMALL_COUNT = LATE + LATE_COUNT
DUE = ((), (), (), (), (), (0,), (), (1,), (), (), (2,), (3, 0), (), (), (1,), (), (), (2,), (0,), (1, 4, 3), (2,), (), (), (5, 0), (1, 3), (4, 2), (), (6,), (7, 3, 0, 5, 4, 1, 2))
REST = (6, 3, 7, 4, 5, 6, 8, 7, 0, 4, 5, 1, 6, 7, 2, 0, 1, 5, 3, 6, 2, 8, 7, 3, 4, 5, 4, 6, 7, 5, 6, 7)
OUTPUTS = tuple(dict(output=0, frames_grad=0, gradients=0))


def split(value):
    high = value.astype(BF16)
    return high, (value - high.astype(F32)).astype(BF16)


def dot(left, right, dims=NN, precision=None):
    return lax.dot_general(
        left, right, (dims, ((), ())), precision=precision, preferred_element_type=F32
    )


def fold(value):
    half = value.shape[1] // 2
    return value[:, :half] + value[:, half:]


def fold_rows(value):
    half = value.shape[0] // 2
    return value[:half] + value[half:]


def tile_sums(value):
    return jnp.sum(value.reshape(-1, 8, value.shape[-1]), axis=0)


def column_sum(tiles):
    return jnp.sum(tiles, axis=0, keepdims=True)


def normal(value):
    bell = jnp.exp(-0.5 * value * value)
    t = 1.0 / (1.0 + 0.2316418882663604 * jnp.abs(value))
    poly = 0.5307027145
    for factor in (-0.7265760135, 0.7107068705, -0.142248368, 0.127414796):
        poly = poly * t + factor
    tail = poly * t * bell
    return jnp.where(value < 0.0, tail, 1.0 - tail), 0.3989422804014327 * bell


def dot_three(left, right, dims=NN):
    left_high, left_low = split(left)
    right_high, right_low = split(right)
    total = dot(left_high, right_high, dims)
    return total + (dot(left_high, right_low, dims) + dot(left_low, right_high, dims))


def group_ones(channels, size):
    rows = lax.broadcasted_iota(jnp.int32, (channels, channels), 0) // size
    columns = lax.broadcasted_iota(jnp.int32, (channels, channels), 1) // size
    return (rows == columns).astype(BF16)


def group_sums(first, second, ones):
    terms = []
    rest = jnp.concatenate([first, second], axis=0)
    for _ in range(3):
        term = rest.astype(BF16)
        terms.append(term)
        rest = rest - term.astype(F32)
    both = dot(jnp.concatenate(terms, axis=0), ones)
    both = both[32:48] + both[16:32] + both[:16]
    return column_sum(both[:8]), column_sum(both[8:])


class LineSwap:

    def __init__(self, line, source, target, inward, across, make):
        far = 3 - line.outer
        self.line = line
        to_inner, to_across = line.device(line.inner), line.device(line.across)
        to_outer = line.device(line.outer)
        here = target(line.here)
        self.to_far = make(source(3 - line.here), inward.at[1], to_inner)
        self.to_second = make(source(3 - line.inner), inward.at[0], to_inner)
        self.to_inner = make(source(line.inner), here, to_inner)
        self.for_far = make(source(far), across.at[0], to_across)
        self.to_across = make(source(line.across), here, to_across)
        self.to_outer = make(source(line.outer), here, to_outer)
        self.pass_far = make(inward.at[1], across.at[1], to_across)
        self.pass_second = make(inward.at[0], target(line.outer), to_across)
        self.pass_across = make(across.at[0], target(line.across), to_outer)
        self.pass_opposite = make(across.at[1], target(far), to_outer)

    def first(self):
        @pl.when(self.line.edge)
        def _():
            for copy in (self.to_far, self.to_second, self.to_inner):
                copy.start()

        @pl.when(self.line.middle)
        def _():
            for copy in (self.for_far, self.to_across, self.to_outer):
                copy.start()

    def second(self):
        @pl.when(self.line.middle)
        def _():
            self.for_far.wait_recv()
            self.pass_across.start()
            self.to_far.wait_recv()
            self.pass_far.start()
            self.to_second.wait_recv()
            self.pass_second.start()

    def third(self):
        @pl.when(self.line.middle)
        def _():
            self.pass_far.wait_recv()
            self.pass_opposite.start()

    def arrive(self):
        @pl.when(self.line.edge)
        def _():
            for copy in (self.to_outer, self.pass_across, self.pass_opposite):
                copy.wait_recv()

        @pl.when(self.line.middle)
        def _():
            for copy in (self.to_inner, self.to_across, self.pass_second):
                copy.wait_recv()

    def sent(self):
        @pl.when(self.line.edge)
        def _():
            for copy in (self.to_far, self.to_second, self.to_inner):
                copy.wait_send()

        @pl.when(self.line.middle)
        def _():
            for copy in (self.for_far, self.to_across, self.to_outer):
                copy.wait_send()
            for copy in (self.pass_far, self.pass_second, self.pass_across, self.pass_opposite):
                copy.wait_send()


class Exchange:

    def __init__(self, place, start, rows, landing, first_sem):
        self.place, self.start, self.rows, self.landing = place, start, rows, landing
        self.sem = first_sem
        self.stage = 0
        self.copies = []
        self.waiting = []
        self.group = place.plane_group
        self.half = rows // 2
        self.base = start + place.core * self.half
        self._finish(self.half)

    def _finish(self, size):
        self.part = size // self.group.count
        self.own = self.base + self.group.here * self.part

    def count(self):
        return 2 * PIECES + 2 * (self.group.count - 1) + 3

    def land_rows(self):
        return self.half + (self.group.count + 1) * self.part

    def _copy(self, source, target, device, only=None):
        place = self.place
        copy = pltpu.make_async_remote_copy(
            src_ref=source,
            dst_ref=target,
            send_sem=place.send.at[self.sem],
            recv_sem=place.recv.at[self.sem],
            device_id=device,
            device_id_type=MESH,
        )
        self.sem += 1
        if only is None:
            copy.start()
            self.waiting.append(copy)
        self.copies.append((copy, only))
        return copy

    def _pieces(self, source, at, target, to, size, device):
        each = size // 8 // PIECES * 8
        for k in range(PIECES):
            here = each if k < PIECES - 1 else size - each * (PIECES - 1)
            self._copy(
                source.at[self._rows(at + k * each, here)],
                target.at[self._rows(to + k * each, here)],
                device,
            )

    def _wait(self):
        for copy in self.waiting:
            copy.wait_recv()
        self.waiting = []

    def _rows(self, at, size):
        return pl.ds(pl.multiple_of(at, 8), size)

    def _swap(self):
        place = self.place
        other = self.start + (1 - place.core) * self.half
        self.land = self.landing
        self.landing += self.half
        self._pieces(place.sums, other, place.landing, self.land, self.half, place.partner)

    def _add_swap(self):
        place = self.place
        block = 64 if self.half % 64 == 0 else 32

        def step(i, carry):
            here = self._rows(self.base + i * block, block)
            there = self._rows(self.land + i * block, block)
            place.sums[here] = place.sums[here] + place.landing[there]
            return carry

        lax.fori_loop(0, self.half // block, step, 0)

    def _scatter(self, group, base, size):
        place = self.place
        self.land = self.landing
        for k in range(1, group.count):
            to = lax.rem(group.here + k, group.count)
            self._copy(
                place.sums.at[self._rows(base + to * size, size)],
                place.landing.at[pl.ds(self.landing, size)],
                group.device(to),
            )
            self.landing += size

    def _total(self, group, own, size, target):
        place = self.place
        block = 16 if size % 16 == 0 else 8

        def step(i, carry):
            here = self._rows(own + i * block, block)
            total = place.sums[here]
            for k in range(group.count - 1):
                there = self._rows(self.land + k * size + i * block, block)
                total = total + place.landing[there]
            target[here] = total
            return carry

        lax.fori_loop(0, size // block, step, 0)

    def _gather(self, group, own, size):
        final = self.place.final
        here = self._rows(own, size)
        for k in range(1, group.count):
            to = lax.rem(group.here + k, group.count)
            self._copy(final.at[here], final.at[here], group.device(to))

    def _steps(self):
        place, group = self.place, self.group
        yield self._swap()
        self._wait()
        self._add_swap()
        yield from self._both()
        self._pieces(place.final, self.base, place.final, self.base, self.half, place.partner)
        yield
        self._wait()
        yield

    def _both(self):
        place, group = self.place, self.group
        self._scatter(group, self.base, self.part)
        yield
        self._wait()
        self._total(group, self.own, self.part, place.sums)
        yield from self._line()
        self._gather(group, self.own, self.part)
        yield
        self._wait()

    def _line(self):
        place, line = self.place, self.place.line
        sums, final, landing = place.sums, place.final, place.landing
        part, own = self.part, self._rows(self.own, self.part)
        inward, across = pl.ds(self.landing, part), pl.ds(self.landing + part, part)
        self.landing += 2 * part
        block = 16 if part % 16 == 0 else 8

        def add(at, target):
            def step(i, carry):
                here = self._rows(self.own + i * block, block)
                target[here] = sums[here] + landing[pl.ds(at + i * block, block)]
                return carry

            lax.fori_loop(0, part // block, step, 0)

        first = self._copy(sums.at[own], landing.at[inward], line.device(line.inner), line.edge)
        second = self._copy(sums.at[own], landing.at[across], line.device(line.across), line.middle)
        third = self._copy(final.at[own], final.at[own], line.device(line.outer), line.middle)
        pl.when(line.edge)(first.start)
        yield

        @pl.when(line.middle)
        def _():
            first.wait_recv()
            add(self.landing - 2 * part, sums)
            second.start()

        yield

        @pl.when(line.middle)
        def _():
            second.wait_recv()
            add(self.landing - part, final)
            third.start()

        yield
        pl.when(line.edge)(third.wait_recv)

    def advance(self):
        if self.stage == 0:
            self.steps = self._steps()
        self.stage += 1
        next(self.steps)

    def done(self):
        return self.stage == 8


class SmallExchange(Exchange):

    def count(self):
        return self.place.cores_group.count + self.place.line.count - 2

    def land_rows(self):
        return self.rows * (self.place.cores_group.count + self.place.line.count)

    def _share(self, group, source):
        place = self.place
        self.land = self.landing
        self.landing += group.count * self.rows
        own = self._rows(self.land + group.here * self.rows, self.rows)
        place.landing[own] = source[...]
        for k in range(1, group.count):
            to = lax.rem(group.here + k, group.count)
            self._copy(source, place.landing.at[own], group.device(to))

    def _sum(self, group):
        total = None
        for k in range(group.count):
            part = self.place.landing[pl.ds(self.land + k * self.rows, self.rows)]
            total = part if total is None else total + part
        return total

    def _steps(self):
        place = self.place
        here = pl.ds(self.start, self.rows)
        self._share(place.line, place.sums.at[here])
        yield
        self._wait()
        place.small[...] = self._sum(place.line)
        self._share(place.cores_group, place.small)
        yield
        self._wait()
        place.final[here] = self._sum(place.cores_group)
        yield

    def done(self):
        return self.stage == 3


def layout_of(shapes):
    starts = {}
    at = 0
    for name in LARGE:
        starts[name] = at
        at += getattr(shapes, name)[0]
    small = at
    begins = SimpleNamespace(**starts)
    late = small + LATE
    tap = shapes.dec_conv2[0] // 3
    part = shapes.dec_conv1[0] // 3
    conv1, up = begins.dec_conv1, begins.up_weight
    edges = (
        (begins.dec_conv2, begins.enc_conv1),
        (conv1, conv1 + part),
        (conv1 + part, conv1 + 2 * part),
        (conv1 + 2 * part, up),
        (up, begins.dec_conv2),
        (begins.enc_conv2, late),
        (begins.enc_conv1, begins.enc_conv1 + 2 * tap),
        (begins.enc_conv1 + 2 * tap, begins.enc_conv2),
        (late, late + LATE_COUNT),
    )
    runs = [(first, last - first) for first, last in edges]
    return starts, small, late + LATE_COUNT, runs


def item_kernel(sizes, scratch_names, *refs):
    line, strip, width, shapes, big_layout = sizes
    begins, small_at, total_rows, runs = big_layout
    starts = SimpleNamespace(**begins)
    inputs = Given(*refs[: len(ARGUMENTS)])
    refs = refs[len(ARGUMENTS) :]
    output_names = OUTPUTS
    outputs = SimpleNamespace(**dict(zip(output_names, refs)))
    scratch = SimpleNamespace(**dict(zip(scratch_names, refs[len(output_names) :])))

    def w_of(name):
        return getattr(scratch, name)

    height = strip * line
    cells = height * width
    c = inputs.lift_weight.shape[1]
    strip_cells = strip * width
    history = inputs.frames.shape[1]

    core = lax.axis_index("section")
    plane = lax.axis_index("batch")
    row = lax.axis_index("rows")
    middle = lax.rem(row + 1, 4) // 2

    def device_at(to):
        return (core, plane, to)

    place = SimpleNamespace(
        core=core,
        partner=(1 - core, plane, row),
        line=SimpleNamespace(
            count=line,
            here=row,
            device=device_at,
            middle=middle == 1,
            edge=middle == 0,
            inner=1 + row // 2,
            across=3 - row,
            outer=3 * (row // 2),
        ),
        plane_group=SimpleNamespace(
            count=4, here=plane, device=lambda to: (core, to, row)
        ),
        cores_group=SimpleNamespace(
            count=8,
            here=core * 4 + plane,
            device=lambda to: (to // 4, lax.rem(to, 4), row),
        ),
        small=scratch.small,
        sums=scratch.sums,
        final=outputs.gradients,
        landing=scratch.landing,
        send=scratch.send,
        recv=scratch.recv,
    )
    local_sem = scratch.local

    frames_in, mask_in, cot = scratch.frames_in, scratch.mask_in, scratch.cot
    here_rows = pl.ds(pl.multiple_of(row * strip_cells, strip_cells), strip_cells)
    frames_from, mask_from, cot_from = scratch.frames_from, scratch.mask_from, scratch.cot_from
    staged = (
        pltpu.make_async_copy(inputs.frames, frames_from, local_sem.at[7]),
        pltpu.make_async_copy(inputs.cell_mask, mask_from, local_sem.at[8]),
        pltpu.make_async_copy(inputs.cotangent, cot_from, local_sem.at[9]),
    )
    for copy in staged:
        copy.start()

    weight_copies = {}
    for k, name in enumerate(LARGE):
        copy = pltpu.make_async_copy(getattr(inputs, name), w_of(name), local_sem.at[k])
        weight_copies[name] = copy
        copy.start()

    barrier = pltpu.get_barrier_semaphore()
    peers = [device_at(lax.rem(row + k, line)) for k in range(1, line)]
    cores_group = place.cores_group
    for k in range(1, 8):
        peers.append(cores_group.device(lax.rem(cores_group.here + k, 8)))
    for device in peers:
        pl.semaphore_signal(barrier, inc=1, device_id=device, device_id_type=MESH)
    pl.semaphore_wait(barrier, len(peers))

    next_sem = 0

    def make(source, target, device):
        nonlocal next_sem
        copy = pltpu.make_async_remote_copy(
            src_ref=source,
            dst_ref=target,
            send_sem=scratch.send.at[next_sem],
            recv_sem=scratch.recv.at[next_sem],
            device_id=device,
            device_id_type=MESH,
        )
        next_sem += 1
        return copy

    def send(source, target, device):
        copy = make(source, target, device)
        copy.start()
        return copy

    def strip_of(ref, to):
        return ref.at[pl.ds(pl.multiple_of(to * strip_cells, strip_cells), strip_cells)]

    frame_copies, output_copies = [], []
    for copy in staged[:2]:
        copy.wait()
    for k in range(1, line):
        to = lax.rem(row + k, line)
        device = device_at(to)
        frame_copies.append(send(frames_from.at[to], frames_in.at[row], device))
        frame_copies.append(send(mask_from.at[to], mask_in.at[row], device))
    staged[2].wait()
    cot_swap = LineSwap(
        place.line,
        lambda to: cot_from.at[to],
        lambda source: strip_of(cot, source),
        scratch.cot_inward,
        scratch.cot_across,
        make,
    )
    cot_swap.first()

    copied = SimpleNamespace(**weight_copies)
    def put_pair(target, block, value):
        high, low = split(value)
        rows = slice(block * c, (block + 1) * c)
        target[rows, 0:c] = high
        target[rows, c : 2 * c] = low

    def stack_conv(source, half, depth, forward, backward):
        for a in range(3):
            for b in range(3):
                at = (3 * a + b) * depth + half * c
                value = source[at : at + c, :]
                turned = value.T
                for places in (HIGH_AT, LOW_AT):
                    put_pair(forward, 6 * a + places[b], value)
                    put_pair(backward, 6 * (2 - a) + places[2 - b], turned)

    copied.enc_conv1.wait()
    stack_conv(scratch.enc_conv1, 0, c, scratch.fe1, scratch.be1)
    copied.enc_conv2.wait()
    stack_conv(scratch.enc_conv2, 0, c, scratch.fe2, scratch.be2)
    copied.reducer_weight.wait()
    for k in range(4):
        value = scratch.reducer_weight[k * c : (k + 1) * c, :]
        turned = value.T
        for block in (k, k + 4):
            put_pair(scratch.f_down, block, value)
        for block in (0, 1):
            put_pair(scratch.b_down.at[k], block, turned)
    copied.up_weight.wait()
    for k in range(4):
        value = scratch.up_weight[k * c : (k + 1) * c, :]
        turned = value.T
        for block in (0, 1):
            put_pair(scratch.f_up.at[k], block, value)
        for block in (k, k + 4):
            put_pair(scratch.b_up, block, turned)
    copied.dec_conv1.wait()
    stack_conv(scratch.dec_conv1, 0, 2 * c, scratch.fd1a, scratch.bd1a)
    stack_conv(scratch.dec_conv1, 1, 2 * c, scratch.fd1b, scratch.bd1b)
    copied.dec_conv2.wait()
    stack_conv(scratch.dec_conv2, 0, c, scratch.fd2, scratch.bd2)
    copied.skip_weight.wait()
    for half in range(2):
        value = scratch.skip_weight[half * c : (half + 1) * c, :]
        turned = value.T
        for block in (half, half + 2):
            put_pair(scratch.f_skip, block, value)
        for block in (0, 1):
            put_pair(scratch.b_skip.at[half], block, turned)

    for buffer in (scratch.xe1, scratch.xe2, scratch.xd1a, scratch.xd1b, scratch.xd2, scratch.xg):
        edge = jnp.zeros((width, 6 * c), BF16)
        buffer[0:width, :] = edge
        buffer[cells + width : cells + 2 * width, :] = edge

    lift = scratch.lift
    lift[...] = jnp.zeros(lift.shape, F32)
    lift[0:history, :] = inputs.lift_weight[...]
    lift[history : history + 1, :] = inputs.lift_bias[...]

    block = 2 * width
    column = lax.rem(lax.broadcasted_iota(jnp.int32, (block, c), 0), width)
    at_first, at_last = column == 0, column == width - 1
    zeros8 = jnp.zeros((8, c), F32)
    ones16 = group_ones(c, c // GROUPS)
    ones32 = group_ones(c, 2 * c // GROUPS)
    count16 = float(cells * (c // GROUPS))
    count32 = float(cells * (2 * c // GROUPS))

    def grid_rows(step, carry=0):
        return lax.fori_loop(0, cells // block, step, carry, unroll=2)

    def row_at(h):
        return pl.ds(pl.multiple_of(h * block, block), block)

    def chunk_at(i):
        return pl.ds(pl.multiple_of(i * CHUNK, CHUNK), CHUNK)

    def put_row(target, h, value):
        rows = pl.ds(pl.multiple_of(h * block + width, width), block)
        left = jnp.where(at_first, 0.0, pltpu.roll(value, 1, 0))
        right = jnp.where(at_last, 0.0, pltpu.roll(value, block - 1, 0))
        for b, piece in enumerate((left, value, right)):
            high, low = split(piece)
            target[rows, HIGH_AT[b] * c : (HIGH_AT[b] + 1) * c] = high
            target[rows, LOW_AT[b] * c : (LOW_AT[b] + 1) * c] = low

    def put_turned(target, columns, value, first=0, second=1):
        high, low = split(value.T)
        target[first * c : (first + 1) * c, columns] = high
        target[second * c : (second + 1) * c, columns] = low

    def conv_chunk(pairs, i):
        total = None
        for data, weight in pairs:
            taps = []
            for a in range(3):
                rows = pl.ds(pl.multiple_of(i * CHUNK + a * width, width), CHUNK)
                taps.append(data[rows, :])
            part = dot(jnp.concatenate(taps, axis=1), weight[...])
            total = part if total is None else total + part
        return total

    def norm_of(first, second, ones, count):
        one, two = group_sums(first, second, ones)
        mean = one / count
        return mean, lax.rsqrt(two / count - mean * mean + EPS)

    def activate(source, target, turned, slope, scale, shift):
        def step(h, carry):
            value = source[row_at(h), :] * scale + shift
            below, density = normal(value)
            slope[row_at(h), :] = below + value * density
            value = value * below
            put_row(target, h, value)
            put_turned(turned, row_at(h), value)
            return carry

        grid_rows(step)

    def conv_norm(pairs, target):
        def step(i, carry):
            value = fold(conv_chunk(pairs, i))
            target[chunk_at(i), :] = value
            return carry[0] + tile_sums(value), carry[1] + tile_sums(value * value)

        return lax.fori_loop(0, cells // CHUNK, step, (zeros8, zeros8))

    def sums_of(source):
        def step(h, carry):
            value = source[row_at(h), :]
            return carry[0] + tile_sums(value), carry[1] + tile_sums(value * value)

        return grid_rows(step, (zeros8, zeros8))

    step_here = jnp.full((1, c), inputs.step_index[row], jnp.int32)

    def condition(table):
        total = jnp.zeros((1, 2 * c), F32)
        chosen = jnp.concatenate([step_here, step_here], axis=1)
        for s in range(table.shape[0]):
            total = total + jnp.where(chosen == s, table[s : s + 1, :], 0.0)
        return total[:, :c], total[:, c:]

    frames_in[row] = frames_from[row]
    mask_in[row] = mask_from[row]
    for copy in frame_copies:
        copy.wait_recv()
    fields = scratch.fields
    fields[...] = jnp.zeros(fields.shape, F32)
    frame_of = lax.broadcasted_iota(jnp.int32, (history, width), 0) // FIELDS
    keep = (frame_of >= HIST - inputs.counts[row]).astype(F32)
    masks = []
    for source in range(line):
        for k in range(strip):
            columns = slice((source * strip + k) * width, (source * strip + k + 1) * width)
            mask = mask_in[source, k : k + 1, :].astype(F32)
            masks.append(mask)
            fields[0:history, columns] = frames_in[source, :, k, :] * keep * mask
            fields[history : history + 1, columns] = mask
    lifted = scratch.lifted
    lifted[...] = dot_three(fields[...], lift[...], TN)

    enc_scale, enc_shift = condition(inputs.enc_step_table)
    dec_scale, dec_shift = condition(inputs.dec_step_table)

    mean_e1, inv_e1 = norm_of(*sums_of(lifted), ones16, count16)
    gain_e1, bias_e1 = inputs.enc_norm1_gain[...], inputs.enc_norm1_bias[...]
    a_e1 = inv_e1 * gain_e1
    activate(lifted, scratch.xe1, scratch.te1, scratch.slope_e1, a_e1, bias_e1 - mean_e1 * a_e1)
    middle_e = scratch.middle_e
    mean_e2, inv_e2 = norm_of(
        *conv_norm([(scratch.xe1, scratch.fe1)], middle_e), ones16, count16
    )
    gain_e2, bias_e2 = inputs.enc_norm2_gain[...], inputs.enc_norm2_bias[...]
    a_e2 = inv_e2 * gain_e2
    activate(
        middle_e,
        scratch.xe2,
        scratch.te2,
        scratch.slope_e2,
        a_e2 * (1.0 + enc_scale),
        (bias_e2 - mean_e2 * a_e2) * (1.0 + enc_scale) + enc_shift,
    )
    cot_swap.second()
    encoded = scratch.encoded
    conv2_bias = inputs.enc_conv2_bias[...]
    joined = scratch.joined

    def encode(i, carry):
        value = fold(conv_chunk([(scratch.xe2, scratch.fe2)], i))
        value = value + conv2_bias + lifted[chunk_at(i), :]
        encoded[chunk_at(i), :] = value
        high, low = split(value)
        joined[chunk_at(i), c : 2 * c] = high
        joined[chunk_at(i), 3 * c : 4 * c] = low
        put_turned(scratch.turned, chunk_at(i), value, 1, 3)
        return carry[0] + tile_sums(value), carry[1] + tile_sums(value * value)

    sums_enc = lax.fori_loop(0, cells // CHUNK, encode, (zeros8, zeros8))

    half_cells, quarter = cells // 2, cells // 4

    def pick(source):
        pieces = []
        for b in range(2):
            value = source[pl.ds(b, half_cells, stride=2), :]
            value = value.reshape(height // 2, 2, width // 2, c)
            pieces.append([value[:, a].reshape(quarter, c) for a in range(2)])
        return [pieces[b][a] for a in range(2) for b in range(2)]

    def place_cells(target, pieces):
        for b in range(2):
            both = [pieces[2 * a + b].reshape(height // 2, 1, width // 2, c) for a in range(2)]
            value = jnp.concatenate(both, axis=1).reshape(half_cells, c)
            target[pl.ds(b, half_cells, stride=2), :] = value

    x_down = scratch.x_down
    for k, piece in enumerate(pick(encoded)):
        high, low = split(piece)
        x_down[:, k * c : (k + 1) * c] = high
        x_down[:, (k + 4) * c : (k + 5) * c] = low
    lowered = fold(dot(x_down[...], scratch.f_down[...])) + inputs.reducer_bias[...]
    x_up = scratch.x_up
    high, low = split(lowered)
    x_up[:, 0:c] = high
    x_up[:, c : 2 * c] = low
    raised = scratch.raised
    up_bias = inputs.up_bias[...]
    place_cells(
        raised, [fold(dot(x_up[...], scratch.f_up[k])) + up_bias for k in range(4)]
    )

    def raise_row(h, carry):
        value = raised[row_at(h), :]
        high, low = split(value)
        joined[row_at(h), 0:c] = high
        joined[row_at(h), 2 * c : 3 * c] = low
        put_turned(scratch.turned, row_at(h), value, 0, 2)
        return carry[0] + tile_sums(value), carry[1] + tile_sums(value * value)

    sums_raised = grid_rows(raise_row, (zeros8, zeros8))

    halves = []
    for half, (source, sums) in enumerate(((raised, sums_raised), (encoded, sums_enc))):
        mean, inv = norm_of(*sums, ones32, count32)
        gain = inputs.dec_norm1_gain[half : half + 1, :]
        bias = inputs.dec_norm1_bias[half : half + 1, :]
        scale = inv * gain
        activate(
            source,
            (scratch.xd1a, scratch.xd1b)[half],
            scratch.td1.at[2 * c * half : 2 * c * (half + 1)],
            (scratch.slope_d1a, scratch.slope_d1b)[half],
            scale,
            bias - mean * scale,
        )
        halves.append((source, mean, inv, gain))
    middle_d = scratch.middle_d
    pairs = [(scratch.xd1a, scratch.fd1a), (scratch.xd1b, scratch.fd1b)]
    mean_d2, inv_d2 = norm_of(*conv_norm(pairs, middle_d), ones16, count16)
    cot_swap.third()
    gain_d2, bias_d2 = inputs.dec_norm2_gain[...], inputs.dec_norm2_bias[...]
    a_d2 = inv_d2 * gain_d2
    activate(
        middle_d,
        scratch.xd2,
        scratch.td2,
        scratch.slope_d2,
        a_d2 * (1.0 + dec_scale),
        (bias_d2 - mean_d2 * a_d2) * (1.0 + dec_scale) + dec_shift,
    )
    result = scratch.result
    last_bias = inputs.dec_conv2_bias[...] + inputs.skip_bias[...]

    def decode(i, carry):
        value = conv_chunk([(scratch.xd2, scratch.fd2)], i)
        value = value + dot(joined[chunk_at(i), :], scratch.f_skip[...])
        result[chunk_at(i), :] = fold(value) + last_bias
        return carry

    lax.fori_loop(0, cells // CHUNK, decode, 0)
    output_here, frames_here = scratch.output_here, scratch.frames_here
    output_here[row] = result[here_rows]
    output_swap = LineSwap(
        place.line,
        lambda to: strip_of(result, to),
        lambda source: output_here.at[source],
        scratch.output_inward,
        scratch.output_across,
        make,
    )
    output_swap.first()

    exchanges = []
    waiting_runs = list(runs)
    landing_at = 0
    sem_at = 3 * (line - 1) + 20
    sums = scratch.sums

    def begin():
        nonlocal landing_at, sem_at
        start, rows = waiting_runs.pop(0)
        kind = Exchange if waiting_runs else SmallExchange
        exchange = kind(place, start, rows, landing_at, sem_at)
        landing_at += exchange.land_rows()
        sem_at += exchange.count()
        exchanges.append(exchange)
        exchange.advance()

    def advance(k):
        exchange = exchanges[k]
        exchange.advance()

    due = list(DUE)

    def point():
        for k in due.pop(0):
            advance(k)

    def small_row(k, value):
        sums[small_at + k : small_at + k + 1, :] = value

    def spread_grad(source):
        def step(h, carry):
            value = source[row_at(h), :]
            put_row(scratch.xg, h, value)
            return carry + tile_sums(value)

        return grid_rows(step, zeros8)

    def weight_grad(turned, at, depth, a):
        rows = pl.ds((2 - a) * width, cells)
        both = dot(turned[...], scratch.xg[rows, :])
        for half in range(depth // c):
            part = fold_rows(both[2 * c * half : 2 * c * (half + 1)])
            for b in range(3):
                high, low = HIGH_AT[2 - b] * c, LOW_AT[2 - b] * c
                to = at + (3 * a + b) * depth + half * c
                sums[to : to + c, :] = part[:, high : high + c] + part[:, low : low + c]

    def back_conv(weight, slope, target, source, mean, inv):
        carry = (zeros8, zeros8)
        for i in range(cells // CHUNK):
            value = fold(conv_chunk([(scratch.xg, weight)], i)) * slope[chunk_at(i), :]
            target[chunk_at(i), :] = value
            normed = (source[chunk_at(i), :] - mean) * inv
            carry = (carry[0] + tile_sums(value), carry[1] + tile_sums(value * normed))
            if i % (cells // CHUNK // 2) == cells // CHUNK // 2 - 1:
                point()
        return carry

    def norm_grad(sums_in, scale, ones, count):
        one, two = group_sums(sums_in[0] * scale, sums_in[1] * scale, ones)
        return one / count, two / count

    cot[here_rows] = cot_from[row]
    cot_swap.arrive()
    total_cot = column_sum(spread_grad(cot))
    for a in range(3):
        weight_grad(scratch.td2, starts.dec_conv2, c, a)
    part = fold(dot(scratch.turned[...], scratch.xg[width : cells + width, 2 * c : 4 * c]))
    sums[starts.skip_weight : starts.skip_weight + 2 * c, :] = fold_rows(part)
    small_row(3, total_cot)
    begin()

    grad = scratch.grad
    sums_d2 = back_conv(scratch.bd2, scratch.slope_d2, grad, middle_d, mean_d2, inv_d2)
    side_grads = (scratch.grad_a, scratch.grad_b)
    for half in range(2):

        def skip_back(i, carry, half=half):
            rows = pl.ds(pl.multiple_of(i * CHUNK + width, width), CHUNK)
            value = dot(scratch.xg[rows, 2 * c : 4 * c], scratch.b_skip[half])
            side_grads[half][chunk_at(i), :] = fold(value)
            return carry

        lax.fori_loop(0, cells // CHUNK, skip_back, 0)
    point()

    def table_rows(k, sums_in, gain, bias, one_plus):
        plain, times = column_sum(sums_in[0]), column_sum(sums_in[1])
        for s in range(inputs.enc_step_table.shape[0]):
            small_row(k + 2 * s, jnp.where(step_here == s, gain * times + bias * plain, 0.0))
            small_row(k + 2 * s + 1, jnp.where(step_here == s, plain, 0.0))
        return one_plus * times, one_plus * plain

    def middle_grad(source, mean, inv, scale, sums_in):
        zero, slope = norm_grad(sums_in, scale, ones16, count16)

        def step(h, carry):
            normed = (source[row_at(h), :] - mean) * inv
            value = inv * (grad[row_at(h), :] * scale - zero - normed * slope)
            put_row(scratch.xg, h, value)
            return carry

        grid_rows(step)

    gain_row, bias_row = table_rows(16, sums_d2, gain_d2, bias_d2, 1.0 + dec_scale)
    small_row(8, gain_row)
    small_row(9, bias_row)
    middle_grad(middle_d, mean_d2, inv_d2, gain_d2 * (1.0 + dec_scale), sums_d2)
    point()
    output_swap.second()
    for a in range(3):
        weight_grad(scratch.td1, starts.dec_conv1, 2 * c, a)
        point()
        begin()

    for half, (source, mean, inv, gain) in enumerate(halves):
        sums_in = back_conv(
            (scratch.bd1a, scratch.bd1b)[half],
            (scratch.slope_d1a, scratch.slope_d1b)[half],
            grad,
            source,
            mean,
            inv,
        )
        small_row(4 + half, column_sum(sums_in[1]))
        small_row(6 + half, column_sum(sums_in[0]))
        zero, slope = norm_grad(sums_in, gain, ones32, count32)
        target = side_grads[half]

        def input_grad(h, carry):
            normed = (source[row_at(h), :] - mean) * inv
            value = inv * (grad[row_at(h), :] * gain - zero - normed * slope)
            value = target[row_at(h), :] + value
            target[row_at(h), :] = value
            return carry + tile_sums(value)

        total = grid_rows(input_grad, zeros8)
        if half == 0:
            small_row(2, column_sum(total))
        point()

    output_swap.third()
    grad_raised, grad_encoded = side_grads
    x_grad_up = scratch.x_grad_up
    for k, piece in enumerate(pick(grad_raised)):
        high, low = split(piece)
        x_grad_up[:, k * c : (k + 1) * c] = high
        x_grad_up[:, (k + 4) * c : (k + 5) * c] = low
    grad_lowered = fold(dot(x_grad_up[...], scratch.b_up[...]))
    small_row(1, jnp.sum(grad_lowered, axis=0, keepdims=True))
    x_grad_low = scratch.x_grad_low
    high, low = split(grad_lowered)
    x_grad_low[:, 0:c] = high
    x_grad_low[:, c : 2 * c] = low
    point()
    part = fold(fold_rows(dot(x_up[...], x_grad_up[...], TN)))
    for k in range(4):
        at = starts.up_weight + k * c
        sums[at : at + c, :] = part[:, k * c : (k + 1) * c]
    part = fold_rows(fold(dot(x_down[...], x_grad_low[...], TN)))
    sums[starts.reducer_weight : starts.reducer_weight + 4 * c, :] = part
    point()
    begin()
    place_cells(
        grad, [fold(dot(x_grad_low[...], scratch.b_down[k])) for k in range(4)]
    )

    def join_row(h, carry):
        value = grad_encoded[row_at(h), :] + grad[row_at(h), :]
        grad_encoded[row_at(h), :] = value
        put_row(scratch.xg, h, value)
        return carry + tile_sums(value)

    small_row(0, column_sum(grid_rows(join_row, zeros8)))
    for k in range(10, 16):
        small_row(k, jnp.zeros((1, c), F32))
    sums[small_at + 24 : small_at + LATE, :] = jnp.zeros((LATE - 24, c), F32)
    point()
    for a in range(3):
        weight_grad(scratch.te2, starts.enc_conv2, c, a)
        point()
    begin()
    sums_e2 = back_conv(scratch.be2, scratch.slope_e2, grad, middle_e, mean_e2, inv_e2)
    gain_row, bias_row = table_rows(LATE + 24, sums_e2, gain_e2, bias_e2, 1.0 + enc_scale)
    small_row(LATE + 18, gain_row)
    small_row(LATE + 19, bias_row)
    middle_grad(middle_e, mean_e2, inv_e2, gain_e2 * (1.0 + enc_scale), sums_e2)
    point()
    for a in range(3):
        weight_grad(scratch.te1, starts.enc_conv1, c, a)
        point()
        if a:
            begin()
    sums_e1 = back_conv(scratch.be1, scratch.slope_e1, grad, lifted, mean_e1, inv_e1)
    small_row(LATE + 16, column_sum(sums_e1[1]))
    small_row(LATE + 17, column_sum(sums_e1[0]))
    zero, slope = norm_grad(sums_e1, gain_e1, ones16, count16)

    def lifted_grad(h, carry):
        normed = (lifted[row_at(h), :] - mean_e1) * inv_e1
        value = inv_e1 * (grad[row_at(h), :] * gain_e1 - zero - normed * slope)
        grad[row_at(h), :] = grad_encoded[row_at(h), :] + value
        return carry

    grid_rows(lifted_grad)
    point()

    late_at = small_at + LATE
    sums[late_at : late_at + 16, :] = dot_three(fields[...], grad[...])
    sums[late_at + 20 : late_at + 24, :] = jnp.zeros((4, c), F32)
    point()
    begin()
    back = dot_three(lift[...], grad[...], NT)
    frames_out = scratch.frames_out
    for source in range(line):
        for k in range(strip):
            h = source * strip + k
            value = back[0:history, h * width : (h + 1) * width]
            frames_out[source, :, k, :] = value * keep * masks[h]
    frames_here[row] = frames_out[row]
    for k in range(1, line):
        to = lax.rem(row + k, line)
        output_copies.append(
            send(frames_out.at[to], frames_here.at[row], device_at(to))
        )

    output_swap.arrive()
    own_output = pltpu.make_async_copy(output_here, outputs.output, local_sem.at[10])
    own_output.start()
    for k in REST:
        advance(k)
    assert not due and all(exchange.done() for exchange in exchanges)

    for copy in output_copies:
        copy.wait_recv()
    own_frames = pltpu.make_async_copy(
        frames_here, outputs.frames_grad, local_sem.at[11 + len(runs)]
    )
    own_frames.start()
    own_output.wait()
    own_frames.wait()
    for copy in frame_copies + output_copies:
        copy.wait_send()
    cot_swap.sent()
    output_swap.sent()
    for exchange in exchanges:
        for copy, only in exchange.copies:
            if only is None:
                copy.wait_send()
            else:
                pl.when(only)(copy.wait_send)


def write_kernel(layout, *refs):
    shapes, starts, small_at = layout
    output, frames_grad, gradients_here = refs[:3]
    outputs = refs[3:-3]
    output_here, frames_here, sem = refs[-3:]
    c = gradients_here.shape[1]
    arriving = [
        pltpu.make_async_copy(output, output_here, sem.at[0]),
        pltpu.make_async_copy(frames_grad, frames_here, sem.at[1]),
    ]
    for copy in arriving:
        copy.start()
    leaving = []

    def leave(source, target):
        leaving.append(pltpu.make_async_copy(source, target, sem.at[2 + len(leaving)]))
        leaving[-1].start()

    for k, name in enumerate(LARGE):
        rows = pl.ds(starts[name], shapes[name][0])
        leave(gradients_here.at[rows], outputs[2 + k])
    for target, (k, rows) in zip(outputs[2 + len(LARGE) :], SMALL_ROWS.values()):
        at = small_at + k
        if rows == 8:
            for s in range(target.shape[0]):
                target[s : s + 1, 0:c] = gradients_here[at + 2 * s : at + 2 * s + 1, :]
                target[s : s + 1, c : 2 * c] = gradients_here[at + 2 * s + 1 : at + 2 * s + 2, :]
        else:
            target[...] = gradients_here[at : at + rows, :]
    for copy, source, target in zip(arriving, (output_here, frames_here), outputs[:2]):
        copy.wait()
        leave(source, target)
    for copy in leaving:
        copy.wait()


def whole_items(shape, *arguments):
    line = shape["rows"]
    whole = Given(*arguments)
    given = whole._asdict()
    frames, cotangent = whole.frames, whole.cotangent
    items, history, strip, width = frames.shape
    c = cotangent.shape[-1]
    cells = strip * line * width
    flat = {}
    for name, value in given.items():
        if value is cotangent:
            value = value.reshape(items, strip * width, c)
        elif name in LARGE:
            value = value.reshape(-1, c)
        elif value.ndim == 1 and name not in IN_SMEM:
            value = value.reshape(-1, c)
        flat[name] = value
    shapes = {name: flat[name].shape for name in LARGE}
    big_layout = layout_of(SimpleNamespace(**shapes))
    starts, small_at, total_rows, runs = big_layout
    copies = 20 + 3 * (line - 1) + len(runs) * (6 + 2 * PIECES + 2 * (line - 1)) + 6
    landing = sum(rows // 2 + 5 * rows // 8 for _, rows in runs) + LATE_COUNT * (8 + line)
    shifted = pltpu.VMEM((cells + 2 * width, 6 * c), BF16)
    forward = pltpu.VMEM((18 * c, 2 * c), BF16)
    backward = forward
    field = pltpu.VMEM((cells, c), F32)
    flipped_field = pltpu.VMEM((2 * c, cells), BF16)
    quarter = cells // 4
    scratch = dict(
        small=pltpu.VMEM((LATE_COUNT, c), F32),
        send=pltpu.SemaphoreType.DMA((copies,)),
        recv=pltpu.SemaphoreType.DMA((copies,)),
        local=pltpu.SemaphoreType.DMA((12 + len(runs),)),
        sums=pltpu.VMEM((total_rows, c), F32),
        landing=pltpu.VMEM((landing, c), F32),
        frames_in=pltpu.VMEM((line, history, strip, width), F32),
        mask_in=pltpu.VMEM((line, strip, width), jnp.int32),
        frames_out=pltpu.VMEM((line, history, strip, width), F32),
        frames_from=pltpu.VMEM((line, history, strip, width), F32),
        frames_here=pltpu.VMEM((line, history, strip, width), F32),
        mask_from=pltpu.VMEM((line, strip, width), jnp.int32),
        cot_from=pltpu.VMEM((items, strip * width, c), F32),
        output_here=pltpu.VMEM((items, strip * width, c), F32),
        cot_inward=pltpu.VMEM((2, strip * width, c), F32),
        cot_across=pltpu.VMEM((2, strip * width, c), F32),
        output_inward=pltpu.VMEM((2, strip * width, c), F32),
        output_across=pltpu.VMEM((2, strip * width, c), F32),
        fields=pltpu.VMEM((16, cells), F32),
        lift=pltpu.VMEM((16, c), F32),
        joined=pltpu.VMEM((cells, 4 * c), BF16),
        x_down=pltpu.VMEM((quarter, 8 * c), BF16),
        x_grad_up=pltpu.VMEM((quarter, 8 * c), BF16),
        x_up=pltpu.VMEM((quarter, 2 * c), BF16),
        x_grad_low=pltpu.VMEM((quarter, 2 * c), BF16),
        f_down=pltpu.VMEM((8 * c, 2 * c), BF16),
        b_down=pltpu.VMEM((4, 2 * c, 2 * c), BF16),
        f_up=pltpu.VMEM((4, 2 * c, 2 * c), BF16),
        b_up=pltpu.VMEM((8 * c, 2 * c), BF16),
        f_skip=pltpu.VMEM((4 * c, 2 * c), BF16),
        b_skip=pltpu.VMEM((2, 2 * c, 2 * c), BF16),
        xe1=shifted,
        xe2=shifted,
        xd1a=shifted,
        xd1b=shifted,
        xd2=shifted,
        xg=shifted,
        te1=flipped_field,
        te2=flipped_field,
        td1=pltpu.VMEM((4 * c, cells), BF16),
        td2=flipped_field,
        turned=pltpu.VMEM((4 * c, cells), BF16),
        fe1=forward,
        fe2=forward,
        fd1a=forward,
        fd1b=forward,
        fd2=forward,
        be1=backward,
        be2=backward,
        bd1a=backward,
        bd1b=backward,
        bd2=backward,
        slope_e1=field,
        slope_e2=field,
        slope_d1a=field,
        slope_d1b=field,
        slope_d2=field,
        lifted=field,
        middle_e=field,
        encoded=field,
        raised=field,
        middle_d=field,
        result=field,
        cot=field,
        grad=field,
        grad_a=field,
        grad_b=field,
    )
    scratch.update({name: pltpu.VMEM(shapes[name], F32) for name in LARGE})

    in_hbm = pl.BlockSpec(memory_space=pl.ANY)
    in_vmem = pl.BlockSpec(memory_space=pltpu.VMEM)
    in_smem = pl.BlockSpec(memory_space=pltpu.SMEM)
    in_specs = [
        in_hbm if name in IN_HBM else in_smem if name in IN_SMEM else in_vmem
        for name in ARGUMENTS
    ]
    out_shape = [
        jax.ShapeDtypeStruct((items, strip * width, c), F32),
        jax.ShapeDtypeStruct(frames.shape, F32),
        pltpu.VMEM((total_rows, c), F32),
    ]
    out_specs = [in_hbm, in_hbm, in_vmem]
    results = pl.pallas_call(
        functools.partial(
            item_kernel,
            (line, strip, width, shapes, big_layout),
            tuple(scratch),
        ),
        out_shape=out_shape,
        in_specs=in_specs,
        out_specs=out_specs,
        scratch_shapes=list(scratch.values()),
        compiler_params=pltpu.CompilerParams(
            collective_id=0, has_side_effects=True, vmem_limit_bytes=56 * 1024 * 1024
        ),
    )(*[flat[name] for name in ARGUMENTS])
    names = LARGE + tuple(SMALL_ROWS)
    written = pl.pallas_call(
        functools.partial(write_kernel, (shapes, starts, small_at)),
        out_shape=out_shape[:2] + [jax.ShapeDtypeStruct(flat[name].shape, F32) for name in names],
        in_specs=[pl.BlockSpec(memory_space=pltpu.HBM)] * 2 + [in_vmem],
        out_specs=[in_hbm] * (2 + len(LARGE)) + [in_vmem] * len(SMALL_ROWS),
        scratch_shapes=[
            pltpu.VMEM((items, strip * width, c), F32),
            pltpu.VMEM(frames.shape, F32),
            pltpu.SemaphoreType.DMA((4 + len(LARGE),)),
        ],
        compiler_params=pltpu.CompilerParams(vmem_limit_bytes=16 * 1024 * 1024),
    )(*results)
    grads = dict(zip(names, written[2:]))
    ordered = [name for name in ARGUMENTS if name in grads]
    return (written[0].reshape(cotangent.shape), written[1]) + tuple(
        grads[name].reshape(given[name].shape) for name in ordered
    )


def body(shape, *arguments):
    items, _, strip, width = arguments[0].shape
    line = shape["rows"]
    whole = (
        shape["section"] == 2
        and shape["batch"] == 4
        and items == line == 4
        and arguments[-1].shape[-1] == 128
        and (strip * line * width) % CHUNK == 0
    )
    return whole_items(shape, *arguments) if whole else strips_body(*arguments)


def solution(mesh):
    in_specs = (
        P(("section", "batch"), None, "rows", None),
        P(("section", "batch")),
        P(("section", "batch"), "rows", None),
        P(("section", "batch")),
        P(),
        P(),
        P(),
        P(),
        P(),
        P(),
        P(),
        P(),
        P(),
        P(),
        P(),
        P(),
        P(),
        P(),
        P(),
        P(),
        P(),
        P(),
        P(),
        P(),
        P(),
        P(),
        P(),
        P(),
        P(("section", "batch"), "rows", None, None),
    )
    out_specs = (
        P(("section", "batch"), "rows", None, None),
        P(("section", "batch"), None, "rows", None),
        P(),
        P(),
        P(),
        P(),
        P(),
        P(),
        P(),
        P(),
        P(),
        P(),
        P(),
        P(),
        P(),
        P(),
        P(),
        P(),
        P(),
        P(),
        P(),
        P(),
        P(),
        P(),
        P(),
        P(),
    )
    return jax.shard_map(functools.partial(body, mesh.shape), mesh=mesh, in_specs=in_specs, out_specs=out_specs, check_vma=False)
```

```python
import functools
from types import SimpleNamespace
from typing import Any, NamedTuple

import jax
import jax.numpy as jnp
from jax import lax
from jax.experimental import pallas as pl
from jax.experimental.pallas import tpu as pltpu
from jax.sharding import PartitionSpec as P

GROUPS = 8
FIELDS = 3
HIST = 4


EPS = 1e-05
HIGH = lax.Precision.HIGHEST


def extended(cells, sides, width):
    for axis, dim in sides:
        count = lax.axis_size(axis)
        ends = count - 1
        head = lax.slice_in_dim(cells, 0, width, axis=dim)
        tail = lax.slice_in_dim(cells, cells.shape[dim] - width, cells.shape[dim], axis=dim)
        cells = jnp.concatenate(
            [
                lax.ppermute(tail, axis, [(i, (i + 1) % count) for i in range(ends)]),
                cells,
                lax.ppermute(head, axis, [((i + 1) % count, i) for i in range(ends)]),
            ],
            axis=dim,
        )
    return cells


def from_behind(value, axis, steps):
    count = lax.axis_size(axis)
    pairs = [(source, (source + steps) % count) for source in range(count)]
    return lax.ppermute(value, axis, pairs)


def group_view(value_arrays):
    extent = value_arrays.shape
    return value_arrays.reshape(extent[:-1] + (GROUPS, extent[-1] // GROUPS))


def global_sums(value_arrays):
    grouped = group_view(value_arrays)
    flat = grouped.reshape(-1, GROUPS, grouped.shape[-1])
    first_sum = jnp.sum(flat, axis=(0, 2))
    second_sum = jnp.sum(flat * flat, axis=(0, 2))
    return lax.psum((first_sum, second_sum), "rows")


def apply_norm(value_arrays, sum_one, sum_two, norm_gain, norm_bias, total):
    grouped = group_view(value_arrays)
    group_mean = sum_one / total
    variance = sum_two / total - group_mean * group_mean
    inverse = lax.rsqrt(variance + EPS)
    normed = (grouped - group_mean[:, None]) * inverse[:, None]
    return normed.reshape(value_arrays.shape) * norm_gain + norm_bias


def norm_back(value_arrays, grad_one, grad_two):
    grouped = group_view(value_arrays)
    extra = grad_one[:, None] + 2.0 * grouped * grad_two[:, None]
    return extra.reshape(value_arrays.shape)


def reduce_grads(grad_one, grad_two):
    return lax.psum((grad_one, grad_two), "rows")


def conv_rows(padded, kernel):
    widened = jnp.pad(padded, ((0, 0), (1, 1), (0, 0)))
    return lax.conv_general_dilated(
        widened[None],
        kernel,
        (1, 1),
        "VALID",
        dimension_numbers=("NHWC", "HWIO", "NHWC"),
        precision=HIGH,
    )[0]


def flipped(kernel):
    return jnp.transpose(kernel[::-1, ::-1], (0, 1, 3, 2))


def pad_grads(value_arrays):
    return extended(value_arrays, (("rows", 0),), 1)


def totals_of(inputs, conv1):
    strip = inputs.shape[0]
    cells = strip * lax.axis_size("rows") * inputs.shape[1]
    return (cells * (inputs.shape[2] // GROUPS), cells * (conv1.shape[3] // GROUPS))


def block_forward(inputs, weights, scale_part, shift_part):
    norm1_gain, norm1_bias, conv1, norm2_gain, norm2_bias, conv2, conv2_bias = weights
    total_in, total_mid = totals_of(inputs, conv1)
    sums_in = global_sums(inputs)

    def pad_rows(value_arrays):
        return extended(value_arrays, (("rows", 0),), 1)

    act_one = pad_rows(
        jax.nn.gelu(
            apply_norm(inputs, sums_in[0], sums_in[1], norm1_gain, norm1_bias, total_in),
            approximate=False,
        )
    )
    middle = conv_rows(act_one, conv1)
    sums_mid = global_sums(middle)
    shaped = (
        apply_norm(middle, sums_mid[0], sums_mid[1], norm2_gain, norm2_bias, total_mid)
        * (1.0 + scale_part)
        + shift_part
    )
    act_two = pad_rows(jax.nn.gelu(shaped, approximate=False))
    branch = conv_rows(act_two, conv2) + conv2_bias
    return (branch, (sums_in[0], sums_in[1], act_one, middle, sums_mid[0], sums_mid[1], act_two))


def block_backward(inputs, weights, scale_part, shift_part, kept, grad_out):
    norm1_gain, norm1_bias, conv1, norm2_gain, norm2_bias, conv2, conv2_bias = weights
    in_one, in_two, act_one, middle, mid_one, mid_two, act_two = kept
    total_in, total_mid = totals_of(inputs, conv1)
    grad_conv2 = jax.vjp(lambda kernel: conv_rows(act_two, kernel), conv2)[1](grad_out)[0]
    grad_bias2 = jnp.sum(grad_out, axis=(0, 1))
    grad_act_two = conv_rows(pad_grads(grad_out), flipped(conv2))

    def second_piece(middle_in, sum_one, sum_two, gain_in, incoming_bias, scale_in, shift_in):
        shaped = (
            apply_norm(middle_in, sum_one, sum_two, gain_in, incoming_bias, total_mid)
            * (1.0 + scale_in)
            + shift_in
        )
        return jax.nn.gelu(shaped, approximate=False)

    second_pull = jax.vjp(
        second_piece, middle, mid_one, mid_two, norm2_gain, norm2_bias, scale_part, shift_part
    )[1](grad_act_two)
    summed_one, summed_two = reduce_grads(second_pull[1], second_pull[2])
    grad_middle = second_pull[0] + norm_back(middle, summed_one, summed_two)
    grad_conv1 = jax.vjp(lambda kernel: conv_rows(act_one, kernel), conv1)[1](grad_middle)[0]
    grad_act_one = conv_rows(pad_grads(grad_middle), flipped(conv1))

    def first_piece(inputs_in, sum_one, sum_two, gain_in, incoming_bias):
        return jax.nn.gelu(
            apply_norm(inputs_in, sum_one, sum_two, gain_in, incoming_bias, total_in),
            approximate=False,
        )

    first_pull = jax.vjp(first_piece, inputs, in_one, in_two, norm1_gain, norm1_bias)[1](
        grad_act_one
    )
    first_one, first_two = reduce_grads(first_pull[1], first_pull[2])
    grad_inputs = first_pull[0] + norm_back(inputs, first_one, first_two)
    grads = (
        first_pull[3],
        first_pull[4],
        grad_conv1,
        second_pull[3],
        second_pull[4],
        grad_conv2,
        grad_bias2,
    )
    return (grad_inputs, grads, second_pull[5], second_pull[6])


def conditioning(step_item, table):
    one_hot = (jnp.arange(table.shape[0], dtype=jnp.int32) == step_item).astype(jnp.float32)
    condition = jnp.dot(one_hot, table, precision=HIGH)
    half_width = table.shape[1] // 2
    return (condition[:half_width], condition[half_width:], one_hot)


def project_in(frames_item, mask_item, count_item, incoming_weight, incoming_bias):
    history = jnp.arange(HIST, dtype=jnp.int32) >= HIST - count_item
    keep = jnp.repeat(history, FIELDS).astype(jnp.float32)
    lifted = (
        jnp.einsum(
            "fhw,fc->hwc", frames_item * keep[:, None, None], incoming_weight, precision=HIGH
        )
        + incoming_bias
    )
    return lifted * mask_item[:, :, None].astype(jnp.float32)


def coarsen_field(value_arrays, incoming_weight, incoming_bias):
    rows_here, width_here, depth_here = value_arrays.shape
    blocks = value_arrays.reshape(rows_here // 2, 2, width_here // 2, 2, depth_here)
    return jnp.einsum("iajbk,abkc->ijc", blocks, incoming_weight, precision=HIGH) + incoming_bias


def upsample(value_arrays, incoming_weight, incoming_bias):
    result = jnp.einsum("ijk,abkc->iajbc", value_arrays, incoming_weight, precision=HIGH)
    extent = result.shape
    return result.reshape(extent[0] * 2, extent[2] * 2, extent[4]) + incoming_bias


def flatten_all(pieces):
    return jnp.concatenate([piece.reshape(-1) for piece in pieces])


def unflatten_all(flat, templates):
    pieces = []
    offset_at = 0
    for template in templates:
        count_here = template.size
        pieces.append(flat[offset_at : offset_at + count_here].reshape(template.shape))
        offset_at += count_here
    return tuple(pieces)


def strips_body(
    frames,
    counts,
    cell_mask,
    step_index,
    lift_weight,
    lift_bias,
    enc_norm1_gain,
    enc_norm1_bias,
    enc_conv1,
    enc_step_table,
    enc_norm2_gain,
    enc_norm2_bias,
    enc_conv2,
    enc_conv2_bias,
    reducer_weight,
    reducer_bias,
    up_weight,
    up_bias,
    dec_norm1_gain,
    dec_norm1_bias,
    dec_conv1,
    dec_step_table,
    dec_norm2_gain,
    dec_norm2_bias,
    dec_conv2,
    dec_conv2_bias,
    skip_weight,
    skip_bias,
    cotangent,
):
    enc_weights = (
        enc_norm1_gain,
        enc_norm1_bias,
        enc_conv1,
        enc_norm2_gain,
        enc_norm2_bias,
        enc_conv2,
        enc_conv2_bias,
    )
    dec_weights = (
        dec_norm1_gain,
        dec_norm1_bias,
        dec_conv1,
        dec_norm2_gain,
        dec_norm2_bias,
        dec_conv2,
        dec_conv2_bias,
    )
    params = (
        lift_weight,
        lift_bias,
        enc_norm1_gain,
        enc_norm1_bias,
        enc_conv1,
        enc_step_table,
        enc_norm2_gain,
        enc_norm2_bias,
        enc_conv2,
        enc_conv2_bias,
        reducer_weight,
        reducer_bias,
        up_weight,
        up_bias,
        dec_norm1_gain,
        dec_norm1_bias,
        dec_conv1,
        dec_step_table,
        dec_norm2_gain,
        dec_norm2_bias,
        dec_conv2,
        dec_conv2_bias,
        skip_weight,
        skip_bias,
    )

    def forward_micro(carry, sliced):
        frames_item, mask_item, count_item, step_item = sliced
        lifted = project_in(frames_item, mask_item, count_item, lift_weight, lift_bias)
        enc_scale, enc_shift, unused_hot = conditioning(step_item, enc_step_table)
        enc_branch, enc_kept = block_forward(lifted, enc_weights, enc_scale, enc_shift)
        encoder_result = lifted + enc_branch
        coarse_field = coarsen_field(encoder_result, reducer_weight, reducer_bias)
        foreign = from_behind(coarse_field, "section", 1)
        raised_foreign = upsample(foreign, up_weight, up_bias)
        raised = from_behind(raised_foreign, "section", 1)
        joined = jnp.concatenate([raised, encoder_result], axis=-1)
        dec_scale, dec_shift, unused_again = conditioning(step_item, dec_step_table)
        dec_branch, dec_kept = block_forward(joined, dec_weights, dec_scale, dec_shift)
        output_item = jnp.dot(joined, skip_weight, precision=HIGH) + skip_bias + dec_branch
        return (carry, (output_item, (lifted, enc_kept, encoder_result, foreign, joined, dec_kept)))

    unused, (output, kept_all) = lax.scan(
        forward_micro, jnp.zeros((), jnp.float32), (frames, cell_mask, counts, step_index)
    )

    def backward_micro(totals, sliced):
        frames_item, mask_item, count_item, step_item, grad_out, kept = sliced
        lifted, enc_kept, encoder_result, foreign, joined, dec_kept = kept
        dec_scale, dec_shift, one_hot = conditioning(step_item, dec_step_table)
        grad_joined, dec_grads, dec_gscale, dec_gshift = block_backward(
            joined, dec_weights, dec_scale, dec_shift, dec_kept, grad_out
        )
        grad_skip_weight = jnp.einsum("hwk,hwc->kc", joined, grad_out, precision=HIGH)
        grad_skip_bias = jnp.sum(grad_out, axis=(0, 1))
        grad_joined = grad_joined + jnp.dot(grad_out, skip_weight.T, precision=HIGH)
        half_width = joined.shape[-1] // 2
        grad_raised = grad_joined[..., :half_width]
        grad_encoded = grad_joined[..., half_width:]
        grad_foreign_up = from_behind(grad_raised, "section", 1)
        up_pull = jax.vjp(upsample, foreign, up_weight, up_bias)[1](grad_foreign_up)
        coarse_gradient = from_behind(up_pull[0], "section", 1)
        reducer_pullback = jax.vjp(coarsen_field, encoder_result, reducer_weight, reducer_bias)[1](
            coarse_gradient
        )
        grad_encoded = grad_encoded + reducer_pullback[0]
        enc_scale, enc_shift, enc_hot = conditioning(step_item, enc_step_table)
        grad_lifted, enc_grads, enc_gscale, enc_gshift = block_backward(
            lifted, enc_weights, enc_scale, enc_shift, enc_kept, grad_encoded
        )
        grad_lifted = grad_lifted + grad_encoded
        proj_pull = jax.vjp(
            lambda frames_in, incoming_weight, incoming_bias: project_in(
                frames_in, mask_item, count_item, incoming_weight, incoming_bias
            ),
            frames_item,
            lift_weight,
            lift_bias,
        )[1](grad_lifted)
        enc_table_grad = enc_hot[:, None] * jnp.concatenate([enc_gscale, enc_gshift])[None, :]
        dec_table_grad = one_hot[:, None] * jnp.concatenate([dec_gscale, dec_gshift])[None, :]
        micro_list = (
            proj_pull[1],
            proj_pull[2],
            enc_grads[0],
            enc_grads[1],
            enc_grads[2],
            enc_table_grad,
            enc_grads[3],
            enc_grads[4],
            enc_grads[5],
            enc_grads[6],
            reducer_pullback[1],
            reducer_pullback[2],
            up_pull[1],
            up_pull[2],
            dec_grads[0],
            dec_grads[1],
            dec_grads[2],
            dec_table_grad,
            dec_grads[3],
            dec_grads[4],
            dec_grads[5],
            dec_grads[6],
            grad_skip_weight,
            grad_skip_bias,
        )
        micro_flat = flatten_all(micro_list)
        return (totals + micro_flat, proj_pull[0])

    total_size = sum((piece.size for piece in params))
    start_totals = jnp.zeros((total_size,), jnp.float32)
    flat_totals, frames_grad = lax.scan(
        backward_micro,
        start_totals,
        (frames, cell_mask, counts, step_index, cotangent, kept_all),
        reverse=True,
    )
    flat_totals = lax.psum(flat_totals, ("section", "batch", "rows"))
    grads = unflatten_all(flat_totals, params)
    return (output, frames_grad) + grads


F32 = jnp.float32
BF16 = jnp.bfloat16
MESH = pl.DeviceIdType.MESH
NN = ((1,), (0,))
NT = ((1,), (1,))
TN = ((0,), (0,))
HIGH_AT = (0, 2, 1)
LOW_AT = (4, 3, 5)
CHUNK = 512
class Given(NamedTuple):
    frames: Any
    counts: Any
    cell_mask: Any
    step_index: Any
    lift_weight: Any
    lift_bias: Any
    enc_norm1_gain: Any
    enc_norm1_bias: Any
    enc_conv1: Any
    enc_step_table: Any
    enc_norm2_gain: Any
    enc_norm2_bias: Any
    enc_conv2: Any
    enc_conv2_bias: Any
    reducer_weight: Any
    reducer_bias: Any
    up_weight: Any
    up_bias: Any
    dec_norm1_gain: Any
    dec_norm1_bias: Any
    dec_conv1: Any
    dec_step_table: Any
    dec_norm2_gain: Any
    dec_norm2_bias: Any
    dec_conv2: Any
    dec_conv2_bias: Any
    skip_weight: Any
    skip_bias: Any
    cotangent: Any


ARGUMENTS = Given._fields
LARGE = tuple(
    dict(
        dec_conv1=0,
        up_weight=0,
        reducer_weight=0,
        dec_conv2=0,
        skip_weight=0,
        enc_conv1=0,
        enc_conv2=0,
    )
)
IN_HBM = tuple(dict(frames=0, cell_mask=0, cotangent=0)) + LARGE
IN_SMEM = tuple(dict(counts=0, step_index=0))
LATE = 64
SMALL_ROWS = dict(
    enc_conv2_bias=(0, 1),
    reducer_bias=(1, 1),
    up_bias=(2, 1),
    dec_conv2_bias=(3, 1),
    skip_bias=(3, 1),
    dec_norm1_gain=(4, 2),
    dec_norm1_bias=(6, 2),
    dec_norm2_gain=(8, 1),
    dec_norm2_bias=(9, 1),
    dec_step_table=(16, 8),
    lift_weight=(LATE, 12),
    lift_bias=(LATE + 12, 1),
    enc_norm1_gain=(LATE + 16, 1),
    enc_norm1_bias=(LATE + 17, 1),
    enc_norm2_gain=(LATE + 18, 1),
    enc_norm2_bias=(LATE + 19, 1),
    enc_step_table=(LATE + 24, 8),
)
LATE_COUNT = 32
PIECES = 1
SMALL_COUNT = LATE + LATE_COUNT
DUE = ((), (), (), (), (), (0,), (), (1,), (), (), (2,), (3, 0), (), (), (1,), (), (), (2,), (0,), (1, 4, 3), (2,), (), (), (5, 0), (1, 3), (4, 2), (), (6,), (7, 3, 0, 5, 4, 1, 2))
REST = (6, 3, 7, 4, 5, 6, 8, 7, 0, 4, 5, 1, 6, 7, 2, 0, 1, 5, 3, 6, 2, 8, 7, 3, 4, 5, 4, 6, 7, 5, 6, 7)
OUTPUTS = tuple(dict(output=0, frames_grad=0, gradients=0))


def split(value):
    high = value.astype(BF16)
    return high, (value - high.astype(F32)).astype(BF16)


def dot(left, right, dims=NN, precision=None):
    return lax.dot_general(
        left, right, (dims, ((), ())), precision=precision, preferred_element_type=F32
    )


def fold(value):
    half = value.shape[1] // 2
    return value[:, :half] + value[:, half:]


def fold_rows(value):
    half = value.shape[0] // 2
    return value[:half] + value[half:]


def tile_sums(value):
    return jnp.sum(value.reshape(-1, 8, value.shape[-1]), axis=0)


def column_sum(tiles):
    return jnp.sum(tiles, axis=0, keepdims=True)


def normal(value):
    bell = jnp.exp(-0.5 * value * value)
    t = 1.0 / (1.0 + 0.2316418882663604 * jnp.abs(value))
    poly = 0.5307027145
    for factor in (-0.7265760135, 0.7107068705, -0.142248368, 0.127414796):
        poly = poly * t + factor
    tail = poly * t * bell
    return jnp.where(value < 0.0, tail, 1.0 - tail), 0.3989422804014327 * bell


def dot_three(left, right, dims=NN):
    left_high, left_low = split(left)
    right_high, right_low = split(right)
    total = dot(left_high, right_high, dims)
    return total + (dot(left_high, right_low, dims) + dot(left_low, right_high, dims))


def group_ones(channels, size):
    rows = lax.broadcasted_iota(jnp.int32, (channels, channels), 0) // size
    columns = lax.broadcasted_iota(jnp.int32, (channels, channels), 1) // size
    return (rows == columns).astype(BF16)


def group_sums(first, second, ones):
    terms = []
    rest = jnp.concatenate([first, second], axis=0)
    for _ in range(3):
        term = rest.astype(BF16)
        terms.append(term)
        rest = rest - term.astype(F32)
    both = dot(jnp.concatenate(terms, axis=0), ones)
    both = both[32:48] + both[16:32] + both[:16]
    return column_sum(both[:8]), column_sum(both[8:])


class LineSwap:

    def __init__(self, line, source, target, inward, across, make):
        far = 3 - line.outer
        self.line = line
        to_inner, to_across = line.device(line.inner), line.device(line.across)
        to_outer = line.device(line.outer)
        here = target(line.here)
        self.to_far = make(source(3 - line.here), inward.at[1], to_inner)
        self.to_second = make(source(3 - line.inner), inward.at[0], to_inner)
        self.to_inner = make(source(line.inner), here, to_inner)
        self.for_far = make(source(far), across.at[0], to_across)
        self.to_across = make(source(line.across), here, to_across)
        self.to_outer = make(source(line.outer), here, to_outer)
        self.pass_far = make(inward.at[1], across.at[1], to_across)
        self.pass_second = make(inward.at[0], target(line.outer), to_across)
        self.pass_across = make(across.at[0], target(line.across), to_outer)
        self.pass_opposite = make(across.at[1], target(far), to_outer)

    def first(self):
        @pl.when(self.line.edge)
        def _():
            for copy in (self.to_far, self.to_second, self.to_inner):
                copy.start()

        @pl.when(self.line.middle)
        def _():
            for copy in (self.for_far, self.to_across, self.to_outer):
                copy.start()

    def second(self):
        @pl.when(self.line.middle)
        def _():
            self.for_far.wait_recv()
            self.pass_across.start()
            self.to_far.wait_recv()
            self.pass_far.start()
            self.to_second.wait_recv()
            self.pass_second.start()

    def third(self):
        @pl.when(self.line.middle)
        def _():
            self.pass_far.wait_recv()
            self.pass_opposite.start()

    def arrive(self):
        @pl.when(self.line.edge)
        def _():
            for copy in (self.to_outer, self.pass_across, self.pass_opposite):
                copy.wait_recv()

        @pl.when(self.line.middle)
        def _():
            for copy in (self.to_inner, self.to_across, self.pass_second):
                copy.wait_recv()

    def sent(self):
        @pl.when(self.line.edge)
        def _():
            for copy in (self.to_far, self.to_second, self.to_inner):
                copy.wait_send()

        @pl.when(self.line.middle)
        def _():
            for copy in (self.for_far, self.to_across, self.to_outer):
                copy.wait_send()
            for copy in (self.pass_far, self.pass_second, self.pass_across, self.pass_opposite):
                copy.wait_send()


class Exchange:

    def __init__(self, place, start, rows, landing, first_sem):
        self.place, self.start, self.rows, self.landing = place, start, rows, landing
        self.sem = first_sem
        self.stage = 0
        self.copies = []
        self.waiting = []
        self.group = place.plane_group
        self.half = rows // 2
        self.base = start + place.core * self.half
        self._finish(self.half)

    def _finish(self, size):
        self.part = size // self.group.count
        self.own = self.base + self.group.here * self.part

    def count(self):
        return 2 * PIECES + 2 * (self.group.count - 1) + 3

    def land_rows(self):
        return self.half + (self.group.count + 1) * self.part

    def _copy(self, source, target, device, only=None):
        place = self.place
        copy = pltpu.make_async_remote_copy(
            src_ref=source,
            dst_ref=target,
            send_sem=place.send.at[self.sem],
            recv_sem=place.recv.at[self.sem],
            device_id=device,
            device_id_type=MESH,
        )
        self.sem += 1
        if only is None:
            copy.start()
            self.waiting.append(copy)
        self.copies.append((copy, only))
        return copy

    def _pieces(self, source, at, target, to, size, device):
        each = size // 8 // PIECES * 8
        for k in range(PIECES):
            here = each if k < PIECES - 1 else size - each * (PIECES - 1)
            self._copy(
                source.at[self._rows(at + k * each, here)],
                target.at[self._rows(to + k * each, here)],
                device,
            )

    def _wait(self):
        for copy in self.waiting:
            copy.wait_recv()
        self.waiting = []

    def _rows(self, at, size):
        return pl.ds(pl.multiple_of(at, 8), size)

    def _swap(self):
        place = self.place
        other = self.start + (1 - place.core) * self.half
        self.land = self.landing
        self.landing += self.half
        self._pieces(place.sums, other, place.landing, self.land, self.half, place.partner)

    def _add_swap(self):
        place = self.place
        block = 64 if self.half % 64 == 0 else 32

        def step(i, carry):
            here = self._rows(self.base + i * block, block)
            there = self._rows(self.land + i * block, block)
            place.sums[here] = place.sums[here] + place.landing[there]
            return carry

        lax.fori_loop(0, self.half // block, step, 0)

    def _scatter(self, group, base, size):
        place = self.place
        self.land = self.landing
        for k in range(1, group.count):
            to = lax.rem(group.here + k, group.count)
            self._copy(
                place.sums.at[self._rows(base + to * size, size)],
                place.landing.at[pl.ds(self.landing, size)],
                group.device(to),
            )
            self.landing += size

    def _total(self, group, own, size, target):
        place = self.place
        block = 16 if size % 16 == 0 else 8

        def step(i, carry):
            here = self._rows(own + i * block, block)
            total = place.sums[here]
            for k in range(group.count - 1):
                there = self._rows(self.land + k * size + i * block, block)
                total = total + place.landing[there]
            target[here] = total
            return carry

        lax.fori_loop(0, size // block, step, 0)

    def _gather(self, group, own, size):
        final = self.place.final
        here = self._rows(own, size)
        for k in range(1, group.count):
            to = lax.rem(group.here + k, group.count)
            self._copy(final.at[here], final.at[here], group.device(to))

    def _steps(self):
        place, group = self.place, self.group
        yield self._swap()
        self._wait()
        self._add_swap()
        yield from self._both()
        self._pieces(place.final, self.base, place.final, self.base, self.half, place.partner)
        yield
        self._wait()
        yield

    def _both(self):
        place, group = self.place, self.group
        self._scatter(group, self.base, self.part)
        yield
        self._wait()
        self._total(group, self.own, self.part, place.sums)
        yield from self._line()
        self._gather(group, self.own, self.part)
        yield
        self._wait()

    def _line(self):
        place, line = self.place, self.place.line
        sums, final, landing = place.sums, place.final, place.landing
        part, own = self.part, self._rows(self.own, self.part)
        inward, across = pl.ds(self.landing, part), pl.ds(self.landing + part, part)
        self.landing += 2 * part
        block = 16 if part % 16 == 0 else 8

        def add(at, target):
            def step(i, carry):
                here = self._rows(self.own + i * block, block)
                target[here] = sums[here] + landing[pl.ds(at + i * block, block)]
                return carry

            lax.fori_loop(0, part // block, step, 0)

        first = self._copy(sums.at[own], landing.at[inward], line.device(line.inner), line.edge)
        second = self._copy(sums.at[own], landing.at[across], line.device(line.across), line.middle)
        third = self._copy(final.at[own], final.at[own], line.device(line.outer), line.middle)
        pl.when(line.edge)(first.start)
        yield

        @pl.when(line.middle)
        def _():
            first.wait_recv()
            add(self.landing - 2 * part, sums)
            second.start()

        yield

        @pl.when(line.middle)
        def _():
            second.wait_recv()
            add(self.landing - part, final)
            third.start()

        yield
        pl.when(line.edge)(third.wait_recv)

    def advance(self):
        if self.stage == 0:
            self.steps = self._steps()
        self.stage += 1
        next(self.steps)

    def done(self):
        return self.stage == 8


class SmallExchange(Exchange):

    def count(self):
        return self.place.cores_group.count + self.place.line.count - 2

    def land_rows(self):
        return self.rows * (self.place.cores_group.count + self.place.line.count)

    def _share(self, group, source):
        place = self.place
        self.land = self.landing
        self.landing += group.count * self.rows
        own = self._rows(self.land + group.here * self.rows, self.rows)
        place.landing[own] = source[...]
        for k in range(1, group.count):
            to = lax.rem(group.here + k, group.count)
            self._copy(source, place.landing.at[own], group.device(to))

    def _sum(self, group):
        total = None
        for k in range(group.count):
            part = self.place.landing[pl.ds(self.land + k * self.rows, self.rows)]
            total = part if total is None else total + part
        return total

    def _steps(self):
        place = self.place
        here = pl.ds(self.start, self.rows)
        self._share(place.line, place.sums.at[here])
        yield
        self._wait()
        place.small[...] = self._sum(place.line)
        self._share(place.cores_group, place.small)
        yield
        self._wait()
        place.final[here] = self._sum(place.cores_group)
        yield

    def done(self):
        return self.stage == 3


def layout_of(shapes):
    starts = {}
    at = 0
    for name in LARGE:
        starts[name] = at
        at += getattr(shapes, name)[0]
    small = at
    begins = SimpleNamespace(**starts)
    late = small + LATE
    tap = shapes.dec_conv2[0] // 3
    part = shapes.dec_conv1[0] // 3
    conv1, up = begins.dec_conv1, begins.up_weight
    edges = (
        (begins.dec_conv2, begins.enc_conv1),
        (conv1, conv1 + part),
        (conv1 + part, conv1 + 2 * part),
        (conv1 + 2 * part, up),
        (up, begins.dec_conv2),
        (begins.enc_conv2, late),
        (begins.enc_conv1, begins.enc_conv1 + 2 * tap),
        (begins.enc_conv1 + 2 * tap, begins.enc_conv2),
        (late, late + LATE_COUNT),
    )
    runs = [(first, last - first) for first, last in edges]
    return starts, small, late + LATE_COUNT, runs


def item_kernel(sizes, scratch_names, *refs):
    line, strip, width, shapes, big_layout = sizes
    begins, small_at, total_rows, runs = big_layout
    starts = SimpleNamespace(**begins)
    inputs = Given(*refs[: len(ARGUMENTS)])
    refs = refs[len(ARGUMENTS) :]
    output_names = OUTPUTS
    outputs = SimpleNamespace(**dict(zip(output_names, refs)))
    scratch = SimpleNamespace(**dict(zip(scratch_names, refs[len(output_names) :])))

    def w_of(name):
        return getattr(scratch, name)

    height = strip * line
    cells = height * width
    c = inputs.lift_weight.shape[1]
    strip_cells = strip * width
    history = inputs.frames.shape[1]

    core = lax.axis_index("section")
    plane = lax.axis_index("batch")
    row = lax.axis_index("rows")
    middle = lax.rem(row + 1, 4) // 2

    def device_at(to):
        return (core, plane, to)

    place = SimpleNamespace(
        core=core,
        partner=(1 - core, plane, row),
        line=SimpleNamespace(
            count=line,
            here=row,
            device=device_at,
            middle=middle == 1,
            edge=middle == 0,
            inner=1 + row // 2,
            across=3 - row,
            outer=3 * (row // 2),
        ),
        plane_group=SimpleNamespace(
            count=4, here=plane, device=lambda to: (core, to, row)
        ),
        cores_group=SimpleNamespace(
            count=8,
            here=core * 4 + plane,
            device=lambda to: (to // 4, lax.rem(to, 4), row),
        ),
        small=scratch.small,
        sums=scratch.sums,
        final=outputs.gradients,
        landing=scratch.landing,
        send=scratch.send,
        recv=scratch.recv,
    )
    local_sem = scratch.local

    frames_in, mask_in, cot = scratch.frames_in, scratch.mask_in, scratch.cot
    here_rows = pl.ds(pl.multiple_of(row * strip_cells, strip_cells), strip_cells)
    frames_from, mask_from, cot_from = scratch.frames_from, scratch.mask_from, scratch.cot_from
    staged = (
        pltpu.make_async_copy(inputs.frames, frames_from, local_sem.at[7]),
        pltpu.make_async_copy(inputs.cell_mask, mask_from, local_sem.at[8]),
        pltpu.make_async_copy(inputs.cotangent, cot_from, local_sem.at[9]),
    )
    for copy in staged:
        copy.start()

    weight_copies = {}
    for k, name in enumerate(LARGE):
        copy = pltpu.make_async_copy(getattr(inputs, name), w_of(name), local_sem.at[k])
        weight_copies[name] = copy
        copy.start()

    barrier = pltpu.get_barrier_semaphore()
    peers = [device_at(lax.rem(row + k, line)) for k in range(1, line)]
    cores_group = place.cores_group
    for k in range(1, 8):
        peers.append(cores_group.device(lax.rem(cores_group.here + k, 8)))
    for device in peers:
        pl.semaphore_signal(barrier, inc=1, device_id=device, device_id_type=MESH)
    pl.semaphore_wait(barrier, len(peers))

    next_sem = 0

    def make(source, target, device):
        nonlocal next_sem
        copy = pltpu.make_async_remote_copy(
            src_ref=source,
            dst_ref=target,
            send_sem=scratch.send.at[next_sem],
            recv_sem=scratch.recv.at[next_sem],
            device_id=device,
            device_id_type=MESH,
        )
        next_sem += 1
        return copy

    def send(source, target, device):
        copy = make(source, target, device)
        copy.start()
        return copy

    def strip_of(ref, to):
        return ref.at[pl.ds(pl.multiple_of(to * strip_cells, strip_cells), strip_cells)]

    frame_copies, output_copies = [], []
    for copy in staged[:2]:
        copy.wait()
    for k in range(1, line):
        to = lax.rem(row + k, line)
        device = device_at(to)
        frame_copies.append(send(frames_from.at[to], frames_in.at[row], device))
        frame_copies.append(send(mask_from.at[to], mask_in.at[row], device))
    staged[2].wait()
    cot_swap = LineSwap(
        place.line,
        lambda to: cot_from.at[to],
        lambda source: strip_of(cot, source),
        scratch.cot_inward,
        scratch.cot_across,
        make,
    )
    cot_swap.first()

    copied = SimpleNamespace(**weight_copies)
    def put_pair(target, block, value):
        high, low = split(value)
        rows = slice(block * c, (block + 1) * c)
        target[rows, 0:c] = high
        target[rows, c : 2 * c] = low

    def stack_conv(source, half, depth, forward, backward):
        for a in range(3):
            for b in range(3):
                at = (3 * a + b) * depth + half * c
                value = source[at : at + c, :]
                turned = value.T
                for places in (HIGH_AT, LOW_AT):
                    put_pair(forward, 6 * a + places[b], value)
                    put_pair(backward, 6 * (2 - a) + places[2 - b], turned)

    copied.enc_conv1.wait()
    stack_conv(scratch.enc_conv1, 0, c, scratch.fe1, scratch.be1)
    copied.enc_conv2.wait()
    stack_conv(scratch.enc_conv2, 0, c, scratch.fe2, scratch.be2)
    copied.reducer_weight.wait()
    for k in range(4):
        value = scratch.reducer_weight[k * c : (k + 1) * c, :]
        turned = value.T
        for block in (k, k + 4):
            put_pair(scratch.f_down, block, value)
        for block in (0, 1):
            put_pair(scratch.b_down.at[k], block, turned)
    copied.up_weight.wait()
    for k in range(4):
        value = scratch.up_weight[k * c : (k + 1) * c, :]
        turned = value.T
        for block in (0, 1):
            put_pair(scratch.f_up.at[k], block, value)
        for block in (k, k + 4):
            put_pair(scratch.b_up, block, turned)
    copied.dec_conv1.wait()
    stack_conv(scratch.dec_conv1, 0, 2 * c, scratch.fd1a, scratch.bd1a)
    stack_conv(scratch.dec_conv1, 1, 2 * c, scratch.fd1b, scratch.bd1b)
    copied.dec_conv2.wait()
    stack_conv(scratch.dec_conv2, 0, c, scratch.fd2, scratch.bd2)
    copied.skip_weight.wait()
    for half in range(2):
        value = scratch.skip_weight[half * c : (half + 1) * c, :]
        turned = value.T
        for block in (half, half + 2):
            put_pair(scratch.f_skip, block, value)
        for block in (0, 1):
            put_pair(scratch.b_skip.at[half], block, turned)

    for buffer in (scratch.xe1, scratch.xe2, scratch.xd1a, scratch.xd1b, scratch.xd2, scratch.xg):
        edge = jnp.zeros((width, 6 * c), BF16)
        buffer[0:width, :] = edge
        buffer[cells + width : cells + 2 * width, :] = edge

    lift = scratch.lift
    lift[...] = jnp.zeros(lift.shape, F32)
    lift[0:history, :] = inputs.lift_weight[...]
    lift[history : history + 1, :] = inputs.lift_bias[...]

    block = 2 * width
    column = lax.rem(lax.broadcasted_iota(jnp.int32, (block, c), 0), width)
    at_first, at_last = column == 0, column == width - 1
    zeros8 = jnp.zeros((8, c), F32)
    ones16 = group_ones(c, c // GROUPS)
    ones32 = group_ones(c, 2 * c // GROUPS)
    count16 = float(cells * (c // GROUPS))
    count32 = float(cells * (2 * c // GROUPS))

    def grid_rows(step, carry=0):
        return lax.fori_loop(0, cells // block, step, carry, unroll=2)

    def row_at(h):
        return pl.ds(pl.multiple_of(h * block, block), block)

    def chunk_at(i):
        return pl.ds(pl.multiple_of(i * CHUNK, CHUNK), CHUNK)

    def put_row(target, h, value):
        rows = pl.ds(pl.multiple_of(h * block + width, width), block)
        left = jnp.where(at_first, 0.0, pltpu.roll(value, 1, 0))
        right = jnp.where(at_last, 0.0, pltpu.roll(value, block - 1, 0))
        for b, piece in enumerate((left, value, right)):
            high, low = split(piece)
            target[rows, HIGH_AT[b] * c : (HIGH_AT[b] + 1) * c] = high
            target[rows, LOW_AT[b] * c : (LOW_AT[b] + 1) * c] = low

    def put_turned(target, columns, value, first=0, second=1):
        high, low = split(value.T)
        target[first * c : (first + 1) * c, columns] = high
        target[second * c : (second + 1) * c, columns] = low

    def conv_chunk(pairs, i):
        total = None
        for data, weight in pairs:
            taps = []
            for a in range(3):
                rows = pl.ds(pl.multiple_of(i * CHUNK + a * width, width), CHUNK)
                taps.append(data[rows, :])
            part = dot(jnp.concatenate(taps, axis=1), weight[...])
            total = part if total is None else total + part
        return total

    def norm_of(first, second, ones, count):
        one, two = group_sums(first, second, ones)
        mean = one / count
        return mean, lax.rsqrt(two / count - mean * mean + EPS)

    def activate(source, target, turned, slope, scale, shift):
        def step(h, carry):
            value = source[row_at(h), :] * scale + shift
            below, density = normal(value)
            slope[row_at(h), :] = below + value * density
            value = value * below
            put_row(target, h, value)
            put_turned(turned, row_at(h), value)
            return carry

        grid_rows(step)

    def conv_norm(pairs, target):
        def step(i, carry):
            value = fold(conv_chunk(pairs, i))
            target[chunk_at(i), :] = value
            return carry[0] + tile_sums(value), carry[1] + tile_sums(value * value)

        return lax.fori_loop(0, cells // CHUNK, step, (zeros8, zeros8))

    def sums_of(source):
        def step(h, carry):
            value = source[row_at(h), :]
            return carry[0] + tile_sums(value), carry[1] + tile_sums(value * value)

        return grid_rows(step, (zeros8, zeros8))

    step_here = jnp.full((1, c), inputs.step_index[row], jnp.int32)

    def condition(table):
        total = jnp.zeros((1, 2 * c), F32)
        chosen = jnp.concatenate([step_here, step_here], axis=1)
        for s in range(table.shape[0]):
            total = total + jnp.where(chosen == s, table[s : s + 1, :], 0.0)
        return total[:, :c], total[:, c:]

    frames_in[row] = frames_from[row]
    mask_in[row] = mask_from[row]
    for copy in frame_copies:
        copy.wait_recv()
    fields = scratch.fields
    fields[...] = jnp.zeros(fields.shape, F32)
    frame_of = lax.broadcasted_iota(jnp.int32, (history, width), 0) // FIELDS
    keep = (frame_of >= HIST - inputs.counts[row]).astype(F32)
    masks = []
    for source in range(line):
        for k in range(strip):
            columns = slice((source * strip + k) * width, (source * strip + k + 1) * width)
            mask = mask_in[source, k : k + 1, :].astype(F32)
            masks.append(mask)
            fields[0:history, columns] = frames_in[source, :, k, :] * keep * mask
            fields[history : history + 1, columns] = mask
    lifted = scratch.lifted
    lifted[...] = dot_three(fields[...], lift[...], TN)

    enc_scale, enc_shift = condition(inputs.enc_step_table)
    dec_scale, dec_shift = condition(inputs.dec_step_table)

    mean_e1, inv_e1 = norm_of(*sums_of(lifted), ones16, count16)
    gain_e1, bias_e1 = inputs.enc_norm1_gain[...], inputs.enc_norm1_bias[...]
    a_e1 = inv_e1 * gain_e1
    activate(lifted, scratch.xe1, scratch.te1, scratch.slope_e1, a_e1, bias_e1 - mean_e1 * a_e1)
    middle_e = scratch.middle_e
    mean_e2, inv_e2 = norm_of(
        *conv_norm([(scratch.xe1, scratch.fe1)], middle_e), ones16, count16
    )
    gain_e2, bias_e2 = inputs.enc_norm2_gain[...], inputs.enc_norm2_bias[...]
    a_e2 = inv_e2 * gain_e2
    activate(
        middle_e,
        scratch.xe2,
        scratch.te2,
        scratch.slope_e2,
        a_e2 * (1.0 + enc_scale),
        (bias_e2 - mean_e2 * a_e2) * (1.0 + enc_scale) + enc_shift,
    )
    cot_swap.second()
    encoded = scratch.encoded
    conv2_bias = inputs.enc_conv2_bias[...]
    joined = scratch.joined

    def encode(i, carry):
        value = fold(conv_chunk([(scratch.xe2, scratch.fe2)], i))
        value = value + conv2_bias + lifted[chunk_at(i), :]
        encoded[chunk_at(i), :] = value
        high, low = split(value)
        joined[chunk_at(i), c : 2 * c] = high
        joined[chunk_at(i), 3 * c : 4 * c] = low
        put_turned(scratch.turned, chunk_at(i), value, 1, 3)
        return carry[0] + tile_sums(value), carry[1] + tile_sums(value * value)

    sums_enc = lax.fori_loop(0, cells // CHUNK, encode, (zeros8, zeros8))

    half_cells, quarter = cells // 2, cells // 4

    def pick(source):
        pieces = []
        for b in range(2):
            value = source[pl.ds(b, half_cells, stride=2), :]
            value = value.reshape(height // 2, 2, width // 2, c)
            pieces.append([value[:, a].reshape(quarter, c) for a in range(2)])
        return [pieces[b][a] for a in range(2) for b in range(2)]

    def place_cells(target, pieces):
        for b in range(2):
            both = [pieces[2 * a + b].reshape(height // 2, 1, width // 2, c) for a in range(2)]
            value = jnp.concatenate(both, axis=1).reshape(half_cells, c)
            target[pl.ds(b, half_cells, stride=2), :] = value

    x_down = scratch.x_down
    for k, piece in enumerate(pick(encoded)):
        high, low = split(piece)
        x_down[:, k * c : (k + 1) * c] = high
        x_down[:, (k + 4) * c : (k + 5) * c] = low
    lowered = fold(dot(x_down[...], scratch.f_down[...])) + inputs.reducer_bias[...]
    x_up = scratch.x_up
    high, low = split(lowered)
    x_up[:, 0:c] = high
    x_up[:, c : 2 * c] = low
    raised = scratch.raised
    up_bias = inputs.up_bias[...]
    place_cells(
        raised, [fold(dot(x_up[...], scratch.f_up[k])) + up_bias for k in range(4)]
    )

    def raise_row(h, carry):
        value = raised[row_at(h), :]
        high, low = split(value)
        joined[row_at(h), 0:c] = high
        joined[row_at(h), 2 * c : 3 * c] = low
        put_turned(scratch.turned, row_at(h), value, 0, 2)
        return carry[0] + tile_sums(value), carry[1] + tile_sums(value * value)

    sums_raised = grid_rows(raise_row, (zeros8, zeros8))

    halves = []
    for half, (source, sums) in enumerate(((raised, sums_raised), (encoded, sums_enc))):
        mean, inv = norm_of(*sums, ones32, count32)
        gain = inputs.dec_norm1_gain[half : half + 1, :]
        bias = inputs.dec_norm1_bias[half : half + 1, :]
        scale = inv * gain
        activate(
            source,
            (scratch.xd1a, scratch.xd1b)[half],
            scratch.td1.at[2 * c * half : 2 * c * (half + 1)],
            (scratch.slope_d1a, scratch.slope_d1b)[half],
            scale,
            bias - mean * scale,
        )
        halves.append((source, mean, inv, gain))
    middle_d = scratch.middle_d
    pairs = [(scratch.xd1a, scratch.fd1a), (scratch.xd1b, scratch.fd1b)]
    mean_d2, inv_d2 = norm_of(*conv_norm(pairs, middle_d), ones16, count16)
    cot_swap.third()
    gain_d2, bias_d2 = inputs.dec_norm2_gain[...], inputs.dec_norm2_bias[...]
    a_d2 = inv_d2 * gain_d2
    activate(
        middle_d,
        scratch.xd2,
        scratch.td2,
        scratch.slope_d2,
        a_d2 * (1.0 + dec_scale),
        (bias_d2 - mean_d2 * a_d2) * (1.0 + dec_scale) + dec_shift,
    )
    result = scratch.result
    last_bias = inputs.dec_conv2_bias[...] + inputs.skip_bias[...]

    def decode(i, carry):
        value = conv_chunk([(scratch.xd2, scratch.fd2)], i)
        value = value + dot(joined[chunk_at(i), :], scratch.f_skip[...])
        result[chunk_at(i), :] = fold(value) + last_bias
        return carry

    lax.fori_loop(0, cells // CHUNK, decode, 0)
    output_here, frames_here = outputs.output, outputs.frames_grad
    output_here[row] = result[here_rows]
    output_swap = LineSwap(
        place.line,
        lambda to: strip_of(result, to),
        lambda source: output_here.at[source],
        scratch.output_inward,
        scratch.output_across,
        make,
    )
    output_swap.first()

    exchanges = []
    waiting_runs = list(runs)
    landing_at = 0
    sem_at = 3 * (line - 1) + 20
    sums = scratch.sums

    def begin():
        nonlocal landing_at, sem_at
        start, rows = waiting_runs.pop(0)
        kind = Exchange if waiting_runs else SmallExchange
        exchange = kind(place, start, rows, landing_at, sem_at)
        landing_at += exchange.land_rows()
        sem_at += exchange.count()
        exchanges.append(exchange)
        exchange.advance()

    def advance(k):
        exchange = exchanges[k]
        exchange.advance()

    due = list(DUE)

    def point():
        for k in due.pop(0):
            advance(k)

    def small_row(k, value):
        sums[small_at + k : small_at + k + 1, :] = value

    def spread_grad(source):
        def step(h, carry):
            value = source[row_at(h), :]
            put_row(scratch.xg, h, value)
            return carry + tile_sums(value)

        return grid_rows(step, zeros8)

    def weight_grad(turned, at, depth, a):
        rows = pl.ds((2 - a) * width, cells)
        both = dot(turned[...], scratch.xg[rows, :])
        for half in range(depth // c):
            part = fold_rows(both[2 * c * half : 2 * c * (half + 1)])
            for b in range(3):
                high, low = HIGH_AT[2 - b] * c, LOW_AT[2 - b] * c
                to = at + (3 * a + b) * depth + half * c
                sums[to : to + c, :] = part[:, high : high + c] + part[:, low : low + c]

    def back_conv(weight, slope, target, source, mean, inv):
        carry = (zeros8, zeros8)
        for i in range(cells // CHUNK):
            value = fold(conv_chunk([(scratch.xg, weight)], i)) * slope[chunk_at(i), :]
            target[chunk_at(i), :] = value
            normed = (source[chunk_at(i), :] - mean) * inv
            carry = (carry[0] + tile_sums(value), carry[1] + tile_sums(value * normed))
            if i % (cells // CHUNK // 2) == cells // CHUNK // 2 - 1:
                point()
        return carry

    def norm_grad(sums_in, scale, ones, count):
        one, two = group_sums(sums_in[0] * scale, sums_in[1] * scale, ones)
        return one / count, two / count

    cot[here_rows] = cot_from[row]
    cot_swap.arrive()
    total_cot = column_sum(spread_grad(cot))
    for a in range(3):
        weight_grad(scratch.td2, starts.dec_conv2, c, a)
    part = fold(dot(scratch.turned[...], scratch.xg[width : cells + width, 2 * c : 4 * c]))
    sums[starts.skip_weight : starts.skip_weight + 2 * c, :] = fold_rows(part)
    small_row(3, total_cot)
    begin()

    grad = scratch.grad
    sums_d2 = back_conv(scratch.bd2, scratch.slope_d2, grad, middle_d, mean_d2, inv_d2)
    side_grads = (scratch.grad_a, scratch.grad_b)
    for half in range(2):

        def skip_back(i, carry, half=half):
            rows = pl.ds(pl.multiple_of(i * CHUNK + width, width), CHUNK)
            value = dot(scratch.xg[rows, 2 * c : 4 * c], scratch.b_skip[half])
            side_grads[half][chunk_at(i), :] = fold(value)
            return carry

        lax.fori_loop(0, cells // CHUNK, skip_back, 0)
    point()

    def table_rows(k, sums_in, gain, bias, one_plus):
        plain, times = column_sum(sums_in[0]), column_sum(sums_in[1])
        for s in range(inputs.enc_step_table.shape[0]):
            small_row(k + 2 * s, jnp.where(step_here == s, gain * times + bias * plain, 0.0))
            small_row(k + 2 * s + 1, jnp.where(step_here == s, plain, 0.0))
        return one_plus * times, one_plus * plain

    def middle_grad(source, mean, inv, scale, sums_in):
        zero, slope = norm_grad(sums_in, scale, ones16, count16)

        def step(h, carry):
            normed = (source[row_at(h), :] - mean) * inv
            value = inv * (grad[row_at(h), :] * scale - zero - normed * slope)
            put_row(scratch.xg, h, value)
            return carry

        grid_rows(step)

    gain_row, bias_row = table_rows(16, sums_d2, gain_d2, bias_d2, 1.0 + dec_scale)
    small_row(8, gain_row)
    small_row(9, bias_row)
    middle_grad(middle_d, mean_d2, inv_d2, gain_d2 * (1.0 + dec_scale), sums_d2)
    point()
    output_swap.second()
    for a in range(3):
        weight_grad(scratch.td1, starts.dec_conv1, 2 * c, a)
        point()
        begin()

    for half, (source, mean, inv, gain) in enumerate(halves):
        sums_in = back_conv(
            (scratch.bd1a, scratch.bd1b)[half],
            (scratch.slope_d1a, scratch.slope_d1b)[half],
            grad,
            source,
            mean,
            inv,
        )
        small_row(4 + half, column_sum(sums_in[1]))
        small_row(6 + half, column_sum(sums_in[0]))
        zero, slope = norm_grad(sums_in, gain, ones32, count32)
        target = side_grads[half]

        def input_grad(h, carry):
            normed = (source[row_at(h), :] - mean) * inv
            value = inv * (grad[row_at(h), :] * gain - zero - normed * slope)
            value = target[row_at(h), :] + value
            target[row_at(h), :] = value
            return carry + tile_sums(value)

        total = grid_rows(input_grad, zeros8)
        if half == 0:
            small_row(2, column_sum(total))
        point()

    output_swap.third()
    grad_raised, grad_encoded = side_grads
    x_grad_up = scratch.x_grad_up
    for k, piece in enumerate(pick(grad_raised)):
        high, low = split(piece)
        x_grad_up[:, k * c : (k + 1) * c] = high
        x_grad_up[:, (k + 4) * c : (k + 5) * c] = low
    grad_lowered = fold(dot(x_grad_up[...], scratch.b_up[...]))
    small_row(1, jnp.sum(grad_lowered, axis=0, keepdims=True))
    x_grad_low = scratch.x_grad_low
    high, low = split(grad_lowered)
    x_grad_low[:, 0:c] = high
    x_grad_low[:, c : 2 * c] = low
    point()
    part = fold(fold_rows(dot(x_up[...], x_grad_up[...], TN)))
    for k in range(4):
        at = starts.up_weight + k * c
        sums[at : at + c, :] = part[:, k * c : (k + 1) * c]
    part = fold_rows(fold(dot(x_down[...], x_grad_low[...], TN)))
    sums[starts.reducer_weight : starts.reducer_weight + 4 * c, :] = part
    point()
    begin()
    place_cells(
        grad, [fold(dot(x_grad_low[...], scratch.b_down[k])) for k in range(4)]
    )

    def join_row(h, carry):
        value = grad_encoded[row_at(h), :] + grad[row_at(h), :]
        grad_encoded[row_at(h), :] = value
        put_row(scratch.xg, h, value)
        return carry + tile_sums(value)

    small_row(0, column_sum(grid_rows(join_row, zeros8)))
    for k in range(10, 16):
        small_row(k, jnp.zeros((1, c), F32))
    sums[small_at + 24 : small_at + LATE, :] = jnp.zeros((LATE - 24, c), F32)
    point()
    for a in range(3):
        weight_grad(scratch.te2, starts.enc_conv2, c, a)
        point()
    begin()
    sums_e2 = back_conv(scratch.be2, scratch.slope_e2, grad, middle_e, mean_e2, inv_e2)
    gain_row, bias_row = table_rows(LATE + 24, sums_e2, gain_e2, bias_e2, 1.0 + enc_scale)
    small_row(LATE + 18, gain_row)
    small_row(LATE + 19, bias_row)
    middle_grad(middle_e, mean_e2, inv_e2, gain_e2 * (1.0 + enc_scale), sums_e2)
    point()
    for a in range(3):
        weight_grad(scratch.te1, starts.enc_conv1, c, a)
        point()
        if a:
            begin()
    sums_e1 = back_conv(scratch.be1, scratch.slope_e1, grad, lifted, mean_e1, inv_e1)
    small_row(LATE + 16, column_sum(sums_e1[1]))
    small_row(LATE + 17, column_sum(sums_e1[0]))
    zero, slope = norm_grad(sums_e1, gain_e1, ones16, count16)

    def lifted_grad(h, carry):
        normed = (lifted[row_at(h), :] - mean_e1) * inv_e1
        value = inv_e1 * (grad[row_at(h), :] * gain_e1 - zero - normed * slope)
        grad[row_at(h), :] = grad_encoded[row_at(h), :] + value
        return carry

    grid_rows(lifted_grad)
    point()

    late_at = small_at + LATE
    sums[late_at : late_at + 16, :] = dot_three(fields[...], grad[...])
    sums[late_at + 20 : late_at + 24, :] = jnp.zeros((4, c), F32)
    point()
    begin()
    back = dot_three(lift[...], grad[...], NT)
    frames_out = scratch.frames_out
    for source in range(line):
        for k in range(strip):
            h = source * strip + k
            value = back[0:history, h * width : (h + 1) * width]
            frames_out[source, :, k, :] = value * keep * masks[h]
    frames_here[row] = frames_out[row]
    for k in range(1, line):
        to = lax.rem(row + k, line)
        output_copies.append(
            send(frames_out.at[to], frames_here.at[row], device_at(to))
        )

    output_swap.arrive()
    for k in REST:
        advance(k)
    assert not due and all(exchange.done() for exchange in exchanges)

    for copy in output_copies:
        copy.wait_recv()
    for copy in frame_copies + output_copies:
        copy.wait_send()
    cot_swap.sent()
    output_swap.sent()
    for exchange in exchanges:
        for copy, only in exchange.copies:
            if only is None:
                copy.wait_send()
            else:
                pl.when(only)(copy.wait_send)


def write_kernel(layout, *refs):
    shapes, starts, small_at = layout
    output, frames_grad, gradients_here = refs[:3]
    outputs = refs[3:-1]
    sem = refs[-1]
    c = gradients_here.shape[1]
    leaving = []

    def leave(source, target):
        leaving.append(pltpu.make_async_copy(source, target, sem.at[len(leaving)]))
        leaving[-1].start()

    for k, name in enumerate(LARGE):
        rows = pl.ds(starts[name], shapes[name][0])
        leave(gradients_here.at[rows], outputs[2 + k])
    for target, (k, rows) in zip(outputs[2 + len(LARGE) :], SMALL_ROWS.values()):
        at = small_at + k
        if rows == 8:
            for s in range(target.shape[0]):
                target[s : s + 1, 0:c] = gradients_here[at + 2 * s : at + 2 * s + 1, :]
                target[s : s + 1, c : 2 * c] = gradients_here[at + 2 * s + 1 : at + 2 * s + 2, :]
        else:
            target[...] = gradients_here[at : at + rows, :]
    leave(output, outputs[0])
    leave(frames_grad, outputs[1])
    for copy in leaving:
        copy.wait()


def whole_items(shape, *arguments):
    line = shape["rows"]
    whole = Given(*arguments)
    given = whole._asdict()
    frames, cotangent = whole.frames, whole.cotangent
    items, history, strip, width = frames.shape
    c = cotangent.shape[-1]
    cells = strip * line * width
    flat = {}
    for name, value in given.items():
        if value is cotangent:
            value = value.reshape(items, strip * width, c)
        elif name in LARGE:
            value = value.reshape(-1, c)
        elif value.ndim == 1 and name not in IN_SMEM:
            value = value.reshape(-1, c)
        flat[name] = value
    shapes = {name: flat[name].shape for name in LARGE}
    big_layout = layout_of(SimpleNamespace(**shapes))
    starts, small_at, total_rows, runs = big_layout
    copies = 20 + 3 * (line - 1) + len(runs) * (6 + 2 * PIECES + 2 * (line - 1)) + 6
    landing = sum(rows // 2 + 5 * rows // 8 for _, rows in runs) + LATE_COUNT * (8 + line)
    shifted = pltpu.VMEM((cells + 2 * width, 6 * c), BF16)
    forward = pltpu.VMEM((18 * c, 2 * c), BF16)
    backward = forward
    field = pltpu.VMEM((cells, c), F32)
    flipped_field = pltpu.VMEM((2 * c, cells), BF16)
    quarter = cells // 4
    scratch = dict(
        small=pltpu.VMEM((LATE_COUNT, c), F32),
        send=pltpu.SemaphoreType.DMA((copies,)),
        recv=pltpu.SemaphoreType.DMA((copies,)),
        local=pltpu.SemaphoreType.DMA((12 + len(runs),)),
        sums=pltpu.VMEM((total_rows, c), F32),
        landing=pltpu.VMEM((landing, c), F32),
        frames_in=pltpu.VMEM((line, history, strip, width), F32),
        mask_in=pltpu.VMEM((line, strip, width), jnp.int32),
        frames_out=pltpu.VMEM((line, history, strip, width), F32),
        frames_from=pltpu.VMEM((line, history, strip, width), F32),
        mask_from=pltpu.VMEM((line, strip, width), jnp.int32),
        cot_from=pltpu.VMEM((items, strip * width, c), F32),
        cot_inward=pltpu.VMEM((2, strip * width, c), F32),
        cot_across=pltpu.VMEM((2, strip * width, c), F32),
        output_inward=pltpu.VMEM((2, strip * width, c), F32),
        output_across=pltpu.VMEM((2, strip * width, c), F32),
        fields=pltpu.VMEM((16, cells), F32),
        lift=pltpu.VMEM((16, c), F32),
        joined=pltpu.VMEM((cells, 4 * c), BF16),
        x_down=pltpu.VMEM((quarter, 8 * c), BF16),
        x_grad_up=pltpu.VMEM((quarter, 8 * c), BF16),
        x_up=pltpu.VMEM((quarter, 2 * c), BF16),
        x_grad_low=pltpu.VMEM((quarter, 2 * c), BF16),
        f_down=pltpu.VMEM((8 * c, 2 * c), BF16),
        b_down=pltpu.VMEM((4, 2 * c, 2 * c), BF16),
        f_up=pltpu.VMEM((4, 2 * c, 2 * c), BF16),
        b_up=pltpu.VMEM((8 * c, 2 * c), BF16),
        f_skip=pltpu.VMEM((4 * c, 2 * c), BF16),
        b_skip=pltpu.VMEM((2, 2 * c, 2 * c), BF16),
        xe1=shifted,
        xe2=shifted,
        xd1a=shifted,
        xd1b=shifted,
        xd2=shifted,
        xg=shifted,
        te1=flipped_field,
        te2=flipped_field,
        td1=pltpu.VMEM((4 * c, cells), BF16),
        td2=flipped_field,
        turned=pltpu.VMEM((4 * c, cells), BF16),
        fe1=forward,
        fe2=forward,
        fd1a=forward,
        fd1b=forward,
        fd2=forward,
        be1=backward,
        be2=backward,
        bd1a=backward,
        bd1b=backward,
        bd2=backward,
        slope_e1=field,
        slope_e2=field,
        slope_d1a=field,
        slope_d1b=field,
        slope_d2=field,
        lifted=field,
        middle_e=field,
        encoded=field,
        raised=field,
        middle_d=field,
        result=field,
        cot=field,
        grad=field,
        grad_a=field,
        grad_b=field,
    )
    scratch.update({name: pltpu.VMEM(shapes[name], F32) for name in LARGE})

    in_hbm = pl.BlockSpec(memory_space=pl.ANY)
    in_vmem = pl.BlockSpec(memory_space=pltpu.VMEM)
    in_smem = pl.BlockSpec(memory_space=pltpu.SMEM)
    in_specs = [
        in_hbm if name in IN_HBM else in_smem if name in IN_SMEM else in_vmem
        for name in ARGUMENTS
    ]
    out_shape = [
        pltpu.VMEM((items, strip * width, c), F32),
        pltpu.VMEM(frames.shape, F32),
        pltpu.VMEM((total_rows, c), F32),
    ]
    out_specs = [in_vmem] * 3
    results = pl.pallas_call(
        functools.partial(
            item_kernel,
            (line, strip, width, shapes, big_layout),
            tuple(scratch),
        ),
        out_shape=out_shape,
        in_specs=in_specs,
        out_specs=out_specs,
        scratch_shapes=list(scratch.values()),
        compiler_params=pltpu.CompilerParams(
            collective_id=0, has_side_effects=True, vmem_limit_bytes=56 * 1024 * 1024
        ),
    )(*[flat[name] for name in ARGUMENTS])
    names = LARGE + tuple(SMALL_ROWS)
    written = pl.pallas_call(
        functools.partial(write_kernel, (shapes, starts, small_at)),
        out_shape=[
            jax.ShapeDtypeStruct((items, strip * width, c), F32),
            jax.ShapeDtypeStruct(frames.shape, F32),
        ]
        + [jax.ShapeDtypeStruct(flat[name].shape, F32) for name in names],
        in_specs=[in_vmem] * 3,
        out_specs=[in_hbm] * (2 + len(LARGE)) + [in_vmem] * len(SMALL_ROWS),
        scratch_shapes=[pltpu.SemaphoreType.DMA((2 + len(LARGE),))],
        compiler_params=pltpu.CompilerParams(vmem_limit_bytes=16 * 1024 * 1024),
    )(*results)
    grads = dict(zip(names, written[2:]))
    ordered = [name for name in ARGUMENTS if name in grads]
    return (written[0].reshape(cotangent.shape), written[1]) + tuple(
        grads[name].reshape(given[name].shape) for name in ordered
    )


def body(shape, *arguments):
    items, _, strip, width = arguments[0].shape
    line = shape["rows"]
    whole = (
        shape["section"] == 2
        and shape["batch"] == 4
        and items == line == 4
        and arguments[-1].shape[-1] == 128
        and (strip * line * width) % CHUNK == 0
    )
    return whole_items(shape, *arguments) if whole else strips_body(*arguments)


def solution(mesh):
    in_specs = (
        P(("section", "batch"), None, "rows", None),
        P(("section", "batch")),
        P(("section", "batch"), "rows", None),
        P(("section", "batch")),
        P(),
        P(),
        P(),
        P(),
        P(),
        P(),
        P(),
        P(),
        P(),
        P(),
        P(),
        P(),
        P(),
        P(),
        P(),
        P(),
        P(),
        P(),
        P(),
        P(),
        P(),
        P(),
        P(),
        P(),
        P(("section", "batch"), "rows", None, None),
    )
    out_specs = (
        P(("section", "batch"), "rows", None, None),
        P(("section", "batch"), None, "rows", None),
        P(),
        P(),
        P(),
        P(),
        P(),
        P(),
        P(),
        P(),
        P(),
        P(),
        P(),
        P(),
        P(),
        P(),
        P(),
        P(),
        P(),
        P(),
        P(),
        P(),
        P(),
        P(),
        P(),
        P(),
    )
    return jax.shard_map(functools.partial(body, mesh.shape), mesh=mesh, in_specs=in_specs, out_specs=out_specs, check_vma=False)
```

```python
import functools
from types import SimpleNamespace
from typing import Any, NamedTuple

import jax
import jax.numpy as jnp
from jax import lax
from jax.experimental import pallas as pl
from jax.experimental.pallas import tpu as pltpu
from jax.sharding import PartitionSpec as P

GROUPS = 8
FIELDS = 3
HIST = 4


EPS = 1e-05
HIGH = lax.Precision.HIGHEST


def extended(cells, sides, width):
    for axis, dim in sides:
        count = lax.axis_size(axis)
        ends = count - 1
        head = lax.slice_in_dim(cells, 0, width, axis=dim)
        tail = lax.slice_in_dim(cells, cells.shape[dim] - width, cells.shape[dim], axis=dim)
        cells = jnp.concatenate(
            [
                lax.ppermute(tail, axis, [(i, (i + 1) % count) for i in range(ends)]),
                cells,
                lax.ppermute(head, axis, [((i + 1) % count, i) for i in range(ends)]),
            ],
            axis=dim,
        )
    return cells


def from_behind(value, axis, steps):
    count = lax.axis_size(axis)
    pairs = [(source, (source + steps) % count) for source in range(count)]
    return lax.ppermute(value, axis, pairs)


def group_view(value_arrays):
    extent = value_arrays.shape
    return value_arrays.reshape(extent[:-1] + (GROUPS, extent[-1] // GROUPS))


def global_sums(value_arrays):
    grouped = group_view(value_arrays)
    flat = grouped.reshape(-1, GROUPS, grouped.shape[-1])
    first_sum = jnp.sum(flat, axis=(0, 2))
    second_sum = jnp.sum(flat * flat, axis=(0, 2))
    return lax.psum((first_sum, second_sum), "rows")


def apply_norm(value_arrays, sum_one, sum_two, norm_gain, norm_bias, total):
    grouped = group_view(value_arrays)
    group_mean = sum_one / total
    variance = sum_two / total - group_mean * group_mean
    inverse = lax.rsqrt(variance + EPS)
    normed = (grouped - group_mean[:, None]) * inverse[:, None]
    return normed.reshape(value_arrays.shape) * norm_gain + norm_bias


def norm_back(value_arrays, grad_one, grad_two):
    grouped = group_view(value_arrays)
    extra = grad_one[:, None] + 2.0 * grouped * grad_two[:, None]
    return extra.reshape(value_arrays.shape)


def reduce_grads(grad_one, grad_two):
    return lax.psum((grad_one, grad_two), "rows")


def conv_rows(padded, kernel):
    widened = jnp.pad(padded, ((0, 0), (1, 1), (0, 0)))
    return lax.conv_general_dilated(
        widened[None],
        kernel,
        (1, 1),
        "VALID",
        dimension_numbers=("NHWC", "HWIO", "NHWC"),
        precision=HIGH,
    )[0]


def flipped(kernel):
    return jnp.transpose(kernel[::-1, ::-1], (0, 1, 3, 2))


def pad_grads(value_arrays):
    return extended(value_arrays, (("rows", 0),), 1)


def totals_of(inputs, conv1):
    strip = inputs.shape[0]
    cells = strip * lax.axis_size("rows") * inputs.shape[1]
    return (cells * (inputs.shape[2] // GROUPS), cells * (conv1.shape[3] // GROUPS))


def block_forward(inputs, weights, scale_part, shift_part):
    norm1_gain, norm1_bias, conv1, norm2_gain, norm2_bias, conv2, conv2_bias = weights
    total_in, total_mid = totals_of(inputs, conv1)
    sums_in = global_sums(inputs)

    def pad_rows(value_arrays):
        return extended(value_arrays, (("rows", 0),), 1)

    act_one = pad_rows(
        jax.nn.gelu(
            apply_norm(inputs, sums_in[0], sums_in[1], norm1_gain, norm1_bias, total_in),
            approximate=False,
        )
    )
    middle = conv_rows(act_one, conv1)
    sums_mid = global_sums(middle)
    shaped = (
        apply_norm(middle, sums_mid[0], sums_mid[1], norm2_gain, norm2_bias, total_mid)
        * (1.0 + scale_part)
        + shift_part
    )
    act_two = pad_rows(jax.nn.gelu(shaped, approximate=False))
    branch = conv_rows(act_two, conv2) + conv2_bias
    return (branch, (sums_in[0], sums_in[1], act_one, middle, sums_mid[0], sums_mid[1], act_two))


def block_backward(inputs, weights, scale_part, shift_part, kept, grad_out):
    norm1_gain, norm1_bias, conv1, norm2_gain, norm2_bias, conv2, conv2_bias = weights
    in_one, in_two, act_one, middle, mid_one, mid_two, act_two = kept
    total_in, total_mid = totals_of(inputs, conv1)
    grad_conv2 = jax.vjp(lambda kernel: conv_rows(act_two, kernel), conv2)[1](grad_out)[0]
    grad_bias2 = jnp.sum(grad_out, axis=(0, 1))
    grad_act_two = conv_rows(pad_grads(grad_out), flipped(conv2))

    def second_piece(middle_in, sum_one, sum_two, gain_in, incoming_bias, scale_in, shift_in):
        shaped = (
            apply_norm(middle_in, sum_one, sum_two, gain_in, incoming_bias, total_mid)
            * (1.0 + scale_in)
            + shift_in
        )
        return jax.nn.gelu(shaped, approximate=False)

    second_pull = jax.vjp(
        second_piece, middle, mid_one, mid_two, norm2_gain, norm2_bias, scale_part, shift_part
    )[1](grad_act_two)
    summed_one, summed_two = reduce_grads(second_pull[1], second_pull[2])
    grad_middle = second_pull[0] + norm_back(middle, summed_one, summed_two)
    grad_conv1 = jax.vjp(lambda kernel: conv_rows(act_one, kernel), conv1)[1](grad_middle)[0]
    grad_act_one = conv_rows(pad_grads(grad_middle), flipped(conv1))

    def first_piece(inputs_in, sum_one, sum_two, gain_in, incoming_bias):
        return jax.nn.gelu(
            apply_norm(inputs_in, sum_one, sum_two, gain_in, incoming_bias, total_in),
            approximate=False,
        )

    first_pull = jax.vjp(first_piece, inputs, in_one, in_two, norm1_gain, norm1_bias)[1](
        grad_act_one
    )
    first_one, first_two = reduce_grads(first_pull[1], first_pull[2])
    grad_inputs = first_pull[0] + norm_back(inputs, first_one, first_two)
    grads = (
        first_pull[3],
        first_pull[4],
        grad_conv1,
        second_pull[3],
        second_pull[4],
        grad_conv2,
        grad_bias2,
    )
    return (grad_inputs, grads, second_pull[5], second_pull[6])


def conditioning(step_item, table):
    one_hot = (jnp.arange(table.shape[0], dtype=jnp.int32) == step_item).astype(jnp.float32)
    condition = jnp.dot(one_hot, table, precision=HIGH)
    half_width = table.shape[1] // 2
    return (condition[:half_width], condition[half_width:], one_hot)


def project_in(frames_item, mask_item, count_item, incoming_weight, incoming_bias):
    history = jnp.arange(HIST, dtype=jnp.int32) >= HIST - count_item
    keep = jnp.repeat(history, FIELDS).astype(jnp.float32)
    lifted = (
        jnp.einsum(
            "fhw,fc->hwc", frames_item * keep[:, None, None], incoming_weight, precision=HIGH
        )
        + incoming_bias
    )
    return lifted * mask_item[:, :, None].astype(jnp.float32)


def coarsen_field(value_arrays, incoming_weight, incoming_bias):
    rows_here, width_here, depth_here = value_arrays.shape
    blocks = value_arrays.reshape(rows_here // 2, 2, width_here // 2, 2, depth_here)
    return jnp.einsum("iajbk,abkc->ijc", blocks, incoming_weight, precision=HIGH) + incoming_bias


def upsample(value_arrays, incoming_weight, incoming_bias):
    result = jnp.einsum("ijk,abkc->iajbc", value_arrays, incoming_weight, precision=HIGH)
    extent = result.shape
    return result.reshape(extent[0] * 2, extent[2] * 2, extent[4]) + incoming_bias


def flatten_all(pieces):
    return jnp.concatenate([piece.reshape(-1) for piece in pieces])


def unflatten_all(flat, templates):
    pieces = []
    offset_at = 0
    for template in templates:
        count_here = template.size
        pieces.append(flat[offset_at : offset_at + count_here].reshape(template.shape))
        offset_at += count_here
    return tuple(pieces)


def strips_body(
    frames,
    counts,
    cell_mask,
    step_index,
    lift_weight,
    lift_bias,
    enc_norm1_gain,
    enc_norm1_bias,
    enc_conv1,
    enc_step_table,
    enc_norm2_gain,
    enc_norm2_bias,
    enc_conv2,
    enc_conv2_bias,
    reducer_weight,
    reducer_bias,
    up_weight,
    up_bias,
    dec_norm1_gain,
    dec_norm1_bias,
    dec_conv1,
    dec_step_table,
    dec_norm2_gain,
    dec_norm2_bias,
    dec_conv2,
    dec_conv2_bias,
    skip_weight,
    skip_bias,
    cotangent,
):
    enc_weights = (
        enc_norm1_gain,
        enc_norm1_bias,
        enc_conv1,
        enc_norm2_gain,
        enc_norm2_bias,
        enc_conv2,
        enc_conv2_bias,
    )
    dec_weights = (
        dec_norm1_gain,
        dec_norm1_bias,
        dec_conv1,
        dec_norm2_gain,
        dec_norm2_bias,
        dec_conv2,
        dec_conv2_bias,
    )
    params = (
        lift_weight,
        lift_bias,
        enc_norm1_gain,
        enc_norm1_bias,
        enc_conv1,
        enc_step_table,
        enc_norm2_gain,
        enc_norm2_bias,
        enc_conv2,
        enc_conv2_bias,
        reducer_weight,
        reducer_bias,
        up_weight,
        up_bias,
        dec_norm1_gain,
        dec_norm1_bias,
        dec_conv1,
        dec_step_table,
        dec_norm2_gain,
        dec_norm2_bias,
        dec_conv2,
        dec_conv2_bias,
        skip_weight,
        skip_bias,
    )

    def forward_micro(carry, sliced):
        frames_item, mask_item, count_item, step_item = sliced
        lifted = project_in(frames_item, mask_item, count_item, lift_weight, lift_bias)
        enc_scale, enc_shift, unused_hot = conditioning(step_item, enc_step_table)
        enc_branch, enc_kept = block_forward(lifted, enc_weights, enc_scale, enc_shift)
        encoder_result = lifted + enc_branch
        coarse_field = coarsen_field(encoder_result, reducer_weight, reducer_bias)
        foreign = from_behind(coarse_field, "section", 1)
        raised_foreign = upsample(foreign, up_weight, up_bias)
        raised = from_behind(raised_foreign, "section", 1)
        joined = jnp.concatenate([raised, encoder_result], axis=-1)
        dec_scale, dec_shift, unused_again = conditioning(step_item, dec_step_table)
        dec_branch, dec_kept = block_forward(joined, dec_weights, dec_scale, dec_shift)
        output_item = jnp.dot(joined, skip_weight, precision=HIGH) + skip_bias + dec_branch
        return (carry, (output_item, (lifted, enc_kept, encoder_result, foreign, joined, dec_kept)))

    unused, (output, kept_all) = lax.scan(
        forward_micro, jnp.zeros((), jnp.float32), (frames, cell_mask, counts, step_index)
    )

    def backward_micro(totals, sliced):
        frames_item, mask_item, count_item, step_item, grad_out, kept = sliced
        lifted, enc_kept, encoder_result, foreign, joined, dec_kept = kept
        dec_scale, dec_shift, one_hot = conditioning(step_item, dec_step_table)
        grad_joined, dec_grads, dec_gscale, dec_gshift = block_backward(
            joined, dec_weights, dec_scale, dec_shift, dec_kept, grad_out
        )
        grad_skip_weight = jnp.einsum("hwk,hwc->kc", joined, grad_out, precision=HIGH)
        grad_skip_bias = jnp.sum(grad_out, axis=(0, 1))
        grad_joined = grad_joined + jnp.dot(grad_out, skip_weight.T, precision=HIGH)
        half_width = joined.shape[-1] // 2
        grad_raised = grad_joined[..., :half_width]
        grad_encoded = grad_joined[..., half_width:]
        grad_foreign_up = from_behind(grad_raised, "section", 1)
        up_pull = jax.vjp(upsample, foreign, up_weight, up_bias)[1](grad_foreign_up)
        coarse_gradient = from_behind(up_pull[0], "section", 1)
        reducer_pullback = jax.vjp(coarsen_field, encoder_result, reducer_weight, reducer_bias)[1](
            coarse_gradient
        )
        grad_encoded = grad_encoded + reducer_pullback[0]
        enc_scale, enc_shift, enc_hot = conditioning(step_item, enc_step_table)
        grad_lifted, enc_grads, enc_gscale, enc_gshift = block_backward(
            lifted, enc_weights, enc_scale, enc_shift, enc_kept, grad_encoded
        )
        grad_lifted = grad_lifted + grad_encoded
        proj_pull = jax.vjp(
            lambda frames_in, incoming_weight, incoming_bias: project_in(
                frames_in, mask_item, count_item, incoming_weight, incoming_bias
            ),
            frames_item,
            lift_weight,
            lift_bias,
        )[1](grad_lifted)
        enc_table_grad = enc_hot[:, None] * jnp.concatenate([enc_gscale, enc_gshift])[None, :]
        dec_table_grad = one_hot[:, None] * jnp.concatenate([dec_gscale, dec_gshift])[None, :]
        micro_list = (
            proj_pull[1],
            proj_pull[2],
            enc_grads[0],
            enc_grads[1],
            enc_grads[2],
            enc_table_grad,
            enc_grads[3],
            enc_grads[4],
            enc_grads[5],
            enc_grads[6],
            reducer_pullback[1],
            reducer_pullback[2],
            up_pull[1],
            up_pull[2],
            dec_grads[0],
            dec_grads[1],
            dec_grads[2],
            dec_table_grad,
            dec_grads[3],
            dec_grads[4],
            dec_grads[5],
            dec_grads[6],
            grad_skip_weight,
            grad_skip_bias,
        )
        micro_flat = flatten_all(micro_list)
        return (totals + micro_flat, proj_pull[0])

    total_size = sum((piece.size for piece in params))
    start_totals = jnp.zeros((total_size,), jnp.float32)
    flat_totals, frames_grad = lax.scan(
        backward_micro,
        start_totals,
        (frames, cell_mask, counts, step_index, cotangent, kept_all),
        reverse=True,
    )
    flat_totals = lax.psum(flat_totals, ("section", "batch", "rows"))
    grads = unflatten_all(flat_totals, params)
    return (output, frames_grad) + grads


F32 = jnp.float32
BF16 = jnp.bfloat16
MESH = pl.DeviceIdType.MESH
NN = ((1,), (0,))
NT = ((1,), (1,))
TN = ((0,), (0,))
HIGH_AT = (0, 2, 1)
LOW_AT = (4, 3, 5)
CHUNK = 512
class Given(NamedTuple):
    frames: Any
    counts: Any
    cell_mask: Any
    step_index: Any
    lift_weight: Any
    lift_bias: Any
    enc_norm1_gain: Any
    enc_norm1_bias: Any
    enc_conv1: Any
    enc_step_table: Any
    enc_norm2_gain: Any
    enc_norm2_bias: Any
    enc_conv2: Any
    enc_conv2_bias: Any
    reducer_weight: Any
    reducer_bias: Any
    up_weight: Any
    up_bias: Any
    dec_norm1_gain: Any
    dec_norm1_bias: Any
    dec_conv1: Any
    dec_step_table: Any
    dec_norm2_gain: Any
    dec_norm2_bias: Any
    dec_conv2: Any
    dec_conv2_bias: Any
    skip_weight: Any
    skip_bias: Any
    cotangent: Any


ARGUMENTS = Given._fields
LARGE = tuple(
    dict(
        dec_conv1=0,
        up_weight=0,
        reducer_weight=0,
        dec_conv2=0,
        skip_weight=0,
        enc_conv1=0,
        enc_conv2=0,
    )
)
IN_HBM = tuple(dict(frames=0, cell_mask=0, cotangent=0)) + LARGE
IN_SMEM = tuple(dict(counts=0, step_index=0))
LATE = 64
SMALL_ROWS = dict(
    enc_conv2_bias=(0, 1),
    reducer_bias=(1, 1),
    up_bias=(2, 1),
    dec_conv2_bias=(3, 1),
    skip_bias=(3, 1),
    dec_norm1_gain=(4, 2),
    dec_norm1_bias=(6, 2),
    dec_norm2_gain=(8, 1),
    dec_norm2_bias=(9, 1),
    dec_step_table=(16, 8),
    lift_weight=(LATE, 12),
    lift_bias=(LATE + 12, 1),
    enc_norm1_gain=(LATE + 16, 1),
    enc_norm1_bias=(LATE + 17, 1),
    enc_norm2_gain=(LATE + 18, 1),
    enc_norm2_bias=(LATE + 19, 1),
    enc_step_table=(LATE + 24, 8),
)
LATE_COUNT = 32
PIECES = 1
SMALL_COUNT = LATE + LATE_COUNT
DUE = ((), (), (), (), (0,), (), (), (), (), (1,), (2, 0), (3,), (), (), (1,), (), (0, 2), (), (), (1, 3), (4, 2), (0,), (1, 3), (5,), (2,), (), (4, 0, 3), (1, 6, 2, 7, 5, 4), (), (3,))
REST = (0, 4, 5, 1, 8, 6, 0, 4, 5, 1, 2, 7, 6, 3, 2, 5, 7, 8, 6, 3, 4, 7, 6, 5, 7, 4, 6, 5, 7, 6, 7)
OUTPUTS = tuple(dict(output=0, frames_grad=0, gradients=0))


def split(value):
    high = value.astype(BF16)
    return high, (value - high.astype(F32)).astype(BF16)


def dot(left, right, dims=NN, precision=None):
    return lax.dot_general(
        left, right, (dims, ((), ())), precision=precision, preferred_element_type=F32
    )


def fold(value):
    half = value.shape[1] // 2
    return value[:, :half] + value[:, half:]


def fold_rows(value):
    half = value.shape[0] // 2
    return value[:half] + value[half:]


def tile_sums(value):
    return jnp.sum(value.reshape(-1, 8, value.shape[-1]), axis=0)


def column_sum(tiles):
    return jnp.sum(tiles, axis=0, keepdims=True)


def normal(value):
    bell = jnp.exp(-0.5 * value * value)
    t = 1.0 / (1.0 + 0.2316418882663604 * jnp.abs(value))
    poly = 0.5307027145
    for factor in (-0.7265760135, 0.7107068705, -0.142248368, 0.127414796):
        poly = poly * t + factor
    tail = poly * t * bell
    return jnp.where(value < 0.0, tail, 1.0 - tail), 0.3989422804014327 * bell


def dot_three(left, right, dims=NN):
    left_high, left_low = split(left)
    right_high, right_low = split(right)
    total = dot(left_high, right_high, dims)
    return total + (dot(left_high, right_low, dims) + dot(left_low, right_high, dims))


def group_ones(channels, size):
    rows = lax.broadcasted_iota(jnp.int32, (channels, channels), 0) // size
    columns = lax.broadcasted_iota(jnp.int32, (channels, channels), 1) // size
    return (rows == columns).astype(BF16)


def group_sums(first, second, ones):
    terms = []
    rest = jnp.concatenate([first, second], axis=0)
    for _ in range(3):
        term = rest.astype(BF16)
        terms.append(term)
        rest = rest - term.astype(F32)
    both = dot(jnp.concatenate(terms, axis=0), ones)
    both = both[32:48] + both[16:32] + both[:16]
    return column_sum(both[:8]), column_sum(both[8:])


class LineSwap:

    def __init__(self, line, source, target, inward, across, make):
        far = 3 - line.outer
        self.line = line
        to_inner, to_across = line.device(line.inner), line.device(line.across)
        to_outer = line.device(line.outer)
        here = target(line.here)
        self.to_far = make(source(3 - line.here), inward.at[1], to_inner)
        self.to_second = make(source(3 - line.inner), inward.at[0], to_inner)
        self.to_inner = make(source(line.inner), here, to_inner)
        self.for_far = make(source(far), across.at[0], to_across)
        self.to_across = make(source(line.across), here, to_across)
        self.to_outer = make(source(line.outer), here, to_outer)
        self.pass_far = make(inward.at[1], across.at[1], to_across)
        self.pass_second = make(inward.at[0], target(line.outer), to_across)
        self.pass_across = make(across.at[0], target(line.across), to_outer)
        self.pass_opposite = make(across.at[1], target(far), to_outer)

    def first(self):
        @pl.when(self.line.edge)
        def _():
            for copy in (self.to_far, self.to_second, self.to_inner):
                copy.start()

        @pl.when(self.line.middle)
        def _():
            for copy in (self.for_far, self.to_across, self.to_outer):
                copy.start()

    def second(self):
        @pl.when(self.line.middle)
        def _():
            self.for_far.wait_recv()
            self.pass_across.start()
            self.to_far.wait_recv()
            self.pass_far.start()
            self.to_second.wait_recv()
            self.pass_second.start()

    def third(self):
        @pl.when(self.line.middle)
        def _():
            self.pass_far.wait_recv()
            self.pass_opposite.start()

    def arrive(self):
        @pl.when(self.line.edge)
        def _():
            for copy in (self.to_outer, self.pass_across, self.pass_opposite):
                copy.wait_recv()

        @pl.when(self.line.middle)
        def _():
            for copy in (self.to_inner, self.to_across, self.pass_second):
                copy.wait_recv()

    def sent(self):
        @pl.when(self.line.edge)
        def _():
            for copy in (self.to_far, self.to_second, self.to_inner):
                copy.wait_send()

        @pl.when(self.line.middle)
        def _():
            for copy in (self.for_far, self.to_across, self.to_outer):
                copy.wait_send()
            for copy in (self.pass_far, self.pass_second, self.pass_across, self.pass_opposite):
                copy.wait_send()


class Exchange:

    def __init__(self, place, start, rows, landing, first_sem):
        self.place, self.start, self.rows, self.landing = place, start, rows, landing
        self.sem = first_sem
        self.stage = 0
        self.copies = []
        self.waiting = []
        self.group = place.plane_group
        self.half = rows // 2
        self.base = start + place.core * self.half
        self._finish(self.half)

    def _finish(self, size):
        self.part = size // self.group.count
        self.own = self.base + self.group.here * self.part

    def count(self):
        return 2 * PIECES + 2 * (self.group.count - 1) + 3

    def land_rows(self):
        return self.half + (self.group.count + 1) * self.part

    def _copy(self, source, target, device, only=None):
        place = self.place
        copy = pltpu.make_async_remote_copy(
            src_ref=source,
            dst_ref=target,
            send_sem=place.send.at[self.sem],
            recv_sem=place.recv.at[self.sem],
            device_id=device,
            device_id_type=MESH,
        )
        self.sem += 1
        if only is None:
            copy.start()
            self.waiting.append(copy)
        self.copies.append((copy, only))
        return copy

    def _pieces(self, source, at, target, to, size, device):
        each = size // 8 // PIECES * 8
        for k in range(PIECES):
            here = each if k < PIECES - 1 else size - each * (PIECES - 1)
            self._copy(
                source.at[self._rows(at + k * each, here)],
                target.at[self._rows(to + k * each, here)],
                device,
            )

    def _wait(self):
        for copy in self.waiting:
            copy.wait_recv()
        self.waiting = []

    def _rows(self, at, size):
        return pl.ds(pl.multiple_of(at, 8), size)

    def _swap(self):
        place = self.place
        other = self.start + (1 - place.core) * self.half
        self.land = self.landing
        self.landing += self.half
        self._pieces(place.sums, other, place.landing, self.land, self.half, place.partner)

    def _add_swap(self):
        place = self.place
        block = 64 if self.half % 64 == 0 else 32

        def step(i, carry):
            here = self._rows(self.base + i * block, block)
            there = self._rows(self.land + i * block, block)
            place.sums[here] = place.sums[here] + place.landing[there]
            return carry

        lax.fori_loop(0, self.half // block, step, 0)

    def _scatter(self, group, base, size):
        place = self.place
        self.land = self.landing
        for k in range(1, group.count):
            to = lax.rem(group.here + k, group.count)
            self._copy(
                place.sums.at[self._rows(base + to * size, size)],
                place.landing.at[pl.ds(self.landing, size)],
                group.device(to),
            )
            self.landing += size

    def _total(self, group, own, size, target):
        place = self.place
        block = 16 if size % 16 == 0 else 8

        def step(i, carry):
            here = self._rows(own + i * block, block)
            total = place.sums[here]
            for k in range(group.count - 1):
                there = self._rows(self.land + k * size + i * block, block)
                total = total + place.landing[there]
            target[here] = total
            return carry

        lax.fori_loop(0, size // block, step, 0)

    def _gather(self, group, own, size):
        final = self.place.final
        here = self._rows(own, size)
        for k in range(1, group.count):
            to = lax.rem(group.here + k, group.count)
            self._copy(final.at[here], final.at[here], group.device(to))

    def _steps(self):
        place, group = self.place, self.group
        yield self._swap()
        self._wait()
        self._add_swap()
        yield from self._both()
        self._pieces(place.final, self.base, place.final, self.base, self.half, place.partner)
        yield
        self._wait()
        yield

    def _both(self):
        place, group = self.place, self.group
        self._scatter(group, self.base, self.part)
        yield
        self._wait()
        self._total(group, self.own, self.part, place.sums)
        yield from self._line()
        self._gather(group, self.own, self.part)
        yield
        self._wait()

    def _line(self):
        place, line = self.place, self.place.line
        sums, final, landing = place.sums, place.final, place.landing
        part, own = self.part, self._rows(self.own, self.part)
        inward, across = pl.ds(self.landing, part), pl.ds(self.landing + part, part)
        self.landing += 2 * part
        block = 16 if part % 16 == 0 else 8

        def add(at, target):
            def step(i, carry):
                here = self._rows(self.own + i * block, block)
                target[here] = sums[here] + landing[pl.ds(at + i * block, block)]
                return carry

            lax.fori_loop(0, part // block, step, 0)

        first = self._copy(sums.at[own], landing.at[inward], line.device(line.inner), line.edge)
        second = self._copy(sums.at[own], landing.at[across], line.device(line.across), line.middle)
        third = self._copy(final.at[own], final.at[own], line.device(line.outer), line.middle)
        pl.when(line.edge)(first.start)
        yield

        @pl.when(line.middle)
        def _():
            first.wait_recv()
            add(self.landing - 2 * part, sums)
            second.start()

        yield

        @pl.when(line.middle)
        def _():
            second.wait_recv()
            add(self.landing - part, final)
            third.start()

        yield
        pl.when(line.edge)(third.wait_recv)

    def advance(self):
        if self.stage == 0:
            self.steps = self._steps()
        self.stage += 1
        next(self.steps)

    def done(self):
        return self.stage == 8


class SmallExchange(Exchange):

    def count(self):
        return self.place.cores_group.count + self.place.line.count - 2

    def land_rows(self):
        return self.rows * (self.place.cores_group.count + self.place.line.count)

    def _share(self, group, source):
        place = self.place
        self.land = self.landing
        self.landing += group.count * self.rows
        own = self._rows(self.land + group.here * self.rows, self.rows)
        place.landing[own] = source[...]
        for k in range(1, group.count):
            to = lax.rem(group.here + k, group.count)
            self._copy(source, place.landing.at[own], group.device(to))

    def _sum(self, group):
        total = None
        for k in range(group.count):
            part = self.place.landing[pl.ds(self.land + k * self.rows, self.rows)]
            total = part if total is None else total + part
        return total

    def _steps(self):
        place = self.place
        here = pl.ds(self.start, self.rows)
        self._share(place.line, place.sums.at[here])
        yield
        self._wait()
        place.small[...] = self._sum(place.line)
        self._share(place.cores_group, place.small)
        yield
        self._wait()
        place.final[here] = self._sum(place.cores_group)
        yield

    def done(self):
        return self.stage == 3


def layout_of(shapes):
    starts = {}
    at = 0
    for name in LARGE:
        starts[name] = at
        at += getattr(shapes, name)[0]
    small = at
    begins = SimpleNamespace(**starts)
    late = small + LATE
    tap = shapes.dec_conv2[0] // 3
    part = shapes.dec_conv1[0] // 3
    conv1, up = begins.dec_conv1, begins.up_weight
    edges = (
        (begins.dec_conv2, begins.enc_conv1),
        (conv1, conv1 + part),
        (conv1 + part, conv1 + 2 * part),
        (conv1 + 2 * part, up),
        (up, begins.dec_conv2),
        (begins.enc_conv2, late),
        (begins.enc_conv1, begins.enc_conv1 + 2 * tap),
        (begins.enc_conv1 + 2 * tap, begins.enc_conv2),
        (late, late + LATE_COUNT),
    )
    runs = [(first, last - first) for first, last in edges]
    return starts, small, late + LATE_COUNT, runs


def item_kernel(sizes, scratch_names, *refs):
    line, strip, width, shapes, big_layout = sizes
    begins, small_at, total_rows, runs = big_layout
    starts = SimpleNamespace(**begins)
    inputs = Given(*refs[: len(ARGUMENTS)])
    refs = refs[len(ARGUMENTS) :]
    output_names = OUTPUTS
    outputs = SimpleNamespace(**dict(zip(output_names, refs)))
    scratch = SimpleNamespace(**dict(zip(scratch_names, refs[len(output_names) :])))

    def w_of(name):
        return getattr(scratch, name)

    height = strip * line
    cells = height * width
    c = inputs.lift_weight.shape[1]
    strip_cells = strip * width
    history = inputs.frames.shape[1]

    core = lax.axis_index("section")
    plane = lax.axis_index("batch")
    row = lax.axis_index("rows")
    middle = lax.rem(row + 1, 4) // 2

    def device_at(to):
        return (core, plane, to)

    place = SimpleNamespace(
        core=core,
        partner=(1 - core, plane, row),
        line=SimpleNamespace(
            count=line,
            here=row,
            device=device_at,
            middle=middle == 1,
            edge=middle == 0,
            inner=1 + row // 2,
            across=3 - row,
            outer=3 * (row // 2),
        ),
        plane_group=SimpleNamespace(
            count=4, here=plane, device=lambda to: (core, to, row)
        ),
        cores_group=SimpleNamespace(
            count=8,
            here=core * 4 + plane,
            device=lambda to: (to // 4, lax.rem(to, 4), row),
        ),
        small=scratch.small,
        sums=scratch.sums,
        final=outputs.gradients,
        landing=scratch.landing,
        send=scratch.send,
        recv=scratch.recv,
    )
    local_sem = scratch.local

    frames_in, mask_in, cot = scratch.frames_in, scratch.mask_in, scratch.cot
    here_rows = pl.ds(pl.multiple_of(row * strip_cells, strip_cells), strip_cells)
    frames_from, mask_from, cot_from = scratch.frames_from, scratch.mask_from, scratch.cot_from
    staged = (
        pltpu.make_async_copy(inputs.frames, frames_from, local_sem.at[7]),
        pltpu.make_async_copy(inputs.cell_mask, mask_from, local_sem.at[8]),
        pltpu.make_async_copy(inputs.cotangent, cot_from, local_sem.at[9]),
    )
    for copy in staged:
        copy.start()

    weight_copies = {}
    for k, name in enumerate(LARGE):
        copy = pltpu.make_async_copy(getattr(inputs, name), w_of(name), local_sem.at[k])
        weight_copies[name] = copy
        copy.start()

    barrier = pltpu.get_barrier_semaphore()
    peers = [device_at(lax.rem(row + k, line)) for k in range(1, line)]
    cores_group = place.cores_group
    for k in range(1, 8):
        peers.append(cores_group.device(lax.rem(cores_group.here + k, 8)))
    for device in peers:
        pl.semaphore_signal(barrier, inc=1, device_id=device, device_id_type=MESH)
    pl.semaphore_wait(barrier, len(peers))

    next_sem = 0

    def make(source, target, device):
        nonlocal next_sem
        copy = pltpu.make_async_remote_copy(
            src_ref=source,
            dst_ref=target,
            send_sem=scratch.send.at[next_sem],
            recv_sem=scratch.recv.at[next_sem],
            device_id=device,
            device_id_type=MESH,
        )
        next_sem += 1
        return copy

    def send(source, target, device):
        copy = make(source, target, device)
        copy.start()
        return copy

    def strip_of(ref, to):
        return ref.at[pl.ds(pl.multiple_of(to * strip_cells, strip_cells), strip_cells)]

    frame_copies, output_copies = [], []
    for copy in staged[:2]:
        copy.wait()
    for k in range(1, line):
        to = lax.rem(row + k, line)
        device = device_at(to)
        frame_copies.append(send(frames_from.at[to], frames_in.at[row], device))
        frame_copies.append(send(mask_from.at[to], mask_in.at[row], device))
    staged[2].wait()
    cot_swap = LineSwap(
        place.line,
        lambda to: cot_from.at[to],
        lambda source: strip_of(cot, source),
        scratch.cot_inward,
        scratch.cot_across,
        make,
    )
    cot_swap.first()

    copied = SimpleNamespace(**weight_copies)
    def put_pair(target, block, value):
        high, low = split(value)
        rows = slice(block * c, (block + 1) * c)
        target[rows, 0:c] = high
        target[rows, c : 2 * c] = low

    def stack_conv(source, half, depth, forward):
        for a in range(3):
            for b in range(3):
                at = (3 * a + b) * depth + half * c
                for places in (HIGH_AT, LOW_AT):
                    put_pair(forward, 6 * a + places[b], source[at : at + c, :])

    def stack_turned(source, half, depth, backward):
        for a in range(3):
            for b in range(3):
                at = (3 * a + b) * depth + half * c
                turned = source[at : at + c, :].T
                for places in (HIGH_AT, LOW_AT):
                    put_pair(backward, 6 * (2 - a) + places[2 - b], turned)

    copied.enc_conv1.wait()
    stack_conv(scratch.enc_conv1, 0, c, scratch.fe1)
    copied.enc_conv2.wait()
    stack_conv(scratch.enc_conv2, 0, c, scratch.fe2)
    copied.reducer_weight.wait()
    for k in range(4):
        value = scratch.reducer_weight[k * c : (k + 1) * c, :]
        turned = value.T
        for block in (k, k + 4):
            put_pair(scratch.f_down, block, value)
        for block in (0, 1):
            put_pair(scratch.b_down.at[k], block, turned)
    copied.up_weight.wait()
    for k in range(4):
        value = scratch.up_weight[k * c : (k + 1) * c, :]
        turned = value.T
        for block in (0, 1):
            put_pair(scratch.f_up.at[k], block, value)
        for block in (k, k + 4):
            put_pair(scratch.b_up, block, turned)
    copied.dec_conv1.wait()
    stack_conv(scratch.dec_conv1, 0, 2 * c, scratch.fd1a)
    stack_conv(scratch.dec_conv1, 1, 2 * c, scratch.fd1b)
    copied.dec_conv2.wait()
    stack_conv(scratch.dec_conv2, 0, c, scratch.fd2)
    copied.skip_weight.wait()
    for half in range(2):
        value = scratch.skip_weight[half * c : (half + 1) * c, :]
        turned = value.T
        for block in (half, half + 2):
            put_pair(scratch.f_skip, block, value)
        for block in (0, 1):
            put_pair(scratch.b_skip.at[half], block, turned)

    for buffer in (scratch.xe1, scratch.xe2, scratch.xd1a, scratch.xd1b, scratch.xd2, scratch.xg):
        edge = jnp.zeros((width, 6 * c), BF16)
        buffer[0:width, :] = edge
        buffer[cells + width : cells + 2 * width, :] = edge

    lift = scratch.lift
    lift[...] = jnp.zeros(lift.shape, F32)
    lift[0:history, :] = inputs.lift_weight[...]
    lift[history : history + 1, :] = inputs.lift_bias[...]

    block = 2 * width
    column = lax.rem(lax.broadcasted_iota(jnp.int32, (block, c), 0), width)
    at_first, at_last = column == 0, column == width - 1
    zeros8 = jnp.zeros((8, c), F32)
    ones16 = group_ones(c, c // GROUPS)
    ones32 = group_ones(c, 2 * c // GROUPS)
    count16 = float(cells * (c // GROUPS))
    count32 = float(cells * (2 * c // GROUPS))

    def grid_rows(step, carry=0):
        return lax.fori_loop(0, cells // block, step, carry, unroll=2)

    def row_at(h):
        return pl.ds(pl.multiple_of(h * block, block), block)

    def chunk_at(i):
        return pl.ds(pl.multiple_of(i * CHUNK, CHUNK), CHUNK)

    def put_row(target, h, value):
        rows = pl.ds(pl.multiple_of(h * block + width, width), block)
        left = jnp.where(at_first, 0.0, pltpu.roll(value, 1, 0))
        right = jnp.where(at_last, 0.0, pltpu.roll(value, block - 1, 0))
        for b, piece in enumerate((left, value, right)):
            high, low = split(piece)
            target[rows, HIGH_AT[b] * c : (HIGH_AT[b] + 1) * c] = high
            target[rows, LOW_AT[b] * c : (LOW_AT[b] + 1) * c] = low

    def put_turned(target, columns, value, first=0, second=1):
        high, low = split(value.T)
        target[first * c : (first + 1) * c, columns] = high
        target[second * c : (second + 1) * c, columns] = low

    def conv_chunk(pairs, i):
        total = None
        for data, weight in pairs:
            taps = []
            for a in range(3):
                rows = pl.ds(pl.multiple_of(i * CHUNK + a * width, width), CHUNK)
                taps.append(data[rows, :])
            part = dot(jnp.concatenate(taps, axis=1), weight[...])
            total = part if total is None else total + part
        return total

    def norm_of(first, second, ones, count):
        one, two = group_sums(first, second, ones)
        mean = one / count
        return mean, lax.rsqrt(two / count - mean * mean + EPS)

    def activate(source, target, turned, slope, scale, shift):
        def step(h, carry):
            value = source[row_at(h), :] * scale + shift
            below, density = normal(value)
            slope[row_at(h), :] = below + value * density
            value = value * below
            put_row(target, h, value)
            put_turned(turned, row_at(h), value)
            return carry

        grid_rows(step)

    def conv_norm(pairs, target):
        def step(i, carry):
            value = fold(conv_chunk(pairs, i))
            target[chunk_at(i), :] = value
            return carry[0] + tile_sums(value), carry[1] + tile_sums(value * value)

        return lax.fori_loop(0, cells // CHUNK, step, (zeros8, zeros8))

    def sums_of(source):
        def step(h, carry):
            value = source[row_at(h), :]
            return carry[0] + tile_sums(value), carry[1] + tile_sums(value * value)

        return grid_rows(step, (zeros8, zeros8))

    step_here = jnp.full((1, c), inputs.step_index[row], jnp.int32)

    def condition(table):
        total = jnp.zeros((1, 2 * c), F32)
        chosen = jnp.concatenate([step_here, step_here], axis=1)
        for s in range(table.shape[0]):
            total = total + jnp.where(chosen == s, table[s : s + 1, :], 0.0)
        return total[:, :c], total[:, c:]

    frames_in[row] = frames_from[row]
    mask_in[row] = mask_from[row]
    for copy in frame_copies:
        copy.wait_recv()
    fields = scratch.fields
    fields[...] = jnp.zeros(fields.shape, F32)
    frame_of = lax.broadcasted_iota(jnp.int32, (history, width), 0) // FIELDS
    keep = (frame_of >= HIST - inputs.counts[row]).astype(F32)
    masks = []
    for source in range(line):
        for k in range(strip):
            columns = slice((source * strip + k) * width, (source * strip + k + 1) * width)
            mask = mask_in[source, k : k + 1, :].astype(F32)
            masks.append(mask)
            fields[0:history, columns] = frames_in[source, :, k, :] * keep * mask
            fields[history : history + 1, columns] = mask
    lifted = scratch.lifted
    lifted[...] = dot_three(fields[...], lift[...], TN)

    enc_scale, enc_shift = condition(inputs.enc_step_table)
    dec_scale, dec_shift = condition(inputs.dec_step_table)

    mean_e1, inv_e1 = norm_of(*sums_of(lifted), ones16, count16)
    gain_e1, bias_e1 = inputs.enc_norm1_gain[...], inputs.enc_norm1_bias[...]
    a_e1 = inv_e1 * gain_e1
    activate(lifted, scratch.xe1, scratch.te1, scratch.slope_e1, a_e1, bias_e1 - mean_e1 * a_e1)
    middle_e = scratch.middle_e
    mean_e2, inv_e2 = norm_of(
        *conv_norm([(scratch.xe1, scratch.fe1)], middle_e), ones16, count16
    )
    gain_e2, bias_e2 = inputs.enc_norm2_gain[...], inputs.enc_norm2_bias[...]
    a_e2 = inv_e2 * gain_e2
    activate(
        middle_e,
        scratch.xe2,
        scratch.te2,
        scratch.slope_e2,
        a_e2 * (1.0 + enc_scale),
        (bias_e2 - mean_e2 * a_e2) * (1.0 + enc_scale) + enc_shift,
    )
    cot_swap.second()
    encoded = scratch.encoded
    conv2_bias = inputs.enc_conv2_bias[...]
    joined = scratch.joined

    def encode(i, carry):
        value = fold(conv_chunk([(scratch.xe2, scratch.fe2)], i))
        value = value + conv2_bias + lifted[chunk_at(i), :]
        encoded[chunk_at(i), :] = value
        high, low = split(value)
        joined[chunk_at(i), c : 2 * c] = high
        joined[chunk_at(i), 3 * c : 4 * c] = low
        put_turned(scratch.turned, chunk_at(i), value, 1, 3)
        return carry[0] + tile_sums(value), carry[1] + tile_sums(value * value)

    sums_enc = lax.fori_loop(0, cells // CHUNK, encode, (zeros8, zeros8))

    half_cells, quarter = cells // 2, cells // 4

    def pick(source):
        pieces = []
        for b in range(2):
            value = source[pl.ds(b, half_cells, stride=2), :]
            value = value.reshape(height // 2, 2, width // 2, c)
            pieces.append([value[:, a].reshape(quarter, c) for a in range(2)])
        return [pieces[b][a] for a in range(2) for b in range(2)]

    def place_cells(target, pieces):
        for b in range(2):
            both = [pieces[2 * a + b].reshape(height // 2, 1, width // 2, c) for a in range(2)]
            value = jnp.concatenate(both, axis=1).reshape(half_cells, c)
            target[pl.ds(b, half_cells, stride=2), :] = value

    x_down = scratch.x_down
    for k, piece in enumerate(pick(encoded)):
        high, low = split(piece)
        x_down[:, k * c : (k + 1) * c] = high
        x_down[:, (k + 4) * c : (k + 5) * c] = low
    lowered = fold(dot(x_down[...], scratch.f_down[...])) + inputs.reducer_bias[...]
    x_up = scratch.x_up
    high, low = split(lowered)
    x_up[:, 0:c] = high
    x_up[:, c : 2 * c] = low
    raised = scratch.raised
    up_bias = inputs.up_bias[...]
    place_cells(
        raised, [fold(dot(x_up[...], scratch.f_up[k])) + up_bias for k in range(4)]
    )

    def raise_row(h, carry):
        value = raised[row_at(h), :]
        high, low = split(value)
        joined[row_at(h), 0:c] = high
        joined[row_at(h), 2 * c : 3 * c] = low
        put_turned(scratch.turned, row_at(h), value, 0, 2)
        return carry[0] + tile_sums(value), carry[1] + tile_sums(value * value)

    sums_raised = grid_rows(raise_row, (zeros8, zeros8))

    halves = []
    for half, (source, sums) in enumerate(((raised, sums_raised), (encoded, sums_enc))):
        mean, inv = norm_of(*sums, ones32, count32)
        gain = inputs.dec_norm1_gain[half : half + 1, :]
        bias = inputs.dec_norm1_bias[half : half + 1, :]
        scale = inv * gain
        activate(
            source,
            (scratch.xd1a, scratch.xd1b)[half],
            scratch.td1.at[2 * c * half : 2 * c * (half + 1)],
            (scratch.slope_d1a, scratch.slope_d1b)[half],
            scale,
            bias - mean * scale,
        )
        halves.append((source, mean, inv, gain))
    middle_d = scratch.middle_d
    pairs = [(scratch.xd1a, scratch.fd1a), (scratch.xd1b, scratch.fd1b)]
    mean_d2, inv_d2 = norm_of(*conv_norm(pairs, middle_d), ones16, count16)
    cot_swap.third()
    gain_d2, bias_d2 = inputs.dec_norm2_gain[...], inputs.dec_norm2_bias[...]
    a_d2 = inv_d2 * gain_d2
    activate(
        middle_d,
        scratch.xd2,
        scratch.td2,
        scratch.slope_d2,
        a_d2 * (1.0 + dec_scale),
        (bias_d2 - mean_d2 * a_d2) * (1.0 + dec_scale) + dec_shift,
    )
    exchanges = []
    waiting_runs = list(runs)
    landing_at = 0
    sem_at = 3 * (line - 1) + 20
    sums = scratch.sums

    def begin():
        nonlocal landing_at, sem_at
        start, rows = waiting_runs.pop(0)
        kind = Exchange if waiting_runs else SmallExchange
        exchange = kind(place, start, rows, landing_at, sem_at)
        landing_at += exchange.land_rows()
        sem_at += exchange.count()
        exchanges.append(exchange)
        exchange.advance()

    def advance(k):
        exchange = exchanges[k]
        exchange.advance()

    due = list(DUE)

    def point():
        for k in due.pop(0):
            advance(k)

    def small_row(k, value):
        sums[small_at + k : small_at + k + 1, :] = value

    def spread_grad(source):
        def step(h, carry):
            value = source[row_at(h), :]
            put_row(scratch.xg, h, value)
            return carry + tile_sums(value)

        return grid_rows(step, zeros8)

    def weight_grad(turned, at, depth, a):
        rows = pl.ds((2 - a) * width, cells)
        both = dot(turned[...], scratch.xg[rows, :])
        for half in range(depth // c):
            part = fold_rows(both[2 * c * half : 2 * c * (half + 1)])
            for b in range(3):
                high, low = HIGH_AT[2 - b] * c, LOW_AT[2 - b] * c
                to = at + (3 * a + b) * depth + half * c
                sums[to : to + c, :] = part[:, high : high + c] + part[:, low : low + c]

    def back_conv(weight, slope, target, source, mean, inv):
        carry = (zeros8, zeros8)
        for i in range(cells // CHUNK):
            value = fold(conv_chunk([(scratch.xg, weight)], i)) * slope[chunk_at(i), :]
            target[chunk_at(i), :] = value
            normed = (source[chunk_at(i), :] - mean) * inv
            carry = (carry[0] + tile_sums(value), carry[1] + tile_sums(value * normed))
            if i % (cells // CHUNK // 2) == cells // CHUNK // 2 - 1:
                point()
        return carry

    def norm_grad(sums_in, scale, ones, count):
        one, two = group_sums(sums_in[0] * scale, sums_in[1] * scale, ones)
        return one / count, two / count

    cot[here_rows] = cot_from[row]
    cot_swap.arrive()
    total_cot = column_sum(spread_grad(cot))
    for a in range(3):
        weight_grad(scratch.td2, starts.dec_conv2, c, a)
    part = fold(dot(scratch.turned[...], scratch.xg[width : cells + width, 2 * c : 4 * c]))
    sums[starts.skip_weight : starts.skip_weight + 2 * c, :] = fold_rows(part)
    small_row(3, total_cot)
    begin()

    result = scratch.result
    last_bias = inputs.dec_conv2_bias[...] + inputs.skip_bias[...]

    def decode(i, carry):
        value = conv_chunk([(scratch.xd2, scratch.fd2)], i)
        value = value + dot(joined[chunk_at(i), :], scratch.f_skip[...])
        result[chunk_at(i), :] = fold(value) + last_bias
        return carry

    lax.fori_loop(0, cells // CHUNK, decode, 0)
    output_here, frames_here = outputs.output, outputs.frames_grad
    output_here[row] = result[here_rows]
    output_swap = LineSwap(
        place.line,
        lambda to: strip_of(result, to),
        lambda source: output_here.at[source],
        scratch.output_inward,
        scratch.output_across,
        make,
    )
    output_swap.first()

    point()

    grad = scratch.grad
    stack_turned(scratch.dec_conv2, 0, c, scratch.bd2)
    sums_d2 = back_conv(scratch.bd2, scratch.slope_d2, grad, middle_d, mean_d2, inv_d2)
    side_grads = (scratch.grad_a, scratch.grad_b)
    for half in range(2):

        def skip_back(i, carry, half=half):
            rows = pl.ds(pl.multiple_of(i * CHUNK + width, width), CHUNK)
            value = dot(scratch.xg[rows, 2 * c : 4 * c], scratch.b_skip[half])
            side_grads[half][chunk_at(i), :] = fold(value)
            return carry

        lax.fori_loop(0, cells // CHUNK, skip_back, 0)
    point()

    def table_rows(k, sums_in, gain, bias, one_plus):
        plain, times = column_sum(sums_in[0]), column_sum(sums_in[1])
        for s in range(inputs.enc_step_table.shape[0]):
            small_row(k + 2 * s, jnp.where(step_here == s, gain * times + bias * plain, 0.0))
            small_row(k + 2 * s + 1, jnp.where(step_here == s, plain, 0.0))
        return one_plus * times, one_plus * plain

    def middle_grad(source, mean, inv, scale, sums_in):
        zero, slope = norm_grad(sums_in, scale, ones16, count16)

        def step(h, carry):
            normed = (source[row_at(h), :] - mean) * inv
            value = inv * (grad[row_at(h), :] * scale - zero - normed * slope)
            put_row(scratch.xg, h, value)
            return carry

        grid_rows(step)

    gain_row, bias_row = table_rows(16, sums_d2, gain_d2, bias_d2, 1.0 + dec_scale)
    small_row(8, gain_row)
    small_row(9, bias_row)
    middle_grad(middle_d, mean_d2, inv_d2, gain_d2 * (1.0 + dec_scale), sums_d2)
    point()
    for a in range(3):
        weight_grad(scratch.td1, starts.dec_conv1, 2 * c, a)
        point()
        begin()

    output_swap.second()
    for half, (source, mean, inv, gain) in enumerate(halves):
        stack_turned(scratch.dec_conv1, half, 2 * c, (scratch.bd1a, scratch.bd1b)[half])
        sums_in = back_conv(
            (scratch.bd1a, scratch.bd1b)[half],
            (scratch.slope_d1a, scratch.slope_d1b)[half],
            grad,
            source,
            mean,
            inv,
        )
        small_row(4 + half, column_sum(sums_in[1]))
        small_row(6 + half, column_sum(sums_in[0]))
        zero, slope = norm_grad(sums_in, gain, ones32, count32)
        target = side_grads[half]

        def input_grad(h, carry):
            normed = (source[row_at(h), :] - mean) * inv
            value = inv * (grad[row_at(h), :] * gain - zero - normed * slope)
            value = target[row_at(h), :] + value
            target[row_at(h), :] = value
            return carry + tile_sums(value)

        total = grid_rows(input_grad, zeros8)
        if half == 0:
            small_row(2, column_sum(total))
        point()

    grad_raised, grad_encoded = side_grads
    x_grad_up = scratch.x_grad_up
    for k, piece in enumerate(pick(grad_raised)):
        high, low = split(piece)
        x_grad_up[:, k * c : (k + 1) * c] = high
        x_grad_up[:, (k + 4) * c : (k + 5) * c] = low
    grad_lowered = fold(dot(x_grad_up[...], scratch.b_up[...]))
    small_row(1, jnp.sum(grad_lowered, axis=0, keepdims=True))
    x_grad_low = scratch.x_grad_low
    high, low = split(grad_lowered)
    x_grad_low[:, 0:c] = high
    x_grad_low[:, c : 2 * c] = low
    point()
    part = fold(fold_rows(dot(x_up[...], x_grad_up[...], TN)))
    for k in range(4):
        at = starts.up_weight + k * c
        sums[at : at + c, :] = part[:, k * c : (k + 1) * c]
    part = fold_rows(fold(dot(x_down[...], x_grad_low[...], TN)))
    sums[starts.reducer_weight : starts.reducer_weight + 4 * c, :] = part
    point()
    begin()
    place_cells(
        grad, [fold(dot(x_grad_low[...], scratch.b_down[k])) for k in range(4)]
    )

    output_swap.third()
    def join_row(h, carry):
        value = grad_encoded[row_at(h), :] + grad[row_at(h), :]
        grad_encoded[row_at(h), :] = value
        put_row(scratch.xg, h, value)
        return carry + tile_sums(value)

    small_row(0, column_sum(grid_rows(join_row, zeros8)))
    for k in range(10, 16):
        small_row(k, jnp.zeros((1, c), F32))
    sums[small_at + 24 : small_at + LATE, :] = jnp.zeros((LATE - 24, c), F32)
    point()
    for a in range(3):
        weight_grad(scratch.te2, starts.enc_conv2, c, a)
        point()
    begin()
    stack_turned(scratch.enc_conv2, 0, c, scratch.be2)
    sums_e2 = back_conv(scratch.be2, scratch.slope_e2, grad, middle_e, mean_e2, inv_e2)
    gain_row, bias_row = table_rows(LATE + 24, sums_e2, gain_e2, bias_e2, 1.0 + enc_scale)
    small_row(LATE + 18, gain_row)
    small_row(LATE + 19, bias_row)
    middle_grad(middle_e, mean_e2, inv_e2, gain_e2 * (1.0 + enc_scale), sums_e2)
    point()
    for a in range(3):
        weight_grad(scratch.te1, starts.enc_conv1, c, a)
        point()
        if a:
            begin()
    stack_turned(scratch.enc_conv1, 0, c, scratch.be1)
    sums_e1 = back_conv(scratch.be1, scratch.slope_e1, grad, lifted, mean_e1, inv_e1)
    small_row(LATE + 16, column_sum(sums_e1[1]))
    small_row(LATE + 17, column_sum(sums_e1[0]))
    zero, slope = norm_grad(sums_e1, gain_e1, ones16, count16)

    def lifted_grad(h, carry):
        normed = (lifted[row_at(h), :] - mean_e1) * inv_e1
        value = inv_e1 * (grad[row_at(h), :] * gain_e1 - zero - normed * slope)
        grad[row_at(h), :] = grad_encoded[row_at(h), :] + value
        return carry

    grid_rows(lifted_grad)
    point()

    late_at = small_at + LATE
    sums[late_at : late_at + 16, :] = dot_three(fields[...], grad[...])
    sums[late_at + 20 : late_at + 24, :] = jnp.zeros((4, c), F32)
    point()
    begin()
    back = dot_three(lift[...], grad[...], NT)
    frames_out = scratch.frames_out
    for source in range(line):
        for k in range(strip):
            h = source * strip + k
            value = back[0:history, h * width : (h + 1) * width]
            frames_out[source, :, k, :] = value * keep * masks[h]
    frames_here[row] = frames_out[row]
    for k in range(1, line):
        to = lax.rem(row + k, line)
        output_copies.append(
            send(frames_out.at[to], frames_here.at[row], device_at(to))
        )

    output_swap.arrive()
    for k in REST:
        advance(k)
    assert not due and all(exchange.done() for exchange in exchanges)

    for copy in output_copies:
        copy.wait_recv()
    for copy in frame_copies + output_copies:
        copy.wait_send()
    cot_swap.sent()
    output_swap.sent()
    for exchange in exchanges:
        for copy, only in exchange.copies:
            if only is None:
                copy.wait_send()
            else:
                pl.when(only)(copy.wait_send)


def write_kernel(layout, *refs):
    shapes, starts, small_at = layout
    output, frames_grad, gradients_here = refs[:3]
    outputs = refs[3:-1]
    sem = refs[-1]
    c = gradients_here.shape[1]
    leaving = []

    def leave(source, target):
        leaving.append(pltpu.make_async_copy(source, target, sem.at[len(leaving)]))
        leaving[-1].start()

    for k, name in enumerate(LARGE):
        rows = pl.ds(starts[name], shapes[name][0])
        leave(gradients_here.at[rows], outputs[2 + k])
    for target, (k, rows) in zip(outputs[2 + len(LARGE) :], SMALL_ROWS.values()):
        at = small_at + k
        if rows == 8:
            for s in range(target.shape[0]):
                target[s : s + 1, 0:c] = gradients_here[at + 2 * s : at + 2 * s + 1, :]
                target[s : s + 1, c : 2 * c] = gradients_here[at + 2 * s + 1 : at + 2 * s + 2, :]
        else:
            target[...] = gradients_here[at : at + rows, :]
    leave(output, outputs[0])
    leave(frames_grad, outputs[1])
    for copy in leaving:
        copy.wait()


def whole_items(shape, *arguments):
    line = shape["rows"]
    whole = Given(*arguments)
    given = whole._asdict()
    frames, cotangent = whole.frames, whole.cotangent
    items, history, strip, width = frames.shape
    c = cotangent.shape[-1]
    cells = strip * line * width
    flat = {}
    for name, value in given.items():
        if value is cotangent:
            value = value.reshape(items, strip * width, c)
        elif name in LARGE:
            value = value.reshape(-1, c)
        elif value.ndim == 1 and name not in IN_SMEM:
            value = value.reshape(-1, c)
        flat[name] = value
    shapes = {name: flat[name].shape for name in LARGE}
    big_layout = layout_of(SimpleNamespace(**shapes))
    starts, small_at, total_rows, runs = big_layout
    copies = 20 + 3 * (line - 1) + len(runs) * (6 + 2 * PIECES + 2 * (line - 1)) + 6
    landing = sum(rows // 2 + 5 * rows // 8 for _, rows in runs) + LATE_COUNT * (8 + line)
    shifted = pltpu.VMEM((cells + 2 * width, 6 * c), BF16)
    forward = pltpu.VMEM((18 * c, 2 * c), BF16)
    backward = forward
    field = pltpu.VMEM((cells, c), F32)
    flipped_field = pltpu.VMEM((2 * c, cells), BF16)
    quarter = cells // 4
    scratch = dict(
        small=pltpu.VMEM((LATE_COUNT, c), F32),
        send=pltpu.SemaphoreType.DMA((copies,)),
        recv=pltpu.SemaphoreType.DMA((copies,)),
        local=pltpu.SemaphoreType.DMA((12 + len(runs),)),
        sums=pltpu.VMEM((total_rows, c), F32),
        landing=pltpu.VMEM((landing, c), F32),
        frames_in=pltpu.VMEM((line, history, strip, width), F32),
        mask_in=pltpu.VMEM((line, strip, width), jnp.int32),
        frames_out=pltpu.VMEM((line, history, strip, width), F32),
        frames_from=pltpu.VMEM((line, history, strip, width), F32),
        mask_from=pltpu.VMEM((line, strip, width), jnp.int32),
        cot_from=pltpu.VMEM((items, strip * width, c), F32),
        cot_inward=pltpu.VMEM((2, strip * width, c), F32),
        cot_across=pltpu.VMEM((2, strip * width, c), F32),
        output_inward=pltpu.VMEM((2, strip * width, c), F32),
        output_across=pltpu.VMEM((2, strip * width, c), F32),
        fields=pltpu.VMEM((16, cells), F32),
        lift=pltpu.VMEM((16, c), F32),
        joined=pltpu.VMEM((cells, 4 * c), BF16),
        x_down=pltpu.VMEM((quarter, 8 * c), BF16),
        x_grad_up=pltpu.VMEM((quarter, 8 * c), BF16),
        x_up=pltpu.VMEM((quarter, 2 * c), BF16),
        x_grad_low=pltpu.VMEM((quarter, 2 * c), BF16),
        f_down=pltpu.VMEM((8 * c, 2 * c), BF16),
        b_down=pltpu.VMEM((4, 2 * c, 2 * c), BF16),
        f_up=pltpu.VMEM((4, 2 * c, 2 * c), BF16),
        b_up=pltpu.VMEM((8 * c, 2 * c), BF16),
        f_skip=pltpu.VMEM((4 * c, 2 * c), BF16),
        b_skip=pltpu.VMEM((2, 2 * c, 2 * c), BF16),
        xe1=shifted,
        xe2=shifted,
        xd1a=shifted,
        xd1b=shifted,
        xd2=shifted,
        xg=shifted,
        te1=flipped_field,
        te2=flipped_field,
        td1=pltpu.VMEM((4 * c, cells), BF16),
        td2=flipped_field,
        turned=pltpu.VMEM((4 * c, cells), BF16),
        fe1=forward,
        fe2=forward,
        fd1a=forward,
        fd1b=forward,
        fd2=forward,
        be1=backward,
        be2=backward,
        bd1a=backward,
        bd1b=backward,
        bd2=backward,
        slope_e1=field,
        slope_e2=field,
        slope_d1a=field,
        slope_d1b=field,
        slope_d2=field,
        lifted=field,
        middle_e=field,
        encoded=field,
        raised=field,
        middle_d=field,
        result=field,
        cot=field,
        grad=field,
        grad_a=field,
        grad_b=field,
    )
    scratch.update({name: pltpu.VMEM(shapes[name], F32) for name in LARGE})

    in_hbm = pl.BlockSpec(memory_space=pl.ANY)
    in_vmem = pl.BlockSpec(memory_space=pltpu.VMEM)
    in_smem = pl.BlockSpec(memory_space=pltpu.SMEM)
    in_specs = [
        in_hbm if name in IN_HBM else in_smem if name in IN_SMEM else in_vmem
        for name in ARGUMENTS
    ]
    out_shape = [
        pltpu.VMEM((items, strip * width, c), F32),
        pltpu.VMEM(frames.shape, F32),
        pltpu.VMEM((total_rows, c), F32),
    ]
    out_specs = [in_vmem] * 3
    results = pl.pallas_call(
        functools.partial(
            item_kernel,
            (line, strip, width, shapes, big_layout),
            tuple(scratch),
        ),
        out_shape=out_shape,
        in_specs=in_specs,
        out_specs=out_specs,
        scratch_shapes=list(scratch.values()),
        compiler_params=pltpu.CompilerParams(
            collective_id=0, has_side_effects=True, vmem_limit_bytes=56 * 1024 * 1024
        ),
    )(*[flat[name] for name in ARGUMENTS])
    names = LARGE + tuple(SMALL_ROWS)
    written = pl.pallas_call(
        functools.partial(write_kernel, (shapes, starts, small_at)),
        out_shape=[
            jax.ShapeDtypeStruct((items, strip * width, c), F32),
            jax.ShapeDtypeStruct(frames.shape, F32),
        ]
        + [jax.ShapeDtypeStruct(flat[name].shape, F32) for name in names],
        in_specs=[in_vmem] * 3,
        out_specs=[in_hbm] * (2 + len(LARGE)) + [in_vmem] * len(SMALL_ROWS),
        scratch_shapes=[pltpu.SemaphoreType.DMA((2 + len(LARGE),))],
        compiler_params=pltpu.CompilerParams(vmem_limit_bytes=16 * 1024 * 1024),
    )(*results)
    grads = dict(zip(names, written[2:]))
    ordered = [name for name in ARGUMENTS if name in grads]
    return (written[0].reshape(cotangent.shape), written[1]) + tuple(
        grads[name].reshape(given[name].shape) for name in ordered
    )


def body(shape, *arguments):
    items, _, strip, width = arguments[0].shape
    line = shape["rows"]
    whole = (
        shape["section"] == 2
        and shape["batch"] == 4
        and items == line == 4
        and arguments[-1].shape[-1] == 128
        and (strip * line * width) % CHUNK == 0
    )
    return whole_items(shape, *arguments) if whole else strips_body(*arguments)


def solution(mesh):
    in_specs = (
        P(("section", "batch"), None, "rows", None),
        P(("section", "batch")),
        P(("section", "batch"), "rows", None),
        P(("section", "batch")),
        P(),
        P(),
        P(),
        P(),
        P(),
        P(),
        P(),
        P(),
        P(),
        P(),
        P(),
        P(),
        P(),
        P(),
        P(),
        P(),
        P(),
        P(),
        P(),
        P(),
        P(),
        P(),
        P(),
        P(),
        P(("section", "batch"), "rows", None, None),
    )
    out_specs = (
        P(("section", "batch"), "rows", None, None),
        P(("section", "batch"), None, "rows", None),
        P(),
        P(),
        P(),
        P(),
        P(),
        P(),
        P(),
        P(),
        P(),
        P(),
        P(),
        P(),
        P(),
        P(),
        P(),
        P(),
        P(),
        P(),
        P(),
        P(),
        P(),
        P(),
        P(),
        P(),
    )
    return jax.shard_map(functools.partial(body, mesh.shape), mesh=mesh, in_specs=in_specs, out_specs=out_specs, check_vma=False)
```

```python
import functools
from types import SimpleNamespace
from typing import Any, NamedTuple

import jax
import jax.numpy as jnp
from jax import lax
from jax.experimental import pallas as pl
from jax.experimental.pallas import tpu as pltpu
from jax.sharding import PartitionSpec as P

GROUPS = 8
FIELDS = 3
HIST = 4


EPS = 1e-05
HIGH = lax.Precision.HIGHEST


def extended(cells, sides, width):
    for axis, dim in sides:
        count = lax.axis_size(axis)
        ends = count - 1
        head = lax.slice_in_dim(cells, 0, width, axis=dim)
        tail = lax.slice_in_dim(cells, cells.shape[dim] - width, cells.shape[dim], axis=dim)
        cells = jnp.concatenate(
            [
                lax.ppermute(tail, axis, [(i, (i + 1) % count) for i in range(ends)]),
                cells,
                lax.ppermute(head, axis, [((i + 1) % count, i) for i in range(ends)]),
            ],
            axis=dim,
        )
    return cells


def from_behind(value, axis, steps):
    count = lax.axis_size(axis)
    pairs = [(source, (source + steps) % count) for source in range(count)]
    return lax.ppermute(value, axis, pairs)


def group_view(value_arrays):
    extent = value_arrays.shape
    return value_arrays.reshape(extent[:-1] + (GROUPS, extent[-1] // GROUPS))


def global_sums(value_arrays):
    grouped = group_view(value_arrays)
    flat = grouped.reshape(-1, GROUPS, grouped.shape[-1])
    first_sum = jnp.sum(flat, axis=(0, 2))
    second_sum = jnp.sum(flat * flat, axis=(0, 2))
    return lax.psum((first_sum, second_sum), "rows")


def apply_norm(value_arrays, sum_one, sum_two, norm_gain, norm_bias, total):
    grouped = group_view(value_arrays)
    group_mean = sum_one / total
    variance = sum_two / total - group_mean * group_mean
    inverse = lax.rsqrt(variance + EPS)
    normed = (grouped - group_mean[:, None]) * inverse[:, None]
    return normed.reshape(value_arrays.shape) * norm_gain + norm_bias


def norm_back(value_arrays, grad_one, grad_two):
    grouped = group_view(value_arrays)
    extra = grad_one[:, None] + 2.0 * grouped * grad_two[:, None]
    return extra.reshape(value_arrays.shape)


def reduce_grads(grad_one, grad_two):
    return lax.psum((grad_one, grad_two), "rows")


def conv_rows(padded, kernel):
    widened = jnp.pad(padded, ((0, 0), (1, 1), (0, 0)))
    return lax.conv_general_dilated(
        widened[None],
        kernel,
        (1, 1),
        "VALID",
        dimension_numbers=("NHWC", "HWIO", "NHWC"),
        precision=HIGH,
    )[0]


def flipped(kernel):
    return jnp.transpose(kernel[::-1, ::-1], (0, 1, 3, 2))


def pad_grads(value_arrays):
    return extended(value_arrays, (("rows", 0),), 1)


def totals_of(inputs, conv1):
    strip = inputs.shape[0]
    cells = strip * lax.axis_size("rows") * inputs.shape[1]
    return (cells * (inputs.shape[2] // GROUPS), cells * (conv1.shape[3] // GROUPS))


def block_forward(inputs, weights, scale_part, shift_part):
    norm1_gain, norm1_bias, conv1, norm2_gain, norm2_bias, conv2, conv2_bias = weights
    total_in, total_mid = totals_of(inputs, conv1)
    sums_in = global_sums(inputs)

    def pad_rows(value_arrays):
        return extended(value_arrays, (("rows", 0),), 1)

    act_one = pad_rows(
        jax.nn.gelu(
            apply_norm(inputs, sums_in[0], sums_in[1], norm1_gain, norm1_bias, total_in),
            approximate=False,
        )
    )
    middle = conv_rows(act_one, conv1)
    sums_mid = global_sums(middle)
    shaped = (
        apply_norm(middle, sums_mid[0], sums_mid[1], norm2_gain, norm2_bias, total_mid)
        * (1.0 + scale_part)
        + shift_part
    )
    act_two = pad_rows(jax.nn.gelu(shaped, approximate=False))
    branch = conv_rows(act_two, conv2) + conv2_bias
    return (branch, (sums_in[0], sums_in[1], act_one, middle, sums_mid[0], sums_mid[1], act_two))


def block_backward(inputs, weights, scale_part, shift_part, kept, grad_out):
    norm1_gain, norm1_bias, conv1, norm2_gain, norm2_bias, conv2, conv2_bias = weights
    in_one, in_two, act_one, middle, mid_one, mid_two, act_two = kept
    total_in, total_mid = totals_of(inputs, conv1)
    grad_conv2 = jax.vjp(lambda kernel: conv_rows(act_two, kernel), conv2)[1](grad_out)[0]
    grad_bias2 = jnp.sum(grad_out, axis=(0, 1))
    grad_act_two = conv_rows(pad_grads(grad_out), flipped(conv2))

    def second_piece(middle_in, sum_one, sum_two, gain_in, incoming_bias, scale_in, shift_in):
        shaped = (
            apply_norm(middle_in, sum_one, sum_two, gain_in, incoming_bias, total_mid)
            * (1.0 + scale_in)
            + shift_in
        )
        return jax.nn.gelu(shaped, approximate=False)

    second_pull = jax.vjp(
        second_piece, middle, mid_one, mid_two, norm2_gain, norm2_bias, scale_part, shift_part
    )[1](grad_act_two)
    summed_one, summed_two = reduce_grads(second_pull[1], second_pull[2])
    grad_middle = second_pull[0] + norm_back(middle, summed_one, summed_two)
    grad_conv1 = jax.vjp(lambda kernel: conv_rows(act_one, kernel), conv1)[1](grad_middle)[0]
    grad_act_one = conv_rows(pad_grads(grad_middle), flipped(conv1))

    def first_piece(inputs_in, sum_one, sum_two, gain_in, incoming_bias):
        return jax.nn.gelu(
            apply_norm(inputs_in, sum_one, sum_two, gain_in, incoming_bias, total_in),
            approximate=False,
        )

    first_pull = jax.vjp(first_piece, inputs, in_one, in_two, norm1_gain, norm1_bias)[1](
        grad_act_one
    )
    first_one, first_two = reduce_grads(first_pull[1], first_pull[2])
    grad_inputs = first_pull[0] + norm_back(inputs, first_one, first_two)
    grads = (
        first_pull[3],
        first_pull[4],
        grad_conv1,
        second_pull[3],
        second_pull[4],
        grad_conv2,
        grad_bias2,
    )
    return (grad_inputs, grads, second_pull[5], second_pull[6])


def conditioning(step_item, table):
    one_hot = (jnp.arange(table.shape[0], dtype=jnp.int32) == step_item).astype(jnp.float32)
    condition = jnp.dot(one_hot, table, precision=HIGH)
    half_width = table.shape[1] // 2
    return (condition[:half_width], condition[half_width:], one_hot)


def project_in(frames_item, mask_item, count_item, incoming_weight, incoming_bias):
    history = jnp.arange(HIST, dtype=jnp.int32) >= HIST - count_item
    keep = jnp.repeat(history, FIELDS).astype(jnp.float32)
    lifted = (
        jnp.einsum(
            "fhw,fc->hwc", frames_item * keep[:, None, None], incoming_weight, precision=HIGH
        )
        + incoming_bias
    )
    return lifted * mask_item[:, :, None].astype(jnp.float32)


def coarsen_field(value_arrays, incoming_weight, incoming_bias):
    rows_here, width_here, depth_here = value_arrays.shape
    blocks = value_arrays.reshape(rows_here // 2, 2, width_here // 2, 2, depth_here)
    return jnp.einsum("iajbk,abkc->ijc", blocks, incoming_weight, precision=HIGH) + incoming_bias


def upsample(value_arrays, incoming_weight, incoming_bias):
    result = jnp.einsum("ijk,abkc->iajbc", value_arrays, incoming_weight, precision=HIGH)
    extent = result.shape
    return result.reshape(extent[0] * 2, extent[2] * 2, extent[4]) + incoming_bias


def flatten_all(pieces):
    return jnp.concatenate([piece.reshape(-1) for piece in pieces])


def unflatten_all(flat, templates):
    pieces = []
    offset_at = 0
    for template in templates:
        count_here = template.size
        pieces.append(flat[offset_at : offset_at + count_here].reshape(template.shape))
        offset_at += count_here
    return tuple(pieces)


def strips_body(
    frames,
    counts,
    cell_mask,
    step_index,
    lift_weight,
    lift_bias,
    enc_norm1_gain,
    enc_norm1_bias,
    enc_conv1,
    enc_step_table,
    enc_norm2_gain,
    enc_norm2_bias,
    enc_conv2,
    enc_conv2_bias,
    reducer_weight,
    reducer_bias,
    up_weight,
    up_bias,
    dec_norm1_gain,
    dec_norm1_bias,
    dec_conv1,
    dec_step_table,
    dec_norm2_gain,
    dec_norm2_bias,
    dec_conv2,
    dec_conv2_bias,
    skip_weight,
    skip_bias,
    cotangent,
):
    enc_weights = (
        enc_norm1_gain,
        enc_norm1_bias,
        enc_conv1,
        enc_norm2_gain,
        enc_norm2_bias,
        enc_conv2,
        enc_conv2_bias,
    )
    dec_weights = (
        dec_norm1_gain,
        dec_norm1_bias,
        dec_conv1,
        dec_norm2_gain,
        dec_norm2_bias,
        dec_conv2,
        dec_conv2_bias,
    )
    params = (
        lift_weight,
        lift_bias,
        enc_norm1_gain,
        enc_norm1_bias,
        enc_conv1,
        enc_step_table,
        enc_norm2_gain,
        enc_norm2_bias,
        enc_conv2,
        enc_conv2_bias,
        reducer_weight,
        reducer_bias,
        up_weight,
        up_bias,
        dec_norm1_gain,
        dec_norm1_bias,
        dec_conv1,
        dec_step_table,
        dec_norm2_gain,
        dec_norm2_bias,
        dec_conv2,
        dec_conv2_bias,
        skip_weight,
        skip_bias,
    )

    def forward_micro(carry, sliced):
        frames_item, mask_item, count_item, step_item = sliced
        lifted = project_in(frames_item, mask_item, count_item, lift_weight, lift_bias)
        enc_scale, enc_shift, unused_hot = conditioning(step_item, enc_step_table)
        enc_branch, enc_kept = block_forward(lifted, enc_weights, enc_scale, enc_shift)
        encoder_result = lifted + enc_branch
        coarse_field = coarsen_field(encoder_result, reducer_weight, reducer_bias)
        foreign = from_behind(coarse_field, "section", 1)
        raised_foreign = upsample(foreign, up_weight, up_bias)
        raised = from_behind(raised_foreign, "section", 1)
        joined = jnp.concatenate([raised, encoder_result], axis=-1)
        dec_scale, dec_shift, unused_again = conditioning(step_item, dec_step_table)
        dec_branch, dec_kept = block_forward(joined, dec_weights, dec_scale, dec_shift)
        output_item = jnp.dot(joined, skip_weight, precision=HIGH) + skip_bias + dec_branch
        return (carry, (output_item, (lifted, enc_kept, encoder_result, foreign, joined, dec_kept)))

    unused, (output, kept_all) = lax.scan(
        forward_micro, jnp.zeros((), jnp.float32), (frames, cell_mask, counts, step_index)
    )

    def backward_micro(totals, sliced):
        frames_item, mask_item, count_item, step_item, grad_out, kept = sliced
        lifted, enc_kept, encoder_result, foreign, joined, dec_kept = kept
        dec_scale, dec_shift, one_hot = conditioning(step_item, dec_step_table)
        grad_joined, dec_grads, dec_gscale, dec_gshift = block_backward(
            joined, dec_weights, dec_scale, dec_shift, dec_kept, grad_out
        )
        grad_skip_weight = jnp.einsum("hwk,hwc->kc", joined, grad_out, precision=HIGH)
        grad_skip_bias = jnp.sum(grad_out, axis=(0, 1))
        grad_joined = grad_joined + jnp.dot(grad_out, skip_weight.T, precision=HIGH)
        half_width = joined.shape[-1] // 2
        grad_raised = grad_joined[..., :half_width]
        grad_encoded = grad_joined[..., half_width:]
        grad_foreign_up = from_behind(grad_raised, "section", 1)
        up_pull = jax.vjp(upsample, foreign, up_weight, up_bias)[1](grad_foreign_up)
        coarse_gradient = from_behind(up_pull[0], "section", 1)
        reducer_pullback = jax.vjp(coarsen_field, encoder_result, reducer_weight, reducer_bias)[1](
            coarse_gradient
        )
        grad_encoded = grad_encoded + reducer_pullback[0]
        enc_scale, enc_shift, enc_hot = conditioning(step_item, enc_step_table)
        grad_lifted, enc_grads, enc_gscale, enc_gshift = block_backward(
            lifted, enc_weights, enc_scale, enc_shift, enc_kept, grad_encoded
        )
        grad_lifted = grad_lifted + grad_encoded
        proj_pull = jax.vjp(
            lambda frames_in, incoming_weight, incoming_bias: project_in(
                frames_in, mask_item, count_item, incoming_weight, incoming_bias
            ),
            frames_item,
            lift_weight,
            lift_bias,
        )[1](grad_lifted)
        enc_table_grad = enc_hot[:, None] * jnp.concatenate([enc_gscale, enc_gshift])[None, :]
        dec_table_grad = one_hot[:, None] * jnp.concatenate([dec_gscale, dec_gshift])[None, :]
        micro_list = (
            proj_pull[1],
            proj_pull[2],
            enc_grads[0],
            enc_grads[1],
            enc_grads[2],
            enc_table_grad,
            enc_grads[3],
            enc_grads[4],
            enc_grads[5],
            enc_grads[6],
            reducer_pullback[1],
            reducer_pullback[2],
            up_pull[1],
            up_pull[2],
            dec_grads[0],
            dec_grads[1],
            dec_grads[2],
            dec_table_grad,
            dec_grads[3],
            dec_grads[4],
            dec_grads[5],
            dec_grads[6],
            grad_skip_weight,
            grad_skip_bias,
        )
        micro_flat = flatten_all(micro_list)
        return (totals + micro_flat, proj_pull[0])

    total_size = sum((piece.size for piece in params))
    start_totals = jnp.zeros((total_size,), jnp.float32)
    flat_totals, frames_grad = lax.scan(
        backward_micro,
        start_totals,
        (frames, cell_mask, counts, step_index, cotangent, kept_all),
        reverse=True,
    )
    flat_totals = lax.psum(flat_totals, ("section", "batch", "rows"))
    grads = unflatten_all(flat_totals, params)
    return (output, frames_grad) + grads


F32 = jnp.float32
BF16 = jnp.bfloat16
MESH = pl.DeviceIdType.MESH
NN = ((1,), (0,))
NT = ((1,), (1,))
TN = ((0,), (0,))
HIGH_AT = (0, 2, 1)
LOW_AT = (4, 3, 5)
CHUNK = 512
class Given(NamedTuple):
    frames: Any
    counts: Any
    cell_mask: Any
    step_index: Any
    lift_weight: Any
    lift_bias: Any
    enc_norm1_gain: Any
    enc_norm1_bias: Any
    enc_conv1: Any
    enc_step_table: Any
    enc_norm2_gain: Any
    enc_norm2_bias: Any
    enc_conv2: Any
    enc_conv2_bias: Any
    reducer_weight: Any
    reducer_bias: Any
    up_weight: Any
    up_bias: Any
    dec_norm1_gain: Any
    dec_norm1_bias: Any
    dec_conv1: Any
    dec_step_table: Any
    dec_norm2_gain: Any
    dec_norm2_bias: Any
    dec_conv2: Any
    dec_conv2_bias: Any
    skip_weight: Any
    skip_bias: Any
    cotangent: Any


ARGUMENTS = Given._fields
LARGE = tuple(
    dict(
        dec_conv1=0,
        up_weight=0,
        reducer_weight=0,
        dec_conv2=0,
        skip_weight=0,
        enc_conv1=0,
        enc_conv2=0,
    )
)
IN_HBM = tuple(dict(frames=0, cell_mask=0, cotangent=0)) + LARGE
IN_SMEM = tuple(dict(counts=0, step_index=0))
LATE = 64
SMALL_ROWS = dict(
    enc_conv2_bias=(0, 1),
    reducer_bias=(1, 1),
    up_bias=(2, 1),
    dec_conv2_bias=(3, 1),
    skip_bias=(3, 1),
    dec_norm1_gain=(4, 2),
    dec_norm1_bias=(6, 2),
    dec_norm2_gain=(8, 1),
    dec_norm2_bias=(9, 1),
    dec_step_table=(16, 8),
    lift_weight=(LATE, 12),
    lift_bias=(LATE + 12, 1),
    enc_norm1_gain=(LATE + 16, 1),
    enc_norm1_bias=(LATE + 17, 1),
    enc_norm2_gain=(LATE + 18, 1),
    enc_norm2_bias=(LATE + 19, 1),
    enc_step_table=(LATE + 24, 8),
)
LATE_COUNT = 32
PIECES = 1
SMALL_COUNT = LATE + LATE_COUNT
DUE = ((), (), (), (), (0,), (), (), (), (1,), (2, 3, 0), (), (), (1,), (), (), (2, 0, 1), (), (3, 4), (2,), (0,), (3, 1), (5, 2, 4), (), (3, 0), (1,), (2, 4, 5, 3, 6), (7,), (), ())
REST = (4, 0, 5, 1, 8, 4, 0, 2, 1, 5, 3, 2, 6, 3, 5, 7, 8, 6, 7, 4, 6, 7, 4, 5, 6, 7, 5, 6, 7, 6, 7)
OUTPUTS = tuple(dict(output=0, frames_grad=0, gradients=0))


def split(value):
    high = value.astype(BF16)
    return high, (value - high.astype(F32)).astype(BF16)


def dot(left, right, dims=NN, precision=None):
    return lax.dot_general(
        left, right, (dims, ((), ())), precision=precision, preferred_element_type=F32
    )


def fold(value):
    half = value.shape[1] // 2
    return value[:, :half] + value[:, half:]


def fold_rows(value):
    half = value.shape[0] // 2
    return value[:half] + value[half:]


def tile_sums(value):
    return jnp.sum(value.reshape(-1, 8, value.shape[-1]), axis=0)


def column_sum(tiles):
    return jnp.sum(tiles, axis=0, keepdims=True)


def normal(value):
    bell = jnp.exp(-0.5 * value * value)
    t = 1.0 / (1.0 + 0.2316418882663604 * jnp.abs(value))
    poly = 0.5307027145
    for factor in (-0.7265760135, 0.7107068705, -0.142248368, 0.127414796):
        poly = poly * t + factor
    tail = poly * t * bell
    return jnp.where(value < 0.0, tail, 1.0 - tail), 0.3989422804014327 * bell


def dot_three(left, right, dims=NN):
    left_high, left_low = split(left)
    right_high, right_low = split(right)
    total = dot(left_high, right_high, dims)
    return total + (dot(left_high, right_low, dims) + dot(left_low, right_high, dims))


def group_ones(channels, size):
    rows = lax.broadcasted_iota(jnp.int32, (channels, channels), 0) // size
    columns = lax.broadcasted_iota(jnp.int32, (channels, channels), 1) // size
    return (rows == columns).astype(BF16)


def group_sums(first, second, ones):
    terms = []
    rest = jnp.concatenate([first, second], axis=0)
    for _ in range(3):
        term = rest.astype(BF16)
        terms.append(term)
        rest = rest - term.astype(F32)
    both = dot(jnp.concatenate(terms, axis=0), ones)
    both = both[32:48] + both[16:32] + both[:16]
    return column_sum(both[:8]), column_sum(both[8:])


class LineSwap:

    def __init__(self, line, source, target, inward, across, make):
        far = 3 - line.outer
        self.line = line
        to_inner, to_across = line.device(line.inner), line.device(line.across)
        to_outer = line.device(line.outer)
        here = target(line.here)
        self.to_far = make(source(3 - line.here), inward.at[1], to_inner)
        self.to_second = make(source(3 - line.inner), inward.at[0], to_inner)
        self.to_inner = make(source(line.inner), here, to_inner)
        self.for_far = make(source(far), across.at[0], to_across)
        self.to_across = make(source(line.across), here, to_across)
        self.to_outer = make(source(line.outer), here, to_outer)
        self.pass_far = make(inward.at[1], across.at[1], to_across)
        self.pass_second = make(inward.at[0], target(line.outer), to_across)
        self.pass_across = make(across.at[0], target(line.across), to_outer)
        self.pass_opposite = make(across.at[1], target(far), to_outer)

    def first(self):
        @pl.when(self.line.edge)
        def _():
            for copy in (self.to_far, self.to_second, self.to_inner):
                copy.start()

        @pl.when(self.line.middle)
        def _():
            for copy in (self.for_far, self.to_across, self.to_outer):
                copy.start()

    def second(self):
        @pl.when(self.line.middle)
        def _():
            self.for_far.wait_recv()
            self.pass_across.start()
            self.to_far.wait_recv()
            self.pass_far.start()
            self.to_second.wait_recv()
            self.pass_second.start()

    def third(self):
        @pl.when(self.line.middle)
        def _():
            self.pass_far.wait_recv()
            self.pass_opposite.start()

    def arrive(self):
        @pl.when(self.line.edge)
        def _():
            for copy in (self.to_outer, self.pass_across, self.pass_opposite):
                copy.wait_recv()

        @pl.when(self.line.middle)
        def _():
            for copy in (self.to_inner, self.to_across, self.pass_second):
                copy.wait_recv()

    def sent(self):
        @pl.when(self.line.edge)
        def _():
            for copy in (self.to_far, self.to_second, self.to_inner):
                copy.wait_send()

        @pl.when(self.line.middle)
        def _():
            for copy in (self.for_far, self.to_across, self.to_outer):
                copy.wait_send()
            for copy in (self.pass_far, self.pass_second, self.pass_across, self.pass_opposite):
                copy.wait_send()


class Exchange:

    def __init__(self, place, start, rows, landing, first_sem):
        self.place, self.start, self.rows, self.landing = place, start, rows, landing
        self.sem = first_sem
        self.stage = 0
        self.copies = []
        self.waiting = []
        self.group = place.plane_group
        self.half = rows // 2
        self.base = start + place.core * self.half
        self._finish(self.half)

    def _finish(self, size):
        self.part = size // self.group.count
        self.own = self.base + self.group.here * self.part

    def count(self):
        return 2 * PIECES + 2 * (self.group.count - 1) + 3

    def land_rows(self):
        return self.half + (self.group.count + 1) * self.part

    def _copy(self, source, target, device, only=None):
        place = self.place
        copy = pltpu.make_async_remote_copy(
            src_ref=source,
            dst_ref=target,
            send_sem=place.send.at[self.sem],
            recv_sem=place.recv.at[self.sem],
            device_id=device,
            device_id_type=MESH,
        )
        self.sem += 1
        if only is None:
            copy.start()
            self.waiting.append(copy)
        self.copies.append((copy, only))
        return copy

    def _pieces(self, source, at, target, to, size, device):
        each = size // 8 // PIECES * 8
        for k in range(PIECES):
            here = each if k < PIECES - 1 else size - each * (PIECES - 1)
            self._copy(
                source.at[self._rows(at + k * each, here)],
                target.at[self._rows(to + k * each, here)],
                device,
            )

    def _wait(self):
        for copy in self.waiting:
            copy.wait_recv()
        self.waiting = []

    def _rows(self, at, size):
        return pl.ds(pl.multiple_of(at, 8), size)

    def _swap(self):
        place = self.place
        other = self.start + (1 - place.core) * self.half
        self.land = self.landing
        self.landing += self.half
        self._pieces(place.sums, other, place.landing, self.land, self.half, place.partner)

    def _add_swap(self):
        place = self.place
        block = 64 if self.half % 64 == 0 else 32

        def step(i, carry):
            here = self._rows(self.base + i * block, block)
            there = self._rows(self.land + i * block, block)
            place.sums[here] = place.sums[here] + place.landing[there]
            return carry

        lax.fori_loop(0, self.half // block, step, 0)

    def _scatter(self, group, base, size):
        place = self.place
        self.land = self.landing
        for k in range(1, group.count):
            to = lax.rem(group.here + k, group.count)
            self._copy(
                place.sums.at[self._rows(base + to * size, size)],
                place.landing.at[pl.ds(self.landing, size)],
                group.device(to),
            )
            self.landing += size

    def _total(self, group, own, size, target):
        place = self.place
        block = 16 if size % 16 == 0 else 8

        def step(i, carry):
            here = self._rows(own + i * block, block)
            total = place.sums[here]
            for k in range(group.count - 1):
                there = self._rows(self.land + k * size + i * block, block)
                total = total + place.landing[there]
            target[here] = total
            return carry

        lax.fori_loop(0, size // block, step, 0)

    def _gather(self, group, own, size):
        final = self.place.final
        here = self._rows(own, size)
        for k in range(1, group.count):
            to = lax.rem(group.here + k, group.count)
            self._copy(final.at[here], final.at[here], group.device(to))

    def _steps(self):
        place, group = self.place, self.group
        yield self._swap()
        self._wait()
        self._add_swap()
        yield from self._both()
        self._pieces(place.final, self.base, place.final, self.base, self.half, place.partner)
        yield
        self._wait()
        yield

    def _both(self):
        place, group = self.place, self.group
        self._scatter(group, self.base, self.part)
        yield
        self._wait()
        self._total(group, self.own, self.part, place.sums)
        yield from self._line()
        self._gather(group, self.own, self.part)
        yield
        self._wait()

    def _line(self):
        place, line = self.place, self.place.line
        sums, final, landing = place.sums, place.final, place.landing
        part, own = self.part, self._rows(self.own, self.part)
        inward, across = pl.ds(self.landing, part), pl.ds(self.landing + part, part)
        self.landing += 2 * part
        block = 16 if part % 16 == 0 else 8

        def add(at, target):
            def step(i, carry):
                here = self._rows(self.own + i * block, block)
                target[here] = sums[here] + landing[pl.ds(at + i * block, block)]
                return carry

            lax.fori_loop(0, part // block, step, 0)

        first = self._copy(sums.at[own], landing.at[inward], line.device(line.inner), line.edge)
        second = self._copy(sums.at[own], landing.at[across], line.device(line.across), line.middle)
        third = self._copy(final.at[own], final.at[own], line.device(line.outer), line.middle)
        pl.when(line.edge)(first.start)
        yield

        @pl.when(line.middle)
        def _():
            first.wait_recv()
            add(self.landing - 2 * part, sums)
            second.start()

        yield

        @pl.when(line.middle)
        def _():
            second.wait_recv()
            add(self.landing - part, final)
            third.start()

        yield
        pl.when(line.edge)(third.wait_recv)

    def advance(self):
        if self.stage == 0:
            self.steps = self._steps()
        self.stage += 1
        next(self.steps)

    def done(self):
        return self.stage == 8


class SmallExchange(Exchange):

    def count(self):
        return self.place.cores_group.count + self.place.line.count - 2

    def land_rows(self):
        return self.rows * (self.place.cores_group.count + self.place.line.count)

    def _share(self, group, source):
        place = self.place
        self.land = self.landing
        self.landing += group.count * self.rows
        own = self._rows(self.land + group.here * self.rows, self.rows)
        place.landing[own] = source[...]
        for k in range(1, group.count):
            to = lax.rem(group.here + k, group.count)
            self._copy(source, place.landing.at[own], group.device(to))

    def _sum(self, group):
        total = None
        for k in range(group.count):
            part = self.place.landing[pl.ds(self.land + k * self.rows, self.rows)]
            total = part if total is None else total + part
        return total

    def _steps(self):
        place = self.place
        here = pl.ds(self.start, self.rows)
        self._share(place.line, place.sums.at[here])
        yield
        self._wait()
        place.small[...] = self._sum(place.line)
        self._share(place.cores_group, place.small)
        yield
        self._wait()
        place.final[here] = self._sum(place.cores_group)
        yield

    def done(self):
        return self.stage == 3


def layout_of(shapes):
    starts = {}
    at = 0
    for name in LARGE:
        starts[name] = at
        at += getattr(shapes, name)[0]
    small = at
    begins = SimpleNamespace(**starts)
    late = small + LATE
    tap = shapes.dec_conv2[0] // 3
    part = shapes.dec_conv1[0] // 3
    conv1, up = begins.dec_conv1, begins.up_weight
    edges = (
        (begins.dec_conv2, begins.enc_conv1),
        (conv1, conv1 + part),
        (conv1 + part, conv1 + 2 * part),
        (conv1 + 2 * part, up),
        (up, begins.dec_conv2),
        (begins.enc_conv2, late),
        (begins.enc_conv1, begins.enc_conv1 + 2 * tap),
        (begins.enc_conv1 + 2 * tap, begins.enc_conv2),
        (late, late + LATE_COUNT),
    )
    runs = [(first, last - first) for first, last in edges]
    return starts, small, late + LATE_COUNT, runs


def item_kernel(sizes, scratch_names, *refs):
    line, strip, width, shapes, big_layout = sizes
    begins, small_at, total_rows, runs = big_layout
    starts = SimpleNamespace(**begins)
    inputs = Given(*refs[: len(ARGUMENTS)])
    refs = refs[len(ARGUMENTS) :]
    output_names = OUTPUTS
    outputs = SimpleNamespace(**dict(zip(output_names, refs)))
    scratch = SimpleNamespace(**dict(zip(scratch_names, refs[len(output_names) :])))

    def w_of(name):
        return getattr(scratch, name)

    height = strip * line
    cells = height * width
    c = inputs.lift_weight.shape[1]
    strip_cells = strip * width
    history = inputs.frames.shape[1]

    core = lax.axis_index("section")
    plane = lax.axis_index("batch")
    row = lax.axis_index("rows")
    middle = lax.rem(row + 1, 4) // 2

    def device_at(to):
        return (core, plane, to)

    place = SimpleNamespace(
        core=core,
        partner=(1 - core, plane, row),
        line=SimpleNamespace(
            count=line,
            here=row,
            device=device_at,
            middle=middle == 1,
            edge=middle == 0,
            inner=1 + row // 2,
            across=3 - row,
            outer=3 * (row // 2),
        ),
        plane_group=SimpleNamespace(
            count=4, here=plane, device=lambda to: (core, to, row)
        ),
        cores_group=SimpleNamespace(
            count=8,
            here=core * 4 + plane,
            device=lambda to: (to // 4, lax.rem(to, 4), row),
        ),
        small=scratch.small,
        sums=scratch.sums,
        final=outputs.gradients,
        landing=scratch.landing,
        send=scratch.send,
        recv=scratch.recv,
    )
    local_sem = scratch.local

    frames_in, mask_in, cot = scratch.frames_in, scratch.mask_in, scratch.cot
    here_rows = pl.ds(pl.multiple_of(row * strip_cells, strip_cells), strip_cells)
    frames_from, mask_from, cot_from = scratch.frames_from, scratch.mask_from, scratch.cot_from
    staged = (
        pltpu.make_async_copy(inputs.frames, frames_from, local_sem.at[7]),
        pltpu.make_async_copy(inputs.cell_mask, mask_from, local_sem.at[8]),
        pltpu.make_async_copy(inputs.cotangent, cot_from, local_sem.at[9]),
    )
    for copy in staged:
        copy.start()

    weight_copies = {}
    for k, name in enumerate(LARGE):
        copy = pltpu.make_async_copy(getattr(inputs, name), w_of(name), local_sem.at[k])
        weight_copies[name] = copy
        copy.start()

    barrier = pltpu.get_barrier_semaphore()
    peers = [device_at(lax.rem(row + k, line)) for k in range(1, line)]
    cores_group = place.cores_group
    for k in range(1, 8):
        peers.append(cores_group.device(lax.rem(cores_group.here + k, 8)))
    for device in peers:
        pl.semaphore_signal(barrier, inc=1, device_id=device, device_id_type=MESH)
    pl.semaphore_wait(barrier, len(peers))

    next_sem = 0

    def make(source, target, device):
        nonlocal next_sem
        copy = pltpu.make_async_remote_copy(
            src_ref=source,
            dst_ref=target,
            send_sem=scratch.send.at[next_sem],
            recv_sem=scratch.recv.at[next_sem],
            device_id=device,
            device_id_type=MESH,
        )
        next_sem += 1
        return copy

    def send(source, target, device):
        copy = make(source, target, device)
        copy.start()
        return copy

    def strip_of(ref, to):
        return ref.at[pl.ds(pl.multiple_of(to * strip_cells, strip_cells), strip_cells)]

    frame_copies, output_copies = [], []
    for copy in staged[:2]:
        copy.wait()
    for k in range(1, line):
        to = lax.rem(row + k, line)
        device = device_at(to)
        frame_copies.append(send(frames_from.at[to], frames_in.at[row], device))
        frame_copies.append(send(mask_from.at[to], mask_in.at[row], device))
    staged[2].wait()
    cot_swap = LineSwap(
        place.line,
        lambda to: cot_from.at[to],
        lambda source: strip_of(cot, source),
        scratch.cot_inward,
        scratch.cot_across,
        make,
    )
    cot_swap.first()

    copied = SimpleNamespace(**weight_copies)
    def put_pair(target, block, value):
        high, low = split(value)
        rows = slice(block * c, (block + 1) * c)
        target[rows, 0:c] = high
        target[rows, c : 2 * c] = low

    def stack_conv(source, half, depth, forward, backward):
        for a in range(3):
            for b in range(3):
                at = (3 * a + b) * depth + half * c
                value = source[at : at + c, :]
                turned = value.T
                for places in (HIGH_AT, LOW_AT):
                    put_pair(forward, 6 * a + places[b], value)
                    put_pair(backward, 6 * (2 - a) + places[2 - b], turned)

    copied.enc_conv1.wait()
    stack_conv(scratch.enc_conv1, 0, c, scratch.fe1, scratch.be1)
    copied.enc_conv2.wait()
    stack_conv(scratch.enc_conv2, 0, c, scratch.fe2, scratch.be2)
    copied.reducer_weight.wait()
    for k in range(4):
        value = scratch.reducer_weight[k * c : (k + 1) * c, :]
        turned = value.T
        for block in (k, k + 4):
            put_pair(scratch.f_down, block, value)
        for block in (0, 1):
            put_pair(scratch.b_down.at[k], block, turned)
    copied.up_weight.wait()
    for k in range(4):
        value = scratch.up_weight[k * c : (k + 1) * c, :]
        turned = value.T
        for block in (0, 1):
            put_pair(scratch.f_up.at[k], block, value)
        for block in (k, k + 4):
            put_pair(scratch.b_up, block, turned)
    copied.dec_conv1.wait()
    stack_conv(scratch.dec_conv1, 0, 2 * c, scratch.fd1a, scratch.bd1a)
    stack_conv(scratch.dec_conv1, 1, 2 * c, scratch.fd1b, scratch.bd1b)
    copied.dec_conv2.wait()
    stack_conv(scratch.dec_conv2, 0, c, scratch.fd2, scratch.bd2)
    copied.skip_weight.wait()
    for half in range(2):
        value = scratch.skip_weight[half * c : (half + 1) * c, :]
        turned = value.T
        for block in (half, half + 2):
            put_pair(scratch.f_skip, block, value)
        for block in (0, 1):
            put_pair(scratch.b_skip.at[half], block, turned)

    for buffer in (scratch.xe1, scratch.xe2, scratch.xd1a, scratch.xd1b, scratch.xd2, scratch.xg):
        edge = jnp.zeros((width, 6 * c), BF16)
        buffer[0:width, :] = edge
        buffer[cells + width : cells + 2 * width, :] = edge

    lift = scratch.lift
    lift[...] = jnp.zeros(lift.shape, F32)
    lift[0:history, :] = inputs.lift_weight[...]
    lift[history : history + 1, :] = inputs.lift_bias[...]

    block = 2 * width
    column = lax.rem(lax.broadcasted_iota(jnp.int32, (block, c), 0), width)
    at_first, at_last = column == 0, column == width - 1
    zeros8 = jnp.zeros((8, c), F32)
    ones16 = group_ones(c, c // GROUPS)
    ones32 = group_ones(c, 2 * c // GROUPS)
    count16 = float(cells * (c // GROUPS))
    count32 = float(cells * (2 * c // GROUPS))

    def grid_rows(step, carry=0):
        return lax.fori_loop(0, cells // block, step, carry, unroll=2)

    def row_at(h):
        return pl.ds(pl.multiple_of(h * block, block), block)

    def chunk_at(i):
        return pl.ds(pl.multiple_of(i * CHUNK, CHUNK), CHUNK)

    def put_row(target, h, value):
        rows = pl.ds(pl.multiple_of(h * block + width, width), block)
        left = jnp.where(at_first, 0.0, pltpu.roll(value, 1, 0))
        right = jnp.where(at_last, 0.0, pltpu.roll(value, block - 1, 0))
        for b, piece in enumerate((left, value, right)):
            high, low = split(piece)
            target[rows, HIGH_AT[b] * c : (HIGH_AT[b] + 1) * c] = high
            target[rows, LOW_AT[b] * c : (LOW_AT[b] + 1) * c] = low

    def put_turned(target, columns, value, first=0, second=1):
        high, low = split(value.T)
        target[first * c : (first + 1) * c, columns] = high
        target[second * c : (second + 1) * c, columns] = low

    def conv_chunk(pairs, i):
        total = None
        for data, weight in pairs:
            taps = []
            for a in range(3):
                rows = pl.ds(pl.multiple_of(i * CHUNK + a * width, width), CHUNK)
                taps.append(data[rows, :])
            part = dot(jnp.concatenate(taps, axis=1), weight[...])
            total = part if total is None else total + part
        return total

    def norm_of(first, second, ones, count):
        one, two = group_sums(first, second, ones)
        mean = one / count
        return mean, lax.rsqrt(two / count - mean * mean + EPS)

    def activate(source, target, turned, slope, scale, shift):
        def step(h, carry):
            value = source[row_at(h), :] * scale + shift
            below, density = normal(value)
            slope[row_at(h), :] = below + value * density
            value = value * below
            put_row(target, h, value)
            put_turned(turned, row_at(h), value)
            return carry

        grid_rows(step)

    def conv_norm(pairs, target):
        def step(i, carry):
            value = fold(conv_chunk(pairs, i))
            target[chunk_at(i), :] = value
            return carry[0] + tile_sums(value), carry[1] + tile_sums(value * value)

        return lax.fori_loop(0, cells // CHUNK, step, (zeros8, zeros8))

    def sums_of(source):
        def step(h, carry):
            value = source[row_at(h), :]
            return carry[0] + tile_sums(value), carry[1] + tile_sums(value * value)

        return grid_rows(step, (zeros8, zeros8))

    step_here = jnp.full((1, c), inputs.step_index[row], jnp.int32)

    def condition(table):
        total = jnp.zeros((1, 2 * c), F32)
        chosen = jnp.concatenate([step_here, step_here], axis=1)
        for s in range(table.shape[0]):
            total = total + jnp.where(chosen == s, table[s : s + 1, :], 0.0)
        return total[:, :c], total[:, c:]

    frames_in[row] = frames_from[row]
    mask_in[row] = mask_from[row]
    for copy in frame_copies:
        copy.wait_recv()
    fields = scratch.fields
    fields[...] = jnp.zeros(fields.shape, F32)
    frame_of = lax.broadcasted_iota(jnp.int32, (history, width), 0) // FIELDS
    keep = (frame_of >= HIST - inputs.counts[row]).astype(F32)
    masks = []
    for source in range(line):
        for k in range(strip):
            columns = slice((source * strip + k) * width, (source * strip + k + 1) * width)
            mask = mask_in[source, k : k + 1, :].astype(F32)
            masks.append(mask)
            fields[0:history, columns] = frames_in[source, :, k, :] * keep * mask
            fields[history : history + 1, columns] = mask
    lifted = scratch.lifted
    lifted[...] = dot_three(fields[...], lift[...], TN)

    enc_scale, enc_shift = condition(inputs.enc_step_table)
    dec_scale, dec_shift = condition(inputs.dec_step_table)

    mean_e1, inv_e1 = norm_of(*sums_of(lifted), ones16, count16)
    gain_e1, bias_e1 = inputs.enc_norm1_gain[...], inputs.enc_norm1_bias[...]
    a_e1 = inv_e1 * gain_e1
    activate(lifted, scratch.xe1, scratch.te1, scratch.slope_e1, a_e1, bias_e1 - mean_e1 * a_e1)
    middle_e = scratch.middle_e
    mean_e2, inv_e2 = norm_of(
        *conv_norm([(scratch.xe1, scratch.fe1)], middle_e), ones16, count16
    )
    gain_e2, bias_e2 = inputs.enc_norm2_gain[...], inputs.enc_norm2_bias[...]
    a_e2 = inv_e2 * gain_e2
    activate(
        middle_e,
        scratch.xe2,
        scratch.te2,
        scratch.slope_e2,
        a_e2 * (1.0 + enc_scale),
        (bias_e2 - mean_e2 * a_e2) * (1.0 + enc_scale) + enc_shift,
    )
    cot_swap.second()
    encoded = scratch.encoded
    conv2_bias = inputs.enc_conv2_bias[...]
    joined = scratch.joined

    def encode(i, carry):
        value = fold(conv_chunk([(scratch.xe2, scratch.fe2)], i))
        value = value + conv2_bias + lifted[chunk_at(i), :]
        encoded[chunk_at(i), :] = value
        high, low = split(value)
        joined[chunk_at(i), c : 2 * c] = high
        joined[chunk_at(i), 3 * c : 4 * c] = low
        put_turned(scratch.turned, chunk_at(i), value, 1, 3)
        return carry[0] + tile_sums(value), carry[1] + tile_sums(value * value)

    sums_enc = lax.fori_loop(0, cells // CHUNK, encode, (zeros8, zeros8))

    half_cells, quarter = cells // 2, cells // 4

    def pick(source):
        pieces = []
        for b in range(2):
            value = source[pl.ds(b, half_cells, stride=2), :]
            value = value.reshape(height // 2, 2, width // 2, c)
            pieces.append([value[:, a].reshape(quarter, c) for a in range(2)])
        return [pieces[b][a] for a in range(2) for b in range(2)]

    def place_cells(target, pieces):
        for b in range(2):
            both = [pieces[2 * a + b].reshape(height // 2, 1, width // 2, c) for a in range(2)]
            value = jnp.concatenate(both, axis=1).reshape(half_cells, c)
            target[pl.ds(b, half_cells, stride=2), :] = value

    x_down = scratch.x_down
    for k, piece in enumerate(pick(encoded)):
        high, low = split(piece)
        x_down[:, k * c : (k + 1) * c] = high
        x_down[:, (k + 4) * c : (k + 5) * c] = low
    lowered = fold(dot(x_down[...], scratch.f_down[...])) + inputs.reducer_bias[...]
    x_up = scratch.x_up
    high, low = split(lowered)
    x_up[:, 0:c] = high
    x_up[:, c : 2 * c] = low
    raised = scratch.raised
    up_bias = inputs.up_bias[...]
    place_cells(
        raised, [fold(dot(x_up[...], scratch.f_up[k])) + up_bias for k in range(4)]
    )

    def raise_row(h, carry):
        value = raised[row_at(h), :]
        high, low = split(value)
        joined[row_at(h), 0:c] = high
        joined[row_at(h), 2 * c : 3 * c] = low
        put_turned(scratch.turned, row_at(h), value, 0, 2)
        return carry[0] + tile_sums(value), carry[1] + tile_sums(value * value)

    sums_raised = grid_rows(raise_row, (zeros8, zeros8))

    halves = []
    for half, (source, sums) in enumerate(((raised, sums_raised), (encoded, sums_enc))):
        mean, inv = norm_of(*sums, ones32, count32)
        gain = inputs.dec_norm1_gain[half : half + 1, :]
        bias = inputs.dec_norm1_bias[half : half + 1, :]
        scale = inv * gain
        activate(
            source,
            (scratch.xd1a, scratch.xd1b)[half],
            scratch.td1.at[2 * c * half : 2 * c * (half + 1)],
            (scratch.slope_d1a, scratch.slope_d1b)[half],
            scale,
            bias - mean * scale,
        )
        halves.append((source, mean, inv, gain))
    middle_d = scratch.middle_d
    pairs = [(scratch.xd1a, scratch.fd1a), (scratch.xd1b, scratch.fd1b)]
    mean_d2, inv_d2 = norm_of(*conv_norm(pairs, middle_d), ones16, count16)
    cot_swap.third()
    gain_d2, bias_d2 = inputs.dec_norm2_gain[...], inputs.dec_norm2_bias[...]
    a_d2 = inv_d2 * gain_d2
    activate(
        middle_d,
        scratch.xd2,
        scratch.td2,
        scratch.slope_d2,
        a_d2 * (1.0 + dec_scale),
        (bias_d2 - mean_d2 * a_d2) * (1.0 + dec_scale) + dec_shift,
    )
    result = scratch.result
    last_bias = inputs.dec_conv2_bias[...] + inputs.skip_bias[...]

    def decode(i, carry):
        value = conv_chunk([(scratch.xd2, scratch.fd2)], i)
        value = value + dot(joined[chunk_at(i), :], scratch.f_skip[...])
        result[chunk_at(i), :] = fold(value) + last_bias
        return carry

    lax.fori_loop(0, cells // CHUNK, decode, 0)
    output_here, frames_here = outputs.output, outputs.frames_grad
    output_here[row] = result[here_rows]
    output_swap = LineSwap(
        place.line,
        lambda to: strip_of(result, to),
        lambda source: output_here.at[source],
        scratch.output_inward,
        scratch.output_across,
        make,
    )
    output_swap.first()

    exchanges = []
    waiting_runs = list(runs)
    landing_at = 0
    sem_at = 3 * (line - 1) + 20
    sums = scratch.sums

    def begin():
        nonlocal landing_at, sem_at
        start, rows = waiting_runs.pop(0)
        kind = Exchange if waiting_runs else SmallExchange
        exchange = kind(place, start, rows, landing_at, sem_at)
        landing_at += exchange.land_rows()
        sem_at += exchange.count()
        exchanges.append(exchange)
        exchange.advance()

    def advance(k):
        exchange = exchanges[k]
        exchange.advance()

    due = list(DUE)

    def point():
        for k in due.pop(0):
            advance(k)

    def small_row(k, value):
        sums[small_at + k : small_at + k + 1, :] = value

    def spread_grad(source):
        def step(h, carry):
            value = source[row_at(h), :]
            put_row(scratch.xg, h, value)
            return carry + tile_sums(value)

        return grid_rows(step, zeros8)

    def weight_grad(turned, at, depth, a):
        rows = pl.ds((2 - a) * width, cells)
        both = dot(turned[...], scratch.xg[rows, :])
        for half in range(depth // c):
            part = fold_rows(both[2 * c * half : 2 * c * (half + 1)])
            for b in range(3):
                high, low = HIGH_AT[2 - b] * c, LOW_AT[2 - b] * c
                to = at + (3 * a + b) * depth + half * c
                sums[to : to + c, :] = part[:, high : high + c] + part[:, low : low + c]

    def back_conv(weight, slope, target, source, mean, inv):
        carry = (zeros8, zeros8)
        for i in range(cells // CHUNK):
            value = fold(conv_chunk([(scratch.xg, weight)], i)) * slope[chunk_at(i), :]
            target[chunk_at(i), :] = value
            normed = (source[chunk_at(i), :] - mean) * inv
            carry = (carry[0] + tile_sums(value), carry[1] + tile_sums(value * normed))
            if i % (cells // CHUNK // 2) == cells // CHUNK // 2 - 1:
                point()
        return carry

    def norm_grad(sums_in, scale, ones, count):
        one, two = group_sums(sums_in[0] * scale, sums_in[1] * scale, ones)
        return one / count, two / count

    cot[here_rows] = cot_from[row]
    cot_swap.arrive()
    total_cot = column_sum(spread_grad(cot))
    for a in range(3):
        weight_grad(scratch.td2, starts.dec_conv2, c, a)
    part = fold(dot(scratch.turned[...], scratch.xg[width : cells + width, 2 * c : 4 * c]))
    sums[starts.skip_weight : starts.skip_weight + 2 * c, :] = fold_rows(part)
    small_row(3, total_cot)
    begin()

    grad = scratch.grad
    sums_d2 = back_conv(scratch.bd2, scratch.slope_d2, grad, middle_d, mean_d2, inv_d2)
    side_grads = (scratch.grad_a, scratch.grad_b)
    for half in range(2):

        def skip_back(i, carry, half=half):
            rows = pl.ds(pl.multiple_of(i * CHUNK + width, width), CHUNK)
            value = dot(scratch.xg[rows, 2 * c : 4 * c], scratch.b_skip[half])
            side_grads[half][chunk_at(i), :] = fold(value)
            return carry

        lax.fori_loop(0, cells // CHUNK, skip_back, 0)
    point()

    def table_rows(k, sums_in, gain, bias, one_plus):
        plain, times = column_sum(sums_in[0]), column_sum(sums_in[1])
        for s in range(inputs.enc_step_table.shape[0]):
            small_row(k + 2 * s, jnp.where(step_here == s, gain * times + bias * plain, 0.0))
            small_row(k + 2 * s + 1, jnp.where(step_here == s, plain, 0.0))
        return one_plus * times, one_plus * plain

    def middle_grad(source, mean, inv, scale, sums_in):
        zero, slope = norm_grad(sums_in, scale, ones16, count16)

        def step(h, carry):
            normed = (source[row_at(h), :] - mean) * inv
            value = inv * (grad[row_at(h), :] * scale - zero - normed * slope)
            put_row(scratch.xg, h, value)
            return carry

        grid_rows(step)

    gain_row, bias_row = table_rows(16, sums_d2, gain_d2, bias_d2, 1.0 + dec_scale)
    small_row(8, gain_row)
    small_row(9, bias_row)
    middle_grad(middle_d, mean_d2, inv_d2, gain_d2 * (1.0 + dec_scale), sums_d2)
    point()
    output_swap.second()
    for a in range(3):
        weight_grad(scratch.td1, starts.dec_conv1, 2 * c, a)
        point()
        begin()

    for half, (source, mean, inv, gain) in enumerate(halves):
        sums_in = back_conv(
            (scratch.bd1a, scratch.bd1b)[half],
            (scratch.slope_d1a, scratch.slope_d1b)[half],
            grad,
            source,
            mean,
            inv,
        )
        small_row(4 + half, column_sum(sums_in[1]))
        small_row(6 + half, column_sum(sums_in[0]))
        zero, slope = norm_grad(sums_in, gain, ones32, count32)
        target = side_grads[half]

        def input_grad(h, carry):
            normed = (source[row_at(h), :] - mean) * inv
            value = inv * (grad[row_at(h), :] * gain - zero - normed * slope)
            value = target[row_at(h), :] + value
            target[row_at(h), :] = value
            return carry + tile_sums(value)

        total = grid_rows(input_grad, zeros8)
        if half == 0:
            small_row(2, column_sum(total))
        point()

    output_swap.third()
    grad_raised, grad_encoded = side_grads
    x_grad_up = scratch.x_grad_up
    for k, piece in enumerate(pick(grad_raised)):
        high, low = split(piece)
        x_grad_up[:, k * c : (k + 1) * c] = high
        x_grad_up[:, (k + 4) * c : (k + 5) * c] = low
    grad_lowered = fold(dot(x_grad_up[...], scratch.b_up[...]))
    small_row(1, jnp.sum(grad_lowered, axis=0, keepdims=True))
    x_grad_low = scratch.x_grad_low
    high, low = split(grad_lowered)
    x_grad_low[:, 0:c] = high
    x_grad_low[:, c : 2 * c] = low
    point()
    part = fold(fold_rows(dot(x_up[...], x_grad_up[...], TN)))
    for k in range(4):
        at = starts.up_weight + k * c
        sums[at : at + c, :] = part[:, k * c : (k + 1) * c]
    part = fold_rows(fold(dot(x_down[...], x_grad_low[...], TN)))
    sums[starts.reducer_weight : starts.reducer_weight + 4 * c, :] = part
    point()
    begin()
    place_cells(
        grad, [fold(dot(x_grad_low[...], scratch.b_down[k])) for k in range(4)]
    )

    def join_row(h, carry):
        value = grad_encoded[row_at(h), :] + grad[row_at(h), :]
        grad_encoded[row_at(h), :] = value
        put_row(scratch.xg, h, value)
        return carry + tile_sums(value)

    small_row(0, column_sum(grid_rows(join_row, zeros8)))
    for k in range(10, 16):
        small_row(k, jnp.zeros((1, c), F32))
    sums[small_at + 24 : small_at + LATE, :] = jnp.zeros((LATE - 24, c), F32)
    point()
    for a in range(3):
        weight_grad(scratch.te2, starts.enc_conv2, c, a)
        point()
    begin()
    sums_e2 = back_conv(scratch.be2, scratch.slope_e2, grad, middle_e, mean_e2, inv_e2)
    gain_row, bias_row = table_rows(LATE + 24, sums_e2, gain_e2, bias_e2, 1.0 + enc_scale)
    small_row(LATE + 18, gain_row)
    small_row(LATE + 19, bias_row)
    middle_grad(middle_e, mean_e2, inv_e2, gain_e2 * (1.0 + enc_scale), sums_e2)
    point()
    for a in range(3):
        weight_grad(scratch.te1, starts.enc_conv1, c, a)
        point()
        if a:
            begin()
    sums_e1 = back_conv(scratch.be1, scratch.slope_e1, grad, lifted, mean_e1, inv_e1)
    small_row(LATE + 16, column_sum(sums_e1[1]))
    small_row(LATE + 17, column_sum(sums_e1[0]))
    zero, slope = norm_grad(sums_e1, gain_e1, ones16, count16)

    def lifted_grad(h, carry):
        normed = (lifted[row_at(h), :] - mean_e1) * inv_e1
        value = inv_e1 * (grad[row_at(h), :] * gain_e1 - zero - normed * slope)
        grad[row_at(h), :] = grad_encoded[row_at(h), :] + value
        return carry

    grid_rows(lifted_grad)
    point()

    late_at = small_at + LATE
    sums[late_at : late_at + 16, :] = dot_three(fields[...], grad[...])
    sums[late_at + 20 : late_at + 24, :] = jnp.zeros((4, c), F32)
    point()
    begin()
    back = dot_three(lift[...], grad[...], NT)
    frames_out = scratch.frames_out
    for source in range(line):
        for k in range(strip):
            h = source * strip + k
            value = back[0:history, h * width : (h + 1) * width]
            frames_out[source, :, k, :] = value * keep * masks[h]
    frames_here[row] = frames_out[row]
    for k in range(1, line):
        to = lax.rem(row + k, line)
        output_copies.append(
            send(frames_out.at[to], frames_here.at[row], device_at(to))
        )

    output_swap.arrive()
    for k in REST:
        advance(k)
    assert not due and all(exchange.done() for exchange in exchanges)

    for copy in output_copies:
        copy.wait_recv()
    for copy in frame_copies + output_copies:
        copy.wait_send()
    cot_swap.sent()
    output_swap.sent()
    for exchange in exchanges:
        for copy, only in exchange.copies:
            if only is None:
                copy.wait_send()
            else:
                pl.when(only)(copy.wait_send)


def write_kernel(layout, *refs):
    shapes, starts, small_at = layout
    output, frames_grad, gradients_here = refs[:3]
    outputs = refs[3:-1]
    sem = refs[-1]
    c = gradients_here.shape[1]
    leaving = []

    def leave(source, target):
        leaving.append(pltpu.make_async_copy(source, target, sem.at[len(leaving)]))
        leaving[-1].start()

    for k, name in enumerate(LARGE):
        rows = pl.ds(starts[name], shapes[name][0])
        leave(gradients_here.at[rows], outputs[2 + k])
    for target, (k, rows) in zip(outputs[2 + len(LARGE) :], SMALL_ROWS.values()):
        at = small_at + k
        if rows == 8:
            for s in range(target.shape[0]):
                target[s : s + 1, 0:c] = gradients_here[at + 2 * s : at + 2 * s + 1, :]
                target[s : s + 1, c : 2 * c] = gradients_here[at + 2 * s + 1 : at + 2 * s + 2, :]
        else:
            target[...] = gradients_here[at : at + rows, :]
    leave(output, outputs[0])
    leave(frames_grad, outputs[1])
    for copy in leaving:
        copy.wait()


def whole_items(shape, *arguments):
    line = shape["rows"]
    whole = Given(*arguments)
    given = whole._asdict()
    frames, cotangent = whole.frames, whole.cotangent
    items, history, strip, width = frames.shape
    c = cotangent.shape[-1]
    cells = strip * line * width
    flat = {}
    for name, value in given.items():
        if value is cotangent:
            value = value.reshape(items, strip * width, c)
        elif name in LARGE:
            value = value.reshape(-1, c)
        elif value.ndim == 1 and name not in IN_SMEM:
            value = value.reshape(-1, c)
        flat[name] = value
    shapes = {name: flat[name].shape for name in LARGE}
    big_layout = layout_of(SimpleNamespace(**shapes))
    starts, small_at, total_rows, runs = big_layout
    copies = 20 + 3 * (line - 1) + len(runs) * (6 + 2 * PIECES + 2 * (line - 1)) + 6
    landing = sum(rows // 2 + 5 * rows // 8 for _, rows in runs) + LATE_COUNT * (8 + line)
    shifted = pltpu.VMEM((cells + 2 * width, 6 * c), BF16)
    forward = pltpu.VMEM((18 * c, 2 * c), BF16)
    backward = forward
    field = pltpu.VMEM((cells, c), F32)
    flipped_field = pltpu.VMEM((2 * c, cells), BF16)
    quarter = cells // 4
    scratch = dict(
        small=pltpu.VMEM((LATE_COUNT, c), F32),
        send=pltpu.SemaphoreType.DMA((copies,)),
        recv=pltpu.SemaphoreType.DMA((copies,)),
        local=pltpu.SemaphoreType.DMA((12 + len(runs),)),
        sums=pltpu.VMEM((total_rows, c), F32),
        landing=pltpu.VMEM((landing, c), F32),
        frames_in=pltpu.VMEM((line, history, strip, width), F32),
        mask_in=pltpu.VMEM((line, strip, width), jnp.int32),
        frames_out=pltpu.VMEM((line, history, strip, width), F32),
        frames_from=pltpu.VMEM((line, history, strip, width), F32),
        mask_from=pltpu.VMEM((line, strip, width), jnp.int32),
        cot_from=pltpu.VMEM((items, strip * width, c), F32),
        cot_inward=pltpu.VMEM((2, strip * width, c), F32),
        cot_across=pltpu.VMEM((2, strip * width, c), F32),
        output_inward=pltpu.VMEM((2, strip * width, c), F32),
        output_across=pltpu.VMEM((2, strip * width, c), F32),
        fields=pltpu.VMEM((16, cells), F32),
        lift=pltpu.VMEM((16, c), F32),
        joined=pltpu.VMEM((cells, 4 * c), BF16),
        x_down=pltpu.VMEM((quarter, 8 * c), BF16),
        x_grad_up=pltpu.VMEM((quarter, 8 * c), BF16),
        x_up=pltpu.VMEM((quarter, 2 * c), BF16),
        x_grad_low=pltpu.VMEM((quarter, 2 * c), BF16),
        f_down=pltpu.VMEM((8 * c, 2 * c), BF16),
        b_down=pltpu.VMEM((4, 2 * c, 2 * c), BF16),
        f_up=pltpu.VMEM((4, 2 * c, 2 * c), BF16),
        b_up=pltpu.VMEM((8 * c, 2 * c), BF16),
        f_skip=pltpu.VMEM((4 * c, 2 * c), BF16),
        b_skip=pltpu.VMEM((2, 2 * c, 2 * c), BF16),
        xe1=shifted,
        xe2=shifted,
        xd1a=shifted,
        xd1b=shifted,
        xd2=shifted,
        xg=shifted,
        te1=flipped_field,
        te2=flipped_field,
        td1=pltpu.VMEM((4 * c, cells), BF16),
        td2=flipped_field,
        turned=pltpu.VMEM((4 * c, cells), BF16),
        fe1=forward,
        fe2=forward,
        fd1a=forward,
        fd1b=forward,
        fd2=forward,
        be1=backward,
        be2=backward,
        bd1a=backward,
        bd1b=backward,
        bd2=backward,
        slope_e1=field,
        slope_e2=field,
        slope_d1a=field,
        slope_d1b=field,
        slope_d2=field,
        lifted=field,
        middle_e=field,
        encoded=field,
        raised=field,
        middle_d=field,
        result=field,
        cot=field,
        grad=field,
        grad_a=field,
        grad_b=field,
    )
    scratch.update({name: pltpu.VMEM(shapes[name], F32) for name in LARGE})

    in_hbm = pl.BlockSpec(memory_space=pl.ANY)
    in_vmem = pl.BlockSpec(memory_space=pltpu.VMEM)
    in_smem = pl.BlockSpec(memory_space=pltpu.SMEM)
    in_specs = [
        in_hbm if name in IN_HBM else in_smem if name in IN_SMEM else in_vmem
        for name in ARGUMENTS
    ]
    out_shape = [
        pltpu.VMEM((items, strip * width, c), F32),
        pltpu.VMEM(frames.shape, F32),
        pltpu.VMEM((total_rows, c), F32),
    ]
    out_specs = [in_vmem] * 3
    results = pl.pallas_call(
        functools.partial(
            item_kernel,
            (line, strip, width, shapes, big_layout),
            tuple(scratch),
        ),
        out_shape=out_shape,
        in_specs=in_specs,
        out_specs=out_specs,
        scratch_shapes=list(scratch.values()),
        compiler_params=pltpu.CompilerParams(
            collective_id=0, has_side_effects=True, vmem_limit_bytes=56 * 1024 * 1024
        ),
    )(*[flat[name] for name in ARGUMENTS])
    names = LARGE + tuple(SMALL_ROWS)
    written = pl.pallas_call(
        functools.partial(write_kernel, (shapes, starts, small_at)),
        out_shape=[
            jax.ShapeDtypeStruct((items, strip * width, c), F32),
            jax.ShapeDtypeStruct(frames.shape, F32),
        ]
        + [jax.ShapeDtypeStruct(flat[name].shape, F32) for name in names],
        in_specs=[in_vmem] * 3,
        out_specs=[in_hbm] * (2 + len(LARGE)) + [in_vmem] * len(SMALL_ROWS),
        scratch_shapes=[pltpu.SemaphoreType.DMA((2 + len(LARGE),))],
        compiler_params=pltpu.CompilerParams(vmem_limit_bytes=16 * 1024 * 1024),
    )(*results)
    grads = dict(zip(names, written[2:]))
    ordered = [name for name in ARGUMENTS if name in grads]
    return (written[0].reshape(cotangent.shape), written[1]) + tuple(
        grads[name].reshape(given[name].shape) for name in ordered
    )


def body(shape, *arguments):
    items, _, strip, width = arguments[0].shape
    line = shape["rows"]
    whole = (
        shape["section"] == 2
        and shape["batch"] == 4
        and items == line == 4
        and arguments[-1].shape[-1] == 128
        and (strip * line * width) % CHUNK == 0
    )
    return whole_items(shape, *arguments) if whole else strips_body(*arguments)


def solution(mesh):
    in_specs = (
        P(("section", "batch"), None, "rows", None),
        P(("section", "batch")),
        P(("section", "batch"), "rows", None),
        P(("section", "batch")),
        P(),
        P(),
        P(),
        P(),
        P(),
        P(),
        P(),
        P(),
        P(),
        P(),
        P(),
        P(),
        P(),
        P(),
        P(),
        P(),
        P(),
        P(),
        P(),
        P(),
        P(),
        P(),
        P(),
        P(),
        P(("section", "batch"), "rows", None, None),
    )
    out_specs = (
        P(("section", "batch"), "rows", None, None),
        P(("section", "batch"), None, "rows", None),
        P(),
        P(),
        P(),
        P(),
        P(),
        P(),
        P(),
        P(),
        P(),
        P(),
        P(),
        P(),
        P(),
        P(),
        P(),
        P(),
        P(),
        P(),
        P(),
        P(),
        P(),
        P(),
        P(),
        P(),
    )
    return jax.shard_map(functools.partial(body, mesh.shape), mesh=mesh, in_specs=in_specs, out_specs=out_specs, check_vma=False)
```
